32 devices in a mesh: batch: 4 (over z), seq: 8 (over y, x, core).
Axes of the slice: x: 2, y: 2, z: 4, core: 2. Of those that a mesh axis runs over, the one named last changes fastest.
Arguments:
- tokens: bfloat16 [4, 4096, 1536], P('batch', 'seq'), may hold values from -6 to 6
- norm_gain: float32 [1536], replicated, may hold values from 0.1 to 1.9
- in_weight: bfloat16 [1536, 6448], P('batch'), may hold values from -0.15625 to 0.15625
- conv_weight: float32 [4, 3328], replicated, may hold values from -3 to 3
- conv_bias: float32 [3328], replicated, may hold values from -3 to 3
- dt_bias: float32 [48], replicated, may hold values from -6 to -1
- decay_log: float32 [48], replicated, may hold values from -8 to 1
- skip_scale: float32 [48], replicated, may hold values from 0.5 to 1.5
- gate_gain: float32 [3072], replicated, may hold values from 0.1 to 1.9
- out_weight: bfloat16 [3072, 1536], P('batch'), may hold values from -0.109375 to 0.109375
- cotangent: bfloat16 [4, 4096, 1536], P('batch', 'seq'), may hold values from -6 to 6
Outputs:
- block_out: bfloat16 [4, 4096, 1536], P('batch', 'seq')
- input_grad: float32 [4, 4096, 1536], P('batch', 'seq')
- norm_gain_grad: float32 [1536], replicated
- in_weight_grad: float32 [1536, 6448], P('batch')
- conv_weight_grad: float32 [4, 3328], replicated
- conv_bias_grad: float32 [3328], replicated
- dt_bias_grad: float32 [48], replicated
- decay_log_grad: float32 [48], replicated
- skip_scale_grad: float32 [48], replicated
- gate_gain_grad: float32 [3072], replicated
- out_weight_grad: float32 [3072, 1536], P('batch')
The draws below stay inside these ranges and needn't reach their ends.
All inputs are finite; a program needn't handle non-finite values.
Results may differ from the reference program's by a relative error of at most 0.015.
The reference program's roundings to bfloat16 on the way count: a program that leaves them out, or rounds other values in their place, can miss the bound.
Values may be sent and summed in bfloat16 or wider, within the bound.
No kernel may reach another device: no remote copies, remote signals or barrier semaphores. Data moves between devices by JAX's collectives and lax.ppermute only.
A program may use at most 320 MiB of HBM per device.

```python
import jax
import jax.numpy as jnp
from jax import lax

D = 1536
H = 48
P_SIZE = 64
NS = 128
KW = 4
GROUP = 256
DI = 3072
CONV = 3328
PROJ = 6448
LENGTH = 4096
SEQS = 4


def level_of(rng, dims, cuts, least, top_value):
    gain = 1.0
    for dim, shards_of in cuts:
        heights = jax.random.uniform(jax.random.fold_in(jax.random.fold_in(rng, 6), dim), (shards_of,), jnp.float32, least / len(cuts), top_value / len(cuts))
        gain = gain * jnp.repeat(jnp.exp(heights), dims[dim] // shards_of).reshape((-1,) + (1,) * (len(dims) - 1 - dim))
    return gain


def gaussian(rng, shape, width, most, shards=(), held_as=jnp.bfloat16):
    values = jax.random.normal(rng, shape, jnp.float32) * width
    if len(shards) > 0:
        values = level_of(rng, shape, shards, -0.22, 0.18) * values
    return jnp.clip(values, min=-most, max=most).astype(held_as)


def setup_inputs(seed: int = 0) -> dict:
    arg_keys = jax.random.split(jax.random.key(seed), 12)
    tokens = gaussian(arg_keys[0], (SEQS, LENGTH, D), 1.0, 6.0, ((0, 4), (1, 8)))
    norm_gain = jnp.clip(1.0 + 0.18 * jax.random.normal(arg_keys[1], (D,), jnp.float32), 0.1, 1.9)
    in_weight = gaussian(arg_keys[2], (D, PROJ), D ** -0.5, 0.15625, ((0, 4),))
    conv_weight = gaussian(arg_keys[3], (KW, CONV), 0.5, 3.0, (), jnp.float32)
    conv_bias = gaussian(arg_keys[4], (CONV,), 0.5, 3.0, (), jnp.float32)
    dt_bias = jnp.clip(jax.random.uniform(arg_keys[5], (H,), jnp.float32, -6.0, -1.0), -6.0, -1.0)
    decay_log = jnp.clip(jax.random.uniform(arg_keys[6], (H,), jnp.float32, -8.0, 1.0), -8.0, 1.0)
    skip_scale = jnp.clip(jax.random.uniform(arg_keys[7], (H,), jnp.float32, 0.5, 1.5), 0.5, 1.5)
    gate_gain = jnp.clip(1.0 + 0.18 * jax.random.normal(arg_keys[8], (DI,), jnp.float32), 0.1, 1.9)
    out_weight = gaussian(arg_keys[9], (DI, D), DI ** -0.5, 0.109375, ((0, 4),))
    cotangent = gaussian(arg_keys[10], (SEQS, LENGTH, D), 1.0, 6.0, ((0, 4), (1, 8)))
    return {"tokens": tokens, "norm_gain": norm_gain, "in_weight": in_weight, "conv_weight": conv_weight, "conv_bias": conv_bias, "dt_bias": dt_bias, "decay_log": decay_log, "skip_scale": skip_scale, "gate_gain": gate_gain, "out_weight": out_weight, "cotangent": cotangent}


highest = lax.Precision.HIGHEST
epsilon = 1e-05

@jax.custom_vjp
def low(v):
    return lax.optimization_barrier(v.astype(jnp.bfloat16)).astype(jnp.float32)

@jax.custom_vjp
def low_back(v):
    return v

def low_keep(v):
    return (low(v), None)

def low_pass(kept, grad):
    return (grad,)

def back_keep(v):
    return (v, None)

def back_low(kept, grad):
    return (low(grad),)
low.defvjp(low_keep, low_pass)
low_back.defvjp(back_keep, back_low)

def group_step(carry_state, block_inputs):
    signal, entry, readout, decay_step, step_size = block_inputs
    running = jnp.cumsum(decay_step, axis=0)
    length = running.shape[0]
    causal = (jnp.arange(length)[:, None] >= jnp.arange(length)[None, :])[None]
    heads_first = running.T
    spread = heads_first[:, :, None] - heads_first[:, None, :]
    kernel = jnp.where(causal, jnp.exp(jnp.where(causal, spread, 0.0)), 0.0)
    scores = jnp.einsum('tn,sn->ts', readout, entry, precision=highest)
    weights = scores[None] * kernel * step_size.T[:, None, :]
    within = jnp.einsum('hts,shp->thp', weights, signal, precision=highest)
    carried = jnp.exp(running)[:, :, None] * jnp.einsum('tn,hpn->thp', readout, carry_state, precision=highest)
    tail_weight = jnp.exp(running[-1][None, :] - running) * step_size
    update = jnp.einsum('sh,shp,sn->hpn', tail_weight, signal, entry, precision=highest)
    new_state = jnp.exp(running[-1])[:, None, None] * carry_state + update
    return (new_state, within + carried)

def block_forward(tokens_row, norm_gain, in_weight, conv_weight, conv_bias, dt_bias, decay_log, skip_scale, gate_gain, out_weight):
    inverse = lax.rsqrt(lax.optimization_barrier(jnp.mean(tokens_row * tokens_row, axis=-1, keepdims=True)) + epsilon)
    normed = low(tokens_row * inverse * norm_gain)
    projected = low_back(jnp.dot(normed, in_weight, precision=highest))
    gate_part = projected[:, :DI]
    conv_input = low(projected[:, DI:DI + CONV])
    step_raw = projected[:, DI + CONV:]
    padded = jnp.concatenate([jnp.zeros((KW - 1, CONV), jnp.float32), conv_input], axis=0)
    mixed_sum = conv_bias + conv_weight[0] * padded[0:LENGTH]
    for offset in range(1, KW):
        mixed_sum = mixed_sum + conv_weight[offset] * padded[offset:offset + LENGTH]
    activated = jax.nn.silu(mixed_sum)
    signal = low(activated[:, :DI]).reshape(LENGTH, H, P_SIZE)
    entry = low(activated[:, DI:DI + NS])
    readout = low(activated[:, DI + NS:])
    step_size = jax.nn.softplus(step_raw + dt_bias)
    decay_step = step_size * -jnp.exp(decay_log)
    num_blocks = LENGTH // GROUP
    block_inputs = (signal.reshape(num_blocks, GROUP, H, P_SIZE), entry.reshape(num_blocks, GROUP, NS), readout.reshape(num_blocks, GROUP, NS), decay_step.reshape(num_blocks, GROUP, H), step_size.reshape(num_blocks, GROUP, H))
    final_state, outputs = lax.scan(jax.checkpoint(group_step), jnp.zeros((H, P_SIZE, NS), jnp.float32), block_inputs)
    ssd_value = outputs.reshape(LENGTH, H, P_SIZE) + skip_scale[None, :, None] * signal
    gated_value = ssd_value.reshape(LENGTH, DI) * jax.nn.silu(gate_part)
    scale_back = lax.rsqrt(lax.optimization_barrier(jnp.mean(gated_value * gated_value, axis=-1, keepdims=True)) + epsilon)
    normed_out = low(gated_value * scale_back * gate_gain)
    return tokens_row + jnp.dot(normed_out, out_weight, precision=highest)

def reference(tokens, norm_gain, in_weight, conv_weight, conv_bias, dt_bias, decay_log, skip_scale, gate_gain, out_weight, cotangent):
    in_wide = in_weight.astype(jnp.float32)
    out_wide = out_weight.astype(jnp.float32)
    params = (norm_gain, in_wide, conv_weight, conv_bias, dt_bias, decay_log, skip_scale, gate_gain, out_wide)

    def one_sequence(totals, couple):
        tokens_row, cot_row = couple
        result, pullback = jax.vjp(block_forward, tokens_row.astype(jnp.float32), norm_gain, in_wide, conv_weight, conv_bias, dt_bias, decay_log, skip_scale, gate_gain, out_wide)
        gradients = pullback(cot_row.astype(jnp.float32))
        totals = tuple((total + piece for total, piece in zip(totals, gradients[1:])))
        return (totals, (result.astype(jnp.bfloat16), gradients[0]))
    starting = tuple((jnp.zeros(param.shape, jnp.float32) for param in params))
    totals, (outputs, input_grad) = lax.scan(one_sequence, starting, (tokens, cotangent))
    return (outputs, input_grad, totals[0], totals[1], totals[2], totals[3], totals[4], totals[5], totals[6], totals[7], totals[8])
```

```python
import functools

import jax
import jax.numpy as jnp
from jax import lax
from jax.experimental import pallas as pl
from jax.experimental.pallas import tpu as pltpu
from jax.sharding import PartitionSpec as P

GROUP = 256
LANES = 128
HALO = 8
epsilon = 1e-05
highest = lax.Precision.HIGHEST
f32 = jnp.float32
bf16 = jnp.bfloat16


def exchange(value, axis, distance):
    count = lax.axis_size(axis)
    return lax.ppermute(value, axis, [(source, source ^ distance) for source in range(count)])


def bits_of(count):
    return [1 << k for k in range(count.bit_length() - 1)]


def gather_relative(value):
    bits = bits_of(lax.axis_size("seq"))
    near, far = bits[:1], bits[1:]
    half = value.shape[0] // 2
    held = []
    for part, order in ((value[:half], far + near), (value[half:], far[::-1] + near)):
        pieces = {0: part}
        for bit in order:
            for index, piece in list(pieces.items()):
                pieces[index | bit] = exchange(piece, "seq", bit)
        held.append(pieces)
    return held


def placed_order(count):
    return [2 * k for k in range(count // 2)] + [2 * k + 1 for k in range(count // 2)]


def gather_tokens(value):
    first, second = gather_relative(value)
    pieces = []
    for index in placed_order(lax.axis_size("seq")):
        pieces += [first[index], second[index]]
    return jnp.concatenate(pieces, axis=0)


def scatter_sum(keep, send):
    count = lax.axis_size("seq")
    bits = bits_of(count)
    total = (keep.astype(f32) + exchange(send, "seq", bits[0]).astype(f32)).astype(bf16)
    half = total.shape[0] // count
    total = total.reshape((count // 2, 2, half) + total.shape[1:])
    results = []
    for part, order in ((0, bits[1:]), (1, bits[:0:-1])):
        pieces = {2 * k: total[k, part] for k in range(count // 2)}
        for bit in order:
            arriving = {k ^ bit: exchange(v, "seq", bit) for k, v in pieces.items() if k & bit}
            pieces = {
                k: (v.astype(f32) + arriving[k].astype(f32)).astype(bf16)
                for k, v in pieces.items()
                if not k & bit
            }
        results.append(pieces[0])
    return jnp.concatenate(results, axis=0)


def sum_relative(value):
    count = lax.axis_size("seq")
    bits = bits_of(count)
    shape = value.shape
    split = value.reshape((shape[0],) + (2,) * len(bits) + (-1,))
    axis_of = {bits[0]: 1}
    for place, bit in enumerate(bits[:0:-1]):
        axis_of[bit] = 2 + place
    for bit in bits:
        split = split + jnp.flip(exchange(split, "seq", bit), axis_of[bit])
    return split.reshape(shape)


def sum_all(value):
    for axis in ("seq", "batch"):
        for bit in bits_of(lax.axis_size(axis)):
            value = value + exchange(value, axis, bit)
    return value


def step_values(raw):
    small = jnp.exp(-jnp.abs(raw))
    step = jnp.maximum(raw, 0.0) + jnp.log1p(small)
    sig = jnp.where(raw >= 0, 1.0, small) / (1.0 + small)
    tiny = raw < -20.0
    log_step = jnp.where(tiny, raw, jnp.log(step))
    ratio = jnp.where(tiny, 1.0, sig / step)
    return step, sig, log_step, ratio


def spread_heads(value, heads, size):
    rows = value.shape[0]
    return jnp.concatenate(
        [jnp.broadcast_to(value[:, h : h + 1], (rows, size)) for h in range(heads)], axis=1
    )


def sum_heads(value, heads, size):
    width = value.shape[1]
    row = lax.broadcasted_iota(jnp.int32, (width, LANES), 0) // size
    lane = lax.broadcasted_iota(jnp.int32, (width, LANES), 1)
    ones = (row == lane).astype(f32)
    return jnp.dot(value, ones, precision=highest, preferred_element_type=f32)


def order_masks(length):
    row = lax.broadcasted_iota(jnp.int32, (length, length), 0)
    column = lax.broadcasted_iota(jnp.int32, (length, length), 1)
    return row, column


def dot_nt(a, b):
    return lax.dot_general(a, b, (((1,), (1,)), ((), ())), preferred_element_type=f32)


def dot_tn(a, b):
    return lax.dot_general(a, b, (((0,), (0,)), ((), ())), preferred_element_type=f32)


def mixed(padded, conv_w, conv_b):
    taps = conv_w.shape[0]
    total = conv_b
    for k in range(taps):
        start = HALO - (taps - 1) + k
        total = total + conv_w[k : k + 1] * padded[start : start + GROUP]
    return total


def forward_kernel(
    heads, size, states, place_ref, normed_ref, w_ref, conv_w_ref, conv_b_ref, step_ref, rows_ref,
    conv_in_ref, gate_ref, slab_ref, ssd_ref, start_ref, scaled_ref, state, padded,
):
    width = heads * size
    conv_cols = width + 2 * states

    @pl.when(pl.program_id(0) == 0)
    def _():
        state[...] = jnp.zeros_like(state)
        padded[0:HALO] = jnp.zeros_like(padded[0:HALO])

    projected = jnp.dot(normed_ref[...], w_ref[...], preferred_element_type=f32)
    gate = projected[:, :width]
    conv_in = projected[:, width : width + conv_cols].astype(bf16)
    raw = projected[:, width + conv_cols :]
    padded[HALO : HALO + GROUP] = conv_in.astype(f32)
    pre = mixed(padded, conv_w_ref[...], conv_b_ref[...])
    padded[0:HALO] = padded[GROUP : GROUP + HALO]
    active = (pre / (1.0 + jnp.exp(-pre))).astype(bf16)
    signal = active[:, :width]
    entry = active[:, width : width + states]
    readout = active[:, width + states :]
    signal_wide = signal.astype(f32)

    step, _, log_step, _ = step_values(raw + step_ref[0:1])
    decay = step * step_ref[1:2]
    row, column = order_masks(GROUP)
    running = jnp.dot(
        (row >= column).astype(f32), decay, precision=highest, preferred_element_type=f32
    )
    later = running - log_step
    total = running[GROUP - 1 : GROUP]
    later_rows = later.T
    scores = dot_nt(readout, entry)
    start = state[...]
    start_ref[0] = start
    carried = jnp.dot(readout, start.astype(bf16), preferred_element_type=f32)
    carried = carried * spread_heads(jnp.exp(running), heads, size)
    within = []
    for h in range(heads):
        spread = running[:, h : h + 1] - later_rows[h : h + 1, :]
        kernel = jnp.exp(jnp.where(row >= column, spread, -1e30))
        weights = (scores * kernel).astype(bf16)
        within.append(
            jnp.dot(weights, signal[:, h * size : (h + 1) * size], preferred_element_type=f32)
        )
    ssd = jnp.concatenate(within, axis=1) + carried + rows_ref[0:1] * signal_wide
    tail = (signal_wide * spread_heads(jnp.exp(total - later), heads, size)).astype(bf16)
    state[...] = start * spread_heads(jnp.exp(total), heads, size) + dot_tn(entry, tail)

    gated = ssd * (gate / (1.0 + jnp.exp(-gate)))
    square = jnp.sum(gated * gated, axis=1, keepdims=True)
    lane = lax.broadcasted_iota(jnp.int32, raw.shape, 1)
    conv_in_ref[...] = conv_in
    gate_ref[...] = gate
    slab_ref[...] = jnp.where(lane == LANES - 1, square, raw)
    ssd_ref[...] = ssd
    scaled_ref[...] = (gated * rows_ref[1:2]).astype(bf16)


def backward_kernel(
    heads, size, states, place_ref, conv_in_ref, before_ref, gate_ref, slab_ref, ssd_ref, start_ref,
    grad_ref, norm_ref, conv_w_ref, conv_b_ref, step_ref, rows_ref,
    out_ref, normed_ref, gain_ref, skip_ref, conv_wg_ref, conv_bg_ref, small_ref,
    state, padded, pre_grads,
):
    width = heads * size
    taps = conv_w_ref.shape[0]
    turn = pl.program_id(0)
    block = pl.num_programs(0) - 1 - turn

    @pl.when(turn == 0)
    def _():
        state[...] = jnp.zeros_like(state)
        pre_grads[GROUP : GROUP + HALO] = jnp.zeros_like(pre_grads[0:HALO])
        gain_ref[...] = jnp.zeros_like(gain_ref)
        skip_ref[...] = jnp.zeros_like(skip_ref)
        conv_wg_ref[...] = jnp.zeros_like(conv_wg_ref)
        conv_bg_ref[...] = jnp.zeros_like(conv_bg_ref)
        small_ref[...] = jnp.zeros_like(small_ref)

    gate, ssd, out_grad = gate_ref[...], ssd_ref[...], grad_ref[...]
    scale, slope = norm_ref[:, 0:1], norm_ref[:, 1:2]
    gate_sig = 1.0 / (1.0 + jnp.exp(-gate))
    gate_act = gate * gate_sig
    gated = ssd * gate_act
    unit = gated * scale
    gain = rows_ref[1:2]
    normed_ref[...] = (unit * gain).astype(bf16)
    gain_ref[...] += jnp.sum(out_grad * unit, axis=0, keepdims=True)
    gated_grad = out_grad * gain * scale - gated * slope
    ssd_grad = gated_grad * gate_act
    gate_grad = gated_grad * ssd * (gate_sig * (1.0 + gate * (1.0 - gate_sig)))

    previous = before_ref[...].astype(f32)[16 - HALO :]
    padded[0:HALO] = jnp.where(block > 0, previous, 0.0)
    padded[HALO : HALO + GROUP] = conv_in_ref[...].astype(f32)
    conv_w = conv_w_ref[...]
    pre = mixed(padded, conv_w, conv_b_ref[...])
    pre_sig = 1.0 / (1.0 + jnp.exp(-pre))
    active = (pre * pre_sig).astype(bf16)
    signal = active[:, :width]
    entry = active[:, width : width + states]
    readout = active[:, width + states :]
    signal_wide = signal.astype(f32)

    raw = slab_ref[...]
    lane = lax.broadcasted_iota(jnp.int32, raw.shape, 1)
    raw = jnp.where(lane < heads, raw, 0.0) + step_ref[0:1]
    step, sig, log_step, ratio = step_values(raw)
    decay = step * step_ref[1:2]
    row, column = order_masks(GROUP)
    running = jnp.dot(
        (row >= column).astype(f32), decay, precision=highest, preferred_element_type=f32
    )
    later = running - log_step
    total = running[GROUP - 1 : GROUP]
    running_rows = running.T

    start = start_ref[0]
    end_grad = state[...]
    start_low, end_low, grad_low = start.astype(bf16), end_grad.astype(bf16), ssd_grad.astype(bf16)
    scores = dot_nt(entry, readout)
    score_grad = jnp.zeros_like(scores)
    within = []
    for h in range(heads):
        part = slice(h * size, (h + 1) * size)
        spread = running_rows[h : h + 1, :] - later[:, h : h + 1]
        kernel = jnp.exp(jnp.where(column >= row, spread, -1e30))
        weights = (scores * kernel).astype(bf16)
        within.append(jnp.dot(weights, grad_low[:, part], preferred_element_type=f32))
        score_grad = score_grad + dot_nt(signal[:, part], grad_low[:, part]) * kernel
    tail_wide = spread_heads(jnp.exp(total - later), heads, size)
    tail_grad = tail_wide * jnp.dot(entry, end_low, preferred_element_type=f32)
    signal_grad = jnp.concatenate(within, axis=1) + tail_grad
    score_low = score_grad.astype(bf16)
    tail = (signal_wide * tail_wide).astype(bf16)
    head_grad = (ssd_grad * spread_heads(jnp.exp(running), heads, size)).astype(bf16)
    entry_grad = jnp.dot(score_low, readout, preferred_element_type=f32) + dot_nt(tail, end_low)
    readout_grad = dot_tn(score_low, entry) + dot_nt(head_grad, start_low)
    total_wide = spread_heads(jnp.exp(total), heads, size)
    state[...] = end_grad * total_wide + dot_tn(readout, head_grad)

    skip = rows_ref[0:1]
    column_part = sum_heads(signal_wide * signal_grad, heads, size)
    row_part = sum_heads(grad_low.astype(f32) * (ssd - skip * signal_wide), heads, size)
    end_part = jnp.sum(signal_wide * tail_grad, axis=0, keepdims=True) + total_wide * jnp.sum(
        start * end_grad, axis=0, keepdims=True
    )
    end_part = sum_heads(jnp.broadcast_to(end_part, (8, width)), heads, size)[0:1]
    decay_grad = (
        jnp.dot(
            (column >= row).astype(f32),
            row_part - column_part,
            precision=highest,
            preferred_element_type=f32,
        )
        + end_part
    )
    raw_grad = column_part * ratio + decay_grad * step_ref[1:2] * sig
    raw_grad = jnp.where(lane < heads, raw_grad, 0.0)
    skip_ref[...] += jnp.sum(ssd_grad * signal_wide, axis=0, keepdims=True)
    small_ref[0:1] += jnp.sum(raw_grad, axis=0, keepdims=True)
    small_ref[1:2] += jnp.sum(decay_grad * decay, axis=0, keepdims=True)

    active_grad = jnp.concatenate([signal_grad + skip * ssd_grad, entry_grad, readout_grad], axis=1)
    pre_grad = active_grad * (pre_sig * (1.0 + pre * (1.0 - pre_sig)))
    pre_grads[0:GROUP] = pre_grad
    conv_grad = jnp.zeros_like(pre_grad)
    for k in range(taps):
        ahead = taps - 1 - k
        conv_grad = conv_grad + conv_w[k : k + 1] * pre_grads[ahead : ahead + GROUP]
        first = HALO - ahead
        conv_wg_ref[k : k + 1] += jnp.sum(
            pre_grad * padded[first : first + GROUP], axis=0, keepdims=True
        )
    conv_bg_ref[...] += jnp.sum(pre_grad, axis=0, keepdims=True)
    pre_grads[GROUP : GROUP + HALO] = pre_grads[0:HALO]
    out_ref[...] = jnp.concatenate([gate_grad, conv_grad, raw_grad], axis=1).astype(bf16)


def row_block(place_ref, block, per_device, count):
    relative = (block // per_device) ^ place_ref[0]
    order = (relative & 1) * (count // 2) + (relative >> 1)
    return order * per_device + block % per_device


def fixed(shape):
    return pl.BlockSpec(shape, lambda turn, place: (0,) * len(shape), pipeline_mode=pl.Buffered(1))


def run_forward(place, normed, w_cols, conv_w, conv_b, step_rows, rows, heads, size, states, count):
    tokens, dim = normed.shape
    width = heads * size
    conv_cols = conv_w.shape[1]
    blocks = tokens // GROUP
    per_device = blocks // count

    def moving(columns):
        return pl.BlockSpec(
            (GROUP, columns), lambda turn, place: (row_block(place, turn, per_device, count), 0)
        )

    flops = tokens * (2 * dim * w_cols.shape[1] + 2 * width * (GROUP + 2 * states))
    return pl.pallas_call(
        functools.partial(forward_kernel, heads, size, states),
        grid_spec=pltpu.PrefetchScalarGridSpec(
            num_scalar_prefetch=1,
            grid=(blocks,),
            in_specs=[
                moving(dim),
                fixed(w_cols.shape),
                fixed(conv_w.shape),
                fixed(conv_b.shape),
                fixed(step_rows.shape),
                fixed(rows.shape),
            ],
            out_specs=[
                moving(conv_cols),
                moving(width),
                moving(LANES),
                moving(width),
                pl.BlockSpec((1, states, width), lambda turn, place: (turn, 0, 0)),
                moving(width),
            ],
            scratch_shapes=[
                pltpu.VMEM((states, width), f32),
                pltpu.VMEM((HALO + GROUP, conv_cols), f32),
            ],
        ),
        out_shape=[
            jax.ShapeDtypeStruct((tokens, conv_cols), bf16),
            jax.ShapeDtypeStruct((tokens, width), f32),
            jax.ShapeDtypeStruct((tokens, LANES), f32),
            jax.ShapeDtypeStruct((tokens, width), f32),
            jax.ShapeDtypeStruct((blocks, states, width), f32),
            jax.ShapeDtypeStruct((tokens, width), bf16),
        ],
        compiler_params=pltpu.CompilerParams(vmem_limit_bytes=48 * 2**20),
        cost_estimate=pl.CostEstimate(
            flops=flops, bytes_accessed=tokens * (2 * dim + 12 * width), transcendentals=0
        ),
        name="forward_blocks",
    )(place, normed, w_cols, conv_w, conv_b, step_rows, rows)


def run_backward(
    place, conv_in, gate, slab, ssd, starts, out_grad, norms, conv_w, conv_b, step_rows, rows,
    heads, size, states, count,
):
    tokens, width = gate.shape
    conv_cols = conv_w.shape[1]
    blocks = tokens // GROUP
    per_device = blocks // count
    ratio = GROUP // 16

    def moving(columns):
        return pl.BlockSpec(
            (GROUP, columns),
            lambda turn, place: (row_block(place, blocks - 1 - turn, per_device, count), 0),
        )

    def before(turn, place):
        earlier = jnp.maximum(blocks - 2 - turn, 0)
        return (row_block(place, earlier, per_device, count) * ratio + ratio - 1, 0)

    out_cols = width + conv_cols + LANES
    return pl.pallas_call(
        functools.partial(backward_kernel, heads, size, states),
        grid_spec=pltpu.PrefetchScalarGridSpec(
            num_scalar_prefetch=1,
            grid=(blocks,),
            in_specs=[
                moving(conv_cols),
                pl.BlockSpec((16, conv_cols), before),
                moving(width),
                moving(LANES),
                moving(width),
                pl.BlockSpec((1, states, width), lambda turn, place: (blocks - 1 - turn, 0, 0)),
                moving(width),
                moving(2),
                fixed(conv_w.shape),
                fixed(conv_b.shape),
                fixed(step_rows.shape),
                fixed(rows.shape),
            ],
            out_specs=[
                moving(out_cols),
                moving(width),
                fixed((1, width)),
                fixed((1, width)),
                fixed(conv_w.shape),
                fixed(conv_b.shape),
                fixed((8, LANES)),
            ],
            scratch_shapes=[
                pltpu.VMEM((states, width), f32),
                pltpu.VMEM((HALO + GROUP, conv_cols), f32),
                pltpu.VMEM((GROUP + HALO, conv_cols), f32),
            ],
        ),
        out_shape=[
            jax.ShapeDtypeStruct((tokens, out_cols), bf16),
            jax.ShapeDtypeStruct((tokens, width), bf16),
            jax.ShapeDtypeStruct((1, width), f32),
            jax.ShapeDtypeStruct((1, width), f32),
            jax.ShapeDtypeStruct(conv_w.shape, f32),
            jax.ShapeDtypeStruct(conv_b.shape, f32),
            jax.ShapeDtypeStruct((8, LANES), f32),
        ],
        compiler_params=pltpu.CompilerParams(vmem_limit_bytes=48 * 2**20),
        cost_estimate=pl.CostEstimate(
            flops=tokens * 2 * width * (2 * GROUP + 6 * states),
            bytes_accessed=tokens * 20 * width,
            transcendentals=0,
        ),
        name="backward_blocks",
    )(
        place, conv_in, conv_in, gate, slab, ssd, starts, out_grad, norms, conv_w, conv_b,
        step_rows, rows,
    )


def assemble_kernel(width, shared, lasting, place_ref, pieces_ref, out_ref):
    count = pieces_ref.shape[0]
    inner = count * width
    sums = jnp.zeros((pieces_ref.shape[1], shared + LANES), f32)
    for device in range(count):
        piece = pieces_ref[place_ref[0] ^ device].astype(f32)
        out_ref[:, device * width : (device + 1) * width] = piece[:, :width]
        out_ref[:, inner + device * width : inner + (device + 1) * width] = piece[
            :, width : 2 * width
        ]
        sums = sums + piece[:, 2 * width :]
    out_ref[:, 2 * inner :] = sums[:, : shared + lasting]


def assemble(place, pieces, width, shared, lasting):
    count, rows, columns = pieces.shape
    tile = 64
    out_cols = 2 * count * width + shared + lasting
    return pl.pallas_call(
        functools.partial(assemble_kernel, width, shared, lasting),
        grid_spec=pltpu.PrefetchScalarGridSpec(
            num_scalar_prefetch=1,
            grid=(rows // tile,),
            in_specs=[pl.BlockSpec((count, tile, columns), lambda turn, place: (0, turn, 0))],
            out_specs=pl.BlockSpec((tile, out_cols), lambda turn, place: (turn, 0)),
        ),
        out_shape=jax.ShapeDtypeStruct((rows, out_cols), f32),
        compiler_params=pltpu.CompilerParams(vmem_limit_bytes=32 * 2**20),
        cost_estimate=pl.CostEstimate(
            flops=0, bytes_accessed=rows * (2 * count * columns + 4 * out_cols), transcendentals=0
        ),
        name="assemble_in_weight_grad",
    )(place, pieces)


def body(
    tokens,
    norm_gain,
    in_weight,
    conv_weight,
    conv_bias,
    dt_bias,
    decay_log,
    skip_scale,
    gate_gain,
    out_weight,
    cotangent,
):
    count, planes = lax.axis_size("seq"), lax.axis_size("batch")
    mine, plane = lax.axis_index("seq"), lax.axis_index("batch")
    place = mine.astype(jnp.int32).reshape(1)
    dim = tokens.shape[2]
    inner, all_heads, conv_all = gate_gain.shape[0], dt_bias.shape[0], conv_bias.shape[0]
    size, states = inner // all_heads, (conv_all - inner) // 2
    heads, width = all_heads // count, inner // count
    shared = 2 * states
    tok_rows = tokens.shape[1]
    owned_in, owned_out = in_weight.shape[0], out_weight.shape[0]
    per_plane = owned_out // width

    def own(vector, per):
        return lax.dynamic_slice_in_dim(vector, mine * per, per, vector.ndim - 1)

    def own_conv(array):
        return jnp.concatenate([own(array[..., :inner], width), array[..., inner:]], axis=-1)

    def lane_row(vector):
        return jnp.pad(vector, (0, LANES - vector.shape[0]))[None]

    tokens_row = tokens[0].astype(f32)
    inverse = lax.rsqrt(jnp.mean(tokens_row * tokens_row, axis=-1, keepdims=True) + epsilon)
    normed_own = (tokens_row * inverse * norm_gain).astype(bf16)
    w_own = jnp.concatenate(
        [
            own(in_weight[:, :inner], width),
            own_conv(in_weight[:, inner : inner + conv_all]),
            jnp.pad(own(in_weight[:, inner + conv_all :], heads), ((0, 0), (0, LANES - heads))),
        ],
        axis=1,
    )
    w_cols = lax.all_gather(w_own, "batch", axis=0, tiled=True)
    normed = gather_tokens(normed_own)
    out_own = lax.dynamic_slice_in_dim(out_weight, (mine % per_plane) * width, width, 0)
    out_all = lax.all_gather(out_own, "batch", axis=0, tiled=False)
    out_rows = lax.dynamic_index_in_dim(out_all, mine // per_plane, 0, keepdims=False)
    cot = gather_tokens(cotangent[0])

    conv_w, conv_b = own_conv(conv_weight), own_conv(conv_bias)[None]
    step_rows = jnp.concatenate(
        [
            lane_row(own(dt_bias, heads)),
            lane_row(-jnp.exp(own(decay_log, heads))),
            jnp.zeros((6, LANES), f32),
        ],
        axis=0,
    )
    gain_own = own(gate_gain, width)
    rows = jnp.concatenate(
        [
            jnp.repeat(own(skip_scale, heads), size)[None],
            gain_own[None],
            jnp.zeros((6, width), f32),
        ],
        axis=0,
    )

    conv_in, gate, slab, ssd, starts, scaled = run_forward(
        place, normed, w_cols, conv_w, conv_b, step_rows, rows, heads, size, states, count
    )

    middle = scaled.shape[0] // 2
    out_grad = jnp.einsum("td,ed->te", cot, out_rows, preferred_element_type=f32)
    sums = sum_relative(
        jnp.stack([slab[:, LANES - 1], jnp.sum(out_grad * scaled.astype(f32), axis=1)])
    )
    scale = lax.rsqrt(sums[0] / inner + epsilon)
    norms = jnp.stack([scale, scale * scale * scale * sums[1] / inner], axis=1)

    def out_part(part):
        return jnp.dot(part, out_rows, preferred_element_type=f32).astype(bf16)

    mixed_out = scatter_sum(out_part(scaled[:middle]), out_part(scaled[middle:]))
    block_out = (tokens_row + scale[:tok_rows, None] * mixed_out.astype(f32)).astype(bf16)

    proj_grad, normed_out, gain_term, skip_term, conv_w_term, conv_b_term, small_term = (
        run_backward(
            place, conv_in, gate, slab, ssd, starts, out_grad, norms, conv_w, conv_b, step_rows,
            rows, heads, size, states, count,
        )
    )

    def back_part(part):
        return jnp.einsum("tf,df->td", part, w_cols, preferred_element_type=f32).astype(bf16)

    normed_grad = scatter_sum(back_part(proj_grad[:middle]), back_part(proj_grad[middle:]))
    normed_grad = normed_grad.astype(f32)
    cot_row = cotangent[0].astype(f32)
    gained = norm_gain * normed_grad
    slope = inverse * inverse * inverse * jnp.mean(gained * tokens_row, axis=-1, keepdims=True)
    input_grad = cot_row + inverse * gained - tokens_row * slope

    out_term = jnp.einsum("te,td->ed", normed_out, cot, preferred_element_type=f32)
    out_sum = lax.psum(out_term.astype(bf16), "batch")
    first, second = gather_relative(out_sum)
    out_sums = jnp.stack([jnp.concatenate([first[k], second[k]]) for k in range(count)])
    out_weight_grad = jnp.concatenate(
        [
            lax.dynamic_index_in_dim(out_sums, (plane * per_plane + k) ^ mine, 0, keepdims=False)
            for k in range(per_plane)
        ]
    ).astype(f32)

    in_term = jnp.einsum("td,tf->df", normed, proj_grad, preferred_element_type=f32)
    norm_gain_term = jnp.sum(in_term * w_cols.astype(f32), axis=1) / norm_gain
    conv_end = 2 * width + shared
    step_slab = lax.dynamic_update_slice_in_dim(
        jnp.zeros((dim, LANES), bf16),
        in_term[:, conv_end : conv_end + heads].astype(bf16),
        mine * heads,
        1,
    )
    in_low = jnp.concatenate([in_term[:, :conv_end].astype(bf16), step_slab], axis=1)
    in_sum = lax.psum_scatter(in_low, "batch", scatter_dimension=0, tiled=True)
    first, second = gather_relative(in_sum)
    in_sums = jnp.stack([jnp.concatenate([first[k], second[k]]) for k in range(count)])
    in_weight_grad = assemble(place, in_sums, width, shared, all_heads)

    def among_heads(vector, per, total):
        return lax.dynamic_update_slice_in_dim(jnp.zeros((total,), f32), vector, mine * per, 0)

    def among_conv(array):
        wide = jnp.zeros((array.shape[0], inner), f32)
        wide = lax.dynamic_update_slice_in_dim(wide, array[:, :width], mine * width, 1)
        return jnp.concatenate([wide, array[:, width:]], axis=1).reshape(-1)

    skip_heads = jnp.sum(skip_term.reshape(heads, size), axis=1)
    terms = [
        norm_gain_term,
        among_conv(conv_w_term),
        among_conv(conv_b_term),
        among_heads(small_term[0, :heads], heads, all_heads),
        among_heads(small_term[1, :heads], heads, all_heads),
        among_heads(skip_heads, heads, all_heads),
        among_heads(gain_term[0], width, inner),
    ]
    vector = jnp.concatenate(terms)
    padding = -vector.shape[0] % (8 * LANES)
    vector = sum_all(jnp.pad(vector, (0, padding)).reshape(-1, LANES)).reshape(-1)
    parts, offset = [], 0
    for term in terms:
        parts.append(vector[offset : offset + term.shape[0]])
        offset += term.shape[0]
    return (
        block_out[None],
        input_grad[None],
        parts[0],
        in_weight_grad,
        parts[1].reshape(conv_weight.shape),
        parts[2],
        parts[3],
        parts[4],
        parts[5],
        parts[6],
        out_weight_grad,
    )


def solution(mesh):
    placed = (
        P("batch", "seq", None),
        P(),
        P("batch", None),
        P(),
        P(),
        P(),
        P(),
        P(),
        P(),
        P("batch", None),
        P("batch", "seq", None),
    )
    return jax.shard_map(
        body,
        mesh=mesh,
        in_specs=placed,
        out_specs=(
            P("batch", "seq", None),
            P("batch", "seq", None),
            P(),
            P("batch", None),
            P(),
            P(),
            P(),
            P(),
            P(),
            P(),
            P("batch", None),
        ),
        check_vma=False,
    )
```

```python
import functools

import jax
import jax.numpy as jnp
from jax import lax
from jax.experimental import pallas as pl
from jax.experimental.pallas import tpu as pltpu
from jax.sharding import PartitionSpec as P

GROUP = 256
LANES = 128
HALO = 8
epsilon = 1e-05
highest = lax.Precision.HIGHEST
f32 = jnp.float32
bf16 = jnp.bfloat16


def exchange(value, axis, distance):
    count = lax.axis_size(axis)
    return lax.ppermute(value, axis, [(source, source ^ distance) for source in range(count)])


def bits_of(count):
    return [1 << k for k in range(count.bit_length() - 1)]


def gather_relative(value):
    bits = bits_of(lax.axis_size("seq"))
    near, far = bits[:1], bits[1:]
    half = value.shape[0] // 2
    held = []
    for part, order in ((value[:half], far + near), (value[half:], far[::-1] + near)):
        pieces = {0: part}
        for bit in order:
            for index, piece in list(pieces.items()):
                pieces[index | bit] = exchange(piece, "seq", bit)
        held.append(pieces)
    return held


def placed_order(count):
    return [2 * k for k in range(count // 2)] + [2 * k + 1 for k in range(count // 2)]


def gather_tokens(value):
    first, second = gather_relative(value)
    pieces = []
    for index in placed_order(lax.axis_size("seq")):
        pieces += [first[index], second[index]]
    return jnp.concatenate(pieces, axis=0)


def scatter_sum(keep, send):
    count = lax.axis_size("seq")
    bits = bits_of(count)
    total = (keep.astype(f32) + exchange(send, "seq", bits[0]).astype(f32)).astype(bf16)
    half = total.shape[0] // count
    total = total.reshape((count // 2, 2, half) + total.shape[1:])
    results = []
    for part, order in ((0, bits[1:]), (1, bits[:0:-1])):
        pieces = {2 * k: total[k, part] for k in range(count // 2)}
        for bit in order:
            arriving = {k ^ bit: exchange(v, "seq", bit) for k, v in pieces.items() if k & bit}
            pieces = {
                k: (v.astype(f32) + arriving[k].astype(f32)).astype(bf16)
                for k, v in pieces.items()
                if not k & bit
            }
        results.append(pieces[0])
    return jnp.concatenate(results, axis=0)


def sum_seq(value):
    for bit in bits_of(lax.axis_size("seq")):
        value = value + exchange(value, "seq", bit)
    return value


def plane_pairs(ahead, back=False):
    planes, count = lax.axis_size("batch"), lax.axis_size("seq")
    per = count // planes
    pairs = []
    for owner in range(planes):
        for piece in range(planes):
            for k in range(per):
                holder = owner * count + piece * per + k
                user = (piece + ahead) % planes * count + owner * per + k
                pairs.append((user, holder) if back else (holder, user))
    return pairs


def rows_from_owner(out_weight, width):
    planes, count = lax.axis_size("batch"), lax.axis_size("seq")
    per, size = count // planes, width // planes
    plane, mine = lax.axis_index("batch"), lax.axis_index("seq")
    piece = lax.dynamic_slice_in_dim(out_weight, mine % per * width + mine // per * size, size, 0)
    arriving = [
        lax.ppermute(piece, ("batch", "seq"), plane_pairs(ahead)) for ahead in range(planes)
    ]
    doubled = jnp.concatenate(arriving[::-1] * 2, axis=0)
    return lax.dynamic_slice_in_dim(doubled, (planes - 1 - plane) * size, width, 0)


def rows_to_owner(value):
    planes = lax.axis_size("batch")
    size = value.shape[0] // planes
    plane = lax.axis_index("batch")
    total = 0.0
    for ahead in range(planes):
        piece = lax.dynamic_slice_in_dim(value, (plane - ahead) % planes * size, size, 0)
        arriving = lax.ppermute(piece, ("batch", "seq"), plane_pairs(ahead, back=True))
        total = total + arriving.astype(f32)
    return total.astype(bf16)


def gather_doubling(value):
    held = value[None]
    for bit in bits_of(lax.axis_size("seq"))[1:] + [1]:
        held = jnp.concatenate([held, exchange(held, "seq", bit)], axis=0)
    return held


def sum_all(value):
    for axis in ("seq", "batch"):
        for bit in bits_of(lax.axis_size(axis)):
            value = value + exchange(value, axis, bit)
    return value


def step_values(raw):
    small = jnp.exp(-jnp.abs(raw))
    step = jnp.maximum(raw, 0.0) + jnp.log1p(small)
    sig = jnp.where(raw >= 0, 1.0, small) / (1.0 + small)
    tiny = raw < -20.0
    log_step = jnp.where(tiny, raw, jnp.log(step))
    ratio = jnp.where(tiny, 1.0, sig / step)
    return step, sig, log_step, ratio


def spread_heads(value, heads, size):
    rows = value.shape[0]
    return jnp.concatenate(
        [jnp.broadcast_to(value[:, h : h + 1], (rows, size)) for h in range(heads)], axis=1
    )


def sum_heads(value, heads, size):
    width = value.shape[1]
    row = lax.broadcasted_iota(jnp.int32, (width, LANES), 0) // size
    lane = lax.broadcasted_iota(jnp.int32, (width, LANES), 1)
    ones = (row == lane).astype(f32)
    return jnp.dot(value, ones, precision=highest, preferred_element_type=f32)


def order_masks(length):
    row = lax.broadcasted_iota(jnp.int32, (length, length), 0)
    column = lax.broadcasted_iota(jnp.int32, (length, length), 1)
    return row, column


def dot_nt(a, b):
    return lax.dot_general(a, b, (((1,), (1,)), ((), ())), preferred_element_type=f32)


def dot_tn(a, b):
    return lax.dot_general(a, b, (((0,), (0,)), ((), ())), preferred_element_type=f32)


def mixed(padded, conv_w, conv_b):
    taps = conv_w.shape[0]
    total = conv_b
    for k in range(taps):
        start = HALO - (taps - 1) + k
        total = total + conv_w[k : k + 1] * padded[start : start + GROUP]
    return total


def forward_kernel(
    heads, size, states, place_ref, normed_ref, w_ref, conv_w_ref, conv_b_ref, step_ref, rows_ref,
    conv_in_ref, gate_ref, slab_ref, ssd_ref, start_ref, scaled_ref, state, padded,
):
    width = heads * size
    conv_cols = width + 2 * states

    @pl.when(pl.program_id(0) == 0)
    def _():
        state[...] = jnp.zeros_like(state)
        padded[0:HALO] = jnp.zeros_like(padded[0:HALO])

    projected = jnp.dot(normed_ref[...], w_ref[...], preferred_element_type=f32)
    gate = projected[:, :width]
    conv_in = projected[:, width : width + conv_cols].astype(bf16)
    raw = projected[:, width + conv_cols :]
    padded[HALO : HALO + GROUP] = conv_in.astype(f32)
    pre = mixed(padded, conv_w_ref[...], conv_b_ref[...])
    padded[0:HALO] = padded[GROUP : GROUP + HALO]
    active = (pre / (1.0 + jnp.exp(-pre))).astype(bf16)
    signal = active[:, :width]
    entry = active[:, width : width + states]
    readout = active[:, width + states :]
    signal_wide = signal.astype(f32)

    step, _, log_step, _ = step_values(raw + step_ref[0:1])
    decay = step * step_ref[1:2]
    row, column = order_masks(GROUP)
    running = jnp.dot(
        (row >= column).astype(f32), decay, precision=highest, preferred_element_type=f32
    )
    later = running - log_step
    total = running[GROUP - 1 : GROUP]
    later_rows = later.T
    scores = dot_nt(readout, entry)
    start = state[...]
    start_ref[0] = start
    carried = jnp.dot(readout, start.astype(bf16), preferred_element_type=f32)
    carried = carried * spread_heads(jnp.exp(running), heads, size)
    within = []
    for h in range(heads):
        spread = running[:, h : h + 1] - later_rows[h : h + 1, :]
        kernel = jnp.exp(jnp.where(row >= column, spread, -1e30))
        weights = (scores * kernel).astype(bf16)
        within.append(
            jnp.dot(weights, signal[:, h * size : (h + 1) * size], preferred_element_type=f32)
        )
    ssd = jnp.concatenate(within, axis=1) + carried + rows_ref[0:1] * signal_wide
    tail = (signal_wide * spread_heads(jnp.exp(total - later), heads, size)).astype(bf16)
    state[...] = start * spread_heads(jnp.exp(total), heads, size) + dot_tn(entry, tail)

    gated = ssd * (gate / (1.0 + jnp.exp(-gate)))
    square = jnp.sum(gated * gated, axis=1, keepdims=True)
    lane = lax.broadcasted_iota(jnp.int32, raw.shape, 1)
    conv_in_ref[...] = conv_in
    gate_ref[...] = gate
    slab_ref[...] = jnp.where(lane == LANES - 1, square, raw)
    ssd_ref[...] = ssd
    scaled_ref[...] = (gated * rows_ref[1:2]).astype(bf16)


def backward_kernel(
    heads, size, states, place_ref, conv_in_ref, before_ref, gate_ref, slab_ref, ssd_ref, start_ref,
    grad_ref, norm_ref, conv_w_ref, conv_b_ref, step_ref, rows_ref,
    out_ref, gain_ref, skip_ref, conv_wg_ref, conv_bg_ref, small_ref,
    state, padded, pre_grads,
):
    width = heads * size
    taps = conv_w_ref.shape[0]
    turn = pl.program_id(0)
    block = pl.num_programs(0) - 1 - turn

    @pl.when(turn == 0)
    def _():
        state[...] = jnp.zeros_like(state)
        pre_grads[GROUP : GROUP + HALO] = jnp.zeros_like(pre_grads[0:HALO])
        gain_ref[...] = jnp.zeros_like(gain_ref)
        skip_ref[...] = jnp.zeros_like(skip_ref)
        conv_wg_ref[...] = jnp.zeros_like(conv_wg_ref)
        conv_bg_ref[...] = jnp.zeros_like(conv_bg_ref)
        small_ref[...] = jnp.zeros_like(small_ref)

    gate, ssd, out_grad = gate_ref[...], ssd_ref[...], grad_ref[...]
    scale, slope = norm_ref[:, 0:1], norm_ref[:, 1:2]
    gate_sig = 1.0 / (1.0 + jnp.exp(-gate))
    gate_act = gate * gate_sig
    gated = ssd * gate_act
    unit = gated * scale
    gain = rows_ref[1:2]
    gain_ref[...] += jnp.sum(out_grad * unit, axis=0, keepdims=True)
    gated_grad = out_grad * gain * scale - gated * slope
    ssd_grad = gated_grad * gate_act
    gate_grad = gated_grad * ssd * (gate_sig * (1.0 + gate * (1.0 - gate_sig)))

    previous = before_ref[...].astype(f32)[16 - HALO :]
    padded[0:HALO] = jnp.where(block > 0, previous, 0.0)
    padded[HALO : HALO + GROUP] = conv_in_ref[...].astype(f32)
    conv_w = conv_w_ref[...]
    pre = mixed(padded, conv_w, conv_b_ref[...])
    pre_sig = 1.0 / (1.0 + jnp.exp(-pre))
    active = (pre * pre_sig).astype(bf16)
    signal = active[:, :width]
    entry = active[:, width : width + states]
    readout = active[:, width + states :]
    signal_wide = signal.astype(f32)

    raw = slab_ref[...]
    lane = lax.broadcasted_iota(jnp.int32, raw.shape, 1)
    raw = jnp.where(lane < heads, raw, 0.0) + step_ref[0:1]
    step, sig, log_step, ratio = step_values(raw)
    decay = step * step_ref[1:2]
    row, column = order_masks(GROUP)
    running = jnp.dot(
        (row >= column).astype(f32), decay, precision=highest, preferred_element_type=f32
    )
    later = running - log_step
    total = running[GROUP - 1 : GROUP]
    running_rows = running.T

    start = start_ref[0]
    end_grad = state[...]
    start_low, end_low, grad_low = start.astype(bf16), end_grad.astype(bf16), ssd_grad.astype(bf16)
    scores = dot_nt(entry, readout)
    score_grad = jnp.zeros_like(scores)
    within = []
    for h in range(heads):
        part = slice(h * size, (h + 1) * size)
        spread = running_rows[h : h + 1, :] - later[:, h : h + 1]
        kernel = jnp.exp(jnp.where(column >= row, spread, -1e30))
        weights = (scores * kernel).astype(bf16)
        within.append(jnp.dot(weights, grad_low[:, part], preferred_element_type=f32))
        score_grad = score_grad + dot_nt(signal[:, part], grad_low[:, part]) * kernel
    tail_wide = spread_heads(jnp.exp(total - later), heads, size)
    tail_grad = tail_wide * jnp.dot(entry, end_low, preferred_element_type=f32)
    signal_grad = jnp.concatenate(within, axis=1) + tail_grad
    score_low = score_grad.astype(bf16)
    tail = (signal_wide * tail_wide).astype(bf16)
    head_grad = (ssd_grad * spread_heads(jnp.exp(running), heads, size)).astype(bf16)
    entry_grad = jnp.dot(score_low, readout, preferred_element_type=f32) + dot_nt(tail, end_low)
    readout_grad = dot_tn(score_low, entry) + dot_nt(head_grad, start_low)
    total_wide = spread_heads(jnp.exp(total), heads, size)
    state[...] = end_grad * total_wide + dot_tn(readout, head_grad)

    skip = rows_ref[0:1]
    column_part = sum_heads(signal_wide * signal_grad, heads, size)
    row_part = sum_heads(grad_low.astype(f32) * (ssd - skip * signal_wide), heads, size)
    end_part = jnp.sum(signal_wide * tail_grad, axis=0, keepdims=True) + total_wide * jnp.sum(
        start * end_grad, axis=0, keepdims=True
    )
    end_part = sum_heads(jnp.broadcast_to(end_part, (8, width)), heads, size)[0:1]
    decay_grad = (
        jnp.dot(
            (column >= row).astype(f32),
            row_part - column_part,
            precision=highest,
            preferred_element_type=f32,
        )
        + end_part
    )
    raw_grad = column_part * ratio + decay_grad * step_ref[1:2] * sig
    raw_grad = jnp.where(lane < heads, raw_grad, 0.0)
    skip_ref[...] += jnp.sum(ssd_grad * signal_wide, axis=0, keepdims=True)
    small_ref[0:1] += jnp.sum(raw_grad, axis=0, keepdims=True)
    small_ref[1:2] += jnp.sum(decay_grad * decay, axis=0, keepdims=True)

    active_grad = jnp.concatenate([signal_grad + skip * ssd_grad, entry_grad, readout_grad], axis=1)
    pre_grad = active_grad * (pre_sig * (1.0 + pre * (1.0 - pre_sig)))
    pre_grads[0:GROUP] = pre_grad
    conv_grad = jnp.zeros_like(pre_grad)
    for k in range(taps):
        ahead = taps - 1 - k
        conv_grad = conv_grad + conv_w[k : k + 1] * pre_grads[ahead : ahead + GROUP]
        first = HALO - ahead
        conv_wg_ref[k : k + 1] += jnp.sum(
            pre_grad * padded[first : first + GROUP], axis=0, keepdims=True
        )
    conv_bg_ref[...] += jnp.sum(pre_grad, axis=0, keepdims=True)
    pre_grads[GROUP : GROUP + HALO] = pre_grads[0:HALO]
    out_ref[...] = jnp.concatenate([gate_grad, conv_grad, raw_grad], axis=1).astype(bf16)


def row_block(place_ref, block, per_device, count):
    relative = (block // per_device) ^ place_ref[0]
    order = (relative & 1) * (count // 2) + (relative >> 1)
    return order * per_device + block % per_device


def time_estimate(microseconds, accessed):
    return pl.CostEstimate(
        flops=int(microseconds * 1.1e9), bytes_accessed=accessed, transcendentals=0
    )


def fixed(shape):
    return pl.BlockSpec(shape, lambda turn, place: (0,) * len(shape), pipeline_mode=pl.Buffered(1))


def run_forward(place, normed, w_cols, conv_w, conv_b, step_rows, rows, heads, size, states, count):
    tokens, dim = normed.shape
    width = heads * size
    conv_cols = conv_w.shape[1]
    blocks = tokens // GROUP
    per_device = blocks // count

    def moving(columns):
        return pl.BlockSpec((GROUP, columns), lambda turn, place: (turn, 0))

    return pl.pallas_call(
        functools.partial(forward_kernel, heads, size, states),
        grid_spec=pltpu.PrefetchScalarGridSpec(
            num_scalar_prefetch=1,
            grid=(blocks,),
            in_specs=[
                pl.BlockSpec(
                    (GROUP, dim),
                    lambda turn, place: (row_block(place, turn, per_device, count), 0),
                ),
                fixed(w_cols.shape),
                fixed(conv_w.shape),
                fixed(conv_b.shape),
                fixed(step_rows.shape),
                fixed(rows.shape),
            ],
            out_specs=[
                moving(conv_cols),
                moving(width),
                moving(LANES),
                moving(width),
                pl.BlockSpec((1, states, width), lambda turn, place: (turn, 0, 0)),
                moving(width),
            ],
            scratch_shapes=[
                pltpu.VMEM((states, width), f32),
                pltpu.VMEM((HALO + GROUP, conv_cols), f32),
            ],
        ),
        out_shape=[
            jax.ShapeDtypeStruct((tokens, conv_cols), bf16),
            jax.ShapeDtypeStruct((tokens, width), f32),
            jax.ShapeDtypeStruct((tokens, LANES), f32),
            jax.ShapeDtypeStruct((tokens, width), f32),
            jax.ShapeDtypeStruct((blocks, states, width), f32),
            jax.ShapeDtypeStruct((tokens, width), bf16),
        ],
        compiler_params=pltpu.CompilerParams(vmem_limit_bytes=48 * 2**20),
        cost_estimate=time_estimate(blocks * 3.4, tokens * (2 * dim + 12 * width)),
        name="forward_blocks",
    )(place, normed, w_cols, conv_w, conv_b, step_rows, rows)


def run_backward(
    place, conv_in, gate, slab, ssd, starts, out_grad, norms, conv_w, conv_b, step_rows, rows,
    heads, size, states, count,
):
    tokens, width = gate.shape
    conv_cols = conv_w.shape[1]
    blocks = tokens // GROUP
    per_device = blocks // count
    ratio = GROUP // 16

    def moving(columns):
        return pl.BlockSpec((GROUP, columns), lambda turn, place: (blocks - 1 - turn, 0))

    def before(turn, place):
        return (jnp.maximum(blocks - 2 - turn, 0) * ratio + ratio - 1, 0)

    out_cols = width + conv_cols + LANES
    return pl.pallas_call(
        functools.partial(backward_kernel, heads, size, states),
        grid_spec=pltpu.PrefetchScalarGridSpec(
            num_scalar_prefetch=1,
            grid=(blocks,),
            in_specs=[
                moving(conv_cols),
                pl.BlockSpec((16, conv_cols), before),
                moving(width),
                moving(LANES),
                moving(width),
                pl.BlockSpec((1, states, width), lambda turn, place: (blocks - 1 - turn, 0, 0)),
                moving(width),
                moving(2),
                fixed(conv_w.shape),
                fixed(conv_b.shape),
                fixed(step_rows.shape),
                fixed(rows.shape),
            ],
            out_specs=[
                pl.BlockSpec(
                    (GROUP, out_cols),
                    lambda turn, place: (
                        row_block(place, blocks - 1 - turn, per_device, count),
                        0,
                    ),
                ),
                fixed((1, width)),
                fixed((1, width)),
                fixed(conv_w.shape),
                fixed(conv_b.shape),
                fixed((8, LANES)),
            ],
            scratch_shapes=[
                pltpu.VMEM((states, width), f32),
                pltpu.VMEM((HALO + GROUP, conv_cols), f32),
                pltpu.VMEM((GROUP + HALO, conv_cols), f32),
            ],
        ),
        out_shape=[
            jax.ShapeDtypeStruct((tokens, out_cols), bf16),
            jax.ShapeDtypeStruct((1, width), f32),
            jax.ShapeDtypeStruct((1, width), f32),
            jax.ShapeDtypeStruct(conv_w.shape, f32),
            jax.ShapeDtypeStruct(conv_b.shape, f32),
            jax.ShapeDtypeStruct((8, LANES), f32),
        ],
        compiler_params=pltpu.CompilerParams(vmem_limit_bytes=48 * 2**20),
        cost_estimate=time_estimate(blocks * 5.2, tokens * 20 * width),
        name="backward_blocks",
    )(
        place, conv_in, conv_in, gate, slab, ssd, starts, out_grad, norms, conv_w, conv_b,
        step_rows, rows,
    )


def widen_kernel(place_ref, piece_ref, out_ref):
    out_ref[...] = piece_ref[0].astype(f32)


def assemble_out(place, pieces, per):
    count, size, dim = pieces.shape
    groups = count // per

    def source(turn, place):
        relative = (turn % groups * per + turn // groups) ^ place[0]
        return ((relative & 1) * (count // 2) + (relative >> 1), 0, 0)

    return pl.pallas_call(
        widen_kernel,
        grid_spec=pltpu.PrefetchScalarGridSpec(
            num_scalar_prefetch=1,
            grid=(count,),
            in_specs=[pl.BlockSpec((1, size, dim), source)],
            out_specs=pl.BlockSpec((size, dim), lambda turn, place: (turn, 0)),
        ),
        out_shape=jax.ShapeDtypeStruct((count * size, dim), f32),
        cost_estimate=time_estimate(3, count * size * dim * 6),
        name="assemble_out_weight_grad",
    )(place, pieces)


def assemble_kernel(width, shared, lasting, place_ref, pieces_ref, out_ref):
    count = pieces_ref.shape[0]
    inner = count * width
    per = lasting // count
    sums = jnp.zeros((pieces_ref.shape[1], shared), f32)
    for device in range(count):
        piece = pieces_ref[place_ref[0] ^ device].astype(f32)
        own = piece[:, : 2 * width].T
        first, second = device * width, inner + device * width
        out_ref[first : first + width] = own[:width]
        out_ref[second : second + width] = own[width:]
        last = 2 * inner + shared + device * per
        out_ref[last : last + per] = piece[:, 2 * width + shared :].T[:per]
        sums = sums + piece[:, 2 * width : 2 * width + shared]
    out_ref[2 * inner : 2 * inner + shared] = sums.T


def assemble(place, pieces, width, shared, lasting):
    count, rows, columns = pieces.shape
    tile = LANES if rows % LANES == 0 else rows
    out_cols = 2 * count * width + shared + lasting
    return pl.pallas_call(
        functools.partial(assemble_kernel, width, shared, lasting),
        grid_spec=pltpu.PrefetchScalarGridSpec(
            num_scalar_prefetch=1,
            grid=(rows // tile,),
            in_specs=[pl.BlockSpec((count, tile, columns), lambda turn, place: (0, turn, 0))],
            out_specs=pl.BlockSpec((out_cols, tile), lambda turn, place: (0, turn)),
        ),
        out_shape=jax.ShapeDtypeStruct((out_cols, rows), f32),
        compiler_params=pltpu.CompilerParams(vmem_limit_bytes=40 * 2**20),
        cost_estimate=time_estimate(8, rows * (2 * count * columns + 4 * out_cols)),
        name="assemble_in_weight_grad",
    )(place, pieces).T


def body(
    tokens,
    norm_gain,
    in_weight,
    conv_weight,
    conv_bias,
    dt_bias,
    decay_log,
    skip_scale,
    gate_gain,
    out_weight,
    cotangent,
):
    count, mine = lax.axis_size("seq"), lax.axis_index("seq")
    place = mine.astype(jnp.int32).reshape(1)
    inner, all_heads, conv_all = gate_gain.shape[0], dt_bias.shape[0], conv_bias.shape[0]
    size, states = inner // all_heads, (conv_all - inner) // 2
    heads, width = all_heads // count, inner // count
    shared = 2 * states
    tok_rows = tokens.shape[1]
    per_plane = out_weight.shape[0] // width

    def own(vector, per):
        return lax.dynamic_slice_in_dim(vector, mine * per, per, vector.ndim - 1)

    def own_conv(array):
        return jnp.concatenate([own(array[..., :inner], width), array[..., inner:]], axis=-1)

    def lane_row(vector):
        return jnp.pad(vector, (0, LANES - vector.shape[0]))[None]

    tokens_row = tokens[0].astype(f32)
    inverse = lax.rsqrt(jnp.mean(tokens_row * tokens_row, axis=-1, keepdims=True) + epsilon)
    normed_own = (tokens_row * inverse * norm_gain).astype(bf16)
    w_own = jnp.concatenate(
        [
            own(in_weight[:, :inner], width),
            own_conv(in_weight[:, inner : inner + conv_all]),
            jnp.pad(own(in_weight[:, inner + conv_all :], heads), ((0, 0), (0, LANES - heads))),
        ],
        axis=1,
    )
    w_cols = lax.all_gather(w_own, "batch", axis=0, tiled=True)
    normed = gather_tokens(normed_own)
    w_cols, normed, cot_own, out_owned = lax.optimization_barrier(
        (w_cols, normed, cotangent[0], out_weight)
    )
    out_rows = rows_from_owner(out_owned, width)
    cot = lax.all_gather(cot_own, "seq", axis=0, tiled=True)

    conv_w, conv_b = own_conv(conv_weight), own_conv(conv_bias)[None]
    step_rows = jnp.concatenate(
        [
            lane_row(own(dt_bias, heads)),
            lane_row(-jnp.exp(own(decay_log, heads))),
            jnp.zeros((6, LANES), f32),
        ],
        axis=0,
    )
    gain_own = own(gate_gain, width)
    rows = jnp.concatenate(
        [
            jnp.repeat(own(skip_scale, heads), size)[None],
            gain_own[None],
            jnp.zeros((6, width), f32),
        ],
        axis=0,
    )

    conv_in, gate, slab, ssd, starts, scaled = run_forward(
        place, normed, w_cols, conv_w, conv_b, step_rows, rows, heads, size, states, count
    )

    out_part = jnp.dot(scaled, out_rows, preferred_element_type=f32).astype(bf16)
    out_part, cot = lax.optimization_barrier((out_part, cot))
    mixed_out = lax.psum_scatter(out_part, "seq", scatter_dimension=0, tiled=True)
    out_grad = jnp.einsum("td,ed->te", cot, out_rows, preferred_element_type=f32)
    sums = sum_seq(jnp.stack([slab[:, LANES - 1], jnp.sum(out_grad * scaled.astype(f32), axis=1)]))
    scale = lax.rsqrt(sums[0] / inner + epsilon)
    norms = jnp.stack([scale, scale * scale * scale * sums[1] / inner], axis=1)
    own_scale = lax.dynamic_slice_in_dim(scale, mine * tok_rows, tok_rows, 0)
    scaled_cot = (cot.astype(f32) * scale[:, None]).astype(bf16)
    out_term = jnp.einsum("te,td->ed", scaled, scaled_cot, preferred_element_type=f32)
    out_low, norms = lax.optimization_barrier((out_term.astype(bf16), norms))
    out_piece = rows_to_owner(out_low)

    proj_grad, gain_term, skip_term, conv_w_term, conv_b_term, small_term = run_backward(
        place, conv_in, gate, slab, ssd, starts, out_grad, norms, conv_w, conv_b, step_rows, rows,
        heads, size, states, count,
    )

    proj_grad, mixed_out, out_piece = lax.optimization_barrier((proj_grad, mixed_out, out_piece))
    in_term = jnp.einsum("td,tf->df", normed, proj_grad, preferred_element_type=f32)
    norm_gain_term = jnp.sum(in_term * w_cols.astype(f32), axis=1) / norm_gain
    in_low = in_term.astype(bf16)
    in_low, back_grad = lax.optimization_barrier((in_low, proj_grad))
    in_sum = lax.psum_scatter(in_low, "batch", scatter_dimension=0, tiled=True)

    def back_part(part):
        return jnp.einsum("tf,df->td", part, w_cols, preferred_element_type=f32).astype(bf16)

    middle = back_grad.shape[0] // 2
    normed_grad = scatter_sum(back_part(back_grad[:middle]), back_part(back_grad[middle:]))
    normed_grad = normed_grad.astype(f32)
    cot_row = cotangent[0].astype(f32)
    gained = norm_gain * normed_grad
    slope = inverse * inverse * inverse * jnp.mean(gained * tokens_row, axis=-1, keepdims=True)
    input_grad = cot_row + inverse * gained - tokens_row * slope

    in_sum, _ = lax.optimization_barrier((in_sum, normed_grad))
    first, second = gather_relative(in_sum)
    in_sums = jnp.stack([jnp.concatenate([first[k], second[k]]) for k in range(count)])
    in_weight_grad = assemble(place, in_sums, width, shared, all_heads)

    out_weight_grad = assemble_out(place, gather_doubling(out_piece), per_plane)
    block_out = (tokens_row + own_scale[:, None] * mixed_out.astype(f32)).astype(bf16)

    def among_heads(vector, per, total):
        return lax.dynamic_update_slice_in_dim(jnp.zeros((total,), f32), vector, mine * per, 0)

    def among_conv(array):
        wide = jnp.zeros((array.shape[0], inner), f32)
        wide = lax.dynamic_update_slice_in_dim(wide, array[:, :width], mine * width, 1)
        return jnp.concatenate([wide, array[:, width:]], axis=1).reshape(-1)

    skip_heads = jnp.sum(skip_term.reshape(heads, size), axis=1)
    terms = [
        norm_gain_term,
        among_conv(conv_w_term),
        among_conv(conv_b_term),
        among_heads(small_term[0, :heads], heads, all_heads),
        among_heads(small_term[1, :heads], heads, all_heads),
        among_heads(skip_heads, heads, all_heads),
        among_heads(gain_term[0], width, inner),
    ]
    vector = jnp.concatenate(terms)
    padding = -vector.shape[0] % (8 * LANES)
    vector = sum_all(jnp.pad(vector, (0, padding)).reshape(-1, LANES)).reshape(-1)
    parts, offset = [], 0
    for term in terms:
        parts.append(vector[offset : offset + term.shape[0]])
        offset += term.shape[0]
    return (
        block_out[None],
        input_grad[None],
        parts[0],
        in_weight_grad,
        parts[1].reshape(conv_weight.shape),
        parts[2],
        parts[3],
        parts[4],
        parts[5],
        parts[6],
        out_weight_grad,
    )


def solution(mesh):
    placed = (
        P("batch", "seq", None),
        P(),
        P("batch", None),
        P(),
        P(),
        P(),
        P(),
        P(),
        P(),
        P("batch", None),
        P("batch", "seq", None),
    )
    return jax.shard_map(
        body,
        mesh=mesh,
        in_specs=placed,
        out_specs=(
            P("batch", "seq", None),
            P("batch", "seq", None),
            P(),
            P("batch", None),
            P(),
            P(),
            P(),
            P(),
            P(),
            P(),
            P("batch", None),
        ),
        check_vma=False,
    )
```

```python
import functools

import jax
import jax.numpy as jnp
from jax import lax
from jax.experimental import pallas as pl
from jax.experimental.pallas import tpu as pltpu
from jax.sharding import PartitionSpec as P

GROUP = 256
LANES = 128
HALO = 8
STEP_ROWS = 16
FORWARD_CALLS = 4
BACKWARD_CALLS = 4
epsilon = 1e-05
highest = lax.Precision.HIGHEST
f32 = jnp.float32
bf16 = jnp.bfloat16
MIB = 2**20


def exchange(value, axis, distance):
    count = lax.axis_size(axis)
    return lax.ppermute(value, axis, [(source, source ^ distance) for source in range(count)])


def bits_of(count):
    return [1 << k for k in range(count.bit_length() - 1)]


def placed_order(count):
    return [2 * k for k in range(count // 2)] + [2 * k + 1 for k in range(count // 2)]


def together(*values):
    return lax.optimization_barrier(values)


def far_orders():
    far = bits_of(lax.axis_size("seq"))[1:]
    return far, far[::-1]


def gather_start(value):
    half = value.shape[0] // 32 * 16
    return tuple({"base": part, "fresh": None, "near": []} for part in (value[:half], value[half:]))


def gather_stage(held, stage):
    grown = []
    for half, order in zip(held, far_orders()):
        base, fresh, near = half["base"], half["fresh"], list(half["near"])
        if stage >= 1:
            merged = base if stage == len(order) else jnp.concatenate([base, fresh], axis=0)
            near.append(exchange(merged if stage == 1 else fresh, "seq", 1))
            base = merged
        if stage < len(order):
            fresh = exchange(base, "seq", order[stage])
        grown.append({"base": base, "fresh": fresh, "near": near})
    return tuple(grown)


def gather_stages():
    return len(bits_of(lax.axis_size("seq")))


def gathered(held):
    arrays, table = [], {}
    for number, (half, order) in enumerate(zip(held, far_orders())):
        indices = [0]
        for bit in order:
            indices += [index | bit for index in indices]
        middle = len(indices) // 2
        groups = [(half["base"], indices[:middle]), (half["fresh"], indices[middle:])]
        bounds = [0] + [2 << k for k in range(len(order))]
        for value, first, last in zip(half["near"], bounds, bounds[1:]):
            groups.append((value, [index | 1 for index in indices[first:last]]))
        for value, members in groups:
            rows = value.shape[0] // len(members)
            for turn, index in enumerate(members):
                table[number, index] = (len(arrays), turn * rows)
            arrays.append(value)
    return arrays, table


def placed_pieces(held):
    arrays, table = gathered(held)
    order = placed_order(lax.axis_size("seq"))
    return arrays, tuple(table[half, index] for index in order for half in range(2))


def gather_all(value):
    held = gather_start(value)
    for stage in range(gather_stages()):
        held = gather_stage(held, stage)
    return held


def scatter_near(keep, send):
    total = (keep.astype(f32) + exchange(send, "seq", 1).astype(f32)).astype(bf16)
    count = lax.axis_size("seq")
    half = total.shape[0] // count
    total = total.reshape((count // 2, 2, half) + total.shape[1:])
    held = []
    for part, order in enumerate(far_orders()):
        members = [0]
        for bit in order[::-1]:
            members += [member | bit >> 1 for member in members]
        held.append(jnp.stack([total[member, part] for member in members]))
    return tuple(held)


def scatter_stage(held, stage):
    smaller = []
    for value, order in zip(held, far_orders()):
        middle = value.shape[0] // 2
        arriving = exchange(value[middle:], "seq", order[stage])
        smaller.append((value[:middle].astype(f32) + arriving.astype(f32)).astype(bf16))
    return tuple(smaller)


def scatter_end(held):
    return jnp.concatenate([value[0] for value in held], axis=0)


def sum_placed(value):
    bits = bits_of(lax.axis_size("seq"))
    shape = value.shape
    split = value.reshape((shape[0],) + (2,) * len(bits) + (-1,))
    axis_of = {bits[0]: 1}
    for place, bit in enumerate(bits[:0:-1]):
        axis_of[bit] = 2 + place
    for bit in bits:
        split = split + jnp.flip(exchange(split, "seq", bit), axis_of[bit])
    return split.reshape(shape)


def sum_all(value):
    for axis in ("seq", "batch"):
        for bit in bits_of(lax.axis_size(axis)):
            value = value + exchange(value, axis, bit)
    return value


def plane_scatter_start(value):
    planes, plane = lax.axis_size("batch"), lax.axis_index("batch")
    return {
        o: lax.dynamic_index_in_dim(value, jnp.clip(plane + o, 0, planes - 1), 0, keepdims=False)
        for o in range(1 - planes, planes)
    }


def plane_scatter_round(held, turn):
    planes = lax.axis_size("batch")
    far = planes - 1 - turn
    held = dict(held)
    for sign in (1, -1):
        sources = [k for k in range(planes) if 0 <= k + sign * far < planes]
        pairs = [(k, k + sign) for k in sources]
        arriving = lax.ppermute(held.pop(sign * far), "batch", pairs)
        nearer = sign * (far - 1)
        held[nearer] = (held[nearer].astype(f32) + arriving.astype(f32)).astype(bf16)
    return held


def plane_pairs(ahead):
    planes, count = lax.axis_size("batch"), lax.axis_size("seq")
    per = count // planes
    pairs = []
    for owner in range(planes):
        for piece in range(planes):
            for k in range(per):
                holder = owner * count + piece * per + k
                user = (piece + ahead) % planes * count + owner * per + k
                pairs.append((holder, user))
    return pairs


def rows_from_owner(out_weight, width, aheads):
    planes, count = lax.axis_size("batch"), lax.axis_size("seq")
    per, size = count // planes, width // planes
    mine = lax.axis_index("seq")
    piece = lax.dynamic_slice_in_dim(out_weight, mine % per * width + mine // per * size, size, 0)
    return [lax.ppermute(piece, ("batch", "seq"), plane_pairs(ahead)) for ahead in aheads]


def rows_joined(arriving):
    planes, plane = lax.axis_size("batch"), lax.axis_index("batch")
    size = arriving[0].shape[0]
    doubled = jnp.concatenate(arriving[::-1] * 2, axis=0)
    return lax.dynamic_slice_in_dim(doubled, (planes - 1 - plane) * size, planes * size, 0)


def to_owner(summed):
    return lax.ppermute(
        summed, ("batch", "seq"), [(user, holder) for holder, user in plane_pairs(0)]
    )


def double(held, turn):
    bits = bits_of(lax.axis_size("seq"))
    return jnp.concatenate([held, exchange(held, "seq", (bits[1:] + [1])[turn])], axis=0)


def step_values(raw):
    small = jnp.exp(-jnp.abs(raw))
    step = jnp.maximum(raw, 0.0) + jnp.log1p(small)
    sig = jnp.where(raw >= 0, 1.0, small) / (1.0 + small)
    tiny = raw < -20.0
    log_step = jnp.where(tiny, raw, jnp.log(step))
    ratio = jnp.where(tiny, 1.0, sig / step)
    return step, sig, log_step, ratio


def spread_heads(value, heads, size):
    rows = value.shape[0]
    return jnp.concatenate(
        [jnp.broadcast_to(value[:, h : h + 1], (rows, size)) for h in range(heads)], axis=1
    )


def sum_heads(value, size):
    width = value.shape[1]
    row = lax.broadcasted_iota(jnp.int32, (width, LANES), 0) // size
    lane = lax.broadcasted_iota(jnp.int32, (width, LANES), 1)
    ones = (row == lane).astype(f32)
    return jnp.dot(value, ones, precision=highest, preferred_element_type=f32)


def sum_lanes(value):
    return dot_nt(jnp.ones((8, value.shape[1]), bf16), value.astype(bf16))


def order_masks(length):
    row = lax.broadcasted_iota(jnp.int32, (length, length), 0)
    column = lax.broadcasted_iota(jnp.int32, (length, length), 1)
    return row, column


def dot(a, b):
    return jnp.dot(a, b, preferred_element_type=f32)


def dot_nt(a, b):
    return lax.dot_general(a, b, (((1,), (1,)), ((), ())), preferred_element_type=f32)


def dot_tn(a, b):
    return lax.dot_general(a, b, (((0,), (0,)), ((), ())), preferred_element_type=f32)


def sigmoid(value):
    return 1.0 / (1.0 + jnp.exp(-value))


def mixed(padded, conv_w, conv_b):
    taps = conv_w.shape[0]
    total = conv_b
    for k in range(taps):
        start = HALO - (taps - 1) + k
        total = total + conv_w[k : k + 1] * padded[start : start + GROUP]
    return total


def fetch(arrays, table, which, buffer, semaphores, slot):
    for index, (array, row) in enumerate(table):

        @pl.when(which == index)
        def _():
            source = arrays[array].at[pl.ds(row, GROUP)]
            pltpu.make_async_copy(source, buffer.at[slot], semaphores.at[slot]).start()


def fetched(arrays, table, buffer, semaphores, order):
    step = pl.program_id(0)
    slot = lax.rem(step, 2)

    @pl.when(step == 0)
    def _():
        fetch(arrays, table, order(0), buffer, semaphores, 0)

    @pl.when(step + 1 < pl.num_programs(0))
    def _():
        fetch(arrays, table, order(step + 1), buffer, semaphores, lax.rem(step + 1, 2))

    source = arrays[0].at[pl.ds(0, GROUP)]
    pltpu.make_async_copy(source, buffer.at[slot], semaphores.at[slot]).wait()
    return buffer[slot]


def block_place(place, block, count):
    relative = (block // 2) ^ place
    order = (relative & 1) * (count // 2) + (relative >> 1)
    return order * 2 + block % 2


def forward_kernel(dims, first_block, table, given, earlier, place_ref, *refs):
    heads, size, states, count = dims
    width = heads * size
    conv_cols = width + 2 * states
    arrays, refs = refs[:given], refs[given:]
    w_ref, conv_w_ref, conv_b_ref, step_ref, rows_ref, state_in, tail_in = refs[:7]
    refs = refs[7 + earlier :]
    conv_in_ref, gate_ref, raw_ref, ssd_ref, start_ref, scaled_ref, square_ref = refs[:7]
    state, tail_ref, padded, buffer, semaphores = refs[7:]

    @pl.when(pl.program_id(0) == 0)
    def _():
        state[...] = state_in[...]
        padded[0:HALO] = tail_in[...]

    normed = fetched(
        arrays,
        table,
        buffer,
        semaphores,
        lambda step: block_place(place_ref[0], first_block + step, count),
    )
    projected = dot(normed, w_ref[...])
    gate = projected[:, :width]
    conv_in = projected[:, width : width + conv_cols].astype(bf16)
    raw = projected[:, width + conv_cols :]
    padded[HALO : HALO + GROUP] = conv_in.astype(f32)
    pre = mixed(padded, conv_w_ref[...], conv_b_ref[...])
    padded[0:HALO] = padded[GROUP : GROUP + HALO]
    tail_ref[...] = padded[0:HALO]
    active = (pre * sigmoid(pre)).astype(bf16)
    signal = active[:, :width]
    entry = active[:, width : width + states]
    readout = active[:, width + states :]
    signal_wide = signal.astype(f32)

    step, _, log_step, _ = step_values(raw + step_ref[0:1])
    decay = step * step_ref[1:2]
    row, column = order_masks(GROUP)
    running = jnp.dot(
        (row >= column).astype(f32), decay, precision=highest, preferred_element_type=f32
    )
    later = running - log_step
    total = running[GROUP - 1 : GROUP]
    later_rows = later.T
    scores = dot_nt(readout, entry)
    start = state[...]
    start_ref[0] = start
    carried = dot(readout, start.astype(bf16)) * spread_heads(jnp.exp(running), heads, size)
    within = []
    for h in range(heads):
        spread = running[:, h : h + 1] - later_rows[h : h + 1, :]
        kernel = jnp.exp(jnp.where(row >= column, spread, -1e30))
        weights = (scores * kernel).astype(bf16)
        within.append(dot(weights, signal[:, h * size : (h + 1) * size]))
    ssd = jnp.concatenate(within, axis=1) + carried + rows_ref[0:1] * signal_wide
    tail = (signal_wide * spread_heads(jnp.exp(total - later), heads, size)).astype(bf16)
    state[...] = start * spread_heads(jnp.exp(total), heads, size) + dot_tn(entry, tail)

    gated = ssd * (gate * sigmoid(gate))
    conv_in_ref[...] = conv_in
    gate_ref[...] = gate.astype(bf16)
    raw_ref[...] = raw
    ssd_ref[...] = ssd
    scaled_ref[...] = (gated * rows_ref[1:2]).astype(bf16)
    square_ref[0] = sum_lanes(gated * gated)


def time_estimate(microseconds, accessed):
    return pl.CostEstimate(
        flops=int(microseconds * 1.1e9), bytes_accessed=int(accessed), transcendentals=0
    )


def fixed(shape):
    return pl.BlockSpec(shape, lambda turn, place: (0,) * len(shape), pipeline_mode=pl.Buffered(1))


def anywhere(values):
    return [pl.BlockSpec(memory_space=pl.ANY)] * len(values)


def forward_call(call, place, pieces, params, dims, outputs, carried):
    heads, size, states, count = dims
    w_cols, conv_w, conv_b, _, _ = params
    dim = w_cols.shape[0]
    width, conv_cols = heads * size, conv_w.shape[1]
    arrays, table = pieces
    blocks = len(table)
    tokens = blocks * GROUP
    share = blocks // FORWARD_CALLS
    first = call * share
    out_shape = [
        jax.ShapeDtypeStruct((tokens, conv_cols), bf16),
        jax.ShapeDtypeStruct((tokens, width), bf16),
        jax.ShapeDtypeStruct((tokens, LANES), f32),
        jax.ShapeDtypeStruct((tokens, width), f32),
        jax.ShapeDtypeStruct((blocks, states, width), f32),
        jax.ShapeDtypeStruct((tokens, width), bf16),
        jax.ShapeDtypeStruct((blocks, 8, GROUP), f32),
    ]

    def moving(columns):
        return pl.BlockSpec(
            (GROUP, columns), lambda turn, place: (block_place(place[0], first + turn, count), 0)
        )

    operands = [place, *arrays, *params, *carried, *outputs]
    aliases = {len(operands) - len(outputs) + k: k for k in range(len(outputs))}
    results = pl.pallas_call(
        functools.partial(forward_kernel, dims, first, table, len(arrays), len(outputs)),
        grid_spec=pltpu.PrefetchScalarGridSpec(
            num_scalar_prefetch=1,
            grid=(share,),
            in_specs=[
                *anywhere(arrays),
                *[fixed(param.shape) for param in params],
                *[fixed(value.shape) for value in carried],
                *anywhere(outputs),
            ],
            out_specs=[
                moving(conv_cols),
                moving(width),
                moving(LANES),
                moving(width),
                pl.BlockSpec((1, states, width), lambda turn, place: (first + turn, 0, 0)),
                moving(width),
                pl.BlockSpec(
                    (1, 8, GROUP),
                    lambda turn, place: (block_place(place[0], first + turn, count), 0, 0),
                ),
                fixed((states, width)),
                fixed((HALO, conv_cols)),
            ],
            scratch_shapes=[
                pltpu.VMEM((HALO + GROUP, conv_cols), f32),
                pltpu.VMEM((2, GROUP, dim), bf16),
                pltpu.SemaphoreType.DMA((2,)),
            ],
        ),
        out_shape=out_shape
        + [
            jax.ShapeDtypeStruct((states, width), f32),
            jax.ShapeDtypeStruct((HALO, conv_cols), f32),
        ],
        input_output_aliases=aliases,
        compiler_params=pltpu.CompilerParams(vmem_limit_bytes=40 * MIB),
        cost_estimate=time_estimate(share * 3.3, share * GROUP * (2 * dim + 12 * width)),
        name="forward_blocks",
    )(*operands)
    return results[:7], results[7:]


def out_grad_kernel(table, cots, scaled_ref, out_rows_ref, out_grad_ref, slope_ref, buffer, semaphores):
    cot = fetched(cots, table, buffer, semaphores, lambda step: step)
    out_grad = dot_nt(cot, out_rows_ref[...])
    out_grad_ref[...] = out_grad.astype(bf16)
    slope_ref[0] = sum_lanes(out_grad * scaled_ref[...].astype(f32))


def run_out_grad(cots, scaled, out_rows):
    arrays, table = cots
    blocks = len(table)
    width, dim = out_rows.shape

    def kernel(*refs):
        out_grad_kernel(table, refs[: len(arrays)], *refs[len(arrays) :])

    return pl.pallas_call(
        kernel,
        grid=(blocks,),
        in_specs=[
            *anywhere(arrays),
            pl.BlockSpec((GROUP, width), lambda turn: (turn, 0)),
            pl.BlockSpec((width, dim), lambda turn: (0, 0), pipeline_mode=pl.Buffered(1)),
        ],
        out_specs=[
            pl.BlockSpec((GROUP, width), lambda turn: (turn, 0)),
            pl.BlockSpec((1, 8, GROUP), lambda turn: (turn, 0, 0)),
        ],
        out_shape=[
            jax.ShapeDtypeStruct((blocks * GROUP, width), bf16),
            jax.ShapeDtypeStruct((blocks, 8, GROUP), f32),
        ],
        scratch_shapes=[pltpu.VMEM((2, GROUP, dim), bf16), pltpu.SemaphoreType.DMA((2,))],
        compiler_params=pltpu.CompilerParams(vmem_limit_bytes=24 * MIB),
        cost_estimate=time_estimate(8, blocks * GROUP * (2 * dim + 6 * width)),
        name="out_grad",
    )(*arrays, scaled, out_rows)


def gate_kernel(
    planes, tables, cots, normeds, out_grad_ref, ssd_ref, gate_ref, norm_ref, gain_ref,
    ssd_grad_ref, gate_grad_ref, out_term_ref, in_term_ref, gain_grad_ref,
    out_sum, in_sum, cot_buffer, cot_semaphores, normed_buffer, normed_semaphores,
):
    step = pl.program_id(0)

    @pl.when(step == 0)
    def _():
        out_sum[...] = jnp.zeros_like(out_sum)
        in_sum[...] = jnp.zeros_like(in_sum)
        gain_grad_ref[...] = jnp.zeros_like(gain_grad_ref)

    cot = fetched(cots, tables[0], cot_buffer, cot_semaphores, lambda step: step)
    normed = fetched(normeds, tables[1], normed_buffer, normed_semaphores, lambda step: step)
    gate, ssd, out_grad = gate_ref[...].astype(f32), ssd_ref[...], out_grad_ref[...].astype(f32)
    norms = norm_ref[0].T
    scale, slope = norms[:, 0:1], norms[:, 1:2]
    gate_sig = sigmoid(gate)
    gate_act = gate * gate_sig
    gated = ssd * gate_act
    unit = gated * scale
    gain = gain_ref[...]
    gain_grad_ref[...] += jnp.sum(out_grad * unit, axis=0, keepdims=True)
    gated_grad = out_grad * gain * scale - gated * slope
    ssd_grad_ref[...] = (gated_grad * gate_act).astype(bf16)
    gate_grad = (gated_grad * ssd * (gate_sig * (1.0 + gate * (1.0 - gate_sig)))).astype(bf16)
    gate_grad_ref[...] = gate_grad
    out_sum[...] += dot_tn((unit * gain).astype(bf16), cot)
    in_sum[...] += dot_tn(gate_grad, normed)

    @pl.when(step == pl.num_programs(0) - 1)
    def _():
        out_term_ref[...] = out_sum[...].astype(bf16)
        part = in_sum.shape[1] // planes
        for plane in range(planes):
            in_term_ref[plane] = in_sum[:, plane * part : (plane + 1) * part].astype(bf16)


def run_gate(cots, normeds, out_grad, ssd, gate, norms, gain, planes):
    arrays = (*cots[0], *normeds[0])
    first, both = len(cots[0]), len(arrays)
    tables = (cots[1], normeds[1])
    blocks = len(cots[1])
    width, dim = gate.shape[1], arrays[0].shape[1]

    def kernel(*refs):
        gate_kernel(planes, tables, refs[:first], refs[first:both], *refs[both:])

    def moving():
        return pl.BlockSpec((GROUP, width), lambda turn: (turn, 0))

    def whole(*shape):
        return pl.BlockSpec(shape, lambda turn: (0,) * len(shape), pipeline_mode=pl.Buffered(1))

    return pl.pallas_call(
        kernel,
        grid=(blocks,),
        in_specs=[
            *anywhere(arrays),
            moving(),
            moving(),
            moving(),
            pl.BlockSpec((1, 8, GROUP), lambda turn: (turn, 0, 0)),
            whole(1, width),
        ],
        out_specs=[
            moving(),
            moving(),
            whole(width, dim),
            whole(planes, width, dim // planes),
            whole(1, width),
        ],
        out_shape=[
            jax.ShapeDtypeStruct((blocks * GROUP, width), bf16),
            jax.ShapeDtypeStruct((blocks * GROUP, width), bf16),
            jax.ShapeDtypeStruct((width, dim), bf16),
            jax.ShapeDtypeStruct((planes, width, dim // planes), bf16),
            jax.ShapeDtypeStruct((1, width), f32),
        ],
        scratch_shapes=[
            pltpu.VMEM((width, dim), f32),
            pltpu.VMEM((width, dim), f32),
            pltpu.VMEM((2, GROUP, dim), bf16),
            pltpu.SemaphoreType.DMA((2,)),
            pltpu.VMEM((2, GROUP, dim), bf16),
            pltpu.SemaphoreType.DMA((2,)),
        ],
        compiler_params=pltpu.CompilerParams(vmem_limit_bytes=40 * MIB),
        cost_estimate=time_estimate(16, blocks * GROUP * (4 * dim + 10 * width)),
        name="gate_grads",
    )(*arrays, out_grad, ssd, gate, norms, gain)


def backward_kernel(dims, last_block, earlier, place_ref, *refs):
    heads, size, states, _ = dims
    width = heads * size
    conv_in_ref, before_ref, raw_ref, ssd_ref, start_ref, grad_ref, gate_grad_ref = refs[:7]
    conv_w_ref, conv_b_ref, step_ref, rows_ref = refs[7:11]
    given = refs[11:17]
    refs = refs[17 + earlier :]
    out_ref, state, pre_tail, skip_ref, conv_wg_ref, conv_bg_ref, small_ref = refs[:7]
    padded, pre_grads = refs[7:]
    taps = conv_w_ref.shape[0]
    turn = pl.program_id(0)
    block = last_block - turn

    @pl.when(turn == 0)
    def _():
        for source, target in zip(
            given, (state, pre_tail, skip_ref, conv_wg_ref, conv_bg_ref, small_ref)
        ):
            target[...] = source[...]

    previous = before_ref[...].astype(f32)[16 - HALO :]
    padded[0:HALO] = jnp.where(block > 0, previous, 0.0)
    padded[HALO : HALO + GROUP] = conv_in_ref[...].astype(f32)
    conv_w = conv_w_ref[...]
    pre = mixed(padded, conv_w, conv_b_ref[...])
    pre_sig = sigmoid(pre)
    active = (pre * pre_sig).astype(bf16)
    signal = active[:, :width]
    entry = active[:, width : width + states]
    readout = active[:, width + states :]
    signal_wide = signal.astype(f32)

    raw = raw_ref[...] + step_ref[0:1]
    lane = lax.broadcasted_iota(jnp.int32, raw.shape, 1)
    step, sig, log_step, ratio = step_values(raw)
    decay = step * step_ref[1:2]
    row, column = order_masks(GROUP)
    running = jnp.dot(
        (row >= column).astype(f32), decay, precision=highest, preferred_element_type=f32
    )
    later = running - log_step
    total = running[GROUP - 1 : GROUP]
    running_rows = running.T

    start = start_ref[0]
    end_grad = state[...]
    grad_low = grad_ref[...]
    ssd_grad = grad_low.astype(f32)
    start_low, end_low = start.astype(bf16), end_grad.astype(bf16)
    scores = dot_nt(entry, readout)
    score_grad = jnp.zeros_like(scores)
    within = []
    for h in range(heads):
        part = slice(h * size, (h + 1) * size)
        spread = running_rows[h : h + 1, :] - later[:, h : h + 1]
        kernel = jnp.exp(jnp.where(column >= row, spread, -1e30))
        weights = (scores * kernel).astype(bf16)
        within.append(dot(weights, grad_low[:, part]))
        score_grad = score_grad + dot_nt(signal[:, part], grad_low[:, part]) * kernel
    tail_wide = spread_heads(jnp.exp(total - later), heads, size)
    tail_grad = tail_wide * dot(entry, end_low)
    signal_grad = jnp.concatenate(within, axis=1) + tail_grad
    score_low = score_grad.astype(bf16)
    tail = (signal_wide * tail_wide).astype(bf16)
    head_grad = (ssd_grad * spread_heads(jnp.exp(running), heads, size)).astype(bf16)
    entry_grad = dot(score_low, readout) + dot_nt(tail, end_low)
    readout_grad = dot_tn(score_low, entry) + dot_nt(head_grad, start_low)
    total_wide = spread_heads(jnp.exp(total), heads, size)
    state[...] = end_grad * total_wide + dot_tn(readout, head_grad)

    skip = rows_ref[0:1]
    column_part = sum_heads(signal_wide * signal_grad, size)
    row_part = sum_heads(ssd_grad * (ssd_ref[...] - skip * signal_wide), size)
    end_part = jnp.sum(signal_wide * tail_grad, axis=0, keepdims=True) + total_wide * jnp.sum(
        start * end_grad, axis=0, keepdims=True
    )
    end_part = sum_heads(jnp.broadcast_to(end_part, (8, width)), size)[0:1]
    decay_grad = (
        jnp.dot(
            (column >= row).astype(f32),
            row_part - column_part,
            precision=highest,
            preferred_element_type=f32,
        )
        + end_part
    )
    raw_grad = column_part * ratio + decay_grad * step_ref[1:2] * sig
    raw_grad = jnp.where(lane < heads, raw_grad, 0.0)
    skip_ref[...] += jnp.sum(ssd_grad * signal_wide, axis=0, keepdims=True)
    small_ref[0:1] += jnp.sum(raw_grad, axis=0, keepdims=True)
    small_ref[1:2] += jnp.sum(decay_grad * decay, axis=0, keepdims=True)

    active_grad = jnp.concatenate([signal_grad + skip * ssd_grad, entry_grad, readout_grad], axis=1)
    pre_grad = active_grad * (pre_sig * (1.0 + pre * (1.0 - pre_sig)))
    pre_grads[0:GROUP] = pre_grad
    pre_grads[GROUP : GROUP + HALO] = pre_tail[...]
    conv_grad = jnp.zeros_like(pre_grad)
    for k in range(taps):
        ahead = taps - 1 - k
        conv_grad = conv_grad + conv_w[k : k + 1] * pre_grads[ahead : ahead + GROUP]
        first = HALO - ahead
        conv_wg_ref[k : k + 1] += jnp.sum(
            pre_grad * padded[first : first + GROUP], axis=0, keepdims=True
        )
    conv_bg_ref[...] += jnp.sum(pre_grad, axis=0, keepdims=True)
    pre_tail[...] = pre_grads[0:HALO]
    out_ref[:, :width] = gate_grad_ref[...]
    out_ref[:, width:] = jnp.concatenate([conv_grad, raw_grad], axis=1).astype(bf16)


def backward_call(call, place, values, params, dims, outputs, carried):
    heads, size, states, count = dims
    conv_in, raw, ssd, starts, ssd_grad, gate_grad = values
    conv_w, conv_b, _, _ = params
    tokens, width = ssd.shape
    conv_cols = conv_w.shape[1]
    blocks = tokens // GROUP
    share = blocks // BACKWARD_CALLS
    last = blocks - 1 - call * share
    ratio = GROUP // 16
    out_cols = width + conv_cols + LANES

    def moving(columns):
        return pl.BlockSpec(
            (GROUP, columns),
            lambda turn, place: (block_place(place[0], last - turn, count), 0),
        )

    def before(turn, place):
        earlier = jnp.maximum(last - 1 - turn, 0)
        return (block_place(place[0], earlier, count) * ratio + ratio - 1, 0)

    operands = [place, conv_in, conv_in, raw, ssd, starts, ssd_grad, gate_grad]
    operands += [*params, *carried, *outputs]
    aliases = {len(operands) - len(outputs) + k: k for k in range(len(outputs))}
    results = pl.pallas_call(
        functools.partial(backward_kernel, dims, last, len(outputs)),
        grid_spec=pltpu.PrefetchScalarGridSpec(
            num_scalar_prefetch=1,
            grid=(share,),
            in_specs=[
                moving(conv_cols),
                pl.BlockSpec((16, conv_cols), before),
                moving(LANES),
                moving(width),
                pl.BlockSpec((1, states, width), lambda turn, place: (last - turn, 0, 0)),
                moving(width),
                moving(width),
                *[fixed(param.shape) for param in params],
                *[fixed(value.shape) for value in carried],
                *anywhere(outputs),
            ],
            out_specs=[moving(out_cols), *[fixed(value.shape) for value in carried]],
            scratch_shapes=[
                pltpu.VMEM((HALO + GROUP, conv_cols), f32),
                pltpu.VMEM((GROUP + HALO, conv_cols), f32),
            ],
        ),
        out_shape=[jax.ShapeDtypeStruct((tokens, out_cols), bf16)]
        + [jax.ShapeDtypeStruct(value.shape, f32) for value in carried],
        input_output_aliases=aliases,
        compiler_params=pltpu.CompilerParams(vmem_limit_bytes=40 * MIB),
        cost_estimate=time_estimate(share * 3.3, share * GROUP * 20 * width),
        name="backward_blocks",
    )(*operands)
    return results[:1], results[1:]


def weight_kernel(planes, first, kept, table, normeds, grad_ref, out_ref, total, buffer, semaphores):
    step = pl.program_id(0)

    @pl.when(step == 0)
    def _():
        total[...] = jnp.zeros_like(total)

    normed = fetched(normeds, table, buffer, semaphores, lambda step: step)
    total[...] += dot_tn(grad_ref[:, first:], normed)

    @pl.when(step == pl.num_programs(0) - 1)
    def _():
        part = total.shape[1] // planes
        for plane in range(planes):
            out_ref[plane] = total[:kept, plane * part : (plane + 1) * part].astype(bf16)


def run_weight(normeds, proj_grad, first, kept, planes):
    arrays, table = normeds
    blocks = len(table)
    dim = arrays[0].shape[1]
    columns = proj_grad.shape[1] - first
    spec = pl.BlockSpec((GROUP, proj_grad.shape[1]), lambda turn: (turn, 0))

    def kernel(*refs):
        weight_kernel(planes, first, kept, table, refs[: len(arrays)], *refs[len(arrays) :])

    return pl.pallas_call(
        kernel,
        grid=(blocks,),
        in_specs=[*anywhere(arrays), spec],
        out_specs=pl.BlockSpec(
            (planes, kept, dim // planes), lambda turn: (0, 0, 0), pipeline_mode=pl.Buffered(1)
        ),
        out_shape=jax.ShapeDtypeStruct((planes, kept, dim // planes), bf16),
        scratch_shapes=[
            pltpu.VMEM((columns, dim), f32),
            pltpu.VMEM((2, GROUP, dim), bf16),
            pltpu.SemaphoreType.DMA((2,)),
        ],
        compiler_params=pltpu.CompilerParams(vmem_limit_bytes=40 * MIB),
        cost_estimate=time_estimate(12, blocks * GROUP * 2 * (dim + columns)),
        name="in_weight_grad",
    )(*arrays, proj_grad)


def widen_kernel(place_ref, piece_ref, out_ref):
    out_ref[...] = piece_ref[0].astype(f32)


def assemble_out(place, pieces, per):
    count, size, dim = pieces.shape
    groups = count // per

    def source(turn, place):
        relative = (turn % groups * per + turn // groups) ^ place[0]
        return ((relative & 1) * (count // 2) + (relative >> 1), 0, 0)

    return pl.pallas_call(
        widen_kernel,
        grid_spec=pltpu.PrefetchScalarGridSpec(
            num_scalar_prefetch=1,
            grid=(count,),
            in_specs=[pl.BlockSpec((1, size, dim), source)],
            out_specs=pl.BlockSpec((size, dim), lambda turn, place: (turn, 0)),
        ),
        out_shape=jax.ShapeDtypeStruct((count * size, dim), f32),
        cost_estimate=time_estimate(5, count * size * dim * 6),
        name="assemble_out_weight_grad",
    )(place, pieces)


def assemble_kernel(dims, heights, table, place_ref, *refs):
    heads, size, states, count = dims
    width, shared = heads * size, 2 * states
    inner = count * width
    gates_ref, convs, out_ref, sums = refs[0], refs[1:-2], refs[-2], refs[-1]
    for relative in range(count):
        device = place_ref[0] ^ relative
        top = pl.multiple_of(device * width, 8)
        gate = gates_ref[(relative >> 1) + (relative & 1) * (count // 2)]
        out_ref[pl.ds(top, width)] = gate.astype(f32)
        middle = pl.multiple_of(inner + device * width, 8)
        parts = []
        for half in range(2):
            array, row = table[half, relative]
            parts.append(convs[array][row : row + heights[half]].astype(f32))
        rows = jnp.concatenate(parts, axis=0)
        out_ref[pl.ds(middle, width)] = rows[:width]
        sums[device] = rows[width:]
    total = sums[0, :shared]
    for device in range(1, count):
        total = total + sums[device, :shared]
    out_ref[2 * inner : 2 * inner + shared] = total
    for device in range(count):
        last = 2 * inner + shared + device * heads
        out_ref[last : last + heads] = sums[device, shared : shared + heads]


def assemble(place, gates, convs, dims):
    heads, size, states, count = dims
    rows = gates.shape[2]
    out_rows = 2 * count * heads * size + 2 * states + count * heads
    arrays, table = gathered(convs)
    kept = heads * size + 2 * states + STEP_ROWS
    heights = (kept // 32 * 16, kept - kept // 32 * 16)

    def whole(value):
        return pl.BlockSpec(
            value.shape,
            lambda turn, place: (0,) * len(value.shape),
            pipeline_mode=pl.Buffered(1),
        )

    return pl.pallas_call(
        functools.partial(assemble_kernel, dims, heights, table),
        grid_spec=pltpu.PrefetchScalarGridSpec(
            num_scalar_prefetch=1,
            grid=(1,),
            in_specs=[whole(value) for value in (gates, *arrays)],
            out_specs=pl.BlockSpec(
                (out_rows, rows), lambda turn, place: (0, 0), pipeline_mode=pl.Buffered(1)
            ),
            scratch_shapes=[pltpu.VMEM((count, 2 * states + STEP_ROWS, rows), f32)],
        ),
        out_shape=jax.ShapeDtypeStruct((out_rows, rows), f32),
        compiler_params=pltpu.CompilerParams(vmem_limit_bytes=40 * MIB),
        cost_estimate=time_estimate(8, out_rows * rows * 6),
        name="assemble_in_weight_grad",
    )(place, gates, *arrays)


def body(
    tokens,
    norm_gain,
    in_weight,
    conv_weight,
    conv_bias,
    dt_bias,
    decay_log,
    skip_scale,
    gate_gain,
    out_weight,
    cotangent,
):
    count, mine = lax.axis_size("seq"), lax.axis_index("seq")
    planes = lax.axis_size("batch")
    place = mine.astype(jnp.int32).reshape(1)
    inner, all_heads, conv_all = gate_gain.shape[0], dt_bias.shape[0], conv_bias.shape[0]
    size, states = inner // all_heads, (conv_all - inner) // 2
    heads, width = all_heads // count, inner // count
    dims = (heads, size, states, count)
    shared = 2 * states
    conv_cols = width + shared
    tok_rows = tokens.shape[1]
    per_plane = out_weight.shape[0] // width

    def own(vector, per):
        return lax.dynamic_slice_in_dim(vector, mine * per, per, vector.ndim - 1)

    def own_conv(array):
        return jnp.concatenate([own(array[..., :inner], width), array[..., inner:]], axis=-1)

    def lane_row(vector):
        return jnp.pad(vector, (0, LANES - vector.shape[0]))[None]

    tokens_row = tokens[0].astype(f32)
    inverse = lax.rsqrt(jnp.mean(tokens_row * tokens_row, axis=-1, keepdims=True) + epsilon)
    normed_own = (tokens_row * inverse * norm_gain).astype(bf16)
    w_own = jnp.concatenate(
        [
            own(in_weight[:, :inner], width),
            own_conv(in_weight[:, inner : inner + conv_all]),
            jnp.pad(own(in_weight[:, inner + conv_all :], heads), ((0, 0), (0, LANES - heads))),
        ],
        axis=1,
    )
    w_cols = lax.all_gather(w_own, "batch", axis=0, tiled=True)
    held = gather_all(normed_own)
    w_cols, held, cot_own, out_owned = together(w_cols, held, cotangent[0], out_weight)
    normeds = placed_pieces(held)
    cots = gather_stage(gather_start(cot_own), 0)
    out_pieces = rows_from_owner(out_owned, width, range(planes - 1))

    conv_w, conv_b = own_conv(conv_weight), own_conv(conv_bias)[None]
    step_rows = jnp.concatenate(
        [
            lane_row(own(dt_bias, heads)),
            lane_row(-jnp.exp(own(decay_log, heads))),
            jnp.zeros((6, LANES), f32),
        ],
        axis=0,
    )
    gain_own = own(gate_gain, width)[None]
    rows = jnp.concatenate(
        [jnp.repeat(own(skip_scale, heads), size)[None], gain_own, jnp.zeros((6, width), f32)],
        axis=0,
    )
    params = (w_cols, conv_w, conv_b, step_rows, rows)
    outputs, carried = [], [jnp.zeros((states, width), f32), jnp.zeros((HALO, conv_cols), f32)]
    stages = gather_stages()
    waits = {1: 1, 3: 2} if stages == 3 else {k: k for k in range(1, stages)}
    for call in range(FORWARD_CALLS):
        if call in waits:
            carried, cots, out_pieces, out_owned = together(carried, cots, out_pieces, out_owned)
            cots = gather_stage(cots, waits[call])
        if call == FORWARD_CALLS - 1:
            out_pieces = out_pieces + rows_from_owner(out_owned, width, [planes - 1])
        outputs, carried = forward_call(call, place, normeds, params, dims, outputs, carried)
    conv_in, gate, raw, ssd, starts, scaled, squares = outputs
    cots = placed_pieces(cots)
    out_rows = rows_joined(out_pieces)

    out_grad, slopes = run_out_grad(cots, scaled, out_rows)
    sums = sum_placed(jnp.stack([squares[:, 0].reshape(-1), slopes[:, 0].reshape(-1)]))
    middle = scaled.shape[0] // 2
    out_send = dot(scaled[middle:], out_rows).astype(bf16)
    out_parts = scatter_near(dot(scaled[:middle], out_rows), out_send)
    scale = lax.rsqrt(sums[0] / inner + epsilon)
    norms = jnp.stack([scale, scale * scale * scale * sums[1] / inner])
    norms = jnp.pad(norms, ((0, 6), (0, 0))).reshape(8, -1, GROUP).swapaxes(0, 1)
    ssd_grad, gate_grad, out_term, gate_term, gain_term = run_gate(
        cots, normeds, out_grad, ssd, gate, norms, gain_own, planes
    )
    out_sum = lax.psum_scatter(out_term, "batch", scatter_dimension=0, tiled=True)
    gate_sum = lax.psum_scatter(gate_term, "batch", scatter_dimension=0)

    values = (conv_in, raw, ssd, starts, ssd_grad, gate_grad)
    params = (conv_w, conv_b, step_rows, rows)
    outputs = []
    carried = [
        jnp.zeros((states, width), f32),
        jnp.zeros((HALO, conv_cols), f32),
        jnp.zeros((1, width), f32),
        jnp.zeros(conv_w.shape, f32),
        jnp.zeros(conv_b.shape, f32),
        jnp.zeros((8, LANES), f32),
    ]
    waits = {0: 0, 2: 1} if stages == 3 else {k: k for k in range(stages - 1)}
    for call in range(BACKWARD_CALLS):
        if call in waits:
            carried, out_parts = together(carried, out_parts)
            out_parts = scatter_stage(out_parts, waits[call])
        if call == 1:
            carried, out_sum = together(carried, out_sum)
            out_pieces = to_owner(out_sum)[None]
        if call == 2:
            carried, out_pieces = together(carried, out_pieces)
            out_pieces = double(out_pieces, 0)
        if call == 3:
            carried, out_pieces, gate_sum = together(carried, out_pieces, gate_sum)
            out_pieces = double(out_pieces, 1)
            gates = double(gate_sum[None], 0)
        outputs, carried = backward_call(call, place, values, params, dims, outputs, carried)
    _, _, skip_term, conv_w_term, conv_b_term, small_term = carried
    mixed_out = scatter_end(out_parts)
    proj_grad, mixed_out, gates, out_pieces = together(outputs[0], mixed_out, gates, out_pieces)

    conv_term = run_weight(normeds, proj_grad, width, conv_cols + STEP_ROWS, planes)
    conv_parts = plane_scatter_start(conv_term)
    conv_parts, back_grad = together(conv_parts, proj_grad)
    conv_parts = plane_scatter_round(conv_parts, 0)

    def back_part(part):
        return jnp.einsum("tf,df->td", part, w_cols, preferred_element_type=f32)

    back_send = back_part(back_grad[middle:]).astype(bf16)
    back_parts = scatter_near(back_part(back_grad[:middle]), back_send)
    for stage in range(2, stages):
        out_pieces = double(out_pieces, stage)
    gates = double(gates, 1)
    for stage in range(stages - 1):
        back_parts, conv_parts, gates = together(back_parts, conv_parts, gates)
        back_parts = scatter_stage(back_parts, stage)
        conv_parts = plane_scatter_round(conv_parts, stage + 1)
        if stage + 2 < stages:
            gates = double(gates, stage + 2)
    for turn in range(stages, planes - 1):
        conv_parts = plane_scatter_round(conv_parts, turn)
    out_weight_grad = assemble_out(place, out_pieces, per_plane)
    normed_grad, conv_sum = together(scatter_end(back_parts), conv_parts[0])
    normed_grad = normed_grad.astype(f32)
    cot_row = cotangent[0].astype(f32)
    gained = norm_gain * normed_grad
    slope = inverse * inverse * inverse * jnp.mean(gained * tokens_row, axis=-1, keepdims=True)
    input_grad = cot_row + inverse * gained - tokens_row * slope
    own_scale = scale[:tok_rows, None]
    block_out = (tokens_row + own_scale * mixed_out.astype(f32)).astype(bf16)

    in_weight_grad = assemble(place, gates, gather_all(conv_sum), dims).T

    w_gate, w_conv = w_cols[:, :width].T, w_cols[:, width : width + conv_cols + STEP_ROWS].T

    def with_weight(term, weight):
        split = weight.reshape(weight.shape[0], planes, -1).swapaxes(0, 1)
        return jnp.sum(term.astype(f32) * split, 1).reshape(-1)

    norm_gain_term = (with_weight(gate_term, w_gate) + with_weight(conv_term, w_conv)) / norm_gain

    def among_heads(vector, per, total):
        return lax.dynamic_update_slice_in_dim(jnp.zeros((total,), f32), vector, mine * per, 0)

    def among_conv(array):
        wide = jnp.zeros((array.shape[0], inner), f32)
        wide = lax.dynamic_update_slice_in_dim(wide, array[:, :width], mine * width, 1)
        return jnp.concatenate([wide, array[:, width:]], axis=1).reshape(-1)

    skip_heads = jnp.sum(skip_term.reshape(heads, size), axis=1)
    terms = [
        norm_gain_term,
        among_conv(conv_w_term),
        among_conv(conv_b_term),
        among_heads(small_term[0, :heads], heads, all_heads),
        among_heads(small_term[1, :heads], heads, all_heads),
        among_heads(skip_heads, heads, all_heads),
        among_heads(gain_term[0], width, inner),
    ]
    vector = jnp.concatenate(terms)
    padding = -vector.shape[0] % (8 * LANES)
    vector = jnp.pad(vector, (0, padding)).reshape(-1, LANES)
    vector, input_grad = together(vector, input_grad)
    vector = sum_all(vector).reshape(-1)
    parts, offset = [], 0
    for term in terms:
        parts.append(vector[offset : offset + term.shape[0]])
        offset += term.shape[0]
    return (
        block_out[None],
        input_grad[None],
        parts[0],
        in_weight_grad,
        parts[1].reshape(conv_weight.shape),
        parts[2],
        parts[3],
        parts[4],
        parts[5],
        parts[6],
        out_weight_grad,
    )


def solution(mesh):
    placed = (
        P("batch", "seq", None),
        P(),
        P("batch", None),
        P(),
        P(),
        P(),
        P(),
        P(),
        P(),
        P("batch", None),
        P("batch", "seq", None),
    )
    return jax.shard_map(
        body,
        mesh=mesh,
        in_specs=placed,
        out_specs=(
            P("batch", "seq", None),
            P("batch", "seq", None),
            P(),
            P("batch", None),
            P(),
            P(),
            P(),
            P(),
            P(),
            P(),
            P("batch", None),
        ),
        check_vma=False,
    )
```

```python
import functools

import jax
import jax.numpy as jnp
from jax import lax
from jax.experimental import pallas as pl
from jax.experimental.pallas import tpu as pltpu
from jax.sharding import PartitionSpec as P

GROUP = 256
LANES = 128
HALO = 8
STEP_ROWS = 16
BACKWARD_CALLS = 2
epsilon = 1e-05
highest = lax.Precision.HIGHEST
f32 = jnp.float32
bf16 = jnp.bfloat16
MIB = 2**20


def exchange(value, axis, distance):
    count = lax.axis_size(axis)
    return lax.ppermute(value, axis, [(source, source ^ distance) for source in range(count)])


def bits_of(count):
    return [1 << k for k in range(count.bit_length() - 1)]


def placed_order(count):
    return [2 * k for k in range(count // 2)] + [2 * k + 1 for k in range(count // 2)]


def together(*values):
    return lax.optimization_barrier(values)


def far_orders():
    far = bits_of(lax.axis_size("seq"))[1:]
    return far, far[::-1]


def gather_start(value):
    half = value.shape[0] // 32 * 16
    return tuple({"base": part, "fresh": None, "near": []} for part in (value[:half], value[half:]))


def gather_stage(held, stage):
    grown = []
    for half, order in zip(held, far_orders()):
        base, fresh, near = half["base"], half["fresh"], list(half["near"])
        if stage >= 1:
            merged = base if stage == len(order) else jnp.concatenate([base, fresh], axis=0)
            near.append(exchange(merged if stage == 1 else fresh, "seq", 1))
            base = merged
        if stage < len(order):
            fresh = exchange(base, "seq", order[stage])
        grown.append({"base": base, "fresh": fresh, "near": near})
    return tuple(grown)


def gather_stages():
    return len(bits_of(lax.axis_size("seq")))


def gathered(held):
    arrays, table = [], {}
    for number, (half, order) in enumerate(zip(held, far_orders())):
        indices = [0]
        for bit in order:
            indices += [index | bit for index in indices]
        middle = len(indices) // 2
        groups = [(half["base"], indices[:middle]), (half["fresh"], indices[middle:])]
        bounds = [0] + [2 << k for k in range(len(order))]
        for value, first, last in zip(half["near"], bounds, bounds[1:]):
            groups.append((value, [index | 1 for index in indices[first:last]]))
        for value, members in groups:
            rows = value.shape[0] // len(members)
            for turn, index in enumerate(members):
                table[number, index] = (len(arrays), turn * rows)
            arrays.append(value)
    return arrays, table


def placed_pieces(held):
    arrays, table = gathered(held)
    order = placed_order(lax.axis_size("seq"))
    return arrays, tuple(table[half, index] for index in order for half in range(2))


def gather_all(value):
    held = gather_start(value)
    for stage in range(gather_stages()):
        held = gather_stage(held, stage)
    return held


def scatter_near(keep, send):
    total = (keep.astype(f32) + exchange(send, "seq", 1).astype(f32)).astype(bf16)
    count = lax.axis_size("seq")
    half = total.shape[0] // count
    total = total.reshape((count // 2, 2, half) + total.shape[1:])
    held = []
    for part, order in enumerate(far_orders()):
        members = [0]
        for bit in order[::-1]:
            members += [member | bit >> 1 for member in members]
        held.append(jnp.stack([total[member, part] for member in members]))
    return tuple(held)


def scatter_stage(held, stage):
    smaller = []
    for value, order in zip(held, far_orders()):
        middle = value.shape[0] // 2
        arriving = exchange(value[middle:], "seq", order[stage])
        smaller.append((value[:middle].astype(f32) + arriving.astype(f32)).astype(bf16))
    return tuple(smaller)


def scatter_end(held):
    return jnp.concatenate([value[0] for value in held], axis=0)


def sum_seq(value):
    for bit in bits_of(lax.axis_size("seq")):
        value = value + exchange(value, "seq", bit)
    return value


def sum_all(value):
    for axis in ("seq", "batch"):
        for bit in bits_of(lax.axis_size(axis)):
            value = value + exchange(value, axis, bit)
    return value


def plane_scatter_start(value):
    planes, plane = lax.axis_size("batch"), lax.axis_index("batch")
    return {
        o: lax.dynamic_index_in_dim(value, jnp.clip(plane + o, 0, planes - 1), 0, keepdims=False)
        for o in range(1 - planes, planes)
    }


def plane_scatter_round(held, turn):
    planes = lax.axis_size("batch")
    far = planes - 1 - turn
    held = dict(held)
    for sign in (1, -1):
        sources = [k for k in range(planes) if 0 <= k + sign * far < planes]
        pairs = [(k, k + sign) for k in sources]
        arriving = lax.ppermute(held.pop(sign * far), "batch", pairs)
        nearer = sign * (far - 1)
        held[nearer] = (held[nearer].astype(f32) + arriving.astype(f32)).astype(bf16)
    return held


def plane_pairs(ahead):
    planes, count = lax.axis_size("batch"), lax.axis_size("seq")
    per = count // planes
    pairs = []
    for owner in range(planes):
        for piece in range(planes):
            for k in range(per):
                holder = owner * count + piece * per + k
                user = (piece + ahead) % planes * count + owner * per + k
                pairs.append((holder, user))
    return pairs


def rows_from_owner(out_weight, width, aheads):
    planes, count = lax.axis_size("batch"), lax.axis_size("seq")
    per, size = count // planes, width // planes
    mine = lax.axis_index("seq")
    piece = lax.dynamic_slice_in_dim(out_weight, mine % per * width + mine // per * size, size, 0)
    return [lax.ppermute(piece, ("batch", "seq"), plane_pairs(ahead)) for ahead in aheads]


def rows_joined(arriving):
    planes, plane = lax.axis_size("batch"), lax.axis_index("batch")
    size = arriving[0].shape[0]
    doubled = jnp.concatenate(arriving[::-1] * 2, axis=0)
    return lax.dynamic_slice_in_dim(doubled, (planes - 1 - plane) * size, planes * size, 0)


def to_owner(summed):
    return lax.ppermute(
        summed, ("batch", "seq"), [(user, holder) for holder, user in plane_pairs(0)]
    )


def double(held, turn):
    bits = bits_of(lax.axis_size("seq"))
    return jnp.concatenate([held, exchange(held, "seq", (bits[1:] + [1])[turn])], axis=0)


def step_values(raw):
    small = jnp.exp(-jnp.abs(raw))
    step = jnp.maximum(raw, 0.0) + jnp.log1p(small)
    sig = jnp.where(raw >= 0, 1.0, small) / (1.0 + small)
    tiny = raw < -20.0
    log_step = jnp.where(tiny, raw, jnp.log(step))
    ratio = jnp.where(tiny, 1.0, sig / step)
    return step, sig, log_step, ratio


def spread_heads(value, heads, size):
    rows = value.shape[0]
    return jnp.concatenate(
        [jnp.broadcast_to(value[:, h : h + 1], (rows, size)) for h in range(heads)], axis=1
    )


def sum_heads(value, size):
    width = value.shape[1]
    row = lax.broadcasted_iota(jnp.int32, (width, LANES), 0) // size
    lane = lax.broadcasted_iota(jnp.int32, (width, LANES), 1)
    ones = (row == lane).astype(f32)
    return jnp.dot(value, ones, precision=highest, preferred_element_type=f32)


def sum_lanes(value):
    return dot_nt(jnp.ones((8, value.shape[1]), bf16), value.astype(bf16))


def order_masks(length):
    row = lax.broadcasted_iota(jnp.int32, (length, length), 0)
    column = lax.broadcasted_iota(jnp.int32, (length, length), 1)
    return row, column


def dot(a, b):
    return jnp.dot(a, b, preferred_element_type=f32)


def dot_nt(a, b):
    return lax.dot_general(a, b, (((1,), (1,)), ((), ())), preferred_element_type=f32)


def dot_tn(a, b):
    return lax.dot_general(a, b, (((0,), (0,)), ((), ())), preferred_element_type=f32)


def sigmoid(value):
    return 1.0 / (1.0 + jnp.exp(-value))


def mixed(padded, conv_w, conv_b):
    taps = conv_w.shape[0]
    total = conv_b
    for k in range(taps):
        start = HALO - (taps - 1) + k
        total = total + conv_w[k : k + 1] * padded[start : start + GROUP]
    return total


def fetch(arrays, table, which, buffer, semaphores, slot):
    for index, (array, row) in enumerate(table):

        @pl.when(which == index)
        def _():
            source = arrays[array].at[pl.ds(row, GROUP)]
            pltpu.make_async_copy(source, buffer.at[slot], semaphores.at[slot]).start()


def fetched(arrays, table, buffer, semaphores, order):
    step = pl.program_id(0)
    slot = lax.rem(step, 2)

    @pl.when(step == 0)
    def _():
        fetch(arrays, table, order(0), buffer, semaphores, 0)

    @pl.when(step + 1 < pl.num_programs(0))
    def _():
        fetch(arrays, table, order(step + 1), buffer, semaphores, lax.rem(step + 1, 2))

    source = arrays[0].at[pl.ds(0, GROUP)]
    pltpu.make_async_copy(source, buffer.at[slot], semaphores.at[slot]).wait()
    return buffer[slot]


def block_place(place, block, count):
    relative = (block // 2) ^ place
    order = (relative & 1) * (count // 2) + (relative >> 1)
    return order * 2 + block % 2


def forward_kernel(dims, table, given, place_ref, *refs):
    heads, size, states, count = dims
    width = heads * size
    conv_cols = width + 2 * states
    arrays, refs = refs[:given], refs[given:]
    w_ref, conv_w_ref, conv_b_ref, step_ref, rows_ref = refs[:5]
    conv_in_ref, gate_ref, raw_ref, ssd_ref, start_ref, scaled_ref, square_ref = refs[5:12]
    placed_ref, normed_ref, state, padded, buffer, semaphores = refs[12:]

    @pl.when(pl.program_id(0) == 0)
    def _():
        state[...] = jnp.zeros_like(state)
        padded[0:HALO] = jnp.zeros_like(padded[0:HALO])

    normed = fetched(
        arrays, table, buffer, semaphores, lambda step: block_place(place_ref[0], step, count)
    )
    normed_ref[...] = normed
    projected = dot(normed, w_ref[...])
    gate = projected[:, :width]
    conv_in = projected[:, width : width + conv_cols].astype(bf16)
    raw = projected[:, width + conv_cols :]
    padded[HALO : HALO + GROUP] = conv_in.astype(f32)
    pre = mixed(padded, conv_w_ref[...], conv_b_ref[...])
    padded[0:HALO] = padded[GROUP : GROUP + HALO]
    active = (pre * sigmoid(pre)).astype(bf16)
    signal = active[:, :width]
    entry = active[:, width : width + states]
    readout = active[:, width + states :]
    signal_wide = signal.astype(f32)

    step, _, log_step, _ = step_values(raw + step_ref[0:1])
    decay = step * step_ref[1:2]
    row, column = order_masks(GROUP)
    running = jnp.dot(
        (row >= column).astype(f32), decay, precision=highest, preferred_element_type=f32
    )
    later = running - log_step
    total = running[GROUP - 1 : GROUP]
    later_rows = later.T
    scores = dot_nt(readout, entry)
    start = state[...]
    start_ref[0] = start
    carried = dot(readout, start.astype(bf16)) * spread_heads(jnp.exp(running), heads, size)
    within = []
    for h in range(heads):
        spread = running[:, h : h + 1] - later_rows[h : h + 1, :]
        kernel = jnp.exp(jnp.where(row >= column, spread, -1e30))
        weights = (scores * kernel).astype(bf16)
        within.append(dot(weights, signal[:, h * size : (h + 1) * size]))
    ssd = jnp.concatenate(within, axis=1) + carried + rows_ref[0:1] * signal_wide
    tail = (signal_wide * spread_heads(jnp.exp(total - later), heads, size)).astype(bf16)
    state[...] = start * spread_heads(jnp.exp(total), heads, size) + dot_tn(entry, tail)

    gated = ssd * (gate * sigmoid(gate))
    conv_in_ref[...] = conv_in
    gate_ref[...] = gate.astype(bf16)
    raw_ref[...] = raw
    ssd_ref[...] = ssd
    scaled = (gated * rows_ref[1:2]).astype(bf16)
    scaled_ref[...] = scaled
    placed_ref[...] = scaled
    square_ref[0] = sum_lanes(gated * gated)


def time_estimate(microseconds, accessed):
    return pl.CostEstimate(
        flops=int(microseconds * 1.1e9), bytes_accessed=int(accessed), transcendentals=0
    )


def fixed(shape):
    return pl.BlockSpec(shape, lambda turn, place: (0,) * len(shape), pipeline_mode=pl.Buffered(1))


def anywhere(values):
    return [pl.BlockSpec(memory_space=pl.ANY)] * len(values)


def run_forward(place, pieces, params, dims):
    heads, size, states, count = dims
    w_cols, conv_w, conv_b, _, _ = params
    dim = w_cols.shape[0]
    width, conv_cols = heads * size, conv_w.shape[1]
    arrays, table = pieces
    blocks = len(table)
    tokens = blocks * GROUP

    def moving(columns):
        return pl.BlockSpec((GROUP, columns), lambda turn, place: (turn, 0))

    def placed(columns):
        return pl.BlockSpec(
            (GROUP, columns), lambda turn, place: (block_place(place[0], turn, count), 0)
        )

    return pl.pallas_call(
        functools.partial(forward_kernel, dims, table, len(arrays)),
        grid_spec=pltpu.PrefetchScalarGridSpec(
            num_scalar_prefetch=1,
            grid=(blocks,),
            in_specs=[*anywhere(arrays), *[fixed(param.shape) for param in params]],
            out_specs=[
                moving(conv_cols),
                moving(width),
                moving(LANES),
                moving(width),
                pl.BlockSpec((1, states, width), lambda turn, place: (turn, 0, 0)),
                moving(width),
                pl.BlockSpec((1, 8, GROUP), lambda turn, place: (turn, 0, 0)),
                placed(width),
                placed(dim),
            ],
            scratch_shapes=[
                pltpu.VMEM((states, width), f32),
                pltpu.VMEM((HALO + GROUP, conv_cols), f32),
                pltpu.VMEM((2, GROUP, dim), bf16),
                pltpu.SemaphoreType.DMA((2,)),
            ],
        ),
        out_shape=[
            jax.ShapeDtypeStruct((tokens, conv_cols), bf16),
            jax.ShapeDtypeStruct((tokens, width), bf16),
            jax.ShapeDtypeStruct((tokens, LANES), f32),
            jax.ShapeDtypeStruct((tokens, width), f32),
            jax.ShapeDtypeStruct((blocks, states, width), f32),
            jax.ShapeDtypeStruct((tokens, width), bf16),
            jax.ShapeDtypeStruct((blocks, 8, GROUP), f32),
            jax.ShapeDtypeStruct((tokens, width), bf16),
            jax.ShapeDtypeStruct((tokens, dim), bf16),
        ],
        compiler_params=pltpu.CompilerParams(vmem_limit_bytes=40 * MIB),
        cost_estimate=time_estimate(blocks * 3.3, tokens * (4 * dim + 12 * width)),
        name="forward_blocks",
    )(place, *arrays, *params)


def backward_kernel(dims, last_block, earlier, place_ref, *refs):
    heads, size, states, count = dims
    width = heads * size
    conv_in_ref, before_ref, gate_ref, raw_ref, ssd_ref, start_ref, out_grad_ref = refs[:7]
    norm_ref, w_ref, conv_w_ref, conv_b_ref, step_ref, rows_ref = refs[7:13]
    given = refs[13:20]
    refs = refs[20 + earlier :]
    out_ref, keep_ref, send_ref = refs[:3]
    state, pre_tail, gain_ref, skip_ref, conv_wg_ref, conv_bg_ref, small_ref = refs[3:10]
    padded, pre_grads, partial, semaphores = refs[10:]
    taps = conv_w_ref.shape[0]
    turn = pl.program_id(0)
    block = last_block - turn

    @pl.when(turn == 0)
    def _():
        for source, target in zip(
            given, (state, pre_tail, gain_ref, skip_ref, conv_wg_ref, conv_bg_ref, small_ref)
        ):
            target[...] = source[...]

    gate, ssd, out_grad = gate_ref[...].astype(f32), ssd_ref[...], out_grad_ref[...]
    norms = norm_ref[0].T
    scale, slope = norms[:, 0:1], norms[:, 1:2]
    gate_sig = sigmoid(gate)
    gate_act = gate * gate_sig
    gated = ssd * gate_act
    gain_ref[...] += jnp.sum(out_grad * (gated * scale), axis=0, keepdims=True)
    gated_grad = out_grad * rows_ref[1:2] * scale - gated * slope
    ssd_grad = gated_grad * gate_act
    gate_grad = gated_grad * ssd * (gate_sig * (1.0 + gate * (1.0 - gate_sig)))

    previous = before_ref[...].astype(f32)[16 - HALO :]
    padded[0:HALO] = jnp.where(block > 0, previous, 0.0)
    padded[HALO : HALO + GROUP] = conv_in_ref[...].astype(f32)
    conv_w = conv_w_ref[...]
    pre = mixed(padded, conv_w, conv_b_ref[...])
    pre_sig = sigmoid(pre)
    active = (pre * pre_sig).astype(bf16)
    signal = active[:, :width]
    entry = active[:, width : width + states]
    readout = active[:, width + states :]
    signal_wide = signal.astype(f32)

    raw = raw_ref[...] + step_ref[0:1]
    lane = lax.broadcasted_iota(jnp.int32, raw.shape, 1)
    step, sig, log_step, ratio = step_values(raw)
    decay = step * step_ref[1:2]
    row, column = order_masks(GROUP)
    running = jnp.dot(
        (row >= column).astype(f32), decay, precision=highest, preferred_element_type=f32
    )
    later = running - log_step
    total = running[GROUP - 1 : GROUP]
    running_rows = running.T

    start = start_ref[0]
    end_grad = state[...]
    grad_low = ssd_grad.astype(bf16)
    start_low, end_low = start.astype(bf16), end_grad.astype(bf16)
    scores = dot_nt(entry, readout)
    score_grad = jnp.zeros_like(scores)
    within = []
    for h in range(heads):
        part = slice(h * size, (h + 1) * size)
        spread = running_rows[h : h + 1, :] - later[:, h : h + 1]
        kernel = jnp.exp(jnp.where(column >= row, spread, -1e30))
        weights = (scores * kernel).astype(bf16)
        within.append(dot(weights, grad_low[:, part]))
        score_grad = score_grad + dot_nt(signal[:, part], grad_low[:, part]) * kernel
    tail_wide = spread_heads(jnp.exp(total - later), heads, size)
    tail_grad = tail_wide * dot(entry, end_low)
    signal_grad = jnp.concatenate(within, axis=1) + tail_grad
    score_low = score_grad.astype(bf16)
    tail = (signal_wide * tail_wide).astype(bf16)
    head_grad = (ssd_grad * spread_heads(jnp.exp(running), heads, size)).astype(bf16)
    entry_grad = dot(score_low, readout) + dot_nt(tail, end_low)
    readout_grad = dot_tn(score_low, entry) + dot_nt(head_grad, start_low)
    total_wide = spread_heads(jnp.exp(total), heads, size)
    state[...] = end_grad * total_wide + dot_tn(readout, head_grad)

    skip = rows_ref[0:1]
    column_part = sum_heads(signal_wide * signal_grad, size)
    row_part = sum_heads(grad_low.astype(f32) * (ssd - skip * signal_wide), size)
    end_part = jnp.sum(signal_wide * tail_grad, axis=0, keepdims=True) + total_wide * jnp.sum(
        start * end_grad, axis=0, keepdims=True
    )
    end_part = sum_heads(jnp.broadcast_to(end_part, (8, width)), size)[0:1]
    decay_grad = (
        jnp.dot(
            (column >= row).astype(f32),
            row_part - column_part,
            precision=highest,
            preferred_element_type=f32,
        )
        + end_part
    )
    raw_grad = column_part * ratio + decay_grad * step_ref[1:2] * sig
    raw_grad = jnp.where(lane < heads, raw_grad, 0.0)
    skip_ref[...] += jnp.sum(ssd_grad * signal_wide, axis=0, keepdims=True)
    small_ref[0:1] += jnp.sum(raw_grad, axis=0, keepdims=True)
    small_ref[1:2] += jnp.sum(decay_grad * decay, axis=0, keepdims=True)

    active_grad = jnp.concatenate([signal_grad + skip * ssd_grad, entry_grad, readout_grad], axis=1)
    pre_grad = active_grad * (pre_sig * (1.0 + pre * (1.0 - pre_sig)))
    pre_grads[0:GROUP] = pre_grad
    pre_grads[GROUP : GROUP + HALO] = pre_tail[...]
    conv_grad = jnp.zeros_like(pre_grad)
    for k in range(taps):
        ahead = taps - 1 - k
        conv_grad = conv_grad + conv_w[k : k + 1] * pre_grads[ahead : ahead + GROUP]
        first = HALO - ahead
        conv_wg_ref[k : k + 1] += jnp.sum(
            pre_grad * padded[first : first + GROUP], axis=0, keepdims=True
        )
    conv_bg_ref[...] += jnp.sum(pre_grad, axis=0, keepdims=True)
    pre_tail[...] = pre_grads[0:HALO]
    projected_grad = jnp.concatenate([gate_grad, conv_grad, raw_grad], axis=1).astype(bf16)
    out_ref[...] = projected_grad

    slot = lax.rem(turn, 2)

    def copy_to(target, row):
        return pltpu.make_async_copy(
            partial.at[slot], target.at[pl.ds(row, GROUP)], semaphores.at[slot]
        )

    @pl.when(turn >= 2)
    def _():
        copy_to(keep_ref, 0).wait()

    partial[slot] = dot_nt(projected_grad, w_ref[...]).astype(bf16)
    position = block_place(place_ref[0], block, count)

    @pl.when(position < count)
    def _():
        copy_to(keep_ref, pl.multiple_of(position * GROUP, GROUP)).start()

    @pl.when(position >= count)
    def _():
        copy_to(send_ref, pl.multiple_of((position - count) * GROUP, GROUP)).start()

    @pl.when(turn == pl.num_programs(0) - 1)
    def _():
        for other in range(2):
            pltpu.make_async_copy(
                partial.at[other], keep_ref.at[pl.ds(0, GROUP)], semaphores.at[other]
            ).wait()


def backward_call(call, place, values, params, dims, outputs, carried):
    heads, size, states, count = dims
    conv_in, gate, raw, ssd, starts, out_grad, norms = values
    w_cols, conv_w = params[:2]
    tokens, width = ssd.shape
    dim, conv_cols = w_cols.shape[0], conv_w.shape[1]
    blocks = tokens // GROUP
    share = blocks // BACKWARD_CALLS
    last = blocks - 1 - call * share
    ratio = GROUP // 16
    out_cols = width + conv_cols + LANES

    def moving(columns):
        return pl.BlockSpec((GROUP, columns), lambda turn, place: (last - turn, 0))

    def before(turn, place):
        return (jnp.maximum(last - 1 - turn, 0) * ratio + ratio - 1, 0)

    operands = [place, conv_in, conv_in, gate, raw, ssd, starts, out_grad, norms]
    operands += [*params, *carried, *outputs]
    aliases = {len(operands) - len(outputs) + k: k for k in range(len(outputs))}
    results = pl.pallas_call(
        functools.partial(backward_kernel, dims, last, len(outputs)),
        grid_spec=pltpu.PrefetchScalarGridSpec(
            num_scalar_prefetch=1,
            grid=(share,),
            in_specs=[
                moving(conv_cols),
                pl.BlockSpec((16, conv_cols), before),
                moving(width),
                moving(LANES),
                moving(width),
                pl.BlockSpec((1, states, width), lambda turn, place: (last - turn, 0, 0)),
                moving(width),
                pl.BlockSpec((1, 8, GROUP), lambda turn, place: (last - turn, 0, 0)),
                *[fixed(param.shape) for param in params],
                *[fixed(value.shape) for value in carried],
                *anywhere(outputs),
            ],
            out_specs=[
                pl.BlockSpec(
                    (GROUP, out_cols),
                    lambda turn, place: (block_place(place[0], last - turn, count), 0),
                ),
                pl.BlockSpec(memory_space=pl.ANY),
                pl.BlockSpec(memory_space=pl.ANY),
                *[fixed(value.shape) for value in carried],
            ],
            scratch_shapes=[
                pltpu.VMEM((HALO + GROUP, conv_cols), f32),
                pltpu.VMEM((GROUP + HALO, conv_cols), f32),
                pltpu.VMEM((2, GROUP, dim), bf16),
                pltpu.SemaphoreType.DMA((2,)),
            ],
        ),
        out_shape=[
            jax.ShapeDtypeStruct((tokens, out_cols), bf16),
            jax.ShapeDtypeStruct((tokens // 2, dim), bf16),
            jax.ShapeDtypeStruct((tokens // 2, dim), bf16),
        ]
        + [jax.ShapeDtypeStruct(value.shape, f32) for value in carried],
        input_output_aliases=aliases,
        compiler_params=pltpu.CompilerParams(vmem_limit_bytes=48 * MIB),
        cost_estimate=time_estimate(share * 5.0, share * GROUP * (24 * width + 4 * dim)),
        name="backward_blocks",
    )(*operands)
    return results[:3], results[3:]


def widen_kernel(place_ref, piece_ref, out_ref):
    out_ref[...] = piece_ref[0].astype(f32)


def assemble_out(place, pieces, per):
    count, size, dim = pieces.shape
    groups = count // per

    def source(turn, place):
        relative = (turn % groups * per + turn // groups) ^ place[0]
        return ((relative & 1) * (count // 2) + (relative >> 1), 0, 0)

    return pl.pallas_call(
        widen_kernel,
        grid_spec=pltpu.PrefetchScalarGridSpec(
            num_scalar_prefetch=1,
            grid=(count,),
            in_specs=[pl.BlockSpec((1, size, dim), source)],
            out_specs=pl.BlockSpec((size, dim), lambda turn, place: (turn, 0)),
        ),
        out_shape=jax.ShapeDtypeStruct((count * size, dim), f32),
        cost_estimate=time_estimate(5, count * size * dim * 6),
        name="assemble_out_weight_grad",
    )(place, pieces)


def assemble_kernel(dims, heights, table, place_ref, *refs):
    heads, size, states, count = dims
    width, shared = heads * size, 2 * states
    inner = count * width
    arrays, out_ref, sums = refs[:-2], refs[-2], refs[-1]
    for relative in range(count):
        device = place_ref[0] ^ relative
        parts = []
        for half in range(2):
            array, row = table[half, relative]
            parts.append(arrays[array][row : row + heights[half]].astype(f32))
        rows = jnp.concatenate(parts, axis=0)
        out_ref[pl.ds(pl.multiple_of(device * width, 8), width)] = rows[:width]
        middle = pl.multiple_of(inner + device * width, 8)
        out_ref[pl.ds(middle, width)] = rows[width : 2 * width]
        sums[device] = rows[2 * width :]
    total = sums[0, :shared]
    for device in range(1, count):
        total = total + sums[device, :shared]
    out_ref[2 * inner : 2 * inner + shared] = total
    for device in range(count):
        last = 2 * inner + shared + device * heads
        out_ref[last : last + heads] = sums[device, shared : shared + heads]


def assemble(place, held, dims):
    heads, size, states, count = dims
    arrays, table = gathered(held)
    rows = arrays[0].shape[1]
    out_rows = 2 * count * heads * size + 2 * states + count * heads
    kept = 2 * heads * size + 2 * states + STEP_ROWS
    heights = (kept // 32 * 16, kept - kept // 32 * 16)

    def whole(value):
        return pl.BlockSpec(
            value.shape,
            lambda turn, place: (0,) * len(value.shape),
            pipeline_mode=pl.Buffered(1),
        )

    return pl.pallas_call(
        functools.partial(assemble_kernel, dims, heights, table),
        grid_spec=pltpu.PrefetchScalarGridSpec(
            num_scalar_prefetch=1,
            grid=(1,),
            in_specs=[whole(value) for value in arrays],
            out_specs=pl.BlockSpec(
                (out_rows, rows), lambda turn, place: (0, 0), pipeline_mode=pl.Buffered(1)
            ),
            scratch_shapes=[pltpu.VMEM((count, 2 * states + STEP_ROWS, rows), f32)],
        ),
        out_shape=jax.ShapeDtypeStruct((out_rows, rows), f32),
        compiler_params=pltpu.CompilerParams(vmem_limit_bytes=40 * MIB),
        cost_estimate=time_estimate(8, out_rows * rows * 6),
        name="assemble_in_weight_grad",
    )(place, *arrays)


def body(
    tokens,
    norm_gain,
    in_weight,
    conv_weight,
    conv_bias,
    dt_bias,
    decay_log,
    skip_scale,
    gate_gain,
    out_weight,
    cotangent,
):
    count, mine = lax.axis_size("seq"), lax.axis_index("seq")
    planes = lax.axis_size("batch")
    place = mine.astype(jnp.int32).reshape(1)
    inner, all_heads, conv_all = gate_gain.shape[0], dt_bias.shape[0], conv_bias.shape[0]
    size, states = inner // all_heads, (conv_all - inner) // 2
    heads, width = all_heads // count, inner // count
    dims = (heads, size, states, count)
    shared = 2 * states
    conv_cols = width + shared
    tok_rows = tokens.shape[1]
    per_plane = out_weight.shape[0] // width

    def own(vector, per):
        return lax.dynamic_slice_in_dim(vector, mine * per, per, vector.ndim - 1)

    def own_conv(array):
        return jnp.concatenate([own(array[..., :inner], width), array[..., inner:]], axis=-1)

    def lane_row(vector):
        return jnp.pad(vector, (0, LANES - vector.shape[0]))[None]

    tokens_row = tokens[0].astype(f32)
    inverse = lax.rsqrt(jnp.mean(tokens_row * tokens_row, axis=-1, keepdims=True) + epsilon)
    normed_own = (tokens_row * inverse * norm_gain).astype(bf16)
    w_own = jnp.concatenate(
        [
            own(in_weight[:, :inner], width),
            own_conv(in_weight[:, inner : inner + conv_all]),
            jnp.pad(own(in_weight[:, inner + conv_all :], heads), ((0, 0), (0, LANES - heads))),
        ],
        axis=1,
    )
    w_cols = lax.all_gather(w_own, "batch", axis=0, tiled=True)
    held = gather_all(normed_own)
    w_cols, held, cot_own, out_owned = together(w_cols, held, cotangent[0], out_weight)
    cot = lax.all_gather(cot_own, "seq", axis=0, tiled=True)
    out_rows = rows_joined(rows_from_owner(out_owned, width, range(planes)))

    conv_w, conv_b = own_conv(conv_weight), own_conv(conv_bias)[None]
    step_rows = jnp.concatenate(
        [
            lane_row(own(dt_bias, heads)),
            lane_row(-jnp.exp(own(decay_log, heads))),
            jnp.zeros((6, LANES), f32),
        ],
        axis=0,
    )
    gain_own = own(gate_gain, width)[None]
    rows = jnp.concatenate(
        [jnp.repeat(own(skip_scale, heads), size)[None], gain_own, jnp.zeros((6, width), f32)],
        axis=0,
    )
    params = (w_cols, conv_w, conv_b, step_rows, rows)
    conv_in, gate, raw, ssd, starts, scaled, squares, placed, normed = run_forward(
        place, placed_pieces(held), params, dims
    )

    middle = placed.shape[0] // 2
    out_send = dot(placed[middle:], out_rows).astype(bf16)
    out_send, cot = together(out_send, cot)
    out_grad = jnp.einsum("td,ed->te", cot, out_rows, preferred_element_type=f32)
    slopes = jnp.sum(out_grad * scaled.astype(f32), axis=1)
    sums = sum_seq(jnp.stack([squares[:, 0].reshape(-1), slopes]))
    out_parts = scatter_near(dot(placed[:middle], out_rows), out_send)
    scale = lax.rsqrt(sums[0] / inner + epsilon)
    norms = jnp.stack([scale, scale * scale * scale * sums[1] / inner])
    norms = jnp.pad(norms, ((0, 6), (0, 0))).reshape(8, -1, GROUP).swapaxes(0, 1)
    scaled_cot = (cot.astype(f32) * scale[:, None]).astype(bf16)
    out_term = jnp.einsum("te,td->ed", scaled, scaled_cot, preferred_element_type=f32)
    out_sum = lax.psum_scatter(out_term.astype(bf16), "batch", scatter_dimension=0, tiled=True)

    values = (conv_in, gate, raw, ssd, starts, out_grad, norms)
    stages = gather_stages()
    outputs = []
    carried = [
        jnp.zeros((states, width), f32),
        jnp.zeros((HALO, conv_cols), f32),
        jnp.zeros((1, width), f32),
        jnp.zeros((1, width), f32),
        jnp.zeros(conv_w.shape, f32),
        jnp.zeros(conv_b.shape, f32),
        jnp.zeros((8, LANES), f32),
    ]
    for call in range(BACKWARD_CALLS):
        if call < stages - 1:
            carried, out_parts = together(carried, out_parts)
            out_parts = scatter_stage(out_parts, call)
        if call == 1:
            carried, out_sum = together(carried, out_sum)
            out_pieces = to_owner(out_sum)[None]
        outputs, carried = backward_call(call, place, values, params, dims, outputs, carried)
    for stage in range(BACKWARD_CALLS, stages - 1):
        out_parts = scatter_stage(out_parts, stage)
    _, _, gain_term, skip_term, conv_w_term, conv_b_term, small_term = carried
    outputs, mixed_out, out_pieces = together(outputs, scatter_end(out_parts), out_pieces)
    proj_grad, back_keep, back_send = outputs

    in_term = jnp.einsum("tf,td->fd", proj_grad, normed, preferred_element_type=f32)
    in_low = in_term.astype(bf16)[: width + conv_cols + STEP_ROWS]
    in_low = in_low.reshape(in_low.shape[0], planes, -1).swapaxes(0, 1)
    back_parts = scatter_near(back_keep, back_send)
    in_parts = plane_scatter_start(in_low)
    back_parts, in_parts, out_pieces = together(back_parts, in_parts, out_pieces)
    for stage in range(stages - 1):
        back_parts = scatter_stage(back_parts, stage)
    for turn in range(planes - 1):
        in_parts = plane_scatter_round(in_parts, turn)
    for turn in range(stages):
        out_pieces = double(out_pieces, turn)
    normed_grad, in_sum, out_pieces = together(scatter_end(back_parts), in_parts[0], out_pieces)
    normed_grad = normed_grad.astype(f32)
    cot_row = cotangent[0].astype(f32)
    gained = norm_gain * normed_grad
    slope = inverse * inverse * inverse * jnp.mean(gained * tokens_row, axis=-1, keepdims=True)
    input_grad = cot_row + inverse * gained - tokens_row * slope
    norm_gain_term = jnp.sum(normed_grad * (tokens_row * inverse), axis=0)
    own_scale = lax.dynamic_slice_in_dim(scale, mine * tok_rows, tok_rows, 0)[:, None]
    block_out = (tokens_row + own_scale * mixed_out.astype(f32)).astype(bf16)
    out_weight_grad = assemble_out(place, out_pieces, per_plane)

    in_weight_grad = assemble(place, gather_all(in_sum), dims).T

    def among_heads(vector, per, total):
        return lax.dynamic_update_slice_in_dim(jnp.zeros((total,), f32), vector, mine * per, 0)

    def among_conv(array):
        wide = jnp.zeros((array.shape[0], inner), f32)
        wide = lax.dynamic_update_slice_in_dim(wide, array[:, :width], mine * width, 1)
        return jnp.concatenate([wide, array[:, width:]], axis=1).reshape(-1)

    skip_heads = jnp.sum(skip_term.reshape(heads, size), axis=1)
    terms = [
        norm_gain_term,
        among_conv(conv_w_term),
        among_conv(conv_b_term),
        among_heads(small_term[0, :heads], heads, all_heads),
        among_heads(small_term[1, :heads], heads, all_heads),
        among_heads(skip_heads, heads, all_heads),
        among_heads(gain_term[0], width, inner),
    ]
    vector = jnp.concatenate(terms)
    padding = -vector.shape[0] % (8 * LANES)
    vector = jnp.pad(vector, (0, padding)).reshape(-1, LANES)
    vector = sum_all(vector).reshape(-1)
    parts, offset = [], 0
    for term in terms:
        parts.append(vector[offset : offset + term.shape[0]])
        offset += term.shape[0]
    return (
        block_out[None],
        input_grad[None],
        parts[0],
        in_weight_grad,
        parts[1].reshape(conv_weight.shape),
        parts[2],
        parts[3],
        parts[4],
        parts[5],
        parts[6],
        out_weight_grad,
    )


def solution(mesh):
    placed = (
        P("batch", "seq", None),
        P(),
        P("batch", None),
        P(),
        P(),
        P(),
        P(),
        P(),
        P(),
        P("batch", None),
        P("batch", "seq", None),
    )
    return jax.shard_map(
        body,
        mesh=mesh,
        in_specs=placed,
        out_specs=(
            P("batch", "seq", None),
            P("batch", "seq", None),
            P(),
            P("batch", None),
            P(),
            P(),
            P(),
            P(),
            P(),
            P(),
            P("batch", None),
        ),
        check_vma=False,
    )
```

```python
import functools

import jax
import jax.numpy as jnp
from jax import lax
from jax.experimental import pallas as pl
from jax.experimental.pallas import tpu as pltpu
from jax.sharding import PartitionSpec as P

GROUP = 256
LANES = 128
HALF = GROUP // 2
HALO = 8
STEP_ROWS = 16
BACKWARD_CALLS = 2
LOG2E = 1.4426950408889634
epsilon = 1e-05
f32 = jnp.float32
bf16 = jnp.bfloat16
MIB = 2**20


def exchange(value, axis, distance):
    count = lax.axis_size(axis)
    return lax.ppermute(value, axis, [(source, source ^ distance) for source in range(count)])


def bits_of(count):
    return [1 << k for k in range(count.bit_length() - 1)]


def placed_order(count):
    return [2 * k for k in range(count // 2)] + [2 * k + 1 for k in range(count // 2)]


def together(*values):
    return lax.optimization_barrier(values)


def far_orders():
    far = bits_of(lax.axis_size("seq"))[1:]
    return far, far[::-1]


def gather_start(value):
    half = value.shape[0] // 32 * 16
    return tuple({"base": part, "fresh": None, "near": []} for part in (value[:half], value[half:]))


def gather_stage(held, stage):
    grown = []
    for half, order in zip(held, far_orders()):
        base, fresh, near = half["base"], half["fresh"], list(half["near"])
        if stage >= 1:
            merged = base if stage == len(order) else jnp.concatenate([base, fresh], axis=0)
            near.append(exchange(merged if stage == 1 else fresh, "seq", 1))
            base = merged
        if stage < len(order):
            fresh = exchange(base, "seq", order[stage])
        grown.append({"base": base, "fresh": fresh, "near": near})
    return tuple(grown)


def gather_stages():
    return len(bits_of(lax.axis_size("seq")))


def gathered(held):
    arrays, table = [], {}
    for number, (half, order) in enumerate(zip(held, far_orders())):
        indices = [0]
        for bit in order:
            indices += [index | bit for index in indices]
        middle = len(indices) // 2
        groups = [(half["base"], indices[:middle]), (half["fresh"], indices[middle:])]
        bounds = [0] + [2 << k for k in range(len(order))]
        for value, first, last in zip(half["near"], bounds, bounds[1:]):
            groups.append((value, [index | 1 for index in indices[first:last]]))
        for value, members in groups:
            rows = value.shape[0] // len(members)
            for turn, index in enumerate(members):
                table[number, index] = (len(arrays), turn * rows, rows)
            arrays.append(value)
    return arrays, table


def placed_pieces(held):
    arrays, table = gathered(held)
    order = placed_order(lax.axis_size("seq"))
    return arrays, tuple(table[half, index] for index in order for half in range(2))


def gather_all(value):
    held = gather_start(value)
    for stage in range(gather_stages()):
        held = gather_stage(held, stage)
    return held


def scatter_near(keep, send):
    total = (keep.astype(f32) + exchange(send, "seq", 1).astype(f32)).astype(bf16)
    count = lax.axis_size("seq")
    half = total.shape[0] // count
    total = total.reshape((count // 2, 2, half) + total.shape[1:])
    held = []
    for part, order in enumerate(far_orders()):
        members = [0]
        for bit in order[::-1]:
            members += [member | bit >> 1 for member in members]
        held.append(jnp.stack([total[member, part] for member in members]))
    return tuple(held)


def scatter_stage(held, stage):
    smaller = []
    for value, order in zip(held, far_orders()):
        middle = value.shape[0] // 2
        arriving = exchange(value[middle:], "seq", order[stage])
        smaller.append((value[:middle].astype(f32) + arriving.astype(f32)).astype(bf16))
    return tuple(smaller)


def scatter_end(held):
    return jnp.concatenate([value[0] for value in held], axis=0)


def sum_seq(value):
    for bit in bits_of(lax.axis_size("seq")):
        value = value + exchange(value, "seq", bit)
    return value


def sum_all(value):
    for axis in ("seq", "batch"):
        for bit in bits_of(lax.axis_size(axis)):
            value = value + exchange(value, axis, bit)
    return value


def plane_pairs(ahead):
    planes, count = lax.axis_size("batch"), lax.axis_size("seq")
    per = count // planes
    pairs = []
    for owner in range(planes):
        for piece in range(planes):
            for k in range(per):
                holder = owner * count + piece * per + k
                user = (piece + ahead) % planes * count + owner * per + k
                pairs.append((holder, user))
    return pairs


def rows_from_owner(out_weight, width, aheads):
    planes, count = lax.axis_size("batch"), lax.axis_size("seq")
    per, size = count // planes, width // planes
    mine = lax.axis_index("seq")
    piece = lax.dynamic_slice_in_dim(out_weight, mine % per * width + mine // per * size, size, 0)
    return [lax.ppermute(piece, ("batch", "seq"), plane_pairs(ahead)) for ahead in aheads]


def rows_joined(arriving):
    planes, plane = lax.axis_size("batch"), lax.axis_index("batch")
    size = arriving[0].shape[0]
    doubled = jnp.concatenate(arriving[::-1] * 2, axis=0)
    return lax.dynamic_slice_in_dim(doubled, (planes - 1 - plane) * size, planes * size, 0)


def to_owner(summed):
    return lax.ppermute(
        summed, ("batch", "seq"), [(user, holder) for holder, user in plane_pairs(0)]
    )


def double(held, turn):
    bits = bits_of(lax.axis_size("seq"))
    return jnp.concatenate([held, exchange(held, "seq", (bits[1:] + [1])[turn])], axis=0)


def step_values(raw):
    small = jnp.exp(-jnp.abs(raw))
    step = jnp.maximum(raw, 0.0) + jnp.log1p(small)
    sig = jnp.where(raw >= 0, 1.0, small) / (1.0 + small)
    tiny = raw < -20.0
    log_step = jnp.where(tiny, raw, jnp.log(step))
    ratio = jnp.where(tiny, 1.0, sig / step)
    return step, sig, log_step, ratio


def dot(a, b):
    return jnp.dot(a, b, preferred_element_type=f32)


def dot_nt(a, b):
    return lax.dot_general(a, b, (((1,), (1,)), ((), ())), preferred_element_type=f32)


def dot_tn(a, b):
    return lax.dot_general(a, b, (((0,), (0,)), ((), ())), preferred_element_type=f32)


def sigmoid(value):
    return 0.5 * jnp.tanh(0.5 * value) + 0.5


def silu_slope(value):
    sig = sigmoid(value)
    active = value * sig
    return active, sig + active * (1.0 - sig)


def split_parts(value, count):
    parts = []
    for _ in range(count):
        part = value.astype(bf16)
        parts.append(part)
        value = value - part.astype(f32)
    return parts


def sum_along(rows, order):
    parts = jnp.concatenate([part.astype(f32) for part in split_parts(rows, 3)], axis=0)
    total = dot(parts.astype(bf16), order)
    return total[:8] + total[8:16] + total[16:24]


def to_columns(rows):
    stacked = jnp.concatenate(rows, axis=0)
    missing = LANES - stacked.shape[0]
    return jnp.concatenate([stacked, jnp.zeros((missing, GROUP), f32)], axis=0).T


def spread_heads(value, first, heads, size):
    rows = value.shape[0]
    return jnp.concatenate(
        [jnp.broadcast_to(value[:, first + h : first + h + 1], (rows, size)) for h in range(heads)],
        axis=1,
    )


def head_ones(width, size):
    row = lax.broadcasted_iota(jnp.int32, (8, width), 0)
    column = lax.broadcasted_iota(jnp.int32, (8, width), 1)
    return (column // size == row).astype(f32).astype(bf16)


def sum_lanes(value):
    return dot_nt(jnp.ones((8, value.shape[1]), bf16), value.astype(bf16))


def ones_where(condition):
    return jnp.where(condition, 1.0, 0.0).astype(bf16)


def order_indices(length):
    row = lax.broadcasted_iota(jnp.int32, (length, length), 0)
    column = lax.broadcasted_iota(jnp.int32, (length, length), 1)
    return row, column


def fetch(arrays, table, which, buffer, semaphores, slot):
    for index, (array, row, _) in enumerate(table):

        @pl.when(which == index)
        def _():
            source = arrays[array].at[pl.ds(row, GROUP)]
            pltpu.make_async_copy(source, buffer.at[slot], semaphores.at[slot]).start()


def fetched(arrays, table, buffer, semaphores, order):
    step = pl.program_id(0)
    slot = lax.rem(step, 2)

    @pl.when(step == 0)
    def _():
        fetch(arrays, table, order(0), buffer, semaphores, 0)

    @pl.when(step + 1 < pl.num_programs(0))
    def _():
        fetch(arrays, table, order(step + 1), buffer, semaphores, lax.rem(step + 1, 2))

    source = arrays[0].at[pl.ds(0, GROUP)]
    pltpu.make_async_copy(source, buffer.at[slot], semaphores.at[slot]).wait()
    return buffer[slot]


def block_place(place, block, count):
    relative = (block // 2) ^ place
    order = (relative & 1) * (count // 2) + (relative >> 1)
    return order * 2 + block % 2


def forward_kernel(dims, table, given, place_ref, *refs):
    heads, size, states, count = dims
    width = heads * size
    conv_cols = width + 2 * states
    arrays, refs = refs[:given], refs[given:]
    w_ref, conv_w_ref, conv_b_ref, step_ref, rows_ref = refs[:5]
    conv_in_ref, active_ref, slope_ref, gate_act_ref, gate_slope_ref = refs[5:10]
    raw_ref, ssd_ref, start_ref, scaled_ref, square_ref, placed_ref, normed_ref = refs[10:17]
    state, padded, order, barred, buffer, semaphores = refs[17:]

    @pl.when(pl.program_id(0) == 0)
    def _():
        state[...] = jnp.zeros_like(state)
        padded[0:HALO] = jnp.zeros_like(padded[0:HALO])
        row, column = order_indices(GROUP)
        order[...] = ones_where(row <= column)
        row, column = order_indices(HALF)
        barred[...] = jnp.where(row >= column, 0.0, -1e30)

    normed = fetched(
        arrays, table, buffer, semaphores, lambda step: block_place(place_ref[0], step, count)
    )
    normed_ref[...] = normed
    projected = dot(normed, w_ref[...])
    conv_in = projected[:, width : width + conv_cols].astype(bf16)
    conv_in_ref[...] = conv_in
    padded[HALO : HALO + GROUP] = conv_in.astype(f32)
    conv_w = conv_w_ref[...]
    taps = conv_w.shape[0]
    pre = conv_b_ref[...]
    for k in range(taps):
        top = HALO - (taps - 1) + k
        pre = pre + conv_w[k : k + 1] * padded[top : top + GROUP]
    padded[0:HALO] = padded[GROUP : GROUP + HALO]
    active, slope = silu_slope(pre)
    active = active.astype(bf16)
    active_ref[...] = active
    slope_ref[...] = slope.astype(bf16)
    signal = active[:, :width]
    entry = active[:, width : width + states]
    readout = active[:, width + states :]
    signal_wide = signal.astype(f32)

    raw = projected[:, width + conv_cols :].T[:8]
    raw_ref[0] = raw
    step, _, log_step, _ = step_values(raw + step_ref[0:8, 0:1])
    running = sum_along(step * step_ref[8:16, 0:1], order[...])
    later = running - log_step
    total = running[:, GROUP - 1 :]
    columns = to_columns([running * LOG2E, jnp.exp(running), jnp.exp(total - later)])
    later = later * LOG2E
    early_wide = spread_heads(columns, 8, heads, size)
    tail_wide = spread_heads(columns, 16, heads, size)
    first, second = slice(0, HALF), slice(HALF, GROUP)
    scores = dot_nt(readout[first], entry[first])
    later_scores = dot_nt(readout[second], entry)
    within = []
    for h in range(heads):
        part = signal[:, h * size : (h + 1) * size]
        begin, end = columns[first, h : h + 1], columns[second, h : h + 1]
        row_first, row_second = later[h : h + 1, first], later[h : h + 1, second]
        near = jnp.exp2(begin - row_first + barred[...]) * scores
        full = jnp.exp2(end - row_first) * later_scores[:, first]
        last = jnp.exp2(end - row_second + barred[...]) * later_scores[:, second]
        both = jnp.concatenate([full.astype(bf16), last.astype(bf16)], axis=1)
        within.append(
            jnp.concatenate([dot(near.astype(bf16), part[first]), dot(both, part)], axis=0)
        )
    start = state[...]
    start_low = start.astype(bf16)
    start_ref[0] = start_low
    carried = dot(readout, start_low) * early_wide
    ssd = jnp.concatenate(within, axis=1) + carried + rows_ref[0:1] * signal_wide
    tail = (signal_wide * tail_wide).astype(bf16)
    state[...] = start * early_wide[GROUP - 1 :] + dot_tn(entry, tail)

    gate_act, gate_slope = silu_slope(projected[:, :width])
    gate_act_ref[...] = gate_act.astype(bf16)
    gate_slope_ref[...] = gate_slope.astype(bf16)
    ssd_ref[...] = ssd
    gated = ssd * gate_act
    scaled = (gated * rows_ref[1:2]).astype(bf16)
    scaled_ref[...] = scaled
    placed_ref[...] = scaled
    square_ref[0] = sum_lanes(gated * gated)


def time_estimate(microseconds, accessed):
    return pl.CostEstimate(
        flops=int(microseconds * 1.1e9), bytes_accessed=int(accessed), transcendentals=0
    )


def fixed(shape):
    return pl.BlockSpec(shape, lambda turn, place: (0,) * len(shape), pipeline_mode=pl.Buffered(1))


def anywhere(values):
    return [pl.BlockSpec(memory_space=pltpu.HBM)] * len(values)


def run_forward(place, pieces, params, dims):
    heads, size, states, count = dims
    w_cols, conv_w, conv_b, _, _ = params
    dim = w_cols.shape[0]
    width, conv_cols = heads * size, conv_w.shape[1]
    arrays, table = pieces
    blocks = len(table)
    tokens = blocks * GROUP

    def moving(columns):
        return pl.BlockSpec((GROUP, columns), lambda turn, place: (turn, 0))

    return pl.pallas_call(
        functools.partial(forward_kernel, dims, table, len(arrays)),
        grid_spec=pltpu.PrefetchScalarGridSpec(
            num_scalar_prefetch=1,
            grid=(blocks,),
            in_specs=[*anywhere(arrays), *[fixed(param.shape) for param in params]],
            out_specs=[
                moving(conv_cols),
                moving(conv_cols),
                moving(conv_cols),
                moving(width),
                moving(width),
                pl.BlockSpec((1, 8, GROUP), lambda turn, place: (turn, 0, 0)),
                moving(width),
                pl.BlockSpec((1, states, width), lambda turn, place: (turn, 0, 0)),
                moving(width),
                pl.BlockSpec((1, 8, GROUP), lambda turn, place: (turn, 0, 0)),
                pl.BlockSpec(
                    (GROUP, width), lambda turn, place: (block_place(place[0], turn, count), 0)
                ),
                moving(dim),
            ],
            scratch_shapes=[
                pltpu.VMEM((states, width), f32),
                pltpu.VMEM((HALO + GROUP, conv_cols), f32),
                pltpu.VMEM((GROUP, GROUP), bf16),
                pltpu.VMEM((HALF, HALF), f32),
                pltpu.VMEM((2, GROUP, dim), bf16),
                pltpu.SemaphoreType.DMA((2,)),
            ],
        ),
        out_shape=[
            jax.ShapeDtypeStruct((tokens, conv_cols), bf16),
            jax.ShapeDtypeStruct((tokens, conv_cols), bf16),
            jax.ShapeDtypeStruct((tokens, conv_cols), bf16),
            jax.ShapeDtypeStruct((tokens, width), bf16),
            jax.ShapeDtypeStruct((tokens, width), bf16),
            jax.ShapeDtypeStruct((blocks, 8, GROUP), f32),
            jax.ShapeDtypeStruct((tokens, width), f32),
            jax.ShapeDtypeStruct((blocks, states, width), bf16),
            jax.ShapeDtypeStruct((tokens, width), bf16),
            jax.ShapeDtypeStruct((blocks, 8, GROUP), f32),
            jax.ShapeDtypeStruct((tokens, width), bf16),
            jax.ShapeDtypeStruct((tokens, dim), bf16),
        ],
        compiler_params=pltpu.CompilerParams(vmem_limit_bytes=40 * MIB),
        cost_estimate=time_estimate(blocks * 2.8, tokens * (4 * dim + 20 * width)),
        name="forward_blocks",
    )(place, *arrays, *params)


def backward_kernel(dims, earlier, place_ref, *refs):
    heads, size, states, _ = dims
    width = heads * size
    conv_cols = width + 2 * states
    conv_in_ref, active_ref, slope_ref, gate_act_ref, gate_slope_ref = refs[:5]
    raw_ref, ssd_ref, start_ref, out_grad_ref, norm_ref = refs[5:10]
    conv_w_ref, step_ref, rows_ref = refs[10:13]
    given = refs[13:21]
    refs = refs[21 + earlier :]
    out_ref, placed_ref = refs[:2]
    carried = refs[2:10]
    state, pre_tail, gain_ref, skip_ref, conv_wg_ref, conv_bg_ref, bias_ref, rate_ref = carried
    pre_grads, order, back_order, barred = refs[10:]
    taps = conv_w_ref.shape[0]

    @pl.when(pl.program_id(0) == 0)
    def _():
        for source, target in zip(given, carried):
            target[...] = source[...]
        row, column = order_indices(GROUP)
        order[...] = ones_where(row <= column)
        back_order[...] = ones_where(row >= column)
        row, column = order_indices(HALF)
        barred[...] = jnp.where(row <= column, 0.0, -1e30)

    gate_act, ssd, out_grad = gate_act_ref[...].astype(f32), ssd_ref[...], out_grad_ref[...]
    norms = norm_ref[0].T
    scale, slope = norms[:, 0:1], norms[:, 1:2]
    gated = ssd * gate_act
    gain_ref[...] += jnp.sum(out_grad * (gated * scale), axis=0, keepdims=True)
    gated_grad = out_grad * (rows_ref[1:2] * scale) - gated * slope
    grad_low = (gated_grad * gate_act).astype(bf16)
    gate_grad = (gated_grad * ssd * gate_slope_ref[...].astype(f32)).astype(bf16)
    out_ref[:, :width] = gate_grad
    placed_ref[:, :width] = gate_grad
    ssd_grad = grad_low.astype(f32)

    raw = raw_ref[0] + step_ref[0:8, 0:1]
    rate = step_ref[8:16, 0:1]
    step, sig, log_step, ratio = step_values(raw)
    decay = step * rate
    running = sum_along(decay, order[...])
    later = running - log_step
    total = running[:, GROUP - 1 :]
    columns = to_columns([later * LOG2E, jnp.exp(running), jnp.exp(total - later)])
    running = running * LOG2E
    early_wide = spread_heads(columns, 8, heads, size)
    tail_wide = spread_heads(columns, 16, heads, size)

    signal = active_ref[:, :width]
    entry = active_ref[:, width : width + states]
    readout = active_ref[:, width + states :]
    signal_wide = signal.astype(f32)
    start_low = start_ref[0]
    end_grad = state[...]
    end_low = end_grad.astype(bf16)
    first, second = slice(0, HALF), slice(HALF, GROUP)
    scores = dot_nt(entry[first], readout)
    later_scores = dot_nt(entry[second], readout[second])
    near_grad, far_grad, last_grad = 0.0, 0.0, 0.0
    within = []
    for h in range(heads):
        part, grad = signal[:, h * size : (h + 1) * size], grad_low[:, h * size : (h + 1) * size]
        begin, end = columns[first, h : h + 1], columns[second, h : h + 1]
        row_first, row_second = running[h : h + 1, first], running[h : h + 1, second]
        near = jnp.exp2(row_first - begin + barred[...])
        full = jnp.exp2(row_second - begin)
        last = jnp.exp2(row_second - end + barred[...])
        both = jnp.concatenate(
            [
                (near * scores[:, first]).astype(bf16),
                (full * scores[:, second]).astype(bf16),
            ],
            axis=1,
        )
        final = (last * later_scores).astype(bf16)
        within.append(jnp.concatenate([dot(both, grad), dot(final, grad[second])], axis=0))
        cross = dot_nt(part[first], grad)
        near_grad = near_grad + cross[:, first] * near
        far_grad = far_grad + cross[:, second] * full
        last_grad = last_grad + dot_nt(part[second], grad[second]) * last
    tail_grad = tail_wide * dot(entry, end_low)
    signal_grad = jnp.concatenate(within, axis=1) + tail_grad
    score_first = jnp.concatenate([near_grad, far_grad], axis=1).astype(bf16)
    score_second = last_grad.astype(bf16)
    tail = (signal_wide * tail_wide).astype(bf16)
    head_grad = (ssd_grad * early_wide).astype(bf16)
    entry_grad = jnp.concatenate(
        [dot(score_first, readout), dot(score_second, readout[second])], axis=0
    ) + dot_nt(tail, end_low)
    readout_grad = dot_tn(score_first, entry[first]) + dot_nt(head_grad, start_low)
    readout_last = readout_grad[second] + dot_tn(score_second, entry[second])
    total_wide = early_wide[GROUP - 1 :]
    state[...] = end_grad * total_wide + dot_tn(readout, head_grad)

    skip = rows_ref[0:1]
    ones = head_ones(width, size)
    column_part = signal_wide * signal_grad
    row_part = ssd_grad * (ssd - skip * signal_wide)
    end_part = jnp.sum(signal_wide * tail_grad, axis=0, keepdims=True) + total_wide * jnp.sum(
        start_low.astype(f32) * end_grad, axis=0, keepdims=True
    )

    def head_sums(value, parts):
        return sum(dot_nt(ones, part) for part in split_parts(value, parts))

    end_rows = head_sums(jnp.broadcast_to(end_part, (8, width)), 2)[:, 0:1]
    decay_grad = sum_along(head_sums(row_part - column_part, 2), back_order[...]) + end_rows
    raw_grad = head_sums(column_part, 1) * ratio + decay_grad * rate * sig
    skip_ref[...] += jnp.sum(ssd_grad * signal_wide, axis=0, keepdims=True)
    bias_ref[...] += raw_grad
    rate_ref[...] += decay_grad * decay
    raw_low = to_columns([raw_grad]).astype(bf16)
    out_ref[:, width + conv_cols :] = raw_low
    placed_ref[:, width + conv_cols :] = raw_low

    pre_grads[0:GROUP, :width] = (signal_grad + skip * ssd_grad) * slope_ref[:, :width].astype(f32)
    sides = slope_ref[:, width:].astype(f32)
    pre_grads[0:GROUP, width : width + states] = entry_grad * sides[:, :states]
    pre_grads[0:HALF, width + states :] = readout_grad[first] * sides[first, states:]
    pre_grads[HALF:GROUP, width + states :] = readout_last * sides[second, states:]
    pre_grads[GROUP : GROUP + HALO] = pre_tail[...]
    pre_tail[...] = pre_grads[0:HALO]
    conv_w = conv_w_ref[...]
    conv_in = conv_in_ref[...].astype(f32)
    conv_grad = 0.0
    for k in range(taps):
        ahead = taps - 1 - k
        shifted = pre_grads[ahead : ahead + GROUP]
        conv_grad = conv_grad + conv_w[k : k + 1] * shifted
        conv_wg_ref[k : k + 1] += jnp.sum(shifted * conv_in, axis=0, keepdims=True)
        if ahead == 0:
            conv_bg_ref[...] += jnp.sum(shifted, axis=0, keepdims=True)
    conv_low = conv_grad.astype(bf16)
    out_ref[:, width : width + conv_cols] = conv_low
    placed_ref[:, width : width + conv_cols] = conv_low


def backward_call(call, place, values, params, dims, outputs, carried):
    heads, size, states, count = dims
    conv_cols, width = values[0].shape[1], heads * size
    tokens = values[0].shape[0]
    blocks = tokens // GROUP
    share = blocks // BACKWARD_CALLS
    last = blocks - 1 - call * share
    out_cols = width + conv_cols + LANES

    def moving(columns):
        return pl.BlockSpec((GROUP, columns), lambda turn, place: (last - turn, 0))

    def rows_of_block():
        return pl.BlockSpec((1, 8, GROUP), lambda turn, place: (last - turn, 0, 0))

    operands = [place, *values, *params, *carried, *outputs]
    aliases = {len(operands) - len(outputs) + k: k for k in range(len(outputs))}
    results = pl.pallas_call(
        functools.partial(backward_kernel, dims, len(outputs)),
        grid_spec=pltpu.PrefetchScalarGridSpec(
            num_scalar_prefetch=1,
            grid=(share,),
            in_specs=[
                moving(conv_cols),
                moving(conv_cols),
                moving(conv_cols),
                moving(width),
                moving(width),
                rows_of_block(),
                moving(width),
                pl.BlockSpec((1, states, width), lambda turn, place: (last - turn, 0, 0)),
                moving(width),
                rows_of_block(),
                *[fixed(param.shape) for param in params],
                *[fixed(value.shape) for value in carried],
                *anywhere(outputs),
            ],
            out_specs=[
                moving(out_cols),
                pl.BlockSpec(
                    (GROUP, out_cols),
                    lambda turn, place: (block_place(place[0], last - turn, count), 0),
                ),
                *[fixed(value.shape) for value in carried],
            ],
            scratch_shapes=[
                pltpu.VMEM((GROUP + HALO, conv_cols), f32),
                pltpu.VMEM((GROUP, GROUP), bf16),
                pltpu.VMEM((GROUP, GROUP), bf16),
                pltpu.VMEM((HALF, HALF), f32),
            ],
        ),
        out_shape=[jax.ShapeDtypeStruct((tokens, out_cols), bf16)] * 2
        + [jax.ShapeDtypeStruct(value.shape, f32) for value in carried],
        input_output_aliases=aliases,
        compiler_params=pltpu.CompilerParams(vmem_limit_bytes=40 * MIB),
        cost_estimate=time_estimate(share * 3.5, share * GROUP * 40 * width),
        name="backward_blocks",
    )(*operands)
    return results[:2], results[2:]


def widen_kernel(place_ref, piece_ref, out_ref):
    out_ref[...] = piece_ref[0].astype(f32)


def assemble_out(place, pieces, per):
    count, size, dim = pieces.shape
    groups = count // per

    def source(turn, place):
        relative = (turn % groups * per + turn // groups) ^ place[0]
        return ((relative & 1) * (count // 2) + (relative >> 1), 0, 0)

    return pl.pallas_call(
        widen_kernel,
        grid_spec=pltpu.PrefetchScalarGridSpec(
            num_scalar_prefetch=1,
            grid=(count,),
            in_specs=[pl.BlockSpec((1, size, dim), source)],
            out_specs=pl.BlockSpec((size, dim), lambda turn, place: (turn, 0)),
        ),
        out_shape=jax.ShapeDtypeStruct((count * size, dim), f32),
        cost_estimate=time_estimate(5, count * size * dim * 6),
        name="assemble_out_weight_grad",
    )(place, pieces)


def assemble_kernel(dims, tables, given, place_ref, *refs):
    heads, size, states, count = dims
    width, shared = heads * size, 2 * states
    inner = count * width
    gates, convs, out_ref, sums = refs[: given[0]], refs[given[0] : given[1]], refs[-2], refs[-1]

    def piece(arrays, table, relative):
        parts = []
        for half in range(2):
            array, row, height = table[half, relative]
            parts.append(arrays[array][row : row + height].astype(f32))
        return jnp.concatenate(parts, axis=0).T

    for relative in range(count):
        device = place_ref[0] ^ relative
        top = pl.multiple_of(device * width, 8)
        out_ref[pl.ds(top, width)] = piece(gates, tables[0], relative)
        middle = pl.multiple_of(inner + device * width, 8)
        columns = piece(convs, tables[1], relative)
        out_ref[pl.ds(middle, width)] = columns[:width]
        sums[device] = columns[width : width + shared + STEP_ROWS]
    total = sums[0, :shared]
    for device in range(1, count):
        total = total + sums[device, :shared]
    out_ref[2 * inner : 2 * inner + shared] = total
    for device in range(count):
        last = 2 * inner + shared + device * heads
        out_ref[last : last + heads] = sums[device, shared : shared + heads]


def assemble(place, gates, convs, dims):
    heads, size, states, count = dims
    gates, gate_table = gathered(gates)
    convs, conv_table = gathered(convs)
    rows = sum(gate_table[half, 0][2] for half in range(2))
    out_rows = 2 * count * heads * size + 2 * states + count * heads

    def whole(value):
        return pl.BlockSpec(
            value.shape,
            lambda turn, place: (0,) * len(value.shape),
            pipeline_mode=pl.Buffered(1),
        )

    return pl.pallas_call(
        functools.partial(
            assemble_kernel, dims, (gate_table, conv_table), (len(gates), len(gates) + len(convs))
        ),
        grid_spec=pltpu.PrefetchScalarGridSpec(
            num_scalar_prefetch=1,
            grid=(1,),
            in_specs=[whole(value) for value in (*gates, *convs)],
            out_specs=pl.BlockSpec(
                (out_rows, rows), lambda turn, place: (0, 0), pipeline_mode=pl.Buffered(1)
            ),
            scratch_shapes=[pltpu.VMEM((count, 2 * states + STEP_ROWS, rows), f32)],
        ),
        out_shape=jax.ShapeDtypeStruct((out_rows, rows), f32),
        compiler_params=pltpu.CompilerParams(vmem_limit_bytes=48 * MIB),
        cost_estimate=time_estimate(8, out_rows * rows * 6),
        name="assemble_in_weight_grad",
    )(place, *gates, *convs)


def body(
    tokens,
    norm_gain,
    in_weight,
    conv_weight,
    conv_bias,
    dt_bias,
    decay_log,
    skip_scale,
    gate_gain,
    out_weight,
    cotangent,
):
    count, mine = lax.axis_size("seq"), lax.axis_index("seq")
    planes = lax.axis_size("batch")
    place = mine.astype(jnp.int32).reshape(1)
    inner, all_heads, conv_all = gate_gain.shape[0], dt_bias.shape[0], conv_bias.shape[0]
    size, states = inner // all_heads, (conv_all - inner) // 2
    heads, width = all_heads // count, inner // count
    dims = (heads, size, states, count)
    shared = 2 * states
    conv_cols = width + shared
    tok_rows = tokens.shape[1]
    per_plane = out_weight.shape[0] // width

    def own(vector, per):
        return lax.dynamic_slice_in_dim(vector, mine * per, per, vector.ndim - 1)

    def own_conv(array):
        return jnp.concatenate([own(array[..., :inner], width), array[..., inner:]], axis=-1)

    tokens_row = tokens[0].astype(f32)
    inverse = lax.rsqrt(jnp.mean(tokens_row * tokens_row, axis=-1, keepdims=True) + epsilon)
    normed_own = (tokens_row * inverse * norm_gain).astype(bf16)
    w_own = jnp.concatenate(
        [
            own(in_weight[:, :inner], width),
            own_conv(in_weight[:, inner : inner + conv_all]),
            jnp.pad(own(in_weight[:, inner + conv_all :], heads), ((0, 0), (0, LANES - heads))),
        ],
        axis=1,
    )
    w_cols = lax.all_gather(w_own, "batch", axis=0, tiled=True)
    held = gather_all(normed_own)
    w_cols, held, cot_own, out_owned = together(w_cols, held, cotangent[0], out_weight)
    cot = lax.all_gather(cot_own, "seq", axis=0, tiled=True)
    out_rows = rows_joined(rows_from_owner(out_owned, width, range(planes)))

    conv_w, conv_b = own_conv(conv_weight), own_conv(conv_bias)[None]
    per_head = jnp.stack([own(dt_bias, heads), -jnp.exp(own(decay_log, heads))])
    per_head = jnp.pad(per_head, ((0, 0), (0, 8 - heads))).reshape(16, 1)
    step_rows = jnp.broadcast_to(per_head, (16, LANES))
    gain_own = own(gate_gain, width)[None]
    rows = jnp.concatenate(
        [jnp.repeat(own(skip_scale, heads), size)[None], gain_own, jnp.zeros((6, width), f32)],
        axis=0,
    )
    params = (w_cols, conv_w, conv_b, step_rows, rows)
    conv_in, active, slope, gate_act, gate_slope, *rest = run_forward(
        place, placed_pieces(held), params, dims
    )
    raw, ssd, starts, scaled, squares, placed, normed = rest

    middle = placed.shape[0] // 2
    out_send = dot(placed[middle:], out_rows).astype(bf16)
    out_send, cot = together(out_send, cot)
    out_grad = jnp.einsum("td,ed->te", cot, out_rows, preferred_element_type=f32)
    slopes = jnp.sum(out_grad * scaled.astype(f32), axis=1)
    sums = sum_seq(jnp.stack([squares[:, 0].reshape(-1), slopes]))
    out_parts = scatter_near(dot(placed[:middle], out_rows), out_send)
    scale = lax.rsqrt(sums[0] / inner + epsilon)
    steep = scale * scale * scale * sums[1] / inner
    norms = jnp.stack([scale, steep])
    norms = jnp.pad(norms, ((0, 6), (0, 0))).reshape(8, -1, GROUP).swapaxes(0, 1)
    scaled_cot = (cot.astype(f32) * scale[:, None]).astype(bf16)
    out_term = jnp.einsum("te,td->ed", scaled, scaled_cot, preferred_element_type=f32)
    out_sum = lax.psum_scatter(out_term.astype(bf16), "batch", scatter_dimension=0, tiled=True)
    gated = ssd * gate_act.astype(f32)
    gated_grad = out_grad * gain_own * scale[:, None] - gated * steep[:, None]
    gate_grad = (gated_grad * ssd * gate_slope.astype(f32)).astype(bf16)
    gate_term = jnp.einsum("td,tf->df", normed, gate_grad, preferred_element_type=f32)
    gate_term = gate_term.astype(bf16)

    values = (conv_in, active, slope, gate_act, gate_slope, raw, ssd, starts, out_grad, norms)
    params = (conv_w, step_rows, rows)
    stages = gather_stages()
    outputs = []
    carried = [
        jnp.zeros((states, width), f32),
        jnp.zeros((HALO, conv_cols), f32),
        jnp.zeros((1, width), f32),
        jnp.zeros((1, width), f32),
        jnp.zeros(conv_w.shape, f32),
        jnp.zeros(conv_b.shape, f32),
        jnp.zeros((8, GROUP), f32),
        jnp.zeros((8, GROUP), f32),
    ]
    for call in range(BACKWARD_CALLS):
        if call == 0:
            carried, gate_term = together(carried, gate_term)
            gate_sum = lax.psum_scatter(gate_term, "batch", scatter_dimension=0, tiled=True)
        if call < stages - 1:
            carried, out_parts = together(carried, out_parts)
            out_parts = scatter_stage(out_parts, call)
        if call == 1:
            carried, out_sum = together(carried, out_sum)
            out_pieces = to_owner(out_sum)[None]
        outputs, carried = backward_call(call, place, values, params, dims, outputs, carried)
    for stage in range(BACKWARD_CALLS, stages - 1):
        out_parts = scatter_stage(out_parts, stage)
    _, _, gain_term, skip_term, conv_w_term, conv_b_term, bias_term, rate_term = carried
    outputs, mixed_out, out_pieces, gate_sum = together(
        outputs, scatter_end(out_parts), out_pieces, gate_sum
    )
    proj_grad, back_grad = outputs

    out_pieces = double(out_pieces, 0)
    gates = gather_stage(gather_start(gate_sum), 0)
    conv_term = jnp.einsum(
        "td,tf->df", normed, proj_grad[:, width:], preferred_element_type=f32
    ).astype(bf16)
    conv_term, back_grad, out_pieces, gates = together(conv_term, back_grad, out_pieces, gates)
    conv_sum = lax.psum_scatter(conv_term, "batch", scatter_dimension=0, tiled=True)

    def back_part(part):
        return jnp.einsum("tf,df->td", part, w_cols, preferred_element_type=f32)

    out_pieces = double(out_pieces, 1)
    gates = gather_stage(gates, 1)
    back_send = back_part(back_grad[middle:]).astype(bf16)
    back_send, back_keep, out_pieces, gates = together(
        back_send, back_grad[:middle], out_pieces, gates
    )
    for stage in range(2, stages):
        out_pieces = double(out_pieces, stage)
        gates = gather_stage(gates, stage)
    back_parts = scatter_near(back_part(back_keep), back_send)
    back_parts, out_pieces, gates = together(back_parts, out_pieces, gates)
    for stage in range(stages - 1):
        back_parts = scatter_stage(back_parts, stage)
    normed_grad, conv_sum = together(scatter_end(back_parts), conv_sum)
    normed_grad = normed_grad.astype(f32)
    cot_row = cotangent[0].astype(f32)
    gained = norm_gain * normed_grad
    slope = inverse * inverse * inverse * jnp.mean(gained * tokens_row, axis=-1, keepdims=True)
    input_grad = cot_row + inverse * gained - tokens_row * slope
    norm_gain_term = jnp.sum(normed_grad * (tokens_row * inverse), axis=0)
    own_scale = lax.dynamic_slice_in_dim(scale, mine * tok_rows, tok_rows, 0)[:, None]
    block_out = (tokens_row + own_scale * mixed_out.astype(f32)).astype(bf16)
    out_weight_grad = assemble_out(place, out_pieces, per_plane)

    in_weight_grad = assemble(place, gates, gather_all(conv_sum), dims).T

    def among_heads(vector, per, total):
        return lax.dynamic_update_slice_in_dim(jnp.zeros((total,), f32), vector, mine * per, 0)

    def among_conv(array):
        wide = jnp.zeros((array.shape[0], inner), f32)
        wide = lax.dynamic_update_slice_in_dim(wide, array[:, :width], mine * width, 1)
        return jnp.concatenate([wide, array[:, width:]], axis=1).reshape(-1)

    skip_heads = jnp.sum(skip_term.reshape(heads, size), axis=1)
    terms = [
        norm_gain_term,
        among_conv(conv_w_term),
        among_conv(conv_b_term),
        among_heads(jnp.sum(bias_term[:heads], axis=1), heads, all_heads),
        among_heads(jnp.sum(rate_term[:heads], axis=1), heads, all_heads),
        among_heads(skip_heads, heads, all_heads),
        among_heads(gain_term[0], width, inner),
    ]
    vector = jnp.concatenate(terms)
    padding = -vector.shape[0] % (8 * LANES)
    vector = jnp.pad(vector, (0, padding)).reshape(-1, LANES)
    vector = sum_all(vector).reshape(-1)
    parts, offset = [], 0
    for term in terms:
        parts.append(vector[offset : offset + term.shape[0]])
        offset += term.shape[0]
    return (
        block_out[None],
        input_grad[None],
        parts[0],
        in_weight_grad,
        parts[1].reshape(conv_weight.shape),
        parts[2],
        parts[3],
        parts[4],
        parts[5],
        parts[6],
        out_weight_grad,
    )


def solution(mesh):
    placed = (
        P("batch", "seq", None),
        P(),
        P("batch", None),
        P(),
        P(),
        P(),
        P(),
        P(),
        P(),
        P("batch", None),
        P("batch", "seq", None),
    )
    return jax.shard_map(
        body,
        mesh=mesh,
        in_specs=placed,
        out_specs=(
            P("batch", "seq", None),
            P("batch", "seq", None),
            P(),
            P("batch", None),
            P(),
            P(),
            P(),
            P(),
            P(),
            P(),
            P("batch", None),
        ),
        check_vma=False,
    )
```

```python
import functools

import jax
import jax.numpy as jnp
from jax import lax
from jax.experimental import pallas as pl
from jax.experimental.pallas import tpu as pltpu
from jax.sharding import PartitionSpec as P

GROUP = 256
LANES = 128
HALF = GROUP // 2
HALO = 8
STEP_ROWS = 16
LOG2E = 1.4426950408889634
epsilon = 1e-05
f32 = jnp.float32
bf16 = jnp.bfloat16
MIB = 2**20


def exchange(value, axis, distance):
    count = lax.axis_size(axis)
    return lax.ppermute(value, axis, [(source, source ^ distance) for source in range(count)])


def bits_of(count):
    return [1 << k for k in range(count.bit_length() - 1)]


def placed_order(count):
    return [2 * k for k in range(count // 2)] + [2 * k + 1 for k in range(count // 2)]


def together(*values):
    return lax.optimization_barrier(values)


def far_orders():
    far = bits_of(lax.axis_size("seq"))[1:]
    return far, far[::-1]


def gather_start(value):
    half = value.shape[0] // 32 * 16
    return tuple({"base": part, "fresh": None, "near": []} for part in (value[:half], value[half:]))


def gather_stage(held, stage):
    grown = []
    for half, order in zip(held, far_orders()):
        base, fresh, near = half["base"], half["fresh"], list(half["near"])
        if stage >= 1:
            merged = base if stage == len(order) else jnp.concatenate([base, fresh], axis=0)
            near.append(exchange(merged if stage == 1 else fresh, "seq", 1))
            base = merged
        if stage < len(order):
            fresh = exchange(base, "seq", order[stage])
        grown.append({"base": base, "fresh": fresh, "near": near})
    return tuple(grown)


def gather_stages():
    return len(bits_of(lax.axis_size("seq")))


def gathered(held):
    arrays, table = [], {}
    for number, (half, order) in enumerate(zip(held, far_orders())):
        indices = [0]
        for bit in order:
            indices += [index | bit for index in indices]
        middle = len(indices) // 2
        groups = [(half["base"], indices[:middle]), (half["fresh"], indices[middle:])]
        bounds = [0] + [2 << k for k in range(len(order))]
        for value, first, last in zip(half["near"], bounds, bounds[1:]):
            groups.append((value, [index | 1 for index in indices[first:last]]))
        for value, members in groups:
            rows = value.shape[0] // len(members)
            for turn, index in enumerate(members):
                table[number, index] = (len(arrays), turn * rows, rows)
            arrays.append(value)
    return arrays, table


def token_pieces(held):
    arrays, table = gathered(held)
    return arrays, tuple(
        tuple(table[half, index] for half in range(2)) for index in range(lax.axis_size("seq"))
    )


def gather_all(value):
    held = gather_start(value)
    for stage in range(gather_stages()):
        held = gather_stage(held, stage)
    return held


def scatter_near(keep, send):
    total = (keep.astype(f32) + exchange(send, "seq", 1).astype(f32)).astype(bf16)
    count = lax.axis_size("seq")
    half = total.shape[0] // count
    total = total.reshape((count // 2, 2, half) + total.shape[1:])
    held = []
    for part, order in enumerate(far_orders()):
        members = [0]
        for bit in order[::-1]:
            members += [member | bit >> 1 for member in members]
        held.append(jnp.stack([total[member, part] for member in members]))
    return tuple(held)


def scatter_stage(held, stage):
    smaller = []
    for value, order in zip(held, far_orders()):
        middle = value.shape[0] // 2
        arriving = exchange(value[middle:], "seq", order[stage])
        smaller.append((value[:middle].astype(f32) + arriving.astype(f32)).astype(bf16))
    return tuple(smaller)


def scatter_end(held):
    return jnp.concatenate([value[0] for value in held], axis=0)


def sum_seq(value):
    for bit in bits_of(lax.axis_size("seq")):
        value = value + exchange(value, "seq", bit)
    return value


def sum_all(value):
    for axis in ("seq", "batch"):
        for bit in bits_of(lax.axis_size(axis)):
            value = value + exchange(value, axis, bit)
    return value


def plane_pairs(ahead):
    planes, count = lax.axis_size("batch"), lax.axis_size("seq")
    per = count // planes
    pairs = []
    for owner in range(planes):
        for piece in range(planes):
            for k in range(per):
                holder = owner * count + piece * per + k
                user = (piece + ahead) % planes * count + owner * per + k
                pairs.append((holder, user))
    return pairs


def rows_from_owner(out_weight, width, aheads):
    planes, count = lax.axis_size("batch"), lax.axis_size("seq")
    per, size = count // planes, width // planes
    mine = lax.axis_index("seq")
    piece = lax.dynamic_slice_in_dim(out_weight, mine % per * width + mine // per * size, size, 0)
    return [lax.ppermute(piece, ("batch", "seq"), plane_pairs(ahead)) for ahead in aheads]


def rows_joined(arriving):
    planes, plane = lax.axis_size("batch"), lax.axis_index("batch")
    size = arriving[0].shape[0]
    doubled = jnp.concatenate(arriving[::-1] * 2, axis=0)
    return lax.dynamic_slice_in_dim(doubled, (planes - 1 - plane) * size, planes * size, 0)


def to_owner(summed):
    return lax.ppermute(
        summed, ("batch", "seq"), [(user, holder) for holder, user in plane_pairs(0)]
    )


def double(held, turn):
    bits = bits_of(lax.axis_size("seq"))
    return jnp.concatenate([held, exchange(held, "seq", (bits[1:] + [1])[turn])], axis=0)


def step_values(raw):
    small = jnp.exp(-jnp.abs(raw))
    step = jnp.maximum(raw, 0.0) + jnp.log1p(small)
    sig = jnp.where(raw >= 0, 1.0, small) / (1.0 + small)
    tiny = raw < -20.0
    log_step = jnp.where(tiny, raw, jnp.log(step))
    ratio = jnp.where(tiny, 1.0, sig / step)
    return step, sig, log_step, ratio


def dot(a, b):
    return jnp.dot(a, b, preferred_element_type=f32)


def dot_nt(a, b):
    return lax.dot_general(a, b, (((1,), (1,)), ((), ())), preferred_element_type=f32)


def dot_tn(a, b):
    return lax.dot_general(a, b, (((0,), (0,)), ((), ())), preferred_element_type=f32)


def sigmoid(value):
    return 0.5 * jnp.tanh(0.5 * value) + 0.5


def silu_slope(value):
    sig = sigmoid(value)
    active = value * sig
    return active, sig + active * (1.0 - sig)


def split_parts(value, count):
    parts = []
    for _ in range(count):
        part = value.astype(bf16)
        parts.append(part)
        value = value - part.astype(f32)
    return parts


def sum_along(rows, order):
    parts = jnp.concatenate([part.astype(f32) for part in split_parts(rows, 3)], axis=0)
    total = dot(parts.astype(bf16), order)
    return total[:8] + total[8:16] + total[16:24]


def to_columns(rows):
    stacked = jnp.concatenate(rows, axis=0)
    missing = LANES - stacked.shape[0]
    return jnp.concatenate([stacked, jnp.zeros((missing, GROUP), f32)], axis=0).T


def spread_heads(value, first, heads, size):
    rows = value.shape[0]
    return jnp.concatenate(
        [jnp.broadcast_to(value[:, first + h : first + h + 1], (rows, size)) for h in range(heads)],
        axis=1,
    )


def head_ones(width, size):
    row = lax.broadcasted_iota(jnp.int32, (8, width), 0)
    column = lax.broadcasted_iota(jnp.int32, (8, width), 1)
    return (column // size == row).astype(f32).astype(bf16)


def sum_lanes(value):
    return dot_nt(jnp.ones((8, value.shape[1]), bf16), value.astype(bf16))


def ones_where(condition):
    return jnp.where(condition, 1.0, 0.0).astype(bf16)


def order_indices(length):
    row = lax.broadcasted_iota(jnp.int32, (length, length), 0)
    column = lax.broadcasted_iota(jnp.int32, (length, length), 1)
    return row, column


def fetch(arrays, table, which, buffer, semaphores, slot):
    for index, halves in enumerate(table):

        @pl.when(which == index)
        def _():
            for half, (array, row, rows) in enumerate(halves):
                pltpu.make_async_copy(
                    arrays[array].at[pl.ds(row, rows)],
                    buffer.at[slot, pl.ds(half * rows, rows)],
                    semaphores.at[slot],
                ).start()


def fetched(arrays, table, buffer, semaphores, order):
    step = pl.program_id(0)
    slot = lax.rem(step, 2)

    @pl.when(step == 0)
    def _():
        fetch(arrays, table, order(0), buffer, semaphores, 0)

    @pl.when(step + 1 < pl.num_programs(0))
    def _():
        fetch(arrays, table, order(step + 1), buffer, semaphores, lax.rem(step + 1, 2))

    for half, (_, _, rows) in enumerate(table[0]):
        pltpu.make_async_copy(
            arrays[0].at[pl.ds(0, rows)],
            buffer.at[slot, pl.ds(half * rows, rows)],
            semaphores.at[slot],
        ).wait()
    return buffer[slot]


def device_place(place, device, count):
    relative = device ^ place
    return (relative & 1) * (count // 2) + (relative >> 1)


def block_place(place, block, count):
    return device_place(place, block // 2, count) * 2 + block % 2


def forward_kernel(dims, table, given, place_ref, *refs):
    heads, size, states, count = dims
    width = heads * size
    conv_cols = width + 2 * states
    arrays, refs = refs[:given], refs[given:]
    w_ref, conv_w_ref, conv_b_ref, step_ref, rows_ref, out_rows_ref = refs[:6]
    conv_in_ref, active_ref, slope_ref, gate_act_ref, gate_slope_ref = refs[6:11]
    raw_ref, ssd_ref, start_ref, scaled_ref, square_ref, normed_ref = refs[11:17]
    keep_ref, send_ref = refs[17:19]
    state, padded, order, barred, projected, partial, buffer, semaphores, out_semaphores = refs[19:]
    turn = pl.program_id(0)
    slot = lax.rem(turn, 2)
    rows = buffer.shape[1]

    def copy_out(target, row):
        return pltpu.make_async_copy(
            partial.at[slot], target.at[pl.ds(row, rows)], out_semaphores.at[slot]
        )

    @pl.when(turn == 0)
    def _():
        state[...] = jnp.zeros_like(state)
        padded[0:HALO] = jnp.zeros_like(padded[0:HALO])
        row, column = order_indices(GROUP)
        order[...] = ones_where(row <= column)
        row, column = order_indices(HALF)
        barred[...] = jnp.where(row >= column, 0.0, -1e30)

    @pl.when(turn >= 2)
    def _():
        copy_out(keep_ref, 0).wait()

    normed = fetched(arrays, table, buffer, semaphores, lambda step: place_ref[0] ^ step)
    normed_ref[...] = normed
    projected[...] = dot(normed, w_ref[...])
    conv_w = conv_w_ref[...]
    taps = conv_w.shape[0]
    for block in range(rows // GROUP):
        here = slice(block * GROUP, (block + 1) * GROUP)
        conv_in = projected[here, width : width + conv_cols].astype(bf16)
        conv_in_ref[here] = conv_in
        padded[HALO : HALO + GROUP] = conv_in.astype(f32)
        pre = conv_b_ref[...]
        for k in range(taps):
            top = HALO - (taps - 1) + k
            pre = pre + conv_w[k : k + 1] * padded[top : top + GROUP]
        padded[0:HALO] = padded[GROUP : GROUP + HALO]
        active, slope = silu_slope(pre)
        active = active.astype(bf16)
        active_ref[here] = active
        slope_ref[here] = slope.astype(bf16)
        signal = active[:, :width]
        entry = active[:, width : width + states]
        readout = active[:, width + states :]
        signal_wide = signal.astype(f32)

        raw = projected[here, width + conv_cols :].T[:8]
        raw_ref[block] = raw
        step, _, log_step, _ = step_values(raw + step_ref[0:8, 0:1])
        running = sum_along(step * step_ref[8:16, 0:1], order[...])
        later = running - log_step
        total = running[:, GROUP - 1 :]
        columns = to_columns([running * LOG2E, jnp.exp(running), jnp.exp(total - later)])
        later = later * LOG2E
        early_wide = spread_heads(columns, 8, heads, size)
        tail_wide = spread_heads(columns, 16, heads, size)
        first, second = slice(0, HALF), slice(HALF, GROUP)
        scores = dot_nt(readout[first], entry[first])
        later_scores = dot_nt(readout[second], entry)
        within = []
        for h in range(heads):
            part = signal[:, h * size : (h + 1) * size]
            begin, end = columns[first, h : h + 1], columns[second, h : h + 1]
            row_first, row_second = later[h : h + 1, first], later[h : h + 1, second]
            near = jnp.exp2(begin - row_first + barred[...]) * scores
            full = jnp.exp2(end - row_first) * later_scores[:, first]
            last = jnp.exp2(end - row_second + barred[...]) * later_scores[:, second]
            both = jnp.concatenate([full.astype(bf16), last.astype(bf16)], axis=1)
            within.append(
                jnp.concatenate([dot(near.astype(bf16), part[first]), dot(both, part)], axis=0)
            )
        start = state[...]
        start_low = start.astype(bf16)
        start_ref[block] = start_low
        carried = dot(readout, start_low) * early_wide
        ssd = jnp.concatenate(within, axis=1) + carried + rows_ref[0:1] * signal_wide
        tail = (signal_wide * tail_wide).astype(bf16)
        state[...] = start * early_wide[GROUP - 1 :] + dot_tn(entry, tail)

        gate_act, gate_slope = silu_slope(projected[here, :width])
        gate_act_ref[here] = gate_act.astype(bf16)
        gate_slope_ref[here] = gate_slope.astype(bf16)
        ssd_ref[here] = ssd
        gated = ssd * gate_act
        scaled_ref[here] = (gated * rows_ref[1:2]).astype(bf16)
        square_ref[block] = sum_lanes(gated * gated)

    partial[slot] = dot(scaled_ref[...], out_rows_ref[...]).astype(bf16)
    position = device_place(place_ref[0], turn, count)

    @pl.when(position < count // 2)
    def _():
        copy_out(keep_ref, pl.multiple_of(position * rows, rows)).start()

    @pl.when(position >= count // 2)
    def _():
        copy_out(send_ref, pl.multiple_of((position - count // 2) * rows, rows)).start()

    @pl.when(turn == pl.num_programs(0) - 1)
    def _():
        for other in range(2):
            pltpu.make_async_copy(
                partial.at[other], keep_ref.at[pl.ds(0, rows)], out_semaphores.at[other]
            ).wait()


def time_estimate(microseconds, accessed):
    return pl.CostEstimate(
        flops=int(microseconds * 1.1e9), bytes_accessed=int(accessed), transcendentals=0
    )


def fixed(shape):
    return pl.BlockSpec(shape, lambda turn, place: (0,) * len(shape), pipeline_mode=pl.Buffered(1))


def anywhere(values):
    return [pl.BlockSpec(memory_space=pltpu.HBM)] * len(values)


def run_forward(place, pieces, params, dims):
    heads, size, states, count = dims
    w_cols, conv_w = params[:2]
    dim = w_cols.shape[0]
    width, conv_cols = heads * size, conv_w.shape[1]
    arrays, table = pieces
    rows = sum(half[2] for half in table[0])
    tokens = count * rows
    blocks, share = tokens // GROUP, rows // GROUP

    def moving(columns):
        return pl.BlockSpec((rows, columns), lambda turn, place: (turn, 0))

    def rows_of_blocks(height, columns):
        return pl.BlockSpec((share, height, columns), lambda turn, place: (turn, 0, 0))

    return pl.pallas_call(
        functools.partial(forward_kernel, dims, table, len(arrays)),
        grid_spec=pltpu.PrefetchScalarGridSpec(
            num_scalar_prefetch=1,
            grid=(count,),
            in_specs=[*anywhere(arrays), *[fixed(param.shape) for param in params]],
            out_specs=[
                moving(conv_cols),
                moving(conv_cols),
                moving(conv_cols),
                moving(width),
                moving(width),
                rows_of_blocks(8, GROUP),
                moving(width),
                rows_of_blocks(states, width),
                moving(width),
                rows_of_blocks(8, GROUP),
                moving(dim),
                *anywhere(range(2)),
            ],
            scratch_shapes=[
                pltpu.VMEM((states, width), f32),
                pltpu.VMEM((HALO + GROUP, conv_cols), f32),
                pltpu.VMEM((GROUP, GROUP), bf16),
                pltpu.VMEM((HALF, HALF), f32),
                pltpu.VMEM((rows, w_cols.shape[1]), f32),
                pltpu.VMEM((2, rows, dim), bf16),
                pltpu.VMEM((2, rows, dim), bf16),
                pltpu.SemaphoreType.DMA((2,)),
                pltpu.SemaphoreType.DMA((2,)),
            ],
        ),
        out_shape=[
            jax.ShapeDtypeStruct((tokens, conv_cols), bf16),
            jax.ShapeDtypeStruct((tokens, conv_cols), bf16),
            jax.ShapeDtypeStruct((tokens, conv_cols), bf16),
            jax.ShapeDtypeStruct((tokens, width), bf16),
            jax.ShapeDtypeStruct((tokens, width), bf16),
            jax.ShapeDtypeStruct((blocks, 8, GROUP), f32),
            jax.ShapeDtypeStruct((tokens, width), f32),
            jax.ShapeDtypeStruct((blocks, states, width), bf16),
            jax.ShapeDtypeStruct((tokens, width), bf16),
            jax.ShapeDtypeStruct((blocks, 8, GROUP), f32),
            jax.ShapeDtypeStruct((tokens, dim), bf16),
            jax.ShapeDtypeStruct((tokens // 2, dim), bf16),
            jax.ShapeDtypeStruct((tokens // 2, dim), bf16),
        ],
        compiler_params=pltpu.CompilerParams(vmem_limit_bytes=60 * MIB),
        cost_estimate=time_estimate(blocks * 2.8, tokens * (4 * dim + 20 * width)),
        name="forward_blocks",
    )(place, *arrays, *params)


def backward_kernel(dims, place_ref, *refs):
    heads, size, states, _ = dims
    width = heads * size
    conv_cols = width + 2 * states
    conv_in_ref, active_ref, slope_ref, gate_act_ref, gate_slope_ref = refs[:5]
    raw_ref, ssd_ref, start_ref, out_grad_ref, norm_ref = refs[5:10]
    conv_w_ref, step_ref, rows_ref = refs[10:13]
    out_ref, placed_ref = refs[13:15]
    sums = refs[15:21]
    gain_ref, skip_ref, conv_wg_ref, conv_bg_ref, bias_ref, rate_ref = sums
    state, pre_grads, order, back_order, barred = refs[21:]
    taps = conv_w_ref.shape[0]

    @pl.when(pl.program_id(0) == 0)
    def _():
        state[...] = jnp.zeros_like(state)
        pre_grads[0:HALO] = jnp.zeros_like(pre_grads[0:HALO])
        for total in sums:
            total[...] = jnp.zeros_like(total)
        row, column = order_indices(GROUP)
        order[...] = ones_where(row <= column)
        back_order[...] = ones_where(row >= column)
        row, column = order_indices(HALF)
        barred[...] = jnp.where(row <= column, 0.0, -1e30)

    gate_act, ssd, out_grad = gate_act_ref[...].astype(f32), ssd_ref[...], out_grad_ref[...]
    norms = norm_ref[0].T
    scale, slope = norms[:, 0:1], norms[:, 1:2]
    gated = ssd * gate_act
    gain_ref[...] += jnp.sum(out_grad * (gated * scale), axis=0, keepdims=True)
    gated_grad = out_grad * (rows_ref[1:2] * scale) - gated * slope
    grad_low = (gated_grad * gate_act).astype(bf16)
    gate_grad = (gated_grad * ssd * gate_slope_ref[...].astype(f32)).astype(bf16)
    out_ref[:, :width] = gate_grad
    placed_ref[:, :width] = gate_grad
    ssd_grad = grad_low.astype(f32)

    raw = raw_ref[0] + step_ref[0:8, 0:1]
    rate = step_ref[8:16, 0:1]
    step, sig, log_step, ratio = step_values(raw)
    decay = step * rate
    running = sum_along(decay, order[...])
    later = running - log_step
    total = running[:, GROUP - 1 :]
    columns = to_columns([later * LOG2E, jnp.exp(running), jnp.exp(total - later)])
    running = running * LOG2E
    early_wide = spread_heads(columns, 8, heads, size)
    tail_wide = spread_heads(columns, 16, heads, size)

    signal = active_ref[:, :width]
    entry = active_ref[:, width : width + states]
    readout = active_ref[:, width + states :]
    signal_wide = signal.astype(f32)
    start_low = start_ref[0]
    end_grad = state[...]
    end_low = end_grad.astype(bf16)
    first, second = slice(0, HALF), slice(HALF, GROUP)
    scores = dot_nt(entry[first], readout)
    later_scores = dot_nt(entry[second], readout[second])
    near_grad, far_grad, last_grad = 0.0, 0.0, 0.0
    within = []
    for h in range(heads):
        part, grad = signal[:, h * size : (h + 1) * size], grad_low[:, h * size : (h + 1) * size]
        begin, end = columns[first, h : h + 1], columns[second, h : h + 1]
        row_first, row_second = running[h : h + 1, first], running[h : h + 1, second]
        near = jnp.exp2(row_first - begin + barred[...])
        full = jnp.exp2(row_second - begin)
        last = jnp.exp2(row_second - end + barred[...])
        both = jnp.concatenate(
            [
                (near * scores[:, first]).astype(bf16),
                (full * scores[:, second]).astype(bf16),
            ],
            axis=1,
        )
        final = (last * later_scores).astype(bf16)
        within.append(jnp.concatenate([dot(both, grad), dot(final, grad[second])], axis=0))
        cross = dot_nt(part[first], grad)
        near_grad = near_grad + cross[:, first] * near
        far_grad = far_grad + cross[:, second] * full
        last_grad = last_grad + dot_nt(part[second], grad[second]) * last
    tail_grad = tail_wide * dot(entry, end_low)
    signal_grad = jnp.concatenate(within, axis=1) + tail_grad
    score_first = jnp.concatenate([near_grad, far_grad], axis=1).astype(bf16)
    score_second = last_grad.astype(bf16)
    tail = (signal_wide * tail_wide).astype(bf16)
    head_grad = (ssd_grad * early_wide).astype(bf16)
    entry_grad = jnp.concatenate(
        [dot(score_first, readout), dot(score_second, readout[second])], axis=0
    ) + dot_nt(tail, end_low)
    readout_grad = dot_tn(score_first, entry[first]) + dot_nt(head_grad, start_low)
    readout_last = readout_grad[second] + dot_tn(score_second, entry[second])
    total_wide = early_wide[GROUP - 1 :]
    state[...] = end_grad * total_wide + dot_tn(readout, head_grad)

    skip = rows_ref[0:1]
    ones = head_ones(width, size)
    column_part = signal_wide * signal_grad
    row_part = ssd_grad * (ssd - skip * signal_wide)
    end_part = jnp.sum(signal_wide * tail_grad, axis=0, keepdims=True) + total_wide * jnp.sum(
        start_low.astype(f32) * end_grad, axis=0, keepdims=True
    )

    def head_sums(value, parts):
        return sum(dot_nt(ones, part) for part in split_parts(value, parts))

    end_rows = head_sums(jnp.broadcast_to(end_part, (8, width)), 2)[:, 0:1]
    decay_grad = sum_along(head_sums(row_part - column_part, 2), back_order[...]) + end_rows
    raw_grad = head_sums(column_part, 1) * ratio + decay_grad * rate * sig
    skip_ref[...] += jnp.sum(ssd_grad * signal_wide, axis=0, keepdims=True)
    bias_ref[...] += raw_grad
    rate_ref[...] += decay_grad * decay
    raw_low = to_columns([raw_grad]).astype(bf16)
    out_ref[:, width + conv_cols :] = raw_low
    placed_ref[:, width + conv_cols :] = raw_low

    pre_grads[GROUP : GROUP + HALO] = pre_grads[0:HALO]
    pre_grads[0:GROUP, :width] = (signal_grad + skip * ssd_grad) * slope_ref[:, :width].astype(f32)
    sides = slope_ref[:, width:].astype(f32)
    pre_grads[0:GROUP, width : width + states] = entry_grad * sides[:, :states]
    pre_grads[0:HALF, width + states :] = readout_grad[first] * sides[first, states:]
    pre_grads[HALF:GROUP, width + states :] = readout_last * sides[second, states:]
    conv_w = conv_w_ref[...]
    conv_in = conv_in_ref[...].astype(f32)
    conv_grad = 0.0
    for k in range(taps):
        ahead = taps - 1 - k
        shifted = pre_grads[ahead : ahead + GROUP]
        conv_grad = conv_grad + conv_w[k : k + 1] * shifted
        conv_wg_ref[k : k + 1] += jnp.sum(shifted * conv_in, axis=0, keepdims=True)
        if ahead == 0:
            conv_bg_ref[...] += jnp.sum(shifted, axis=0, keepdims=True)
    conv_low = conv_grad.astype(bf16)
    out_ref[:, width : width + conv_cols] = conv_low
    placed_ref[:, width : width + conv_cols] = conv_low


def run_backward(place, values, params, dims):
    heads, size, states, count = dims
    conv_cols, width = values[0].shape[1], heads * size
    tokens = values[0].shape[0]
    blocks = tokens // GROUP
    last = blocks - 1
    out_cols = width + conv_cols + LANES

    def moving(columns):
        return pl.BlockSpec((GROUP, columns), lambda turn, place: (last - turn, 0))

    def rows_of_block():
        return pl.BlockSpec((1, 8, GROUP), lambda turn, place: (last - turn, 0, 0))

    sums = [(1, width), (1, width), params[0].shape, (1, conv_cols), (8, GROUP), (8, GROUP)]
    return pl.pallas_call(
        functools.partial(backward_kernel, dims),
        grid_spec=pltpu.PrefetchScalarGridSpec(
            num_scalar_prefetch=1,
            grid=(blocks,),
            in_specs=[
                moving(conv_cols),
                moving(conv_cols),
                moving(conv_cols),
                moving(width),
                moving(width),
                rows_of_block(),
                moving(width),
                pl.BlockSpec((1, states, width), lambda turn, place: (last - turn, 0, 0)),
                moving(width),
                rows_of_block(),
                *[fixed(param.shape) for param in params],
            ],
            out_specs=[
                moving(out_cols),
                pl.BlockSpec(
                    (GROUP, out_cols),
                    lambda turn, place: (block_place(place[0], last - turn, count), 0),
                ),
                *[fixed(shape) for shape in sums],
            ],
            scratch_shapes=[
                pltpu.VMEM((states, width), f32),
                pltpu.VMEM((GROUP + HALO, conv_cols), f32),
                pltpu.VMEM((GROUP, GROUP), bf16),
                pltpu.VMEM((GROUP, GROUP), bf16),
                pltpu.VMEM((HALF, HALF), f32),
            ],
        ),
        out_shape=[jax.ShapeDtypeStruct((tokens, out_cols), bf16)] * 2
        + [jax.ShapeDtypeStruct(shape, f32) for shape in sums],
        compiler_params=pltpu.CompilerParams(vmem_limit_bytes=60 * MIB),
        cost_estimate=time_estimate(blocks * 3.5, tokens * 40 * width),
        name="backward_blocks",
    )(place, *values, *params)


def widen_kernel(place_ref, piece_ref, out_ref):
    out_ref[...] = piece_ref[0].astype(f32)


def assemble_out(place, pieces, per):
    count, size, dim = pieces.shape
    groups = count // per

    def source(turn, place):
        relative = (turn % groups * per + turn // groups) ^ place[0]
        return ((relative & 1) * (count // 2) + (relative >> 1), 0, 0)

    return pl.pallas_call(
        widen_kernel,
        grid_spec=pltpu.PrefetchScalarGridSpec(
            num_scalar_prefetch=1,
            grid=(count,),
            in_specs=[pl.BlockSpec((1, size, dim), source)],
            out_specs=pl.BlockSpec((size, dim), lambda turn, place: (turn, 0)),
        ),
        out_shape=jax.ShapeDtypeStruct((count * size, dim), f32),
        cost_estimate=time_estimate(5, count * size * dim * 6),
        name="assemble_out_weight_grad",
    )(place, pieces)


def assemble_kernel(dims, tables, given, place_ref, *refs):
    heads, size, states, count = dims
    width, shared = heads * size, 2 * states
    inner = count * width
    mains, sides, out_ref, sums = refs[: given[0]], refs[given[0] : given[1]], refs[-2], refs[-1]

    def piece(arrays, table, relative):
        parts = []
        for half in range(2):
            array, row, height = table[half, relative]
            parts.append(arrays[array][row : row + height].astype(f32))
        return jnp.concatenate(parts, axis=0).T

    for relative in range(count):
        device = place_ref[0] ^ relative
        columns = piece(mains, tables[0], relative)
        out_ref[pl.ds(pl.multiple_of(device * width, 8), width)] = columns[:width]
        middle = pl.multiple_of(inner + device * width, 8)
        out_ref[pl.ds(middle, width)] = columns[width:]
        sums[device] = piece(sides, tables[1], relative)[: shared + STEP_ROWS]
    total = sums[0, :shared]
    for device in range(1, count):
        total = total + sums[device, :shared]
    out_ref[2 * inner : 2 * inner + shared] = total
    for device in range(count):
        last = 2 * inner + shared + device * heads
        out_ref[last : last + heads] = sums[device, shared : shared + heads]


def assemble(place, mains, sides, dims):
    heads, size, states, count = dims
    mains, main_table = gathered(mains)
    sides, side_table = gathered(sides)
    rows = sum(main_table[half, 0][2] for half in range(2))
    out_rows = 2 * count * heads * size + 2 * states + count * heads

    def whole(value):
        return pl.BlockSpec(
            value.shape,
            lambda turn, place: (0,) * len(value.shape),
            pipeline_mode=pl.Buffered(1),
        )

    return pl.pallas_call(
        functools.partial(
            assemble_kernel, dims, (main_table, side_table), (len(mains), len(mains) + len(sides))
        ),
        grid_spec=pltpu.PrefetchScalarGridSpec(
            num_scalar_prefetch=1,
            grid=(1,),
            in_specs=[whole(value) for value in (*mains, *sides)],
            out_specs=pl.BlockSpec(
                (out_rows, rows), lambda turn, place: (0, 0), pipeline_mode=pl.Buffered(1)
            ),
            scratch_shapes=[pltpu.VMEM((count, 2 * states + STEP_ROWS, rows), f32)],
        ),
        out_shape=jax.ShapeDtypeStruct((out_rows, rows), f32),
        compiler_params=pltpu.CompilerParams(vmem_limit_bytes=60 * MIB),
        cost_estimate=time_estimate(8, out_rows * rows * 6),
        name="assemble_in_weight_grad",
    )(place, *mains, *sides)


def body(
    tokens,
    norm_gain,
    in_weight,
    conv_weight,
    conv_bias,
    dt_bias,
    decay_log,
    skip_scale,
    gate_gain,
    out_weight,
    cotangent,
):
    count, mine = lax.axis_size("seq"), lax.axis_index("seq")
    planes = lax.axis_size("batch")
    place = mine.astype(jnp.int32).reshape(1)
    inner, all_heads, conv_all = gate_gain.shape[0], dt_bias.shape[0], conv_bias.shape[0]
    size, states = inner // all_heads, (conv_all - inner) // 2
    heads, width = all_heads // count, inner // count
    dims = (heads, size, states, count)
    shared = 2 * states
    conv_cols = width + shared
    tok_rows = tokens.shape[1]
    per_plane = out_weight.shape[0] // width

    def own(vector, per, first=0):
        return lax.dynamic_slice_in_dim(vector, first + mine * per, per, vector.ndim - 1)

    def own_conv(array, first=0):
        return jnp.concatenate(
            [own(array, width, first), array[..., first + inner : first + conv_all]], axis=-1
        )

    tokens_row = tokens[0].astype(f32)
    inverse = lax.rsqrt(jnp.mean(tokens_row * tokens_row, axis=-1, keepdims=True) + epsilon)
    normed_own = (tokens_row * inverse * norm_gain).astype(bf16)
    step_own = own(in_weight, heads, inner + conv_all)
    w_own = jnp.concatenate(
        [
            own(in_weight, width),
            own_conv(in_weight, inner),
            jnp.pad(step_own, ((0, 0), (0, LANES - heads))),
        ],
        axis=1,
    )
    w_cols = lax.all_gather(w_own, "batch", axis=0, tiled=True)
    stages = gather_stages()
    held = gather_stage(gather_start(normed_own), 0)
    out_rows = rows_from_owner(out_weight, width, range(planes))
    held, out_rows = together(held, out_rows)
    for stage in range(1, stages):
        held = gather_stage(held, stage)
    w_cols, held, out_rows, cot_own = together(w_cols, held, out_rows, cotangent[0])
    out_rows = rows_joined(out_rows)
    cot = lax.all_gather(cot_own, "seq", axis=0, tiled=True)

    conv_w, conv_b = own_conv(conv_weight), own_conv(conv_bias)[None]
    per_head = jnp.stack([own(dt_bias, heads), -jnp.exp(own(decay_log, heads))])
    per_head = jnp.pad(per_head, ((0, 0), (0, 8 - heads))).reshape(16, 1)
    step_rows = jnp.broadcast_to(per_head, (16, LANES))
    gain_own = own(gate_gain, width)[None]
    rows = jnp.concatenate(
        [jnp.repeat(own(skip_scale, heads), size)[None], gain_own, jnp.zeros((6, width), f32)],
        axis=0,
    )
    params = (w_cols, conv_w, conv_b, step_rows, rows, out_rows)
    conv_in, active, slope, gate_act, gate_slope, raw, *rest = run_forward(
        place, token_pieces(held), params, dims
    )
    ssd, starts, scaled, squares, normed, out_keep, out_send = rest

    out_grad = jnp.einsum("td,ed->te", cot, out_rows, preferred_element_type=f32)
    slopes = jnp.sum(out_grad * scaled.astype(f32), axis=1)
    sums = sum_seq(jnp.stack([squares[:, 0].reshape(-1), slopes]))
    out_parts = scatter_stage(scatter_near(out_keep, out_send), 0)
    scale = lax.rsqrt(sums[0] / inner + epsilon)
    norms = jnp.stack([scale, scale * scale * scale * sums[1] / inner])
    norms = jnp.pad(norms, ((0, 6), (0, 0))).reshape(8, -1, GROUP).swapaxes(0, 1)
    scaled_cot = (cot.astype(f32) * scale[:, None]).astype(bf16)
    out_term = jnp.einsum("te,td->ed", scaled, scaled_cot, preferred_element_type=f32)
    out_term, norms, out_parts = together(out_term.astype(bf16), norms, out_parts)
    out_sum = lax.psum_scatter(out_term, "batch", scatter_dimension=0, tiled=True)
    for stage in range(1, stages - 1):
        out_parts = scatter_stage(out_parts, stage)

    values = (conv_in, active, slope, gate_act, gate_slope, raw, ssd, starts, out_grad, norms)
    proj_grad, back_grad, *terms = run_backward(place, values, (conv_w, step_rows, rows), dims)
    gain_term, skip_term, conv_w_term, conv_b_term, bias_term, rate_term = terms
    proj_grad, back_grad, mixed_out, out_sum = together(
        proj_grad, back_grad, scatter_end(out_parts), out_sum
    )

    def back_part(part):
        return jnp.einsum("tf,df->td", part, w_cols, preferred_element_type=f32)

    def weight_part(part):
        return jnp.einsum("td,tf->df", normed, part, preferred_element_type=f32).astype(bf16)

    middle = back_grad.shape[0] // 2
    back_send = back_part(back_grad[middle:]).astype(bf16)
    out_pieces = to_owner(out_sum)[None]
    back_send, proj_grad, out_pieces = together(back_send, proj_grad, out_pieces)
    main_term = weight_part(proj_grad[:, : 2 * width])
    out_pieces = double(out_pieces, 0)
    main_term, back_keep, proj_grad, out_pieces = together(
        main_term, back_grad[:middle], proj_grad, out_pieces
    )
    main_sum = lax.psum_scatter(main_term, "batch", scatter_dimension=0, tiled=True)
    back_parts = scatter_near(back_part(back_keep), back_send)
    back_parts, proj_grad, out_pieces, main_term = together(
        back_parts, proj_grad, out_pieces, main_term
    )
    back_parts = scatter_stage(back_parts, 0)
    out_pieces = double(out_pieces, 1)
    side_term = weight_part(proj_grad[:, 2 * width :])
    side_sum = lax.psum_scatter(side_term, "batch", scatter_dimension=0, tiled=True)
    weights = w_cols.astype(f32)
    norm_gain_term = jnp.sum(main_term.astype(f32) * weights[:, : 2 * width], axis=1)
    norm_gain_term += jnp.sum(side_term.astype(f32) * weights[:, 2 * width :], axis=1)
    norm_gain_term /= norm_gain

    def among_heads(vector, per, total):
        return lax.dynamic_update_slice_in_dim(jnp.zeros((total,), f32), vector, mine * per, 0)

    def among_conv(array):
        wide = jnp.zeros((array.shape[0], inner), f32)
        wide = lax.dynamic_update_slice_in_dim(wide, array[:, :width], mine * width, 1)
        return jnp.concatenate([wide, array[:, width:]], axis=1).reshape(-1)

    skip_heads = jnp.sum(skip_term.reshape(heads, size), axis=1)
    terms = [
        norm_gain_term,
        among_conv(conv_w_term),
        among_conv(conv_b_term),
        among_heads(jnp.sum(bias_term[:heads], axis=1), heads, all_heads),
        among_heads(jnp.sum(rate_term[:heads], axis=1), heads, all_heads),
        among_heads(skip_heads, heads, all_heads),
        among_heads(gain_term[0], width, inner),
    ]
    vector = jnp.concatenate(terms)
    padding = -vector.shape[0] % (8 * LANES)
    vector = jnp.pad(vector, (0, padding)).reshape(-1, LANES)

    back_parts, main_sum, out_pieces = together(back_parts, main_sum, out_pieces)
    mains = gather_stage(gather_start(main_sum), 0)
    for stage in range(2, stages):
        out_pieces = double(out_pieces, stage)
    for stage in range(1, stages - 1):
        back_parts = scatter_stage(back_parts, stage)
    normed_grad, mains, out_pieces, side_sum, vector = together(
        scatter_end(back_parts), mains, out_pieces, side_sum, vector
    )
    for stage in range(1, stages):
        mains = gather_stage(mains, stage)
    normed_grad = normed_grad.astype(f32)
    cot_row = cotangent[0].astype(f32)
    gained = norm_gain * normed_grad
    slope = inverse * inverse * inverse * jnp.mean(gained * tokens_row, axis=-1, keepdims=True)
    input_grad = cot_row + inverse * gained - tokens_row * slope
    own_scale = lax.dynamic_slice_in_dim(scale, mine * tok_rows, tok_rows, 0)[:, None]
    block_out = (tokens_row + own_scale * mixed_out.astype(f32)).astype(bf16)
    out_weight_grad = assemble_out(place, out_pieces, per_plane)
    in_weight_grad = assemble(place, mains, gather_all(side_sum), dims).T

    vector = sum_all(vector).reshape(-1)
    parts, offset = [], 0
    for term in terms:
        parts.append(vector[offset : offset + term.shape[0]])
        offset += term.shape[0]
    return (
        block_out[None],
        input_grad[None],
        parts[0],
        in_weight_grad,
        parts[1].reshape(conv_weight.shape),
        parts[2],
        parts[3],
        parts[4],
        parts[5],
        parts[6],
        out_weight_grad,
    )


def solution(mesh):
    placed = (
        P("batch", "seq", None),
        P(),
        P("batch", None),
        P(),
        P(),
        P(),
        P(),
        P(),
        P(),
        P("batch", None),
        P("batch", "seq", None),
    )
    return jax.shard_map(
        body,
        mesh=mesh,
        in_specs=placed,
        out_specs=(
            P("batch", "seq", None),
            P("batch", "seq", None),
            P(),
            P("batch", None),
            P(),
            P(),
            P(),
            P(),
            P(),
            P(),
            P("batch", None),
        ),
        check_vma=False,
    )
```

```python
import functools

import jax
import jax.numpy as jnp
from jax import lax
from jax.experimental import pallas as pl
from jax.experimental.pallas import tpu as pltpu
from jax.sharding import PartitionSpec as P

GROUP = 256
LANES = 128
HALF = GROUP // 2
HALO = 8
STEP_ROWS = 16
LOG2E = 1.4426950408889634
epsilon = 1e-05
f32 = jnp.float32
bf16 = jnp.bfloat16
MIB = 2**20


def exchange(value, axis, distance):
    count = lax.axis_size(axis)
    return lax.ppermute(value, axis, [(source, source ^ distance) for source in range(count)])


def bits_of(count):
    return [1 << k for k in range(count.bit_length() - 1)]


def placed_order(count):
    return [2 * k for k in range(count // 2)] + [2 * k + 1 for k in range(count // 2)]


def together(*values):
    return lax.optimization_barrier(values)


def far_orders():
    far = bits_of(lax.axis_size("seq"))[1:]
    return far, far[::-1]


def gather_start(value):
    half = value.shape[0] // 32 * 16
    return tuple({"base": part, "fresh": None, "near": []} for part in (value[:half], value[half:]))


def gather_stage(held, stage):
    grown = []
    for half, order in zip(held, far_orders()):
        base, fresh, near = half["base"], half["fresh"], list(half["near"])
        if stage >= 1:
            merged = base if stage == len(order) else jnp.concatenate([base, fresh], axis=0)
            near.append(exchange(merged if stage == 1 else fresh, "seq", 1))
            base = merged
        if stage < len(order):
            fresh = exchange(base, "seq", order[stage])
        grown.append({"base": base, "fresh": fresh, "near": near})
    return tuple(grown)


def gather_stages():
    return len(bits_of(lax.axis_size("seq")))


def gathered(held):
    arrays, table = [], {}
    for number, (half, order) in enumerate(zip(held, far_orders())):
        indices = [0]
        for bit in order:
            indices += [index | bit for index in indices]
        middle = len(indices) // 2
        groups = [(half["base"], indices[:middle]), (half["fresh"], indices[middle:])]
        bounds = [0] + [2 << k for k in range(len(order))]
        for value, first, last in zip(half["near"], bounds, bounds[1:]):
            groups.append((value, [index | 1 for index in indices[first:last]]))
        for value, members in groups:
            rows = value.shape[0] // len(members)
            for turn, index in enumerate(members):
                table[number, index] = (len(arrays), turn * rows, rows)
            arrays.append(value)
    return arrays, table


def token_pieces(held):
    arrays, table = gathered(held)
    indices = range(lax.axis_size("seq"))
    return arrays, tuple(table[half, index] for index in indices for half in range(2))


def gather_all(value):
    held = gather_start(value)
    for stage in range(gather_stages()):
        held = gather_stage(held, stage)
    return held


def scatter_near(keep, send):
    total = (keep.astype(f32) + exchange(send, "seq", 1).astype(f32)).astype(bf16)
    count = lax.axis_size("seq")
    half = total.shape[0] // count
    total = total.reshape((count // 2, 2, half) + total.shape[1:])
    held = []
    for part, order in enumerate(far_orders()):
        members = [0]
        for bit in order[::-1]:
            members += [member | bit >> 1 for member in members]
        held.append(jnp.stack([total[member, part] for member in members]))
    return tuple(held)


def scatter_stage(held, stage):
    smaller = []
    for value, order in zip(held, far_orders()):
        middle = value.shape[0] // 2
        arriving = exchange(value[middle:], "seq", order[stage])
        smaller.append((value[:middle].astype(f32) + arriving.astype(f32)).astype(bf16))
    return tuple(smaller)


def scatter_end(held):
    return jnp.concatenate([value[0] for value in held], axis=0)


def sum_seq(value):
    for bit in bits_of(lax.axis_size("seq")):
        value = value + exchange(value, "seq", bit)
    return value


def plane_pairs(ahead):
    planes, count = lax.axis_size("batch"), lax.axis_size("seq")
    per = count // planes
    pairs = []
    for owner in range(planes):
        for piece in range(planes):
            for k in range(per):
                holder = owner * count + piece * per + k
                user = (piece + ahead) % planes * count + owner * per + k
                pairs.append((holder, user))
    return pairs


def rows_from_owner(out_weight, width, aheads):
    planes, count = lax.axis_size("batch"), lax.axis_size("seq")
    per, size = count // planes, width // planes
    mine = lax.axis_index("seq")
    piece = lax.dynamic_slice_in_dim(out_weight, mine % per * width + mine // per * size, size, 0)
    return [lax.ppermute(piece, ("batch", "seq"), plane_pairs(ahead)) for ahead in aheads]


def rows_joined(arriving):
    planes, plane = lax.axis_size("batch"), lax.axis_index("batch")
    size = arriving[0].shape[0]
    doubled = jnp.concatenate(arriving[::-1] * 2, axis=0)
    return lax.dynamic_slice_in_dim(doubled, (planes - 1 - plane) * size, planes * size, 0)


def to_owner(summed):
    return lax.ppermute(
        summed, ("batch", "seq"), [(user, holder) for holder, user in plane_pairs(0)]
    )


def double(held, turn):
    bits = bits_of(lax.axis_size("seq"))
    return jnp.concatenate([held, exchange(held, "seq", (bits[1:] + [1])[turn])], axis=0)


def step_values(raw):
    small = jnp.exp(-jnp.abs(raw))
    step = jnp.maximum(raw, 0.0) + jnp.log1p(small)
    sig = jnp.where(raw >= 0, 1.0, small) / (1.0 + small)
    tiny = raw < -20.0
    log_step = jnp.where(tiny, raw, jnp.log(step))
    ratio = jnp.where(tiny, 1.0, sig / step)
    return step, sig, log_step, ratio


def dot(a, b):
    return jnp.dot(a, b, preferred_element_type=f32)


def dot_nt(a, b):
    return lax.dot_general(a, b, (((1,), (1,)), ((), ())), preferred_element_type=f32)


def dot_tn(a, b):
    return lax.dot_general(a, b, (((0,), (0,)), ((), ())), preferred_element_type=f32)


def sigmoid(value):
    return 0.5 * jnp.tanh(0.5 * value) + 0.5


def silu_slope(value):
    sig = sigmoid(value)
    active = value * sig
    return active, sig + active * (1.0 - sig)


def split_parts(value, count):
    parts = []
    for _ in range(count):
        part = value.astype(bf16)
        parts.append(part)
        value = value - part.astype(f32)
    return parts


def sum_along(rows, order):
    parts = jnp.concatenate([part.astype(f32) for part in split_parts(rows, 3)], axis=0)
    total = dot(parts.astype(bf16), order)
    return total[:8] + total[8:16] + total[16:24]


def to_columns(rows):
    stacked = jnp.concatenate(rows, axis=0)
    missing = LANES - stacked.shape[0]
    return jnp.concatenate([stacked, jnp.zeros((missing, GROUP), f32)], axis=0).T


def spread_heads(value, first, heads, size):
    rows = value.shape[0]
    return jnp.concatenate(
        [jnp.broadcast_to(value[:, first + h : first + h + 1], (rows, size)) for h in range(heads)],
        axis=1,
    )


def head_ones(width, size):
    row = lax.broadcasted_iota(jnp.int32, (8, width), 0)
    column = lax.broadcasted_iota(jnp.int32, (8, width), 1)
    return (column // size == row).astype(f32).astype(bf16)


def sum_lanes(value):
    return dot_nt(jnp.ones((8, value.shape[1]), bf16), value.astype(bf16))


def ones_where(condition):
    return jnp.where(condition, 1.0, 0.0).astype(bf16)


def order_indices(length):
    row = lax.broadcasted_iota(jnp.int32, (length, length), 0)
    column = lax.broadcasted_iota(jnp.int32, (length, length), 1)
    return row, column


def fetch(arrays, table, which, target, semaphore):
    for index, (array, row, rows) in enumerate(table):

        @pl.when(which == index)
        def _():
            pltpu.make_async_copy(arrays[array].at[pl.ds(row, rows)], target, semaphore).start()


def fetched(arrays, table, buffer, semaphores, order):
    step = pl.program_id(0)
    slot, other = lax.rem(step, 2), lax.rem(step + 1, 2)

    @pl.when(step == 0)
    def _():
        fetch(arrays, table, order(0), buffer.at[0], semaphores.at[0])

    @pl.when(step + 1 < pl.num_programs(0))
    def _():
        fetch(arrays, table, order(step + 1), buffer.at[other], semaphores.at[other])

    source = arrays[0].at[pl.ds(0, table[0][2])]
    pltpu.make_async_copy(source, buffer.at[slot], semaphores.at[slot]).wait()
    return buffer[slot]


def in_time(place, block):
    return ((block // 2) ^ place) * 2 + block % 2


def device_place(place, device, count):
    relative = device ^ place
    return (relative & 1) * (count // 2) + (relative >> 1)


def block_place(place, block, count):
    return device_place(place, block // 2, count) * 2 + block % 2


def forward_kernel(dims, table, given, place_ref, *refs):
    heads, size, states, _ = dims
    width = heads * size
    conv_cols = width + 2 * states
    arrays, normeds, refs = refs[:given], refs[given : 2 * given], refs[2 * given :]
    conv_w_ref, conv_b_ref, step_ref, rows_ref = refs[:4]
    conv_in_ref, active_ref, slope_ref, gate_act_ref, gate_slope_ref = refs[4:9]
    raw_ref, ssd_ref, start_ref, scaled_ref, square_ref, placed_ref, normed_ref = refs[9:16]
    state, padded, order, barred, buffer, semaphores, copied = refs[16:]
    turn = pl.program_id(0)

    @pl.when(turn == 0)
    def _():
        state[...] = jnp.zeros_like(state)
        padded[0:HALO] = jnp.zeros_like(padded[0:HALO])
        row, column = order_indices(GROUP)
        order[...] = ones_where(row <= column)
        row, column = order_indices(HALF)
        barred[...] = jnp.where(row >= column, 0.0, -1e30)

    projected = fetched(
        arrays, table, buffer, semaphores, lambda step: in_time(place_ref[0], step)
    )
    target = normed_ref.at[pl.ds(pl.multiple_of(turn * GROUP, GROUP), GROUP)]
    fetch(normeds, table, in_time(place_ref[0], turn), target, copied)
    conv_in = projected[:, width : width + conv_cols].astype(bf16)
    conv_in_ref[...] = conv_in
    padded[HALO : HALO + GROUP] = conv_in.astype(f32)
    conv_w = conv_w_ref[...]
    taps = conv_w.shape[0]
    pre = conv_b_ref[...]
    for k in range(taps):
        top = HALO - (taps - 1) + k
        pre = pre + conv_w[k : k + 1] * padded[top : top + GROUP]
    padded[0:HALO] = padded[GROUP : GROUP + HALO]
    active, slope = silu_slope(pre)
    active = active.astype(bf16)
    active_ref[...] = active
    slope_ref[...] = slope.astype(bf16)
    signal = active[:, :width]
    entry = active[:, width : width + states]
    readout = active[:, width + states :]
    signal_wide = signal.astype(f32)

    raw = projected[:, width + conv_cols :].T[:8]
    raw_ref[0] = raw
    step, _, log_step, _ = step_values(raw + step_ref[0:8, 0:1])
    running = sum_along(step * step_ref[8:16, 0:1], order[...])
    later = running - log_step
    total = running[:, GROUP - 1 :]
    columns = to_columns([running * LOG2E, jnp.exp(running), jnp.exp(total - later)])
    later = later * LOG2E
    early_wide = spread_heads(columns, 8, heads, size)
    tail_wide = spread_heads(columns, 16, heads, size)
    first, second = slice(0, HALF), slice(HALF, GROUP)
    scores = dot_nt(readout[first], entry[first])
    later_scores = dot_nt(readout[second], entry)
    within = []
    for h in range(heads):
        part = signal[:, h * size : (h + 1) * size]
        begin, end = columns[first, h : h + 1], columns[second, h : h + 1]
        row_first, row_second = later[h : h + 1, first], later[h : h + 1, second]
        near = jnp.exp2(begin - row_first + barred[...]) * scores
        full = jnp.exp2(end - row_first) * later_scores[:, first]
        last = jnp.exp2(end - row_second + barred[...]) * later_scores[:, second]
        both = jnp.concatenate([full.astype(bf16), last.astype(bf16)], axis=1)
        within.append(
            jnp.concatenate([dot(near.astype(bf16), part[first]), dot(both, part)], axis=0)
        )
    start = state[...]
    start_low = start.astype(bf16)
    start_ref[0] = start_low
    carried = dot(readout, start_low) * early_wide
    ssd = jnp.concatenate(within, axis=1) + carried + rows_ref[0:1] * signal_wide
    tail = (signal_wide * tail_wide).astype(bf16)
    state[...] = start * early_wide[GROUP - 1 :] + dot_tn(entry, tail)

    gate_act, gate_slope = silu_slope(projected[:, :width])
    gate_act_ref[...] = gate_act.astype(bf16)
    gate_slope_ref[...] = gate_slope.astype(bf16)
    ssd_ref[...] = ssd
    gated = ssd * gate_act
    scaled = (gated * rows_ref[1:2]).astype(bf16)
    scaled_ref[...] = scaled
    placed_ref[...] = scaled
    square_ref[0] = sum_lanes(gated * gated)

    @pl.when(turn == pl.num_programs(0) - 1)
    def _():
        pltpu.make_async_copy(normed_ref, normed_ref, copied).wait()


def time_estimate(microseconds, accessed):
    return pl.CostEstimate(
        flops=int(microseconds * 1.1e9), bytes_accessed=int(accessed), transcendentals=0
    )


def fixed(shape):
    return pl.BlockSpec(shape, lambda turn, place: (0,) * len(shape), pipeline_mode=pl.Buffered(1))


def anywhere(values):
    return [pl.BlockSpec(memory_space=pltpu.HBM)] * len(values)


def run_forward(place, projected, normeds, params, dims):
    heads, size, states, count = dims
    arrays, table = projected
    normeds = normeds[0]
    dim, columns = normeds[0].shape[1], arrays[0].shape[1]
    width, conv_cols = heads * size, params[0].shape[1]
    blocks = len(table)
    tokens = blocks * GROUP

    def moving(columns):
        return pl.BlockSpec((GROUP, columns), lambda turn, place: (turn, 0))

    def rows_of_block(height, columns):
        return pl.BlockSpec((1, height, columns), lambda turn, place: (turn, 0, 0))

    return pl.pallas_call(
        functools.partial(forward_kernel, dims, table, len(arrays)),
        grid_spec=pltpu.PrefetchScalarGridSpec(
            num_scalar_prefetch=1,
            grid=(blocks,),
            in_specs=[
                *anywhere(arrays),
                *anywhere(normeds),
                *[fixed(param.shape) for param in params],
            ],
            out_specs=[
                moving(conv_cols),
                moving(conv_cols),
                moving(conv_cols),
                moving(width),
                moving(width),
                rows_of_block(8, GROUP),
                moving(width),
                rows_of_block(states, width),
                moving(width),
                rows_of_block(8, GROUP),
                pl.BlockSpec(
                    (GROUP, width), lambda turn, place: (block_place(place[0], turn, count), 0)
                ),
                *anywhere(range(1)),
            ],
            scratch_shapes=[
                pltpu.VMEM((states, width), f32),
                pltpu.VMEM((HALO + GROUP, conv_cols), f32),
                pltpu.VMEM((GROUP, GROUP), bf16),
                pltpu.VMEM((HALF, HALF), f32),
                pltpu.VMEM((2, GROUP, columns), f32),
                pltpu.SemaphoreType.DMA((2,)),
                pltpu.SemaphoreType.DMA,
            ],
        ),
        out_shape=[
            jax.ShapeDtypeStruct((tokens, conv_cols), bf16),
            jax.ShapeDtypeStruct((tokens, conv_cols), bf16),
            jax.ShapeDtypeStruct((tokens, conv_cols), bf16),
            jax.ShapeDtypeStruct((tokens, width), bf16),
            jax.ShapeDtypeStruct((tokens, width), bf16),
            jax.ShapeDtypeStruct((blocks, 8, GROUP), f32),
            jax.ShapeDtypeStruct((tokens, width), f32),
            jax.ShapeDtypeStruct((blocks, states, width), bf16),
            jax.ShapeDtypeStruct((tokens, width), bf16),
            jax.ShapeDtypeStruct((blocks, 8, GROUP), f32),
            jax.ShapeDtypeStruct((tokens, width), bf16),
            jax.ShapeDtypeStruct((tokens, dim), bf16),
        ],
        compiler_params=pltpu.CompilerParams(vmem_limit_bytes=60 * MIB),
        cost_estimate=time_estimate(blocks * 2.2, tokens * (4 * dim + 24 * width)),
        name="forward_blocks",
    )(place, *arrays, *normeds, *params)


def out_grad_kernel(table, given, place_ref, *refs):
    arrays, refs = refs[:given], refs[given:]
    scaled_ref, out_rows_ref, out_grad_ref, slope_ref, cot_ref = refs[:5]
    buffer, semaphores, copied = refs[5:]
    turn = pl.program_id(0)
    cot = fetched(arrays, table, buffer, semaphores, lambda step: in_time(place_ref[0], step))
    target = cot_ref.at[pl.ds(pl.multiple_of(turn * GROUP, GROUP), GROUP)]
    fetch(arrays, table, in_time(place_ref[0], turn), target, copied)
    out_grad = dot_nt(cot, out_rows_ref[...])
    out_grad_ref[...] = out_grad
    slope_ref[0] = sum_lanes(out_grad * scaled_ref[...].astype(f32))

    @pl.when(turn == pl.num_programs(0) - 1)
    def _():
        pltpu.make_async_copy(cot_ref, cot_ref, copied).wait()


def run_out_grad(place, cots, scaled, out_rows):
    arrays, table = cots
    width, dim = out_rows.shape
    blocks = len(table)
    tokens = blocks * GROUP
    return pl.pallas_call(
        functools.partial(out_grad_kernel, table, len(arrays)),
        grid_spec=pltpu.PrefetchScalarGridSpec(
            num_scalar_prefetch=1,
            grid=(blocks,),
            in_specs=[
                *anywhere(arrays),
                pl.BlockSpec((GROUP, width), lambda turn, place: (turn, 0)),
                fixed(out_rows.shape),
            ],
            out_specs=[
                pl.BlockSpec((GROUP, width), lambda turn, place: (turn, 0)),
                pl.BlockSpec((1, 8, GROUP), lambda turn, place: (turn, 0, 0)),
                *anywhere(range(1)),
            ],
            scratch_shapes=[
                pltpu.VMEM((2, GROUP, dim), bf16),
                pltpu.SemaphoreType.DMA((2,)),
                pltpu.SemaphoreType.DMA,
            ],
        ),
        out_shape=[
            jax.ShapeDtypeStruct((tokens, width), f32),
            jax.ShapeDtypeStruct((blocks, 8, GROUP), f32),
            jax.ShapeDtypeStruct((tokens, dim), bf16),
        ],
        compiler_params=pltpu.CompilerParams(vmem_limit_bytes=60 * MIB),
        cost_estimate=time_estimate(12, tokens * (6 * dim + 6 * width)),
        name="out_grad",
    )(place, *arrays, scaled, out_rows)


def backward_kernel(dims, place_ref, *refs):
    heads, size, states, count = dims
    width = heads * size
    conv_cols = width + 2 * states
    conv_in_ref, active_ref, slope_ref, gate_act_ref, gate_slope_ref = refs[:5]
    raw_ref, ssd_ref, start_ref, out_grad_ref, norm_ref = refs[5:10]
    conv_w_ref, step_ref, rows_ref = refs[10:13]
    out_ref, keep_ref, send_ref = refs[13:16]
    sums = refs[16:22]
    gain_ref, skip_ref, conv_wg_ref, conv_bg_ref, bias_ref, rate_ref = sums
    state, pre_grads, order, back_order, barred, placed, semaphores = refs[22:]
    taps = conv_w_ref.shape[0]
    turn = pl.program_id(0)
    slot = lax.rem(turn, 2)

    def copy_to(target, row):
        return pltpu.make_async_copy(
            placed.at[slot], target.at[pl.ds(row, GROUP)], semaphores.at[slot]
        )

    @pl.when(turn >= 2)
    def _():
        copy_to(keep_ref, 0).wait()

    @pl.when(pl.program_id(0) == 0)
    def _():
        state[...] = jnp.zeros_like(state)
        pre_grads[0:HALO] = jnp.zeros_like(pre_grads[0:HALO])
        for total in sums:
            total[...] = jnp.zeros_like(total)
        row, column = order_indices(GROUP)
        order[...] = ones_where(row <= column)
        back_order[...] = ones_where(row >= column)
        row, column = order_indices(HALF)
        barred[...] = jnp.where(row <= column, 0.0, -1e30)

    gate_act, ssd, out_grad = gate_act_ref[...].astype(f32), ssd_ref[...], out_grad_ref[...]
    norms = norm_ref[0].T
    scale, slope = norms[:, 0:1], norms[:, 1:2]
    gated = ssd * gate_act
    gain_ref[...] += jnp.sum(out_grad * (gated * scale), axis=0, keepdims=True)
    gated_grad = out_grad * (rows_ref[1:2] * scale) - gated * slope
    grad_low = (gated_grad * gate_act).astype(bf16)
    gate_grad = (gated_grad * ssd * gate_slope_ref[...].astype(f32)).astype(bf16)
    out_ref[:, :width] = gate_grad
    placed[slot, :, :width] = gate_grad
    ssd_grad = grad_low.astype(f32)

    raw = raw_ref[0] + step_ref[0:8, 0:1]
    rate = step_ref[8:16, 0:1]
    step, sig, log_step, ratio = step_values(raw)
    decay = step * rate
    running = sum_along(decay, order[...])
    later = running - log_step
    total = running[:, GROUP - 1 :]
    columns = to_columns([later * LOG2E, jnp.exp(running), jnp.exp(total - later)])
    running = running * LOG2E
    early_wide = spread_heads(columns, 8, heads, size)
    tail_wide = spread_heads(columns, 16, heads, size)

    signal = active_ref[:, :width]
    entry = active_ref[:, width : width + states]
    readout = active_ref[:, width + states :]
    signal_wide = signal.astype(f32)
    start_low = start_ref[0]
    end_grad = state[...]
    end_low = end_grad.astype(bf16)
    first, second = slice(0, HALF), slice(HALF, GROUP)
    scores = dot_nt(entry[first], readout)
    later_scores = dot_nt(entry[second], readout[second])
    near_grad, far_grad, last_grad = 0.0, 0.0, 0.0
    within = []
    for h in range(heads):
        part, grad = signal[:, h * size : (h + 1) * size], grad_low[:, h * size : (h + 1) * size]
        begin, end = columns[first, h : h + 1], columns[second, h : h + 1]
        row_first, row_second = running[h : h + 1, first], running[h : h + 1, second]
        near = jnp.exp2(row_first - begin + barred[...])
        full = jnp.exp2(row_second - begin)
        last = jnp.exp2(row_second - end + barred[...])
        both = jnp.concatenate(
            [
                (near * scores[:, first]).astype(bf16),
                (full * scores[:, second]).astype(bf16),
            ],
            axis=1,
        )
        final = (last * later_scores).astype(bf16)
        within.append(jnp.concatenate([dot(both, grad), dot(final, grad[second])], axis=0))
        cross = dot_nt(part[first], grad)
        near_grad = near_grad + cross[:, first] * near
        far_grad = far_grad + cross[:, second] * full
        last_grad = last_grad + dot_nt(part[second], grad[second]) * last
    tail_grad = tail_wide * dot(entry, end_low)
    signal_grad = jnp.concatenate(within, axis=1) + tail_grad
    score_first = jnp.concatenate([near_grad, far_grad], axis=1).astype(bf16)
    score_second = last_grad.astype(bf16)
    tail = (signal_wide * tail_wide).astype(bf16)
    head_grad = (ssd_grad * early_wide).astype(bf16)
    entry_grad = jnp.concatenate(
        [dot(score_first, readout), dot(score_second, readout[second])], axis=0
    ) + dot_nt(tail, end_low)
    readout_grad = dot_tn(score_first, entry[first]) + dot_nt(head_grad, start_low)
    readout_last = readout_grad[second] + dot_tn(score_second, entry[second])
    total_wide = early_wide[GROUP - 1 :]
    state[...] = end_grad * total_wide + dot_tn(readout, head_grad)

    skip = rows_ref[0:1]
    ones = head_ones(width, size)
    column_part = signal_wide * signal_grad
    row_part = ssd_grad * (ssd - skip * signal_wide)
    end_part = jnp.sum(signal_wide * tail_grad, axis=0, keepdims=True) + total_wide * jnp.sum(
        start_low.astype(f32) * end_grad, axis=0, keepdims=True
    )

    def head_sums(value, parts):
        return sum(dot_nt(ones, part) for part in split_parts(value, parts))

    end_rows = head_sums(jnp.broadcast_to(end_part, (8, width)), 2)[:, 0:1]
    decay_grad = sum_along(head_sums(row_part - column_part, 2), back_order[...]) + end_rows
    raw_grad = head_sums(column_part, 1) * ratio + decay_grad * rate * sig
    skip_ref[...] += jnp.sum(ssd_grad * signal_wide, axis=0, keepdims=True)
    bias_ref[...] += raw_grad
    rate_ref[...] += decay_grad * decay
    raw_low = to_columns([raw_grad]).astype(bf16)
    out_ref[:, width + conv_cols :] = raw_low
    placed[slot, :, width + conv_cols :] = raw_low

    pre_grads[GROUP : GROUP + HALO] = pre_grads[0:HALO]
    pre_grads[0:GROUP, :width] = (signal_grad + skip * ssd_grad) * slope_ref[:, :width].astype(f32)
    sides = slope_ref[:, width:].astype(f32)
    pre_grads[0:GROUP, width : width + states] = entry_grad * sides[:, :states]
    pre_grads[0:HALF, width + states :] = readout_grad[first] * sides[first, states:]
    pre_grads[HALF:GROUP, width + states :] = readout_last * sides[second, states:]
    conv_w = conv_w_ref[...]
    conv_in = conv_in_ref[...].astype(f32)
    conv_grad = 0.0
    for k in range(taps):
        ahead = taps - 1 - k
        shifted = pre_grads[ahead : ahead + GROUP]
        conv_grad = conv_grad + conv_w[k : k + 1] * shifted
        conv_wg_ref[k : k + 1] += jnp.sum(shifted * conv_in, axis=0, keepdims=True)
        if ahead == 0:
            conv_bg_ref[...] += jnp.sum(shifted, axis=0, keepdims=True)
    conv_low = conv_grad.astype(bf16)
    out_ref[:, width : width + conv_cols] = conv_low
    placed[slot, :, width : width + conv_cols] = conv_low

    position = block_place(place_ref[0], pl.num_programs(0) - 1 - turn, count)

    @pl.when(position < count)
    def _():
        copy_to(keep_ref, pl.multiple_of(position * GROUP, GROUP)).start()

    @pl.when(position >= count)
    def _():
        copy_to(send_ref, pl.multiple_of((position - count) * GROUP, GROUP)).start()

    @pl.when(turn == pl.num_programs(0) - 1)
    def _():
        for other in range(2):
            pltpu.make_async_copy(
                placed.at[other], keep_ref.at[pl.ds(0, GROUP)], semaphores.at[other]
            ).wait()


def run_backward(place, values, params, dims):
    heads, size, states, _ = dims
    conv_cols, width = values[0].shape[1], heads * size
    tokens = values[0].shape[0]
    blocks = tokens // GROUP
    last = blocks - 1
    out_cols = width + conv_cols + LANES

    def moving(columns):
        return pl.BlockSpec((GROUP, columns), lambda turn, place: (last - turn, 0))

    def rows_of_block():
        return pl.BlockSpec((1, 8, GROUP), lambda turn, place: (last - turn, 0, 0))

    sums = [(1, width), (1, width), params[0].shape, (1, conv_cols), (8, GROUP), (8, GROUP)]
    return pl.pallas_call(
        functools.partial(backward_kernel, dims),
        grid_spec=pltpu.PrefetchScalarGridSpec(
            num_scalar_prefetch=1,
            grid=(blocks,),
            in_specs=[
                moving(conv_cols),
                moving(conv_cols),
                moving(conv_cols),
                moving(width),
                moving(width),
                rows_of_block(),
                moving(width),
                pl.BlockSpec((1, states, width), lambda turn, place: (last - turn, 0, 0)),
                moving(width),
                rows_of_block(),
                *[fixed(param.shape) for param in params],
            ],
            out_specs=[
                moving(out_cols),
                *anywhere(range(2)),
                *[fixed(shape) for shape in sums],
            ],
            scratch_shapes=[
                pltpu.VMEM((states, width), f32),
                pltpu.VMEM((GROUP + HALO, conv_cols), f32),
                pltpu.VMEM((GROUP, GROUP), bf16),
                pltpu.VMEM((GROUP, GROUP), bf16),
                pltpu.VMEM((HALF, HALF), f32),
                pltpu.VMEM((2, GROUP, out_cols), bf16),
                pltpu.SemaphoreType.DMA((2,)),
            ],
        ),
        out_shape=[
            jax.ShapeDtypeStruct((tokens, out_cols), bf16),
            jax.ShapeDtypeStruct((tokens // 2, out_cols), bf16),
            jax.ShapeDtypeStruct((tokens // 2, out_cols), bf16),
        ]
        + [jax.ShapeDtypeStruct(shape, f32) for shape in sums],
        compiler_params=pltpu.CompilerParams(vmem_limit_bytes=60 * MIB),
        cost_estimate=time_estimate(blocks * 3.5, tokens * 40 * width),
        name="backward_blocks",
    )(place, *values, *params)


def widen_kernel(place_ref, piece_ref, out_ref):
    out_ref[...] = piece_ref[0].astype(f32)


def assemble_out(place, pieces, per):
    count, size, dim = pieces.shape
    groups = count // per

    def source(turn, place):
        relative = (turn % groups * per + turn // groups) ^ place[0]
        return ((relative & 1) * (count // 2) + (relative >> 1), 0, 0)

    return pl.pallas_call(
        widen_kernel,
        grid_spec=pltpu.PrefetchScalarGridSpec(
            num_scalar_prefetch=1,
            grid=(count,),
            in_specs=[pl.BlockSpec((1, size, dim), source)],
            out_specs=pl.BlockSpec((size, dim), lambda turn, place: (turn, 0)),
        ),
        out_shape=jax.ShapeDtypeStruct((count * size, dim), f32),
        cost_estimate=time_estimate(5, count * size * dim * 6),
        name="assemble_out_weight_grad",
    )(place, pieces)


def assemble_kernel(dims, table, place_ref, *refs):
    heads, size, states, count = dims
    width, shared = heads * size, 2 * states
    inner = count * width
    arrays, out_ref, sums = refs[:-2], refs[-2], refs[-1]
    for relative in range(count):
        device = place_ref[0] ^ relative
        parts = []
        for half in range(2):
            array, row, height = table[half, relative]
            parts.append(arrays[array][row : row + height].astype(f32))
        columns = jnp.concatenate(parts, axis=0).T
        out_ref[pl.ds(pl.multiple_of(device * width, 8), width)] = columns[:width]
        middle = pl.multiple_of(inner + device * width, 8)
        out_ref[pl.ds(middle, width)] = columns[width : 2 * width]
        sums[device] = columns[2 * width : 2 * width + shared + STEP_ROWS]
    total = sums[0, :shared]
    for device in range(1, count):
        total = total + sums[device, :shared]
    out_ref[2 * inner : 2 * inner + shared] = total
    for device in range(count):
        last = 2 * inner + shared + device * heads
        out_ref[last : last + heads] = sums[device, shared : shared + heads]


def assemble(place, held, dims):
    heads, size, states, count = dims
    arrays, table = gathered(held)
    rows = sum(table[half, 0][2] for half in range(2))
    out_rows = 2 * count * heads * size + 2 * states + count * heads

    def whole(value):
        return pl.BlockSpec(
            value.shape,
            lambda turn, place: (0,) * len(value.shape),
            pipeline_mode=pl.Buffered(1),
        )

    return pl.pallas_call(
        functools.partial(assemble_kernel, dims, table),
        grid_spec=pltpu.PrefetchScalarGridSpec(
            num_scalar_prefetch=1,
            grid=(1,),
            in_specs=[whole(value) for value in arrays],
            out_specs=pl.BlockSpec(
                (out_rows, rows), lambda turn, place: (0, 0), pipeline_mode=pl.Buffered(1)
            ),
            scratch_shapes=[pltpu.VMEM((count, 2 * states + STEP_ROWS, rows), f32)],
        ),
        out_shape=jax.ShapeDtypeStruct((out_rows, rows), f32),
        compiler_params=pltpu.CompilerParams(vmem_limit_bytes=60 * MIB),
        cost_estimate=time_estimate(8, out_rows * rows * 6),
        name="assemble_in_weight_grad",
    )(place, *arrays)


def body(
    tokens,
    norm_gain,
    in_weight,
    conv_weight,
    conv_bias,
    dt_bias,
    decay_log,
    skip_scale,
    gate_gain,
    out_weight,
    cotangent,
):
    count, mine = lax.axis_size("seq"), lax.axis_index("seq")
    planes = lax.axis_size("batch")
    place = mine.astype(jnp.int32).reshape(1)
    inner, all_heads, conv_all = gate_gain.shape[0], dt_bias.shape[0], conv_bias.shape[0]
    size, states = inner // all_heads, (conv_all - inner) // 2
    heads, width = all_heads // count, inner // count
    dims = (heads, size, states, count)
    shared = 2 * states
    conv_cols = width + shared
    tok_rows = tokens.shape[1]
    per_plane = out_weight.shape[0] // width

    def own(vector, per, first=0):
        return lax.dynamic_slice_in_dim(vector, first + mine * per, per, vector.ndim - 1)

    def own_conv(array, first=0):
        return jnp.concatenate(
            [own(array, width, first), array[..., first + inner : first + conv_all]], axis=-1
        )

    tokens_row = tokens[0].astype(f32)
    inverse = lax.rsqrt(jnp.mean(tokens_row * tokens_row, axis=-1, keepdims=True) + epsilon)
    normed_own = (tokens_row * inverse * norm_gain).astype(bf16)
    step_own = own(in_weight, heads, inner + conv_all)
    w_own = jnp.concatenate(
        [
            own(in_weight, width),
            own_conv(in_weight, inner),
            jnp.pad(step_own, ((0, 0), (0, LANES - heads))),
        ],
        axis=1,
    )
    w_cols = lax.all_gather(w_own, "batch", axis=0, tiled=True)
    stages = gather_stages()
    held = gather_stage(gather_stage(gather_start(normed_own), 0), 1)
    held, cot_own = together(held, cotangent[0])
    cots = gather_stage(gather_start(cot_own), 0)
    for stage in range(2, stages):
        held = gather_stage(held, stage)
    w_cols, held, cots, out_owned = together(w_cols, held, cots, out_weight)
    normeds = token_pieces(held)
    cots = gather_stage(cots, 1)
    out_pieces = rows_from_owner(out_owned, width, range(1))

    conv_w, conv_b = own_conv(conv_weight), own_conv(conv_bias)[None]
    per_head = jnp.stack([own(dt_bias, heads), -jnp.exp(own(decay_log, heads))])
    per_head = jnp.pad(per_head, ((0, 0), (0, 8 - heads))).reshape(16, 1)
    step_rows = jnp.broadcast_to(per_head, (16, LANES))
    gain_own = own(gate_gain, width)[None]
    rows = jnp.concatenate(
        [jnp.repeat(own(skip_scale, heads), size)[None], gain_own, jnp.zeros((6, width), f32)],
        axis=0,
    )
    projected = [jnp.dot(array, w_cols, preferred_element_type=f32) for array in normeds[0]]
    projected, out_pieces, out_owned = together(projected, out_pieces, out_owned)
    out_pieces = out_pieces + rows_from_owner(out_owned, width, range(1, planes))
    conv_in, active, slope, gate_act, gate_slope, raw, *rest = run_forward(
        place, (projected, normeds[1]), normeds, (conv_w, conv_b, step_rows, rows), dims
    )
    ssd, starts, scaled, squares, placed, normed = rest
    placed, cots, out_pieces = together(placed, cots, out_pieces)
    for stage in range(2, stages):
        cots = gather_stage(cots, stage)
    out_rows = rows_joined(out_pieces)

    middle = placed.shape[0] // 2
    out_send = dot(placed[middle:], out_rows).astype(bf16)
    out_send, cots = together(out_send, cots)
    out_grad, slopes, cot = run_out_grad(place, token_pieces(cots), scaled, out_rows)
    sums = sum_seq(jnp.stack([squares[:, 0].reshape(-1), slopes[:, 0].reshape(-1)]))
    out_parts = scatter_near(dot(placed[:middle], out_rows), out_send)
    scale = lax.rsqrt(sums[0] / inner + epsilon)
    norms = jnp.stack([scale, scale * scale * scale * sums[1] / inner])
    norms = jnp.pad(norms, ((0, 6), (0, 0))).reshape(8, -1, GROUP).swapaxes(0, 1)
    scaled_cot = (cot.astype(f32) * scale[:, None]).astype(bf16)
    out_term = jnp.einsum("te,td->ed", scaled, scaled_cot, preferred_element_type=f32)
    out_term, norms, out_parts = together(out_term.astype(bf16), norms, out_parts)
    out_sum = lax.psum_scatter(out_term, "batch", scatter_dimension=0, tiled=True)
    out_parts = scatter_stage(out_parts, 0)

    values = (conv_in, active, slope, gate_act, gate_slope, raw, ssd, starts, out_grad, norms)
    proj_grad, back_keep, back_send, *terms = run_backward(
        place, values, (conv_w, step_rows, rows), dims
    )
    gain_term, skip_term, conv_w_term, conv_b_term, bias_term, rate_term = terms
    proj_grad, back_keep, back_send, out_parts, out_sum = together(
        proj_grad, back_keep, back_send, out_parts, out_sum
    )

    out_parts = scatter_stage(out_parts, 1)
    out_pieces = to_owner(out_sum)[None]
    in_term = jnp.einsum("td,tf->df", normed, proj_grad, preferred_element_type=f32).astype(bf16)
    in_term, back_keep, back_send, out_parts, out_pieces = together(
        in_term, back_keep, back_send, out_parts, out_pieces
    )
    in_sum = lax.psum_scatter(in_term, "batch", scatter_dimension=0, tiled=True)

    def back_part(part):
        return jnp.einsum("tf,df->td", part, w_cols, preferred_element_type=f32)

    for stage in range(2, stages - 1):
        out_parts = scatter_stage(out_parts, stage)
    out_pieces = double(out_pieces, 0)
    back_send = back_part(back_send).astype(bf16)
    back_send, back_keep, out_pieces = together(back_send, back_keep, out_pieces)
    out_pieces = double(out_pieces, 1)
    back_parts = scatter_near(back_part(back_keep), back_send)
    back_parts, out_pieces, in_term = together(back_parts, out_pieces, in_term)
    back_parts = scatter_stage(back_parts, 0)
    for stage in range(2, stages):
        out_pieces = double(out_pieces, stage)

    norm_gain_term = jnp.sum(in_term.astype(f32) * w_cols.astype(f32), axis=1) / norm_gain

    def among_heads(vector, per, total):
        return lax.dynamic_update_slice_in_dim(jnp.zeros((total,), f32), vector, mine * per, 0)

    def among_conv(array):
        wide = jnp.zeros((array.shape[0], inner), f32)
        wide = lax.dynamic_update_slice_in_dim(wide, array[:, :width], mine * width, 1)
        return jnp.concatenate([wide, array[:, width:]], axis=1).reshape(-1)

    skip_heads = jnp.sum(skip_term.reshape(heads, size), axis=1)
    terms = [
        norm_gain_term,
        among_conv(conv_w_term),
        among_conv(conv_b_term),
        among_heads(jnp.sum(bias_term[:heads], axis=1), heads, all_heads),
        among_heads(jnp.sum(rate_term[:heads], axis=1), heads, all_heads),
        among_heads(skip_heads, heads, all_heads),
        among_heads(gain_term[0], width, inner),
    ]
    vector = jnp.concatenate(terms)
    padding = -vector.shape[0] % (8 * LANES)
    vector = jnp.pad(vector, (0, padding)).reshape(-1, LANES)

    axes = [(axis, bit) for axis in ("seq", "batch") for bit in bits_of(lax.axis_size(axis))]
    for axis, bit in axes[:-1]:
        vector = vector + exchange(vector, axis, bit)
    out_weight_grad = assemble_out(place, out_pieces, per_plane)
    back_parts, vector, out_weight_grad, in_sum = together(
        back_parts, vector, out_weight_grad, in_sum
    )
    columns = gather_stage(gather_start(in_sum), 0)
    for stage in range(1, stages - 1):
        back_parts = scatter_stage(back_parts, stage)
    vector = (vector + exchange(vector, *axes[-1])).reshape(-1)
    normed_grad, columns, vector = together(scatter_end(back_parts), columns, vector)
    for stage in range(1, stages):
        columns = gather_stage(columns, stage)
    normed_grad = normed_grad.astype(f32)
    cot_row = cotangent[0].astype(f32)
    gained = norm_gain * normed_grad
    slope = inverse * inverse * inverse * jnp.mean(gained * tokens_row, axis=-1, keepdims=True)
    input_grad = cot_row + inverse * gained - tokens_row * slope
    own_scale = lax.dynamic_slice_in_dim(scale, mine * tok_rows, tok_rows, 0)[:, None]
    mixed_out = scatter_end(out_parts).astype(f32)
    block_out = (tokens_row + own_scale * mixed_out).astype(bf16)
    in_weight_grad = assemble(place, columns, dims).T

    parts, offset = [], 0
    for term in terms:
        parts.append(vector[offset : offset + term.shape[0]])
        offset += term.shape[0]
    return (
        block_out[None],
        input_grad[None],
        parts[0],
        in_weight_grad,
        parts[1].reshape(conv_weight.shape),
        parts[2],
        parts[3],
        parts[4],
        parts[5],
        parts[6],
        out_weight_grad,
    )


def solution(mesh):
    placed = (
        P("batch", "seq", None),
        P(),
        P("batch", None),
        P(),
        P(),
        P(),
        P(),
        P(),
        P(),
        P("batch", None),
        P("batch", "seq", None),
    )
    return jax.shard_map(
        body,
        mesh=mesh,
        in_specs=placed,
        out_specs=(
            P("batch", "seq", None),
            P("batch", "seq", None),
            P(),
            P("batch", None),
            P(),
            P(),
            P(),
            P(),
            P(),
            P(),
            P("batch", None),
        ),
        check_vma=False,
    )
```

```python
import functools

import jax
import jax.numpy as jnp
from jax import lax
from jax.experimental import pallas as pl
from jax.experimental.pallas import tpu as pltpu
from jax.sharding import PartitionSpec as P

GROUP = 256
LANES = 128
HALF = GROUP // 2
HALO = 8
STEP_ROWS = 16
LOG2E = 1.4426950408889634
epsilon = 1e-05
f32 = jnp.float32
bf16 = jnp.bfloat16
MIB = 2**20


def exchange(value, axis, distance):
    count = lax.axis_size(axis)
    return lax.ppermute(value, axis, [(source, source ^ distance) for source in range(count)])


def bits_of(count):
    return [1 << k for k in range(count.bit_length() - 1)]


def placed_order(count):
    return [2 * k for k in range(count // 2)] + [2 * k + 1 for k in range(count // 2)]


def together(*values):
    return lax.optimization_barrier(values)


def far_orders():
    far = bits_of(lax.axis_size("seq"))[1:]
    return far, far[::-1]


def gather_start(value):
    half = value.shape[0] // 32 * 16
    return tuple({"base": part, "fresh": None, "near": []} for part in (value[:half], value[half:]))


def gather_stage(held, stage):
    grown = []
    for half, order in zip(held, far_orders()):
        base, fresh, near = half["base"], half["fresh"], list(half["near"])
        if stage >= 1:
            merged = base if stage == len(order) else jnp.concatenate([base, fresh], axis=0)
            near.append(exchange(merged if stage == 1 else fresh, "seq", 1))
            base = merged
        if stage < len(order):
            fresh = exchange(base, "seq", order[stage])
        grown.append({"base": base, "fresh": fresh, "near": near})
    return tuple(grown)


def gather_stages():
    return len(bits_of(lax.axis_size("seq")))


def gathered(held):
    arrays, table = [], {}
    for number, (half, order) in enumerate(zip(held, far_orders())):
        indices = [0]
        for bit in order:
            indices += [index | bit for index in indices]
        middle = len(indices) // 2
        groups = [(half["base"], indices[:middle]), (half["fresh"], indices[middle:])]
        bounds = [0] + [2 << k for k in range(len(order))]
        for value, first, last in zip(half["near"], bounds, bounds[1:]):
            groups.append((value, [index | 1 for index in indices[first:last]]))
        for value, members in groups:
            rows = value.shape[0] // len(members)
            for turn, index in enumerate(members):
                table[number, index] = (len(arrays), turn * rows, rows)
            arrays.append(value)
    return arrays, table


def token_pieces(held):
    arrays, table = gathered(held)
    indices = range(lax.axis_size("seq"))
    return arrays, tuple(table[half, index] for index in indices for half in range(2))


def gather_all(value):
    held = gather_start(value)
    for stage in range(gather_stages()):
        held = gather_stage(held, stage)
    return held


def scatter_places(count):
    far = bits_of(count)[1:]
    table = {}
    row = {}
    for near in (1, 0):
        for sent in (True, False):
            for half, order in enumerate((far, far[::-1])):
                members = [0]
                for bit in order[:0:-1]:
                    members += [member | bit for member in members]
                for member in members:
                    index = member | near | (order[0] if sent else 0)
                    array = 0 if near else (1 + half if sent else 3)
                    table[index * 2 + half] = (array, row.get(array, 0))
                    row[array] = row.get(array, 0) + GROUP
    return tuple(table[k] for k in range(2 * count))


def scatter_shapes(count, columns):
    blocks = (count, count // 4, count // 4, count // 2)
    return [jax.ShapeDtypeStruct((part * GROUP, columns), bf16) for part in blocks]


def scatter_near(product, parts, sent):
    arriving = exchange(sent, "seq", 1)
    first, second, kept = parts
    rows = first.shape[0]

    def summed(part, row):
        return (product(part) + arriving[row : row + part.shape[0]].astype(f32)).astype(bf16)

    sends = (summed(first, 0), summed(second, rows))
    sends, kept = together(sends, kept)
    kept = summed(kept, 2 * rows)
    middle = kept.shape[0] // 2
    return sends, ([kept[:middle]], [kept[middle:]])


def scatter_far(sends, held, stage):
    last = len(bits_of(lax.axis_size("seq"))) - 2
    ready, kept = [], []
    for send, addends, order in zip(sends, held, far_orders()):
        addends = [*addends, exchange(send, "seq", order[stage])]
        if stage < last:
            middle = send.shape[0] // 2
            ready.append(sum(value[middle:].astype(f32) for value in addends).astype(bf16))
            addends = [value[:middle] for value in addends]
        kept.append(addends)
    return tuple(ready), tuple(kept)


def scatter_end(held):
    return jnp.concatenate([sum(v.astype(f32) for v in addends) for addends in held], axis=0)


def sum_seq(value):
    for bit in bits_of(lax.axis_size("seq")):
        value = value + exchange(value, "seq", bit)
    return value


def plane_pairs(ahead):
    planes, count = lax.axis_size("batch"), lax.axis_size("seq")
    per = count // planes
    pairs = []
    for owner in range(planes):
        for piece in range(planes):
            for k in range(per):
                holder = owner * count + piece * per + k
                user = (piece + ahead) % planes * count + owner * per + k
                pairs.append((holder, user))
    return pairs


def rows_from_owner(out_weight, width):
    per = lax.axis_size("seq") // lax.axis_size("batch")
    plane, mine = lax.axis_index("batch"), lax.axis_index("seq")
    rows = lax.dynamic_slice_in_dim(out_weight, mine % per * width, width, 0)
    return lax.psum(jnp.where(plane == mine // per, rows, jnp.zeros_like(rows)), "batch")


def to_owner(summed):
    return lax.ppermute(
        summed, ("batch", "seq"), [(user, holder) for holder, user in plane_pairs(0)]
    )


def double(held, turn):
    bits = bits_of(lax.axis_size("seq"))
    return jnp.concatenate([held, exchange(held, "seq", (bits[1:] + [1])[turn])], axis=0)


def step_values(raw):
    small = jnp.exp(-jnp.abs(raw))
    step = jnp.maximum(raw, 0.0) + jnp.log1p(small)
    sig = jnp.where(raw >= 0, 1.0, small) / (1.0 + small)
    tiny = raw < -20.0
    log_step = jnp.where(tiny, raw, jnp.log(step))
    ratio = jnp.where(tiny, 1.0, sig / step)
    return step, sig, log_step, ratio


def dot(a, b):
    return jnp.dot(a, b, preferred_element_type=f32)


def dot_nt(a, b):
    return lax.dot_general(a, b, (((1,), (1,)), ((), ())), preferred_element_type=f32)


def dot_tn(a, b):
    return lax.dot_general(a, b, (((0,), (0,)), ((), ())), preferred_element_type=f32)


def sigmoid(value):
    return 0.5 * jnp.tanh(0.5 * value) + 0.5


def silu_slope(value):
    sig = sigmoid(value)
    active = value * sig
    return active, sig + active * (1.0 - sig)


def split_parts(value, count):
    parts = []
    for _ in range(count):
        part = value.astype(bf16)
        parts.append(part)
        value = value - part.astype(f32)
    return parts


def sum_along(rows, order):
    parts = jnp.concatenate([part.astype(f32) for part in split_parts(rows, 3)], axis=0)
    total = dot(parts.astype(bf16), order)
    return total[:8] + total[8:16] + total[16:24]


def to_columns(rows):
    stacked = jnp.concatenate(rows, axis=0)
    missing = LANES - stacked.shape[0]
    return jnp.concatenate([stacked, jnp.zeros((missing, GROUP), f32)], axis=0).T


def spread_heads(value, first, heads, size):
    rows = value.shape[0]
    return jnp.concatenate(
        [jnp.broadcast_to(value[:, first + h : first + h + 1], (rows, size)) for h in range(heads)],
        axis=1,
    )


def head_ones(width, size):
    row = lax.broadcasted_iota(jnp.int32, (8, width), 0)
    column = lax.broadcasted_iota(jnp.int32, (8, width), 1)
    return (column // size == row).astype(f32).astype(bf16)


def sum_lanes(value):
    return dot_nt(jnp.ones((8, value.shape[1]), bf16), value.astype(bf16))


def ones_where(condition):
    return jnp.where(condition, 1.0, 0.0).astype(bf16)


def order_indices(length):
    row = lax.broadcasted_iota(jnp.int32, (length, length), 0)
    column = lax.broadcasted_iota(jnp.int32, (length, length), 1)
    return row, column


def fetch(arrays, table, which, target, semaphore):
    for index, (array, row, rows) in enumerate(table):

        @pl.when(which == index)
        def _():
            pltpu.make_async_copy(arrays[array].at[pl.ds(row, rows)], target, semaphore).start()


def fetched(arrays, table, buffer, semaphores, order):
    step = pl.program_id(0)
    slot, other = lax.rem(step, 2), lax.rem(step + 1, 2)

    @pl.when(step == 0)
    def _():
        fetch(arrays, table, order(0), buffer.at[0], semaphores.at[0])

    @pl.when(step + 1 < pl.num_programs(0))
    def _():
        fetch(arrays, table, order(step + 1), buffer.at[other], semaphores.at[other])

    source = arrays[0].at[pl.ds(0, table[0][2])]
    pltpu.make_async_copy(source, buffer.at[slot], semaphores.at[slot]).wait()
    return buffer[slot]


def store(source, targets, table, which, semaphore):
    for index, (array, row) in enumerate(table):

        @pl.when(which == index)
        def _():
            target = targets[array].at[pl.ds(row, GROUP)]
            pltpu.make_async_copy(source, target, semaphore).start()


def stored(buffer, targets, semaphores, slot):
    target = targets[0].at[pl.ds(0, GROUP)]
    pltpu.make_async_copy(buffer.at[slot], target, semaphores.at[slot]).wait()


def in_time(place, block):
    return ((block // 2) ^ place) * 2 + block % 2


def forward_kernel(dims, table, given, place_ref, *refs):
    heads, size, states, count = dims
    width = heads * size
    conv_cols = width + 2 * states
    arrays, refs = refs[:given], refs[given:]
    w_ref, conv_w_ref, conv_b_ref, step_ref, rows_ref = refs[:5]
    conv_in_ref, active_ref, slope_ref, gate_act_ref, gate_slope_ref = refs[5:10]
    raw_ref, ssd_ref, start_ref, scaled_ref, square_ref, normed_ref = refs[10:16]
    targets = refs[16:20]
    state, padded, order, barred, buffer, semaphores, placed, out_semaphores = refs[20:]
    turn = pl.program_id(0)
    slot = lax.rem(turn, 2)

    @pl.when(turn == 0)
    def _():
        state[...] = jnp.zeros_like(state)
        padded[0:HALO] = jnp.zeros_like(padded[0:HALO])
        row, column = order_indices(GROUP)
        order[...] = ones_where(row <= column)
        row, column = order_indices(HALF)
        barred[...] = jnp.where(row >= column, 0.0, -1e30)

    @pl.when(turn >= 2)
    def _():
        stored(placed, targets, out_semaphores, slot)

    normed = fetched(
        arrays, table, buffer, semaphores, lambda step: in_time(place_ref[0], step)
    )
    normed_ref[...] = normed
    projected = dot(normed, w_ref[...])
    conv_in = projected[:, width : width + conv_cols].astype(bf16)
    conv_in_ref[...] = conv_in
    padded[HALO : HALO + GROUP] = conv_in.astype(f32)
    conv_w = conv_w_ref[...]
    taps = conv_w.shape[0]
    pre = conv_b_ref[...]
    for k in range(taps):
        top = HALO - (taps - 1) + k
        pre = pre + conv_w[k : k + 1] * padded[top : top + GROUP]
    padded[0:HALO] = padded[GROUP : GROUP + HALO]
    active, slope = silu_slope(pre)
    active = active.astype(bf16)
    active_ref[...] = active
    slope_ref[...] = slope.astype(bf16)
    signal = active[:, :width]
    entry = active[:, width : width + states]
    readout = active[:, width + states :]
    signal_wide = signal.astype(f32)

    raw = projected[:, width + conv_cols :].T[:8]
    raw_ref[0] = raw
    step, _, log_step, _ = step_values(raw + step_ref[0:8, 0:1])
    running = sum_along(step * step_ref[8:16, 0:1], order[...])
    later = running - log_step
    total = running[:, GROUP - 1 :]
    columns = to_columns([running * LOG2E, jnp.exp(running), jnp.exp(total - later)])
    later = later * LOG2E
    early_wide = spread_heads(columns, 8, heads, size)
    tail_wide = spread_heads(columns, 16, heads, size)
    first, second = slice(0, HALF), slice(HALF, GROUP)
    scores = dot_nt(readout[first], entry[first])
    later_scores = dot_nt(readout[second], entry)
    within = []
    for h in range(heads):
        part = signal[:, h * size : (h + 1) * size]
        begin, end = columns[first, h : h + 1], columns[second, h : h + 1]
        row_first, row_second = later[h : h + 1, first], later[h : h + 1, second]
        near = jnp.exp2(begin - row_first + barred[...]) * scores
        full = jnp.exp2(end - row_first) * later_scores[:, first]
        last = jnp.exp2(end - row_second + barred[...]) * later_scores[:, second]
        both = jnp.concatenate([full.astype(bf16), last.astype(bf16)], axis=1)
        within.append(
            jnp.concatenate([dot(near.astype(bf16), part[first]), dot(both, part)], axis=0)
        )
    start = state[...]
    start_low = start.astype(bf16)
    start_ref[0] = start_low
    carried = dot(readout, start_low) * early_wide
    ssd = jnp.concatenate(within, axis=1) + carried + rows_ref[0:1] * signal_wide
    tail = (signal_wide * tail_wide).astype(bf16)
    state[...] = start * early_wide[GROUP - 1 :] + dot_tn(entry, tail)

    gate_act, gate_slope = silu_slope(projected[:, :width])
    gate_act_ref[...] = gate_act.astype(bf16)
    gate_slope_ref[...] = gate_slope.astype(bf16)
    ssd_ref[...] = ssd
    gated = ssd * gate_act
    scaled = (gated * rows_ref[1:2]).astype(bf16)
    scaled_ref[...] = scaled
    square_ref[0] = sum_lanes(gated * gated)
    placed[slot] = scaled
    where = in_time(place_ref[0], turn)
    store(placed.at[slot], targets, scatter_places(count), where, out_semaphores.at[slot])

    @pl.when(turn == pl.num_programs(0) - 1)
    def _():
        for other in range(2):
            stored(placed, targets, out_semaphores, other)


def time_estimate(microseconds, accessed):
    return pl.CostEstimate(
        flops=int(microseconds * 1.1e9), bytes_accessed=int(accessed), transcendentals=0
    )


def fixed(shape):
    return pl.BlockSpec(shape, lambda turn, place: (0,) * len(shape), pipeline_mode=pl.Buffered(1))


def anywhere(values):
    return [pl.BlockSpec(memory_space=pltpu.HBM)] * len(values)


def run_forward(place, pieces, params, dims):
    heads, size, states, count = dims
    arrays, table = pieces
    dim = params[0].shape[0]
    width, conv_cols = heads * size, params[1].shape[1]
    blocks = len(table)
    tokens = blocks * GROUP

    def moving(columns):
        return pl.BlockSpec((GROUP, columns), lambda turn, place: (turn, 0))

    def rows_of_block(height, columns):
        return pl.BlockSpec((1, height, columns), lambda turn, place: (turn, 0, 0))

    results = pl.pallas_call(
        functools.partial(forward_kernel, dims, table, len(arrays)),
        grid_spec=pltpu.PrefetchScalarGridSpec(
            num_scalar_prefetch=1,
            grid=(blocks,),
            in_specs=[*anywhere(arrays), *[fixed(param.shape) for param in params]],
            out_specs=[
                moving(conv_cols),
                moving(conv_cols),
                moving(conv_cols),
                moving(width),
                moving(width),
                rows_of_block(8, GROUP),
                moving(width),
                rows_of_block(states, width),
                moving(width),
                rows_of_block(8, GROUP),
                moving(dim),
                *anywhere(range(4)),
            ],
            scratch_shapes=[
                pltpu.VMEM((states, width), f32),
                pltpu.VMEM((HALO + GROUP, conv_cols), f32),
                pltpu.VMEM((GROUP, GROUP), bf16),
                pltpu.VMEM((HALF, HALF), f32),
                pltpu.VMEM((2, GROUP, dim), bf16),
                pltpu.SemaphoreType.DMA((2,)),
                pltpu.VMEM((2, GROUP, width), bf16),
                pltpu.SemaphoreType.DMA((2,)),
            ],
        ),
        out_shape=[
            jax.ShapeDtypeStruct((tokens, conv_cols), bf16),
            jax.ShapeDtypeStruct((tokens, conv_cols), bf16),
            jax.ShapeDtypeStruct((tokens, conv_cols), bf16),
            jax.ShapeDtypeStruct((tokens, width), bf16),
            jax.ShapeDtypeStruct((tokens, width), bf16),
            jax.ShapeDtypeStruct((blocks, 8, GROUP), f32),
            jax.ShapeDtypeStruct((tokens, width), f32),
            jax.ShapeDtypeStruct((blocks, states, width), bf16),
            jax.ShapeDtypeStruct((tokens, width), bf16),
            jax.ShapeDtypeStruct((blocks, 8, GROUP), f32),
            jax.ShapeDtypeStruct((tokens, dim), bf16),
            *scatter_shapes(count, width),
        ],
        compiler_params=pltpu.CompilerParams(vmem_limit_bytes=60 * MIB),
        cost_estimate=time_estimate(blocks * 3.0, tokens * (4 * dim + 24 * width)),
        name="forward_blocks",
    )(place, *arrays, *params)
    return results[:11], results[11:]


def out_grad_kernel(table, given, place_ref, *refs):
    arrays, refs = refs[:given], refs[given:]
    scaled_ref, out_rows_ref, out_grad_ref, slope_ref, cot_ref, buffer, semaphores = refs
    cot = fetched(arrays, table, buffer, semaphores, lambda step: in_time(place_ref[0], step))
    cot_ref[...] = cot
    out_grad = dot_nt(cot, out_rows_ref[...])
    out_grad_ref[...] = out_grad
    slope_ref[0] = sum_lanes(out_grad * scaled_ref[...].astype(f32))


def run_out_grad(place, cots, scaled, out_rows):
    arrays, table = cots
    width, dim = out_rows.shape
    blocks = len(table)
    tokens = blocks * GROUP
    return pl.pallas_call(
        functools.partial(out_grad_kernel, table, len(arrays)),
        grid_spec=pltpu.PrefetchScalarGridSpec(
            num_scalar_prefetch=1,
            grid=(blocks,),
            in_specs=[
                *anywhere(arrays),
                pl.BlockSpec((GROUP, width), lambda turn, place: (turn, 0)),
                fixed(out_rows.shape),
            ],
            out_specs=[
                pl.BlockSpec((GROUP, width), lambda turn, place: (turn, 0)),
                pl.BlockSpec((1, 8, GROUP), lambda turn, place: (turn, 0, 0)),
                pl.BlockSpec((GROUP, dim), lambda turn, place: (turn, 0)),
            ],
            scratch_shapes=[pltpu.VMEM((2, GROUP, dim), bf16), pltpu.SemaphoreType.DMA((2,))],
        ),
        out_shape=[
            jax.ShapeDtypeStruct((tokens, width), f32),
            jax.ShapeDtypeStruct((blocks, 8, GROUP), f32),
            jax.ShapeDtypeStruct((tokens, dim), bf16),
        ],
        compiler_params=pltpu.CompilerParams(vmem_limit_bytes=60 * MIB),
        cost_estimate=time_estimate(12, tokens * (4 * dim + 6 * width)),
        name="out_grad",
    )(place, *arrays, scaled, out_rows)


def backward_kernel(dims, place_ref, *refs):
    heads, size, states, count = dims
    width = heads * size
    conv_cols = width + 2 * states
    conv_in_ref, active_ref, slope_ref, gate_act_ref, gate_slope_ref = refs[:5]
    raw_ref, ssd_ref, start_ref, out_grad_ref, norm_ref = refs[5:10]
    conv_w_ref, step_ref, rows_ref = refs[10:13]
    out_ref, targets = refs[13], refs[14:18]
    sums = refs[18:24]
    gain_ref, skip_ref, conv_wg_ref, conv_bg_ref, bias_ref, rate_ref = sums
    state, pre_grads, order, back_order, barred, placed, semaphores = refs[24:]
    taps = conv_w_ref.shape[0]
    turn = pl.program_id(0)
    slot = lax.rem(turn, 2)

    @pl.when(turn >= 2)
    def _():
        stored(placed, targets, semaphores, slot)

    @pl.when(pl.program_id(0) == 0)
    def _():
        state[...] = jnp.zeros_like(state)
        pre_grads[0:HALO] = jnp.zeros_like(pre_grads[0:HALO])
        for total in sums:
            total[...] = jnp.zeros_like(total)
        row, column = order_indices(GROUP)
        order[...] = ones_where(row <= column)
        back_order[...] = ones_where(row >= column)
        row, column = order_indices(HALF)
        barred[...] = jnp.where(row <= column, 0.0, -1e30)

    gate_act, ssd, out_grad = gate_act_ref[...].astype(f32), ssd_ref[...], out_grad_ref[...]
    norms = norm_ref[0].T
    scale, slope = norms[:, 0:1], norms[:, 1:2]
    gated = ssd * gate_act
    gain_ref[...] += jnp.sum(out_grad * (gated * scale), axis=0, keepdims=True)
    gated_grad = out_grad * (rows_ref[1:2] * scale) - gated * slope
    grad_low = (gated_grad * gate_act).astype(bf16)
    gate_grad = (gated_grad * ssd * gate_slope_ref[...].astype(f32)).astype(bf16)
    out_ref[:, :width] = gate_grad
    placed[slot, :, :width] = gate_grad
    ssd_grad = grad_low.astype(f32)

    raw = raw_ref[0] + step_ref[0:8, 0:1]
    rate = step_ref[8:16, 0:1]
    step, sig, log_step, ratio = step_values(raw)
    decay = step * rate
    running = sum_along(decay, order[...])
    later = running - log_step
    total = running[:, GROUP - 1 :]
    columns = to_columns([later * LOG2E, jnp.exp(running), jnp.exp(total - later)])
    running = running * LOG2E
    early_wide = spread_heads(columns, 8, heads, size)
    tail_wide = spread_heads(columns, 16, heads, size)

    signal = active_ref[:, :width]
    entry = active_ref[:, width : width + states]
    readout = active_ref[:, width + states :]
    signal_wide = signal.astype(f32)
    start_low = start_ref[0]
    end_grad = state[...]
    end_low = end_grad.astype(bf16)
    first, second = slice(0, HALF), slice(HALF, GROUP)
    scores = dot_nt(entry[first], readout)
    later_scores = dot_nt(entry[second], readout[second])
    near_grad, far_grad, last_grad = 0.0, 0.0, 0.0
    within = []
    for h in range(heads):
        part, grad = signal[:, h * size : (h + 1) * size], grad_low[:, h * size : (h + 1) * size]
        begin, end = columns[first, h : h + 1], columns[second, h : h + 1]
        row_first, row_second = running[h : h + 1, first], running[h : h + 1, second]
        near = jnp.exp2(row_first - begin + barred[...])
        full = jnp.exp2(row_second - begin)
        last = jnp.exp2(row_second - end + barred[...])
        both = jnp.concatenate(
            [
                (near * scores[:, first]).astype(bf16),
                (full * scores[:, second]).astype(bf16),
            ],
            axis=1,
        )
        final = (last * later_scores).astype(bf16)
        within.append(jnp.concatenate([dot(both, grad), dot(final, grad[second])], axis=0))
        cross = dot_nt(part[first], grad)
        near_grad = near_grad + cross[:, first] * near
        far_grad = far_grad + cross[:, second] * full
        last_grad = last_grad + dot_nt(part[second], grad[second]) * last
    tail_grad = tail_wide * dot(entry, end_low)
    signal_grad = jnp.concatenate(within, axis=1) + tail_grad
    score_first = jnp.concatenate([near_grad, far_grad], axis=1).astype(bf16)
    score_second = last_grad.astype(bf16)
    tail = (signal_wide * tail_wide).astype(bf16)
    head_grad = (ssd_grad * early_wide).astype(bf16)
    entry_grad = jnp.concatenate(
        [dot(score_first, readout), dot(score_second, readout[second])], axis=0
    ) + dot_nt(tail, end_low)
    readout_grad = dot_tn(score_first, entry[first]) + dot_nt(head_grad, start_low)
    readout_last = readout_grad[second] + dot_tn(score_second, entry[second])
    total_wide = early_wide[GROUP - 1 :]
    state[...] = end_grad * total_wide + dot_tn(readout, head_grad)

    skip = rows_ref[0:1]
    ones = head_ones(width, size)
    column_part = signal_wide * signal_grad
    row_part = ssd_grad * (ssd - skip * signal_wide)
    end_part = jnp.sum(signal_wide * tail_grad, axis=0, keepdims=True) + total_wide * jnp.sum(
        start_low.astype(f32) * end_grad, axis=0, keepdims=True
    )

    def head_sums(value, parts):
        return sum(dot_nt(ones, part) for part in split_parts(value, parts))

    end_rows = head_sums(jnp.broadcast_to(end_part, (8, width)), 2)[:, 0:1]
    decay_grad = sum_along(head_sums(row_part - column_part, 2), back_order[...]) + end_rows
    raw_grad = head_sums(column_part, 1) * ratio + decay_grad * rate * sig
    skip_ref[...] += jnp.sum(ssd_grad * signal_wide, axis=0, keepdims=True)
    bias_ref[...] += raw_grad
    rate_ref[...] += decay_grad * decay
    raw_low = to_columns([raw_grad]).astype(bf16)
    out_ref[:, width + conv_cols :] = raw_low
    placed[slot, :, width + conv_cols :] = raw_low

    pre_grads[GROUP : GROUP + HALO] = pre_grads[0:HALO]
    pre_grads[0:GROUP, :width] = (signal_grad + skip * ssd_grad) * slope_ref[:, :width].astype(f32)
    sides = slope_ref[:, width:].astype(f32)
    pre_grads[0:GROUP, width : width + states] = entry_grad * sides[:, :states]
    pre_grads[0:HALF, width + states :] = readout_grad[first] * sides[first, states:]
    pre_grads[HALF:GROUP, width + states :] = readout_last * sides[second, states:]
    conv_w = conv_w_ref[...]
    conv_in = conv_in_ref[...].astype(f32)
    conv_grad = 0.0
    for k in range(taps):
        ahead = taps - 1 - k
        shifted = pre_grads[ahead : ahead + GROUP]
        conv_grad = conv_grad + conv_w[k : k + 1] * shifted
        conv_wg_ref[k : k + 1] += jnp.sum(shifted * conv_in, axis=0, keepdims=True)
        if ahead == 0:
            conv_bg_ref[...] += jnp.sum(shifted, axis=0, keepdims=True)
    conv_low = conv_grad.astype(bf16)
    out_ref[:, width : width + conv_cols] = conv_low
    placed[slot, :, width : width + conv_cols] = conv_low

    where = in_time(place_ref[0], pl.num_programs(0) - 1 - turn)
    store(placed.at[slot], targets, scatter_places(count), where, semaphores.at[slot])

    @pl.when(turn == pl.num_programs(0) - 1)
    def _():
        for other in range(2):
            stored(placed, targets, semaphores, other)


def run_backward(place, values, params, dims):
    heads, size, states, count = dims
    conv_cols, width = values[0].shape[1], heads * size
    tokens = values[0].shape[0]
    blocks = tokens // GROUP
    last = blocks - 1
    out_cols = width + conv_cols + LANES

    def moving(columns):
        return pl.BlockSpec((GROUP, columns), lambda turn, place: (last - turn, 0))

    def rows_of_block():
        return pl.BlockSpec((1, 8, GROUP), lambda turn, place: (last - turn, 0, 0))

    sums = [(1, width), (1, width), params[0].shape, (1, conv_cols), (8, GROUP), (8, GROUP)]
    return pl.pallas_call(
        functools.partial(backward_kernel, dims),
        grid_spec=pltpu.PrefetchScalarGridSpec(
            num_scalar_prefetch=1,
            grid=(blocks,),
            in_specs=[
                moving(conv_cols),
                moving(conv_cols),
                moving(conv_cols),
                moving(width),
                moving(width),
                rows_of_block(),
                moving(width),
                pl.BlockSpec((1, states, width), lambda turn, place: (last - turn, 0, 0)),
                moving(width),
                rows_of_block(),
                *[fixed(param.shape) for param in params],
            ],
            out_specs=[
                moving(out_cols),
                *anywhere(range(4)),
                *[fixed(shape) for shape in sums],
            ],
            scratch_shapes=[
                pltpu.VMEM((states, width), f32),
                pltpu.VMEM((GROUP + HALO, conv_cols), f32),
                pltpu.VMEM((GROUP, GROUP), bf16),
                pltpu.VMEM((GROUP, GROUP), bf16),
                pltpu.VMEM((HALF, HALF), f32),
                pltpu.VMEM((2, GROUP, out_cols), bf16),
                pltpu.SemaphoreType.DMA((2,)),
            ],
        ),
        out_shape=[
            jax.ShapeDtypeStruct((tokens, out_cols), bf16),
            *scatter_shapes(count, out_cols),
        ]
        + [jax.ShapeDtypeStruct(shape, f32) for shape in sums],
        compiler_params=pltpu.CompilerParams(vmem_limit_bytes=60 * MIB),
        cost_estimate=time_estimate(blocks * 3.5, tokens * 40 * width),
        name="backward_blocks",
    )(place, *values, *params)


def widen_kernel(place_ref, piece_ref, out_ref):
    out_ref[...] = piece_ref[0].astype(f32)


def assemble_out(place, pieces, per):
    count, size, dim = pieces.shape
    groups = count // per

    def source(turn, place):
        relative = (turn % groups * per + turn // groups) ^ place[0]
        return ((relative & 1) * (count // 2) + (relative >> 1), 0, 0)

    return pl.pallas_call(
        widen_kernel,
        grid_spec=pltpu.PrefetchScalarGridSpec(
            num_scalar_prefetch=1,
            grid=(count,),
            in_specs=[pl.BlockSpec((1, size, dim), source)],
            out_specs=pl.BlockSpec((size, dim), lambda turn, place: (turn, 0)),
        ),
        out_shape=jax.ShapeDtypeStruct((count * size, dim), f32),
        cost_estimate=time_estimate(5, count * size * dim * 6),
        name="assemble_out_weight_grad",
    )(place, pieces)


def assemble_kernel(dims, table, place_ref, *refs):
    heads, size, states, count = dims
    width, shared = heads * size, 2 * states
    inner = count * width
    arrays, out_ref, sums = refs[:-2], refs[-2], refs[-1]
    for relative in range(count):
        device = place_ref[0] ^ relative
        parts = []
        for half in range(2):
            array, row, height = table[half, relative]
            parts.append(arrays[array][row : row + height].astype(f32))
        columns = jnp.concatenate(parts, axis=0).T
        out_ref[pl.ds(pl.multiple_of(device * width, 8), width)] = columns[:width]
        middle = pl.multiple_of(inner + device * width, 8)
        out_ref[pl.ds(middle, width)] = columns[width : 2 * width]
        sums[device] = columns[2 * width : 2 * width + shared + STEP_ROWS]
    total = sums[0, :shared]
    for device in range(1, count):
        total = total + sums[device, :shared]
    out_ref[2 * inner : 2 * inner + shared] = total
    for device in range(count):
        last = 2 * inner + shared + device * heads
        out_ref[last : last + heads] = sums[device, shared : shared + heads]


def assemble(place, held, dims):
    heads, size, states, count = dims
    arrays, table = gathered(held)
    rows = sum(table[half, 0][2] for half in range(2))
    out_rows = 2 * count * heads * size + 2 * states + count * heads

    def whole(value):
        return pl.BlockSpec(
            value.shape,
            lambda turn, place: (0,) * len(value.shape),
            pipeline_mode=pl.Buffered(1),
        )

    return pl.pallas_call(
        functools.partial(assemble_kernel, dims, table),
        grid_spec=pltpu.PrefetchScalarGridSpec(
            num_scalar_prefetch=1,
            grid=(1,),
            in_specs=[whole(value) for value in arrays],
            out_specs=pl.BlockSpec(
                (out_rows, rows), lambda turn, place: (0, 0), pipeline_mode=pl.Buffered(1)
            ),
            scratch_shapes=[pltpu.VMEM((count, 2 * states + STEP_ROWS, rows), f32)],
        ),
        out_shape=jax.ShapeDtypeStruct((out_rows, rows), f32),
        compiler_params=pltpu.CompilerParams(vmem_limit_bytes=60 * MIB),
        cost_estimate=time_estimate(8, out_rows * rows * 6),
        name="assemble_in_weight_grad",
    )(place, *arrays)


def body(
    tokens,
    norm_gain,
    in_weight,
    conv_weight,
    conv_bias,
    dt_bias,
    decay_log,
    skip_scale,
    gate_gain,
    out_weight,
    cotangent,
):
    count, mine = lax.axis_size("seq"), lax.axis_index("seq")
    place = mine.astype(jnp.int32).reshape(1)
    inner, all_heads, conv_all = gate_gain.shape[0], dt_bias.shape[0], conv_bias.shape[0]
    size, states = inner // all_heads, (conv_all - inner) // 2
    heads, width = all_heads // count, inner // count
    dims = (heads, size, states, count)
    shared = 2 * states
    conv_cols = width + shared
    tok_rows = tokens.shape[1]
    per_plane = out_weight.shape[0] // width

    def own(vector, per, first=0):
        return lax.dynamic_slice_in_dim(vector, first + mine * per, per, vector.ndim - 1)

    def own_conv(array, first=0):
        return jnp.concatenate(
            [own(array, width, first), array[..., first + inner : first + conv_all]], axis=-1
        )

    tokens_row = tokens[0].astype(f32)
    inverse = lax.rsqrt(jnp.mean(tokens_row * tokens_row, axis=-1, keepdims=True) + epsilon)
    normed_own = (tokens_row * inverse * norm_gain).astype(bf16)
    step_own = own(in_weight, heads, inner + conv_all)
    w_own = jnp.concatenate(
        [
            own(in_weight, width),
            own_conv(in_weight, inner),
            jnp.pad(step_own, ((0, 0), (0, LANES - heads))),
        ],
        axis=1,
    )
    w_cols = lax.all_gather(w_own, "batch", axis=0, tiled=True)
    stages = gather_stages()
    held = gather_stage(gather_stage(gather_start(normed_own), 0), 1)
    held, cots = together(held, gather_start(cotangent[0]))
    cots = gather_stage(cots, 0)
    for stage in range(2, stages):
        held = gather_stage(held, stage)
    w_cols, held, cots, out_owned = together(w_cols, held, cots, out_weight)
    cots = gather_stage(cots, 1)
    out_rows = rows_from_owner(out_owned, width)

    conv_w, conv_b = own_conv(conv_weight), own_conv(conv_bias)[None]
    per_head = jnp.stack([own(dt_bias, heads), -jnp.exp(own(decay_log, heads))])
    per_head = jnp.pad(per_head, ((0, 0), (0, 8 - heads))).reshape(16, 1)
    step_rows = jnp.broadcast_to(per_head, (16, LANES))
    gain_own = own(gate_gain, width)[None]
    rows = jnp.concatenate(
        [jnp.repeat(own(skip_scale, heads), size)[None], gain_own, jnp.zeros((6, width), f32)],
        axis=0,
    )
    results, out_parts = run_forward(
        place, token_pieces(held), (w_cols, conv_w, conv_b, step_rows, rows), dims
    )
    conv_in, active, slope, gate_act, gate_slope, raw, ssd, starts, scaled, squares, normed = results
    out_parts, cots, out_rows = together(out_parts, cots, out_rows)
    for stage in range(2, stages):
        cots = gather_stage(cots, stage)

    def out_product(part):
        return dot(part, out_rows)

    out_send = out_product(out_parts[0]).astype(bf16)
    out_send, cots = together(out_send, cots)
    out_grad, slopes, cot = run_out_grad(place, token_pieces(cots), scaled, out_rows)
    sums = sum_seq(jnp.stack([squares[:, 0].reshape(-1), slopes[:, 0].reshape(-1)]))
    out_ready, out_held = scatter_near(out_product, out_parts[1:], out_send)
    scale = lax.rsqrt(sums[0] / inner + epsilon)
    norms = jnp.stack([scale, scale * scale * scale * sums[1] / inner])
    norms = jnp.pad(norms, ((0, 6), (0, 0))).reshape(8, -1, GROUP).swapaxes(0, 1)
    scaled_cot = (cot.astype(f32) * scale[:, None]).astype(bf16)
    out_term = jnp.einsum("te,td->ed", scaled, scaled_cot, preferred_element_type=f32)
    out_term, norms, out_ready = together(out_term.astype(bf16), norms, out_ready)
    out_sum = lax.psum_scatter(out_term, "batch", scatter_dimension=0, tiled=True)
    out_ready, out_held = scatter_far(out_ready, out_held, 0)

    values = (conv_in, active, slope, gate_act, gate_slope, raw, ssd, starts, out_grad, norms)
    results = run_backward(place, values, (conv_w, step_rows, rows), dims)
    proj_grad, back_parts = results[0], results[1:5]
    gain_term, skip_term, conv_w_term, conv_b_term, bias_term, rate_term = results[5:]
    proj_grad, back_parts, out_ready, out_held, out_sum = together(
        proj_grad, back_parts, out_ready, out_held, out_sum
    )

    for stage in range(1, stages - 1):
        out_ready, out_held = scatter_far(out_ready, out_held, stage)
    out_pieces = to_owner(out_sum)[None]
    in_term = jnp.einsum("td,tf->df", normed, proj_grad, preferred_element_type=f32).astype(bf16)
    in_term, back_parts, out_held, out_pieces = together(in_term, back_parts, out_held, out_pieces)
    in_sum = lax.psum_scatter(in_term, "batch", scatter_dimension=0, tiled=True)

    def back_product(part):
        return jnp.einsum("tf,df->td", part, w_cols, preferred_element_type=f32)

    out_pieces = double(out_pieces, 0)
    back_send = back_product(back_parts[0]).astype(bf16)
    back_send, keeps, out_pieces, in_term = together(
        back_send, back_parts[1:], out_pieces, in_term
    )
    back_ready, back_held = scatter_near(back_product, keeps, back_send)

    norm_gain_term = jnp.sum(in_term.astype(f32) * w_cols.astype(f32), axis=1) / norm_gain

    def among_heads(vector, per, total):
        return lax.dynamic_update_slice_in_dim(jnp.zeros((total,), f32), vector, mine * per, 0)

    def among_conv(array):
        wide = jnp.zeros((array.shape[0], inner), f32)
        wide = lax.dynamic_update_slice_in_dim(wide, array[:, :width], mine * width, 1)
        return jnp.concatenate([wide, array[:, width:]], axis=1).reshape(-1)

    skip_heads = jnp.sum(skip_term.reshape(heads, size), axis=1)
    terms = [
        norm_gain_term,
        among_conv(conv_w_term),
        among_conv(conv_b_term),
        among_heads(jnp.sum(bias_term[:heads], axis=1), heads, all_heads),
        among_heads(jnp.sum(rate_term[:heads], axis=1), heads, all_heads),
        among_heads(skip_heads, heads, all_heads),
        among_heads(gain_term[0], width, inner),
    ]
    vector = jnp.concatenate(terms)
    padding = -vector.shape[0] % (8 * LANES)
    vector = jnp.pad(vector, (0, padding)).reshape(-1, LANES)

    axes = [(axis, bit) for axis in ("seq", "batch") for bit in bits_of(lax.axis_size(axis))]
    back_ready, out_pieces, vector = together(back_ready, out_pieces, vector)
    back_ready, back_held = scatter_far(back_ready, back_held, 0)
    out_pieces = double(out_pieces, 1)
    vector = vector + exchange(vector, *axes.pop(0))
    back_ready, back_held, out_pieces, vector, in_sum = together(
        back_ready, back_held, out_pieces, vector, in_sum
    )
    columns = gather_stage(gather_start(in_sum), 0)
    for stage in range(1, stages - 1):
        back_ready, back_held = scatter_far(back_ready, back_held, stage)
    for stage in range(2, stages):
        out_pieces = double(out_pieces, stage)
    vector = vector + exchange(vector, *axes.pop(0))
    back_held, columns, out_pieces, vector = together(back_held, columns, out_pieces, vector)
    for stage in range(1, stages):
        columns = gather_stage(columns, stage)
        vector = vector + exchange(vector, *axes.pop(0))
        columns, vector = together(columns, vector)
    normed_grad = scatter_end(back_held)
    cot_row = cotangent[0].astype(f32)
    gained = norm_gain * normed_grad
    slope = inverse * inverse * inverse * jnp.mean(gained * tokens_row, axis=-1, keepdims=True)
    input_grad = cot_row + inverse * gained - tokens_row * slope
    own_scale = lax.dynamic_slice_in_dim(scale, mine * tok_rows, tok_rows, 0)[:, None]
    block_out = (tokens_row + own_scale * scatter_end(out_held)).astype(bf16)
    out_weight_grad = assemble_out(place, out_pieces, per_plane)
    in_weight_grad = assemble(place, columns, dims).T
    while axes:
        vector = vector + exchange(vector, *axes.pop(0))
    vector = vector.reshape(-1)

    parts, offset = [], 0
    for term in terms:
        parts.append(vector[offset : offset + term.shape[0]])
        offset += term.shape[0]
    return (
        block_out[None],
        input_grad[None],
        parts[0],
        in_weight_grad,
        parts[1].reshape(conv_weight.shape),
        parts[2],
        parts[3],
        parts[4],
        parts[5],
        parts[6],
        out_weight_grad,
    )


def solution(mesh):
    placed = (
        P("batch", "seq", None),
        P(),
        P("batch", None),
        P(),
        P(),
        P(),
        P(),
        P(),
        P(),
        P("batch", None),
        P("batch", "seq", None),
    )
    return jax.shard_map(
        body,
        mesh=mesh,
        in_specs=placed,
        out_specs=(
            P("batch", "seq", None),
            P("batch", "seq", None),
            P(),
            P("batch", None),
            P(),
            P(),
            P(),
            P(),
            P(),
            P(),
            P("batch", None),
        ),
        check_vma=False,
    )
```

```python
import functools

import jax
import jax.numpy as jnp
from jax import lax
from jax.experimental import pallas as pl
from jax.experimental.pallas import tpu as pltpu
from jax.sharding import PartitionSpec as P

GROUP = 256
LANES = 128
HALF = GROUP // 2
HALO = 8
STEP_ROWS = 16
LOG2E = 1.4426950408889634
epsilon = 1e-05
f32 = jnp.float32
bf16 = jnp.bfloat16
MIB = 2**20


def exchange(value, axis, distance):
    count = lax.axis_size(axis)
    return lax.ppermute(value, axis, [(source, source ^ distance) for source in range(count)])


def bits_of(count):
    return [1 << k for k in range(count.bit_length() - 1)]


def placed_order(count):
    return [2 * k for k in range(count // 2)] + [2 * k + 1 for k in range(count // 2)]


def together(*values):
    return lax.optimization_barrier(values)


def far_orders():
    far = bits_of(lax.axis_size("seq"))[1:]
    return far, far[::-1]


def gather_start(value):
    half = value.shape[0] // 32 * 16
    return tuple({"base": part, "fresh": None, "near": []} for part in (value[:half], value[half:]))


def gather_stage(held, stage, late=False):
    grown = []
    for half, order in zip(held, far_orders()):
        base, fresh, near = half["base"], half["fresh"], list(half["near"])
        if stage >= 1:
            merged = base if stage == len(order) else jnp.concatenate([base, fresh], axis=0)
            if not late:
                near.append(exchange(merged if stage == 1 else fresh, "seq", 1))
            elif stage == len(order):
                near = [exchange(base, "seq", 1), exchange(fresh, "seq", 1)]
            base = merged
        if stage < len(order):
            fresh = exchange(base, "seq", order[stage])
        grown.append({"base": base, "fresh": fresh, "near": near})
    return tuple(grown)


def gather_stages():
    return len(bits_of(lax.axis_size("seq")))


def gathered(held):
    arrays, table = [], {}
    for number, (half, order) in enumerate(zip(held, far_orders())):
        indices = [0]
        for bit in order:
            indices += [index | bit for index in indices]
        middle = len(indices) // 2
        groups = [(half["base"], indices[:middle]), (half["fresh"], indices[middle:])]
        bounds = [0] + [2 << k for k in range(len(order))]
        if len(half["near"]) < len(order):
            bounds = [0, middle, len(indices)]
        for value, first, last in zip(half["near"], bounds, bounds[1:]):
            groups.append((value, [index | 1 for index in indices[first:last]]))
        for value, members in groups:
            rows = value.shape[0] // len(members)
            for turn, index in enumerate(members):
                table[number, index] = (len(arrays), turn * rows, rows)
            arrays.append(value)
    return arrays, table


def token_pieces(held):
    arrays, table = gathered(held)
    indices = range(lax.axis_size("seq"))
    return arrays, tuple(table[half, index] for index in indices for half in range(2))


def gather_all(value):
    held = gather_start(value)
    for stage in range(gather_stages()):
        held = gather_stage(held, stage)
    return held


def scatter_places(count):
    far = bits_of(count)[1:]
    table = {}
    row = {}
    for near in (1, 0):
        for sent in (True, False):
            for half, order in enumerate((far, far[::-1])):
                members = [0]
                for bit in order[:0:-1]:
                    members += [member | bit for member in members]
                for member in members:
                    index = member | near | (order[0] if sent else 0)
                    array = 0 if near else (1 + half if sent else 3)
                    table[index * 2 + half] = (array, row.get(array, 0))
                    row[array] = row.get(array, 0) + GROUP
    return tuple(table[k] for k in range(2 * count))


def scatter_shapes(count, columns):
    blocks = (count, count // 4, count // 4, count // 2)
    return [jax.ShapeDtypeStruct((part * GROUP, columns), bf16) for part in blocks]


def scatter_near(product, parts, sent):
    arriving = exchange(sent, "seq", 1)
    first, second, kept = parts
    rows = first.shape[0]

    def summed(part, row):
        return (product(part) + arriving[row : row + part.shape[0]].astype(f32)).astype(bf16)

    sends = (summed(first, 0), summed(second, rows))
    sends, kept = together(sends, kept)
    kept = summed(kept, 2 * rows)
    middle = kept.shape[0] // 2
    return sends, ([kept[:middle]], [kept[middle:]])


def scatter_far(sends, held, stage):
    last = len(bits_of(lax.axis_size("seq"))) - 2
    ready, kept = [], []
    for send, addends, order in zip(sends, held, far_orders()):
        addends = [*addends, exchange(send, "seq", order[stage])]
        if stage < last:
            middle = send.shape[0] // 2
            ready.append(sum(value[middle:].astype(f32) for value in addends).astype(bf16))
            addends = [value[:middle] for value in addends]
        kept.append(addends)
    return tuple(ready), tuple(kept)


def scatter_end(held):
    return jnp.concatenate([sum(v.astype(f32) for v in addends) for addends in held], axis=0)


def sum_seq(value):
    for bit in bits_of(lax.axis_size("seq")):
        value = value + exchange(value, "seq", bit)
    return value


def plane_pairs(ahead):
    planes, count = lax.axis_size("batch"), lax.axis_size("seq")
    per = count // planes
    pairs = []
    for owner in range(planes):
        for piece in range(planes):
            for k in range(per):
                holder = owner * count + piece * per + k
                user = (piece + ahead) % planes * count + owner * per + k
                pairs.append((holder, user))
    return pairs


def rows_from_owner(out_weight, width):
    per = lax.axis_size("seq") // lax.axis_size("batch")
    plane, mine = lax.axis_index("batch"), lax.axis_index("seq")
    rows = lax.dynamic_slice_in_dim(out_weight, mine % per * width, width, 0)
    return lax.psum(jnp.where(plane == mine // per, rows, jnp.zeros_like(rows)), "batch")


def to_owner(summed):
    return lax.ppermute(
        summed, ("batch", "seq"), [(user, holder) for holder, user in plane_pairs(0)]
    )


def double(held, turn):
    bits = bits_of(lax.axis_size("seq"))
    return jnp.concatenate([held, exchange(held, "seq", (bits[1:] + [1])[turn])], axis=0)


def step_values(raw):
    small = jnp.exp(-jnp.abs(raw))
    step = jnp.maximum(raw, 0.0) + jnp.log1p(small)
    sig = jnp.where(raw >= 0, 1.0, small) / (1.0 + small)
    tiny = raw < -20.0
    log_step = jnp.where(tiny, raw, jnp.log(step))
    ratio = jnp.where(tiny, 1.0, sig / step)
    return step, sig, log_step, ratio


def dot(a, b):
    return jnp.dot(a, b, preferred_element_type=f32)


def dot_nt(a, b):
    return lax.dot_general(a, b, (((1,), (1,)), ((), ())), preferred_element_type=f32)


def dot_tn(a, b):
    return lax.dot_general(a, b, (((0,), (0,)), ((), ())), preferred_element_type=f32)


def sigmoid(value):
    return 0.5 * jnp.tanh(0.5 * value) + 0.5


def silu_slope(value):
    sig = sigmoid(value)
    active = value * sig
    return active, sig + active * (1.0 - sig)


def split_parts(value, count):
    parts = []
    for _ in range(count):
        part = value.astype(bf16)
        parts.append(part)
        value = value - part.astype(f32)
    return parts


def sum_along(rows, order):
    parts = jnp.concatenate([part.astype(f32) for part in split_parts(rows, 3)], axis=0)
    total = dot(parts.astype(bf16), order)
    return total[:8] + total[8:16] + total[16:24]


def to_columns(rows):
    stacked = jnp.concatenate(rows, axis=0)
    missing = LANES - stacked.shape[0]
    return jnp.concatenate([stacked, jnp.zeros((missing, GROUP), f32)], axis=0).T


def spread_heads(value, first, heads, size):
    rows = value.shape[0]
    return jnp.concatenate(
        [jnp.broadcast_to(value[:, first + h : first + h + 1], (rows, size)) for h in range(heads)],
        axis=1,
    )


def head_ones(width, size):
    row = lax.broadcasted_iota(jnp.int32, (8, width), 0)
    column = lax.broadcasted_iota(jnp.int32, (8, width), 1)
    return (column // size == row).astype(f32).astype(bf16)


def sum_lanes(value):
    return dot_nt(jnp.ones((8, value.shape[1]), bf16), value.astype(bf16))


def ones_where(condition):
    return jnp.where(condition, 1.0, 0.0).astype(bf16)


def order_indices(length):
    row = lax.broadcasted_iota(jnp.int32, (length, length), 0)
    column = lax.broadcasted_iota(jnp.int32, (length, length), 1)
    return row, column


def fetch(arrays, table, which, target, semaphore):
    for index, (array, row, rows) in enumerate(table):

        @pl.when(which == index)
        def _():
            pltpu.make_async_copy(arrays[array].at[pl.ds(row, rows)], target, semaphore).start()


def fetched(arrays, table, buffer, semaphores, order, blocks=1):
    step = pl.program_id(0)
    slot, other = lax.rem(step, 2), lax.rem(step + 1, 2)

    def start(step, slot):
        for k in range(blocks):
            target = buffer.at[slot, pl.ds(k * GROUP, GROUP)]
            fetch(arrays, table, order(step * blocks + k), target, semaphores.at[slot])

    @pl.when(step == 0)
    def _():
        start(0, 0)

    @pl.when(step + 1 < pl.num_programs(0))
    def _():
        start(step + 1, other)

    for k in range(blocks):
        source = arrays[0].at[pl.ds(0, GROUP)]
        target = buffer.at[slot, pl.ds(k * GROUP, GROUP)]
        pltpu.make_async_copy(source, target, semaphores.at[slot]).wait()
    return buffer[slot]


def store(source, targets, table, which, semaphore):
    for index, (array, row) in enumerate(table):

        @pl.when(which == index)
        def _():
            target = targets[array].at[pl.ds(row, GROUP)]
            pltpu.make_async_copy(source, target, semaphore).start()


def stored(buffer, targets, semaphores, slot):
    target = targets[0].at[pl.ds(0, GROUP)]
    pltpu.make_async_copy(buffer.at[slot], target, semaphores.at[slot]).wait()


def in_time(place, block):
    return ((block // 2) ^ place) * 2 + block % 2


def forward_kernel(dims, table, given, place_ref, *refs):
    heads, size, states, count = dims
    width = heads * size
    conv_cols = width + 2 * states
    arrays, refs = refs[:given], refs[given:]
    w_ref, conv_w_ref, conv_b_ref, step_ref, rows_ref = refs[:5]
    conv_in_ref, active_ref, slope_ref, gate_act_ref, gate_slope_ref = refs[5:10]
    raw_ref, ssd_ref, start_ref, scaled_ref, square_ref, normed_ref = refs[10:16]
    targets = refs[16:20]
    state, padded, order, barred, buffer, semaphores, placed, out_semaphores = refs[20:]
    turn = pl.program_id(0)
    slot = lax.rem(turn, 2)

    @pl.when(turn == 0)
    def _():
        state[...] = jnp.zeros_like(state)
        padded[0:HALO] = jnp.zeros_like(padded[0:HALO])
        row, column = order_indices(GROUP)
        order[...] = ones_where(row <= column)
        row, column = order_indices(HALF)
        barred[...] = jnp.where(row >= column, 0.0, -1e30)

    @pl.when(turn >= 2)
    def _():
        stored(placed, targets, out_semaphores, slot)

    normed = fetched(
        arrays, table, buffer, semaphores, lambda step: in_time(place_ref[0], step)
    )
    normed_ref[...] = normed
    projected = dot(normed, w_ref[...])
    conv_in = projected[:, width : width + conv_cols].astype(bf16)
    conv_in_ref[...] = conv_in
    padded[HALO : HALO + GROUP] = conv_in.astype(f32)
    conv_w = conv_w_ref[...]
    taps = conv_w.shape[0]
    pre = conv_b_ref[...]
    for k in range(taps):
        top = HALO - (taps - 1) + k
        pre = pre + conv_w[k : k + 1] * padded[top : top + GROUP]
    padded[0:HALO] = padded[GROUP : GROUP + HALO]
    active, slope = silu_slope(pre)
    active = active.astype(bf16)
    active_ref[...] = active
    slope_ref[...] = slope.astype(bf16)
    signal = active[:, :width]
    entry = active[:, width : width + states]
    readout = active[:, width + states :]
    signal_wide = signal.astype(f32)

    raw = projected[:, width + conv_cols :].T[:8]
    raw_ref[0] = raw
    step, _, log_step, _ = step_values(raw + step_ref[0:8, 0:1])
    running = sum_along(step * step_ref[8:16, 0:1], order[...])
    later = running - log_step
    total = running[:, GROUP - 1 :]
    columns = to_columns([running * LOG2E, jnp.exp(running), jnp.exp(total - later)])
    later = later * LOG2E
    early_wide = spread_heads(columns, 8, heads, size)
    tail_wide = spread_heads(columns, 16, heads, size)
    first, second = slice(0, HALF), slice(HALF, GROUP)
    scores = dot_nt(readout[first], entry[first])
    later_scores = dot_nt(readout[second], entry)
    within = []
    for h in range(heads):
        part = signal[:, h * size : (h + 1) * size]
        begin, end = columns[first, h : h + 1], columns[second, h : h + 1]
        row_first, row_second = later[h : h + 1, first], later[h : h + 1, second]
        near = jnp.exp2(begin - row_first + barred[...]) * scores
        full = jnp.exp2(end - row_first) * later_scores[:, first]
        last = jnp.exp2(end - row_second + barred[...]) * later_scores[:, second]
        both = jnp.concatenate([full.astype(bf16), last.astype(bf16)], axis=1)
        within.append(
            jnp.concatenate([dot(near.astype(bf16), part[first]), dot(both, part)], axis=0)
        )
    start = state[...]
    start_low = start.astype(bf16)
    start_ref[0] = start_low
    carried = dot(readout, start_low) * early_wide
    ssd = jnp.concatenate(within, axis=1) + carried + rows_ref[0:1] * signal_wide
    tail = (signal_wide * tail_wide).astype(bf16)
    state[...] = start * early_wide[GROUP - 1 :] + dot_tn(entry, tail)

    gate_act, gate_slope = silu_slope(projected[:, :width])
    gate_act_ref[...] = gate_act.astype(bf16)
    gate_slope_ref[...] = gate_slope.astype(bf16)
    ssd_ref[...] = ssd
    gated = ssd * gate_act
    scaled = (gated * rows_ref[1:2]).astype(bf16)
    scaled_ref[...] = scaled
    square_ref[0] = sum_lanes(gated * gated)
    placed[slot] = scaled
    where = in_time(place_ref[0], turn)
    store(placed.at[slot], targets, scatter_places(count), where, out_semaphores.at[slot])

    @pl.when(turn == pl.num_programs(0) - 1)
    def _():
        for other in range(2):
            stored(placed, targets, out_semaphores, other)


def time_estimate(microseconds, accessed):
    return pl.CostEstimate(
        flops=int(microseconds * 1.1e9), bytes_accessed=int(accessed), transcendentals=0
    )


def fixed(shape):
    return pl.BlockSpec(shape, lambda turn, place: (0,) * len(shape), pipeline_mode=pl.Buffered(1))


def anywhere(values):
    return [pl.BlockSpec(memory_space=pltpu.HBM)] * len(values)


def run_forward(place, pieces, params, dims):
    heads, size, states, count = dims
    arrays, table = pieces
    dim = params[0].shape[0]
    width, conv_cols = heads * size, params[1].shape[1]
    blocks = len(table)
    tokens = blocks * GROUP

    def moving(columns):
        return pl.BlockSpec((GROUP, columns), lambda turn, place: (turn, 0))

    def rows_of_block(height, columns):
        return pl.BlockSpec((1, height, columns), lambda turn, place: (turn, 0, 0))

    results = pl.pallas_call(
        functools.partial(forward_kernel, dims, table, len(arrays)),
        grid_spec=pltpu.PrefetchScalarGridSpec(
            num_scalar_prefetch=1,
            grid=(blocks,),
            in_specs=[*anywhere(arrays), *[fixed(param.shape) for param in params]],
            out_specs=[
                moving(conv_cols),
                moving(conv_cols),
                moving(conv_cols),
                moving(width),
                moving(width),
                rows_of_block(8, GROUP),
                moving(width),
                rows_of_block(states, width),
                moving(width),
                rows_of_block(8, GROUP),
                moving(dim),
                *anywhere(range(4)),
            ],
            scratch_shapes=[
                pltpu.VMEM((states, width), f32),
                pltpu.VMEM((HALO + GROUP, conv_cols), f32),
                pltpu.VMEM((GROUP, GROUP), bf16),
                pltpu.VMEM((HALF, HALF), f32),
                pltpu.VMEM((2, GROUP, dim), bf16),
                pltpu.SemaphoreType.DMA((2,)),
                pltpu.VMEM((2, GROUP, width), bf16),
                pltpu.SemaphoreType.DMA((2,)),
            ],
        ),
        out_shape=[
            jax.ShapeDtypeStruct((tokens, conv_cols), bf16),
            jax.ShapeDtypeStruct((tokens, conv_cols), bf16),
            jax.ShapeDtypeStruct((tokens, conv_cols), bf16),
            jax.ShapeDtypeStruct((tokens, width), bf16),
            jax.ShapeDtypeStruct((tokens, width), bf16),
            jax.ShapeDtypeStruct((blocks, 8, GROUP), f32),
            jax.ShapeDtypeStruct((tokens, width), f32),
            jax.ShapeDtypeStruct((blocks, states, width), bf16),
            jax.ShapeDtypeStruct((tokens, width), bf16),
            jax.ShapeDtypeStruct((blocks, 8, GROUP), f32),
            jax.ShapeDtypeStruct((tokens, dim), bf16),
            *scatter_shapes(count, width),
        ],
        compiler_params=pltpu.CompilerParams(vmem_limit_bytes=60 * MIB),
        cost_estimate=time_estimate(blocks * 3.0, tokens * (4 * dim + 24 * width)),
        name="forward_blocks",
    )(place, *arrays, *params)
    return results[:11], results[11:]


def out_grad_kernel(table, given, place_ref, *refs):
    arrays, refs = refs[:given], refs[given:]
    scaled_ref, out_rows_ref, out_grad_ref, slope_ref, cot_ref, buffer, semaphores = refs
    place = place_ref[0]
    cot = fetched(arrays, table, buffer, semaphores, lambda block: in_time(place, block), 2)
    cot_ref[...] = cot
    out_grad = dot_nt(cot, out_rows_ref[...])
    out_grad_ref[...] = out_grad
    for block in range(2):
        here = slice(block * GROUP, (block + 1) * GROUP)
        slope_ref[block] = sum_lanes(out_grad[here] * scaled_ref[here].astype(f32))


def run_out_grad(place, cots, scaled, out_rows):
    arrays, table = cots
    width, dim = out_rows.shape
    blocks = len(table)
    tokens = blocks * GROUP
    return pl.pallas_call(
        functools.partial(out_grad_kernel, table, len(arrays)),
        grid_spec=pltpu.PrefetchScalarGridSpec(
            num_scalar_prefetch=1,
            grid=(blocks // 2,),
            in_specs=[
                *anywhere(arrays),
                pl.BlockSpec((2 * GROUP, width), lambda turn, place: (turn, 0)),
                fixed(out_rows.shape),
            ],
            out_specs=[
                pl.BlockSpec((2 * GROUP, width), lambda turn, place: (turn, 0)),
                pl.BlockSpec((2, 8, GROUP), lambda turn, place: (turn, 0, 0)),
                pl.BlockSpec((2 * GROUP, dim), lambda turn, place: (turn, 0)),
            ],
            scratch_shapes=[pltpu.VMEM((2, 2 * GROUP, dim), bf16), pltpu.SemaphoreType.DMA((2,))],
        ),
        out_shape=[
            jax.ShapeDtypeStruct((tokens, width), f32),
            jax.ShapeDtypeStruct((blocks, 8, GROUP), f32),
            jax.ShapeDtypeStruct((tokens, dim), bf16),
        ],
        compiler_params=pltpu.CompilerParams(vmem_limit_bytes=60 * MIB),
        cost_estimate=time_estimate(12, tokens * (4 * dim + 6 * width)),
        name="out_grad",
    )(place, *arrays, scaled, out_rows)


def backward_kernel(dims, place_ref, *refs):
    heads, size, states, count = dims
    width = heads * size
    conv_cols = width + 2 * states
    conv_in_ref, active_ref, slope_ref, gate_act_ref, gate_slope_ref = refs[:5]
    raw_ref, ssd_ref, start_ref, out_grad_ref, norm_ref = refs[5:10]
    conv_w_ref, step_ref, rows_ref = refs[10:13]
    out_ref, targets = refs[13], refs[14:18]
    sums = refs[18:24]
    gain_ref, skip_ref, conv_wg_ref, conv_bg_ref, bias_ref, rate_ref = sums
    state, pre_grads, order, back_order, barred, placed, semaphores = refs[24:]
    taps = conv_w_ref.shape[0]
    turn = pl.program_id(0)
    slot = lax.rem(turn, 2)

    @pl.when(turn >= 2)
    def _():
        stored(placed, targets, semaphores, slot)

    @pl.when(pl.program_id(0) == 0)
    def _():
        state[...] = jnp.zeros_like(state)
        pre_grads[0:HALO] = jnp.zeros_like(pre_grads[0:HALO])
        for total in sums:
            total[...] = jnp.zeros_like(total)
        row, column = order_indices(GROUP)
        order[...] = ones_where(row <= column)
        back_order[...] = ones_where(row >= column)
        row, column = order_indices(HALF)
        barred[...] = jnp.where(row <= column, 0.0, -1e30)

    gate_act, ssd, out_grad = gate_act_ref[...].astype(f32), ssd_ref[...], out_grad_ref[...]
    norms = norm_ref[0].T
    scale, slope = norms[:, 0:1], norms[:, 1:2]
    gated = ssd * gate_act
    gain_ref[...] += jnp.sum(out_grad * (gated * scale), axis=0, keepdims=True)
    gated_grad = out_grad * (rows_ref[1:2] * scale) - gated * slope
    grad_low = (gated_grad * gate_act).astype(bf16)
    gate_grad = (gated_grad * ssd * gate_slope_ref[...].astype(f32)).astype(bf16)
    out_ref[:, :width] = gate_grad
    placed[slot, :, :width] = gate_grad
    ssd_grad = grad_low.astype(f32)

    raw = raw_ref[0] + step_ref[0:8, 0:1]
    rate = step_ref[8:16, 0:1]
    step, sig, log_step, ratio = step_values(raw)
    decay = step * rate
    running = sum_along(decay, order[...])
    later = running - log_step
    total = running[:, GROUP - 1 :]
    columns = to_columns([later * LOG2E, jnp.exp(running), jnp.exp(total - later)])
    running = running * LOG2E
    early_wide = spread_heads(columns, 8, heads, size)
    tail_wide = spread_heads(columns, 16, heads, size)

    signal = active_ref[:, :width]
    entry = active_ref[:, width : width + states]
    readout = active_ref[:, width + states :]
    signal_wide = signal.astype(f32)
    start_low = start_ref[0]
    end_grad = state[...]
    end_low = end_grad.astype(bf16)
    first, second = slice(0, HALF), slice(HALF, GROUP)
    scores = dot_nt(entry[first], readout)
    later_scores = dot_nt(entry[second], readout[second])
    near_grad, far_grad, last_grad = 0.0, 0.0, 0.0
    within = []
    for h in range(heads):
        part, grad = signal[:, h * size : (h + 1) * size], grad_low[:, h * size : (h + 1) * size]
        begin, end = columns[first, h : h + 1], columns[second, h : h + 1]
        row_first, row_second = running[h : h + 1, first], running[h : h + 1, second]
        near = jnp.exp2(row_first - begin + barred[...])
        full = jnp.exp2(row_second - begin)
        last = jnp.exp2(row_second - end + barred[...])
        both = jnp.concatenate(
            [
                (near * scores[:, first]).astype(bf16),
                (full * scores[:, second]).astype(bf16),
            ],
            axis=1,
        )
        final = (last * later_scores).astype(bf16)
        within.append(jnp.concatenate([dot(both, grad), dot(final, grad[second])], axis=0))
        cross = dot_nt(part[first], grad)
        near_grad = near_grad + cross[:, first] * near
        far_grad = far_grad + cross[:, second] * full
        last_grad = last_grad + dot_nt(part[second], grad[second]) * last
    tail_grad = tail_wide * dot(entry, end_low)
    signal_grad = jnp.concatenate(within, axis=1) + tail_grad
    score_first = jnp.concatenate([near_grad, far_grad], axis=1).astype(bf16)
    score_second = last_grad.astype(bf16)
    tail = (signal_wide * tail_wide).astype(bf16)
    head_grad = (ssd_grad * early_wide).astype(bf16)
    entry_grad = jnp.concatenate(
        [dot(score_first, readout), dot(score_second, readout[second])], axis=0
    ) + dot_nt(tail, end_low)
    readout_grad = dot_tn(score_first, entry[first]) + dot_nt(head_grad, start_low)
    readout_last = readout_grad[second] + dot_tn(score_second, entry[second])
    total_wide = early_wide[GROUP - 1 :]
    state[...] = end_grad * total_wide + dot_tn(readout, head_grad)

    skip = rows_ref[0:1]
    ones = head_ones(width, size)
    column_part = signal_wide * signal_grad
    row_part = ssd_grad * (ssd - skip * signal_wide)
    end_part = jnp.sum(signal_wide * tail_grad, axis=0, keepdims=True) + total_wide * jnp.sum(
        start_low.astype(f32) * end_grad, axis=0, keepdims=True
    )

    def head_sums(value, parts):
        return sum(dot_nt(ones, part) for part in split_parts(value, parts))

    end_rows = head_sums(jnp.broadcast_to(end_part, (8, width)), 2)[:, 0:1]
    decay_grad = sum_along(head_sums(row_part - column_part, 2), back_order[...]) + end_rows
    raw_grad = head_sums(column_part, 1) * ratio + decay_grad * rate * sig
    skip_ref[...] += jnp.sum(ssd_grad * signal_wide, axis=0, keepdims=True)
    bias_ref[...] += raw_grad
    rate_ref[...] += decay_grad * decay
    raw_low = to_columns([raw_grad]).astype(bf16)
    out_ref[:, width + conv_cols :] = raw_low
    placed[slot, :, width + conv_cols :] = raw_low

    pre_grads[GROUP : GROUP + HALO] = pre_grads[0:HALO]
    pre_grads[0:GROUP, :width] = (signal_grad + skip * ssd_grad) * slope_ref[:, :width].astype(f32)
    sides = slope_ref[:, width:].astype(f32)
    pre_grads[0:GROUP, width : width + states] = entry_grad * sides[:, :states]
    pre_grads[0:HALF, width + states :] = readout_grad[first] * sides[first, states:]
    pre_grads[HALF:GROUP, width + states :] = readout_last * sides[second, states:]
    conv_w = conv_w_ref[...]
    conv_in = conv_in_ref[...].astype(f32)
    conv_grad = 0.0
    for k in range(taps):
        ahead = taps - 1 - k
        shifted = pre_grads[ahead : ahead + GROUP]
        conv_grad = conv_grad + conv_w[k : k + 1] * shifted
        conv_wg_ref[k : k + 1] += jnp.sum(shifted * conv_in, axis=0, keepdims=True)
        if ahead == 0:
            conv_bg_ref[...] += jnp.sum(shifted, axis=0, keepdims=True)
    conv_low = conv_grad.astype(bf16)
    out_ref[:, width : width + conv_cols] = conv_low
    placed[slot, :, width : width + conv_cols] = conv_low

    where = in_time(place_ref[0], pl.num_programs(0) - 1 - turn)
    store(placed.at[slot], targets, scatter_places(count), where, semaphores.at[slot])

    @pl.when(turn == pl.num_programs(0) - 1)
    def _():
        for other in range(2):
            stored(placed, targets, semaphores, other)


def run_backward(place, values, params, dims):
    heads, size, states, count = dims
    conv_cols, width = values[0].shape[1], heads * size
    tokens = values[0].shape[0]
    blocks = tokens // GROUP
    last = blocks - 1
    out_cols = width + conv_cols + LANES

    def moving(columns):
        return pl.BlockSpec((GROUP, columns), lambda turn, place: (last - turn, 0))

    def rows_of_block():
        return pl.BlockSpec((1, 8, GROUP), lambda turn, place: (last - turn, 0, 0))

    sums = [(1, width), (1, width), params[0].shape, (1, conv_cols), (8, GROUP), (8, GROUP)]
    return pl.pallas_call(
        functools.partial(backward_kernel, dims),
        grid_spec=pltpu.PrefetchScalarGridSpec(
            num_scalar_prefetch=1,
            grid=(blocks,),
            in_specs=[
                moving(conv_cols),
                moving(conv_cols),
                moving(conv_cols),
                moving(width),
                moving(width),
                rows_of_block(),
                moving(width),
                pl.BlockSpec((1, states, width), lambda turn, place: (last - turn, 0, 0)),
                moving(width),
                rows_of_block(),
                *[fixed(param.shape) for param in params],
            ],
            out_specs=[
                moving(out_cols),
                *anywhere(range(4)),
                *[fixed(shape) for shape in sums],
            ],
            scratch_shapes=[
                pltpu.VMEM((states, width), f32),
                pltpu.VMEM((GROUP + HALO, conv_cols), f32),
                pltpu.VMEM((GROUP, GROUP), bf16),
                pltpu.VMEM((GROUP, GROUP), bf16),
                pltpu.VMEM((HALF, HALF), f32),
                pltpu.VMEM((2, GROUP, out_cols), bf16),
                pltpu.SemaphoreType.DMA((2,)),
            ],
        ),
        out_shape=[
            jax.ShapeDtypeStruct((tokens, out_cols), bf16),
            *scatter_shapes(count, out_cols),
        ]
        + [jax.ShapeDtypeStruct(shape, f32) for shape in sums],
        compiler_params=pltpu.CompilerParams(vmem_limit_bytes=60 * MIB),
        cost_estimate=time_estimate(blocks * 3.5, tokens * 40 * width),
        name="backward_blocks",
    )(place, *values, *params)


def widen_kernel(place_ref, piece_ref, out_ref):
    out_ref[...] = piece_ref[0].astype(f32)


def assemble_out(place, pieces, per):
    count, size, dim = pieces.shape
    groups = count // per

    def source(turn, place):
        relative = (turn % groups * per + turn // groups) ^ place[0]
        return ((relative & 1) * (count // 2) + (relative >> 1), 0, 0)

    return pl.pallas_call(
        widen_kernel,
        grid_spec=pltpu.PrefetchScalarGridSpec(
            num_scalar_prefetch=1,
            grid=(count,),
            in_specs=[pl.BlockSpec((1, size, dim), source)],
            out_specs=pl.BlockSpec((size, dim), lambda turn, place: (turn, 0)),
        ),
        out_shape=jax.ShapeDtypeStruct((count * size, dim), f32),
        cost_estimate=time_estimate(5, count * size * dim * 6),
        name="assemble_out_weight_grad",
    )(place, pieces)


def assemble_kernel(dims, tables, given, place_ref, *refs):
    heads, size, states, count = dims
    width, shared = heads * size, 2 * states
    inner = count * width
    mains, sides, out_ref, sums = refs[: given[0]], refs[given[0] : given[1]], refs[-2], refs[-1]

    def piece(arrays, table, relative):
        parts = []
        for half in range(2):
            array, row, height = table[half, relative]
            parts.append(arrays[array][row : row + height].astype(f32))
        return jnp.concatenate(parts, axis=0).T

    for relative in range(count):
        device = place_ref[0] ^ relative
        columns = piece(mains, tables[0], relative)
        out_ref[pl.ds(pl.multiple_of(device * width, 8), width)] = columns[:width]
        middle = pl.multiple_of(inner + device * width, 8)
        out_ref[pl.ds(middle, width)] = columns[width:]
        sums[device] = piece(sides, tables[1], relative)[: shared + STEP_ROWS]
    total = sums[0, :shared]
    for device in range(1, count):
        total = total + sums[device, :shared]
    out_ref[2 * inner : 2 * inner + shared] = total
    for device in range(count):
        last = 2 * inner + shared + device * heads
        out_ref[last : last + heads] = sums[device, shared : shared + heads]


def assemble(place, mains, sides, dims):
    heads, size, states, count = dims
    mains, main_table = gathered(mains)
    sides, side_table = gathered(sides)
    rows = sum(main_table[half, 0][2] for half in range(2))
    out_rows = 2 * count * heads * size + 2 * states + count * heads

    def whole(value):
        return pl.BlockSpec(
            value.shape,
            lambda turn, place: (0,) * len(value.shape),
            pipeline_mode=pl.Buffered(1),
        )

    return pl.pallas_call(
        functools.partial(
            assemble_kernel, dims, (main_table, side_table), (len(mains), len(mains) + len(sides))
        ),
        grid_spec=pltpu.PrefetchScalarGridSpec(
            num_scalar_prefetch=1,
            grid=(1,),
            in_specs=[whole(value) for value in (*mains, *sides)],
            out_specs=pl.BlockSpec(
                (out_rows, rows), lambda turn, place: (0, 0), pipeline_mode=pl.Buffered(1)
            ),
            scratch_shapes=[pltpu.VMEM((count, 2 * states + STEP_ROWS, rows), f32)],
        ),
        out_shape=jax.ShapeDtypeStruct((out_rows, rows), f32),
        compiler_params=pltpu.CompilerParams(vmem_limit_bytes=60 * MIB),
        cost_estimate=time_estimate(8, out_rows * rows * 6),
        name="assemble_in_weight_grad",
    )(place, *mains, *sides)


def body(
    tokens,
    norm_gain,
    in_weight,
    conv_weight,
    conv_bias,
    dt_bias,
    decay_log,
    skip_scale,
    gate_gain,
    out_weight,
    cotangent,
):
    count, mine = lax.axis_size("seq"), lax.axis_index("seq")
    place = mine.astype(jnp.int32).reshape(1)
    inner, all_heads, conv_all = gate_gain.shape[0], dt_bias.shape[0], conv_bias.shape[0]
    size, states = inner // all_heads, (conv_all - inner) // 2
    heads, width = all_heads // count, inner // count
    dims = (heads, size, states, count)
    shared = 2 * states
    conv_cols = width + shared
    tok_rows = tokens.shape[1]
    per_plane = out_weight.shape[0] // width

    def own(vector, per, first=0):
        return lax.dynamic_slice_in_dim(vector, first + mine * per, per, vector.ndim - 1)

    def own_conv(array, first=0):
        return jnp.concatenate(
            [own(array, width, first), array[..., first + inner : first + conv_all]], axis=-1
        )

    tokens_row = tokens[0].astype(f32)
    inverse = lax.rsqrt(jnp.mean(tokens_row * tokens_row, axis=-1, keepdims=True) + epsilon)
    normed_own = (tokens_row * inverse * norm_gain).astype(bf16)
    step_own = own(in_weight, heads, inner + conv_all)
    w_own = jnp.concatenate(
        [
            own(in_weight, width),
            own_conv(in_weight, inner),
            jnp.pad(step_own, ((0, 0), (0, LANES - heads))),
        ],
        axis=1,
    )
    w_cols = lax.all_gather(w_own, "batch", axis=0, tiled=True)
    stages = gather_stages()
    held = gather_stage(gather_stage(gather_start(normed_own), 0), 1)
    held, cots = together(held, gather_start(cotangent[0]))
    cots = gather_stage(cots, 0)
    for stage in range(2, stages):
        held = gather_stage(held, stage)
    w_cols, held, cots, out_owned = together(w_cols, held, cots, out_weight)
    cots = gather_stage(cots, 1)
    out_rows = rows_from_owner(out_owned, width)

    conv_w, conv_b = own_conv(conv_weight), own_conv(conv_bias)[None]
    per_head = jnp.stack([own(dt_bias, heads), -jnp.exp(own(decay_log, heads))])
    per_head = jnp.pad(per_head, ((0, 0), (0, 8 - heads))).reshape(16, 1)
    step_rows = jnp.broadcast_to(per_head, (16, LANES))
    gain_own = own(gate_gain, width)[None]
    rows = jnp.concatenate(
        [jnp.repeat(own(skip_scale, heads), size)[None], gain_own, jnp.zeros((6, width), f32)],
        axis=0,
    )
    results, out_parts = run_forward(
        place, token_pieces(held), (w_cols, conv_w, conv_b, step_rows, rows), dims
    )
    conv_in, active, slope, gate_act, gate_slope, raw, ssd, starts, scaled, squares, normed = results
    out_parts, cots, out_rows = together(out_parts, cots, out_rows)
    for stage in range(2, stages):
        cots = gather_stage(cots, stage)

    def out_product(part):
        return dot(part, out_rows)

    out_send = out_product(out_parts[0]).astype(bf16)
    out_send, cots = together(out_send, cots)
    out_grad, slopes, cot = run_out_grad(place, token_pieces(cots), scaled, out_rows)
    sums = jnp.stack([squares[:, 0].reshape(-1), slopes[:, 0].reshape(-1)])
    out_ready, out_held = scatter_near(out_product, out_parts[1:], out_send)
    sums = sum_seq(sums)
    scale = lax.rsqrt(sums[0] / inner + epsilon)
    norms = jnp.stack([scale, scale * scale * scale * sums[1] / inner])
    norms = jnp.pad(norms, ((0, 6), (0, 0))).reshape(8, -1, GROUP).swapaxes(0, 1)
    scaled_cot = (cot.astype(f32) * scale[:, None]).astype(bf16)
    out_term = jnp.einsum("te,td->ed", scaled, scaled_cot, preferred_element_type=f32)
    out_term, norms, out_ready = together(out_term.astype(bf16), norms, out_ready)
    out_sum = lax.psum_scatter(out_term, "batch", scatter_dimension=0, tiled=True)
    out_ready, out_held = scatter_far(out_ready, out_held, 0)

    values = (conv_in, active, slope, gate_act, gate_slope, raw, ssd, starts, out_grad, norms)
    results = run_backward(place, values, (conv_w, step_rows, rows), dims)
    proj_grad, back_parts = results[0], results[1:5]
    gain_term, skip_term, conv_w_term, conv_b_term, bias_term, rate_term = results[5:]
    proj_grad, back_parts, out_ready, out_held, out_sum = together(
        proj_grad, back_parts, out_ready, out_held, out_sum
    )

    def back_product(part):
        return jnp.einsum("tf,df->td", part, w_cols, preferred_element_type=f32)

    def weight_product(part):
        return jnp.einsum("td,tf->df", normed, part, preferred_element_type=f32).astype(bf16)

    for stage in range(1, stages - 1):
        out_ready, out_held = scatter_far(out_ready, out_held, stage)
    out_pieces = to_owner(out_sum)[None]
    back_send = back_product(back_parts[0]).astype(bf16)
    back_send, proj_grad, out_pieces = together(back_send, proj_grad, out_pieces)
    out_pieces = double(out_pieces, 0)
    main_term = weight_product(proj_grad[:, : 2 * width])
    main_term, keeps, out_pieces, out_held = together(
        main_term, back_parts[1:], out_pieces, out_held
    )
    main_sum = lax.psum_scatter(main_term, "batch", scatter_dimension=0, tiled=True)
    out_pieces = double(out_pieces, 1)
    back_ready, back_held = scatter_near(back_product, keeps, back_send)
    back_ready, proj_grad, main_term, out_pieces = together(
        back_ready, proj_grad, main_term, out_pieces
    )
    back_ready, back_held = scatter_far(back_ready, back_held, 0)
    for stage in range(2, stages):
        out_pieces = double(out_pieces, stage)
    side_term = weight_product(proj_grad[:, 2 * width :])
    side_sum = lax.psum_scatter(side_term, "batch", scatter_dimension=0, tiled=True)
    out_weight_grad = assemble_out(place, out_pieces, per_plane)

    norm_gain_term = jnp.sum(main_term.astype(f32) * w_cols[:, : 2 * width].astype(f32), axis=1)
    norm_gain_term += jnp.sum(side_term.astype(f32) * w_cols[:, 2 * width :].astype(f32), axis=1)
    norm_gain_term /= norm_gain

    def among_heads(vector, per, total):
        return lax.dynamic_update_slice_in_dim(jnp.zeros((total,), f32), vector, mine * per, 0)

    def among_conv(array):
        wide = jnp.zeros((array.shape[0], inner), f32)
        wide = lax.dynamic_update_slice_in_dim(wide, array[:, :width], mine * width, 1)
        return jnp.concatenate([wide, array[:, width:]], axis=1).reshape(-1)

    skip_heads = jnp.sum(skip_term.reshape(heads, size), axis=1)
    terms = [
        norm_gain_term,
        among_conv(conv_w_term),
        among_conv(conv_b_term),
        among_heads(jnp.sum(bias_term[:heads], axis=1), heads, all_heads),
        among_heads(jnp.sum(rate_term[:heads], axis=1), heads, all_heads),
        among_heads(skip_heads, heads, all_heads),
        among_heads(gain_term[0], width, inner),
    ]
    vector = jnp.concatenate(terms)
    padding = -vector.shape[0] % (8 * LANES)
    vector = jnp.pad(vector, (0, padding)).reshape(-1, LANES)

    axes = [(axis, bit) for axis in ("seq", "batch") for bit in bits_of(lax.axis_size(axis))]
    back_ready, back_held, main_sum, vector, out_weight_grad = together(
        back_ready, back_held, main_sum, vector, out_weight_grad
    )
    mains = gather_stage(gather_start(main_sum), 0)
    for stage in range(1, stages - 1):
        back_ready, back_held = scatter_far(back_ready, back_held, stage)
    vector = vector + exchange(vector, *axes.pop(0))
    back_held, mains, side_sum, vector = together(back_held, mains, side_sum, vector)
    sides = gather_start(side_sum)
    for stage in range(1, stages):
        mains = gather_stage(mains, stage, late=True)
        sides = gather_stage(sides, stage - 1, late=True)
        vector = vector + exchange(vector, *axes.pop(0))
        mains, sides, vector = together(mains, sides, vector)
    sides = gather_stage(sides, stages - 1, late=True)
    normed_grad = scatter_end(back_held)
    cot_row = cotangent[0].astype(f32)
    gained = norm_gain * normed_grad
    slope = inverse * inverse * inverse * jnp.mean(gained * tokens_row, axis=-1, keepdims=True)
    input_grad = cot_row + inverse * gained - tokens_row * slope
    own_scale = lax.dynamic_slice_in_dim(scale, mine * tok_rows, tok_rows, 0)[:, None]
    block_out = (tokens_row + own_scale * scatter_end(out_held)).astype(bf16)
    vector = vector + exchange(vector, *axes.pop(0))
    in_weight_grad = assemble(place, mains, sides, dims).T
    while axes:
        vector = vector + exchange(vector, *axes.pop(0))
    vector = vector.reshape(-1)

    parts, offset = [], 0
    for term in terms:
        parts.append(vector[offset : offset + term.shape[0]])
        offset += term.shape[0]
    return (
        block_out[None],
        input_grad[None],
        parts[0],
        in_weight_grad,
        parts[1].reshape(conv_weight.shape),
        parts[2],
        parts[3],
        parts[4],
        parts[5],
        parts[6],
        out_weight_grad,
    )


def solution(mesh):
    placed = (
        P("batch", "seq", None),
        P(),
        P("batch", None),
        P(),
        P(),
        P(),
        P(),
        P(),
        P(),
        P("batch", None),
        P("batch", "seq", None),
    )
    return jax.shard_map(
        body,
        mesh=mesh,
        in_specs=placed,
        out_specs=(
            P("batch", "seq", None),
            P("batch", "seq", None),
            P(),
            P("batch", None),
            P(),
            P(),
            P(),
            P(),
            P(),
            P(),
            P("batch", None),
        ),
        check_vma=False,
    )
```

```python
import functools

import jax
import jax.numpy as jnp
from jax import lax
from jax.experimental import pallas as pl
from jax.experimental.pallas import tpu as pltpu
from jax.sharding import PartitionSpec as P

GROUP = 256
LANES = 128
HALF = GROUP // 2
HALO = 8
STEP_ROWS = 16
LOG2E = 1.4426950408889634
epsilon = 1e-05
f32 = jnp.float32
bf16 = jnp.bfloat16
MIB = 2**20


def exchange(value, axis, distance):
    count = lax.axis_size(axis)
    return lax.ppermute(value, axis, [(source, source ^ distance) for source in range(count)])


def bits_of(count):
    return [1 << k for k in range(count.bit_length() - 1)]


def placed_order(count):
    return [2 * k for k in range(count // 2)] + [2 * k + 1 for k in range(count // 2)]


def together(*values):
    return lax.optimization_barrier(values)


def far_orders():
    far = bits_of(lax.axis_size("seq"))[1:]
    return far, far[::-1]


def gather_start(value):
    half = value.shape[0] // 32 * 16
    return tuple({"base": part, "fresh": None, "near": []} for part in (value[:half], value[half:]))


def gather_stage(held, stage, late=False):
    grown = []
    for half, order in zip(held, far_orders()):
        base, fresh, near = half["base"], half["fresh"], list(half["near"])
        if stage >= 1:
            merged = base if stage == len(order) else jnp.concatenate([base, fresh], axis=0)
            if not late:
                near.append(exchange(merged if stage == 1 else fresh, "seq", 1))
            elif stage == len(order):
                near = [exchange(base, "seq", 1), exchange(fresh, "seq", 1)]
            base = merged
        if stage < len(order):
            fresh = exchange(base, "seq", order[stage])
        grown.append({"base": base, "fresh": fresh, "near": near})
    return tuple(grown)


def gather_stages():
    return len(bits_of(lax.axis_size("seq")))


def gathered(held):
    arrays, table = [], {}
    for number, (half, order) in enumerate(zip(held, far_orders())):
        indices = [0]
        for bit in order:
            indices += [index | bit for index in indices]
        middle = len(indices) // 2
        groups = [(half["base"], indices[:middle]), (half["fresh"], indices[middle:])]
        bounds = [0] + [2 << k for k in range(len(order))]
        if len(half["near"]) < len(order):
            bounds = [0, middle, len(indices)]
        for value, first, last in zip(half["near"], bounds, bounds[1:]):
            groups.append((value, [index | 1 for index in indices[first:last]]))
        for value, members in groups:
            rows = value.shape[0] // len(members)
            for turn, index in enumerate(members):
                table[number, index] = (len(arrays), turn * rows, rows)
            arrays.append(value)
    return arrays, table


def token_pieces(held):
    arrays, table = gathered(held)
    indices = range(lax.axis_size("seq"))
    return arrays, tuple(table[half, index] for index in indices for half in range(2))


def gather_all(value):
    held = gather_start(value)
    for stage in range(gather_stages()):
        held = gather_stage(held, stage)
    return held


def scatter_places(count):
    far = bits_of(count)[1:]
    table = {}
    row = {}
    for near in (1, 0):
        for sent in (True, False):
            for half, order in enumerate((far, far[::-1])):
                members = [0]
                for bit in order[:0:-1]:
                    members += [member | bit for member in members]
                for member in members:
                    index = member | near | (order[0] if sent else 0)
                    array = 0 if near else (1 + half if sent else 3)
                    table[index * 2 + half] = (array, row.get(array, 0))
                    row[array] = row.get(array, 0) + GROUP
    return tuple(table[k] for k in range(2 * count))


def scatter_shapes(count, columns):
    blocks = (count, count // 4, count // 4, count // 2)
    return [jax.ShapeDtypeStruct((part * GROUP, columns), bf16) for part in blocks]


def scatter_near(product, parts, sent):
    arriving = exchange(sent, "seq", 1)
    first, second, kept = parts
    rows = first.shape[0]

    def summed(part, row):
        return (product(part) + arriving[row : row + part.shape[0]].astype(f32)).astype(bf16)

    sends = (summed(first, 0), summed(second, rows))
    sends, kept = together(sends, kept)
    return sends, {"kept": summed(kept, 2 * rows), "arrived": ([], [])}


def scatter_rows(held, half, first, last):
    top = half * (held["kept"].shape[0] // 2)
    total = held["kept"][top + first : top + last].astype(f32)
    for value in held["arrived"][half]:
        total = total + value[first:last].astype(f32)
    return total


def scatter_far(sends, held, stage):
    orders = far_orders()
    arrived = tuple(
        [*held["arrived"][half], exchange(sends[half], "seq", orders[half][stage])]
        for half in range(2)
    )
    held = {"kept": held["kept"], "arrived": arrived}
    rows = sends[0].shape[0]
    if stage + 1 == len(orders[0]):
        return (), held
    ready = tuple(
        scatter_rows(held, half, rows // 2, rows).astype(bf16) for half in range(2)
    )
    return ready, held


def scatter_end(held):
    rows = held["arrived"][0][-1].shape[0]
    return jnp.concatenate([scatter_rows(held, half, 0, rows) for half in range(2)], axis=0)


def sum_seq(value):
    for bit in bits_of(lax.axis_size("seq")):
        value = value + exchange(value, "seq", bit)
    return value


def plane_pairs(ahead):
    planes, count = lax.axis_size("batch"), lax.axis_size("seq")
    per = count // planes
    pairs = []
    for owner in range(planes):
        for piece in range(planes):
            for k in range(per):
                holder = owner * count + piece * per + k
                user = (piece + ahead) % planes * count + owner * per + k
                pairs.append((holder, user))
    return pairs


def rows_from_owner(out_weight, width, aheads):
    planes, count = lax.axis_size("batch"), lax.axis_size("seq")
    per, size = count // planes, width // planes
    mine = lax.axis_index("seq")
    piece = lax.dynamic_slice_in_dim(out_weight, mine % per * width + mine // per * size, size, 0)
    return [lax.ppermute(piece, ("batch", "seq"), plane_pairs(ahead)) for ahead in aheads]


def rows_joined(arriving):
    planes, plane = lax.axis_size("batch"), lax.axis_index("batch")
    size = arriving[0].shape[0]
    doubled = jnp.concatenate(arriving[::-1] * 2, axis=0)
    return lax.dynamic_slice_in_dim(doubled, (planes - 1 - plane) * size, planes * size, 0)


def to_owner(summed):
    return lax.ppermute(
        summed, ("batch", "seq"), [(user, holder) for holder, user in plane_pairs(0)]
    )


def double(held, turn):
    bits = bits_of(lax.axis_size("seq"))
    return jnp.concatenate([held, exchange(held, "seq", (bits[1:] + [1])[turn])], axis=0)


def step_values(raw):
    small = jnp.exp(-jnp.abs(raw))
    step = jnp.maximum(raw, 0.0) + jnp.log1p(small)
    sig = jnp.where(raw >= 0, 1.0, small) / (1.0 + small)
    tiny = raw < -20.0
    log_step = jnp.where(tiny, raw, jnp.log(step))
    ratio = jnp.where(tiny, 1.0, sig / step)
    return step, sig, log_step, ratio


def dot(a, b):
    return jnp.dot(a, b, preferred_element_type=f32)


def dot_nt(a, b):
    return lax.dot_general(a, b, (((1,), (1,)), ((), ())), preferred_element_type=f32)


def dot_tn(a, b):
    return lax.dot_general(a, b, (((0,), (0,)), ((), ())), preferred_element_type=f32)


def sigmoid(value):
    return 0.5 * jnp.tanh(0.5 * value) + 0.5


def silu_slope(value):
    sig = sigmoid(value)
    active = value * sig
    return active, sig + active * (1.0 - sig)


def split_parts(value, count):
    parts = []
    for _ in range(count):
        part = value.astype(bf16)
        parts.append(part)
        value = value - part.astype(f32)
    return parts


def sum_along(rows, order):
    parts = jnp.concatenate([part.astype(f32) for part in split_parts(rows, 3)], axis=0)
    total = dot(parts.astype(bf16), order)
    return total[:8] + total[8:16] + total[16:24]


def to_columns(rows):
    stacked = jnp.concatenate(rows, axis=0)
    missing = LANES - stacked.shape[0]
    return jnp.concatenate([stacked, jnp.zeros((missing, GROUP), f32)], axis=0).T


def spread_heads(value, first, heads, size):
    rows = value.shape[0]
    return jnp.concatenate(
        [jnp.broadcast_to(value[:, first + h : first + h + 1], (rows, size)) for h in range(heads)],
        axis=1,
    )


def head_ones(width, size):
    row = lax.broadcasted_iota(jnp.int32, (8, width), 0)
    column = lax.broadcasted_iota(jnp.int32, (8, width), 1)
    return (column // size == row).astype(f32).astype(bf16)


def sum_lanes(value):
    return dot_nt(jnp.ones((8, value.shape[1]), bf16), value.astype(bf16))


def ones_where(condition):
    return jnp.where(condition, 1.0, 0.0).astype(bf16)


def order_indices(length):
    row = lax.broadcasted_iota(jnp.int32, (length, length), 0)
    column = lax.broadcasted_iota(jnp.int32, (length, length), 1)
    return row, column


def fetch(arrays, table, which, target, semaphore):
    for index, (array, row, rows) in enumerate(table):

        @pl.when(which == index)
        def _():
            pltpu.make_async_copy(arrays[array].at[pl.ds(row, rows)], target, semaphore).start()


def fetched(arrays, table, buffer, semaphores, order, blocks=1):
    step = pl.program_id(0)
    slot, other = lax.rem(step, 2), lax.rem(step + 1, 2)

    def start(step, slot):
        for k in range(blocks):
            target = buffer.at[slot, pl.ds(k * GROUP, GROUP)]
            fetch(arrays, table, order(step * blocks + k), target, semaphores.at[slot])

    @pl.when(step == 0)
    def _():
        start(0, 0)

    @pl.when(step + 1 < pl.num_programs(0))
    def _():
        start(step + 1, other)

    for k in range(blocks):
        source = arrays[0].at[pl.ds(0, GROUP)]
        target = buffer.at[slot, pl.ds(k * GROUP, GROUP)]
        pltpu.make_async_copy(source, target, semaphores.at[slot]).wait()
    return buffer[slot]


def store(source, targets, table, which, semaphore):
    for index, (array, row) in enumerate(table):

        @pl.when(which == index)
        def _():
            target = targets[array].at[pl.ds(row, GROUP)]
            pltpu.make_async_copy(source, target, semaphore).start()


def stored(buffer, targets, semaphores, slot):
    target = targets[0].at[pl.ds(0, GROUP)]
    pltpu.make_async_copy(buffer.at[slot], target, semaphores.at[slot]).wait()


def in_time(place, block):
    return ((block // 2) ^ place) * 2 + block % 2


def forward_kernel(dims, table, given, place_ref, *refs):
    heads, size, states, count = dims
    width = heads * size
    conv_cols = width + 2 * states
    arrays, refs = refs[:given], refs[given:]
    w_ref, conv_w_ref, conv_b_ref, step_ref, rows_ref = refs[:5]
    conv_in_ref, active_ref, slope_ref, gate_act_ref, gate_slope_ref = refs[5:10]
    raw_ref, ssd_ref, start_ref, scaled_ref, square_ref, normed_ref = refs[10:16]
    targets = refs[16:20]
    state, padded, order, barred, buffer, semaphores, placed, out_semaphores = refs[20:]
    turn = pl.program_id(0)
    slot = lax.rem(turn, 2)

    @pl.when(turn == 0)
    def _():
        state[...] = jnp.zeros_like(state)
        padded[0:HALO] = jnp.zeros_like(padded[0:HALO])
        row, column = order_indices(GROUP)
        order[...] = ones_where(row <= column)
        row, column = order_indices(HALF)
        barred[...] = jnp.where(row >= column, 0.0, -1e30)

    @pl.when(turn >= 2)
    def _():
        stored(placed, targets, out_semaphores, slot)

    normed = fetched(
        arrays, table, buffer, semaphores, lambda step: in_time(place_ref[0], step)
    )
    normed_ref[...] = normed
    projected = dot(normed, w_ref[...])
    conv_in = projected[:, width : width + conv_cols].astype(bf16)
    conv_in_ref[...] = conv_in
    padded[HALO : HALO + GROUP] = conv_in.astype(f32)
    conv_w = conv_w_ref[...]
    taps = conv_w.shape[0]
    pre = conv_b_ref[...]
    for k in range(taps):
        top = HALO - (taps - 1) + k
        pre = pre + conv_w[k : k + 1] * padded[top : top + GROUP]
    padded[0:HALO] = padded[GROUP : GROUP + HALO]
    active, slope = silu_slope(pre)
    active = active.astype(bf16)
    active_ref[...] = active
    slope_ref[...] = slope.astype(bf16)
    signal = active[:, :width]
    entry = active[:, width : width + states]
    readout = active[:, width + states :]
    signal_wide = signal.astype(f32)

    raw = projected[:, width + conv_cols :].T[:8]
    raw_ref[0] = raw
    step, _, log_step, _ = step_values(raw + step_ref[0:8, 0:1])
    running = sum_along(step * step_ref[8:16, 0:1], order[...])
    later = running - log_step
    total = running[:, GROUP - 1 :]
    columns = to_columns([running * LOG2E, jnp.exp(running), jnp.exp(total - later)])
    later = later * LOG2E
    early_wide = spread_heads(columns, 8, heads, size)
    tail_wide = spread_heads(columns, 16, heads, size)
    first, second = slice(0, HALF), slice(HALF, GROUP)
    scores = dot_nt(readout[first], entry[first])
    later_scores = dot_nt(readout[second], entry)
    within = []
    for h in range(heads):
        part = signal[:, h * size : (h + 1) * size]
        begin, end = columns[first, h : h + 1], columns[second, h : h + 1]
        row_first, row_second = later[h : h + 1, first], later[h : h + 1, second]
        near = jnp.exp2(begin - row_first + barred[...]) * scores
        full = jnp.exp2(end - row_first) * later_scores[:, first]
        last = jnp.exp2(end - row_second + barred[...]) * later_scores[:, second]
        both = jnp.concatenate([full.astype(bf16), last.astype(bf16)], axis=1)
        within.append(
            jnp.concatenate([dot(near.astype(bf16), part[first]), dot(both, part)], axis=0)
        )
    start = state[...]
    start_low = start.astype(bf16)
    start_ref[0] = start_low
    carried = dot(readout, start_low) * early_wide
    ssd = jnp.concatenate(within, axis=1) + carried + rows_ref[0:1] * signal_wide
    tail = (signal_wide * tail_wide).astype(bf16)
    state[...] = start * early_wide[GROUP - 1 :] + dot_tn(entry, tail)

    gate_act, gate_slope = silu_slope(projected[:, :width])
    gate_act_ref[...] = gate_act.astype(bf16)
    gate_slope_ref[...] = gate_slope.astype(bf16)
    ssd_ref[...] = ssd
    gated = ssd * gate_act
    scaled = (gated * rows_ref[1:2]).astype(bf16)
    scaled_ref[...] = scaled
    square_ref[0] = sum_lanes(gated * gated)
    placed[slot] = scaled
    where = in_time(place_ref[0], turn)
    store(placed.at[slot], targets, scatter_places(count), where, out_semaphores.at[slot])

    @pl.when(turn == pl.num_programs(0) - 1)
    def _():
        for other in range(2):
            stored(placed, targets, out_semaphores, other)


def time_estimate(microseconds, accessed):
    return pl.CostEstimate(
        flops=int(microseconds * 1.1e9), bytes_accessed=int(accessed), transcendentals=0
    )


def fixed(shape):
    return pl.BlockSpec(shape, lambda turn, place: (0,) * len(shape), pipeline_mode=pl.Buffered(1))


def anywhere(values):
    return [pl.BlockSpec(memory_space=pltpu.HBM)] * len(values)


def run_forward(place, pieces, params, dims):
    heads, size, states, count = dims
    arrays, table = pieces
    dim = params[0].shape[0]
    width, conv_cols = heads * size, params[1].shape[1]
    blocks = len(table)
    tokens = blocks * GROUP

    def moving(columns):
        return pl.BlockSpec((GROUP, columns), lambda turn, place: (turn, 0))

    def rows_of_block(height, columns):
        return pl.BlockSpec((1, height, columns), lambda turn, place: (turn, 0, 0))

    results = pl.pallas_call(
        functools.partial(forward_kernel, dims, table, len(arrays)),
        grid_spec=pltpu.PrefetchScalarGridSpec(
            num_scalar_prefetch=1,
            grid=(blocks,),
            in_specs=[*anywhere(arrays), *[fixed(param.shape) for param in params]],
            out_specs=[
                moving(conv_cols),
                moving(conv_cols),
                moving(conv_cols),
                moving(width),
                moving(width),
                rows_of_block(8, GROUP),
                moving(width),
                rows_of_block(states, width),
                moving(width),
                rows_of_block(8, GROUP),
                moving(dim),
                *anywhere(range(4)),
            ],
            scratch_shapes=[
                pltpu.VMEM((states, width), f32),
                pltpu.VMEM((HALO + GROUP, conv_cols), f32),
                pltpu.VMEM((GROUP, GROUP), bf16),
                pltpu.VMEM((HALF, HALF), f32),
                pltpu.VMEM((2, GROUP, dim), bf16),
                pltpu.SemaphoreType.DMA((2,)),
                pltpu.VMEM((2, GROUP, width), bf16),
                pltpu.SemaphoreType.DMA((2,)),
            ],
        ),
        out_shape=[
            jax.ShapeDtypeStruct((tokens, conv_cols), bf16),
            jax.ShapeDtypeStruct((tokens, conv_cols), bf16),
            jax.ShapeDtypeStruct((tokens, conv_cols), bf16),
            jax.ShapeDtypeStruct((tokens, width), bf16),
            jax.ShapeDtypeStruct((tokens, width), bf16),
            jax.ShapeDtypeStruct((blocks, 8, GROUP), f32),
            jax.ShapeDtypeStruct((tokens, width), f32),
            jax.ShapeDtypeStruct((blocks, states, width), bf16),
            jax.ShapeDtypeStruct((tokens, width), bf16),
            jax.ShapeDtypeStruct((blocks, 8, GROUP), f32),
            jax.ShapeDtypeStruct((tokens, dim), bf16),
            *scatter_shapes(count, width),
        ],
        compiler_params=pltpu.CompilerParams(vmem_limit_bytes=60 * MIB),
        cost_estimate=time_estimate(blocks * 3.0, tokens * (4 * dim + 24 * width)),
        name="forward_blocks",
    )(place, *arrays, *params)
    return results[:11], results[11:]


def backward_kernel(dims, place_ref, *refs):
    heads, size, states, count = dims
    width = heads * size
    conv_cols = width + 2 * states
    conv_in_ref, active_ref, slope_ref, gate_act_ref, gate_slope_ref = refs[:5]
    raw_ref, ssd_ref, start_ref, out_grad_ref, norm_ref = refs[5:10]
    conv_w_ref, step_ref, rows_ref = refs[10:13]
    out_ref, targets = refs[13], refs[14:18]
    sums = refs[18:24]
    gain_ref, skip_ref, conv_wg_ref, conv_bg_ref, bias_ref, rate_ref = sums
    state, pre_grads, order, back_order, barred, placed, semaphores = refs[24:]
    taps = conv_w_ref.shape[0]
    turn = pl.program_id(0)
    slot = lax.rem(turn, 2)

    @pl.when(turn >= 2)
    def _():
        stored(placed, targets, semaphores, slot)

    @pl.when(pl.program_id(0) == 0)
    def _():
        state[...] = jnp.zeros_like(state)
        pre_grads[0:HALO] = jnp.zeros_like(pre_grads[0:HALO])
        for total in sums:
            total[...] = jnp.zeros_like(total)
        row, column = order_indices(GROUP)
        order[...] = ones_where(row <= column)
        back_order[...] = ones_where(row >= column)
        row, column = order_indices(HALF)
        barred[...] = jnp.where(row <= column, 0.0, -1e30)

    gate_act, ssd, out_grad = gate_act_ref[...].astype(f32), ssd_ref[...], out_grad_ref[...]
    norms = norm_ref[0].T
    scale, slope = norms[:, 0:1], norms[:, 1:2]
    gated = ssd * gate_act
    gain_ref[...] += jnp.sum(out_grad * (gated * scale), axis=0, keepdims=True)
    gated_grad = out_grad * (rows_ref[1:2] * scale) - gated * slope
    grad_low = (gated_grad * gate_act).astype(bf16)
    gate_grad = (gated_grad * ssd * gate_slope_ref[...].astype(f32)).astype(bf16)
    out_ref[:, :width] = gate_grad
    placed[slot, :, :width] = gate_grad
    ssd_grad = grad_low.astype(f32)

    raw = raw_ref[0] + step_ref[0:8, 0:1]
    rate = step_ref[8:16, 0:1]
    step, sig, log_step, ratio = step_values(raw)
    decay = step * rate
    running = sum_along(decay, order[...])
    later = running - log_step
    total = running[:, GROUP - 1 :]
    columns = to_columns([later * LOG2E, jnp.exp(running), jnp.exp(total - later)])
    running = running * LOG2E
    early_wide = spread_heads(columns, 8, heads, size)
    tail_wide = spread_heads(columns, 16, heads, size)

    signal = active_ref[:, :width]
    entry = active_ref[:, width : width + states]
    readout = active_ref[:, width + states :]
    signal_wide = signal.astype(f32)
    start_low = start_ref[0]
    end_grad = state[...]
    end_low = end_grad.astype(bf16)
    first, second = slice(0, HALF), slice(HALF, GROUP)
    scores = dot_nt(entry[first], readout)
    later_scores = dot_nt(entry[second], readout[second])
    near_grad, far_grad, last_grad = 0.0, 0.0, 0.0
    within = []
    for h in range(heads):
        part, grad = signal[:, h * size : (h + 1) * size], grad_low[:, h * size : (h + 1) * size]
        begin, end = columns[first, h : h + 1], columns[second, h : h + 1]
        row_first, row_second = running[h : h + 1, first], running[h : h + 1, second]
        near = jnp.exp2(row_first - begin + barred[...])
        full = jnp.exp2(row_second - begin)
        last = jnp.exp2(row_second - end + barred[...])
        both = jnp.concatenate(
            [
                (near * scores[:, first]).astype(bf16),
                (full * scores[:, second]).astype(bf16),
            ],
            axis=1,
        )
        final = (last * later_scores).astype(bf16)
        within.append(jnp.concatenate([dot(both, grad), dot(final, grad[second])], axis=0))
        cross = dot_nt(part[first], grad)
        near_grad = near_grad + cross[:, first] * near
        far_grad = far_grad + cross[:, second] * full
        last_grad = last_grad + dot_nt(part[second], grad[second]) * last
    tail_grad = tail_wide * dot(entry, end_low)
    signal_grad = jnp.concatenate(within, axis=1) + tail_grad
    score_first = jnp.concatenate([near_grad, far_grad], axis=1).astype(bf16)
    score_second = last_grad.astype(bf16)
    tail = (signal_wide * tail_wide).astype(bf16)
    head_grad = (ssd_grad * early_wide).astype(bf16)
    entry_grad = jnp.concatenate(
        [dot(score_first, readout), dot(score_second, readout[second])], axis=0
    ) + dot_nt(tail, end_low)
    readout_grad = dot_tn(score_first, entry[first]) + dot_nt(head_grad, start_low)
    readout_last = readout_grad[second] + dot_tn(score_second, entry[second])
    total_wide = early_wide[GROUP - 1 :]
    state[...] = end_grad * total_wide + dot_tn(readout, head_grad)

    skip = rows_ref[0:1]
    ones = head_ones(width, size)
    column_part = signal_wide * signal_grad
    row_part = ssd_grad * (ssd - skip * signal_wide)
    end_part = jnp.sum(signal_wide * tail_grad, axis=0, keepdims=True) + total_wide * jnp.sum(
        start_low.astype(f32) * end_grad, axis=0, keepdims=True
    )

    def head_sums(value, parts):
        return sum(dot_nt(ones, part) for part in split_parts(value, parts))

    end_rows = head_sums(jnp.broadcast_to(end_part, (8, width)), 2)[:, 0:1]
    decay_grad = sum_along(head_sums(row_part - column_part, 2), back_order[...]) + end_rows
    raw_grad = head_sums(column_part, 1) * ratio + decay_grad * rate * sig
    skip_ref[...] += jnp.sum(ssd_grad * signal_wide, axis=0, keepdims=True)
    bias_ref[...] += raw_grad
    rate_ref[...] += decay_grad * decay
    raw_low = to_columns([raw_grad]).astype(bf16)
    out_ref[:, width + conv_cols :] = raw_low
    placed[slot, :, width + conv_cols :] = raw_low

    pre_grads[GROUP : GROUP + HALO] = pre_grads[0:HALO]
    pre_grads[0:GROUP, :width] = (signal_grad + skip * ssd_grad) * slope_ref[:, :width].astype(f32)
    sides = slope_ref[:, width:].astype(f32)
    pre_grads[0:GROUP, width : width + states] = entry_grad * sides[:, :states]
    pre_grads[0:HALF, width + states :] = readout_grad[first] * sides[first, states:]
    pre_grads[HALF:GROUP, width + states :] = readout_last * sides[second, states:]
    conv_w = conv_w_ref[...]
    conv_in = conv_in_ref[...].astype(f32)
    conv_grad = 0.0
    for k in range(taps):
        ahead = taps - 1 - k
        shifted = pre_grads[ahead : ahead + GROUP]
        conv_grad = conv_grad + conv_w[k : k + 1] * shifted
        conv_wg_ref[k : k + 1] += jnp.sum(shifted * conv_in, axis=0, keepdims=True)
        if ahead == 0:
            conv_bg_ref[...] += jnp.sum(shifted, axis=0, keepdims=True)
    conv_low = conv_grad.astype(bf16)
    out_ref[:, width : width + conv_cols] = conv_low
    placed[slot, :, width : width + conv_cols] = conv_low

    where = in_time(place_ref[0], pl.num_programs(0) - 1 - turn)
    store(placed.at[slot], targets, scatter_places(count), where, semaphores.at[slot])

    @pl.when(turn == pl.num_programs(0) - 1)
    def _():
        for other in range(2):
            stored(placed, targets, semaphores, other)


def run_backward(place, values, params, dims):
    heads, size, states, count = dims
    conv_cols, width = values[0].shape[1], heads * size
    tokens = values[0].shape[0]
    blocks = tokens // GROUP
    last = blocks - 1
    out_cols = width + conv_cols + LANES

    def moving(columns):
        return pl.BlockSpec((GROUP, columns), lambda turn, place: (last - turn, 0))

    def rows_of_block():
        return pl.BlockSpec((1, 8, GROUP), lambda turn, place: (last - turn, 0, 0))

    sums = [(1, width), (1, width), params[0].shape, (1, conv_cols), (8, GROUP), (8, GROUP)]
    return pl.pallas_call(
        functools.partial(backward_kernel, dims),
        grid_spec=pltpu.PrefetchScalarGridSpec(
            num_scalar_prefetch=1,
            grid=(blocks,),
            in_specs=[
                moving(conv_cols),
                moving(conv_cols),
                moving(conv_cols),
                moving(width),
                moving(width),
                rows_of_block(),
                moving(width),
                pl.BlockSpec((1, states, width), lambda turn, place: (last - turn, 0, 0)),
                moving(width),
                rows_of_block(),
                *[fixed(param.shape) for param in params],
            ],
            out_specs=[
                moving(out_cols),
                *anywhere(range(4)),
                *[fixed(shape) for shape in sums],
            ],
            scratch_shapes=[
                pltpu.VMEM((states, width), f32),
                pltpu.VMEM((GROUP + HALO, conv_cols), f32),
                pltpu.VMEM((GROUP, GROUP), bf16),
                pltpu.VMEM((GROUP, GROUP), bf16),
                pltpu.VMEM((HALF, HALF), f32),
                pltpu.VMEM((2, GROUP, out_cols), bf16),
                pltpu.SemaphoreType.DMA((2,)),
            ],
        ),
        out_shape=[
            jax.ShapeDtypeStruct((tokens, out_cols), bf16),
            *scatter_shapes(count, out_cols),
        ]
        + [jax.ShapeDtypeStruct(shape, f32) for shape in sums],
        compiler_params=pltpu.CompilerParams(vmem_limit_bytes=60 * MIB),
        cost_estimate=time_estimate(blocks * 3.5, tokens * 40 * width),
        name="backward_blocks",
    )(place, *values, *params)


def widen_kernel(place_ref, piece_ref, out_ref):
    out_ref[...] = piece_ref[0].astype(f32)


def assemble_out(place, pieces, per):
    count, size, dim = pieces.shape
    groups = count // per

    def source(turn, place):
        relative = (turn % groups * per + turn // groups) ^ place[0]
        return ((relative & 1) * (count // 2) + (relative >> 1), 0, 0)

    return pl.pallas_call(
        widen_kernel,
        grid_spec=pltpu.PrefetchScalarGridSpec(
            num_scalar_prefetch=1,
            grid=(count,),
            in_specs=[pl.BlockSpec((1, size, dim), source)],
            out_specs=pl.BlockSpec((size, dim), lambda turn, place: (turn, 0)),
        ),
        out_shape=jax.ShapeDtypeStruct((count * size, dim), f32),
        cost_estimate=time_estimate(5, count * size * dim * 6),
        name="assemble_out_weight_grad",
    )(place, pieces)


def assemble_kernel(dims, tables, given, place_ref, *refs):
    heads, size, states, count = dims
    width, shared = heads * size, 2 * states
    inner = count * width
    mains, sides, out_ref, sums = refs[: given[0]], refs[given[0] : given[1]], refs[-2], refs[-1]

    def piece(arrays, table, relative):
        parts = []
        for half in range(2):
            array, row, height = table[half, relative]
            parts.append(arrays[array][row : row + height].astype(f32))
        return jnp.concatenate(parts, axis=0).T

    for relative in range(count):
        device = place_ref[0] ^ relative
        columns = piece(mains, tables[0], relative)
        out_ref[pl.ds(pl.multiple_of(device * width, 8), width)] = columns[:width]
        middle = pl.multiple_of(inner + device * width, 8)
        out_ref[pl.ds(middle, width)] = columns[width:]
        sums[device] = piece(sides, tables[1], relative)[: shared + STEP_ROWS]
    total = sums[0, :shared]
    for device in range(1, count):
        total = total + sums[device, :shared]
    out_ref[2 * inner : 2 * inner + shared] = total
    for device in range(count):
        last = 2 * inner + shared + device * heads
        out_ref[last : last + heads] = sums[device, shared : shared + heads]


def assemble(place, mains, sides, dims):
    heads, size, states, count = dims
    mains, main_table = gathered(mains)
    sides, side_table = gathered(sides)
    rows = sum(main_table[half, 0][2] for half in range(2))
    out_rows = 2 * count * heads * size + 2 * states + count * heads

    def whole(value):
        return pl.BlockSpec(
            value.shape,
            lambda turn, place: (0,) * len(value.shape),
            pipeline_mode=pl.Buffered(1),
        )

    return pl.pallas_call(
        functools.partial(
            assemble_kernel, dims, (main_table, side_table), (len(mains), len(mains) + len(sides))
        ),
        grid_spec=pltpu.PrefetchScalarGridSpec(
            num_scalar_prefetch=1,
            grid=(1,),
            in_specs=[whole(value) for value in (*mains, *sides)],
            out_specs=pl.BlockSpec(
                (out_rows, rows), lambda turn, place: (0, 0), pipeline_mode=pl.Buffered(1)
            ),
            scratch_shapes=[pltpu.VMEM((count, 2 * states + STEP_ROWS, rows), f32)],
        ),
        out_shape=jax.ShapeDtypeStruct((out_rows, rows), f32),
        compiler_params=pltpu.CompilerParams(vmem_limit_bytes=60 * MIB),
        cost_estimate=time_estimate(8, out_rows * rows * 6),
        name="assemble_in_weight_grad",
    )(place, *mains, *sides)


def body(
    tokens,
    norm_gain,
    in_weight,
    conv_weight,
    conv_bias,
    dt_bias,
    decay_log,
    skip_scale,
    gate_gain,
    out_weight,
    cotangent,
):
    count, mine = lax.axis_size("seq"), lax.axis_index("seq")
    planes = lax.axis_size("batch")
    place = mine.astype(jnp.int32).reshape(1)
    inner, all_heads, conv_all = gate_gain.shape[0], dt_bias.shape[0], conv_bias.shape[0]
    size, states = inner // all_heads, (conv_all - inner) // 2
    heads, width = all_heads // count, inner // count
    dims = (heads, size, states, count)
    shared = 2 * states
    conv_cols = width + shared
    tok_rows = tokens.shape[1]
    per_plane = out_weight.shape[0] // width

    def own(vector, per, first=0):
        return lax.dynamic_slice_in_dim(vector, first + mine * per, per, vector.ndim - 1)

    def own_conv(array, first=0):
        return jnp.concatenate(
            [own(array, width, first), array[..., first + inner : first + conv_all]], axis=-1
        )

    tokens_row = tokens[0].astype(f32)
    inverse = lax.rsqrt(jnp.mean(tokens_row * tokens_row, axis=-1, keepdims=True) + epsilon)
    normed_own = (tokens_row * inverse * norm_gain).astype(bf16)
    step_own = own(in_weight, heads, inner + conv_all)
    w_own = jnp.concatenate(
        [
            own(in_weight, width),
            own_conv(in_weight, inner),
            jnp.pad(step_own, ((0, 0), (0, LANES - heads))),
        ],
        axis=1,
    )
    w_cols = lax.all_gather(w_own, "batch", axis=0, tiled=True)
    stages = gather_stages()
    held = gather_stage(gather_stage(gather_start(normed_own), 0), 1)
    held, out_owned = together(held, out_weight)
    out_rows = rows_from_owner(out_owned, width, range(planes))
    for stage in range(2, stages):
        held = gather_stage(held, stage)
    w_cols, held, cot_own = together(w_cols, held, cotangent[0])
    cot = lax.all_gather(cot_own, "seq", axis=0, tiled=True)
    out_rows = rows_joined(out_rows)

    conv_w, conv_b = own_conv(conv_weight), own_conv(conv_bias)[None]
    per_head = jnp.stack([own(dt_bias, heads), -jnp.exp(own(decay_log, heads))])
    per_head = jnp.pad(per_head, ((0, 0), (0, 8 - heads))).reshape(16, 1)
    step_rows = jnp.broadcast_to(per_head, (16, LANES))
    gain_own = own(gate_gain, width)[None]
    rows = jnp.concatenate(
        [jnp.repeat(own(skip_scale, heads), size)[None], gain_own, jnp.zeros((6, width), f32)],
        axis=0,
    )
    results, out_parts = run_forward(
        place, token_pieces(held), (w_cols, conv_w, conv_b, step_rows, rows), dims
    )
    conv_in, active, slope, gate_act, gate_slope, raw, ssd, starts, scaled, squares, normed = results

    def out_product(part):
        return dot(part, out_rows)

    out_send = out_product(out_parts[0]).astype(bf16)
    out_ready, out_held = scatter_near(out_product, out_parts[1:], out_send)
    out_ready, out_held, cot = together(out_ready, out_held, cot)
    out_grad = jnp.einsum("td,ed->te", cot, out_rows, preferred_element_type=f32)
    slopes = jnp.sum(out_grad * scaled.astype(f32), axis=1)
    sums = sum_seq(jnp.stack([squares[:, 0].reshape(-1), slopes]))
    scale = lax.rsqrt(sums[0] / inner + epsilon)
    norms = jnp.stack([scale, scale * scale * scale * sums[1] / inner])
    norms = jnp.pad(norms, ((0, 6), (0, 0))).reshape(8, -1, GROUP).swapaxes(0, 1)
    scaled_cot = (cot.astype(f32) * scale[:, None]).astype(bf16)
    out_term = jnp.einsum("te,td->ed", scaled, scaled_cot, preferred_element_type=f32)
    out_term, norms, out_ready = together(out_term.astype(bf16), norms, out_ready)
    out_sum = lax.psum_scatter(out_term, "batch", scatter_dimension=0, tiled=True)
    out_ready, out_held = scatter_far(out_ready, out_held, 0)

    values = (conv_in, active, slope, gate_act, gate_slope, raw, ssd, starts, out_grad, norms)
    results = run_backward(place, values, (conv_w, step_rows, rows), dims)
    proj_grad, back_parts = results[0], results[1:5]
    gain_term, skip_term, conv_w_term, conv_b_term, bias_term, rate_term = results[5:]
    proj_grad, back_parts, out_ready, out_held, out_sum = together(
        proj_grad, back_parts, out_ready, out_held, out_sum
    )

    def back_product(part):
        return jnp.einsum("tf,df->td", part, w_cols, preferred_element_type=f32)

    def weight_product(part):
        return jnp.einsum("td,tf->df", normed, part, preferred_element_type=f32).astype(bf16)

    for stage in range(1, stages - 1):
        out_ready, out_held = scatter_far(out_ready, out_held, stage)
    back_send = back_product(back_parts[0]).astype(bf16)
    back_send, proj_grad = together(back_send, proj_grad)
    main_term = weight_product(proj_grad[:, : 2 * width])
    main_term, keeps, out_held = together(main_term, back_parts[1:], out_held)
    main_sum = lax.psum_scatter(main_term, "batch", scatter_dimension=0, tiled=True)
    back_ready, back_held = scatter_near(back_product, keeps, back_send)
    back_ready, proj_grad, main_term, out_sum = together(back_ready, proj_grad, main_term, out_sum)
    back_ready, back_held = scatter_far(back_ready, back_held, 0)
    out_pieces = to_owner(out_sum)[None]
    side_term = weight_product(proj_grad[:, 2 * width :])
    side_sum = lax.psum_scatter(side_term, "batch", scatter_dimension=0, tiled=True)

    norm_gain_term = jnp.sum(main_term.astype(f32) * w_cols[:, : 2 * width].astype(f32), axis=1)
    norm_gain_term += jnp.sum(side_term.astype(f32) * w_cols[:, 2 * width :].astype(f32), axis=1)
    norm_gain_term /= norm_gain

    def among_heads(vector, per, total):
        return lax.dynamic_update_slice_in_dim(jnp.zeros((total,), f32), vector, mine * per, 0)

    def among_conv(array):
        wide = jnp.zeros((array.shape[0], inner), f32)
        wide = lax.dynamic_update_slice_in_dim(wide, array[:, :width], mine * width, 1)
        return jnp.concatenate([wide, array[:, width:]], axis=1).reshape(-1)

    skip_heads = jnp.sum(skip_term.reshape(heads, size), axis=1)
    terms = [
        norm_gain_term,
        among_conv(conv_w_term),
        among_conv(conv_b_term),
        among_heads(jnp.sum(bias_term[:heads], axis=1), heads, all_heads),
        among_heads(jnp.sum(rate_term[:heads], axis=1), heads, all_heads),
        among_heads(skip_heads, heads, all_heads),
        among_heads(gain_term[0], width, inner),
    ]
    vector = jnp.concatenate(terms)
    padding = -vector.shape[0] % (8 * LANES)
    vector = jnp.pad(vector, (0, padding)).reshape(-1, LANES)

    axes = [(axis, bit) for axis in ("seq", "batch") for bit in bits_of(lax.axis_size(axis))]
    back_ready, main_sum, vector, out_pieces = together(back_ready, main_sum, vector, out_pieces)
    for stage in range(1, stages - 1):
        back_ready, back_held = scatter_far(back_ready, back_held, stage)
    mains = gather_stage(gather_start(main_sum), 0)
    vector = vector + exchange(vector, *axes.pop(0))
    back_held["arrived"], mains, side_sum, vector, out_pieces = together(
        back_held["arrived"], mains, side_sum, vector, out_pieces
    )
    sides = gather_start(side_sum)
    for stage in range(1, stages):
        mains = gather_stage(mains, stage, late=True)
        sides = gather_stage(sides, stage - 1, late=True)
        out_pieces = double(out_pieces, stage - 1)
        vector = vector + exchange(vector, *axes.pop(0))
        mains, sides, vector, out_pieces = together(mains, sides, vector, out_pieces)
    sides = gather_stage(sides, stages - 1, late=True)
    out_pieces = double(out_pieces, stages - 1)
    vector = vector + exchange(vector, *axes.pop(0))
    normed_grad = scatter_end(back_held)
    cot_row = cotangent[0].astype(f32)
    gained = norm_gain * normed_grad
    slope = inverse * inverse * inverse * jnp.mean(gained * tokens_row, axis=-1, keepdims=True)
    input_grad = cot_row + inverse * gained - tokens_row * slope
    own_scale = lax.dynamic_slice_in_dim(scale, mine * tok_rows, tok_rows, 0)[:, None]
    block_out = (tokens_row + own_scale * scatter_end(out_held)).astype(bf16)
    in_weight_grad = assemble(place, mains, sides, dims).T
    out_weight_grad = assemble_out(place, out_pieces, per_plane)
    while axes:
        vector = vector + exchange(vector, *axes.pop(0))
    vector = vector.reshape(-1)

    parts, offset = [], 0
    for term in terms:
        parts.append(vector[offset : offset + term.shape[0]])
        offset += term.shape[0]
    return (
        block_out[None],
        input_grad[None],
        parts[0],
        in_weight_grad,
        parts[1].reshape(conv_weight.shape),
        parts[2],
        parts[3],
        parts[4],
        parts[5],
        parts[6],
        out_weight_grad,
    )


def solution(mesh):
    placed = (
        P("batch", "seq", None),
        P(),
        P("batch", None),
        P(),
        P(),
        P(),
        P(),
        P(),
        P(),
        P("batch", None),
        P("batch", "seq", None),
    )
    return jax.shard_map(
        body,
        mesh=mesh,
        in_specs=placed,
        out_specs=(
            P("batch", "seq", None),
            P("batch", "seq", None),
            P(),
            P("batch", None),
            P(),
            P(),
            P(),
            P(),
            P(),
            P(),
            P("batch", None),
        ),
        check_vma=False,
    )
```

```python
import functools

import jax
import jax.numpy as jnp
from jax import lax
from jax.experimental import pallas as pl
from jax.experimental.pallas import tpu as pltpu
from jax.sharding import PartitionSpec as P

GROUP = 256
LANES = 128
HALF = GROUP // 2
HALO = 8
STEP_ROWS = 16
LOG2E = 1.4426950408889634
epsilon = 1e-05
f32 = jnp.float32
bf16 = jnp.bfloat16
MIB = 2**20


def exchange(value, axis, distance):
    count = lax.axis_size(axis)
    return lax.ppermute(value, axis, [(source, source ^ distance) for source in range(count)])


def bits_of(count):
    return [1 << k for k in range(count.bit_length() - 1)]


def placed_order(count):
    return [2 * k for k in range(count // 2)] + [2 * k + 1 for k in range(count // 2)]


def together(*values):
    return lax.optimization_barrier(values)


def far_orders():
    far = bits_of(lax.axis_size("seq"))[1:]
    return far, far[::-1]


def gather_start(value):
    half = value.shape[0] // 32 * 16
    return tuple({"base": part, "fresh": None, "near": []} for part in (value[:half], value[half:]))


def gather_stage(held, stage, late=False):
    grown = []
    for half, order in zip(held, far_orders()):
        base, fresh, near = half["base"], half["fresh"], list(half["near"])
        if stage >= 1:
            merged = base if stage == len(order) else jnp.concatenate([base, fresh], axis=0)
            if not late:
                near.append(exchange(merged if stage == 1 else fresh, "seq", 1))
            elif stage == len(order):
                near = [exchange(base, "seq", 1), exchange(fresh, "seq", 1)]
            base = merged
        if stage < len(order):
            fresh = exchange(base, "seq", order[stage])
        grown.append({"base": base, "fresh": fresh, "near": near})
    return tuple(grown)


def gather_stages():
    return len(bits_of(lax.axis_size("seq")))


def gathered(held):
    arrays, table = [], {}
    for number, (half, order) in enumerate(zip(held, far_orders())):
        indices = [0]
        for bit in order:
            indices += [index | bit for index in indices]
        middle = len(indices) // 2
        groups = [(half["base"], indices[:middle]), (half["fresh"], indices[middle:])]
        bounds = [0] + [2 << k for k in range(len(order))]
        if len(half["near"]) < len(order):
            bounds = [0, middle, len(indices)]
        for value, first, last in zip(half["near"], bounds, bounds[1:]):
            groups.append((value, [index | 1 for index in indices[first:last]]))
        for value, members in groups:
            rows = value.shape[0] // len(members)
            for turn, index in enumerate(members):
                table[number, index] = (len(arrays), turn * rows, rows)
            arrays.append(value)
    return arrays, table


def token_pieces(held):
    arrays, table = gathered(held)
    indices = range(lax.axis_size("seq"))
    return arrays, tuple(table[half, index] for index in indices for half in range(2))


def gather_all(value):
    held = gather_start(value)
    for stage in range(gather_stages()):
        held = gather_stage(held, stage)
    return held


def scatter_places(count):
    far = bits_of(count)[1:]
    table = {}
    row = {}
    for near in (1, 0):
        for sent in (True, False):
            for half, order in enumerate((far, far[::-1])):
                members = [0]
                for bit in order[:0:-1]:
                    members += [member | bit for member in members]
                for member in members:
                    index = member | near | (order[0] if sent else 0)
                    array = 0 if near else (1 + half if sent else 3)
                    table[index * 2 + half] = (array, row.get(array, 0))
                    row[array] = row.get(array, 0) + GROUP
    return tuple(table[k] for k in range(2 * count))


def scatter_shapes(count, columns):
    blocks = (count, count // 4, count // 4, count // 2)
    return [jax.ShapeDtypeStruct((part * GROUP, columns), bf16) for part in blocks]


def scatter_near(product, parts, sent):
    arriving = exchange(sent, "seq", 1)
    first, second, kept = parts
    rows = first.shape[0]

    def summed(part, row):
        return (product(part) + arriving[row : row + part.shape[0]].astype(f32)).astype(bf16)

    sends = (summed(first, 0), summed(second, rows))
    sends, kept = together(sends, kept)
    return sends, {"kept": summed(kept, 2 * rows), "arrived": ([], [])}


def scatter_rows(held, half, first, last):
    top = half * (held["kept"].shape[0] // 2)
    total = held["kept"][top + first : top + last].astype(f32)
    for value in held["arrived"][half]:
        total = total + value[first:last].astype(f32)
    return total


def scatter_far(sends, held, stage):
    orders = far_orders()
    arrived = tuple(
        [*held["arrived"][half], exchange(sends[half], "seq", orders[half][stage])]
        for half in range(2)
    )
    held = {"kept": held["kept"], "arrived": arrived}
    rows = sends[0].shape[0]
    if stage + 1 == len(orders[0]):
        return (), held
    ready = tuple(
        scatter_rows(held, half, rows // 2, rows).astype(bf16) for half in range(2)
    )
    return ready, held


def scatter_end(held):
    rows = held["arrived"][0][-1].shape[0]
    return jnp.concatenate([scatter_rows(held, half, 0, rows) for half in range(2)], axis=0)


def sum_seq(value):
    for bit in bits_of(lax.axis_size("seq")):
        value = value + exchange(value, "seq", bit)
    return value


def plane_pairs(ahead):
    planes, count = lax.axis_size("batch"), lax.axis_size("seq")
    per = count // planes
    pairs = []
    for owner in range(planes):
        for piece in range(planes):
            for k in range(per):
                holder = owner * count + piece * per + k
                user = (piece + ahead) % planes * count + owner * per + k
                pairs.append((holder, user))
    return pairs


def rows_from_owner(out_weight, width):
    planes, count = lax.axis_size("batch"), lax.axis_size("seq")
    per = count // planes
    plane, mine = lax.axis_index("batch"), lax.axis_index("seq")
    owner = mine // per
    rows = lax.dynamic_slice_in_dim(out_weight, mine % per * width, width, 0)
    result = rows
    for ahead in range(1, planes):
        pairs = [
            (index // per * count + index, (index // per + ahead) % planes * count + index)
            for index in range(count)
        ]
        arriving = lax.ppermute(rows, ("batch", "seq"), pairs)
        result = jnp.where((owner + ahead) % planes == plane, arriving, result)
    return result


def to_owner(summed):
    return lax.ppermute(
        summed, ("batch", "seq"), [(user, holder) for holder, user in plane_pairs(0)]
    )


def double(held, turn):
    bits = bits_of(lax.axis_size("seq"))
    return jnp.concatenate([held, exchange(held, "seq", (bits[1:] + [1])[turn])], axis=0)


def step_values(raw):
    small = jnp.exp(-jnp.abs(raw))
    step = jnp.maximum(raw, 0.0) + jnp.log1p(small)
    sig = jnp.where(raw >= 0, 1.0, small) / (1.0 + small)
    tiny = raw < -20.0
    log_step = jnp.where(tiny, raw, jnp.log(step))
    ratio = jnp.where(tiny, 1.0, sig / step)
    return step, sig, log_step, ratio


def dot(a, b):
    return jnp.dot(a, b, preferred_element_type=f32)


def dot_nt(a, b):
    return lax.dot_general(a, b, (((1,), (1,)), ((), ())), preferred_element_type=f32)


def dot_tn(a, b):
    return lax.dot_general(a, b, (((0,), (0,)), ((), ())), preferred_element_type=f32)


def sigmoid(value):
    return 0.5 * jnp.tanh(0.5 * value) + 0.5


def silu_slope(value):
    sig = sigmoid(value)
    active = value * sig
    return active, sig + active * (1.0 - sig)


def split_parts(value, count):
    parts = []
    for _ in range(count):
        part = value.astype(bf16)
        parts.append(part)
        value = value - part.astype(f32)
    return parts


def sum_along(rows, order):
    parts = jnp.concatenate([part.astype(f32) for part in split_parts(rows, 3)], axis=0)
    total = dot(parts.astype(bf16), order)
    return total[:8] + total[8:16] + total[16:24]


def to_columns(rows):
    stacked = jnp.concatenate(rows, axis=0)
    missing = LANES - stacked.shape[0]
    return jnp.concatenate([stacked, jnp.zeros((missing, GROUP), f32)], axis=0).T


def spread_heads(value, first, heads, size):
    rows = value.shape[0]
    return jnp.concatenate(
        [jnp.broadcast_to(value[:, first + h : first + h + 1], (rows, size)) for h in range(heads)],
        axis=1,
    )


def head_ones(width, size):
    row = lax.broadcasted_iota(jnp.int32, (8, width), 0)
    column = lax.broadcasted_iota(jnp.int32, (8, width), 1)
    return (column // size == row).astype(f32).astype(bf16)


def sum_lanes(value):
    return dot_nt(jnp.ones((8, value.shape[1]), bf16), value.astype(bf16))


def ones_where(condition):
    return jnp.where(condition, 1.0, 0.0).astype(bf16)


def order_indices(length):
    row = lax.broadcasted_iota(jnp.int32, (length, length), 0)
    column = lax.broadcasted_iota(jnp.int32, (length, length), 1)
    return row, column


def fetch(arrays, table, which, target, semaphore):
    for index, (array, row, rows) in enumerate(table):

        @pl.when(which == index)
        def _():
            pltpu.make_async_copy(arrays[array].at[pl.ds(row, rows)], target, semaphore).start()


def fetched(arrays, table, buffer, semaphores, order, blocks=1):
    step = pl.program_id(0)
    slot, other = lax.rem(step, 2), lax.rem(step + 1, 2)

    def start(step, slot):
        for k in range(blocks):
            target = buffer.at[slot, pl.ds(k * GROUP, GROUP)]
            fetch(arrays, table, order(step * blocks + k), target, semaphores.at[slot])

    @pl.when(step == 0)
    def _():
        start(0, 0)

    @pl.when(step + 1 < pl.num_programs(0))
    def _():
        start(step + 1, other)

    for k in range(blocks):
        source = arrays[0].at[pl.ds(0, GROUP)]
        target = buffer.at[slot, pl.ds(k * GROUP, GROUP)]
        pltpu.make_async_copy(source, target, semaphores.at[slot]).wait()
    return buffer[slot]


def store(source, targets, table, which, semaphore):
    for index, (array, row) in enumerate(table):

        @pl.when(which == index)
        def _():
            target = targets[array].at[pl.ds(row, GROUP)]
            pltpu.make_async_copy(source, target, semaphore).start()


def stored(buffer, targets, semaphores, slot):
    target = targets[0].at[pl.ds(0, GROUP)]
    pltpu.make_async_copy(buffer.at[slot], target, semaphores.at[slot]).wait()


def in_time(place, block):
    return ((block // 2) ^ place) * 2 + block % 2


def forward_kernel(dims, table, given, place_ref, *refs):
    heads, size, states, count = dims
    width = heads * size
    conv_cols = width + 2 * states
    arrays, refs = refs[:given], refs[given:]
    w_ref, conv_w_ref, conv_b_ref, step_ref, rows_ref = refs[:5]
    conv_in_ref, active_ref, slope_ref, gate_act_ref, gate_slope_ref = refs[5:10]
    raw_ref, ssd_ref, start_ref, scaled_ref, square_ref, normed_ref = refs[10:16]
    targets = refs[16:20]
    state, padded, order, barred, buffer, semaphores, placed, out_semaphores = refs[20:]
    turn = pl.program_id(0)
    slot = lax.rem(turn, 2)

    @pl.when(turn == 0)
    def _():
        state[...] = jnp.zeros_like(state)
        padded[0:HALO] = jnp.zeros_like(padded[0:HALO])
        row, column = order_indices(GROUP)
        order[...] = ones_where(row <= column)
        row, column = order_indices(HALF)
        barred[...] = jnp.where(row >= column, 0.0, -1e30)

    @pl.when(turn >= 2)
    def _():
        stored(placed, targets, out_semaphores, slot)

    normed = fetched(
        arrays, table, buffer, semaphores, lambda step: in_time(place_ref[0], step)
    )
    normed_ref[...] = normed
    projected = dot(normed, w_ref[...])
    conv_in = projected[:, width : width + conv_cols].astype(bf16)
    conv_in_ref[...] = conv_in
    padded[HALO : HALO + GROUP] = conv_in.astype(f32)
    conv_w = conv_w_ref[...]
    taps = conv_w.shape[0]
    pre = conv_b_ref[...]
    for k in range(taps):
        top = HALO - (taps - 1) + k
        pre = pre + conv_w[k : k + 1] * padded[top : top + GROUP]
    padded[0:HALO] = padded[GROUP : GROUP + HALO]
    active, slope = silu_slope(pre)
    active = active.astype(bf16)
    active_ref[...] = active
    slope_ref[...] = slope.astype(bf16)
    signal = active[:, :width]
    entry = active[:, width : width + states]
    readout = active[:, width + states :]
    signal_wide = signal.astype(f32)

    raw = projected[:, width + conv_cols :].T[:8]
    raw_ref[0] = raw
    step, _, log_step, _ = step_values(raw + step_ref[0:8, 0:1])
    running = sum_along(step * step_ref[8:16, 0:1], order[...])
    later = running - log_step
    total = running[:, GROUP - 1 :]
    columns = to_columns([running * LOG2E, jnp.exp(running), jnp.exp(total - later)])
    later = later * LOG2E
    early_wide = spread_heads(columns, 8, heads, size)
    tail_wide = spread_heads(columns, 16, heads, size)
    first, second = slice(0, HALF), slice(HALF, GROUP)
    scores = dot_nt(readout[first], entry[first])
    later_scores = dot_nt(readout[second], entry)
    within = []
    for h in range(heads):
        part = signal[:, h * size : (h + 1) * size]
        begin, end = columns[first, h : h + 1], columns[second, h : h + 1]
        row_first, row_second = later[h : h + 1, first], later[h : h + 1, second]
        near = jnp.exp2(begin - row_first + barred[...]) * scores
        full = jnp.exp2(end - row_first) * later_scores[:, first]
        last = jnp.exp2(end - row_second + barred[...]) * later_scores[:, second]
        both = jnp.concatenate([full.astype(bf16), last.astype(bf16)], axis=1)
        within.append(
            jnp.concatenate([dot(near.astype(bf16), part[first]), dot(both, part)], axis=0)
        )
    start = state[...]
    start_low = start.astype(bf16)
    start_ref[0] = start_low
    carried = dot(readout, start_low) * early_wide
    ssd = jnp.concatenate(within, axis=1) + carried + rows_ref[0:1] * signal_wide
    tail = (signal_wide * tail_wide).astype(bf16)
    state[...] = start * early_wide[GROUP - 1 :] + dot_tn(entry, tail)

    gate_act, gate_slope = silu_slope(projected[:, :width])
    gate_act_ref[...] = gate_act.astype(bf16)
    gate_slope_ref[...] = gate_slope.astype(bf16)
    ssd_ref[...] = ssd
    gated = ssd * gate_act
    scaled = (gated * rows_ref[1:2]).astype(bf16)
    scaled_ref[...] = scaled
    square_ref[0] = sum_lanes(gated * gated)
    placed[slot] = scaled
    where = in_time(place_ref[0], turn)
    store(placed.at[slot], targets, scatter_places(count), where, out_semaphores.at[slot])

    @pl.when(turn == pl.num_programs(0) - 1)
    def _():
        for other in range(2):
            stored(placed, targets, out_semaphores, other)


def time_estimate(microseconds, accessed):
    return pl.CostEstimate(
        flops=int(microseconds * 1.1e9), bytes_accessed=int(accessed), transcendentals=0
    )


def fixed(shape):
    return pl.BlockSpec(shape, lambda turn, place: (0,) * len(shape), pipeline_mode=pl.Buffered(1))


def anywhere(values):
    return [pl.BlockSpec(memory_space=pltpu.HBM)] * len(values)


def run_forward(place, pieces, params, dims):
    heads, size, states, count = dims
    arrays, table = pieces
    dim = params[0].shape[0]
    width, conv_cols = heads * size, params[1].shape[1]
    blocks = len(table)
    tokens = blocks * GROUP

    def moving(columns):
        return pl.BlockSpec((GROUP, columns), lambda turn, place: (turn, 0))

    def rows_of_block(height, columns):
        return pl.BlockSpec((1, height, columns), lambda turn, place: (turn, 0, 0))

    results = pl.pallas_call(
        functools.partial(forward_kernel, dims, table, len(arrays)),
        grid_spec=pltpu.PrefetchScalarGridSpec(
            num_scalar_prefetch=1,
            grid=(blocks,),
            in_specs=[*anywhere(arrays), *[fixed(param.shape) for param in params]],
            out_specs=[
                moving(conv_cols),
                moving(conv_cols),
                moving(conv_cols),
                moving(width),
                moving(width),
                rows_of_block(8, GROUP),
                moving(width),
                rows_of_block(states, width),
                moving(width),
                rows_of_block(8, GROUP),
                moving(dim),
                *anywhere(range(4)),
            ],
            scratch_shapes=[
                pltpu.VMEM((states, width), f32),
                pltpu.VMEM((HALO + GROUP, conv_cols), f32),
                pltpu.VMEM((GROUP, GROUP), bf16),
                pltpu.VMEM((HALF, HALF), f32),
                pltpu.VMEM((2, GROUP, dim), bf16),
                pltpu.SemaphoreType.DMA((2,)),
                pltpu.VMEM((2, GROUP, width), bf16),
                pltpu.SemaphoreType.DMA((2,)),
            ],
        ),
        out_shape=[
            jax.ShapeDtypeStruct((tokens, conv_cols), bf16),
            jax.ShapeDtypeStruct((tokens, conv_cols), bf16),
            jax.ShapeDtypeStruct((tokens, conv_cols), bf16),
            jax.ShapeDtypeStruct((tokens, width), bf16),
            jax.ShapeDtypeStruct((tokens, width), bf16),
            jax.ShapeDtypeStruct((blocks, 8, GROUP), f32),
            jax.ShapeDtypeStruct((tokens, width), f32),
            jax.ShapeDtypeStruct((blocks, states, width), bf16),
            jax.ShapeDtypeStruct((tokens, width), bf16),
            jax.ShapeDtypeStruct((blocks, 8, GROUP), f32),
            jax.ShapeDtypeStruct((tokens, dim), bf16),
            *scatter_shapes(count, width),
        ],
        compiler_params=pltpu.CompilerParams(vmem_limit_bytes=60 * MIB),
        cost_estimate=time_estimate(blocks * 3.0, tokens * (4 * dim + 24 * width)),
        name="forward_blocks",
    )(place, *arrays, *params)
    return results[:11], results[11:]


def backward_kernel(dims, place_ref, *refs):
    heads, size, states, count = dims
    width = heads * size
    conv_cols = width + 2 * states
    conv_in_ref, active_ref, slope_ref, gate_act_ref, gate_slope_ref = refs[:5]
    raw_ref, ssd_ref, start_ref, out_grad_ref, norm_ref = refs[5:10]
    conv_w_ref, step_ref, rows_ref = refs[10:13]
    out_ref, targets = refs[13], refs[14:18]
    sums = refs[18:24]
    gain_ref, skip_ref, conv_wg_ref, conv_bg_ref, bias_ref, rate_ref = sums
    state, pre_grads, order, back_order, barred, placed, semaphores = refs[24:]
    taps = conv_w_ref.shape[0]
    turn = pl.program_id(0)
    slot = lax.rem(turn, 2)

    @pl.when(turn >= 2)
    def _():
        stored(placed, targets, semaphores, slot)

    @pl.when(pl.program_id(0) == 0)
    def _():
        state[...] = jnp.zeros_like(state)
        pre_grads[0:HALO] = jnp.zeros_like(pre_grads[0:HALO])
        for total in sums:
            total[...] = jnp.zeros_like(total)
        row, column = order_indices(GROUP)
        order[...] = ones_where(row <= column)
        back_order[...] = ones_where(row >= column)
        row, column = order_indices(HALF)
        barred[...] = jnp.where(row <= column, 0.0, -1e30)

    gate_act, ssd, out_grad = gate_act_ref[...].astype(f32), ssd_ref[...], out_grad_ref[...]
    norms = norm_ref[0].T
    scale, slope = norms[:, 0:1], norms[:, 1:2]
    gated = ssd * gate_act
    gain_ref[...] += jnp.sum(out_grad * (gated * scale), axis=0, keepdims=True)
    gated_grad = out_grad * (rows_ref[1:2] * scale) - gated * slope
    grad_low = (gated_grad * gate_act).astype(bf16)
    gate_grad = (gated_grad * ssd * gate_slope_ref[...].astype(f32)).astype(bf16)
    out_ref[:, :width] = gate_grad
    placed[slot, :, :width] = gate_grad
    ssd_grad = grad_low.astype(f32)

    raw = raw_ref[0] + step_ref[0:8, 0:1]
    rate = step_ref[8:16, 0:1]
    step, sig, log_step, ratio = step_values(raw)
    decay = step * rate
    running = sum_along(decay, order[...])
    later = running - log_step
    total = running[:, GROUP - 1 :]
    columns = to_columns([later * LOG2E, jnp.exp(running), jnp.exp(total - later)])
    running = running * LOG2E
    early_wide = spread_heads(columns, 8, heads, size)
    tail_wide = spread_heads(columns, 16, heads, size)

    signal = active_ref[:, :width]
    entry = active_ref[:, width : width + states]
    readout = active_ref[:, width + states :]
    signal_wide = signal.astype(f32)
    start_low = start_ref[0]
    end_grad = state[...]
    end_low = end_grad.astype(bf16)
    first, second = slice(0, HALF), slice(HALF, GROUP)
    scores = dot_nt(entry[first], readout)
    later_scores = dot_nt(entry[second], readout[second])
    near_grad, far_grad, last_grad = 0.0, 0.0, 0.0
    within = []
    for h in range(heads):
        part, grad = signal[:, h * size : (h + 1) * size], grad_low[:, h * size : (h + 1) * size]
        begin, end = columns[first, h : h + 1], columns[second, h : h + 1]
        row_first, row_second = running[h : h + 1, first], running[h : h + 1, second]
        near = jnp.exp2(row_first - begin + barred[...])
        full = jnp.exp2(row_second - begin)
        last = jnp.exp2(row_second - end + barred[...])
        both = jnp.concatenate(
            [
                (near * scores[:, first]).astype(bf16),
                (full * scores[:, second]).astype(bf16),
            ],
            axis=1,
        )
        final = (last * later_scores).astype(bf16)
        within.append(jnp.concatenate([dot(both, grad), dot(final, grad[second])], axis=0))
        cross = dot_nt(part[first], grad)
        near_grad = near_grad + cross[:, first] * near
        far_grad = far_grad + cross[:, second] * full
        last_grad = last_grad + dot_nt(part[second], grad[second]) * last
    tail_grad = tail_wide * dot(entry, end_low)
    signal_grad = jnp.concatenate(within, axis=1) + tail_grad
    score_first = jnp.concatenate([near_grad, far_grad], axis=1).astype(bf16)
    score_second = last_grad.astype(bf16)
    tail = (signal_wide * tail_wide).astype(bf16)
    head_grad = (ssd_grad * early_wide).astype(bf16)
    entry_grad = jnp.concatenate(
        [dot(score_first, readout), dot(score_second, readout[second])], axis=0
    ) + dot_nt(tail, end_low)
    readout_grad = dot_tn(score_first, entry[first]) + dot_nt(head_grad, start_low)
    readout_last = readout_grad[second] + dot_tn(score_second, entry[second])
    total_wide = early_wide[GROUP - 1 :]
    state[...] = end_grad * total_wide + dot_tn(readout, head_grad)

    skip = rows_ref[0:1]
    ones = head_ones(width, size)
    column_part = signal_wide * signal_grad
    row_part = ssd_grad * (ssd - skip * signal_wide)
    end_part = jnp.sum(signal_wide * tail_grad, axis=0, keepdims=True) + total_wide * jnp.sum(
        start_low.astype(f32) * end_grad, axis=0, keepdims=True
    )

    def head_sums(value, parts):
        return sum(dot_nt(ones, part) for part in split_parts(value, parts))

    end_rows = head_sums(jnp.broadcast_to(end_part, (8, width)), 2)[:, 0:1]
    decay_grad = sum_along(head_sums(row_part - column_part, 2), back_order[...]) + end_rows
    raw_grad = head_sums(column_part, 1) * ratio + decay_grad * rate * sig
    skip_ref[...] += jnp.sum(ssd_grad * signal_wide, axis=0, keepdims=True)
    bias_ref[...] += raw_grad
    rate_ref[...] += decay_grad * decay
    raw_low = to_columns([raw_grad]).astype(bf16)
    out_ref[:, width + conv_cols :] = raw_low
    placed[slot, :, width + conv_cols :] = raw_low

    pre_grads[GROUP : GROUP + HALO] = pre_grads[0:HALO]
    pre_grads[0:GROUP, :width] = (signal_grad + skip * ssd_grad) * slope_ref[:, :width].astype(f32)
    sides = slope_ref[:, width:].astype(f32)
    pre_grads[0:GROUP, width : width + states] = entry_grad * sides[:, :states]
    pre_grads[0:HALF, width + states :] = readout_grad[first] * sides[first, states:]
    pre_grads[HALF:GROUP, width + states :] = readout_last * sides[second, states:]
    conv_w = conv_w_ref[...]
    conv_in = conv_in_ref[...].astype(f32)
    conv_grad = 0.0
    for k in range(taps):
        ahead = taps - 1 - k
        shifted = pre_grads[ahead : ahead + GROUP]
        conv_grad = conv_grad + conv_w[k : k + 1] * shifted
        conv_wg_ref[k : k + 1] += jnp.sum(shifted * conv_in, axis=0, keepdims=True)
        if ahead == 0:
            conv_bg_ref[...] += jnp.sum(shifted, axis=0, keepdims=True)
    conv_low = conv_grad.astype(bf16)
    out_ref[:, width : width + conv_cols] = conv_low
    placed[slot, :, width : width + conv_cols] = conv_low

    where = in_time(place_ref[0], pl.num_programs(0) - 1 - turn)
    store(placed.at[slot], targets, scatter_places(count), where, semaphores.at[slot])

    @pl.when(turn == pl.num_programs(0) - 1)
    def _():
        for other in range(2):
            stored(placed, targets, semaphores, other)


def run_backward(place, values, params, dims):
    heads, size, states, count = dims
    conv_cols, width = values[0].shape[1], heads * size
    tokens = values[0].shape[0]
    blocks = tokens // GROUP
    last = blocks - 1
    out_cols = width + conv_cols + LANES

    def moving(columns):
        return pl.BlockSpec((GROUP, columns), lambda turn, place: (last - turn, 0))

    def rows_of_block():
        return pl.BlockSpec((1, 8, GROUP), lambda turn, place: (last - turn, 0, 0))

    sums = [(1, width), (1, width), params[0].shape, (1, conv_cols), (8, GROUP), (8, GROUP)]
    return pl.pallas_call(
        functools.partial(backward_kernel, dims),
        grid_spec=pltpu.PrefetchScalarGridSpec(
            num_scalar_prefetch=1,
            grid=(blocks,),
            in_specs=[
                moving(conv_cols),
                moving(conv_cols),
                moving(conv_cols),
                moving(width),
                moving(width),
                rows_of_block(),
                moving(width),
                pl.BlockSpec((1, states, width), lambda turn, place: (last - turn, 0, 0)),
                moving(width),
                rows_of_block(),
                *[fixed(param.shape) for param in params],
            ],
            out_specs=[
                moving(out_cols),
                *anywhere(range(4)),
                *[fixed(shape) for shape in sums],
            ],
            scratch_shapes=[
                pltpu.VMEM((states, width), f32),
                pltpu.VMEM((GROUP + HALO, conv_cols), f32),
                pltpu.VMEM((GROUP, GROUP), bf16),
                pltpu.VMEM((GROUP, GROUP), bf16),
                pltpu.VMEM((HALF, HALF), f32),
                pltpu.VMEM((2, GROUP, out_cols), bf16),
                pltpu.SemaphoreType.DMA((2,)),
            ],
        ),
        out_shape=[
            jax.ShapeDtypeStruct((tokens, out_cols), bf16),
            *scatter_shapes(count, out_cols),
        ]
        + [jax.ShapeDtypeStruct(shape, f32) for shape in sums],
        compiler_params=pltpu.CompilerParams(vmem_limit_bytes=60 * MIB),
        cost_estimate=time_estimate(blocks * 3.5, tokens * 40 * width),
        name="backward_blocks",
    )(place, *values, *params)


def widen_kernel(place_ref, piece_ref, out_ref):
    out_ref[...] = piece_ref[0].astype(f32)


def assemble_out(place, pieces, per):
    count, size, dim = pieces.shape
    groups = count // per

    def source(turn, place):
        relative = (turn % groups * per + turn // groups) ^ place[0]
        return ((relative & 1) * (count // 2) + (relative >> 1), 0, 0)

    return pl.pallas_call(
        widen_kernel,
        grid_spec=pltpu.PrefetchScalarGridSpec(
            num_scalar_prefetch=1,
            grid=(count,),
            in_specs=[pl.BlockSpec((1, size, dim), source)],
            out_specs=pl.BlockSpec((size, dim), lambda turn, place: (turn, 0)),
        ),
        out_shape=jax.ShapeDtypeStruct((count * size, dim), f32),
        cost_estimate=time_estimate(5, count * size * dim * 6),
        name="assemble_out_weight_grad",
    )(place, pieces)


def assemble_kernel(dims, pieces_ref, out_ref):
    heads, size, states, count = dims
    width, shared = heads * size, 2 * states
    inner = count * width
    total = 0.0
    for device in range(count):
        columns = pieces_ref[device].astype(f32).T
        out_ref[device * width : (device + 1) * width] = columns[:width]
        out_ref[inner + device * width : inner + (device + 1) * width] = columns[width : 2 * width]
        total = total + columns[2 * width : 2 * width + shared]
        last = 2 * inner + shared + device * heads
        out_ref[last : last + heads] = columns[2 * width + shared : 2 * width + shared + heads]
    out_ref[2 * inner : 2 * inner + shared] = total


def assemble(pieces, dims):
    heads, size, states, count = dims
    _, rows, columns = pieces.shape
    tile = LANES if rows % LANES == 0 else rows
    out_rows = 2 * count * heads * size + 2 * states + count * heads
    return pl.pallas_call(
        functools.partial(assemble_kernel, dims),
        grid=(rows // tile,),
        in_specs=[pl.BlockSpec((count, tile, columns), lambda turn: (0, turn, 0))],
        out_specs=pl.BlockSpec((out_rows, tile), lambda turn: (0, turn)),
        out_shape=jax.ShapeDtypeStruct((out_rows, rows), f32),
        compiler_params=pltpu.CompilerParams(vmem_limit_bytes=60 * MIB),
        cost_estimate=time_estimate(8, out_rows * rows * 6),
        name="assemble_in_weight_grad",
    )(pieces)


def body(
    tokens,
    norm_gain,
    in_weight,
    conv_weight,
    conv_bias,
    dt_bias,
    decay_log,
    skip_scale,
    gate_gain,
    out_weight,
    cotangent,
):
    count, mine = lax.axis_size("seq"), lax.axis_index("seq")
    place = mine.astype(jnp.int32).reshape(1)
    inner, all_heads, conv_all = gate_gain.shape[0], dt_bias.shape[0], conv_bias.shape[0]
    size, states = inner // all_heads, (conv_all - inner) // 2
    heads, width = all_heads // count, inner // count
    dims = (heads, size, states, count)
    shared = 2 * states
    conv_cols = width + shared
    tok_rows = tokens.shape[1]
    per_plane = out_weight.shape[0] // width

    def own(vector, per, first=0):
        return lax.dynamic_slice_in_dim(vector, first + mine * per, per, vector.ndim - 1)

    def own_conv(array, first=0):
        return jnp.concatenate(
            [own(array, width, first), array[..., first + inner : first + conv_all]], axis=-1
        )

    tokens_row = tokens[0].astype(f32)
    inverse = lax.rsqrt(jnp.mean(tokens_row * tokens_row, axis=-1, keepdims=True) + epsilon)
    normed_own = (tokens_row * inverse * norm_gain).astype(bf16)
    step_own = own(in_weight, heads, inner + conv_all)
    w_own = jnp.concatenate(
        [
            own(in_weight, width),
            own_conv(in_weight, inner),
            jnp.pad(step_own, ((0, 0), (0, LANES - heads))),
        ],
        axis=1,
    )
    w_cols = lax.all_gather(w_own, "batch", axis=0, tiled=True)
    stages = gather_stages()
    held = gather_stage(gather_stage(gather_start(normed_own), 0), 1)
    for stage in range(2, stages):
        held = gather_stage(held, stage)
    w_cols, held, cot_own, out_owned = together(w_cols, held, cotangent[0], out_weight)
    out_rows = rows_from_owner(out_owned, width)
    cot = lax.all_gather(cot_own, "seq", axis=0, tiled=True)

    conv_w, conv_b = own_conv(conv_weight), own_conv(conv_bias)[None]
    per_head = jnp.stack([own(dt_bias, heads), -jnp.exp(own(decay_log, heads))])
    per_head = jnp.pad(per_head, ((0, 0), (0, 8 - heads))).reshape(16, 1)
    step_rows = jnp.broadcast_to(per_head, (16, LANES))
    gain_own = own(gate_gain, width)[None]
    rows = jnp.concatenate(
        [jnp.repeat(own(skip_scale, heads), size)[None], gain_own, jnp.zeros((6, width), f32)],
        axis=0,
    )
    results, out_parts = run_forward(
        place, token_pieces(held), (w_cols, conv_w, conv_b, step_rows, rows), dims
    )
    conv_in, active, slope, gate_act, gate_slope, raw, ssd, starts, scaled, squares, normed = results

    def out_product(part):
        return dot(part, out_rows)

    out_send = out_product(out_parts[0]).astype(bf16)
    out_ready, out_held = scatter_near(out_product, out_parts[1:], out_send)
    out_ready, out_held, cot = together(out_ready, out_held, cot)
    out_grad = jnp.einsum("td,ed->te", cot, out_rows, preferred_element_type=f32)
    slopes = jnp.sum(out_grad * scaled.astype(f32), axis=1)
    sums = sum_seq(jnp.stack([squares[:, 0].reshape(-1), slopes]))
    scale = lax.rsqrt(sums[0] / inner + epsilon)
    norms = jnp.stack([scale, scale * scale * scale * sums[1] / inner])
    norms = jnp.pad(norms, ((0, 6), (0, 0))).reshape(8, -1, GROUP).swapaxes(0, 1)
    scaled_cot = (cot.astype(f32) * scale[:, None]).astype(bf16)
    out_term = jnp.einsum("te,td->ed", scaled, scaled_cot, preferred_element_type=f32)
    out_term, norms, out_ready = together(out_term.astype(bf16), norms, out_ready)
    out_sum = lax.psum_scatter(out_term, "batch", scatter_dimension=0, tiled=True)
    out_ready, out_held = scatter_far(out_ready, out_held, 0)

    values = (conv_in, active, slope, gate_act, gate_slope, raw, ssd, starts, out_grad, norms)
    results = run_backward(place, values, (conv_w, step_rows, rows), dims)
    proj_grad, back_parts = results[0], results[1:5]
    gain_term, skip_term, conv_w_term, conv_b_term, bias_term, rate_term = results[5:]
    proj_grad, back_parts, out_ready, out_held, out_sum = together(
        proj_grad, back_parts, out_ready, out_held, out_sum
    )

    def back_product(part):
        return jnp.einsum("tf,df->td", part, w_cols, preferred_element_type=f32)

    def weight_product(part):
        return jnp.einsum("td,tf->df", normed, part, preferred_element_type=f32).astype(bf16)

    for stage in range(1, stages - 1):
        out_ready, out_held = scatter_far(out_ready, out_held, stage)
    back_send = back_product(back_parts[0]).astype(bf16)
    back_send, proj_grad = together(back_send, proj_grad)
    in_term = weight_product(proj_grad)
    in_term, keeps, out_held = together(in_term, back_parts[1:], out_held)
    in_sum = lax.psum_scatter(in_term, "batch", scatter_dimension=0, tiled=True)
    back_ready, back_held = scatter_near(back_product, keeps, back_send)
    back_ready, in_term, out_sum = together(back_ready, in_term, out_sum)
    back_ready, back_held = scatter_far(back_ready, back_held, 0)
    out_pieces = to_owner(out_sum)[None]

    norm_gain_term = jnp.sum(in_term.astype(f32) * w_cols.astype(f32), axis=1) / norm_gain

    def among_heads(vector, per, total):
        return lax.dynamic_update_slice_in_dim(jnp.zeros((total,), f32), vector, mine * per, 0)

    def among_conv(array):
        wide = jnp.zeros((array.shape[0], inner), f32)
        wide = lax.dynamic_update_slice_in_dim(wide, array[:, :width], mine * width, 1)
        return jnp.concatenate([wide, array[:, width:]], axis=1).reshape(-1)

    skip_heads = jnp.sum(skip_term.reshape(heads, size), axis=1)
    terms = [
        norm_gain_term,
        among_conv(conv_w_term),
        among_conv(conv_b_term),
        among_heads(jnp.sum(bias_term[:heads], axis=1), heads, all_heads),
        among_heads(jnp.sum(rate_term[:heads], axis=1), heads, all_heads),
        among_heads(skip_heads, heads, all_heads),
        among_heads(gain_term[0], width, inner),
    ]
    vector = jnp.concatenate(terms)
    padding = -vector.shape[0] % (8 * LANES)
    vector = jnp.pad(vector, (0, padding)).reshape(-1, LANES)

    axes = [(axis, bit) for axis in ("seq", "batch") for bit in bits_of(lax.axis_size(axis))]
    back_ready, vector, out_pieces, in_sum = together(back_ready, vector, out_pieces, in_sum)
    pieces = lax.all_gather(in_sum, "seq", axis=0, tiled=False)
    in_weight_grad = assemble(pieces, dims).T
    for stage in range(1, stages - 1):
        back_ready, back_held = scatter_far(back_ready, back_held, stage)
    out_pieces = double(out_pieces, 0)
    vector = vector + exchange(vector, *axes.pop(0))
    back_held["arrived"], vector, out_pieces = together(back_held["arrived"], vector, out_pieces)
    for stage in range(1, stages):
        out_pieces = double(out_pieces, stage)
    while axes:
        vector = vector + exchange(vector, *axes.pop(0))
    vector = vector.reshape(-1)
    normed_grad = scatter_end(back_held)
    cot_row = cotangent[0].astype(f32)
    gained = norm_gain * normed_grad
    slope = inverse * inverse * inverse * jnp.mean(gained * tokens_row, axis=-1, keepdims=True)
    input_grad = cot_row + inverse * gained - tokens_row * slope
    own_scale = lax.dynamic_slice_in_dim(scale, mine * tok_rows, tok_rows, 0)[:, None]
    block_out = (tokens_row + own_scale * scatter_end(out_held)).astype(bf16)
    out_weight_grad = assemble_out(place, out_pieces, per_plane)

    parts, offset = [], 0
    for term in terms:
        parts.append(vector[offset : offset + term.shape[0]])
        offset += term.shape[0]
    return (
        block_out[None],
        input_grad[None],
        parts[0],
        in_weight_grad,
        parts[1].reshape(conv_weight.shape),
        parts[2],
        parts[3],
        parts[4],
        parts[5],
        parts[6],
        out_weight_grad,
    )


def solution(mesh):
    placed = (
        P("batch", "seq", None),
        P(),
        P("batch", None),
        P(),
        P(),
        P(),
        P(),
        P(),
        P(),
        P("batch", None),
        P("batch", "seq", None),
    )
    return jax.shard_map(
        body,
        mesh=mesh,
        in_specs=placed,
        out_specs=(
            P("batch", "seq", None),
            P("batch", "seq", None),
            P(),
            P("batch", None),
            P(),
            P(),
            P(),
            P(),
            P(),
            P(),
            P("batch", None),
        ),
        check_vma=False,
    )
```

```python
import functools

import jax
import jax.numpy as jnp
from jax import lax
from jax.experimental import pallas as pl
from jax.experimental.pallas import tpu as pltpu
from jax.sharding import PartitionSpec as P

GROUP = 256
LANES = 128
HALF = GROUP // 2
HALO = 8
STEP_ROWS = 16
LOG2E = 1.4426950408889634
epsilon = 1e-05
f32 = jnp.float32
bf16 = jnp.bfloat16
MIB = 2**20


def exchange(value, axis, distance):
    count = lax.axis_size(axis)
    return lax.ppermute(value, axis, [(source, source ^ distance) for source in range(count)])


def bits_of(count):
    return [1 << k for k in range(count.bit_length() - 1)]


def placed_order(count):
    return [2 * k for k in range(count // 2)] + [2 * k + 1 for k in range(count // 2)]


def together(*values):
    return lax.optimization_barrier(values)


def far_orders():
    far = bits_of(lax.axis_size("seq"))[1:]
    return far, far[::-1]


def gather_start(value):
    half = value.shape[0] // 32 * 16
    return tuple({"base": part, "fresh": None, "near": []} for part in (value[:half], value[half:]))


def gather_stage(held, stage, late=False):
    grown = []
    for half, order in zip(held, far_orders()):
        base, fresh, near = half["base"], half["fresh"], list(half["near"])
        if stage >= 1:
            merged = base if stage == len(order) else jnp.concatenate([base, fresh], axis=0)
            if not late:
                near.append(exchange(merged if stage == 1 else fresh, "seq", 1))
            elif stage == len(order):
                near = [exchange(base, "seq", 1), exchange(fresh, "seq", 1)]
            base = merged
        if stage < len(order):
            fresh = exchange(base, "seq", order[stage])
        grown.append({"base": base, "fresh": fresh, "near": near})
    return tuple(grown)


def gather_stages():
    return len(bits_of(lax.axis_size("seq")))


def gathered(held):
    arrays, table = [], {}
    for number, (half, order) in enumerate(zip(held, far_orders())):
        indices = [0]
        for bit in order:
            indices += [index | bit for index in indices]
        middle = len(indices) // 2
        groups = [(half["base"], indices[:middle]), (half["fresh"], indices[middle:])]
        bounds = [0] + [2 << k for k in range(len(order))]
        if len(half["near"]) < len(order):
            bounds = [0, middle, len(indices)]
        for value, first, last in zip(half["near"], bounds, bounds[1:]):
            groups.append((value, [index | 1 for index in indices[first:last]]))
        for value, members in groups:
            rows = value.shape[0] // len(members)
            for turn, index in enumerate(members):
                table[number, index] = (len(arrays), turn * rows, rows)
            arrays.append(value)
    return arrays, table


def token_pieces(held):
    arrays, table = gathered(held)
    indices = range(lax.axis_size("seq"))
    return arrays, tuple(table[half, index] for index in indices for half in range(2))


def gather_all(value):
    held = gather_start(value)
    for stage in range(gather_stages()):
        held = gather_stage(held, stage)
    return held


def scatter_places(count):
    far = bits_of(count)[1:]
    table = {}
    row = {}
    for near in (1, 0):
        for sent in (True, False):
            for half, order in enumerate((far, far[::-1])):
                members = [0]
                for bit in order[:0:-1]:
                    members += [member | bit for member in members]
                for member in members:
                    index = member | near | (order[0] if sent else 0)
                    array = 0 if near else (1 + half if sent else 3)
                    table[index * 2 + half] = (array, row.get(array, 0))
                    row[array] = row.get(array, 0) + GROUP
    return tuple(table[k] for k in range(2 * count))


def scatter_shapes(count, columns):
    blocks = (count, count // 4, count // 4, count // 2)
    return [jax.ShapeDtypeStruct((part * GROUP, columns), bf16) for part in blocks]


def scatter_near(product, parts, sent):
    arriving = exchange(sent, "seq", 1)
    first, second, kept = parts
    rows = first.shape[0]

    def summed(part, row):
        return (product(part) + arriving[row : row + part.shape[0]].astype(f32)).astype(bf16)

    sends = (summed(first, 0), summed(second, rows))
    sends, kept = together(sends, kept)
    return sends, {"kept": summed(kept, 2 * rows), "arrived": ([], [])}


def scatter_rows(held, half, first, last):
    top = half * (held["kept"].shape[0] // 2)
    total = held["kept"][top + first : top + last].astype(f32)
    for value in held["arrived"][half]:
        total = total + value[first:last].astype(f32)
    return total


def scatter_far(sends, held, stage):
    orders = far_orders()
    arrived = tuple(
        [*held["arrived"][half], exchange(sends[half], "seq", orders[half][stage])]
        for half in range(2)
    )
    held = {"kept": held["kept"], "arrived": arrived}
    rows = sends[0].shape[0]
    if stage + 1 == len(orders[0]):
        return (), held
    ready = tuple(
        scatter_rows(held, half, rows // 2, rows).astype(bf16) for half in range(2)
    )
    return ready, held


def scatter_end(held):
    rows = held["arrived"][0][-1].shape[0]
    return jnp.concatenate([scatter_rows(held, half, 0, rows) for half in range(2)], axis=0)


def sum_seq(value):
    for bit in bits_of(lax.axis_size("seq")):
        value = value + exchange(value, "seq", bit)
    return value


def plane_pairs(ahead):
    planes, count = lax.axis_size("batch"), lax.axis_size("seq")
    per = count // planes
    pairs = []
    for owner in range(planes):
        for piece in range(planes):
            for k in range(per):
                holder = owner * count + piece * per + k
                user = (piece + ahead) % planes * count + owner * per + k
                pairs.append((holder, user))
    return pairs


def rows_from_owner(out_weight, width):
    per = lax.axis_size("seq") // lax.axis_size("batch")
    plane, mine = lax.axis_index("batch"), lax.axis_index("seq")
    rows = lax.dynamic_slice_in_dim(out_weight, mine % per * width, width, 0)
    return lax.psum(jnp.where(plane == mine // per, rows, jnp.zeros_like(rows)), "batch")


def to_owner(summed):
    return lax.ppermute(
        summed, ("batch", "seq"), [(user, holder) for holder, user in plane_pairs(0)]
    )


def double(held, turn):
    bits = bits_of(lax.axis_size("seq"))
    return jnp.concatenate([held, exchange(held, "seq", (bits[1:] + [1])[turn])], axis=0)


def step_values(raw):
    small = jnp.exp(-jnp.abs(raw))
    step = jnp.maximum(raw, 0.0) + jnp.log1p(small)
    sig = jnp.where(raw >= 0, 1.0, small) / (1.0 + small)
    tiny = raw < -20.0
    log_step = jnp.where(tiny, raw, jnp.log(step))
    ratio = jnp.where(tiny, 1.0, sig / step)
    return step, sig, log_step, ratio


def dot(a, b):
    return jnp.dot(a, b, preferred_element_type=f32)


def dot_nt(a, b):
    return lax.dot_general(a, b, (((1,), (1,)), ((), ())), preferred_element_type=f32)


def dot_tn(a, b):
    return lax.dot_general(a, b, (((0,), (0,)), ((), ())), preferred_element_type=f32)


def sigmoid(value):
    return 0.5 * jnp.tanh(0.5 * value) + 0.5


def silu_slope(value):
    sig = sigmoid(value)
    active = value * sig
    return active, sig + active * (1.0 - sig)


def split_parts(value, count):
    parts = []
    for _ in range(count):
        part = value.astype(bf16)
        parts.append(part)
        value = value - part.astype(f32)
    return parts


def sum_along(rows, order):
    parts = jnp.concatenate([part.astype(f32) for part in split_parts(rows, 3)], axis=0)
    total = dot(parts.astype(bf16), order)
    return total[:8] + total[8:16] + total[16:24]


def to_columns(rows):
    stacked = jnp.concatenate(rows, axis=0)
    missing = LANES - stacked.shape[0]
    return jnp.concatenate([stacked, jnp.zeros((missing, GROUP), f32)], axis=0).T


def spread_heads(value, first, heads, size):
    rows = value.shape[0]
    return jnp.concatenate(
        [jnp.broadcast_to(value[:, first + h : first + h + 1], (rows, size)) for h in range(heads)],
        axis=1,
    )


def head_ones(width, size):
    row = lax.broadcasted_iota(jnp.int32, (8, width), 0)
    column = lax.broadcasted_iota(jnp.int32, (8, width), 1)
    return (column // size == row).astype(f32).astype(bf16)


def sum_lanes(value):
    return dot_nt(jnp.ones((8, value.shape[1]), bf16), value.astype(bf16))


def ones_where(condition):
    return jnp.where(condition, 1.0, 0.0).astype(bf16)


def order_indices(length):
    row = lax.broadcasted_iota(jnp.int32, (length, length), 0)
    column = lax.broadcasted_iota(jnp.int32, (length, length), 1)
    return row, column


def fetch(arrays, table, which, target, semaphore):
    for index, (array, row, rows) in enumerate(table):

        @pl.when(which == index)
        def _():
            pltpu.make_async_copy(arrays[array].at[pl.ds(row, rows)], target, semaphore).start()


def fetched(arrays, table, buffer, semaphores, order, blocks=1):
    step = pl.program_id(0)
    slot, other = lax.rem(step, 2), lax.rem(step + 1, 2)

    def start(step, slot):
        for k in range(blocks):
            target = buffer.at[slot, pl.ds(k * GROUP, GROUP)]
            fetch(arrays, table, order(step * blocks + k), target, semaphores.at[slot])

    @pl.when(step == 0)
    def _():
        start(0, 0)

    @pl.when(step + 1 < pl.num_programs(0))
    def _():
        start(step + 1, other)

    for k in range(blocks):
        source = arrays[0].at[pl.ds(0, GROUP)]
        target = buffer.at[slot, pl.ds(k * GROUP, GROUP)]
        pltpu.make_async_copy(source, target, semaphores.at[slot]).wait()
    return buffer[slot]


def store(source, targets, table, which, semaphore):
    for index, (array, row) in enumerate(table):

        @pl.when(which == index)
        def _():
            target = targets[array].at[pl.ds(row, GROUP)]
            pltpu.make_async_copy(source, target, semaphore).start()


def stored(buffer, targets, semaphores, slot):
    target = targets[0].at[pl.ds(0, GROUP)]
    pltpu.make_async_copy(buffer.at[slot], target, semaphores.at[slot]).wait()


def in_time(place, block):
    return ((block // 2) ^ place) * 2 + block % 2


def forward_kernel(dims, table, given, place_ref, *refs):
    heads, size, states, count = dims
    width = heads * size
    conv_cols = width + 2 * states
    arrays, refs = refs[:given], refs[given:]
    w_ref, conv_w_ref, conv_b_ref, step_ref, rows_ref = refs[:5]
    conv_in_ref, active_ref, slope_ref, gate_act_ref, gate_slope_ref = refs[5:10]
    raw_ref, ssd_ref, start_ref, scaled_ref, square_ref, normed_ref = refs[10:16]
    targets = refs[16:20]
    state, padded, order, barred, buffer, semaphores, placed, out_semaphores = refs[20:]
    turn = pl.program_id(0)
    slot = lax.rem(turn, 2)

    @pl.when(turn == 0)
    def _():
        state[...] = jnp.zeros_like(state)
        padded[0:HALO] = jnp.zeros_like(padded[0:HALO])
        row, column = order_indices(GROUP)
        order[...] = ones_where(row <= column)
        row, column = order_indices(HALF)
        barred[...] = jnp.where(row >= column, 0.0, -1e30)

    @pl.when(turn >= 2)
    def _():
        stored(placed, targets, out_semaphores, slot)

    normed = fetched(
        arrays, table, buffer, semaphores, lambda step: in_time(place_ref[0], step)
    )
    normed_ref[...] = normed
    projected = dot(normed, w_ref[...])
    conv_in = projected[:, width : width + conv_cols].astype(bf16)
    conv_in_ref[...] = conv_in
    padded[HALO : HALO + GROUP] = conv_in.astype(f32)
    conv_w = conv_w_ref[...]
    taps = conv_w.shape[0]
    pre = conv_b_ref[...]
    for k in range(taps):
        top = HALO - (taps - 1) + k
        pre = pre + conv_w[k : k + 1] * padded[top : top + GROUP]
    padded[0:HALO] = padded[GROUP : GROUP + HALO]
    active, slope = silu_slope(pre)
    active = active.astype(bf16)
    active_ref[...] = active
    slope_ref[...] = slope.astype(bf16)
    signal = active[:, :width]
    entry = active[:, width : width + states]
    readout = active[:, width + states :]
    signal_wide = signal.astype(f32)

    raw = projected[:, width + conv_cols :].T[:8]
    raw_ref[0] = raw
    step, _, log_step, _ = step_values(raw + step_ref[0:8, 0:1])
    running = sum_along(step * step_ref[8:16, 0:1], order[...])
    later = running - log_step
    total = running[:, GROUP - 1 :]
    columns = to_columns([running * LOG2E, jnp.exp(running), jnp.exp(total - later)])
    later = later * LOG2E
    early_wide = spread_heads(columns, 8, heads, size)
    tail_wide = spread_heads(columns, 16, heads, size)
    first, second = slice(0, HALF), slice(HALF, GROUP)
    scores = dot_nt(readout[first], entry[first])
    later_scores = dot_nt(readout[second], entry)
    within = []
    for h in range(heads):
        part = signal[:, h * size : (h + 1) * size]
        begin, end = columns[first, h : h + 1], columns[second, h : h + 1]
        row_first, row_second = later[h : h + 1, first], later[h : h + 1, second]
        near = jnp.exp2(begin - row_first + barred[...]) * scores
        full = jnp.exp2(end - row_first) * later_scores[:, first]
        last = jnp.exp2(end - row_second + barred[...]) * later_scores[:, second]
        both = jnp.concatenate([full.astype(bf16), last.astype(bf16)], axis=1)
        within.append(
            jnp.concatenate([dot(near.astype(bf16), part[first]), dot(both, part)], axis=0)
        )
    start = state[...]
    start_low = start.astype(bf16)
    start_ref[0] = start_low
    carried = dot(readout, start_low) * early_wide
    ssd = jnp.concatenate(within, axis=1) + carried + rows_ref[0:1] * signal_wide
    tail = (signal_wide * tail_wide).astype(bf16)
    state[...] = start * early_wide[GROUP - 1 :] + dot_tn(entry, tail)

    gate_act, gate_slope = silu_slope(projected[:, :width])
    gate_act_ref[...] = gate_act.astype(bf16)
    gate_slope_ref[...] = gate_slope.astype(bf16)
    ssd_ref[...] = ssd
    gated = ssd * gate_act
    scaled = (gated * rows_ref[1:2]).astype(bf16)
    scaled_ref[...] = scaled
    square_ref[0] = sum_lanes(gated * gated)
    placed[slot] = scaled
    where = in_time(place_ref[0], turn)
    store(placed.at[slot], targets, scatter_places(count), where, out_semaphores.at[slot])

    @pl.when(turn == pl.num_programs(0) - 1)
    def _():
        for other in range(2):
            stored(placed, targets, out_semaphores, other)


def time_estimate(microseconds, accessed):
    return pl.CostEstimate(
        flops=int(microseconds * 1.1e9), bytes_accessed=int(accessed), transcendentals=0
    )


def fixed(shape):
    return pl.BlockSpec(shape, lambda turn, place: (0,) * len(shape), pipeline_mode=pl.Buffered(1))


def anywhere(values):
    return [pl.BlockSpec(memory_space=pltpu.HBM)] * len(values)


def run_forward(place, pieces, params, dims):
    heads, size, states, count = dims
    arrays, table = pieces
    dim = params[0].shape[0]
    width, conv_cols = heads * size, params[1].shape[1]
    blocks = len(table)
    tokens = blocks * GROUP

    def moving(columns):
        return pl.BlockSpec((GROUP, columns), lambda turn, place: (turn, 0))

    def rows_of_block(height, columns):
        return pl.BlockSpec((1, height, columns), lambda turn, place: (turn, 0, 0))

    results = pl.pallas_call(
        functools.partial(forward_kernel, dims, table, len(arrays)),
        grid_spec=pltpu.PrefetchScalarGridSpec(
            num_scalar_prefetch=1,
            grid=(blocks,),
            in_specs=[*anywhere(arrays), *[fixed(param.shape) for param in params]],
            out_specs=[
                moving(conv_cols),
                moving(conv_cols),
                moving(conv_cols),
                moving(width),
                moving(width),
                rows_of_block(8, GROUP),
                moving(width),
                rows_of_block(states, width),
                moving(width),
                rows_of_block(8, GROUP),
                moving(dim),
                *anywhere(range(4)),
            ],
            scratch_shapes=[
                pltpu.VMEM((states, width), f32),
                pltpu.VMEM((HALO + GROUP, conv_cols), f32),
                pltpu.VMEM((GROUP, GROUP), bf16),
                pltpu.VMEM((HALF, HALF), f32),
                pltpu.VMEM((2, GROUP, dim), bf16),
                pltpu.SemaphoreType.DMA((2,)),
                pltpu.VMEM((2, GROUP, width), bf16),
                pltpu.SemaphoreType.DMA((2,)),
            ],
        ),
        out_shape=[
            jax.ShapeDtypeStruct((tokens, conv_cols), bf16),
            jax.ShapeDtypeStruct((tokens, conv_cols), bf16),
            jax.ShapeDtypeStruct((tokens, conv_cols), bf16),
            jax.ShapeDtypeStruct((tokens, width), bf16),
            jax.ShapeDtypeStruct((tokens, width), bf16),
            jax.ShapeDtypeStruct((blocks, 8, GROUP), f32),
            jax.ShapeDtypeStruct((tokens, width), f32),
            jax.ShapeDtypeStruct((blocks, states, width), bf16),
            jax.ShapeDtypeStruct((tokens, width), bf16),
            jax.ShapeDtypeStruct((blocks, 8, GROUP), f32),
            jax.ShapeDtypeStruct((tokens, dim), bf16),
            *scatter_shapes(count, width),
        ],
        compiler_params=pltpu.CompilerParams(vmem_limit_bytes=60 * MIB),
        cost_estimate=time_estimate(blocks * 3.0, tokens * (4 * dim + 24 * width)),
        name="forward_blocks",
    )(place, *arrays, *params)
    return results[:11], results[11:]


def out_grad_kernel(table, given, place_ref, *refs):
    arrays, refs = refs[:given], refs[given:]
    scaled_ref, out_rows_ref, out_grad_ref, slope_ref, cot_ref, buffer, semaphores = refs
    place = place_ref[0]
    cot = fetched(arrays, table, buffer, semaphores, lambda block: in_time(place, block), 2)
    cot_ref[...] = cot
    out_grad = dot_nt(cot, out_rows_ref[...])
    out_grad_ref[...] = out_grad
    for block in range(2):
        here = slice(block * GROUP, (block + 1) * GROUP)
        slope_ref[block] = sum_lanes(out_grad[here] * scaled_ref[here].astype(f32))


def run_out_grad(place, cots, scaled, out_rows):
    arrays, table = cots
    width, dim = out_rows.shape
    blocks = len(table)
    tokens = blocks * GROUP
    return pl.pallas_call(
        functools.partial(out_grad_kernel, table, len(arrays)),
        grid_spec=pltpu.PrefetchScalarGridSpec(
            num_scalar_prefetch=1,
            grid=(blocks // 2,),
            in_specs=[
                *anywhere(arrays),
                pl.BlockSpec((2 * GROUP, width), lambda turn, place: (turn, 0)),
                fixed(out_rows.shape),
            ],
            out_specs=[
                pl.BlockSpec((2 * GROUP, width), lambda turn, place: (turn, 0)),
                pl.BlockSpec((2, 8, GROUP), lambda turn, place: (turn, 0, 0)),
                pl.BlockSpec((2 * GROUP, dim), lambda turn, place: (turn, 0)),
            ],
            scratch_shapes=[pltpu.VMEM((2, 2 * GROUP, dim), bf16), pltpu.SemaphoreType.DMA((2,))],
        ),
        out_shape=[
            jax.ShapeDtypeStruct((tokens, width), f32),
            jax.ShapeDtypeStruct((blocks, 8, GROUP), f32),
            jax.ShapeDtypeStruct((tokens, dim), bf16),
        ],
        compiler_params=pltpu.CompilerParams(vmem_limit_bytes=60 * MIB),
        cost_estimate=time_estimate(12, tokens * (4 * dim + 6 * width)),
        name="out_grad",
    )(place, *arrays, scaled, out_rows)


def backward_kernel(dims, place_ref, *refs):
    heads, size, states, count = dims
    width = heads * size
    conv_cols = width + 2 * states
    conv_in_ref, active_ref, slope_ref, gate_act_ref, gate_slope_ref = refs[:5]
    raw_ref, ssd_ref, start_ref, out_grad_ref, norm_ref = refs[5:10]
    conv_w_ref, step_ref, rows_ref = refs[10:13]
    out_ref, targets = refs[13], refs[14:18]
    sums = refs[18:24]
    gain_ref, skip_ref, conv_wg_ref, conv_bg_ref, bias_ref, rate_ref = sums
    state, pre_grads, order, back_order, barred, placed, semaphores = refs[24:]
    taps = conv_w_ref.shape[0]
    turn = pl.program_id(0)
    slot = lax.rem(turn, 2)

    @pl.when(turn >= 2)
    def _():
        stored(placed, targets, semaphores, slot)

    @pl.when(pl.program_id(0) == 0)
    def _():
        state[...] = jnp.zeros_like(state)
        pre_grads[0:HALO] = jnp.zeros_like(pre_grads[0:HALO])
        for total in sums:
            total[...] = jnp.zeros_like(total)
        row, column = order_indices(GROUP)
        order[...] = ones_where(row <= column)
        back_order[...] = ones_where(row >= column)
        row, column = order_indices(HALF)
        barred[...] = jnp.where(row <= column, 0.0, -1e30)

    gate_act, ssd, out_grad = gate_act_ref[...].astype(f32), ssd_ref[...], out_grad_ref[...]
    norms = norm_ref[0].T
    scale, slope = norms[:, 0:1], norms[:, 1:2]
    gated = ssd * gate_act
    gain_ref[...] += jnp.sum(out_grad * (gated * scale), axis=0, keepdims=True)
    gated_grad = out_grad * (rows_ref[1:2] * scale) - gated * slope
    grad_low = (gated_grad * gate_act).astype(bf16)
    gate_grad = (gated_grad * ssd * gate_slope_ref[...].astype(f32)).astype(bf16)
    out_ref[:, :width] = gate_grad
    placed[slot, :, :width] = gate_grad
    ssd_grad = grad_low.astype(f32)

    raw = raw_ref[0] + step_ref[0:8, 0:1]
    rate = step_ref[8:16, 0:1]
    step, sig, log_step, ratio = step_values(raw)
    decay = step * rate
    running = sum_along(decay, order[...])
    later = running - log_step
    total = running[:, GROUP - 1 :]
    columns = to_columns([later * LOG2E, jnp.exp(running), jnp.exp(total - later)])
    running = running * LOG2E
    early_wide = spread_heads(columns, 8, heads, size)
    tail_wide = spread_heads(columns, 16, heads, size)

    signal = active_ref[:, :width]
    entry = active_ref[:, width : width + states]
    readout = active_ref[:, width + states :]
    signal_wide = signal.astype(f32)
    start_low = start_ref[0]
    end_grad = state[...]
    end_low = end_grad.astype(bf16)
    first, second = slice(0, HALF), slice(HALF, GROUP)
    scores = dot_nt(entry[first], readout)
    later_scores = dot_nt(entry[second], readout[second])
    near_grad, far_grad, last_grad = 0.0, 0.0, 0.0
    within = []
    for h in range(heads):
        part, grad = signal[:, h * size : (h + 1) * size], grad_low[:, h * size : (h + 1) * size]
        begin, end = columns[first, h : h + 1], columns[second, h : h + 1]
        row_first, row_second = running[h : h + 1, first], running[h : h + 1, second]
        near = jnp.exp2(row_first - begin + barred[...])
        full = jnp.exp2(row_second - begin)
        last = jnp.exp2(row_second - end + barred[...])
        both = jnp.concatenate(
            [
                (near * scores[:, first]).astype(bf16),
                (full * scores[:, second]).astype(bf16),
            ],
            axis=1,
        )
        final = (last * later_scores).astype(bf16)
        within.append(jnp.concatenate([dot(both, grad), dot(final, grad[second])], axis=0))
        cross = dot_nt(part[first], grad)
        near_grad = near_grad + cross[:, first] * near
        far_grad = far_grad + cross[:, second] * full
        last_grad = last_grad + dot_nt(part[second], grad[second]) * last
    tail_grad = tail_wide * dot(entry, end_low)
    signal_grad = jnp.concatenate(within, axis=1) + tail_grad
    score_first = jnp.concatenate([near_grad, far_grad], axis=1).astype(bf16)
    score_second = last_grad.astype(bf16)
    tail = (signal_wide * tail_wide).astype(bf16)
    head_grad = (ssd_grad * early_wide).astype(bf16)
    entry_grad = jnp.concatenate(
        [dot(score_first, readout), dot(score_second, readout[second])], axis=0
    ) + dot_nt(tail, end_low)
    readout_grad = dot_tn(score_first, entry[first]) + dot_nt(head_grad, start_low)
    readout_last = readout_grad[second] + dot_tn(score_second, entry[second])
    total_wide = early_wide[GROUP - 1 :]
    state[...] = end_grad * total_wide + dot_tn(readout, head_grad)

    skip = rows_ref[0:1]
    ones = head_ones(width, size)
    column_part = signal_wide * signal_grad
    row_part = ssd_grad * (ssd - skip * signal_wide)
    end_part = jnp.sum(signal_wide * tail_grad, axis=0, keepdims=True) + total_wide * jnp.sum(
        start_low.astype(f32) * end_grad, axis=0, keepdims=True
    )

    def head_sums(value, parts):
        return sum(dot_nt(ones, part) for part in split_parts(value, parts))

    end_rows = head_sums(jnp.broadcast_to(end_part, (8, width)), 2)[:, 0:1]
    decay_grad = sum_along(head_sums(row_part - column_part, 2), back_order[...]) + end_rows
    raw_grad = head_sums(column_part, 1) * ratio + decay_grad * rate * sig
    skip_ref[...] += jnp.sum(ssd_grad * signal_wide, axis=0, keepdims=True)
    bias_ref[...] += raw_grad
    rate_ref[...] += decay_grad * decay
    raw_low = to_columns([raw_grad]).astype(bf16)
    out_ref[:, width + conv_cols :] = raw_low
    placed[slot, :, width + conv_cols :] = raw_low

    pre_grads[GROUP : GROUP + HALO] = pre_grads[0:HALO]
    pre_grads[0:GROUP, :width] = (signal_grad + skip * ssd_grad) * slope_ref[:, :width].astype(f32)
    sides = slope_ref[:, width:].astype(f32)
    pre_grads[0:GROUP, width : width + states] = entry_grad * sides[:, :states]
    pre_grads[0:HALF, width + states :] = readout_grad[first] * sides[first, states:]
    pre_grads[HALF:GROUP, width + states :] = readout_last * sides[second, states:]
    conv_w = conv_w_ref[...]
    conv_in = conv_in_ref[...].astype(f32)
    conv_grad = 0.0
    for k in range(taps):
        ahead = taps - 1 - k
        shifted = pre_grads[ahead : ahead + GROUP]
        conv_grad = conv_grad + conv_w[k : k + 1] * shifted
        conv_wg_ref[k : k + 1] += jnp.sum(shifted * conv_in, axis=0, keepdims=True)
        if ahead == 0:
            conv_bg_ref[...] += jnp.sum(shifted, axis=0, keepdims=True)
    conv_low = conv_grad.astype(bf16)
    out_ref[:, width : width + conv_cols] = conv_low
    placed[slot, :, width : width + conv_cols] = conv_low

    where = in_time(place_ref[0], pl.num_programs(0) - 1 - turn)
    store(placed.at[slot], targets, scatter_places(count), where, semaphores.at[slot])

    @pl.when(turn == pl.num_programs(0) - 1)
    def _():
        for other in range(2):
            stored(placed, targets, semaphores, other)


def run_backward(place, values, params, dims):
    heads, size, states, count = dims
    conv_cols, width = values[0].shape[1], heads * size
    tokens = values[0].shape[0]
    blocks = tokens // GROUP
    last = blocks - 1
    out_cols = width + conv_cols + LANES

    def moving(columns):
        return pl.BlockSpec((GROUP, columns), lambda turn, place: (last - turn, 0))

    def rows_of_block():
        return pl.BlockSpec((1, 8, GROUP), lambda turn, place: (last - turn, 0, 0))

    sums = [(1, width), (1, width), params[0].shape, (1, conv_cols), (8, GROUP), (8, GROUP)]
    return pl.pallas_call(
        functools.partial(backward_kernel, dims),
        grid_spec=pltpu.PrefetchScalarGridSpec(
            num_scalar_prefetch=1,
            grid=(blocks,),
            in_specs=[
                moving(conv_cols),
                moving(conv_cols),
                moving(conv_cols),
                moving(width),
                moving(width),
                rows_of_block(),
                moving(width),
                pl.BlockSpec((1, states, width), lambda turn, place: (last - turn, 0, 0)),
                moving(width),
                rows_of_block(),
                *[fixed(param.shape) for param in params],
            ],
            out_specs=[
                moving(out_cols),
                *anywhere(range(4)),
                *[fixed(shape) for shape in sums],
            ],
            scratch_shapes=[
                pltpu.VMEM((states, width), f32),
                pltpu.VMEM((GROUP + HALO, conv_cols), f32),
                pltpu.VMEM((GROUP, GROUP), bf16),
                pltpu.VMEM((GROUP, GROUP), bf16),
                pltpu.VMEM((HALF, HALF), f32),
                pltpu.VMEM((2, GROUP, out_cols), bf16),
                pltpu.SemaphoreType.DMA((2,)),
            ],
        ),
        out_shape=[
            jax.ShapeDtypeStruct((tokens, out_cols), bf16),
            *scatter_shapes(count, out_cols),
        ]
        + [jax.ShapeDtypeStruct(shape, f32) for shape in sums],
        compiler_params=pltpu.CompilerParams(vmem_limit_bytes=60 * MIB),
        cost_estimate=time_estimate(blocks * 3.5, tokens * 40 * width),
        name="backward_blocks",
    )(place, *values, *params)


def widen_kernel(place_ref, piece_ref, out_ref):
    out_ref[...] = piece_ref[0].astype(f32)


def assemble_out(place, pieces, per):
    count, size, dim = pieces.shape
    groups = count // per

    def source(turn, place):
        relative = (turn % groups * per + turn // groups) ^ place[0]
        return ((relative & 1) * (count // 2) + (relative >> 1), 0, 0)

    return pl.pallas_call(
        widen_kernel,
        grid_spec=pltpu.PrefetchScalarGridSpec(
            num_scalar_prefetch=1,
            grid=(count,),
            in_specs=[pl.BlockSpec((1, size, dim), source)],
            out_specs=pl.BlockSpec((size, dim), lambda turn, place: (turn, 0)),
        ),
        out_shape=jax.ShapeDtypeStruct((count * size, dim), f32),
        cost_estimate=time_estimate(5, count * size * dim * 6),
        name="assemble_out_weight_grad",
    )(place, pieces)


def assemble_kernel(dims, pieces_ref, out_ref):
    heads, size, states, count = dims
    width, shared = heads * size, 2 * states
    inner = count * width
    total = 0.0
    for device in range(count):
        columns = pieces_ref[device].astype(f32).T
        out_ref[device * width : (device + 1) * width] = columns[:width]
        out_ref[inner + device * width : inner + (device + 1) * width] = columns[width : 2 * width]
        total = total + columns[2 * width : 2 * width + shared]
        last = 2 * inner + shared + device * heads
        out_ref[last : last + heads] = columns[2 * width + shared : 2 * width + shared + heads]
    out_ref[2 * inner : 2 * inner + shared] = total


def assemble(pieces, dims):
    heads, size, states, count = dims
    _, rows, columns = pieces.shape
    tile = LANES if rows % LANES == 0 else rows
    out_rows = 2 * count * heads * size + 2 * states + count * heads
    return pl.pallas_call(
        functools.partial(assemble_kernel, dims),
        grid=(rows // tile,),
        in_specs=[pl.BlockSpec((count, tile, columns), lambda turn: (0, turn, 0))],
        out_specs=pl.BlockSpec((out_rows, tile), lambda turn: (0, turn)),
        out_shape=jax.ShapeDtypeStruct((out_rows, rows), f32),
        compiler_params=pltpu.CompilerParams(vmem_limit_bytes=60 * MIB),
        cost_estimate=time_estimate(8, out_rows * rows * 6),
        name="assemble_in_weight_grad",
    )(pieces)


def body(
    tokens,
    norm_gain,
    in_weight,
    conv_weight,
    conv_bias,
    dt_bias,
    decay_log,
    skip_scale,
    gate_gain,
    out_weight,
    cotangent,
):
    count, mine = lax.axis_size("seq"), lax.axis_index("seq")
    place = mine.astype(jnp.int32).reshape(1)
    inner, all_heads, conv_all = gate_gain.shape[0], dt_bias.shape[0], conv_bias.shape[0]
    size, states = inner // all_heads, (conv_all - inner) // 2
    heads, width = all_heads // count, inner // count
    dims = (heads, size, states, count)
    shared = 2 * states
    conv_cols = width + shared
    tok_rows = tokens.shape[1]
    per_plane = out_weight.shape[0] // width

    def own(vector, per, first=0):
        return lax.dynamic_slice_in_dim(vector, first + mine * per, per, vector.ndim - 1)

    def own_conv(array, first=0):
        return jnp.concatenate(
            [own(array, width, first), array[..., first + inner : first + conv_all]], axis=-1
        )

    tokens_row = tokens[0].astype(f32)
    inverse = lax.rsqrt(jnp.mean(tokens_row * tokens_row, axis=-1, keepdims=True) + epsilon)
    normed_own = (tokens_row * inverse * norm_gain).astype(bf16)
    step_own = own(in_weight, heads, inner + conv_all)
    w_own = jnp.concatenate(
        [
            own(in_weight, width),
            own_conv(in_weight, inner),
            jnp.pad(step_own, ((0, 0), (0, LANES - heads))),
        ],
        axis=1,
    )
    w_cols = lax.all_gather(w_own, "batch", axis=0, tiled=True)
    stages = gather_stages()
    held = gather_stage(gather_stage(gather_start(normed_own), 0), 1)
    held, cots = together(held, gather_start(cotangent[0]))
    cots = gather_stage(cots, 0)
    for stage in range(2, stages):
        held = gather_stage(held, stage)
    w_cols, held, cots, out_owned = together(w_cols, held, cots, out_weight)
    cots = gather_stage(cots, 1)
    out_rows = rows_from_owner(out_owned, width)

    conv_w, conv_b = own_conv(conv_weight), own_conv(conv_bias)[None]
    per_head = jnp.stack([own(dt_bias, heads), -jnp.exp(own(decay_log, heads))])
    per_head = jnp.pad(per_head, ((0, 0), (0, 8 - heads))).reshape(16, 1)
    step_rows = jnp.broadcast_to(per_head, (16, LANES))
    gain_own = own(gate_gain, width)[None]
    rows = jnp.concatenate(
        [jnp.repeat(own(skip_scale, heads), size)[None], gain_own, jnp.zeros((6, width), f32)],
        axis=0,
    )
    results, out_parts = run_forward(
        place, token_pieces(held), (w_cols, conv_w, conv_b, step_rows, rows), dims
    )
    conv_in, active, slope, gate_act, gate_slope, raw, ssd, starts, scaled, squares, normed = results
    out_parts, cots, out_rows = together(out_parts, cots, out_rows)
    for stage in range(2, stages):
        cots = gather_stage(cots, stage)

    def out_product(part):
        return dot(part, out_rows)

    out_send = out_product(out_parts[0]).astype(bf16)
    out_send, cots = together(out_send, cots)
    out_grad, slopes, cot = run_out_grad(place, token_pieces(cots), scaled, out_rows)
    sums = jnp.stack([squares[:, 0].reshape(-1), slopes[:, 0].reshape(-1)])
    out_ready, out_held = scatter_near(out_product, out_parts[1:], out_send)
    sums = sums + exchange(sums, "seq", 1)
    sums, first = together(sums, out_ready[0])
    sums = sums + exchange(sums, "seq", 2)
    sums, second = together(sums, out_ready[1])
    for bit in bits_of(count)[2:]:
        sums = sums + exchange(sums, "seq", bit)
    scale = lax.rsqrt(sums[0] / inner + epsilon)
    norms = jnp.stack([scale, scale * scale * scale * sums[1] / inner])
    norms = jnp.pad(norms, ((0, 6), (0, 0))).reshape(8, -1, GROUP).swapaxes(0, 1)
    normed_out = (scaled.astype(f32) * scale[:, None]).astype(bf16)
    out_term = jnp.einsum("te,td->ed", normed_out, cot, preferred_element_type=f32)
    out_term, norms, first, second = together(out_term.astype(bf16), norms, first, second)
    out_sum = lax.psum_scatter(out_term, "batch", scatter_dimension=0, tiled=True)
    out_ready, out_held = scatter_far((first, second), out_held, 0)

    values = (conv_in, active, slope, gate_act, gate_slope, raw, ssd, starts, out_grad, norms)
    results = run_backward(place, values, (conv_w, step_rows, rows), dims)
    proj_grad, back_parts = results[0], results[1:5]
    proj_grad, back_parts, out_ready, out_held, out_sum = together(
        proj_grad, back_parts, out_ready, out_held, out_sum
    )

    def back_product(part):
        return jnp.einsum("tf,df->td", part, w_cols, preferred_element_type=f32)

    def weight_product(part):
        return jnp.einsum("td,tf->df", normed, part, preferred_element_type=f32).astype(bf16)

    for stage in range(1, stages - 1):
        out_ready, out_held = scatter_far(out_ready, out_held, stage)
    back_send = back_product(back_parts[0]).astype(bf16)
    back_send, proj_grad = together(back_send, proj_grad)
    in_term = weight_product(proj_grad)
    in_term, keeps, out_held = together(in_term, back_parts[1:], out_held)
    in_sum = lax.psum_scatter(in_term, "batch", scatter_dimension=0, tiled=True)
    back_ready, back_held = scatter_near(back_product, keeps, back_send)
    back_ready, out_sum = together(back_ready, out_sum)
    back_ready, back_held = scatter_far(back_ready, back_held, 0)
    out_pieces = to_owner(out_sum)[None]

    back_held["kept"], in_term, results = together(back_held["kept"], in_term, results[5:])
    gain_term, skip_term, conv_w_term, conv_b_term, bias_term, rate_term = results
    norm_gain_term = jnp.sum(in_term.astype(f32) * w_cols.astype(f32), axis=1) / norm_gain

    def among_heads(vector, per, total):
        return lax.dynamic_update_slice_in_dim(jnp.zeros((total,), f32), vector, mine * per, 0)

    def among_conv(array):
        wide = jnp.zeros((array.shape[0], inner), f32)
        wide = lax.dynamic_update_slice_in_dim(wide, array[:, :width], mine * width, 1)
        return jnp.concatenate([wide, array[:, width:]], axis=1).reshape(-1)

    skip_heads = jnp.sum(skip_term.reshape(heads, size), axis=1)
    terms = [
        norm_gain_term,
        among_conv(conv_w_term),
        among_conv(conv_b_term),
        among_heads(jnp.sum(bias_term[:heads], axis=1), heads, all_heads),
        among_heads(jnp.sum(rate_term[:heads], axis=1), heads, all_heads),
        among_heads(skip_heads, heads, all_heads),
        among_heads(gain_term[0], width, inner),
    ]
    vector = jnp.concatenate(terms)
    padding = -vector.shape[0] % (8 * LANES)
    vector = jnp.pad(vector, (0, padding)).reshape(-1, LANES)

    axes = [(axis, bit) for axis in ("seq", "batch") for bit in bits_of(lax.axis_size(axis))]
    vector = vector + exchange(vector, *axes.pop(0))
    back_ready, vector, out_pieces, in_sum = together(back_ready, vector, out_pieces, in_sum)
    pieces = lax.all_gather(in_sum, "seq", axis=0, tiled=False)
    in_weight_grad = assemble(pieces, dims).T
    for stage in range(1, stages - 1):
        back_ready, back_held = scatter_far(back_ready, back_held, stage)
    out_pieces = double(out_pieces, 0)
    vector = vector + exchange(vector, *axes.pop(0))
    back_held["arrived"], vector, out_pieces = together(back_held["arrived"], vector, out_pieces)
    for stage in range(1, stages):
        out_pieces = double(out_pieces, stage)
    while axes:
        vector = vector + exchange(vector, *axes.pop(0))
    vector = vector.reshape(-1)
    normed_grad = scatter_end(back_held)
    cot_row = cotangent[0].astype(f32)
    gained = norm_gain * normed_grad
    slope = inverse * inverse * inverse * jnp.mean(gained * tokens_row, axis=-1, keepdims=True)
    input_grad = cot_row + inverse * gained - tokens_row * slope
    own_scale = lax.dynamic_slice_in_dim(scale, mine * tok_rows, tok_rows, 0)[:, None]
    block_out = (tokens_row + own_scale * scatter_end(out_held)).astype(bf16)
    out_weight_grad = assemble_out(place, out_pieces, per_plane)

    parts, offset = [], 0
    for term in terms:
        parts.append(vector[offset : offset + term.shape[0]])
        offset += term.shape[0]
    return (
        block_out[None],
        input_grad[None],
        parts[0],
        in_weight_grad,
        parts[1].reshape(conv_weight.shape),
        parts[2],
        parts[3],
        parts[4],
        parts[5],
        parts[6],
        out_weight_grad,
    )


def solution(mesh):
    placed = (
        P("batch", "seq", None),
        P(),
        P("batch", None),
        P(),
        P(),
        P(),
        P(),
        P(),
        P(),
        P("batch", None),
        P("batch", "seq", None),
    )
    return jax.shard_map(
        body,
        mesh=mesh,
        in_specs=placed,
        out_specs=(
            P("batch", "seq", None),
            P("batch", "seq", None),
            P(),
            P("batch", None),
            P(),
            P(),
            P(),
            P(),
            P(),
            P(),
            P("batch", None),
        ),
        check_vma=False,
    )
```

```python
import functools

import jax
import jax.numpy as jnp
from jax import lax
from jax.experimental import pallas as pl
from jax.experimental.pallas import tpu as pltpu
from jax.sharding import PartitionSpec as P

GROUP = 256
LANES = 128
HALF = GROUP // 2
HALO = 8
LOG2E = 1.4426950408889634
epsilon = 1e-05
f32 = jnp.float32
bf16 = jnp.bfloat16
MIB = 2**20


def exchange(value, axis, distance):
    count = lax.axis_size(axis)
    return lax.ppermute(value, axis, [(source, source ^ distance) for source in range(count)])


def bits_of(count):
    return [1 << k for k in range(count.bit_length() - 1)]


def placed_order(count):
    return [2 * k for k in range(count // 2)] + [2 * k + 1 for k in range(count // 2)]


def together(*values):
    return lax.optimization_barrier(values)


def far_orders():
    far = bits_of(lax.axis_size("seq"))[1:]
    return far, far[::-1]


def gather_start(value):
    half = value.shape[0] // 32 * 16
    return tuple({"base": part, "fresh": None, "near": []} for part in (value[:half], value[half:]))


def gather_stage(held, stage, late=False):
    grown = []
    for half, order in zip(held, far_orders()):
        base, fresh, near = half["base"], half["fresh"], list(half["near"])
        if stage >= 1:
            merged = base if stage == len(order) else jnp.concatenate([base, fresh], axis=0)
            if not late:
                near.append(exchange(merged if stage == 1 else fresh, "seq", 1))
            elif stage == len(order):
                near = [exchange(base, "seq", 1), exchange(fresh, "seq", 1)]
            base = merged
        if stage < len(order):
            fresh = exchange(base, "seq", order[stage])
        grown.append({"base": base, "fresh": fresh, "near": near})
    return tuple(grown)


def gather_stages():
    return len(bits_of(lax.axis_size("seq")))


def gathered(held):
    arrays, table = [], {}
    for number, (half, order) in enumerate(zip(held, far_orders())):
        indices = [0]
        for bit in order:
            indices += [index | bit for index in indices]
        middle = len(indices) // 2
        groups = [(half["base"], indices[:middle]), (half["fresh"], indices[middle:])]
        bounds = [0] + [2 << k for k in range(len(order))]
        if len(half["near"]) < len(order):
            bounds = [0, middle, len(indices)]
        for value, first, last in zip(half["near"], bounds, bounds[1:]):
            groups.append((value, [index | 1 for index in indices[first:last]]))
        for value, members in groups:
            rows = value.shape[0] // len(members)
            for turn, index in enumerate(members):
                table[number, index] = (len(arrays), turn * rows, rows)
            arrays.append(value)
    return arrays, table


def token_pieces(held):
    arrays, table = gathered(held)
    indices = range(lax.axis_size("seq"))
    return arrays, tuple(table[half, index] for index in indices for half in range(2))


def gather_all(value):
    held = gather_start(value)
    for stage in range(gather_stages()):
        held = gather_stage(held, stage)
    return held


def scatter_places(count):
    far = bits_of(count)[1:]
    table = {}
    row = {}
    for near in (1, 0):
        for sent in (True, False):
            for half, order in enumerate((far, far[::-1])):
                members = [0]
                for bit in order[:0:-1]:
                    members += [member | bit for member in members]
                for member in members:
                    index = member | near | (order[0] if sent else 0)
                    array = 0 if near else (1 + half if sent else 3)
                    table[index * 2 + half] = (array, row.get(array, 0))
                    row[array] = row.get(array, 0) + GROUP
    return tuple(table[k] for k in range(2 * count))


def scatter_shapes(count, columns):
    blocks = (count, count // 4, count // 4, count // 2)
    return [jax.ShapeDtypeStruct((part * GROUP, columns), bf16) for part in blocks]


def scatter_near(product, parts, sent):
    arriving = exchange(sent, "seq", 1)
    first, second, kept = parts
    rows = first.shape[0]

    def summed(part, row):
        return (product(part) + arriving[row : row + part.shape[0]].astype(f32)).astype(bf16)

    sends = (summed(first, 0), summed(second, rows))
    sends, kept = together(sends, kept)
    return sends, {"kept": summed(kept, 2 * rows), "arrived": ([], [])}


def scatter_rows(held, half, first, last):
    top = half * (held["kept"].shape[0] // 2)
    total = held["kept"][top + first : top + last].astype(f32)
    for value in held["arrived"][half]:
        total = total + value[first:last].astype(f32)
    return total


def scatter_far(sends, held, stage):
    orders = far_orders()
    arrived = tuple(
        [*held["arrived"][half], exchange(sends[half], "seq", orders[half][stage])]
        for half in range(2)
    )
    held = {"kept": held["kept"], "arrived": arrived}
    rows = sends[0].shape[0]
    if stage + 1 == len(orders[0]):
        return (), held
    ready = tuple(
        scatter_rows(held, half, rows // 2, rows).astype(bf16) for half in range(2)
    )
    return ready, held


def scatter_end(held):
    rows = held["arrived"][0][-1].shape[0]
    return jnp.concatenate([scatter_rows(held, half, 0, rows) for half in range(2)], axis=0)


def add_exchanged(value, distance):
    return (value.astype(f32) + exchange(value, "seq", distance).astype(f32)).astype(bf16)


def plane_pairs(ahead):
    planes, count = lax.axis_size("batch"), lax.axis_size("seq")
    per = count // planes
    pairs = []
    for owner in range(planes):
        for piece in range(planes):
            for k in range(per):
                holder = owner * count + piece * per + k
                user = (piece + ahead) % planes * count + owner * per + k
                pairs.append((holder, user))
    return pairs


def rows_from_owner(out_weight, width):
    per = lax.axis_size("seq") // lax.axis_size("batch")
    plane, mine = lax.axis_index("batch"), lax.axis_index("seq")
    rows = lax.dynamic_slice_in_dim(out_weight, mine % per * width, width, 0)
    return lax.psum(jnp.where(plane == mine // per, rows, jnp.zeros_like(rows)), "batch")


def to_owner(summed):
    return lax.ppermute(
        summed, ("batch", "seq"), [(user, holder) for holder, user in plane_pairs(0)]
    )


def double(held, turn):
    bits = bits_of(lax.axis_size("seq"))
    return jnp.concatenate([held, exchange(held, "seq", (bits[1:] + [1])[turn])], axis=0)


def step_values(raw):
    small = jnp.exp(-jnp.abs(raw))
    step = jnp.maximum(raw, 0.0) + jnp.log1p(small)
    sig = jnp.where(raw >= 0, 1.0, small) / (1.0 + small)
    tiny = raw < -20.0
    log_step = jnp.where(tiny, raw, jnp.log(step))
    ratio = jnp.where(tiny, 1.0, sig / step)
    return step, sig, log_step, ratio


def dot(a, b):
    return jnp.dot(a, b, preferred_element_type=f32)


def dot_nt(a, b):
    return lax.dot_general(a, b, (((1,), (1,)), ((), ())), preferred_element_type=f32)


def dot_tn(a, b):
    return lax.dot_general(a, b, (((0,), (0,)), ((), ())), preferred_element_type=f32)


def sigmoid(value):
    return 0.5 * jnp.tanh(0.5 * value) + 0.5


def silu_slope(value):
    sig = sigmoid(value)
    active = value * sig
    return active, sig + active * (1.0 - sig)


def split_parts(value, count):
    parts = []
    for _ in range(count):
        part = value.astype(bf16)
        parts.append(part)
        value = value - part.astype(f32)
    return parts


def sum_along(rows, order):
    parts = jnp.concatenate([part.astype(f32) for part in split_parts(rows, 3)], axis=0)
    total = dot(parts.astype(bf16), order)
    return total[:8] + total[8:16] + total[16:24]


def to_columns(rows):
    stacked = jnp.concatenate(rows, axis=0)
    missing = LANES - stacked.shape[0]
    return jnp.concatenate([stacked, jnp.zeros((missing, GROUP), f32)], axis=0).T


def spread_heads(value, first, heads, size):
    rows = value.shape[0]
    return jnp.concatenate(
        [jnp.broadcast_to(value[:, first + h : first + h + 1], (rows, size)) for h in range(heads)],
        axis=1,
    )


def head_ones(width, size):
    row = lax.broadcasted_iota(jnp.int32, (8, width), 0)
    column = lax.broadcasted_iota(jnp.int32, (8, width), 1)
    return (column // size == row).astype(f32).astype(bf16)


def sum_lanes(value):
    return dot_nt(jnp.ones((8, value.shape[1]), bf16), value.astype(bf16))


def ones_where(condition):
    return jnp.where(condition, 1.0, 0.0).astype(bf16)


def order_indices(length):
    row = lax.broadcasted_iota(jnp.int32, (length, length), 0)
    column = lax.broadcasted_iota(jnp.int32, (length, length), 1)
    return row, column


def fetch(arrays, table, which, target, semaphore):
    for index, (array, row, rows) in enumerate(table):

        @pl.when(which == index)
        def _():
            pltpu.make_async_copy(arrays[array].at[pl.ds(row, rows)], target, semaphore).start()


def fetched(arrays, table, buffer, semaphores, order, blocks=1):
    step = pl.program_id(0)
    slot, other = lax.rem(step, 2), lax.rem(step + 1, 2)

    def start(step, slot):
        for k in range(blocks):
            target = buffer.at[slot, pl.ds(k * GROUP, GROUP)]
            fetch(arrays, table, order(step * blocks + k), target, semaphores.at[slot])

    @pl.when(step == 0)
    def _():
        start(0, 0)

    @pl.when(step + 1 < pl.num_programs(0))
    def _():
        start(step + 1, other)

    for k in range(blocks):
        source = arrays[0].at[pl.ds(0, GROUP)]
        target = buffer.at[slot, pl.ds(k * GROUP, GROUP)]
        pltpu.make_async_copy(source, target, semaphores.at[slot]).wait()
    return buffer[slot]


def store(source, targets, table, which, semaphore):
    for index, (array, row) in enumerate(table):

        @pl.when(which == index)
        def _():
            target = targets[array].at[pl.ds(row, GROUP)]
            pltpu.make_async_copy(source, target, semaphore).start()


def stored(buffer, targets, semaphores, slot):
    target = targets[0].at[pl.ds(0, GROUP)]
    pltpu.make_async_copy(buffer.at[slot], target, semaphores.at[slot]).wait()


def in_time(place, block):
    return ((block // 2) ^ place) * 2 + block % 2


def forward_kernel(dims, table, given, place_ref, *refs):
    heads, size, states, count = dims
    width = heads * size
    conv_cols = width + 2 * states
    arrays, refs = refs[:given], refs[given:]
    w_ref, conv_w_ref, conv_b_ref, step_ref, rows_ref = refs[:5]
    conv_in_ref, active_ref, slope_ref, gate_act_ref, gate_slope_ref = refs[5:10]
    raw_ref, ssd_ref, start_ref, scaled_ref, square_ref, normed_ref = refs[10:16]
    targets = refs[16:20]
    state, padded, order, barred, buffer, semaphores, placed, out_semaphores = refs[20:]
    turn = pl.program_id(0)
    slot = lax.rem(turn, 2)

    @pl.when(turn == 0)
    def _():
        state[...] = jnp.zeros_like(state)
        padded[0:HALO] = jnp.zeros_like(padded[0:HALO])
        row, column = order_indices(GROUP)
        order[...] = ones_where(row <= column)
        row, column = order_indices(HALF)
        barred[...] = jnp.where(row >= column, 0.0, -1e30)

    @pl.when(turn >= 2)
    def _():
        stored(placed, targets, out_semaphores, slot)

    normed = fetched(
        arrays, table, buffer, semaphores, lambda step: in_time(place_ref[0], step)
    )
    normed_ref[...] = normed
    projected = dot(normed, w_ref[...])
    conv_in = projected[:, width : width + conv_cols].astype(bf16)
    conv_in_ref[...] = conv_in
    padded[HALO : HALO + GROUP] = conv_in.astype(f32)
    conv_w = conv_w_ref[...]
    taps = conv_w.shape[0]
    pre = conv_b_ref[...]
    for k in range(taps):
        top = HALO - (taps - 1) + k
        pre = pre + conv_w[k : k + 1] * padded[top : top + GROUP]
    padded[0:HALO] = padded[GROUP : GROUP + HALO]
    active, slope = silu_slope(pre)
    active = active.astype(bf16)
    active_ref[...] = active
    slope_ref[...] = slope.astype(bf16)
    signal = active[:, :width]
    entry = active[:, width : width + states]
    readout = active[:, width + states :]
    signal_wide = signal.astype(f32)

    lanes = pltpu.roll(
        projected[:, width + conv_cols :], lax.rem(LANES - heads * place_ref[0], LANES), 1
    )
    raw = lanes.T[:8]
    raw_ref[0] = raw
    step, _, log_step, _ = step_values(raw + step_ref[0:8, 0:1])
    running = sum_along(step * step_ref[8:16, 0:1], order[...])
    later = running - log_step
    total = running[:, GROUP - 1 :]
    columns = to_columns([running * LOG2E, jnp.exp(running), jnp.exp(total - later)])
    later = later * LOG2E
    early_wide = spread_heads(columns, 8, heads, size)
    tail_wide = spread_heads(columns, 16, heads, size)
    first, second = slice(0, HALF), slice(HALF, GROUP)
    scores = dot_nt(readout[first], entry[first])
    later_scores = dot_nt(readout[second], entry)
    within = []
    for h in range(heads):
        part = signal[:, h * size : (h + 1) * size]
        begin, end = columns[first, h : h + 1], columns[second, h : h + 1]
        row_first, row_second = later[h : h + 1, first], later[h : h + 1, second]
        near = jnp.exp2(begin - row_first + barred[...]) * scores
        full = jnp.exp2(end - row_first) * later_scores[:, first]
        last = jnp.exp2(end - row_second + barred[...]) * later_scores[:, second]
        both = jnp.concatenate([full.astype(bf16), last.astype(bf16)], axis=1)
        within.append(
            jnp.concatenate([dot(near.astype(bf16), part[first]), dot(both, part)], axis=0)
        )
    start = state[...]
    start_low = start.astype(bf16)
    start_ref[0] = start_low
    carried = dot(readout, start_low) * early_wide
    ssd = jnp.concatenate(within, axis=1) + carried + rows_ref[0:1] * signal_wide
    tail = (signal_wide * tail_wide).astype(bf16)
    state[...] = start * early_wide[GROUP - 1 :] + dot_tn(entry, tail)

    gate_act, gate_slope = silu_slope(projected[:, :width])
    gate_act_ref[...] = gate_act.astype(bf16)
    gate_slope_ref[...] = gate_slope.astype(bf16)
    ssd_ref[...] = ssd
    gated = ssd * gate_act
    scaled = (gated * rows_ref[1:2]).astype(bf16)
    scaled_ref[...] = scaled
    square_ref[0] = sum_lanes(gated * gated)
    placed[slot] = scaled
    where = in_time(place_ref[0], turn)
    store(placed.at[slot], targets, scatter_places(count), where, out_semaphores.at[slot])

    @pl.when(turn == pl.num_programs(0) - 1)
    def _():
        for other in range(2):
            stored(placed, targets, out_semaphores, other)


def time_estimate(microseconds, accessed):
    return pl.CostEstimate(
        flops=int(microseconds * 1.1e9), bytes_accessed=int(accessed), transcendentals=0
    )


def fixed(shape):
    return pl.BlockSpec(shape, lambda turn, place: (0,) * len(shape), pipeline_mode=pl.Buffered(1))


def anywhere(values):
    return [pl.BlockSpec(memory_space=pltpu.HBM)] * len(values)


def run_forward(place, pieces, params, dims):
    heads, size, states, count = dims
    arrays, table = pieces
    dim = params[0].shape[0]
    width, conv_cols = heads * size, params[1].shape[1]
    blocks = len(table)
    tokens = blocks * GROUP

    def moving(columns):
        return pl.BlockSpec((GROUP, columns), lambda turn, place: (turn, 0))

    def rows_of_block(height, columns):
        return pl.BlockSpec((1, height, columns), lambda turn, place: (turn, 0, 0))

    results = pl.pallas_call(
        functools.partial(forward_kernel, dims, table, len(arrays)),
        grid_spec=pltpu.PrefetchScalarGridSpec(
            num_scalar_prefetch=1,
            grid=(blocks,),
            in_specs=[*anywhere(arrays), *[fixed(param.shape) for param in params]],
            out_specs=[
                moving(conv_cols),
                moving(conv_cols),
                moving(conv_cols),
                moving(width),
                moving(width),
                rows_of_block(8, GROUP),
                moving(width),
                rows_of_block(states, width),
                moving(width),
                rows_of_block(8, GROUP),
                moving(dim),
                *anywhere(range(4)),
            ],
            scratch_shapes=[
                pltpu.VMEM((states, width), f32),
                pltpu.VMEM((HALO + GROUP, conv_cols), f32),
                pltpu.VMEM((GROUP, GROUP), bf16),
                pltpu.VMEM((HALF, HALF), f32),
                pltpu.VMEM((2, GROUP, dim), bf16),
                pltpu.SemaphoreType.DMA((2,)),
                pltpu.VMEM((2, GROUP, width), bf16),
                pltpu.SemaphoreType.DMA((2,)),
            ],
        ),
        out_shape=[
            jax.ShapeDtypeStruct((tokens, conv_cols), bf16),
            jax.ShapeDtypeStruct((tokens, conv_cols), bf16),
            jax.ShapeDtypeStruct((tokens, conv_cols), bf16),
            jax.ShapeDtypeStruct((tokens, width), bf16),
            jax.ShapeDtypeStruct((tokens, width), bf16),
            jax.ShapeDtypeStruct((blocks, 8, GROUP), f32),
            jax.ShapeDtypeStruct((tokens, width), f32),
            jax.ShapeDtypeStruct((blocks, states, width), bf16),
            jax.ShapeDtypeStruct((tokens, width), bf16),
            jax.ShapeDtypeStruct((blocks, 8, GROUP), f32),
            jax.ShapeDtypeStruct((tokens, dim), bf16),
            *scatter_shapes(count, width),
        ],
        compiler_params=pltpu.CompilerParams(vmem_limit_bytes=60 * MIB),
        cost_estimate=time_estimate(blocks * 3.0, tokens * (4 * dim + 24 * width)),
        name="forward_blocks",
    )(place, *arrays, *params)
    return results[:11], results[11:]


def out_grad_kernel(table, given, place_ref, *refs):
    arrays, refs = refs[:given], refs[given:]
    scaled_ref, out_rows_ref, out_grad_ref, slope_ref, cot_ref, buffer, semaphores = refs
    place = place_ref[0]
    cot = fetched(arrays, table, buffer, semaphores, lambda block: in_time(place, block), 2)
    cot_ref[...] = cot
    out_grad = dot_nt(cot, out_rows_ref[...])
    out_grad_ref[...] = out_grad
    for block in range(2):
        here = slice(block * GROUP, (block + 1) * GROUP)
        slope_ref[block] = sum_lanes(out_grad[here] * scaled_ref[here].astype(f32))


def run_out_grad(place, cots, scaled, out_rows):
    arrays, table = cots
    width, dim = out_rows.shape
    blocks = len(table)
    tokens = blocks * GROUP
    return pl.pallas_call(
        functools.partial(out_grad_kernel, table, len(arrays)),
        grid_spec=pltpu.PrefetchScalarGridSpec(
            num_scalar_prefetch=1,
            grid=(blocks // 2,),
            in_specs=[
                *anywhere(arrays),
                pl.BlockSpec((2 * GROUP, width), lambda turn, place: (turn, 0)),
                fixed(out_rows.shape),
            ],
            out_specs=[
                pl.BlockSpec((2 * GROUP, width), lambda turn, place: (turn, 0)),
                pl.BlockSpec((2, 8, GROUP), lambda turn, place: (turn, 0, 0)),
                pl.BlockSpec((2 * GROUP, dim), lambda turn, place: (turn, 0)),
            ],
            scratch_shapes=[pltpu.VMEM((2, 2 * GROUP, dim), bf16), pltpu.SemaphoreType.DMA((2,))],
        ),
        out_shape=[
            jax.ShapeDtypeStruct((tokens, width), f32),
            jax.ShapeDtypeStruct((blocks, 8, GROUP), f32),
            jax.ShapeDtypeStruct((tokens, dim), bf16),
        ],
        compiler_params=pltpu.CompilerParams(vmem_limit_bytes=60 * MIB),
        cost_estimate=time_estimate(12, tokens * (4 * dim + 6 * width)),
        name="out_grad",
    )(place, *arrays, scaled, out_rows)


def backward_kernel(dims, place_ref, *refs):
    heads, size, states, count = dims
    width = heads * size
    conv_cols = width + 2 * states
    conv_in_ref, active_ref, slope_ref, gate_act_ref, gate_slope_ref = refs[:5]
    raw_ref, ssd_ref, start_ref, out_grad_ref, norm_ref = refs[5:10]
    conv_w_ref, step_ref, rows_ref = refs[10:13]
    out_ref, targets = refs[13], refs[14:18]
    gain_ref, conv_wg_ref, conv_bg_ref, small_ref = refs[18:22]
    state, pre_grads, order, back_order, barred, placed, semaphores = refs[22:29]
    skip_ref, bias_ref, rate_ref = refs[29:]
    sums = (gain_ref, conv_wg_ref, conv_bg_ref, skip_ref, bias_ref, rate_ref)
    taps = conv_w_ref.shape[0]
    turn = pl.program_id(0)
    slot = lax.rem(turn, 2)

    @pl.when(turn >= 2)
    def _():
        stored(placed, targets, semaphores, slot)

    @pl.when(pl.program_id(0) == 0)
    def _():
        state[...] = jnp.zeros_like(state)
        pre_grads[0:HALO] = jnp.zeros_like(pre_grads[0:HALO])
        for total in sums:
            total[...] = jnp.zeros_like(total)
        row, column = order_indices(GROUP)
        order[...] = ones_where(row <= column)
        back_order[...] = ones_where(row >= column)
        row, column = order_indices(HALF)
        barred[...] = jnp.where(row <= column, 0.0, -1e30)

    gate_act, ssd, out_grad = gate_act_ref[...].astype(f32), ssd_ref[...], out_grad_ref[...]
    norms = norm_ref[0].T
    scale, slope = norms[:, 0:1], norms[:, 1:2]
    gated = ssd * gate_act
    gain_ref[...] += jnp.sum(out_grad * (gated * scale), axis=0, keepdims=True)
    gated_grad = out_grad * (rows_ref[1:2] * scale) - gated * slope
    grad_low = (gated_grad * gate_act).astype(bf16)
    gate_grad = (gated_grad * ssd * gate_slope_ref[...].astype(f32)).astype(bf16)
    out_ref[:, :width] = gate_grad
    placed[slot, :, :width] = gate_grad
    ssd_grad = grad_low.astype(f32)

    raw = raw_ref[0] + step_ref[0:8, 0:1]
    rate = step_ref[8:16, 0:1]
    step, sig, log_step, ratio = step_values(raw)
    decay = step * rate
    running = sum_along(decay, order[...])
    later = running - log_step
    total = running[:, GROUP - 1 :]
    columns = to_columns([later * LOG2E, jnp.exp(running), jnp.exp(total - later)])
    running = running * LOG2E
    early_wide = spread_heads(columns, 8, heads, size)
    tail_wide = spread_heads(columns, 16, heads, size)

    signal = active_ref[:, :width]
    entry = active_ref[:, width : width + states]
    readout = active_ref[:, width + states :]
    signal_wide = signal.astype(f32)
    start_low = start_ref[0]
    end_grad = state[...]
    end_low = end_grad.astype(bf16)
    first, second = slice(0, HALF), slice(HALF, GROUP)
    scores = dot_nt(entry[first], readout)
    later_scores = dot_nt(entry[second], readout[second])
    near_grad, far_grad, last_grad = 0.0, 0.0, 0.0
    within = []
    for h in range(heads):
        part, grad = signal[:, h * size : (h + 1) * size], grad_low[:, h * size : (h + 1) * size]
        begin, end = columns[first, h : h + 1], columns[second, h : h + 1]
        row_first, row_second = running[h : h + 1, first], running[h : h + 1, second]
        near = jnp.exp2(row_first - begin + barred[...])
        full = jnp.exp2(row_second - begin)
        last = jnp.exp2(row_second - end + barred[...])
        both = jnp.concatenate(
            [
                (near * scores[:, first]).astype(bf16),
                (full * scores[:, second]).astype(bf16),
            ],
            axis=1,
        )
        final = (last * later_scores).astype(bf16)
        within.append(jnp.concatenate([dot(both, grad), dot(final, grad[second])], axis=0))
        cross = dot_nt(part[first], grad)
        near_grad = near_grad + cross[:, first] * near
        far_grad = far_grad + cross[:, second] * full
        last_grad = last_grad + dot_nt(part[second], grad[second]) * last
    tail_grad = tail_wide * dot(entry, end_low)
    signal_grad = jnp.concatenate(within, axis=1) + tail_grad
    score_first = jnp.concatenate([near_grad, far_grad], axis=1).astype(bf16)
    score_second = last_grad.astype(bf16)
    tail = (signal_wide * tail_wide).astype(bf16)
    head_grad = (ssd_grad * early_wide).astype(bf16)
    entry_grad = jnp.concatenate(
        [dot(score_first, readout), dot(score_second, readout[second])], axis=0
    ) + dot_nt(tail, end_low)
    readout_grad = dot_tn(score_first, entry[first]) + dot_nt(head_grad, start_low)
    readout_last = readout_grad[second] + dot_tn(score_second, entry[second])
    total_wide = early_wide[GROUP - 1 :]
    state[...] = end_grad * total_wide + dot_tn(readout, head_grad)

    skip = rows_ref[0:1]
    ones = head_ones(width, size)
    column_part = signal_wide * signal_grad
    row_part = ssd_grad * (ssd - skip * signal_wide)
    end_part = jnp.sum(signal_wide * tail_grad, axis=0, keepdims=True) + total_wide * jnp.sum(
        start_low.astype(f32) * end_grad, axis=0, keepdims=True
    )

    def head_sums(value, parts):
        return sum(dot_nt(ones, part) for part in split_parts(value, parts))

    end_rows = head_sums(jnp.broadcast_to(end_part, (8, width)), 2)[:, 0:1]
    decay_grad = sum_along(head_sums(row_part - column_part, 2), back_order[...]) + end_rows
    raw_grad = head_sums(column_part, 1) * ratio + decay_grad * rate * sig
    skip_ref[...] += jnp.sum(ssd_grad * signal_wide, axis=0, keepdims=True)
    bias_ref[...] += raw_grad
    rate_ref[...] += decay_grad * decay
    raw_low = pltpu.roll(to_columns([raw_grad]), heads * place_ref[0], 1).astype(bf16)
    out_ref[:, width + conv_cols :] = raw_low
    placed[slot, :, width + conv_cols :] = raw_low

    pre_grads[GROUP : GROUP + HALO] = pre_grads[0:HALO]
    pre_grads[0:GROUP, :width] = (signal_grad + skip * ssd_grad) * slope_ref[:, :width].astype(f32)
    sides = slope_ref[:, width:].astype(f32)
    pre_grads[0:GROUP, width : width + states] = entry_grad * sides[:, :states]
    pre_grads[0:HALF, width + states :] = readout_grad[first] * sides[first, states:]
    pre_grads[HALF:GROUP, width + states :] = readout_last * sides[second, states:]
    conv_w = conv_w_ref[...]
    conv_in = conv_in_ref[...].astype(f32)
    conv_grad = 0.0
    for k in range(taps):
        ahead = taps - 1 - k
        shifted = pre_grads[ahead : ahead + GROUP]
        conv_grad = conv_grad + conv_w[k : k + 1] * shifted
        conv_wg_ref[k : k + 1] += jnp.sum(shifted * conv_in, axis=0, keepdims=True)
        if ahead == 0:
            conv_bg_ref[...] += jnp.sum(shifted, axis=0, keepdims=True)
    conv_low = conv_grad.astype(bf16)
    out_ref[:, width : width + conv_cols] = conv_low
    placed[slot, :, width : width + conv_cols] = conv_low

    where = in_time(place_ref[0], pl.num_programs(0) - 1 - turn)
    store(placed.at[slot], targets, scatter_places(count), where, semaphores.at[slot])

    @pl.when(turn == pl.num_programs(0) - 1)
    def _():
        skips = head_sums(jnp.broadcast_to(skip_ref[...], (8, width)), 3)[:, 0:1]
        place_of = lax.broadcasted_iota(jnp.int32, small_ref.shape, 1)
        small = jnp.where(place_of == 0, jnp.sum(bias_ref[...], axis=1, keepdims=True), skips)
        rates = jnp.sum(rate_ref[...], axis=1, keepdims=True)
        small_ref[...] = jnp.where(place_of == 1, rates, small)
        for other in range(2):
            stored(placed, targets, semaphores, other)


def run_backward(place, values, params, dims):
    heads, size, states, count = dims
    conv_cols, width = values[0].shape[1], heads * size
    tokens = values[0].shape[0]
    blocks = tokens // GROUP
    last = blocks - 1
    out_cols = width + conv_cols + LANES

    def moving(columns):
        return pl.BlockSpec((GROUP, columns), lambda turn, place: (last - turn, 0))

    def rows_of_block():
        return pl.BlockSpec((1, 8, GROUP), lambda turn, place: (last - turn, 0, 0))

    sums = [(1, width), params[0].shape, (1, conv_cols), (8, LANES)]
    return pl.pallas_call(
        functools.partial(backward_kernel, dims),
        grid_spec=pltpu.PrefetchScalarGridSpec(
            num_scalar_prefetch=1,
            grid=(blocks,),
            in_specs=[
                moving(conv_cols),
                moving(conv_cols),
                moving(conv_cols),
                moving(width),
                moving(width),
                rows_of_block(),
                moving(width),
                pl.BlockSpec((1, states, width), lambda turn, place: (last - turn, 0, 0)),
                moving(width),
                rows_of_block(),
                *[fixed(param.shape) for param in params],
            ],
            out_specs=[
                moving(out_cols),
                *anywhere(range(4)),
                *[fixed(shape) for shape in sums],
            ],
            scratch_shapes=[
                pltpu.VMEM((states, width), f32),
                pltpu.VMEM((GROUP + HALO, conv_cols), f32),
                pltpu.VMEM((GROUP, GROUP), bf16),
                pltpu.VMEM((GROUP, GROUP), bf16),
                pltpu.VMEM((HALF, HALF), f32),
                pltpu.VMEM((2, GROUP, out_cols), bf16),
                pltpu.SemaphoreType.DMA((2,)),
                pltpu.VMEM((1, width), f32),
                pltpu.VMEM((8, GROUP), f32),
                pltpu.VMEM((8, GROUP), f32),
            ],
        ),
        out_shape=[
            jax.ShapeDtypeStruct((tokens, out_cols), bf16),
            *scatter_shapes(count, out_cols),
        ]
        + [jax.ShapeDtypeStruct(shape, f32) for shape in sums],
        compiler_params=pltpu.CompilerParams(vmem_limit_bytes=60 * MIB),
        cost_estimate=time_estimate(blocks * 3.5, tokens * 40 * width),
        name="backward_blocks",
    )(place, *values, *params)


def widen_kernel(place_ref, piece_ref, out_ref):
    out_ref[...] = piece_ref[0].astype(f32)


def assemble_out(place, pieces, per):
    count, size, dim = pieces.shape
    groups = count // per

    def source(turn, place):
        relative = (turn % groups * per + turn // groups) ^ place[0]
        return ((relative & 1) * (count // 2) + (relative >> 1), 0, 0)

    return pl.pallas_call(
        widen_kernel,
        grid_spec=pltpu.PrefetchScalarGridSpec(
            num_scalar_prefetch=1,
            grid=(count,),
            in_specs=[pl.BlockSpec((1, size, dim), source)],
            out_specs=pl.BlockSpec((size, dim), lambda turn, place: (turn, 0)),
        ),
        out_shape=jax.ShapeDtypeStruct((count * size, dim), f32),
        cost_estimate=time_estimate(5, count * size * dim * 6),
        name="assemble_out_weight_grad",
    )(place, pieces)


def assemble_kernel(dims, lasting, pieces_ref, side_ref, out_ref):
    heads, size, states, count = dims
    width = heads * size
    inner = count * width
    for device in range(count):
        columns = pieces_ref[device].astype(f32).T
        out_ref[device * width : (device + 1) * width] = columns[:width]
        out_ref[inner + device * width : inner + (device + 1) * width] = columns[width:]
    out_ref[2 * inner :] = side_ref[...].astype(f32).T[:lasting]


def assemble(pieces, side, dims):
    heads, size, states, count = dims
    _, rows, columns = pieces.shape
    tile = LANES if rows % LANES == 0 else rows
    lasting = 2 * states + count * heads
    out_rows = 2 * count * heads * size + lasting
    return pl.pallas_call(
        functools.partial(assemble_kernel, dims, lasting),
        grid=(rows // tile,),
        in_specs=[
            pl.BlockSpec((count, tile, columns), lambda turn: (0, turn, 0)),
            pl.BlockSpec((tile, side.shape[1]), lambda turn: (turn, 0)),
        ],
        out_specs=pl.BlockSpec((out_rows, tile), lambda turn: (0, turn)),
        out_shape=jax.ShapeDtypeStruct((out_rows, rows), f32),
        compiler_params=pltpu.CompilerParams(vmem_limit_bytes=60 * MIB),
        cost_estimate=time_estimate(8, out_rows * rows * 6),
        name="assemble_in_weight_grad",
    )(pieces, side)


def body(
    tokens,
    norm_gain,
    in_weight,
    conv_weight,
    conv_bias,
    dt_bias,
    decay_log,
    skip_scale,
    gate_gain,
    out_weight,
    cotangent,
):
    count, mine = lax.axis_size("seq"), lax.axis_index("seq")
    place = mine.astype(jnp.int32).reshape(1)
    inner, all_heads, conv_all = gate_gain.shape[0], dt_bias.shape[0], conv_bias.shape[0]
    size, states = inner // all_heads, (conv_all - inner) // 2
    heads, width = all_heads // count, inner // count
    dims = (heads, size, states, count)
    shared = 2 * states
    conv_cols = width + shared
    tok_rows = tokens.shape[1]
    per_plane = out_weight.shape[0] // width

    def own(vector, per, first=0):
        return lax.dynamic_slice_in_dim(vector, first + mine * per, per, vector.ndim - 1)

    def own_conv(array, first=0):
        return jnp.concatenate(
            [own(array, width, first), array[..., first + inner : first + conv_all]], axis=-1
        )

    tokens_row = tokens[0].astype(f32)
    inverse = lax.rsqrt(jnp.mean(tokens_row * tokens_row, axis=-1, keepdims=True) + epsilon)
    normed_own = (tokens_row * inverse * norm_gain).astype(bf16)
    step_own = own(in_weight, heads, inner + conv_all)
    w_own = jnp.concatenate(
        [
            own(in_weight, width),
            own_conv(in_weight, inner),
            lax.dynamic_update_slice_in_dim(
                jnp.zeros((step_own.shape[0], LANES), bf16), step_own, mine * heads, 1
            ),
        ],
        axis=1,
    )
    w_cols = lax.all_gather(w_own, "batch", axis=0, tiled=True)
    stages = gather_stages()
    held = gather_stage(gather_stage(gather_start(normed_own), 0), 1)
    held, cots = together(held, gather_start(cotangent[0]))
    cots = gather_stage(cots, 0)
    for stage in range(2, stages):
        held = gather_stage(held, stage)
    w_cols, held, cots, out_owned = together(w_cols, held, cots, out_weight)
    cots = gather_stage(cots, 1)
    out_rows = rows_from_owner(out_owned, width)

    conv_w, conv_b = own_conv(conv_weight), own_conv(conv_bias)[None]
    per_head = jnp.stack([own(dt_bias, heads), -jnp.exp(own(decay_log, heads))])
    per_head = jnp.pad(per_head, ((0, 0), (0, 8 - heads))).reshape(16, 1)
    step_rows = jnp.broadcast_to(per_head, (16, LANES))
    gain_own = own(gate_gain, width)[None]
    rows = jnp.concatenate(
        [jnp.repeat(own(skip_scale, heads), size)[None], gain_own, jnp.zeros((6, width), f32)],
        axis=0,
    )
    results, out_parts = run_forward(
        place, token_pieces(held), (w_cols, conv_w, conv_b, step_rows, rows), dims
    )
    conv_in, active, slope, gate_act, gate_slope, raw, ssd, starts, scaled, squares, normed = results
    out_parts, cots, out_rows = together(out_parts, cots, out_rows)
    for stage in range(2, stages):
        cots = gather_stage(cots, stage)

    def out_product(part):
        return dot(part, out_rows)

    out_send = out_product(out_parts[0]).astype(bf16)
    out_send, cots = together(out_send, cots)
    out_grad, slopes, cot = run_out_grad(place, token_pieces(cots), scaled, out_rows)
    sums = jnp.stack([squares[:, 0].reshape(-1), slopes[:, 0].reshape(-1)])
    out_ready, out_held = scatter_near(out_product, out_parts[1:], out_send)
    sums = sums + exchange(sums, "seq", 1)
    sums, first = together(sums, out_ready[0])
    sums = sums + exchange(sums, "seq", 2)
    sums, second = together(sums, out_ready[1])
    for bit in bits_of(count)[2:]:
        sums = sums + exchange(sums, "seq", bit)
    scale = lax.rsqrt(sums[0] / inner + epsilon)
    norms = jnp.stack([scale, scale * scale * scale * sums[1] / inner])
    norms = jnp.pad(norms, ((0, 6), (0, 0))).reshape(8, -1, GROUP).swapaxes(0, 1)
    normed_out = (scaled.astype(f32) * scale[:, None]).astype(bf16)
    out_term = jnp.einsum("te,td->ed", normed_out, cot, preferred_element_type=f32)
    out_term, norms, first, second = together(out_term.astype(bf16), norms, first, second)
    out_sum = lax.psum_scatter(out_term, "batch", scatter_dimension=0, tiled=True)
    out_ready, out_held = scatter_far((first, second), out_held, 0)

    values = (conv_in, active, slope, gate_act, gate_slope, raw, ssd, starts, out_grad, norms)
    results = run_backward(place, values, (conv_w, step_rows, rows), dims)
    proj_grad, back_parts = results[0], results[1:5]
    proj_grad, back_parts, out_ready, out_held, out_sum = together(
        proj_grad, back_parts, out_ready, out_held, out_sum
    )

    def back_product(part):
        return jnp.einsum("tf,df->td", part, w_cols, preferred_element_type=f32)

    def weight_product(part):
        return jnp.einsum("td,tf->df", normed, part, preferred_element_type=f32).astype(bf16)

    for stage in range(1, stages - 1):
        out_ready, out_held = scatter_far(out_ready, out_held, stage)
    back_send = back_product(back_parts[0]).astype(bf16)
    back_send, proj_grad = together(back_send, proj_grad)
    main_term = weight_product(proj_grad[:, : 2 * width])
    main_term, keeps, out_held = together(main_term, back_parts[1:], out_held)
    main_sum = lax.psum_scatter(main_term, "batch", scatter_dimension=0, tiled=True)
    back_ready, back_held = scatter_near(back_product, keeps, back_send)
    back_ready, out_sum, proj_grad = together(back_ready, out_sum, proj_grad)
    back_ready, back_held = scatter_far(back_ready, back_held, 0)
    out_pieces = to_owner(out_sum)[None]
    side_term = weight_product(proj_grad[:, 2 * width :])
    side_sum = lax.psum_scatter(side_term, "batch", scatter_dimension=0, tiled=True)

    back_ready, out_pieces, main_sum, side_sum = together(
        back_ready, out_pieces, main_sum, side_sum
    )
    pieces = lax.all_gather(main_sum, "seq", axis=0, tiled=False)
    back_held["arrived"], results = together(back_held["arrived"], results[5:])
    gain_term, conv_w_term, conv_b_term, small_term = results
    norm_gain_term = jnp.sum(main_term.astype(f32) * w_cols[:, : 2 * width].astype(f32), axis=1)
    norm_gain_term += jnp.sum(side_term.astype(f32) * w_cols[:, 2 * width :].astype(f32), axis=1)
    norm_gain_term /= norm_gain

    taps = conv_weight.shape[0]
    conv_terms = jnp.concatenate([conv_w_term, conv_b_term], axis=0)
    own_terms = jnp.concatenate([conv_terms[:, :width], gain_term], axis=0)
    own_terms = lax.dynamic_update_slice_in_dim(
        jnp.zeros((taps + 2, inner), f32), own_terms, mine * width, 1
    )
    head_terms = lax.dynamic_update_slice_in_dim(
        jnp.zeros((all_heads, 3), f32), small_term[:heads, :3], mine * heads, 0
    )
    terms = [own_terms, conv_terms[:, width:], norm_gain_term, head_terms]
    vector = jnp.concatenate([term.reshape(-1) for term in terms])
    padding = -vector.shape[0] % (8 * LANES)
    vector = jnp.pad(vector, (0, padding)).reshape(-1, LANES)
    for stage in range(1, stages - 1):
        back_ready, back_held = scatter_far(back_ready, back_held, stage)
    out_pieces = double(out_pieces, 0)
    side_sum = add_exchanged(side_sum, 1)
    axes = [(axis, bit) for axis in ("seq", "batch") for bit in bits_of(lax.axis_size(axis))]
    vector = vector + exchange(vector, *axes.pop(0))
    back_held["arrived"], vector, out_pieces, side_sum = together(
        back_held["arrived"], vector, out_pieces, side_sum
    )
    for stage in range(1, stages):
        side_sum = add_exchanged(side_sum, 1 << stage)
        out_pieces = double(out_pieces, stage)
    in_weight_grad = assemble(pieces, side_sum, dims).T
    while axes:
        vector = vector + exchange(vector, *axes.pop(0))
    vector = vector.reshape(-1)
    normed_grad = scatter_end(back_held)
    cot_row = cotangent[0].astype(f32)
    gained = norm_gain * normed_grad
    slope = inverse * inverse * inverse * jnp.mean(gained * tokens_row, axis=-1, keepdims=True)
    input_grad = cot_row + inverse * gained - tokens_row * slope
    own_scale = lax.dynamic_slice_in_dim(scale, mine * tok_rows, tok_rows, 0)[:, None]
    block_out = (tokens_row + own_scale * scatter_end(out_held)).astype(bf16)
    out_weight_grad = assemble_out(place, out_pieces, per_plane)

    parts, offset = [], 0
    for term in terms:
        parts.append(vector[offset : offset + term.size].reshape(term.shape))
        offset += term.size
    own_terms, shared_terms, norm_gain_grad, head_terms = parts
    conv_terms = jnp.concatenate([own_terms[: taps + 1], shared_terms], axis=1)
    return (
        block_out[None],
        input_grad[None],
        norm_gain_grad,
        in_weight_grad,
        conv_terms[:taps],
        conv_terms[taps],
        head_terms[:, 0],
        head_terms[:, 1],
        head_terms[:, 2],
        own_terms[taps + 1],
        out_weight_grad,
    )


def solution(mesh):
    placed = (
        P("batch", "seq", None),
        P(),
        P("batch", None),
        P(),
        P(),
        P(),
        P(),
        P(),
        P(),
        P("batch", None),
        P("batch", "seq", None),
    )
    return jax.shard_map(
        body,
        mesh=mesh,
        in_specs=placed,
        out_specs=(
            P("batch", "seq", None),
            P("batch", "seq", None),
            P(),
            P("batch", None),
            P(),
            P(),
            P(),
            P(),
            P(),
            P(),
            P("batch", None),
        ),
        check_vma=False,
    )
```

```python
import functools

import jax
import jax.numpy as jnp
from jax import lax
from jax.experimental import pallas as pl
from jax.experimental.pallas import tpu as pltpu
from jax.sharding import PartitionSpec as P

GROUP = 256
LANES = 128
HALF = GROUP // 2
HALO = 8
LOG2E = 1.4426950408889634
epsilon = 1e-05
f32 = jnp.float32
bf16 = jnp.bfloat16
MIB = 2**20


def exchange(value, axis, distance):
    count = lax.axis_size(axis)
    return lax.ppermute(value, axis, [(source, source ^ distance) for source in range(count)])


def bits_of(count):
    return [1 << k for k in range(count.bit_length() - 1)]


def placed_order(count):
    return [2 * k for k in range(count // 2)] + [2 * k + 1 for k in range(count // 2)]


def together(*values):
    return lax.optimization_barrier(values)


def far_orders():
    far = bits_of(lax.axis_size("seq"))[1:]
    return far, far[::-1]


def gather_start(value):
    half = value.shape[0] // 32 * 16
    return tuple({"base": part, "fresh": None, "near": []} for part in (value[:half], value[half:]))


def gather_stage(held, stage, late=False):
    grown = []
    for half, order in zip(held, far_orders()):
        base, fresh, near = half["base"], half["fresh"], list(half["near"])
        if stage >= 1:
            merged = base if stage == len(order) else jnp.concatenate([base, fresh], axis=0)
            if not late:
                near.append(exchange(merged if stage == 1 else fresh, "seq", 1))
            elif stage == len(order):
                near = [exchange(base, "seq", 1), exchange(fresh, "seq", 1)]
            base = merged
        if stage < len(order):
            fresh = exchange(base, "seq", order[stage])
        grown.append({"base": base, "fresh": fresh, "near": near})
    return tuple(grown)


def gather_stages():
    return len(bits_of(lax.axis_size("seq")))


def gathered(held):
    arrays, table = [], {}
    for number, (half, order) in enumerate(zip(held, far_orders())):
        indices = [0]
        for bit in order:
            indices += [index | bit for index in indices]
        middle = len(indices) // 2
        groups = [(half["base"], indices[:middle]), (half["fresh"], indices[middle:])]
        bounds = [0] + [2 << k for k in range(len(order))]
        if len(half["near"]) < len(order):
            bounds = [0, middle, len(indices)]
        for value, first, last in zip(half["near"], bounds, bounds[1:]):
            groups.append((value, [index | 1 for index in indices[first:last]]))
        for value, members in groups:
            rows = value.shape[0] // len(members)
            for turn, index in enumerate(members):
                table[number, index] = (len(arrays), turn * rows, rows)
            arrays.append(value)
    return arrays, table


def token_pieces(held):
    arrays, table = gathered(held)
    indices = range(lax.axis_size("seq"))
    return arrays, tuple(table[half, index] for index in indices for half in range(2))


def gather_all(value):
    held = gather_start(value)
    for stage in range(gather_stages()):
        held = gather_stage(held, stage)
    return held


def scatter_places(count):
    far = bits_of(count)[1:]
    table = {}
    row = {}
    for near in (1, 0):
        for sent in (True, False):
            for half, order in enumerate((far, far[::-1])):
                members = [0]
                for bit in order[:0:-1]:
                    members += [member | bit for member in members]
                for member in members:
                    index = member | near | (order[0] if sent else 0)
                    array = 0 if near else (1 + half if sent else 3)
                    table[index * 2 + half] = (array, row.get(array, 0))
                    row[array] = row.get(array, 0) + GROUP
    return tuple(table[k] for k in range(2 * count))


def scatter_shapes(count, columns):
    blocks = (count, count // 4, count // 4, count // 2)
    return [jax.ShapeDtypeStruct((part * GROUP, columns), bf16) for part in blocks]


def scatter_near(product, parts, sent):
    arriving = exchange(sent, "seq", 1)
    first, second, kept = parts
    rows = first.shape[0]

    def summed(part, row):
        return (product(part) + arriving[row : row + part.shape[0]].astype(f32)).astype(bf16)

    sends = (summed(first, 0), summed(second, rows))
    sends, kept = together(sends, kept)
    return sends, {"kept": summed(kept, 2 * rows), "arrived": ([], [])}


def scatter_rows(held, half, first, last):
    top = half * (held["kept"].shape[0] // 2)
    total = held["kept"][top + first : top + last].astype(f32)
    for value in held["arrived"][half]:
        total = total + value[first:last].astype(f32)
    return total


def scatter_far(sends, held, stage):
    orders = far_orders()
    arrived = tuple(
        [*held["arrived"][half], exchange(sends[half], "seq", orders[half][stage])]
        for half in range(2)
    )
    held = {"kept": held["kept"], "arrived": arrived}
    rows = sends[0].shape[0]
    if stage + 1 == len(orders[0]):
        return (), held
    ready = tuple(
        scatter_rows(held, half, rows // 2, rows).astype(bf16) for half in range(2)
    )
    return ready, held


def scatter_end(held):
    rows = held["arrived"][0][-1].shape[0]
    return jnp.concatenate([scatter_rows(held, half, 0, rows) for half in range(2)], axis=0)


def pairs_of(bits):
    odd = len(bits) % 2
    return [bits[:odd]] * odd + [bits[k : k + 2] for k in range(odd, len(bits), 2)]


def add_exchanged(value, axis, bits):
    total = value.astype(f32) + exchange(value, axis, bits[0]).astype(f32)
    if len(bits) == 2:
        other = exchange(value, axis, bits[1]).astype(f32)
        total = total + (other + exchange(value, axis, bits[0] | bits[1]).astype(f32))
    return total.astype(value.dtype)


def plane_pairs(ahead):
    planes, count = lax.axis_size("batch"), lax.axis_size("seq")
    per = count // planes
    pairs = []
    for owner in range(planes):
        for piece in range(planes):
            for k in range(per):
                holder = owner * count + piece * per + k
                user = (piece + ahead) % planes * count + owner * per + k
                pairs.append((holder, user))
    return pairs


def rows_from_owner(out_weight, width):
    per = lax.axis_size("seq") // lax.axis_size("batch")
    plane, mine = lax.axis_index("batch"), lax.axis_index("seq")
    rows = lax.dynamic_slice_in_dim(out_weight, mine % per * width, width, 0)
    return lax.psum(jnp.where(plane == mine // per, rows, jnp.zeros_like(rows)), "batch")


def to_owner(summed):
    return lax.ppermute(
        summed, ("batch", "seq"), [(user, holder) for holder, user in plane_pairs(0)]
    )


def grow_groups():
    bits = bits_of(lax.axis_size("seq"))
    order = bits[1:] + [1]
    return [order[k : k + 2] for k in range(0, len(order), 2)]


def grow(held, bits):
    parts = [held, exchange(held, "seq", bits[0])]
    if len(bits) == 2:
        parts += [exchange(held, "seq", bits[1]), exchange(held, "seq", bits[0] | bits[1])]
    return jnp.concatenate(parts, axis=0)


def step_values(raw):
    small = jnp.exp(-jnp.abs(raw))
    step = jnp.maximum(raw, 0.0) + jnp.log1p(small)
    sig = jnp.where(raw >= 0, 1.0, small) / (1.0 + small)
    tiny = raw < -20.0
    log_step = jnp.where(tiny, raw, jnp.log(step))
    ratio = jnp.where(tiny, 1.0, sig / step)
    return step, sig, log_step, ratio


def dot(a, b):
    return jnp.dot(a, b, preferred_element_type=f32)


def dot_nt(a, b):
    return lax.dot_general(a, b, (((1,), (1,)), ((), ())), preferred_element_type=f32)


def dot_tn(a, b):
    return lax.dot_general(a, b, (((0,), (0,)), ((), ())), preferred_element_type=f32)


def sigmoid(value):
    return 0.5 * jnp.tanh(0.5 * value) + 0.5


def silu_slope(value):
    sig = sigmoid(value)
    active = value * sig
    return active, sig + active * (1.0 - sig)


def split_parts(value, count):
    parts = []
    for _ in range(count):
        part = value.astype(bf16)
        parts.append(part)
        value = value - part.astype(f32)
    return parts


def sum_along(rows, order):
    parts = jnp.concatenate([part.astype(f32) for part in split_parts(rows, 3)], axis=0)
    total = dot(parts.astype(bf16), order)
    return total[:8] + total[8:16] + total[16:24]


def to_columns(rows):
    stacked = jnp.concatenate(rows, axis=0)
    missing = LANES - stacked.shape[0]
    return jnp.concatenate([stacked, jnp.zeros((missing, GROUP), f32)], axis=0).T


def spread_heads(value, first, heads, size):
    rows = value.shape[0]
    return jnp.concatenate(
        [jnp.broadcast_to(value[:, first + h : first + h + 1], (rows, size)) for h in range(heads)],
        axis=1,
    )


def head_ones(width, size):
    row = lax.broadcasted_iota(jnp.int32, (8, width), 0)
    column = lax.broadcasted_iota(jnp.int32, (8, width), 1)
    return (column // size == row).astype(f32).astype(bf16)


def sum_lanes(value):
    return dot_nt(jnp.ones((8, value.shape[1]), bf16), value.astype(bf16))


def ones_where(condition):
    return jnp.where(condition, 1.0, 0.0).astype(bf16)


def order_indices(length):
    row = lax.broadcasted_iota(jnp.int32, (length, length), 0)
    column = lax.broadcasted_iota(jnp.int32, (length, length), 1)
    return row, column


def fetch(arrays, table, which, target, semaphore):
    for index, (array, row, rows) in enumerate(table):

        @pl.when(which == index)
        def _():
            pltpu.make_async_copy(arrays[array].at[pl.ds(row, rows)], target, semaphore).start()


def fetched(arrays, table, buffer, semaphores, order, blocks=1):
    step = pl.program_id(0)
    slot, other = lax.rem(step, 2), lax.rem(step + 1, 2)

    def start(step, slot):
        for k in range(blocks):
            target = buffer.at[slot, pl.ds(k * GROUP, GROUP)]
            fetch(arrays, table, order(step * blocks + k), target, semaphores.at[slot])

    @pl.when(step == 0)
    def _():
        start(0, 0)

    @pl.when(step + 1 < pl.num_programs(0))
    def _():
        start(step + 1, other)

    for k in range(blocks):
        source = arrays[0].at[pl.ds(0, GROUP)]
        target = buffer.at[slot, pl.ds(k * GROUP, GROUP)]
        pltpu.make_async_copy(source, target, semaphores.at[slot]).wait()
    return buffer[slot]


def store(source, targets, table, which, semaphore):
    for index, (array, row) in enumerate(table):

        @pl.when(which == index)
        def _():
            target = targets[array].at[pl.ds(row, GROUP)]
            pltpu.make_async_copy(source, target, semaphore).start()


def stored(buffer, targets, semaphores, slot):
    target = targets[0].at[pl.ds(0, GROUP)]
    pltpu.make_async_copy(buffer.at[slot], target, semaphores.at[slot]).wait()


def in_time(place, block):
    return ((block // 2) ^ place) * 2 + block % 2


def forward_kernel(dims, table, given, place_ref, *refs):
    heads, size, states, count = dims
    width = heads * size
    conv_cols = width + 2 * states
    arrays, refs = refs[:given], refs[given:]
    w_ref, conv_w_ref, conv_b_ref, step_ref, rows_ref = refs[:5]
    conv_in_ref, active_ref, slope_ref, gate_act_ref, gate_slope_ref = refs[5:10]
    raw_ref, ssd_ref, start_ref, scaled_ref, square_ref, normed_ref = refs[10:16]
    targets = refs[16:20]
    state, padded, order, barred, buffer, semaphores, placed, out_semaphores = refs[20:]
    turn = pl.program_id(0)
    slot = lax.rem(turn, 2)

    @pl.when(turn == 0)
    def _():
        state[...] = jnp.zeros_like(state)
        padded[0:HALO] = jnp.zeros_like(padded[0:HALO])
        row, column = order_indices(GROUP)
        order[...] = ones_where(row <= column)
        row, column = order_indices(HALF)
        barred[...] = jnp.where(row >= column, 0.0, -1e30)

    @pl.when(turn >= 2)
    def _():
        stored(placed, targets, out_semaphores, slot)

    normed = fetched(
        arrays, table, buffer, semaphores, lambda step: in_time(place_ref[0], step)
    )
    normed_ref[...] = normed
    projected = dot(normed, w_ref[...])
    conv_in = projected[:, width : width + conv_cols].astype(bf16)
    conv_in_ref[...] = conv_in
    padded[HALO : HALO + GROUP] = conv_in.astype(f32)
    conv_w = conv_w_ref[...]
    taps = conv_w.shape[0]
    pre = conv_b_ref[...]
    for k in range(taps):
        top = HALO - (taps - 1) + k
        pre = pre + conv_w[k : k + 1] * padded[top : top + GROUP]
    padded[0:HALO] = padded[GROUP : GROUP + HALO]
    active, slope = silu_slope(pre)
    active = active.astype(bf16)
    active_ref[...] = active
    slope_ref[...] = slope.astype(bf16)
    signal = active[:, :width]
    entry = active[:, width : width + states]
    readout = active[:, width + states :]
    signal_wide = signal.astype(f32)

    lanes = pltpu.roll(
        projected[:, width + conv_cols :], lax.rem(LANES - heads * place_ref[0], LANES), 1
    )
    raw = lanes.T[:8]
    raw_ref[0] = raw
    step, _, log_step, _ = step_values(raw + step_ref[0:8, 0:1])
    running = sum_along(step * step_ref[8:16, 0:1], order[...])
    later = running - log_step
    total = running[:, GROUP - 1 :]
    columns = to_columns([running * LOG2E, jnp.exp(running), jnp.exp(total - later)])
    later = later * LOG2E
    early_wide = spread_heads(columns, 8, heads, size)
    tail_wide = spread_heads(columns, 16, heads, size)
    first, second = slice(0, HALF), slice(HALF, GROUP)
    scores = dot_nt(readout[first], entry[first])
    later_scores = dot_nt(readout[second], entry)
    within = []
    for h in range(heads):
        part = signal[:, h * size : (h + 1) * size]
        begin, end = columns[first, h : h + 1], columns[second, h : h + 1]
        row_first, row_second = later[h : h + 1, first], later[h : h + 1, second]
        near = jnp.exp2(begin - row_first + barred[...]) * scores
        full = jnp.exp2(end - row_first) * later_scores[:, first]
        last = jnp.exp2(end - row_second + barred[...]) * later_scores[:, second]
        both = jnp.concatenate([full.astype(bf16), last.astype(bf16)], axis=1)
        within.append(
            jnp.concatenate([dot(near.astype(bf16), part[first]), dot(both, part)], axis=0)
        )
    start = state[...]
    start_low = start.astype(bf16)
    start_ref[0] = start_low
    carried = dot(readout, start_low) * early_wide
    ssd = jnp.concatenate(within, axis=1) + carried + rows_ref[0:1] * signal_wide
    tail = (signal_wide * tail_wide).astype(bf16)
    state[...] = start * early_wide[GROUP - 1 :] + dot_tn(entry, tail)

    gate_act, gate_slope = silu_slope(projected[:, :width])
    gate_act_ref[...] = gate_act.astype(bf16)
    gate_slope_ref[...] = gate_slope.astype(bf16)
    ssd_ref[...] = ssd
    gated = ssd * gate_act
    scaled = (gated * rows_ref[1:2]).astype(bf16)
    scaled_ref[...] = scaled
    square_ref[0] = sum_lanes(gated * gated)
    placed[slot] = scaled
    where = in_time(place_ref[0], turn)
    store(placed.at[slot], targets, scatter_places(count), where, out_semaphores.at[slot])

    @pl.when(turn == pl.num_programs(0) - 1)
    def _():
        for other in range(2):
            stored(placed, targets, out_semaphores, other)


def time_estimate(microseconds, accessed):
    return pl.CostEstimate(
        flops=int(microseconds * 1.1e9), bytes_accessed=int(accessed), transcendentals=0
    )


def fixed(shape):
    return pl.BlockSpec(shape, lambda turn, place: (0,) * len(shape), pipeline_mode=pl.Buffered(1))


def anywhere(values):
    return [pl.BlockSpec(memory_space=pltpu.HBM)] * len(values)


def run_forward(place, pieces, params, dims):
    heads, size, states, count = dims
    arrays, table = pieces
    dim = params[0].shape[0]
    width, conv_cols = heads * size, params[1].shape[1]
    blocks = len(table)
    tokens = blocks * GROUP

    def moving(columns):
        return pl.BlockSpec((GROUP, columns), lambda turn, place: (turn, 0))

    def rows_of_block(height, columns):
        return pl.BlockSpec((1, height, columns), lambda turn, place: (turn, 0, 0))

    results = pl.pallas_call(
        functools.partial(forward_kernel, dims, table, len(arrays)),
        grid_spec=pltpu.PrefetchScalarGridSpec(
            num_scalar_prefetch=1,
            grid=(blocks,),
            in_specs=[*anywhere(arrays), *[fixed(param.shape) for param in params]],
            out_specs=[
                moving(conv_cols),
                moving(conv_cols),
                moving(conv_cols),
                moving(width),
                moving(width),
                rows_of_block(8, GROUP),
                moving(width),
                rows_of_block(states, width),
                moving(width),
                rows_of_block(8, GROUP),
                moving(dim),
                *anywhere(range(4)),
            ],
            scratch_shapes=[
                pltpu.VMEM((states, width), f32),
                pltpu.VMEM((HALO + GROUP, conv_cols), f32),
                pltpu.VMEM((GROUP, GROUP), bf16),
                pltpu.VMEM((HALF, HALF), f32),
                pltpu.VMEM((2, GROUP, dim), bf16),
                pltpu.SemaphoreType.DMA((2,)),
                pltpu.VMEM((2, GROUP, width), bf16),
                pltpu.SemaphoreType.DMA((2,)),
            ],
        ),
        out_shape=[
            jax.ShapeDtypeStruct((tokens, conv_cols), bf16),
            jax.ShapeDtypeStruct((tokens, conv_cols), bf16),
            jax.ShapeDtypeStruct((tokens, conv_cols), bf16),
            jax.ShapeDtypeStruct((tokens, width), bf16),
            jax.ShapeDtypeStruct((tokens, width), bf16),
            jax.ShapeDtypeStruct((blocks, 8, GROUP), f32),
            jax.ShapeDtypeStruct((tokens, width), f32),
            jax.ShapeDtypeStruct((blocks, states, width), bf16),
            jax.ShapeDtypeStruct((tokens, width), bf16),
            jax.ShapeDtypeStruct((blocks, 8, GROUP), f32),
            jax.ShapeDtypeStruct((tokens, dim), bf16),
            *scatter_shapes(count, width),
        ],
        compiler_params=pltpu.CompilerParams(vmem_limit_bytes=60 * MIB),
        cost_estimate=time_estimate(blocks * 3.0, tokens * (4 * dim + 24 * width)),
        name="forward_blocks",
    )(place, *arrays, *params)
    return results[:11], results[11:]


def out_grad_kernel(table, given, place_ref, *refs):
    arrays, refs = refs[:given], refs[given:]
    scaled_ref, out_rows_ref, out_grad_ref, slope_ref, cot_ref, buffer, semaphores = refs
    place = place_ref[0]
    cot = fetched(arrays, table, buffer, semaphores, lambda block: in_time(place, block), 2)
    cot_ref[...] = cot
    out_grad = dot_nt(cot, out_rows_ref[...])
    out_grad_ref[...] = out_grad
    for block in range(2):
        here = slice(block * GROUP, (block + 1) * GROUP)
        slope_ref[block] = sum_lanes(out_grad[here] * scaled_ref[here].astype(f32))


def run_out_grad(place, cots, scaled, out_rows):
    arrays, table = cots
    width, dim = out_rows.shape
    blocks = len(table)
    tokens = blocks * GROUP
    return pl.pallas_call(
        functools.partial(out_grad_kernel, table, len(arrays)),
        grid_spec=pltpu.PrefetchScalarGridSpec(
            num_scalar_prefetch=1,
            grid=(blocks // 2,),
            in_specs=[
                *anywhere(arrays),
                pl.BlockSpec((2 * GROUP, width), lambda turn, place: (turn, 0)),
                fixed(out_rows.shape),
            ],
            out_specs=[
                pl.BlockSpec((2 * GROUP, width), lambda turn, place: (turn, 0)),
                pl.BlockSpec((2, 8, GROUP), lambda turn, place: (turn, 0, 0)),
                pl.BlockSpec((2 * GROUP, dim), lambda turn, place: (turn, 0)),
            ],
            scratch_shapes=[pltpu.VMEM((2, 2 * GROUP, dim), bf16), pltpu.SemaphoreType.DMA((2,))],
        ),
        out_shape=[
            jax.ShapeDtypeStruct((tokens, width), f32),
            jax.ShapeDtypeStruct((blocks, 8, GROUP), f32),
            jax.ShapeDtypeStruct((tokens, dim), bf16),
        ],
        compiler_params=pltpu.CompilerParams(vmem_limit_bytes=60 * MIB),
        cost_estimate=time_estimate(12, tokens * (4 * dim + 6 * width)),
        name="out_grad",
    )(place, *arrays, scaled, out_rows)


def backward_kernel(dims, place_ref, *refs):
    heads, size, states, count = dims
    width = heads * size
    conv_cols = width + 2 * states
    conv_in_ref, active_ref, slope_ref, gate_act_ref, gate_slope_ref = refs[:5]
    raw_ref, ssd_ref, start_ref, out_grad_ref, norm_ref = refs[5:10]
    conv_w_ref, step_ref, rows_ref = refs[10:13]
    out_ref, targets = refs[13], refs[14:18]
    gain_ref, conv_wg_ref, conv_bg_ref, small_ref = refs[18:22]
    state, pre_grads, order, back_order, barred, placed, semaphores = refs[22:29]
    skip_ref, bias_ref, rate_ref = refs[29:]
    sums = (gain_ref, conv_wg_ref, conv_bg_ref, skip_ref, bias_ref, rate_ref)
    taps = conv_w_ref.shape[0]
    turn = pl.program_id(0)
    slot = lax.rem(turn, 2)

    @pl.when(turn >= 2)
    def _():
        stored(placed, targets, semaphores, slot)

    @pl.when(pl.program_id(0) == 0)
    def _():
        state[...] = jnp.zeros_like(state)
        pre_grads[0:HALO] = jnp.zeros_like(pre_grads[0:HALO])
        for total in sums:
            total[...] = jnp.zeros_like(total)
        row, column = order_indices(GROUP)
        order[...] = ones_where(row <= column)
        back_order[...] = ones_where(row >= column)
        row, column = order_indices(HALF)
        barred[...] = jnp.where(row <= column, 0.0, -1e30)

    gate_act, ssd, out_grad = gate_act_ref[...].astype(f32), ssd_ref[...], out_grad_ref[...]
    norms = norm_ref[0].T
    scale, slope = norms[:, 0:1], norms[:, 1:2]
    gated = ssd * gate_act
    gain_ref[...] += jnp.sum(out_grad * (gated * scale), axis=0, keepdims=True)
    gated_grad = out_grad * (rows_ref[1:2] * scale) - gated * slope
    grad_low = (gated_grad * gate_act).astype(bf16)
    gate_grad = (gated_grad * ssd * gate_slope_ref[...].astype(f32)).astype(bf16)
    out_ref[:, :width] = gate_grad
    placed[slot, :, :width] = gate_grad
    ssd_grad = grad_low.astype(f32)

    raw = raw_ref[0] + step_ref[0:8, 0:1]
    rate = step_ref[8:16, 0:1]
    step, sig, log_step, ratio = step_values(raw)
    decay = step * rate
    running = sum_along(decay, order[...])
    later = running - log_step
    total = running[:, GROUP - 1 :]
    columns = to_columns([later * LOG2E, jnp.exp(running), jnp.exp(total - later)])
    running = running * LOG2E
    early_wide = spread_heads(columns, 8, heads, size)
    tail_wide = spread_heads(columns, 16, heads, size)

    signal = active_ref[:, :width]
    entry = active_ref[:, width : width + states]
    readout = active_ref[:, width + states :]
    signal_wide = signal.astype(f32)
    start_low = start_ref[0]
    end_grad = state[...]
    end_low = end_grad.astype(bf16)
    first, second = slice(0, HALF), slice(HALF, GROUP)
    scores = dot_nt(entry[first], readout)
    later_scores = dot_nt(entry[second], readout[second])
    near_grad, far_grad, last_grad = 0.0, 0.0, 0.0
    within = []
    for h in range(heads):
        part, grad = signal[:, h * size : (h + 1) * size], grad_low[:, h * size : (h + 1) * size]
        begin, end = columns[first, h : h + 1], columns[second, h : h + 1]
        row_first, row_second = running[h : h + 1, first], running[h : h + 1, second]
        near = jnp.exp2(row_first - begin + barred[...])
        full = jnp.exp2(row_second - begin)
        last = jnp.exp2(row_second - end + barred[...])
        both = jnp.concatenate(
            [
                (near * scores[:, first]).astype(bf16),
                (full * scores[:, second]).astype(bf16),
            ],
            axis=1,
        )
        final = (last * later_scores).astype(bf16)
        within.append(jnp.concatenate([dot(both, grad), dot(final, grad[second])], axis=0))
        cross = dot_nt(part[first], grad)
        near_grad = near_grad + cross[:, first] * near
        far_grad = far_grad + cross[:, second] * full
        last_grad = last_grad + dot_nt(part[second], grad[second]) * last
    tail_grad = tail_wide * dot(entry, end_low)
    signal_grad = jnp.concatenate(within, axis=1) + tail_grad
    score_first = jnp.concatenate([near_grad, far_grad], axis=1).astype(bf16)
    score_second = last_grad.astype(bf16)
    tail = (signal_wide * tail_wide).astype(bf16)
    head_grad = (ssd_grad * early_wide).astype(bf16)
    entry_grad = jnp.concatenate(
        [dot(score_first, readout), dot(score_second, readout[second])], axis=0
    ) + dot_nt(tail, end_low)
    readout_grad = dot_tn(score_first, entry[first]) + dot_nt(head_grad, start_low)
    readout_last = readout_grad[second] + dot_tn(score_second, entry[second])
    total_wide = early_wide[GROUP - 1 :]
    state[...] = end_grad * total_wide + dot_tn(readout, head_grad)

    skip = rows_ref[0:1]
    ones = head_ones(width, size)
    column_part = signal_wide * signal_grad
    row_part = ssd_grad * (ssd - skip * signal_wide)
    end_part = jnp.sum(signal_wide * tail_grad, axis=0, keepdims=True) + total_wide * jnp.sum(
        start_low.astype(f32) * end_grad, axis=0, keepdims=True
    )

    def head_sums(value, parts):
        return sum(dot_nt(ones, part) for part in split_parts(value, parts))

    end_rows = head_sums(jnp.broadcast_to(end_part, (8, width)), 2)[:, 0:1]
    decay_grad = sum_along(head_sums(row_part - column_part, 2), back_order[...]) + end_rows
    raw_grad = head_sums(column_part, 1) * ratio + decay_grad * rate * sig
    skip_ref[...] += jnp.sum(ssd_grad * signal_wide, axis=0, keepdims=True)
    bias_ref[...] += raw_grad
    rate_ref[...] += decay_grad * decay
    raw_low = pltpu.roll(to_columns([raw_grad]), heads * place_ref[0], 1).astype(bf16)
    out_ref[:, width + conv_cols :] = raw_low
    placed[slot, :, width + conv_cols :] = raw_low

    pre_grads[GROUP : GROUP + HALO] = pre_grads[0:HALO]
    pre_grads[0:GROUP, :width] = (signal_grad + skip * ssd_grad) * slope_ref[:, :width].astype(f32)
    sides = slope_ref[:, width:].astype(f32)
    pre_grads[0:GROUP, width : width + states] = entry_grad * sides[:, :states]
    pre_grads[0:HALF, width + states :] = readout_grad[first] * sides[first, states:]
    pre_grads[HALF:GROUP, width + states :] = readout_last * sides[second, states:]
    conv_w = conv_w_ref[...]
    conv_in = conv_in_ref[...].astype(f32)
    conv_grad = 0.0
    for k in range(taps):
        ahead = taps - 1 - k
        shifted = pre_grads[ahead : ahead + GROUP]
        conv_grad = conv_grad + conv_w[k : k + 1] * shifted
        conv_wg_ref[k : k + 1] += jnp.sum(shifted * conv_in, axis=0, keepdims=True)
        if ahead == 0:
            conv_bg_ref[...] += jnp.sum(shifted, axis=0, keepdims=True)
    conv_low = conv_grad.astype(bf16)
    out_ref[:, width : width + conv_cols] = conv_low
    placed[slot, :, width : width + conv_cols] = conv_low

    where = in_time(place_ref[0], pl.num_programs(0) - 1 - turn)
    store(placed.at[slot], targets, scatter_places(count), where, semaphores.at[slot])

    @pl.when(turn == pl.num_programs(0) - 1)
    def _():
        skips = head_sums(jnp.broadcast_to(skip_ref[...], (8, width)), 3)[:, 0:1]
        place_of = lax.broadcasted_iota(jnp.int32, small_ref.shape, 1)
        small = jnp.where(place_of == 0, jnp.sum(bias_ref[...], axis=1, keepdims=True), skips)
        rates = jnp.sum(rate_ref[...], axis=1, keepdims=True)
        small_ref[...] = jnp.where(place_of == 1, rates, small)
        for other in range(2):
            stored(placed, targets, semaphores, other)


def run_backward(place, values, params, dims):
    heads, size, states, count = dims
    conv_cols, width = values[0].shape[1], heads * size
    tokens = values[0].shape[0]
    blocks = tokens // GROUP
    last = blocks - 1
    out_cols = width + conv_cols + LANES

    def moving(columns):
        return pl.BlockSpec((GROUP, columns), lambda turn, place: (last - turn, 0))

    def rows_of_block():
        return pl.BlockSpec((1, 8, GROUP), lambda turn, place: (last - turn, 0, 0))

    sums = [(1, width), params[0].shape, (1, conv_cols), (8, LANES)]
    return pl.pallas_call(
        functools.partial(backward_kernel, dims),
        grid_spec=pltpu.PrefetchScalarGridSpec(
            num_scalar_prefetch=1,
            grid=(blocks,),
            in_specs=[
                moving(conv_cols),
                moving(conv_cols),
                moving(conv_cols),
                moving(width),
                moving(width),
                rows_of_block(),
                moving(width),
                pl.BlockSpec((1, states, width), lambda turn, place: (last - turn, 0, 0)),
                moving(width),
                rows_of_block(),
                *[fixed(param.shape) for param in params],
            ],
            out_specs=[
                moving(out_cols),
                *anywhere(range(4)),
                *[fixed(shape) for shape in sums],
            ],
            scratch_shapes=[
                pltpu.VMEM((states, width), f32),
                pltpu.VMEM((GROUP + HALO, conv_cols), f32),
                pltpu.VMEM((GROUP, GROUP), bf16),
                pltpu.VMEM((GROUP, GROUP), bf16),
                pltpu.VMEM((HALF, HALF), f32),
                pltpu.VMEM((2, GROUP, out_cols), bf16),
                pltpu.SemaphoreType.DMA((2,)),
                pltpu.VMEM((1, width), f32),
                pltpu.VMEM((8, GROUP), f32),
                pltpu.VMEM((8, GROUP), f32),
            ],
        ),
        out_shape=[
            jax.ShapeDtypeStruct((tokens, out_cols), bf16),
            *scatter_shapes(count, out_cols),
        ]
        + [jax.ShapeDtypeStruct(shape, f32) for shape in sums],
        compiler_params=pltpu.CompilerParams(vmem_limit_bytes=60 * MIB),
        cost_estimate=time_estimate(blocks * 3.5, tokens * 40 * width),
        name="backward_blocks",
    )(place, *values, *params)


def widen_kernel(place_ref, piece_ref, out_ref):
    out_ref[...] = piece_ref[0].astype(f32)


def assemble_out(place, pieces, per):
    count, size, dim = pieces.shape
    groups = count // per

    def source(turn, place):
        relative = (turn % groups * per + turn // groups) ^ place[0]
        return ((relative & 1) * (count // 2) + (relative >> 1), 0, 0)

    return pl.pallas_call(
        widen_kernel,
        grid_spec=pltpu.PrefetchScalarGridSpec(
            num_scalar_prefetch=1,
            grid=(count,),
            in_specs=[pl.BlockSpec((1, size, dim), source)],
            out_specs=pl.BlockSpec((size, dim), lambda turn, place: (turn, 0)),
        ),
        out_shape=jax.ShapeDtypeStruct((count * size, dim), f32),
        cost_estimate=time_estimate(5, count * size * dim * 6),
        name="assemble_out_weight_grad",
    )(place, pieces)


def assemble_kernel(dims, lasting, pieces_ref, side_ref, out_ref):
    heads, size, states, count = dims
    width = heads * size
    inner = count * width
    for device in range(count):
        columns = pieces_ref[device].astype(f32).T
        out_ref[device * width : (device + 1) * width] = columns[:width]
        out_ref[inner + device * width : inner + (device + 1) * width] = columns[width:]
    out_ref[2 * inner :] = side_ref[...].astype(f32).T[:lasting]


def assemble(pieces, side, dims):
    heads, size, states, count = dims
    _, rows, columns = pieces.shape
    tile = LANES if rows % LANES == 0 else rows
    lasting = 2 * states + count * heads
    out_rows = 2 * count * heads * size + lasting
    return pl.pallas_call(
        functools.partial(assemble_kernel, dims, lasting),
        grid=(rows // tile,),
        in_specs=[
            pl.BlockSpec((count, tile, columns), lambda turn: (0, turn, 0)),
            pl.BlockSpec((tile, side.shape[1]), lambda turn: (turn, 0)),
        ],
        out_specs=pl.BlockSpec((out_rows, tile), lambda turn: (0, turn)),
        out_shape=jax.ShapeDtypeStruct((out_rows, rows), f32),
        compiler_params=pltpu.CompilerParams(vmem_limit_bytes=60 * MIB),
        cost_estimate=time_estimate(8, out_rows * rows * 6),
        name="assemble_in_weight_grad",
    )(pieces, side)


def body(
    tokens,
    norm_gain,
    in_weight,
    conv_weight,
    conv_bias,
    dt_bias,
    decay_log,
    skip_scale,
    gate_gain,
    out_weight,
    cotangent,
):
    count, mine = lax.axis_size("seq"), lax.axis_index("seq")
    place = mine.astype(jnp.int32).reshape(1)
    inner, all_heads, conv_all = gate_gain.shape[0], dt_bias.shape[0], conv_bias.shape[0]
    size, states = inner // all_heads, (conv_all - inner) // 2
    heads, width = all_heads // count, inner // count
    dims = (heads, size, states, count)
    shared = 2 * states
    conv_cols = width + shared
    tok_rows = tokens.shape[1]
    per_plane = out_weight.shape[0] // width

    def own(vector, per, first=0):
        return lax.dynamic_slice_in_dim(vector, first + mine * per, per, vector.ndim - 1)

    def own_conv(array, first=0):
        return jnp.concatenate(
            [own(array, width, first), array[..., first + inner : first + conv_all]], axis=-1
        )

    tokens_row = tokens[0].astype(f32)
    inverse = lax.rsqrt(jnp.mean(tokens_row * tokens_row, axis=-1, keepdims=True) + epsilon)
    normed_own = (tokens_row * inverse * norm_gain).astype(bf16)
    step_own = own(in_weight, heads, inner + conv_all)
    w_own = jnp.concatenate(
        [
            own(in_weight, width),
            own_conv(in_weight, inner),
            lax.dynamic_update_slice_in_dim(
                jnp.zeros((step_own.shape[0], LANES), bf16), step_own, mine * heads, 1
            ),
        ],
        axis=1,
    )
    w_cols = lax.all_gather(w_own, "batch", axis=0, tiled=True)
    stages = gather_stages()
    held = gather_stage(gather_stage(gather_start(normed_own), 0), 1)
    held, cots = together(held, gather_start(cotangent[0]))
    cots = gather_stage(cots, 0)
    for stage in range(2, stages):
        held = gather_stage(held, stage)
    w_cols, held, cots, out_owned = together(w_cols, held, cots, out_weight)
    cots = gather_stage(cots, 1)
    out_rows = rows_from_owner(out_owned, width)

    conv_w, conv_b = own_conv(conv_weight), own_conv(conv_bias)[None]
    per_head = jnp.stack([own(dt_bias, heads), -jnp.exp(own(decay_log, heads))])
    per_head = jnp.pad(per_head, ((0, 0), (0, 8 - heads))).reshape(16, 1)
    step_rows = jnp.broadcast_to(per_head, (16, LANES))
    gain_own = own(gate_gain, width)[None]
    rows = jnp.concatenate(
        [jnp.repeat(own(skip_scale, heads), size)[None], gain_own, jnp.zeros((6, width), f32)],
        axis=0,
    )
    results, out_parts = run_forward(
        place, token_pieces(held), (w_cols, conv_w, conv_b, step_rows, rows), dims
    )
    conv_in, active, slope, gate_act, gate_slope, raw, ssd, starts, scaled, squares, normed = results
    out_parts, cots, out_rows = together(out_parts, cots, out_rows)
    for stage in range(2, stages):
        cots = gather_stage(cots, stage)

    def out_product(part):
        return dot(part, out_rows)

    out_send = out_product(out_parts[0]).astype(bf16)
    out_send, cots = together(out_send, cots)
    out_grad, slopes, cot = run_out_grad(place, token_pieces(cots), scaled, out_rows)
    sums = jnp.stack([squares[:, 0].reshape(-1), slopes[:, 0].reshape(-1)])
    out_ready, out_held = scatter_near(out_product, out_parts[1:], out_send)
    sums = sums + exchange(sums, "seq", 1)
    sums, first = together(sums, out_ready[0])
    sums = sums + exchange(sums, "seq", 2)
    sums, second = together(sums, out_ready[1])
    for bit in bits_of(count)[2:]:
        sums = sums + exchange(sums, "seq", bit)
    scale = lax.rsqrt(sums[0] / inner + epsilon)
    norms = jnp.stack([scale, scale * scale * scale * sums[1] / inner])
    norms = jnp.pad(norms, ((0, 6), (0, 0))).reshape(8, -1, GROUP).swapaxes(0, 1)
    normed_out = (scaled.astype(f32) * scale[:, None]).astype(bf16)
    out_term = jnp.einsum("te,td->ed", normed_out, cot, preferred_element_type=f32)
    out_term, norms, first, second = together(out_term.astype(bf16), norms, first, second)
    out_sum = lax.psum_scatter(out_term, "batch", scatter_dimension=0, tiled=True)
    out_ready, out_held = scatter_far((first, second), out_held, 0)

    values = (conv_in, active, slope, gate_act, gate_slope, raw, ssd, starts, out_grad, norms)
    results = run_backward(place, values, (conv_w, step_rows, rows), dims)
    proj_grad, back_parts = results[0], results[1:5]
    proj_grad, back_parts, out_ready, out_held, out_sum = together(
        proj_grad, back_parts, out_ready, out_held, out_sum
    )

    def back_product(part):
        return jnp.einsum("tf,df->td", part, w_cols, preferred_element_type=f32)

    def weight_product(part):
        return jnp.einsum("td,tf->df", normed, part, preferred_element_type=f32).astype(bf16)

    for stage in range(1, stages - 1):
        out_ready, out_held = scatter_far(out_ready, out_held, stage)
    side_term = weight_product(proj_grad[:, 2 * width :])
    side_term, proj_grad, back_parts = together(side_term, proj_grad, back_parts)
    side_sum = lax.psum_scatter(side_term, "batch", scatter_dimension=0, tiled=True)
    back_send = back_product(back_parts[0]).astype(bf16)
    back_send, proj_grad = together(back_send, proj_grad)
    main_term = weight_product(proj_grad[:, : 2 * width])
    main_term, keeps, out_held, side_sum = together(main_term, back_parts[1:], out_held, side_sum)
    main_sum = lax.psum_scatter(main_term, "batch", scatter_dimension=0, tiled=True)
    back_ready, back_held = scatter_near(back_product, keeps, back_send)
    back_ready, out_sum = together(back_ready, out_sum)
    back_ready, back_held = scatter_far(back_ready, back_held, 0)
    out_pieces = to_owner(out_sum)[None]

    back_ready, out_pieces, main_sum = together(back_ready, out_pieces, main_sum)
    pieces = lax.all_gather(main_sum, "seq", axis=0, tiled=False)
    for stage in range(1, stages - 1):
        back_ready, back_held = scatter_far(back_ready, back_held, stage)

    back_held["arrived"], out_pieces, side_sum, results, main_term = together(
        back_held["arrived"], out_pieces, side_sum, results[5:], main_term
    )
    gain_term, conv_w_term, conv_b_term, small_term = results
    norm_gain_term = jnp.sum(main_term.astype(f32) * w_cols[:, : 2 * width].astype(f32), axis=1)
    norm_gain_term += jnp.sum(side_term.astype(f32) * w_cols[:, 2 * width :].astype(f32), axis=1)
    norm_gain_term /= norm_gain

    taps = conv_weight.shape[0]
    conv_terms = jnp.concatenate([conv_w_term, conv_b_term], axis=0)
    own_terms = jnp.concatenate([conv_terms[:, :width], gain_term], axis=0)
    own_terms = lax.dynamic_update_slice_in_dim(
        jnp.zeros((taps + 2, inner), f32), own_terms, mine * width, 1
    )
    head_terms = lax.dynamic_update_slice_in_dim(
        jnp.zeros((all_heads, 3), f32), small_term[:heads, :3], mine * heads, 0
    )
    terms = [own_terms, conv_terms[:, width:], norm_gain_term, head_terms]
    vector = jnp.concatenate([term.reshape(-1) for term in terms])
    padding = -vector.shape[0] % (8 * LANES)
    vector = jnp.pad(vector, (0, padding)).reshape(-1, LANES)
    for group in pairs_of(bits_of(count)):
        vector = add_exchanged(vector, "seq", group)
    for group in pairs_of(bits_of(lax.axis_size("batch"))):
        vector = add_exchanged(vector, "batch", group)
    for group in pairs_of(bits_of(count)):
        side_sum = add_exchanged(side_sum, "seq", group)
    for group in grow_groups():
        out_pieces = grow(out_pieces, group)
    in_weight_grad = assemble(pieces, side_sum, dims).T
    vector = vector.reshape(-1)
    normed_grad = scatter_end(back_held)
    cot_row = cotangent[0].astype(f32)
    gained = norm_gain * normed_grad
    slope = inverse * inverse * inverse * jnp.mean(gained * tokens_row, axis=-1, keepdims=True)
    input_grad = cot_row + inverse * gained - tokens_row * slope
    own_scale = lax.dynamic_slice_in_dim(scale, mine * tok_rows, tok_rows, 0)[:, None]
    block_out = (tokens_row + own_scale * scatter_end(out_held)).astype(bf16)
    out_weight_grad = assemble_out(place, out_pieces, per_plane)

    parts, offset = [], 0
    for term in terms:
        parts.append(vector[offset : offset + term.size].reshape(term.shape))
        offset += term.size
    own_terms, shared_terms, norm_gain_grad, head_terms = parts
    conv_terms = jnp.concatenate([own_terms[: taps + 1], shared_terms], axis=1)
    return (
        block_out[None],
        input_grad[None],
        norm_gain_grad,
        in_weight_grad,
        conv_terms[:taps],
        conv_terms[taps],
        head_terms[:, 0],
        head_terms[:, 1],
        head_terms[:, 2],
        own_terms[taps + 1],
        out_weight_grad,
    )


def solution(mesh):
    placed = (
        P("batch", "seq", None),
        P(),
        P("batch", None),
        P(),
        P(),
        P(),
        P(),
        P(),
        P(),
        P("batch", None),
        P("batch", "seq", None),
    )
    return jax.shard_map(
        body,
        mesh=mesh,
        in_specs=placed,
        out_specs=(
            P("batch", "seq", None),
            P("batch", "seq", None),
            P(),
            P("batch", None),
            P(),
            P(),
            P(),
            P(),
            P(),
            P(),
            P("batch", None),
        ),
        check_vma=False,
    )
```

```python
import functools

import jax
import jax.numpy as jnp
from jax import lax
from jax.experimental import pallas as pl
from jax.experimental.pallas import tpu as pltpu
from jax.sharding import PartitionSpec as P

GROUP = 256
LANES = 128
HALF = GROUP // 2
HALO = 8
STEP_BLOCKS = 4
LOG2E = 1.4426950408889634
epsilon = 1e-05
f32 = jnp.float32
bf16 = jnp.bfloat16
MIB = 2**20


def exchange(value, axis, distance):
    count = lax.axis_size(axis)
    return lax.ppermute(value, axis, [(source, source ^ distance) for source in range(count)])


def bits_of(count):
    return [1 << k for k in range(count.bit_length() - 1)]


def placed_order(count):
    return [2 * k for k in range(count // 2)] + [2 * k + 1 for k in range(count // 2)]


def together(*values):
    return lax.optimization_barrier(values)


def far_orders():
    far = bits_of(lax.axis_size("seq"))[1:]
    return far, far[::-1]


def gather_start(value):
    half = value.shape[0] // 32 * 16
    return tuple({"base": part, "fresh": None, "near": []} for part in (value[:half], value[half:]))


def gather_stage(held, stage, late=False):
    grown = []
    for half, order in zip(held, far_orders()):
        base, fresh, near = half["base"], half["fresh"], list(half["near"])
        if stage >= 1:
            merged = base if stage == len(order) else jnp.concatenate([base, fresh], axis=0)
            if not late:
                near.append(exchange(merged if stage == 1 else fresh, "seq", 1))
            elif stage == len(order):
                near = [exchange(base, "seq", 1), exchange(fresh, "seq", 1)]
            base = merged
        if stage < len(order):
            fresh = exchange(base, "seq", order[stage])
        grown.append({"base": base, "fresh": fresh, "near": near})
    return tuple(grown)


def gather_stages():
    return len(bits_of(lax.axis_size("seq")))


def gathered(held):
    arrays, table = [], {}
    for number, (half, order) in enumerate(zip(held, far_orders())):
        indices = [0]
        for bit in order:
            indices += [index | bit for index in indices]
        middle = len(indices) // 2
        groups = [(half["base"], indices[:middle]), (half["fresh"], indices[middle:])]
        bounds = [0] + [2 << k for k in range(len(order))]
        if len(half["near"]) < len(order):
            bounds = [0, middle, len(indices)]
        for value, first, last in zip(half["near"], bounds, bounds[1:]):
            groups.append((value, [index | 1 for index in indices[first:last]]))
        for value, members in groups:
            rows = value.shape[0] // len(members)
            for turn, index in enumerate(members):
                table[number, index] = (len(arrays), turn * rows, rows)
            arrays.append(value)
    return arrays, table


def token_pieces(held):
    arrays, table = gathered(held)
    indices = range(lax.axis_size("seq"))
    return arrays, tuple(table[half, index] for index in indices for half in range(2))


def gather_all(value):
    held = gather_start(value)
    for stage in range(gather_stages()):
        held = gather_stage(held, stage)
    return held


def scatter_places(count):
    far = bits_of(count)[1:]
    table = {}
    row = {}
    for near in (1, 0):
        for sent in (True, False):
            for half, order in enumerate((far, far[::-1])):
                members = [0]
                for bit in order[:0:-1]:
                    members += [member | bit for member in members]
                for member in members:
                    index = member | near | (order[0] if sent else 0)
                    array = 0 if near else (1 + half if sent else 3)
                    table[index * 2 + half] = (array, row.get(array, 0))
                    row[array] = row.get(array, 0) + GROUP
    return tuple(table[k] for k in range(2 * count))


def scatter_shapes(count, columns):
    blocks = (count, count // 4, count // 4, count // 2)
    return [jax.ShapeDtypeStruct((part * GROUP, columns), bf16) for part in blocks]


def scatter_near(product, parts, sent):
    arriving = exchange(sent, "seq", 1)
    first, second, kept = parts
    rows = first.shape[0]

    def summed(part, row):
        return (product(part) + arriving[row : row + part.shape[0]].astype(f32)).astype(bf16)

    sends = (summed(first, 0), summed(second, rows))
    sends, kept = together(sends, kept)
    return sends, {"kept": summed(kept, 2 * rows), "arrived": ([], [])}


def scatter_rows(held, half, first, last):
    top = half * (held["kept"].shape[0] // 2)
    total = held["kept"][top + first : top + last].astype(f32)
    for value in held["arrived"][half]:
        total = total + value[first:last].astype(f32)
    return total


def scatter_far(sends, held, stage):
    orders = far_orders()
    arrived = tuple(
        [*held["arrived"][half], exchange(sends[half], "seq", orders[half][stage])]
        for half in range(2)
    )
    held = {"kept": held["kept"], "arrived": arrived}
    rows = sends[0].shape[0]
    if stage + 1 == len(orders[0]):
        return (), held
    ready = tuple(
        scatter_rows(held, half, rows // 2, rows).astype(bf16) for half in range(2)
    )
    return ready, held


def scatter_end(held):
    rows = held["arrived"][0][-1].shape[0]
    return jnp.concatenate([scatter_rows(held, half, 0, rows) for half in range(2)], axis=0)


def plane_pairs(ahead):
    planes, count = lax.axis_size("batch"), lax.axis_size("seq")
    per = count // planes
    pairs = []
    for owner in range(planes):
        for piece in range(planes):
            for k in range(per):
                holder = owner * count + piece * per + k
                user = (piece + ahead) % planes * count + owner * per + k
                pairs.append((holder, user))
    return pairs


def rows_from_owner(out_weight, width):
    per = lax.axis_size("seq") // lax.axis_size("batch")
    plane, mine = lax.axis_index("batch"), lax.axis_index("seq")
    rows = lax.dynamic_slice_in_dim(out_weight, mine % per * width, width, 0)
    return lax.psum(jnp.where(plane == mine // per, rows, jnp.zeros_like(rows)), "batch")


def to_owner(summed):
    return lax.ppermute(
        summed, ("batch", "seq"), [(user, holder) for holder, user in plane_pairs(0)]
    )


def double(held, turn):
    bits = bits_of(lax.axis_size("seq"))
    return jnp.concatenate([held, exchange(held, "seq", (bits[1:] + [1])[turn])], axis=0)


def step_values(raw):
    small = jnp.exp(-jnp.abs(raw))
    step = jnp.maximum(raw, 0.0) + jnp.log1p(small)
    sig = jnp.where(raw >= 0, 1.0, small) / (1.0 + small)
    tiny = raw < -20.0
    log_step = jnp.where(tiny, raw, jnp.log(step))
    ratio = jnp.where(tiny, 1.0, sig / step)
    return step, sig, log_step, ratio


def dot(a, b):
    return jnp.dot(a, b, preferred_element_type=f32)


def dot_nt(a, b):
    return lax.dot_general(a, b, (((1,), (1,)), ((), ())), preferred_element_type=f32)


def dot_tn(a, b):
    return lax.dot_general(a, b, (((0,), (0,)), ((), ())), preferred_element_type=f32)


def sigmoid(value):
    return 0.5 * jnp.tanh(0.5 * value) + 0.5


def silu_slope(value):
    sig = sigmoid(value)
    active = value * sig
    return active, sig + active * (1.0 - sig)


def split_parts(value, count):
    parts = []
    for _ in range(count):
        part = value.astype(bf16)
        parts.append(part)
        value = value - part.astype(f32)
    return parts


def sum_along(rows, order):
    parts = jnp.concatenate([part.astype(f32) for part in split_parts(rows, 3)], axis=0)
    total = dot(parts.astype(bf16), order)
    return total[:8] + total[8:16] + total[16:24]


def to_columns(rows):
    stacked = jnp.concatenate(rows, axis=0)
    missing = LANES - stacked.shape[0]
    return jnp.concatenate([stacked, jnp.zeros((missing, GROUP), f32)], axis=0).T


def spread_heads(value, first, heads, size):
    rows = value.shape[0]
    return jnp.concatenate(
        [jnp.broadcast_to(value[:, first + h : first + h + 1], (rows, size)) for h in range(heads)],
        axis=1,
    )


def head_ones(width, size):
    row = lax.broadcasted_iota(jnp.int32, (8, width), 0)
    column = lax.broadcasted_iota(jnp.int32, (8, width), 1)
    return (column // size == row).astype(f32).astype(bf16)


def sum_lanes(value):
    return dot_nt(jnp.ones((8, value.shape[1]), bf16), value.astype(bf16))


def ones_where(condition):
    return jnp.where(condition, 1.0, 0.0).astype(bf16)


def order_indices(length):
    row = lax.broadcasted_iota(jnp.int32, (length, length), 0)
    column = lax.broadcasted_iota(jnp.int32, (length, length), 1)
    return row, column


def fetch(arrays, table, which, target, semaphore):
    for index, (array, row, rows) in enumerate(table):

        @pl.when(which == index)
        def _():
            pltpu.make_async_copy(arrays[array].at[pl.ds(row, rows)], target, semaphore).start()


def fetched(arrays, table, buffer, semaphores, order, blocks=1):
    step = pl.program_id(0)
    slot, other = lax.rem(step, 2), lax.rem(step + 1, 2)

    def start(step, slot):
        for k in range(blocks):
            target = buffer.at[slot, pl.ds(k * GROUP, GROUP)]
            fetch(arrays, table, order(step * blocks + k), target, semaphores.at[slot])

    @pl.when(step == 0)
    def _():
        start(0, 0)

    @pl.when(step + 1 < pl.num_programs(0))
    def _():
        start(step + 1, other)

    for k in range(blocks):
        source = arrays[0].at[pl.ds(0, GROUP)]
        target = buffer.at[slot, pl.ds(k * GROUP, GROUP)]
        pltpu.make_async_copy(source, target, semaphores.at[slot]).wait()
    return buffer[slot]


def store(source, targets, table, which, semaphore):
    for index, (array, row) in enumerate(table):

        @pl.when(which == index)
        def _():
            target = targets[array].at[pl.ds(row, GROUP)]
            pltpu.make_async_copy(source, target, semaphore).start()


def stored(buffer, targets, semaphores, slot):
    target = targets[0].at[pl.ds(0, GROUP)]
    pltpu.make_async_copy(buffer.at[slot], target, semaphores.at[slot]).wait()


def in_time(place, block):
    return ((block // 2) ^ place) * 2 + block % 2


def forward_kernel(dims, table, given, place_ref, *refs):
    heads, size, states, count = dims
    width = heads * size
    conv_cols = width + 2 * states
    arrays, refs = refs[:given], refs[given:]
    w_ref, conv_w_ref, conv_b_ref, step_ref, rows_ref = refs[:5]
    conv_in_ref, active_ref, slope_ref, gate_act_ref, gate_slope_ref = refs[5:10]
    raw_ref, ssd_ref, start_ref, scaled_ref, square_ref, normed_ref = refs[10:16]
    targets = refs[16:20]
    state, padded, order, barred, projected, buffer, semaphores, placed, out_semaphores = refs[20:]
    turn = pl.program_id(0)
    place = place_ref[0]

    @pl.when(turn == 0)
    def _():
        state[...] = jnp.zeros_like(state)
        padded[0:HALO] = jnp.zeros_like(padded[0:HALO])
        row, column = order_indices(GROUP)
        order[...] = ones_where(row <= column)
        row, column = order_indices(HALF)
        barred[...] = jnp.where(row >= column, 0.0, -1e30)

    @pl.when(turn >= 1)
    def _():
        for block in range(STEP_BLOCKS):
            stored(placed, targets, out_semaphores, block)

    normed = fetched(
        arrays, table, buffer, semaphores, lambda block: in_time(place, block), STEP_BLOCKS
    )
    normed_ref[...] = normed
    projected[...] = dot(normed, w_ref[...])
    conv_w = conv_w_ref[...]
    taps = conv_w.shape[0]
    for block in range(STEP_BLOCKS):
        here = slice(block * GROUP, (block + 1) * GROUP)
        conv_in = projected[here, width : width + conv_cols].astype(bf16)
        conv_in_ref[here] = conv_in
        padded[HALO : HALO + GROUP] = conv_in.astype(f32)
        pre = conv_b_ref[...]
        for k in range(taps):
            top = HALO - (taps - 1) + k
            pre = pre + conv_w[k : k + 1] * padded[top : top + GROUP]
        padded[0:HALO] = padded[GROUP : GROUP + HALO]
        active, slope = silu_slope(pre)
        active = active.astype(bf16)
        active_ref[here] = active
        slope_ref[here] = slope.astype(bf16)
        signal = active[:, :width]
        entry = active[:, width : width + states]
        readout = active[:, width + states :]
        signal_wide = signal.astype(f32)

        lanes = pltpu.roll(
            projected[here, width + conv_cols :], lax.rem(LANES - heads * place, LANES), 1
        )
        raw = lanes.T[:8]
        raw_ref[block] = raw
        step, _, log_step, _ = step_values(raw + step_ref[0:8, 0:1])
        running = sum_along(step * step_ref[8:16, 0:1], order[...])
        later = running - log_step
        total = running[:, GROUP - 1 :]
        columns = to_columns([running * LOG2E, jnp.exp(running), jnp.exp(total - later)])
        later = later * LOG2E
        early_wide = spread_heads(columns, 8, heads, size)
        tail_wide = spread_heads(columns, 16, heads, size)
        first, second = slice(0, HALF), slice(HALF, GROUP)
        scores = dot_nt(readout[first], entry[first])
        later_scores = dot_nt(readout[second], entry)
        within = []
        for h in range(heads):
            part = signal[:, h * size : (h + 1) * size]
            begin, end = columns[first, h : h + 1], columns[second, h : h + 1]
            row_first, row_second = later[h : h + 1, first], later[h : h + 1, second]
            near = jnp.exp2(begin - row_first + barred[...]) * scores
            full = jnp.exp2(end - row_first) * later_scores[:, first]
            last = jnp.exp2(end - row_second + barred[...]) * later_scores[:, second]
            both = jnp.concatenate([full.astype(bf16), last.astype(bf16)], axis=1)
            within.append(
                jnp.concatenate([dot(near.astype(bf16), part[first]), dot(both, part)], axis=0)
            )
        start = state[...]
        start_low = start.astype(bf16)
        start_ref[block] = start_low
        carried = dot(readout, start_low) * early_wide
        ssd = jnp.concatenate(within, axis=1) + carried + rows_ref[0:1] * signal_wide
        tail = (signal_wide * tail_wide).astype(bf16)
        state[...] = start * early_wide[GROUP - 1 :] + dot_tn(entry, tail)

        gate_act, gate_slope = silu_slope(projected[here, :width])
        gate_act_ref[here] = gate_act.astype(bf16)
        gate_slope_ref[here] = gate_slope.astype(bf16)
        ssd_ref[here] = ssd
        gated = ssd * gate_act
        scaled = (gated * rows_ref[1:2]).astype(bf16)
        scaled_ref[here] = scaled
        placed[block] = scaled
        square_ref[block] = sum_lanes(gated * gated)

    for block in range(STEP_BLOCKS):
        where = in_time(place, turn * STEP_BLOCKS + block)
        store(placed.at[block], targets, scatter_places(count), where, out_semaphores.at[block])

    @pl.when(turn == pl.num_programs(0) - 1)
    def _():
        for block in range(STEP_BLOCKS):
            stored(placed, targets, out_semaphores, block)


def time_estimate(microseconds, accessed):
    return pl.CostEstimate(
        flops=int(microseconds * 1.1e9), bytes_accessed=int(accessed), transcendentals=0
    )


def fixed(shape):
    return pl.BlockSpec(shape, lambda turn, place: (0,) * len(shape), pipeline_mode=pl.Buffered(1))


def anywhere(values):
    return [pl.BlockSpec(memory_space=pltpu.HBM)] * len(values)


def run_forward(place, pieces, params, dims):
    heads, size, states, count = dims
    arrays, table = pieces
    dim = params[0].shape[0]
    width, conv_cols = heads * size, params[1].shape[1]
    blocks = len(table)
    tokens = blocks * GROUP

    rows = STEP_BLOCKS * GROUP

    def moving(columns):
        return pl.BlockSpec((rows, columns), lambda turn, place: (turn, 0))

    def rows_of_block(height, columns):
        return pl.BlockSpec((STEP_BLOCKS, height, columns), lambda turn, place: (turn, 0, 0))

    results = pl.pallas_call(
        functools.partial(forward_kernel, dims, table, len(arrays)),
        grid_spec=pltpu.PrefetchScalarGridSpec(
            num_scalar_prefetch=1,
            grid=(blocks // STEP_BLOCKS,),
            in_specs=[*anywhere(arrays), *[fixed(param.shape) for param in params]],
            out_specs=[
                moving(conv_cols),
                moving(conv_cols),
                moving(conv_cols),
                moving(width),
                moving(width),
                rows_of_block(8, GROUP),
                moving(width),
                rows_of_block(states, width),
                moving(width),
                rows_of_block(8, GROUP),
                moving(dim),
                *anywhere(range(4)),
            ],
            scratch_shapes=[
                pltpu.VMEM((states, width), f32),
                pltpu.VMEM((HALO + GROUP, conv_cols), f32),
                pltpu.VMEM((GROUP, GROUP), bf16),
                pltpu.VMEM((HALF, HALF), f32),
                pltpu.VMEM((rows, params[0].shape[1]), f32),
                pltpu.VMEM((2, rows, dim), bf16),
                pltpu.SemaphoreType.DMA((2,)),
                pltpu.VMEM((STEP_BLOCKS, GROUP, width), bf16),
                pltpu.SemaphoreType.DMA((STEP_BLOCKS,)),
            ],
        ),
        out_shape=[
            jax.ShapeDtypeStruct((tokens, conv_cols), bf16),
            jax.ShapeDtypeStruct((tokens, conv_cols), bf16),
            jax.ShapeDtypeStruct((tokens, conv_cols), bf16),
            jax.ShapeDtypeStruct((tokens, width), bf16),
            jax.ShapeDtypeStruct((tokens, width), bf16),
            jax.ShapeDtypeStruct((blocks, 8, GROUP), f32),
            jax.ShapeDtypeStruct((tokens, width), f32),
            jax.ShapeDtypeStruct((blocks, states, width), bf16),
            jax.ShapeDtypeStruct((tokens, width), bf16),
            jax.ShapeDtypeStruct((blocks, 8, GROUP), f32),
            jax.ShapeDtypeStruct((tokens, dim), bf16),
            *scatter_shapes(count, width),
        ],
        compiler_params=pltpu.CompilerParams(vmem_limit_bytes=60 * MIB),
        cost_estimate=time_estimate(blocks * 3.0, tokens * (4 * dim + 24 * width)),
        name="forward_blocks",
    )(place, *arrays, *params)
    return results[:11], results[11:]


def out_grad_kernel(table, given, place_ref, *refs):
    arrays, refs = refs[:given], refs[given:]
    scaled_ref, out_rows_ref, out_grad_ref, slope_ref, cot_ref = refs[:5]
    buffer, semaphores, copied = refs[5:]
    place, turn = place_ref[0], pl.program_id(0)
    rows = buffer.shape[1]

    def copy_on(turn):
        target = cot_ref.at[pl.ds(pl.multiple_of(turn * rows, rows), rows)]
        return pltpu.make_async_copy(buffer.at[lax.rem(turn, 2)], target, copied)

    @pl.when(turn >= 1)
    def _():
        copy_on(turn - 1).wait()

    cot = fetched(arrays, table, buffer, semaphores, lambda block: in_time(place, block), 2)
    copy_on(turn).start()
    out_grad = dot_nt(cot, out_rows_ref[...])
    out_grad_ref[...] = out_grad
    for block in range(2):
        here = slice(block * GROUP, (block + 1) * GROUP)
        slope_ref[block] = sum_lanes(out_grad[here] * scaled_ref[here].astype(f32))

    @pl.when(turn == pl.num_programs(0) - 1)
    def _():
        copy_on(turn).wait()


def run_out_grad(place, cots, scaled, out_rows):
    arrays, table = cots
    width, dim = out_rows.shape
    blocks = len(table)
    tokens = blocks * GROUP
    return pl.pallas_call(
        functools.partial(out_grad_kernel, table, len(arrays)),
        grid_spec=pltpu.PrefetchScalarGridSpec(
            num_scalar_prefetch=1,
            grid=(blocks // 2,),
            in_specs=[
                *anywhere(arrays),
                pl.BlockSpec((2 * GROUP, width), lambda turn, place: (turn, 0)),
                fixed(out_rows.shape),
            ],
            out_specs=[
                pl.BlockSpec((2 * GROUP, width), lambda turn, place: (turn, 0)),
                pl.BlockSpec((2, 8, GROUP), lambda turn, place: (turn, 0, 0)),
                *anywhere(range(1)),
            ],
            scratch_shapes=[
                pltpu.VMEM((2, 2 * GROUP, dim), bf16),
                pltpu.SemaphoreType.DMA((2,)),
                pltpu.SemaphoreType.DMA,
            ],
        ),
        out_shape=[
            jax.ShapeDtypeStruct((tokens, width), f32),
            jax.ShapeDtypeStruct((blocks, 8, GROUP), f32),
            jax.ShapeDtypeStruct((tokens, dim), bf16),
        ],
        compiler_params=pltpu.CompilerParams(vmem_limit_bytes=60 * MIB),
        cost_estimate=time_estimate(12, tokens * (4 * dim + 6 * width)),
        name="out_grad",
    )(place, *arrays, scaled, out_rows)


def backward_kernel(dims, place_ref, *refs):
    heads, size, states, count = dims
    width = heads * size
    conv_cols = width + 2 * states
    conv_in_ref, active_ref, slope_ref, gate_act_ref, gate_slope_ref = refs[:5]
    raw_ref, ssd_ref, start_ref, out_grad_ref, norm_ref = refs[5:10]
    conv_w_ref, step_ref, rows_ref = refs[10:13]
    out_ref, targets = refs[13], refs[14:18]
    sums_ref = refs[18]
    state, pre_grads, order, back_order, barred, placed, semaphores = refs[19:26]
    sums = gain_ref, conv_wg_ref, conv_bg_ref, skip_ref, bias_ref, rate_ref = refs[26:]
    taps = conv_w_ref.shape[0]
    turn = pl.program_id(0)
    slot = lax.rem(turn, 2)

    @pl.when(turn >= 2)
    def _():
        stored(placed, targets, semaphores, slot)

    @pl.when(pl.program_id(0) == 0)
    def _():
        state[...] = jnp.zeros_like(state)
        pre_grads[0:HALO] = jnp.zeros_like(pre_grads[0:HALO])
        for total in sums:
            total[...] = jnp.zeros_like(total)
        row, column = order_indices(GROUP)
        order[...] = ones_where(row <= column)
        back_order[...] = ones_where(row >= column)
        row, column = order_indices(HALF)
        barred[...] = jnp.where(row <= column, 0.0, -1e30)

    gate_act, ssd, out_grad = gate_act_ref[...].astype(f32), ssd_ref[...], out_grad_ref[...]
    norms = norm_ref[0].T
    scale, slope = norms[:, 0:1], norms[:, 1:2]
    gated = ssd * gate_act
    gain_ref[...] += jnp.sum(out_grad * (gated * scale), axis=0, keepdims=True)
    gated_grad = out_grad * (rows_ref[1:2] * scale) - gated * slope
    grad_low = (gated_grad * gate_act).astype(bf16)
    gate_grad = (gated_grad * ssd * gate_slope_ref[...].astype(f32)).astype(bf16)
    out_ref[:, :width] = gate_grad
    placed[slot, :, :width] = gate_grad
    ssd_grad = grad_low.astype(f32)

    raw = raw_ref[0] + step_ref[0:8, 0:1]
    rate = step_ref[8:16, 0:1]
    step, sig, log_step, ratio = step_values(raw)
    decay = step * rate
    running = sum_along(decay, order[...])
    later = running - log_step
    total = running[:, GROUP - 1 :]
    columns = to_columns([later * LOG2E, jnp.exp(running), jnp.exp(total - later)])
    running = running * LOG2E
    early_wide = spread_heads(columns, 8, heads, size)
    tail_wide = spread_heads(columns, 16, heads, size)

    signal = active_ref[:, :width]
    entry = active_ref[:, width : width + states]
    readout = active_ref[:, width + states :]
    signal_wide = signal.astype(f32)
    start_low = start_ref[0]
    end_grad = state[...]
    end_low = end_grad.astype(bf16)
    first, second = slice(0, HALF), slice(HALF, GROUP)
    scores = dot_nt(entry[first], readout)
    later_scores = dot_nt(entry[second], readout[second])
    near_grad, far_grad, last_grad = 0.0, 0.0, 0.0
    within = []
    for h in range(heads):
        part, grad = signal[:, h * size : (h + 1) * size], grad_low[:, h * size : (h + 1) * size]
        begin, end = columns[first, h : h + 1], columns[second, h : h + 1]
        row_first, row_second = running[h : h + 1, first], running[h : h + 1, second]
        near = jnp.exp2(row_first - begin + barred[...])
        full = jnp.exp2(row_second - begin)
        last = jnp.exp2(row_second - end + barred[...])
        both = jnp.concatenate(
            [
                (near * scores[:, first]).astype(bf16),
                (full * scores[:, second]).astype(bf16),
            ],
            axis=1,
        )
        final = (last * later_scores).astype(bf16)
        within.append(jnp.concatenate([dot(both, grad), dot(final, grad[second])], axis=0))
        cross = dot_nt(part[first], grad)
        near_grad = near_grad + cross[:, first] * near
        far_grad = far_grad + cross[:, second] * full
        last_grad = last_grad + dot_nt(part[second], grad[second]) * last
    tail_grad = tail_wide * dot(entry, end_low)
    signal_grad = jnp.concatenate(within, axis=1) + tail_grad
    score_first = jnp.concatenate([near_grad, far_grad], axis=1).astype(bf16)
    score_second = last_grad.astype(bf16)
    tail = (signal_wide * tail_wide).astype(bf16)
    head_grad = (ssd_grad * early_wide).astype(bf16)
    entry_grad = jnp.concatenate(
        [dot(score_first, readout), dot(score_second, readout[second])], axis=0
    ) + dot_nt(tail, end_low)
    readout_grad = dot_tn(score_first, entry[first]) + dot_nt(head_grad, start_low)
    readout_last = readout_grad[second] + dot_tn(score_second, entry[second])
    total_wide = early_wide[GROUP - 1 :]
    state[...] = end_grad * total_wide + dot_tn(readout, head_grad)

    skip = rows_ref[0:1]
    ones = head_ones(width, size)
    column_part = signal_wide * signal_grad
    row_part = ssd_grad * (ssd - skip * signal_wide)
    end_part = jnp.sum(signal_wide * tail_grad, axis=0, keepdims=True) + total_wide * jnp.sum(
        start_low.astype(f32) * end_grad, axis=0, keepdims=True
    )

    def head_sums(value, parts):
        return sum(dot_nt(ones, part) for part in split_parts(value, parts))

    end_rows = head_sums(jnp.broadcast_to(end_part, (8, width)), 2)[:, 0:1]
    decay_grad = sum_along(head_sums(row_part - column_part, 2), back_order[...]) + end_rows
    raw_grad = head_sums(column_part, 1) * ratio + decay_grad * rate * sig
    skip_ref[...] += jnp.sum(ssd_grad * signal_wide, axis=0, keepdims=True)
    bias_ref[...] += raw_grad
    rate_ref[...] += decay_grad * decay
    raw_low = pltpu.roll(to_columns([raw_grad]), heads * place_ref[0], 1).astype(bf16)
    out_ref[:, width + conv_cols :] = raw_low
    placed[slot, :, width + conv_cols :] = raw_low

    pre_grads[GROUP : GROUP + HALO] = pre_grads[0:HALO]
    pre_grads[0:GROUP, :width] = (signal_grad + skip * ssd_grad) * slope_ref[:, :width].astype(f32)
    sides = slope_ref[:, width:].astype(f32)
    pre_grads[0:GROUP, width : width + states] = entry_grad * sides[:, :states]
    pre_grads[0:HALF, width + states :] = readout_grad[first] * sides[first, states:]
    pre_grads[HALF:GROUP, width + states :] = readout_last * sides[second, states:]
    conv_w = conv_w_ref[...]
    conv_in = conv_in_ref[...].astype(f32)
    conv_grad = 0.0
    for k in range(taps):
        ahead = taps - 1 - k
        shifted = pre_grads[ahead : ahead + GROUP]
        conv_grad = conv_grad + conv_w[k : k + 1] * shifted
        conv_wg_ref[k : k + 1] += jnp.sum(shifted * conv_in, axis=0, keepdims=True)
        if ahead == 0:
            conv_bg_ref[...] += jnp.sum(shifted, axis=0, keepdims=True)
    conv_low = conv_grad.astype(bf16)
    out_ref[:, width : width + conv_cols] = conv_low
    placed[slot, :, width : width + conv_cols] = conv_low

    where = in_time(place_ref[0], pl.num_programs(0) - 1 - turn)
    store(placed.at[slot], targets, scatter_places(count), where, semaphores.at[slot])

    @pl.when(turn == pl.num_programs(0) - 1)
    def _():
        sums_ref[...] = jnp.zeros_like(sums_ref)
        sums_ref[0:taps] = conv_wg_ref[...]
        sums_ref[taps : taps + 1] = conv_bg_ref[...]
        sums_ref[taps + 1 : taps + 2, :width] = gain_ref[...]
        skips = head_sums(jnp.broadcast_to(skip_ref[...], (8, width)), 3)[:, 0:1]
        lane = lax.broadcasted_iota(jnp.int32, (8, LANES), 1)
        small = jnp.where(lane == 0, jnp.sum(bias_ref[...], axis=1, keepdims=True), skips)
        small = jnp.where(lane == 1, jnp.sum(rate_ref[...], axis=1, keepdims=True), small)
        small = jnp.concatenate([small, jnp.zeros((LANES - 8, LANES), f32)], axis=0).T
        sums_ref[8:16, :LANES] = small[0:8]
        for other in range(2):
            stored(placed, targets, semaphores, other)


def run_backward(place, values, params, dims):
    heads, size, states, count = dims
    conv_cols, width = values[0].shape[1], heads * size
    tokens = values[0].shape[0]
    blocks = tokens // GROUP
    last = blocks - 1
    out_cols = width + conv_cols + LANES

    def moving(columns):
        return pl.BlockSpec((GROUP, columns), lambda turn, place: (last - turn, 0))

    def rows_of_block():
        return pl.BlockSpec((1, 8, GROUP), lambda turn, place: (last - turn, 0, 0))

    taps = params[0].shape[0]
    return pl.pallas_call(
        functools.partial(backward_kernel, dims),
        grid_spec=pltpu.PrefetchScalarGridSpec(
            num_scalar_prefetch=1,
            grid=(blocks,),
            in_specs=[
                moving(conv_cols),
                moving(conv_cols),
                moving(conv_cols),
                moving(width),
                moving(width),
                rows_of_block(),
                moving(width),
                pl.BlockSpec((1, states, width), lambda turn, place: (last - turn, 0, 0)),
                moving(width),
                rows_of_block(),
                *[fixed(param.shape) for param in params],
            ],
            out_specs=[
                moving(out_cols),
                *anywhere(range(4)),
                fixed((16, conv_cols)),
            ],
            scratch_shapes=[
                pltpu.VMEM((states, width), f32),
                pltpu.VMEM((GROUP + HALO, conv_cols), f32),
                pltpu.VMEM((GROUP, GROUP), bf16),
                pltpu.VMEM((GROUP, GROUP), bf16),
                pltpu.VMEM((HALF, HALF), f32),
                pltpu.VMEM((2, GROUP, out_cols), bf16),
                pltpu.SemaphoreType.DMA((2,)),
                pltpu.VMEM((1, width), f32),
                pltpu.VMEM((taps, conv_cols), f32),
                pltpu.VMEM((1, conv_cols), f32),
                pltpu.VMEM((1, width), f32),
                pltpu.VMEM((8, GROUP), f32),
                pltpu.VMEM((8, GROUP), f32),
            ],
        ),
        out_shape=[
            jax.ShapeDtypeStruct((tokens, out_cols), bf16),
            *scatter_shapes(count, out_cols),
        ]
        + [jax.ShapeDtypeStruct((16, conv_cols), f32)],
        compiler_params=pltpu.CompilerParams(vmem_limit_bytes=60 * MIB),
        cost_estimate=time_estimate(blocks * 3.5, tokens * 40 * width),
        name="backward_blocks",
    )(place, *values, *params)


def widen_kernel(place_ref, piece_ref, out_ref):
    out_ref[...] = piece_ref[0].astype(f32)


def assemble_out(place, pieces, per):
    count, size, dim = pieces.shape
    groups = count // per

    def source(turn, place):
        relative = (turn % groups * per + turn // groups) ^ place[0]
        return ((relative & 1) * (count // 2) + (relative >> 1), 0, 0)

    return pl.pallas_call(
        widen_kernel,
        grid_spec=pltpu.PrefetchScalarGridSpec(
            num_scalar_prefetch=1,
            grid=(count,),
            in_specs=[pl.BlockSpec((1, size, dim), source)],
            out_specs=pl.BlockSpec((size, dim), lambda turn, place: (turn, 0)),
        ),
        out_shape=jax.ShapeDtypeStruct((count * size, dim), f32),
        cost_estimate=time_estimate(5, count * size * dim * 6),
        name="assemble_out_weight_grad",
    )(place, pieces)


def assemble_kernel(dims, lasting, pieces_ref, out_ref):
    heads, size, states, count = dims
    width = heads * size
    inner = count * width
    total = 0.0
    for device in range(count):
        columns = pieces_ref[device].astype(f32).T
        out_ref[device * width : (device + 1) * width] = columns[:width]
        out_ref[inner + device * width : inner + (device + 1) * width] = columns[width : 2 * width]
        total = total + columns[2 * width :]
    out_ref[2 * inner :] = total[:lasting]


def assemble(pieces, dims):
    heads, size, states, count = dims
    _, rows, columns = pieces.shape
    tile = LANES if rows % LANES == 0 else rows
    lasting = 2 * states + count * heads
    out_rows = 2 * count * heads * size + lasting
    return pl.pallas_call(
        functools.partial(assemble_kernel, dims, lasting),
        grid=(rows // tile,),
        in_specs=[pl.BlockSpec((count, tile, columns), lambda turn: (0, turn, 0))],
        out_specs=pl.BlockSpec((out_rows, tile), lambda turn: (0, turn)),
        out_shape=jax.ShapeDtypeStruct((out_rows, rows), f32),
        compiler_params=pltpu.CompilerParams(vmem_limit_bytes=60 * MIB),
        cost_estimate=time_estimate(8, out_rows * rows * 6),
        name="assemble_in_weight_grad",
    )(pieces)


def body(
    tokens,
    norm_gain,
    in_weight,
    conv_weight,
    conv_bias,
    dt_bias,
    decay_log,
    skip_scale,
    gate_gain,
    out_weight,
    cotangent,
):
    count, mine = lax.axis_size("seq"), lax.axis_index("seq")
    place = mine.astype(jnp.int32).reshape(1)
    inner, all_heads, conv_all = gate_gain.shape[0], dt_bias.shape[0], conv_bias.shape[0]
    size, states = inner // all_heads, (conv_all - inner) // 2
    heads, width = all_heads // count, inner // count
    dims = (heads, size, states, count)
    shared = 2 * states
    conv_cols = width + shared
    tok_rows = tokens.shape[1]
    per_plane = out_weight.shape[0] // width

    def own(vector, per, first=0):
        return lax.dynamic_slice_in_dim(vector, first + mine * per, per, vector.ndim - 1)

    def own_conv(array, first=0):
        return jnp.concatenate(
            [own(array, width, first), array[..., first + inner : first + conv_all]], axis=-1
        )

    tokens_row = tokens[0].astype(f32)
    inverse = lax.rsqrt(jnp.mean(tokens_row * tokens_row, axis=-1, keepdims=True) + epsilon)
    normed_own = (tokens_row * inverse * norm_gain).astype(bf16)
    step_own = own(in_weight, heads, inner + conv_all)
    w_own = jnp.concatenate(
        [
            own(in_weight, width),
            own_conv(in_weight, inner),
            lax.dynamic_update_slice_in_dim(
                jnp.zeros((step_own.shape[0], LANES), bf16), step_own, mine * heads, 1
            ),
        ],
        axis=1,
    )
    w_cols = lax.all_gather(w_own, "batch", axis=0, tiled=True)
    stages = gather_stages()
    held = gather_stage(gather_stage(gather_start(normed_own), 0), 1)
    held, cots = together(held, gather_start(cotangent[0]))
    cots = gather_stage(cots, 0)
    for stage in range(2, stages):
        held = gather_stage(held, stage)
    w_cols, held, cots, out_owned = together(w_cols, held, cots, out_weight)
    cots = gather_stage(cots, 1)
    out_rows = rows_from_owner(out_owned, width)

    conv_w, conv_b = own_conv(conv_weight), own_conv(conv_bias)[None]
    per_head = jnp.stack([own(dt_bias, heads), -jnp.exp(own(decay_log, heads))])
    per_head = jnp.pad(per_head, ((0, 0), (0, 8 - heads))).reshape(16, 1)
    step_rows = jnp.broadcast_to(per_head, (16, LANES))
    gain_own = own(gate_gain, width)[None]
    rows = jnp.concatenate(
        [jnp.repeat(own(skip_scale, heads), size)[None], gain_own, jnp.zeros((6, width), f32)],
        axis=0,
    )
    results, out_parts = run_forward(
        place, token_pieces(held), (w_cols, conv_w, conv_b, step_rows, rows), dims
    )
    conv_in, active, slope, gate_act, gate_slope, raw, ssd, starts, scaled, squares, normed = results
    out_parts, cots, out_rows = together(out_parts, cots, out_rows)
    for stage in range(2, stages):
        cots = gather_stage(cots, stage)

    def out_product(part):
        return dot(part, out_rows)

    out_send = out_product(out_parts[0]).astype(bf16)
    out_send, cots = together(out_send, cots)
    out_grad, slopes, cot = run_out_grad(place, token_pieces(cots), scaled, out_rows)
    sums = jnp.stack([squares[:, 0].reshape(-1), slopes[:, 0].reshape(-1)])
    out_ready, out_held = scatter_near(out_product, out_parts[1:], out_send)
    sums = sums + exchange(sums, "seq", 1)
    sums, first = together(sums, out_ready[0])
    sums = sums + exchange(sums, "seq", 2)
    sums, second = together(sums, out_ready[1])
    for bit in bits_of(count)[2:]:
        sums = sums + exchange(sums, "seq", bit)
    scale = lax.rsqrt(sums[0] / inner + epsilon)
    norms = jnp.stack([scale, scale * scale * scale * sums[1] / inner])
    norms = jnp.pad(norms, ((0, 6), (0, 0))).reshape(8, -1, GROUP).swapaxes(0, 1)
    normed_out = (scaled.astype(f32) * scale[:, None]).astype(bf16)
    out_term = jnp.einsum("te,td->ed", normed_out, cot, preferred_element_type=f32)
    out_term, norms, first, second = together(out_term.astype(bf16), norms, first, second)
    out_sum = lax.psum_scatter(out_term, "batch", scatter_dimension=0, tiled=True)
    out_ready, out_held = scatter_far((first, second), out_held, 0)

    values = (conv_in, active, slope, gate_act, gate_slope, raw, ssd, starts, out_grad, norms)
    results = run_backward(place, values, (conv_w, step_rows, rows), dims)
    proj_grad, back_parts = results[0], results[1:5]
    proj_grad, back_parts, out_ready, out_held, out_sum = together(
        proj_grad, back_parts, out_ready, out_held, out_sum
    )

    def back_product(part):
        return jnp.einsum("tf,df->td", part, w_cols, preferred_element_type=f32)

    def weight_product(part):
        return jnp.einsum("td,tf->df", normed, part, preferred_element_type=f32).astype(bf16)

    for stage in range(1, stages - 1):
        out_ready, out_held = scatter_far(out_ready, out_held, stage)
    small_sums = lax.all_gather(results[5], ("batch", "seq"), axis=0, tiled=False)
    back_send = back_product(back_parts[0]).astype(bf16)
    back_send, proj_grad = together(back_send, proj_grad)
    in_term = weight_product(proj_grad)
    in_term, keeps, out_held, small_sums = together(
        in_term, back_parts[1:], out_held, small_sums
    )
    in_sum = lax.psum_scatter(in_term, "batch", scatter_dimension=0, tiled=True)
    back_ready, back_held = scatter_near(back_product, keeps, back_send)
    back_ready, out_sum, in_term = together(back_ready, out_sum, in_term)
    back_ready, back_held = scatter_far(back_ready, back_held, 0)
    out_pieces = to_owner(out_sum)[None]
    norm_gain_term = jnp.sum(in_term.astype(f32) * w_cols.astype(f32), axis=1) / norm_gain
    norm_gain_term = norm_gain_term.reshape(-1, LANES)

    back_ready, out_pieces, in_sum, norm_gain_term = together(
        back_ready, out_pieces, in_sum, norm_gain_term
    )
    pieces = lax.all_gather(in_sum, "seq", axis=0, tiled=False)
    for stage in range(1, stages - 1):
        back_ready, back_held = scatter_far(back_ready, back_held, stage)
    back_held["arrived"], out_pieces, norm_gain_grad, small_sums = together(
        back_held["arrived"], out_pieces, norm_gain_term, small_sums
    )
    for stage in range(stages):
        out_pieces = double(out_pieces, stage)
    for axis in ("seq", "batch"):
        for bit in bits_of(lax.axis_size(axis)):
            norm_gain_grad = norm_gain_grad + exchange(norm_gain_grad, axis, bit)
    in_weight_grad = assemble(pieces, dims).T

    planes, taps = lax.axis_size("batch"), conv_weight.shape[0]
    by_device = small_sums.reshape(planes, count, *small_sums.shape[1:])
    by_device = sum(by_device[plane] for plane in range(planes))
    own_sums = by_device[:, : taps + 2, :width].swapaxes(0, 1).reshape(taps + 2, inner)
    shared_sums = sum(by_device[device, : taps + 1, width:] for device in range(count))
    conv_sums = jnp.concatenate([own_sums[: taps + 1], shared_sums], axis=1)
    head_sums = by_device[:, 8:11, :heads].swapaxes(0, 1).reshape(3, all_heads)
    normed_grad = scatter_end(back_held)
    cot_row = cotangent[0].astype(f32)
    gained = norm_gain * normed_grad
    slope = inverse * inverse * inverse * jnp.mean(gained * tokens_row, axis=-1, keepdims=True)
    input_grad = cot_row + inverse * gained - tokens_row * slope
    own_scale = lax.dynamic_slice_in_dim(scale, mine * tok_rows, tok_rows, 0)[:, None]
    block_out = (tokens_row + own_scale * scatter_end(out_held)).astype(bf16)
    out_weight_grad = assemble_out(place, out_pieces, per_plane)

    return (
        block_out[None],
        input_grad[None],
        norm_gain_grad.reshape(-1),
        in_weight_grad,
        conv_sums[:taps],
        conv_sums[taps],
        head_sums[0],
        head_sums[1],
        head_sums[2],
        own_sums[taps + 1],
        out_weight_grad,
    )


def solution(mesh):
    placed = (
        P("batch", "seq", None),
        P(),
        P("batch", None),
        P(),
        P(),
        P(),
        P(),
        P(),
        P(),
        P("batch", None),
        P("batch", "seq", None),
    )
    return jax.shard_map(
        body,
        mesh=mesh,
        in_specs=placed,
        out_specs=(
            P("batch", "seq", None),
            P("batch", "seq", None),
            P(),
            P("batch", None),
            P(),
            P(),
            P(),
            P(),
            P(),
            P(),
            P("batch", None),
        ),
        check_vma=False,
    )
```

```python
import functools

import jax
import jax.numpy as jnp
from jax import lax
from jax.experimental import pallas as pl
from jax.experimental.pallas import tpu as pltpu
from jax.sharding import PartitionSpec as P

GROUP = 256
LANES = 128
HALF = GROUP // 2
HALO = 8
STEP_ROWS = 16
LOG2E = 1.4426950408889634
epsilon = 1e-05
f32 = jnp.float32
bf16 = jnp.bfloat16
MIB = 2**20


def exchange(value, axis, distance):
    count = lax.axis_size(axis)
    return lax.ppermute(value, axis, [(source, source ^ distance) for source in range(count)])


def bits_of(count):
    return [1 << k for k in range(count.bit_length() - 1)]


def placed_order(count):
    return [2 * k for k in range(count // 2)] + [2 * k + 1 for k in range(count // 2)]


def together(*values):
    return lax.optimization_barrier(values)


def far_orders():
    far = bits_of(lax.axis_size("seq"))[1:]
    return far, far[::-1]


def gather_start(value):
    half = value.shape[0] // 32 * 16
    return tuple({"base": part, "fresh": None, "near": []} for part in (value[:half], value[half:]))


def gather_stage(held, stage, late=False):
    grown = []
    for half, order in zip(held, far_orders()):
        base, fresh, near = half["base"], half["fresh"], list(half["near"])
        if stage >= 1:
            merged = base if stage == len(order) else jnp.concatenate([base, fresh], axis=0)
            if not late:
                near.append(exchange(merged if stage == 1 else fresh, "seq", 1))
            elif stage == len(order):
                near = [exchange(base, "seq", 1), exchange(fresh, "seq", 1)]
            base = merged
        if stage < len(order):
            fresh = exchange(base, "seq", order[stage])
        grown.append({"base": base, "fresh": fresh, "near": near})
    return tuple(grown)


def gather_stages():
    return len(bits_of(lax.axis_size("seq")))


def gathered(held):
    arrays, table = [], {}
    for number, (half, order) in enumerate(zip(held, far_orders())):
        indices = [0]
        for bit in order:
            indices += [index | bit for index in indices]
        middle = len(indices) // 2
        groups = [(half["base"], indices[:middle]), (half["fresh"], indices[middle:])]
        bounds = [0] + [2 << k for k in range(len(order))]
        if len(half["near"]) < len(order):
            bounds = [0, middle, len(indices)]
        for value, first, last in zip(half["near"], bounds, bounds[1:]):
            groups.append((value, [index | 1 for index in indices[first:last]]))
        for value, members in groups:
            rows = value.shape[0] // len(members)
            for turn, index in enumerate(members):
                table[number, index] = (len(arrays), turn * rows, rows)
            arrays.append(value)
    return arrays, table


def token_pieces(held):
    arrays, table = gathered(held)
    indices = range(lax.axis_size("seq"))
    return arrays, tuple(table[half, index] for index in indices for half in range(2))


def gather_all(value):
    held = gather_start(value)
    for stage in range(gather_stages()):
        held = gather_stage(held, stage)
    return held


def scatter_places(count):
    far = bits_of(count)[1:]
    table = {}
    row = {}
    for near in (1, 0):
        for sent in (True, False):
            for half, order in enumerate((far, far[::-1])):
                members = [0]
                for bit in order[:0:-1]:
                    members += [member | bit for member in members]
                for member in members:
                    index = member | near | (order[0] if sent else 0)
                    array = 0 if near else (1 + half if sent else 3)
                    table[index * 2 + half] = (array, row.get(array, 0))
                    row[array] = row.get(array, 0) + GROUP
    return tuple(table[k] for k in range(2 * count))


def scatter_shapes(count, columns):
    blocks = (count, count // 4, count // 4, count // 2)
    return [jax.ShapeDtypeStruct((part * GROUP, columns), bf16) for part in blocks]


def scatter_near(product, parts, sent):
    arriving = exchange(sent, "seq", 1)
    first, second, kept = parts
    rows = first.shape[0]

    def summed(part, row):
        return (product(part) + arriving[row : row + part.shape[0]].astype(f32)).astype(bf16)

    sends = (summed(first, 0), summed(second, rows))
    sends, kept = together(sends, kept)
    return sends, {"kept": summed(kept, 2 * rows), "arrived": ([], [])}


def scatter_rows(held, half, first, last):
    top = half * (held["kept"].shape[0] // 2)
    total = held["kept"][top + first : top + last].astype(f32)
    for value in held["arrived"][half]:
        total = total + value[first:last].astype(f32)
    return total


def scatter_far(sends, held, stage):
    orders = far_orders()
    arrived = tuple(
        [*held["arrived"][half], exchange(sends[half], "seq", orders[half][stage])]
        for half in range(2)
    )
    held = {"kept": held["kept"], "arrived": arrived}
    rows = sends[0].shape[0]
    if stage + 1 == len(orders[0]):
        return (), held
    ready = tuple(
        scatter_rows(held, half, rows // 2, rows).astype(bf16) for half in range(2)
    )
    return ready, held


def scatter_end(held):
    rows = held["arrived"][0][-1].shape[0]
    return jnp.concatenate([scatter_rows(held, half, 0, rows) for half in range(2)], axis=0)


def sum_seq(value):
    for bit in bits_of(lax.axis_size("seq")):
        value = value + exchange(value, "seq", bit)
    return value


def plane_pairs(ahead):
    planes, count = lax.axis_size("batch"), lax.axis_size("seq")
    per = count // planes
    pairs = []
    for owner in range(planes):
        for piece in range(planes):
            for k in range(per):
                holder = owner * count + piece * per + k
                user = (piece + ahead) % planes * count + owner * per + k
                pairs.append((holder, user))
    return pairs


def rows_from_owner(out_weight, width):
    per = lax.axis_size("seq") // lax.axis_size("batch")
    plane, mine = lax.axis_index("batch"), lax.axis_index("seq")
    rows = lax.dynamic_slice_in_dim(out_weight, mine % per * width, width, 0)
    return lax.psum(jnp.where(plane == mine // per, rows, jnp.zeros_like(rows)), "batch")


def to_owner(summed):
    return lax.ppermute(
        summed, ("batch", "seq"), [(user, holder) for holder, user in plane_pairs(0)]
    )


def double(held, turn):
    bits = bits_of(lax.axis_size("seq"))
    return jnp.concatenate([held, exchange(held, "seq", (bits[1:] + [1])[turn])], axis=0)


def step_values(raw):
    small = jnp.exp(-jnp.abs(raw))
    step = jnp.maximum(raw, 0.0) + jnp.log1p(small)
    sig = jnp.where(raw >= 0, 1.0, small) / (1.0 + small)
    tiny = raw < -20.0
    log_step = jnp.where(tiny, raw, jnp.log(step))
    ratio = jnp.where(tiny, 1.0, sig / step)
    return step, sig, log_step, ratio


def dot(a, b):
    return jnp.dot(a, b, preferred_element_type=f32)


def dot_nt(a, b):
    return lax.dot_general(a, b, (((1,), (1,)), ((), ())), preferred_element_type=f32)


def dot_tn(a, b):
    return lax.dot_general(a, b, (((0,), (0,)), ((), ())), preferred_element_type=f32)


def sigmoid(value):
    return 0.5 * jnp.tanh(0.5 * value) + 0.5


def silu_slope(value):
    sig = sigmoid(value)
    active = value * sig
    return active, sig + active * (1.0 - sig)


def split_parts(value, count):
    parts = []
    for _ in range(count):
        part = value.astype(bf16)
        parts.append(part)
        value = value - part.astype(f32)
    return parts


def sum_along(rows, order):
    parts = jnp.concatenate([part.astype(f32) for part in split_parts(rows, 3)], axis=0)
    total = dot(parts.astype(bf16), order)
    return total[:8] + total[8:16] + total[16:24]


def to_columns(rows):
    stacked = jnp.concatenate(rows, axis=0)
    missing = LANES - stacked.shape[0]
    return jnp.concatenate([stacked, jnp.zeros((missing, GROUP), f32)], axis=0).T


def spread_heads(value, first, heads, size):
    rows = value.shape[0]
    return jnp.concatenate(
        [jnp.broadcast_to(value[:, first + h : first + h + 1], (rows, size)) for h in range(heads)],
        axis=1,
    )


def head_ones(width, size):
    row = lax.broadcasted_iota(jnp.int32, (8, width), 0)
    column = lax.broadcasted_iota(jnp.int32, (8, width), 1)
    return (column // size == row).astype(f32).astype(bf16)


def sum_lanes(value):
    return dot_nt(jnp.ones((8, value.shape[1]), bf16), value.astype(bf16))


def ones_where(condition):
    return jnp.where(condition, 1.0, 0.0).astype(bf16)


def order_indices(length):
    row = lax.broadcasted_iota(jnp.int32, (length, length), 0)
    column = lax.broadcasted_iota(jnp.int32, (length, length), 1)
    return row, column


def fetch(arrays, table, which, target, semaphore):
    for index, (array, row, rows) in enumerate(table):

        @pl.when(which == index)
        def _():
            pltpu.make_async_copy(arrays[array].at[pl.ds(row, rows)], target, semaphore).start()


def fetched(arrays, table, buffer, semaphores, order, blocks=1):
    step = pl.program_id(0)
    slot, other = lax.rem(step, 2), lax.rem(step + 1, 2)

    def start(step, slot):
        for k in range(blocks):
            target = buffer.at[slot, pl.ds(k * GROUP, GROUP)]
            fetch(arrays, table, order(step * blocks + k), target, semaphores.at[slot])

    @pl.when(step == 0)
    def _():
        start(0, 0)

    @pl.when(step + 1 < pl.num_programs(0))
    def _():
        start(step + 1, other)

    for k in range(blocks):
        source = arrays[0].at[pl.ds(0, GROUP)]
        target = buffer.at[slot, pl.ds(k * GROUP, GROUP)]
        pltpu.make_async_copy(source, target, semaphores.at[slot]).wait()
    return buffer[slot]


def store(source, targets, table, which, semaphore):
    for index, (array, row) in enumerate(table):

        @pl.when(which == index)
        def _():
            target = targets[array].at[pl.ds(row, GROUP)]
            pltpu.make_async_copy(source, target, semaphore).start()


def stored(buffer, targets, semaphores, slot):
    target = targets[0].at[pl.ds(0, GROUP)]
    pltpu.make_async_copy(buffer.at[slot], target, semaphores.at[slot]).wait()


def in_time(place, block):
    return ((block // 2) ^ place) * 2 + block % 2


def forward_kernel(dims, table, given, place_ref, *refs):
    heads, size, states, count = dims
    width = heads * size
    conv_cols = width + 2 * states
    arrays, refs = refs[:given], refs[given:]
    w_ref, conv_w_ref, conv_b_ref, step_ref, rows_ref = refs[:5]
    conv_in_ref, active_ref, slope_ref, gate_act_ref, gate_slope_ref = refs[5:10]
    raw_ref, ssd_ref, start_ref, scaled_ref, square_ref, normed_ref = refs[10:16]
    targets = refs[16:20]
    state, padded, order, barred, buffer, semaphores, placed, out_semaphores = refs[20:]
    turn = pl.program_id(0)
    slot = lax.rem(turn, 2)

    @pl.when(turn == 0)
    def _():
        state[...] = jnp.zeros_like(state)
        padded[0:HALO] = jnp.zeros_like(padded[0:HALO])
        row, column = order_indices(GROUP)
        order[...] = ones_where(row <= column)
        row, column = order_indices(HALF)
        barred[...] = jnp.where(row >= column, 0.0, -1e30)

    @pl.when(turn >= 2)
    def _():
        stored(placed, targets, out_semaphores, slot)

    normed = fetched(
        arrays, table, buffer, semaphores, lambda step: in_time(place_ref[0], step)
    )
    normed_ref[...] = normed
    projected = dot(normed, w_ref[...])
    conv_in = projected[:, width : width + conv_cols].astype(bf16)
    conv_in_ref[...] = conv_in
    padded[HALO : HALO + GROUP] = conv_in.astype(f32)
    conv_w = conv_w_ref[...]
    taps = conv_w.shape[0]
    pre = conv_b_ref[...]
    for k in range(taps):
        top = HALO - (taps - 1) + k
        pre = pre + conv_w[k : k + 1] * padded[top : top + GROUP]
    padded[0:HALO] = padded[GROUP : GROUP + HALO]
    active, slope = silu_slope(pre)
    active = active.astype(bf16)
    active_ref[...] = active
    slope_ref[...] = slope.astype(bf16)
    signal = active[:, :width]
    entry = active[:, width : width + states]
    readout = active[:, width + states :]
    signal_wide = signal.astype(f32)

    raw = projected[:, width + conv_cols :].T[:8]
    raw_ref[0] = raw
    step, _, log_step, _ = step_values(raw + step_ref[0:8, 0:1])
    running = sum_along(step * step_ref[8:16, 0:1], order[...])
    later = running - log_step
    total = running[:, GROUP - 1 :]
    columns = to_columns([running * LOG2E, jnp.exp(running), jnp.exp(total - later)])
    later = later * LOG2E
    early_wide = spread_heads(columns, 8, heads, size)
    tail_wide = spread_heads(columns, 16, heads, size)
    first, second = slice(0, HALF), slice(HALF, GROUP)
    scores = dot_nt(readout[first], entry[first])
    later_scores = dot_nt(readout[second], entry)
    within = []
    for h in range(heads):
        part = signal[:, h * size : (h + 1) * size]
        begin, end = columns[first, h : h + 1], columns[second, h : h + 1]
        row_first, row_second = later[h : h + 1, first], later[h : h + 1, second]
        near = jnp.exp2(begin - row_first + barred[...]) * scores
        full = jnp.exp2(end - row_first) * later_scores[:, first]
        last = jnp.exp2(end - row_second + barred[...]) * later_scores[:, second]
        both = jnp.concatenate([full.astype(bf16), last.astype(bf16)], axis=1)
        within.append(
            jnp.concatenate([dot(near.astype(bf16), part[first]), dot(both, part)], axis=0)
        )
    start = state[...]
    start_low = start.astype(bf16)
    start_ref[0] = start_low
    carried = dot(readout, start_low) * early_wide
    ssd = jnp.concatenate(within, axis=1) + carried + rows_ref[0:1] * signal_wide
    tail = (signal_wide * tail_wide).astype(bf16)
    state[...] = start * early_wide[GROUP - 1 :] + dot_tn(entry, tail)

    gate_act, gate_slope = silu_slope(projected[:, :width])
    gate_act_ref[...] = gate_act.astype(bf16)
    gate_slope_ref[...] = gate_slope.astype(bf16)
    ssd_ref[...] = ssd
    gated = ssd * gate_act
    scaled = (gated * rows_ref[1:2]).astype(bf16)
    scaled_ref[...] = scaled
    square_ref[0] = sum_lanes(gated * gated)
    placed[slot] = scaled
    where = in_time(place_ref[0], turn)
    store(placed.at[slot], targets, scatter_places(count), where, out_semaphores.at[slot])

    @pl.when(turn == pl.num_programs(0) - 1)
    def _():
        for other in range(2):
            stored(placed, targets, out_semaphores, other)


def time_estimate(microseconds, accessed):
    return pl.CostEstimate(
        flops=int(microseconds * 1.1e9), bytes_accessed=int(accessed), transcendentals=0
    )


def fixed(shape):
    return pl.BlockSpec(shape, lambda turn, place: (0,) * len(shape), pipeline_mode=pl.Buffered(1))


def anywhere(values):
    return [pl.BlockSpec(memory_space=pltpu.HBM)] * len(values)


def run_forward(place, pieces, params, dims):
    heads, size, states, count = dims
    arrays, table = pieces
    dim = params[0].shape[0]
    width, conv_cols = heads * size, params[1].shape[1]
    blocks = len(table)
    tokens = blocks * GROUP

    def moving(columns):
        return pl.BlockSpec((GROUP, columns), lambda turn, place: (turn, 0))

    def rows_of_block(height, columns):
        return pl.BlockSpec((1, height, columns), lambda turn, place: (turn, 0, 0))

    results = pl.pallas_call(
        functools.partial(forward_kernel, dims, table, len(arrays)),
        grid_spec=pltpu.PrefetchScalarGridSpec(
            num_scalar_prefetch=1,
            grid=(blocks,),
            in_specs=[*anywhere(arrays), *[fixed(param.shape) for param in params]],
            out_specs=[
                moving(conv_cols),
                moving(conv_cols),
                moving(conv_cols),
                moving(width),
                moving(width),
                rows_of_block(8, GROUP),
                moving(width),
                rows_of_block(states, width),
                moving(width),
                rows_of_block(8, GROUP),
                moving(dim),
                *anywhere(range(4)),
            ],
            scratch_shapes=[
                pltpu.VMEM((states, width), f32),
                pltpu.VMEM((HALO + GROUP, conv_cols), f32),
                pltpu.VMEM((GROUP, GROUP), bf16),
                pltpu.VMEM((HALF, HALF), f32),
                pltpu.VMEM((2, GROUP, dim), bf16),
                pltpu.SemaphoreType.DMA((2,)),
                pltpu.VMEM((2, GROUP, width), bf16),
                pltpu.SemaphoreType.DMA((2,)),
            ],
        ),
        out_shape=[
            jax.ShapeDtypeStruct((tokens, conv_cols), bf16),
            jax.ShapeDtypeStruct((tokens, conv_cols), bf16),
            jax.ShapeDtypeStruct((tokens, conv_cols), bf16),
            jax.ShapeDtypeStruct((tokens, width), bf16),
            jax.ShapeDtypeStruct((tokens, width), bf16),
            jax.ShapeDtypeStruct((blocks, 8, GROUP), f32),
            jax.ShapeDtypeStruct((tokens, width), f32),
            jax.ShapeDtypeStruct((blocks, states, width), bf16),
            jax.ShapeDtypeStruct((tokens, width), bf16),
            jax.ShapeDtypeStruct((blocks, 8, GROUP), f32),
            jax.ShapeDtypeStruct((tokens, dim), bf16),
            *scatter_shapes(count, width),
        ],
        compiler_params=pltpu.CompilerParams(vmem_limit_bytes=60 * MIB),
        cost_estimate=time_estimate(blocks * 3.0, tokens * (4 * dim + 24 * width)),
        name="forward_blocks",
    )(place, *arrays, *params)
    return results[:11], results[11:]


def out_grad_kernel(table, given, place_ref, *refs):
    arrays, refs = refs[:given], refs[given:]
    scaled_ref, out_rows_ref, out_grad_ref, slope_ref, cot_ref = refs[:5]
    buffer, semaphores, copied = refs[5:]
    place, turn = place_ref[0], pl.program_id(0)
    rows = buffer.shape[1]

    def copy_on(turn):
        target = cot_ref.at[pl.ds(pl.multiple_of(turn * rows, rows), rows)]
        return pltpu.make_async_copy(buffer.at[lax.rem(turn, 2)], target, copied)

    @pl.when(turn >= 1)
    def _():
        copy_on(turn - 1).wait()

    cot = fetched(arrays, table, buffer, semaphores, lambda block: in_time(place, block), 2)
    copy_on(turn).start()
    out_grad = dot_nt(cot, out_rows_ref[...])
    out_grad_ref[...] = out_grad
    for block in range(2):
        here = slice(block * GROUP, (block + 1) * GROUP)
        slope_ref[block] = sum_lanes(out_grad[here] * scaled_ref[here].astype(f32))

    @pl.when(turn == pl.num_programs(0) - 1)
    def _():
        copy_on(turn).wait()


def run_out_grad(place, cots, scaled, out_rows):
    arrays, table = cots
    width, dim = out_rows.shape
    blocks = len(table)
    tokens = blocks * GROUP
    return pl.pallas_call(
        functools.partial(out_grad_kernel, table, len(arrays)),
        grid_spec=pltpu.PrefetchScalarGridSpec(
            num_scalar_prefetch=1,
            grid=(blocks // 2,),
            in_specs=[
                *anywhere(arrays),
                pl.BlockSpec((2 * GROUP, width), lambda turn, place: (turn, 0)),
                fixed(out_rows.shape),
            ],
            out_specs=[
                pl.BlockSpec((2 * GROUP, width), lambda turn, place: (turn, 0)),
                pl.BlockSpec((2, 8, GROUP), lambda turn, place: (turn, 0, 0)),
                *anywhere(range(1)),
            ],
            scratch_shapes=[
                pltpu.VMEM((2, 2 * GROUP, dim), bf16),
                pltpu.SemaphoreType.DMA((2,)),
                pltpu.SemaphoreType.DMA,
            ],
        ),
        out_shape=[
            jax.ShapeDtypeStruct((tokens, width), f32),
            jax.ShapeDtypeStruct((blocks, 8, GROUP), f32),
            jax.ShapeDtypeStruct((tokens, dim), bf16),
        ],
        compiler_params=pltpu.CompilerParams(vmem_limit_bytes=60 * MIB),
        cost_estimate=time_estimate(12, tokens * (4 * dim + 6 * width)),
        name="out_grad",
    )(place, *arrays, scaled, out_rows)


def backward_kernel(dims, place_ref, *refs):
    heads, size, states, count = dims
    width = heads * size
    conv_cols = width + 2 * states
    conv_in_ref, active_ref, slope_ref, gate_act_ref, gate_slope_ref = refs[:5]
    raw_ref, ssd_ref, start_ref, out_grad_ref, norm_ref = refs[5:10]
    conv_w_ref, step_ref, rows_ref = refs[10:13]
    out_ref, targets = refs[13], refs[14:18]
    sums = refs[18:24]
    gain_ref, skip_ref, conv_wg_ref, conv_bg_ref, bias_ref, rate_ref = sums
    state, pre_grads, order, back_order, barred, placed, semaphores = refs[24:]
    taps = conv_w_ref.shape[0]
    turn = pl.program_id(0)
    slot = lax.rem(turn, 2)

    @pl.when(turn >= 2)
    def _():
        stored(placed, targets, semaphores, slot)

    @pl.when(pl.program_id(0) == 0)
    def _():
        state[...] = jnp.zeros_like(state)
        pre_grads[0:HALO] = jnp.zeros_like(pre_grads[0:HALO])
        for total in sums:
            total[...] = jnp.zeros_like(total)
        row, column = order_indices(GROUP)
        order[...] = ones_where(row <= column)
        back_order[...] = ones_where(row >= column)
        row, column = order_indices(HALF)
        barred[...] = jnp.where(row <= column, 0.0, -1e30)

    gate_act, ssd, out_grad = gate_act_ref[...].astype(f32), ssd_ref[...], out_grad_ref[...]
    norms = norm_ref[0].T
    scale, slope = norms[:, 0:1], norms[:, 1:2]
    gated = ssd * gate_act
    gain_ref[...] += jnp.sum(out_grad * (gated * scale), axis=0, keepdims=True)
    gated_grad = out_grad * (rows_ref[1:2] * scale) - gated * slope
    grad_low = (gated_grad * gate_act).astype(bf16)
    gate_grad = (gated_grad * ssd * gate_slope_ref[...].astype(f32)).astype(bf16)
    out_ref[:, :width] = gate_grad
    placed[slot, :, :width] = gate_grad
    ssd_grad = grad_low.astype(f32)

    raw = raw_ref[0] + step_ref[0:8, 0:1]
    rate = step_ref[8:16, 0:1]
    step, sig, log_step, ratio = step_values(raw)
    decay = step * rate
    running = sum_along(decay, order[...])
    later = running - log_step
    total = running[:, GROUP - 1 :]
    columns = to_columns([later * LOG2E, jnp.exp(running), jnp.exp(total - later)])
    running = running * LOG2E
    early_wide = spread_heads(columns, 8, heads, size)
    tail_wide = spread_heads(columns, 16, heads, size)

    signal = active_ref[:, :width]
    entry = active_ref[:, width : width + states]
    readout = active_ref[:, width + states :]
    signal_wide = signal.astype(f32)
    start_low = start_ref[0]
    end_grad = state[...]
    end_low = end_grad.astype(bf16)
    first, second = slice(0, HALF), slice(HALF, GROUP)
    scores = dot_nt(entry[first], readout)
    later_scores = dot_nt(entry[second], readout[second])
    near_grad, far_grad, last_grad = 0.0, 0.0, 0.0
    within = []
    for h in range(heads):
        part, grad = signal[:, h * size : (h + 1) * size], grad_low[:, h * size : (h + 1) * size]
        begin, end = columns[first, h : h + 1], columns[second, h : h + 1]
        row_first, row_second = running[h : h + 1, first], running[h : h + 1, second]
        near = jnp.exp2(row_first - begin + barred[...])
        full = jnp.exp2(row_second - begin)
        last = jnp.exp2(row_second - end + barred[...])
        both = jnp.concatenate(
            [
                (near * scores[:, first]).astype(bf16),
                (full * scores[:, second]).astype(bf16),
            ],
            axis=1,
        )
        final = (last * later_scores).astype(bf16)
        within.append(jnp.concatenate([dot(both, grad), dot(final, grad[second])], axis=0))
        cross = dot_nt(part[first], grad)
        near_grad = near_grad + cross[:, first] * near
        far_grad = far_grad + cross[:, second] * full
        last_grad = last_grad + dot_nt(part[second], grad[second]) * last
    tail_grad = tail_wide * dot(entry, end_low)
    signal_grad = jnp.concatenate(within, axis=1) + tail_grad
    score_first = jnp.concatenate([near_grad, far_grad], axis=1).astype(bf16)
    score_second = last_grad.astype(bf16)
    tail = (signal_wide * tail_wide).astype(bf16)
    head_grad = (ssd_grad * early_wide).astype(bf16)
    entry_grad = jnp.concatenate(
        [dot(score_first, readout), dot(score_second, readout[second])], axis=0
    ) + dot_nt(tail, end_low)
    readout_grad = dot_tn(score_first, entry[first]) + dot_nt(head_grad, start_low)
    readout_last = readout_grad[second] + dot_tn(score_second, entry[second])
    total_wide = early_wide[GROUP - 1 :]
    state[...] = end_grad * total_wide + dot_tn(readout, head_grad)

    skip = rows_ref[0:1]
    ones = head_ones(width, size)
    column_part = signal_wide * signal_grad
    row_part = ssd_grad * (ssd - skip * signal_wide)
    end_part = jnp.sum(signal_wide * tail_grad, axis=0, keepdims=True) + total_wide * jnp.sum(
        start_low.astype(f32) * end_grad, axis=0, keepdims=True
    )

    def head_sums(value, parts):
        return sum(dot_nt(ones, part) for part in split_parts(value, parts))

    end_rows = head_sums(jnp.broadcast_to(end_part, (8, width)), 2)[:, 0:1]
    decay_grad = sum_along(head_sums(row_part - column_part, 2), back_order[...]) + end_rows
    raw_grad = head_sums(column_part, 1) * ratio + decay_grad * rate * sig
    skip_ref[...] += jnp.sum(ssd_grad * signal_wide, axis=0, keepdims=True)
    bias_ref[...] += raw_grad
    rate_ref[...] += decay_grad * decay
    raw_low = to_columns([raw_grad]).astype(bf16)
    out_ref[:, width + conv_cols :] = raw_low
    placed[slot, :, width + conv_cols :] = raw_low

    pre_grads[GROUP : GROUP + HALO] = pre_grads[0:HALO]
    pre_grads[0:GROUP, :width] = (signal_grad + skip * ssd_grad) * slope_ref[:, :width].astype(f32)
    sides = slope_ref[:, width:].astype(f32)
    pre_grads[0:GROUP, width : width + states] = entry_grad * sides[:, :states]
    pre_grads[0:HALF, width + states :] = readout_grad[first] * sides[first, states:]
    pre_grads[HALF:GROUP, width + states :] = readout_last * sides[second, states:]
    conv_w = conv_w_ref[...]
    conv_in = conv_in_ref[...].astype(f32)
    conv_grad = 0.0
    for k in range(taps):
        ahead = taps - 1 - k
        shifted = pre_grads[ahead : ahead + GROUP]
        conv_grad = conv_grad + conv_w[k : k + 1] * shifted
        conv_wg_ref[k : k + 1] += jnp.sum(shifted * conv_in, axis=0, keepdims=True)
        if ahead == 0:
            conv_bg_ref[...] += jnp.sum(shifted, axis=0, keepdims=True)
    conv_low = conv_grad.astype(bf16)
    out_ref[:, width : width + conv_cols] = conv_low
    placed[slot, :, width : width + conv_cols] = conv_low

    where = in_time(place_ref[0], pl.num_programs(0) - 1 - turn)
    store(placed.at[slot], targets, scatter_places(count), where, semaphores.at[slot])

    @pl.when(turn == pl.num_programs(0) - 1)
    def _():
        for other in range(2):
            stored(placed, targets, semaphores, other)


def run_backward(place, values, params, dims):
    heads, size, states, count = dims
    conv_cols, width = values[0].shape[1], heads * size
    tokens = values[0].shape[0]
    blocks = tokens // GROUP
    last = blocks - 1
    out_cols = width + conv_cols + LANES

    def moving(columns):
        return pl.BlockSpec((GROUP, columns), lambda turn, place: (last - turn, 0))

    def rows_of_block():
        return pl.BlockSpec((1, 8, GROUP), lambda turn, place: (last - turn, 0, 0))

    sums = [(1, width), (1, width), params[0].shape, (1, conv_cols), (8, GROUP), (8, GROUP)]
    return pl.pallas_call(
        functools.partial(backward_kernel, dims),
        grid_spec=pltpu.PrefetchScalarGridSpec(
            num_scalar_prefetch=1,
            grid=(blocks,),
            in_specs=[
                moving(conv_cols),
                moving(conv_cols),
                moving(conv_cols),
                moving(width),
                moving(width),
                rows_of_block(),
                moving(width),
                pl.BlockSpec((1, states, width), lambda turn, place: (last - turn, 0, 0)),
                moving(width),
                rows_of_block(),
                *[fixed(param.shape) for param in params],
            ],
            out_specs=[
                moving(out_cols),
                *anywhere(range(4)),
                *[fixed(shape) for shape in sums],
            ],
            scratch_shapes=[
                pltpu.VMEM((states, width), f32),
                pltpu.VMEM((GROUP + HALO, conv_cols), f32),
                pltpu.VMEM((GROUP, GROUP), bf16),
                pltpu.VMEM((GROUP, GROUP), bf16),
                pltpu.VMEM((HALF, HALF), f32),
                pltpu.VMEM((2, GROUP, out_cols), bf16),
                pltpu.SemaphoreType.DMA((2,)),
            ],
        ),
        out_shape=[
            jax.ShapeDtypeStruct((tokens, out_cols), bf16),
            *scatter_shapes(count, out_cols),
        ]
        + [jax.ShapeDtypeStruct(shape, f32) for shape in sums],
        compiler_params=pltpu.CompilerParams(vmem_limit_bytes=60 * MIB),
        cost_estimate=time_estimate(blocks * 3.5, tokens * 40 * width),
        name="backward_blocks",
    )(place, *values, *params)


def widen_kernel(place_ref, piece_ref, out_ref):
    out_ref[...] = piece_ref[0].astype(f32)


def assemble_out(place, pieces, per):
    count, size, dim = pieces.shape
    groups = count // per

    def source(turn, place):
        relative = (turn % groups * per + turn // groups) ^ place[0]
        return ((relative & 1) * (count // 2) + (relative >> 1), 0, 0)

    return pl.pallas_call(
        widen_kernel,
        grid_spec=pltpu.PrefetchScalarGridSpec(
            num_scalar_prefetch=1,
            grid=(count,),
            in_specs=[pl.BlockSpec((1, size, dim), source)],
            out_specs=pl.BlockSpec((size, dim), lambda turn, place: (turn, 0)),
        ),
        out_shape=jax.ShapeDtypeStruct((count * size, dim), f32),
        cost_estimate=time_estimate(5, count * size * dim * 6),
        name="assemble_out_weight_grad",
    )(place, pieces)


def assemble_kernel(dims, pieces_ref, out_ref):
    heads, size, states, count = dims
    width, shared = heads * size, 2 * states
    inner = count * width
    total = 0.0
    for device in range(count):
        columns = pieces_ref[device].astype(f32).T
        out_ref[device * width : (device + 1) * width] = columns[:width]
        out_ref[inner + device * width : inner + (device + 1) * width] = columns[width : 2 * width]
        total = total + columns[2 * width : 2 * width + shared]
        last = 2 * inner + shared + device * heads
        out_ref[last : last + heads] = columns[2 * width + shared : 2 * width + shared + heads]
    out_ref[2 * inner : 2 * inner + shared] = total


def assemble(pieces, dims):
    heads, size, states, count = dims
    _, rows, columns = pieces.shape
    tile = LANES if rows % LANES == 0 else rows
    out_rows = 2 * count * heads * size + 2 * states + count * heads
    return pl.pallas_call(
        functools.partial(assemble_kernel, dims),
        grid=(rows // tile,),
        in_specs=[pl.BlockSpec((count, tile, columns), lambda turn: (0, turn, 0))],
        out_specs=pl.BlockSpec((out_rows, tile), lambda turn: (0, turn)),
        out_shape=jax.ShapeDtypeStruct((out_rows, rows), f32),
        compiler_params=pltpu.CompilerParams(vmem_limit_bytes=60 * MIB),
        cost_estimate=time_estimate(8, out_rows * rows * 6),
        name="assemble_in_weight_grad",
    )(pieces)


def body(
    tokens,
    norm_gain,
    in_weight,
    conv_weight,
    conv_bias,
    dt_bias,
    decay_log,
    skip_scale,
    gate_gain,
    out_weight,
    cotangent,
):
    count, mine = lax.axis_size("seq"), lax.axis_index("seq")
    place = mine.astype(jnp.int32).reshape(1)
    inner, all_heads, conv_all = gate_gain.shape[0], dt_bias.shape[0], conv_bias.shape[0]
    size, states = inner // all_heads, (conv_all - inner) // 2
    heads, width = all_heads // count, inner // count
    dims = (heads, size, states, count)
    shared = 2 * states
    conv_cols = width + shared
    tok_rows = tokens.shape[1]
    per_plane = out_weight.shape[0] // width

    def own(vector, per, first=0):
        return lax.dynamic_slice_in_dim(vector, first + mine * per, per, vector.ndim - 1)

    def own_conv(array, first=0):
        return jnp.concatenate(
            [own(array, width, first), array[..., first + inner : first + conv_all]], axis=-1
        )

    tokens_row = tokens[0].astype(f32)
    inverse = lax.rsqrt(jnp.mean(tokens_row * tokens_row, axis=-1, keepdims=True) + epsilon)
    normed_own = (tokens_row * inverse * norm_gain).astype(bf16)
    step_own = own(in_weight, heads, inner + conv_all)
    w_own = jnp.concatenate(
        [
            own(in_weight, width),
            own_conv(in_weight, inner),
            jnp.pad(step_own, ((0, 0), (0, LANES - heads))),
        ],
        axis=1,
    )
    w_cols = lax.all_gather(w_own, "batch", axis=0, tiled=True)
    stages = gather_stages()
    held = gather_stage(gather_stage(gather_start(normed_own), 0), 1)
    held, cots = together(held, gather_start(cotangent[0]))
    cots = gather_stage(cots, 0)
    for stage in range(2, stages):
        held = gather_stage(held, stage)
    w_cols, held, cots, out_owned = together(w_cols, held, cots, out_weight)
    cots = gather_stage(cots, 1)
    out_rows = rows_from_owner(out_owned, width)

    conv_w, conv_b = own_conv(conv_weight), own_conv(conv_bias)[None]
    per_head = jnp.stack([own(dt_bias, heads), -jnp.exp(own(decay_log, heads))])
    per_head = jnp.pad(per_head, ((0, 0), (0, 8 - heads))).reshape(16, 1)
    step_rows = jnp.broadcast_to(per_head, (16, LANES))
    gain_own = own(gate_gain, width)[None]
    rows = jnp.concatenate(
        [jnp.repeat(own(skip_scale, heads), size)[None], gain_own, jnp.zeros((6, width), f32)],
        axis=0,
    )
    results, out_parts = run_forward(
        place, token_pieces(held), (w_cols, conv_w, conv_b, step_rows, rows), dims
    )
    conv_in, active, slope, gate_act, gate_slope, raw, ssd, starts, scaled, squares, normed = results
    out_parts, cots, out_rows = together(out_parts, cots, out_rows)
    for stage in range(2, stages):
        cots = gather_stage(cots, stage)

    def out_product(part):
        return dot(part, out_rows)

    out_send = out_product(out_parts[0]).astype(bf16)
    out_send, cots = together(out_send, cots)
    out_grad, slopes, cot = run_out_grad(place, token_pieces(cots), scaled, out_rows)
    sums = jnp.stack([squares[:, 0].reshape(-1), slopes[:, 0].reshape(-1)])
    out_ready, out_held = scatter_near(out_product, out_parts[1:], out_send)
    sums = sums + exchange(sums, "seq", 1)
    sums, first = together(sums, out_ready[0])
    sums = sums + exchange(sums, "seq", 2)
    sums, second = together(sums, out_ready[1])
    for bit in bits_of(count)[2:]:
        sums = sums + exchange(sums, "seq", bit)
    scale = lax.rsqrt(sums[0] / inner + epsilon)
    norms = jnp.stack([scale, scale * scale * scale * sums[1] / inner])
    norms = jnp.pad(norms, ((0, 6), (0, 0))).reshape(8, -1, GROUP).swapaxes(0, 1)
    normed_out = (scaled.astype(f32) * scale[:, None]).astype(bf16)
    out_term = jnp.einsum("te,td->ed", normed_out, cot, preferred_element_type=f32)
    out_term, norms, first, second = together(out_term.astype(bf16), norms, first, second)
    out_sum = lax.psum_scatter(out_term, "batch", scatter_dimension=0, tiled=True)
    out_ready, out_held = scatter_far((first, second), out_held, 0)

    values = (conv_in, active, slope, gate_act, gate_slope, raw, ssd, starts, out_grad, norms)
    results = run_backward(place, values, (conv_w, step_rows, rows), dims)
    proj_grad, back_parts = results[0], results[1:5]
    proj_grad, back_parts, out_ready, out_held, out_sum = together(
        proj_grad, back_parts, out_ready, out_held, out_sum
    )

    def back_product(part):
        return jnp.einsum("tf,df->td", part, w_cols, preferred_element_type=f32)

    def weight_product(part):
        return jnp.einsum("td,tf->df", normed, part, preferred_element_type=f32).astype(bf16)

    for stage in range(1, stages - 1):
        out_ready, out_held = scatter_far(out_ready, out_held, stage)
    back_send = back_product(back_parts[0]).astype(bf16)
    back_send, proj_grad = together(back_send, proj_grad)
    in_term = weight_product(proj_grad)
    in_term, keeps, out_held = together(in_term, back_parts[1:], out_held)
    in_sum = lax.psum_scatter(in_term, "batch", scatter_dimension=0, tiled=True)
    back_ready, back_held = scatter_near(back_product, keeps, back_send)
    back_ready, out_sum = together(back_ready, out_sum)
    back_ready, back_held = scatter_far(back_ready, back_held, 0)
    out_pieces = to_owner(out_sum)[None]

    back_held["kept"], in_term, results = together(back_held["kept"], in_term, results[5:])
    gain_term, skip_term, conv_w_term, conv_b_term, bias_term, rate_term = results
    norm_gain_term = jnp.sum(in_term.astype(f32) * w_cols.astype(f32), axis=1) / norm_gain

    def among_heads(vector, per, total):
        return lax.dynamic_update_slice_in_dim(jnp.zeros((total,), f32), vector, mine * per, 0)

    def among_conv(array):
        wide = jnp.zeros((array.shape[0], inner), f32)
        wide = lax.dynamic_update_slice_in_dim(wide, array[:, :width], mine * width, 1)
        return jnp.concatenate([wide, array[:, width:]], axis=1).reshape(-1)

    skip_heads = jnp.sum(skip_term.reshape(heads, size), axis=1)
    terms = [
        norm_gain_term,
        among_conv(conv_w_term),
        among_conv(conv_b_term),
        among_heads(jnp.sum(bias_term[:heads], axis=1), heads, all_heads),
        among_heads(jnp.sum(rate_term[:heads], axis=1), heads, all_heads),
        among_heads(skip_heads, heads, all_heads),
        among_heads(gain_term[0], width, inner),
    ]
    vector = jnp.concatenate(terms)
    padding = -vector.shape[0] % (8 * LANES)
    vector = jnp.pad(vector, (0, padding)).reshape(-1, LANES)

    axes = [(axis, bit) for axis in ("seq", "batch") for bit in bits_of(lax.axis_size(axis))]
    vector = vector + exchange(vector, *axes.pop(0))
    back_ready, vector, out_pieces = together(back_ready, vector, out_pieces)
    for stage in range(1, stages - 1):
        back_ready, back_held = scatter_far(back_ready, back_held, stage)
    out_pieces = double(out_pieces, 0)
    vector = vector + exchange(vector, *axes.pop(0))
    back_held["arrived"], vector, out_pieces, in_sum = together(
        back_held["arrived"], vector, out_pieces, in_sum
    )
    pieces = lax.all_gather(in_sum, "seq", axis=0, tiled=False)
    in_weight_grad = assemble(pieces, dims).T
    for stage in range(1, stages):
        out_pieces = double(out_pieces, stage)
    while axes:
        vector = vector + exchange(vector, *axes.pop(0))
    vector = vector.reshape(-1)
    normed_grad = scatter_end(back_held)
    cot_row = cotangent[0].astype(f32)
    gained = norm_gain * normed_grad
    slope = inverse * inverse * inverse * jnp.mean(gained * tokens_row, axis=-1, keepdims=True)
    input_grad = cot_row + inverse * gained - tokens_row * slope
    own_scale = lax.dynamic_slice_in_dim(scale, mine * tok_rows, tok_rows, 0)[:, None]
    block_out = (tokens_row + own_scale * scatter_end(out_held)).astype(bf16)
    out_weight_grad = assemble_out(place, out_pieces, per_plane)

    parts, offset = [], 0
    for term in terms:
        parts.append(vector[offset : offset + term.shape[0]])
        offset += term.shape[0]
    return (
        block_out[None],
        input_grad[None],
        parts[0],
        in_weight_grad,
        parts[1].reshape(conv_weight.shape),
        parts[2],
        parts[3],
        parts[4],
        parts[5],
        parts[6],
        out_weight_grad,
    )


def solution(mesh):
    placed = (
        P("batch", "seq", None),
        P(),
        P("batch", None),
        P(),
        P(),
        P(),
        P(),
        P(),
        P(),
        P("batch", None),
        P("batch", "seq", None),
    )
    return jax.shard_map(
        body,
        mesh=mesh,
        in_specs=placed,
        out_specs=(
            P("batch", "seq", None),
            P("batch", "seq", None),
            P(),
            P("batch", None),
            P(),
            P(),
            P(),
            P(),
            P(),
            P(),
            P("batch", None),
        ),
        check_vma=False,
    )
```

```python
import functools

import jax
import jax.numpy as jnp
from jax import lax
from jax.experimental import pallas as pl
from jax.experimental.pallas import tpu as pltpu
from jax.sharding import PartitionSpec as P

GROUP = 256
LANES = 128
HALF = GROUP // 2
HALO = 8
STEP_ROWS = 16
LOG2E = 1.4426950408889634
epsilon = 1e-05
f32 = jnp.float32
bf16 = jnp.bfloat16
MIB = 2**20


def exchange(value, axis, distance):
    count = lax.axis_size(axis)
    return lax.ppermute(value, axis, [(source, source ^ distance) for source in range(count)])


def bits_of(count):
    return [1 << k for k in range(count.bit_length() - 1)]


def placed_order(count):
    return [2 * k for k in range(count // 2)] + [2 * k + 1 for k in range(count // 2)]


def together(*values):
    return lax.optimization_barrier(values)


def far_orders():
    far = bits_of(lax.axis_size("seq"))[1:]
    return far, far[::-1]


def gather_start(value):
    half = value.shape[0] // 32 * 16
    return tuple({"base": part, "fresh": None, "near": []} for part in (value[:half], value[half:]))


def gather_stage(held, stage, late=False):
    grown = []
    for half, order in zip(held, far_orders()):
        base, fresh, near = half["base"], half["fresh"], list(half["near"])
        if stage >= 1:
            merged = base if stage == len(order) else jnp.concatenate([base, fresh], axis=0)
            if not late:
                near.append(exchange(merged if stage == 1 else fresh, "seq", 1))
            elif stage == len(order):
                near = [exchange(base, "seq", 1), exchange(fresh, "seq", 1)]
            base = merged
        if stage < len(order):
            fresh = exchange(base, "seq", order[stage])
        grown.append({"base": base, "fresh": fresh, "near": near})
    return tuple(grown)


def gather_stages():
    return len(bits_of(lax.axis_size("seq")))


def gathered(held):
    arrays, table = [], {}
    for number, (half, order) in enumerate(zip(held, far_orders())):
        indices = [0]
        for bit in order:
            indices += [index | bit for index in indices]
        middle = len(indices) // 2
        groups = [(half["base"], indices[:middle]), (half["fresh"], indices[middle:])]
        bounds = [0] + [2 << k for k in range(len(order))]
        if len(half["near"]) < len(order):
            bounds = [0, middle, len(indices)]
        for value, first, last in zip(half["near"], bounds, bounds[1:]):
            groups.append((value, [index | 1 for index in indices[first:last]]))
        for value, members in groups:
            rows = value.shape[0] // len(members)
            for turn, index in enumerate(members):
                table[number, index] = (len(arrays), turn * rows, rows)
            arrays.append(value)
    return arrays, table


def token_pieces(held):
    arrays, table = gathered(held)
    indices = range(lax.axis_size("seq"))
    return arrays, tuple(table[half, index] for index in indices for half in range(2))


def gather_all(value):
    held = gather_start(value)
    for stage in range(gather_stages()):
        held = gather_stage(held, stage)
    return held


def scatter_places(count):
    far = bits_of(count)[1:]
    table = {}
    row = {}
    for near in (1, 0):
        for sent in (True, False):
            for half, order in enumerate((far, far[::-1])):
                members = [0]
                for bit in order[:0:-1]:
                    members += [member | bit for member in members]
                for member in members:
                    index = member | near | (order[0] if sent else 0)
                    array = 0 if near else (1 + half if sent else 3)
                    table[index * 2 + half] = (array, row.get(array, 0))
                    row[array] = row.get(array, 0) + GROUP
    return tuple(table[k] for k in range(2 * count))


def scatter_shapes(count, columns):
    blocks = (count, count // 4, count // 4, count // 2)
    return [jax.ShapeDtypeStruct((part * GROUP, columns), bf16) for part in blocks]


def scatter_near(product, parts, sent):
    arriving = exchange(sent, "seq", 1)
    first, second, kept = parts
    rows = first.shape[0]

    def summed(part, row):
        return (product(part) + arriving[row : row + part.shape[0]].astype(f32)).astype(bf16)

    sends = (summed(first, 0), summed(second, rows))
    sends, kept = together(sends, kept)
    return sends, {"kept": summed(kept, 2 * rows), "arrived": ([], [])}


def scatter_rows(held, half, first, last):
    top = half * (held["kept"].shape[0] // 2)
    total = held["kept"][top + first : top + last].astype(f32)
    for value in held["arrived"][half]:
        total = total + value[first:last].astype(f32)
    return total


def scatter_far(sends, held, stage):
    orders = far_orders()
    arrived = tuple(
        [*held["arrived"][half], exchange(sends[half], "seq", orders[half][stage])]
        for half in range(2)
    )
    held = {"kept": held["kept"], "arrived": arrived}
    rows = sends[0].shape[0]
    if stage + 1 == len(orders[0]):
        return (), held
    ready = tuple(
        scatter_rows(held, half, rows // 2, rows).astype(bf16) for half in range(2)
    )
    return ready, held


def scatter_end(held):
    rows = held["arrived"][0][-1].shape[0]
    return jnp.concatenate([scatter_rows(held, half, 0, rows) for half in range(2)], axis=0)


def sum_seq(value):
    for bit in bits_of(lax.axis_size("seq")):
        value = value + exchange(value, "seq", bit)
    return value


def plane_pairs(ahead):
    planes, count = lax.axis_size("batch"), lax.axis_size("seq")
    per = count // planes
    pairs = []
    for owner in range(planes):
        for piece in range(planes):
            for k in range(per):
                holder = owner * count + piece * per + k
                user = (piece + ahead) % planes * count + owner * per + k
                pairs.append((holder, user))
    return pairs


def rows_from_owner(out_weight, width):
    per = lax.axis_size("seq") // lax.axis_size("batch")
    plane, mine = lax.axis_index("batch"), lax.axis_index("seq")
    rows = lax.dynamic_slice_in_dim(out_weight, mine % per * width, width, 0)
    return lax.psum(jnp.where(plane == mine // per, rows, jnp.zeros_like(rows)), "batch")


def to_owner(summed):
    return lax.ppermute(
        summed, ("batch", "seq"), [(user, holder) for holder, user in plane_pairs(0)]
    )


def double(held, turn):
    bits = bits_of(lax.axis_size("seq"))
    return jnp.concatenate([held, exchange(held, "seq", (bits[1:] + [1])[turn])], axis=0)


def step_values(raw):
    small = jnp.exp(-jnp.abs(raw))
    step = jnp.maximum(raw, 0.0) + jnp.log1p(small)
    sig = jnp.where(raw >= 0, 1.0, small) / (1.0 + small)
    tiny = raw < -20.0
    log_step = jnp.where(tiny, raw, jnp.log(step))
    ratio = jnp.where(tiny, 1.0, sig / step)
    return step, sig, log_step, ratio


def dot(a, b):
    return jnp.dot(a, b, preferred_element_type=f32)


def dot_nt(a, b):
    return lax.dot_general(a, b, (((1,), (1,)), ((), ())), preferred_element_type=f32)


def dot_tn(a, b):
    return lax.dot_general(a, b, (((0,), (0,)), ((), ())), preferred_element_type=f32)


def sigmoid(value):
    return 0.5 * jnp.tanh(0.5 * value) + 0.5


def silu_slope(value):
    sig = sigmoid(value)
    active = value * sig
    return active, sig + active * (1.0 - sig)


def split_parts(value, count):
    parts = []
    for _ in range(count):
        part = value.astype(bf16)
        parts.append(part)
        value = value - part.astype(f32)
    return parts


def sum_along(rows, order):
    parts = jnp.concatenate([part.astype(f32) for part in split_parts(rows, 3)], axis=0)
    total = dot(parts.astype(bf16), order)
    return total[:8] + total[8:16] + total[16:24]


def to_columns(rows):
    stacked = jnp.concatenate(rows, axis=0)
    missing = LANES - stacked.shape[0]
    return jnp.concatenate([stacked, jnp.zeros((missing, GROUP), f32)], axis=0).T


def spread_heads(value, first, heads, size):
    rows = value.shape[0]
    return jnp.concatenate(
        [jnp.broadcast_to(value[:, first + h : first + h + 1], (rows, size)) for h in range(heads)],
        axis=1,
    )


def head_ones(width, size):
    row = lax.broadcasted_iota(jnp.int32, (8, width), 0)
    column = lax.broadcasted_iota(jnp.int32, (8, width), 1)
    return (column // size == row).astype(f32).astype(bf16)


def sum_lanes(value):
    return dot_nt(jnp.ones((8, value.shape[1]), bf16), value.astype(bf16))


def ones_where(condition):
    return jnp.where(condition, 1.0, 0.0).astype(bf16)


def order_indices(length):
    row = lax.broadcasted_iota(jnp.int32, (length, length), 0)
    column = lax.broadcasted_iota(jnp.int32, (length, length), 1)
    return row, column


def fetch(arrays, table, which, target, semaphore):
    for index, (array, row, rows) in enumerate(table):

        @pl.when(which == index)
        def _():
            pltpu.make_async_copy(arrays[array].at[pl.ds(row, rows)], target, semaphore).start()


def fetched(arrays, table, buffer, semaphores, order, blocks=1):
    step = pl.program_id(0)
    slot, other = lax.rem(step, 2), lax.rem(step + 1, 2)

    def start(step, slot):
        for k in range(blocks):
            target = buffer.at[slot, pl.ds(k * GROUP, GROUP)]
            fetch(arrays, table, order(step * blocks + k), target, semaphores.at[slot])

    @pl.when(step == 0)
    def _():
        start(0, 0)

    @pl.when(step + 1 < pl.num_programs(0))
    def _():
        start(step + 1, other)

    for k in range(blocks):
        source = arrays[0].at[pl.ds(0, GROUP)]
        target = buffer.at[slot, pl.ds(k * GROUP, GROUP)]
        pltpu.make_async_copy(source, target, semaphores.at[slot]).wait()
    return buffer[slot]


def store(source, targets, table, which, semaphore):
    for index, (array, row) in enumerate(table):

        @pl.when(which == index)
        def _():
            target = targets[array].at[pl.ds(row, GROUP)]
            pltpu.make_async_copy(source, target, semaphore).start()


def stored(buffer, targets, semaphores, slot):
    target = targets[0].at[pl.ds(0, GROUP)]
    pltpu.make_async_copy(buffer.at[slot], target, semaphores.at[slot]).wait()


def in_time(place, block):
    return ((block // 2) ^ place) * 2 + block % 2


def forward_kernel(dims, table, given, place_ref, *refs):
    heads, size, states, count = dims
    width = heads * size
    conv_cols = width + 2 * states
    arrays, refs = refs[:given], refs[given:]
    w_ref, conv_w_ref, conv_b_ref, step_ref, rows_ref = refs[:5]
    conv_in_ref, active_ref, slope_ref, gate_act_ref, gate_slope_ref = refs[5:10]
    raw_ref, ssd_ref, start_ref, scaled_ref, square_ref, normed_ref = refs[10:16]
    targets = refs[16:20]
    state, padded, order, barred, buffer, semaphores, placed, out_semaphores = refs[20:]
    turn = pl.program_id(0)
    slot = lax.rem(turn, 2)

    @pl.when(turn == 0)
    def _():
        state[...] = jnp.zeros_like(state)
        padded[0:HALO] = jnp.zeros_like(padded[0:HALO])
        row, column = order_indices(GROUP)
        order[...] = ones_where(row <= column)
        row, column = order_indices(HALF)
        barred[...] = jnp.where(row >= column, 0.0, -1e30)

    @pl.when(turn >= 2)
    def _():
        stored(placed, targets, out_semaphores, slot)

    normed = fetched(
        arrays, table, buffer, semaphores, lambda step: in_time(place_ref[0], step)
    )
    normed_ref[...] = normed
    projected = dot(normed, w_ref[...])
    conv_in = projected[:, width : width + conv_cols].astype(bf16)
    conv_in_ref[...] = conv_in
    padded[HALO : HALO + GROUP] = conv_in.astype(f32)
    conv_w = conv_w_ref[...]
    taps = conv_w.shape[0]
    pre = conv_b_ref[...]
    for k in range(taps):
        top = HALO - (taps - 1) + k
        pre = pre + conv_w[k : k + 1] * padded[top : top + GROUP]
    padded[0:HALO] = padded[GROUP : GROUP + HALO]
    active, slope = silu_slope(pre)
    active = active.astype(bf16)
    active_ref[...] = active
    slope_ref[...] = slope.astype(bf16)
    signal = active[:, :width]
    entry = active[:, width : width + states]
    readout = active[:, width + states :]
    signal_wide = signal.astype(f32)

    raw = projected[:, width + conv_cols :].T[:8]
    raw_ref[0] = raw
    step, _, log_step, _ = step_values(raw + step_ref[0:8, 0:1])
    running = sum_along(step * step_ref[8:16, 0:1], order[...])
    later = running - log_step
    total = running[:, GROUP - 1 :]
    columns = to_columns([running * LOG2E, jnp.exp(running), jnp.exp(total - later)])
    later = later * LOG2E
    early_wide = spread_heads(columns, 8, heads, size)
    tail_wide = spread_heads(columns, 16, heads, size)
    first, second = slice(0, HALF), slice(HALF, GROUP)
    scores = dot_nt(readout[first], entry[first])
    later_scores = dot_nt(readout[second], entry)
    within = []
    for h in range(heads):
        part = signal[:, h * size : (h + 1) * size]
        begin, end = columns[first, h : h + 1], columns[second, h : h + 1]
        row_first, row_second = later[h : h + 1, first], later[h : h + 1, second]
        near = jnp.exp2(begin - row_first + barred[...]) * scores
        full = jnp.exp2(end - row_first) * later_scores[:, first]
        last = jnp.exp2(end - row_second + barred[...]) * later_scores[:, second]
        both = jnp.concatenate([full.astype(bf16), last.astype(bf16)], axis=1)
        within.append(
            jnp.concatenate([dot(near.astype(bf16), part[first]), dot(both, part)], axis=0)
        )
    start = state[...]
    start_low = start.astype(bf16)
    start_ref[0] = start_low
    carried = dot(readout, start_low) * early_wide
    ssd = jnp.concatenate(within, axis=1) + carried + rows_ref[0:1] * signal_wide
    tail = (signal_wide * tail_wide).astype(bf16)
    state[...] = start * early_wide[GROUP - 1 :] + dot_tn(entry, tail)

    gate_act, gate_slope = silu_slope(projected[:, :width])
    gate_act_ref[...] = gate_act.astype(bf16)
    gate_slope_ref[...] = gate_slope.astype(bf16)
    ssd_ref[...] = ssd
    gated = ssd * gate_act
    scaled = (gated * rows_ref[1:2]).astype(bf16)
    scaled_ref[...] = scaled
    square_ref[0] = sum_lanes(gated * gated)
    placed[slot] = scaled
    where = in_time(place_ref[0], turn)
    store(placed.at[slot], targets, scatter_places(count), where, out_semaphores.at[slot])

    @pl.when(turn == pl.num_programs(0) - 1)
    def _():
        for other in range(2):
            stored(placed, targets, out_semaphores, other)


def time_estimate(microseconds, accessed):
    return pl.CostEstimate(
        flops=int(microseconds * 1.1e9), bytes_accessed=int(accessed), transcendentals=0
    )


def fixed(shape):
    return pl.BlockSpec(shape, lambda turn, place: (0,) * len(shape), pipeline_mode=pl.Buffered(1))


def anywhere(values):
    return [pl.BlockSpec(memory_space=pltpu.HBM)] * len(values)


def run_forward(place, pieces, params, dims):
    heads, size, states, count = dims
    arrays, table = pieces
    dim = params[0].shape[0]
    width, conv_cols = heads * size, params[1].shape[1]
    blocks = len(table)
    tokens = blocks * GROUP

    def moving(columns):
        return pl.BlockSpec((GROUP, columns), lambda turn, place: (turn, 0))

    def rows_of_block(height, columns):
        return pl.BlockSpec((1, height, columns), lambda turn, place: (turn, 0, 0))

    results = pl.pallas_call(
        functools.partial(forward_kernel, dims, table, len(arrays)),
        grid_spec=pltpu.PrefetchScalarGridSpec(
            num_scalar_prefetch=1,
            grid=(blocks,),
            in_specs=[*anywhere(arrays), *[fixed(param.shape) for param in params]],
            out_specs=[
                moving(conv_cols),
                moving(conv_cols),
                moving(conv_cols),
                moving(width),
                moving(width),
                rows_of_block(8, GROUP),
                moving(width),
                rows_of_block(states, width),
                moving(width),
                rows_of_block(8, GROUP),
                moving(dim),
                *anywhere(range(4)),
            ],
            scratch_shapes=[
                pltpu.VMEM((states, width), f32),
                pltpu.VMEM((HALO + GROUP, conv_cols), f32),
                pltpu.VMEM((GROUP, GROUP), bf16),
                pltpu.VMEM((HALF, HALF), f32),
                pltpu.VMEM((2, GROUP, dim), bf16),
                pltpu.SemaphoreType.DMA((2,)),
                pltpu.VMEM((2, GROUP, width), bf16),
                pltpu.SemaphoreType.DMA((2,)),
            ],
        ),
        out_shape=[
            jax.ShapeDtypeStruct((tokens, conv_cols), bf16),
            jax.ShapeDtypeStruct((tokens, conv_cols), bf16),
            jax.ShapeDtypeStruct((tokens, conv_cols), bf16),
            jax.ShapeDtypeStruct((tokens, width), bf16),
            jax.ShapeDtypeStruct((tokens, width), bf16),
            jax.ShapeDtypeStruct((blocks, 8, GROUP), f32),
            jax.ShapeDtypeStruct((tokens, width), f32),
            jax.ShapeDtypeStruct((blocks, states, width), bf16),
            jax.ShapeDtypeStruct((tokens, width), bf16),
            jax.ShapeDtypeStruct((blocks, 8, GROUP), f32),
            jax.ShapeDtypeStruct((tokens, dim), bf16),
            *scatter_shapes(count, width),
        ],
        compiler_params=pltpu.CompilerParams(vmem_limit_bytes=60 * MIB),
        cost_estimate=time_estimate(blocks * 3.0, tokens * (4 * dim + 24 * width)),
        name="forward_blocks",
    )(place, *arrays, *params)
    return results[:11], results[11:]


def out_grad_kernel(table, given, place_ref, *refs):
    arrays, refs = refs[:given], refs[given:]
    scaled_ref, out_rows_ref, out_grad_ref, slope_ref, cot_ref = refs[:5]
    buffer, semaphores, copied = refs[5:]
    place, turn = place_ref[0], pl.program_id(0)
    rows = buffer.shape[1]

    def copy_on(turn):
        target = cot_ref.at[pl.ds(pl.multiple_of(turn * rows, rows), rows)]
        return pltpu.make_async_copy(buffer.at[lax.rem(turn, 2)], target, copied)

    @pl.when(turn >= 1)
    def _():
        copy_on(turn - 1).wait()

    cot = fetched(arrays, table, buffer, semaphores, lambda block: in_time(place, block), 2)
    copy_on(turn).start()
    out_grad = dot_nt(cot, out_rows_ref[...])
    out_grad_ref[...] = out_grad
    for block in range(2):
        here = slice(block * GROUP, (block + 1) * GROUP)
        slope_ref[block] = sum_lanes(out_grad[here] * scaled_ref[here].astype(f32))

    @pl.when(turn == pl.num_programs(0) - 1)
    def _():
        copy_on(turn).wait()


def run_out_grad(place, cots, scaled, out_rows):
    arrays, table = cots
    width, dim = out_rows.shape
    blocks = len(table)
    tokens = blocks * GROUP
    return pl.pallas_call(
        functools.partial(out_grad_kernel, table, len(arrays)),
        grid_spec=pltpu.PrefetchScalarGridSpec(
            num_scalar_prefetch=1,
            grid=(blocks // 2,),
            in_specs=[
                *anywhere(arrays),
                pl.BlockSpec((2 * GROUP, width), lambda turn, place: (turn, 0)),
                fixed(out_rows.shape),
            ],
            out_specs=[
                pl.BlockSpec((2 * GROUP, width), lambda turn, place: (turn, 0)),
                pl.BlockSpec((2, 8, GROUP), lambda turn, place: (turn, 0, 0)),
                *anywhere(range(1)),
            ],
            scratch_shapes=[
                pltpu.VMEM((2, 2 * GROUP, dim), bf16),
                pltpu.SemaphoreType.DMA((2,)),
                pltpu.SemaphoreType.DMA,
            ],
        ),
        out_shape=[
            jax.ShapeDtypeStruct((tokens, width), f32),
            jax.ShapeDtypeStruct((blocks, 8, GROUP), f32),
            jax.ShapeDtypeStruct((tokens, dim), bf16),
        ],
        compiler_params=pltpu.CompilerParams(vmem_limit_bytes=60 * MIB),
        cost_estimate=time_estimate(12, tokens * (4 * dim + 6 * width)),
        name="out_grad",
    )(place, *arrays, scaled, out_rows)


def backward_kernel(dims, place_ref, *refs):
    heads, size, states, count = dims
    width = heads * size
    conv_cols = width + 2 * states
    conv_in_ref, active_ref, slope_ref, gate_act_ref, gate_slope_ref = refs[:5]
    raw_ref, ssd_ref, start_ref, out_grad_ref, norm_ref = refs[5:10]
    conv_w_ref, step_ref, rows_ref = refs[10:13]
    out_ref, targets = refs[13], refs[14:18]
    sums = refs[18:24]
    gain_ref, skip_ref, conv_wg_ref, conv_bg_ref, bias_ref, rate_ref = sums
    state, pre_grads, order, back_order, barred, placed, semaphores = refs[24:]
    taps = conv_w_ref.shape[0]
    turn = pl.program_id(0)
    slot = lax.rem(turn, 2)

    @pl.when(turn >= 2)
    def _():
        stored(placed, targets, semaphores, slot)

    @pl.when(pl.program_id(0) == 0)
    def _():
        state[...] = jnp.zeros_like(state)
        pre_grads[0:HALO] = jnp.zeros_like(pre_grads[0:HALO])
        for total in sums:
            total[...] = jnp.zeros_like(total)
        row, column = order_indices(GROUP)
        order[...] = ones_where(row <= column)
        back_order[...] = ones_where(row >= column)
        row, column = order_indices(HALF)
        barred[...] = jnp.where(row <= column, 0.0, -1e30)

    gate_act, ssd, out_grad = gate_act_ref[...].astype(f32), ssd_ref[...], out_grad_ref[...]
    norms = norm_ref[0].T
    scale, slope = norms[:, 0:1], norms[:, 1:2]
    gated = ssd * gate_act
    gain_ref[...] += jnp.sum(out_grad * (gated * scale), axis=0, keepdims=True)
    gated_grad = out_grad * (rows_ref[1:2] * scale) - gated * slope
    grad_low = (gated_grad * gate_act).astype(bf16)
    gate_grad = (gated_grad * ssd * gate_slope_ref[...].astype(f32)).astype(bf16)
    out_ref[:, :width] = gate_grad
    placed[slot, :, :width] = gate_grad
    ssd_grad = grad_low.astype(f32)

    raw = raw_ref[0] + step_ref[0:8, 0:1]
    rate = step_ref[8:16, 0:1]
    step, sig, log_step, ratio = step_values(raw)
    decay = step * rate
    running = sum_along(decay, order[...])
    later = running - log_step
    total = running[:, GROUP - 1 :]
    columns = to_columns([later * LOG2E, jnp.exp(running), jnp.exp(total - later)])
    running = running * LOG2E
    early_wide = spread_heads(columns, 8, heads, size)
    tail_wide = spread_heads(columns, 16, heads, size)

    signal = active_ref[:, :width]
    entry = active_ref[:, width : width + states]
    readout = active_ref[:, width + states :]
    signal_wide = signal.astype(f32)
    start_low = start_ref[0]
    end_grad = state[...]
    end_low = end_grad.astype(bf16)
    first, second = slice(0, HALF), slice(HALF, GROUP)
    scores = dot_nt(entry[first], readout)
    later_scores = dot_nt(entry[second], readout[second])
    near_grad, far_grad, last_grad = 0.0, 0.0, 0.0
    within = []
    for h in range(heads):
        part, grad = signal[:, h * size : (h + 1) * size], grad_low[:, h * size : (h + 1) * size]
        begin, end = columns[first, h : h + 1], columns[second, h : h + 1]
        row_first, row_second = running[h : h + 1, first], running[h : h + 1, second]
        near = jnp.exp2(row_first - begin + barred[...])
        full = jnp.exp2(row_second - begin)
        last = jnp.exp2(row_second - end + barred[...])
        both = jnp.concatenate(
            [
                (near * scores[:, first]).astype(bf16),
                (full * scores[:, second]).astype(bf16),
            ],
            axis=1,
        )
        final = (last * later_scores).astype(bf16)
        within.append(jnp.concatenate([dot(both, grad), dot(final, grad[second])], axis=0))
        cross = dot_nt(part[first], grad)
        near_grad = near_grad + cross[:, first] * near
        far_grad = far_grad + cross[:, second] * full
        last_grad = last_grad + dot_nt(part[second], grad[second]) * last
    tail_grad = tail_wide * dot(entry, end_low)
    signal_grad = jnp.concatenate(within, axis=1) + tail_grad
    score_first = jnp.concatenate([near_grad, far_grad], axis=1).astype(bf16)
    score_second = last_grad.astype(bf16)
    tail = (signal_wide * tail_wide).astype(bf16)
    head_grad = (ssd_grad * early_wide).astype(bf16)
    entry_grad = jnp.concatenate(
        [dot(score_first, readout), dot(score_second, readout[second])], axis=0
    ) + dot_nt(tail, end_low)
    readout_grad = dot_tn(score_first, entry[first]) + dot_nt(head_grad, start_low)
    readout_last = readout_grad[second] + dot_tn(score_second, entry[second])
    total_wide = early_wide[GROUP - 1 :]
    state[...] = end_grad * total_wide + dot_tn(readout, head_grad)

    skip = rows_ref[0:1]
    ones = head_ones(width, size)
    column_part = signal_wide * signal_grad
    row_part = ssd_grad * (ssd - skip * signal_wide)
    end_part = jnp.sum(signal_wide * tail_grad, axis=0, keepdims=True) + total_wide * jnp.sum(
        start_low.astype(f32) * end_grad, axis=0, keepdims=True
    )

    def head_sums(value, parts):
        return sum(dot_nt(ones, part) for part in split_parts(value, parts))

    end_rows = head_sums(jnp.broadcast_to(end_part, (8, width)), 2)[:, 0:1]
    decay_grad = sum_along(head_sums(row_part - column_part, 2), back_order[...]) + end_rows
    raw_grad = head_sums(column_part, 1) * ratio + decay_grad * rate * sig
    skip_ref[...] += jnp.sum(ssd_grad * signal_wide, axis=0, keepdims=True)
    bias_ref[...] += raw_grad
    rate_ref[...] += decay_grad * decay
    raw_low = to_columns([raw_grad]).astype(bf16)
    out_ref[:, width + conv_cols :] = raw_low
    placed[slot, :, width + conv_cols :] = raw_low

    pre_grads[GROUP : GROUP + HALO] = pre_grads[0:HALO]
    pre_grads[0:GROUP, :width] = (signal_grad + skip * ssd_grad) * slope_ref[:, :width].astype(f32)
    sides = slope_ref[:, width:].astype(f32)
    pre_grads[0:GROUP, width : width + states] = entry_grad * sides[:, :states]
    pre_grads[0:HALF, width + states :] = readout_grad[first] * sides[first, states:]
    pre_grads[HALF:GROUP, width + states :] = readout_last * sides[second, states:]
    conv_w = conv_w_ref[...]
    conv_in = conv_in_ref[...].astype(f32)
    conv_grad = 0.0
    for k in range(taps):
        ahead = taps - 1 - k
        shifted = pre_grads[ahead : ahead + GROUP]
        conv_grad = conv_grad + conv_w[k : k + 1] * shifted
        conv_wg_ref[k : k + 1] += jnp.sum(shifted * conv_in, axis=0, keepdims=True)
        if ahead == 0:
            conv_bg_ref[...] += jnp.sum(shifted, axis=0, keepdims=True)
    conv_low = conv_grad.astype(bf16)
    out_ref[:, width : width + conv_cols] = conv_low
    placed[slot, :, width : width + conv_cols] = conv_low

    where = in_time(place_ref[0], pl.num_programs(0) - 1 - turn)
    store(placed.at[slot], targets, scatter_places(count), where, semaphores.at[slot])

    @pl.when(turn == pl.num_programs(0) - 1)
    def _():
        for other in range(2):
            stored(placed, targets, semaphores, other)


def run_backward(place, values, params, dims):
    heads, size, states, count = dims
    conv_cols, width = values[0].shape[1], heads * size
    tokens = values[0].shape[0]
    blocks = tokens // GROUP
    last = blocks - 1
    out_cols = width + conv_cols + LANES

    def moving(columns):
        return pl.BlockSpec((GROUP, columns), lambda turn, place: (last - turn, 0))

    def rows_of_block():
        return pl.BlockSpec((1, 8, GROUP), lambda turn, place: (last - turn, 0, 0))

    sums = [(1, width), (1, width), params[0].shape, (1, conv_cols), (8, GROUP), (8, GROUP)]
    return pl.pallas_call(
        functools.partial(backward_kernel, dims),
        grid_spec=pltpu.PrefetchScalarGridSpec(
            num_scalar_prefetch=1,
            grid=(blocks,),
            in_specs=[
                moving(conv_cols),
                moving(conv_cols),
                moving(conv_cols),
                moving(width),
                moving(width),
                rows_of_block(),
                moving(width),
                pl.BlockSpec((1, states, width), lambda turn, place: (last - turn, 0, 0)),
                moving(width),
                rows_of_block(),
                *[fixed(param.shape) for param in params],
            ],
            out_specs=[
                moving(out_cols),
                *anywhere(range(4)),
                *[fixed(shape) for shape in sums],
            ],
            scratch_shapes=[
                pltpu.VMEM((states, width), f32),
                pltpu.VMEM((GROUP + HALO, conv_cols), f32),
                pltpu.VMEM((GROUP, GROUP), bf16),
                pltpu.VMEM((GROUP, GROUP), bf16),
                pltpu.VMEM((HALF, HALF), f32),
                pltpu.VMEM((2, GROUP, out_cols), bf16),
                pltpu.SemaphoreType.DMA((2,)),
            ],
        ),
        out_shape=[
            jax.ShapeDtypeStruct((tokens, out_cols), bf16),
            *scatter_shapes(count, out_cols),
        ]
        + [jax.ShapeDtypeStruct(shape, f32) for shape in sums],
        compiler_params=pltpu.CompilerParams(vmem_limit_bytes=60 * MIB),
        cost_estimate=time_estimate(blocks * 3.5, tokens * 40 * width),
        name="backward_blocks",
    )(place, *values, *params)


def widen_kernel(place_ref, piece_ref, out_ref):
    out_ref[...] = piece_ref[0].astype(f32)


def assemble_out(place, pieces, per):
    count, size, dim = pieces.shape
    groups = count // per

    def source(turn, place):
        relative = (turn % groups * per + turn // groups) ^ place[0]
        return ((relative & 1) * (count // 2) + (relative >> 1), 0, 0)

    return pl.pallas_call(
        widen_kernel,
        grid_spec=pltpu.PrefetchScalarGridSpec(
            num_scalar_prefetch=1,
            grid=(count,),
            in_specs=[pl.BlockSpec((1, size, dim), source)],
            out_specs=pl.BlockSpec((size, dim), lambda turn, place: (turn, 0)),
        ),
        out_shape=jax.ShapeDtypeStruct((count * size, dim), f32),
        cost_estimate=time_estimate(5, count * size * dim * 6),
        name="assemble_out_weight_grad",
    )(place, pieces)


def assemble_kernel(dims, pieces_ref, out_ref):
    heads, size, states, count = dims
    width, shared = heads * size, 2 * states
    inner = count * width
    total = 0.0
    for device in range(count):
        columns = pieces_ref[device].astype(f32).T
        out_ref[device * width : (device + 1) * width] = columns[:width]
        out_ref[inner + device * width : inner + (device + 1) * width] = columns[width : 2 * width]
        total = total + columns[2 * width : 2 * width + shared]
        last = 2 * inner + shared + device * heads
        out_ref[last : last + heads] = columns[2 * width + shared : 2 * width + shared + heads]
    out_ref[2 * inner : 2 * inner + shared] = total


def assemble(pieces, dims):
    heads, size, states, count = dims
    _, rows, columns = pieces.shape
    tile = LANES if rows % LANES == 0 else rows
    out_rows = 2 * count * heads * size + 2 * states + count * heads
    return pl.pallas_call(
        functools.partial(assemble_kernel, dims),
        grid=(rows // tile,),
        in_specs=[pl.BlockSpec((count, tile, columns), lambda turn: (0, turn, 0))],
        out_specs=pl.BlockSpec((out_rows, tile), lambda turn: (0, turn)),
        out_shape=jax.ShapeDtypeStruct((out_rows, rows), f32),
        compiler_params=pltpu.CompilerParams(vmem_limit_bytes=60 * MIB),
        cost_estimate=time_estimate(8, out_rows * rows * 6),
        name="assemble_in_weight_grad",
    )(pieces)


def body(
    tokens,
    norm_gain,
    in_weight,
    conv_weight,
    conv_bias,
    dt_bias,
    decay_log,
    skip_scale,
    gate_gain,
    out_weight,
    cotangent,
):
    count, mine = lax.axis_size("seq"), lax.axis_index("seq")
    place = mine.astype(jnp.int32).reshape(1)
    inner, all_heads, conv_all = gate_gain.shape[0], dt_bias.shape[0], conv_bias.shape[0]
    size, states = inner // all_heads, (conv_all - inner) // 2
    heads, width = all_heads // count, inner // count
    dims = (heads, size, states, count)
    shared = 2 * states
    conv_cols = width + shared
    tok_rows = tokens.shape[1]
    per_plane = out_weight.shape[0] // width

    def own(vector, per, first=0):
        return lax.dynamic_slice_in_dim(vector, first + mine * per, per, vector.ndim - 1)

    def own_conv(array, first=0):
        return jnp.concatenate(
            [own(array, width, first), array[..., first + inner : first + conv_all]], axis=-1
        )

    tokens_row = tokens[0].astype(f32)
    inverse = lax.rsqrt(jnp.mean(tokens_row * tokens_row, axis=-1, keepdims=True) + epsilon)
    normed_own = (tokens_row * inverse * norm_gain).astype(bf16)
    step_own = own(in_weight, heads, inner + conv_all)
    w_own = jnp.concatenate(
        [
            own(in_weight, width),
            own_conv(in_weight, inner),
            jnp.pad(step_own, ((0, 0), (0, LANES - heads))),
        ],
        axis=1,
    )
    w_cols = lax.all_gather(w_own, "batch", axis=0, tiled=True)
    stages = gather_stages()
    held = gather_stage(gather_stage(gather_start(normed_own), 0), 1)
    held, cots = together(held, gather_start(cotangent[0]))
    cots = gather_stage(cots, 0)
    for stage in range(2, stages):
        held = gather_stage(held, stage)
    w_cols, held, cots, out_owned = together(w_cols, held, cots, out_weight)
    cots = gather_stage(cots, 1)
    out_rows = rows_from_owner(out_owned, width)

    conv_w, conv_b = own_conv(conv_weight), own_conv(conv_bias)[None]
    per_head = jnp.stack([own(dt_bias, heads), -jnp.exp(own(decay_log, heads))])
    per_head = jnp.pad(per_head, ((0, 0), (0, 8 - heads))).reshape(16, 1)
    step_rows = jnp.broadcast_to(per_head, (16, LANES))
    gain_own = own(gate_gain, width)[None]
    rows = jnp.concatenate(
        [jnp.repeat(own(skip_scale, heads), size)[None], gain_own, jnp.zeros((6, width), f32)],
        axis=0,
    )
    results, out_parts = run_forward(
        place, token_pieces(held), (w_cols, conv_w, conv_b, step_rows, rows), dims
    )
    conv_in, active, slope, gate_act, gate_slope, raw, ssd, starts, scaled, squares, normed = results
    out_parts, cots, out_rows = together(out_parts, cots, out_rows)
    for stage in range(2, stages):
        cots = gather_stage(cots, stage)

    def out_product(part):
        return dot(part, out_rows)

    out_send = out_product(out_parts[0]).astype(bf16)
    out_send, cots = together(out_send, cots)
    out_grad, slopes, cot = run_out_grad(place, token_pieces(cots), scaled, out_rows)
    sums = jnp.stack([squares[:, 0].reshape(-1), slopes[:, 0].reshape(-1)])
    out_ready, out_held = scatter_near(out_product, out_parts[1:], out_send)
    sums = sums + exchange(sums, "seq", 1)
    sums, first = together(sums, out_ready[0])
    sums = sums + exchange(sums, "seq", 2)
    sums, second = together(sums, out_ready[1])
    for bit in bits_of(count)[2:]:
        sums = sums + exchange(sums, "seq", bit)
    scale = lax.rsqrt(sums[0] / inner + epsilon)
    norms = jnp.stack([scale, scale * scale * scale * sums[1] / inner])
    norms = jnp.pad(norms, ((0, 6), (0, 0))).reshape(8, -1, GROUP).swapaxes(0, 1)
    normed_out = (scaled.astype(f32) * scale[:, None]).astype(bf16)
    out_term = jnp.einsum("te,td->ed", normed_out, cot, preferred_element_type=f32)
    out_term, norms, first, second = together(out_term.astype(bf16), norms, first, second)
    out_sum = lax.psum_scatter(out_term, "batch", scatter_dimension=0, tiled=True)
    out_ready, out_held = scatter_far((first, second), out_held, 0)

    values = (conv_in, active, slope, gate_act, gate_slope, raw, ssd, starts, out_grad, norms)
    results = run_backward(place, values, (conv_w, step_rows, rows), dims)
    proj_grad, back_parts = results[0], results[1:5]
    proj_grad, back_parts, out_ready, out_held, out_sum = together(
        proj_grad, back_parts, out_ready, out_held, out_sum
    )

    def back_product(part):
        return jnp.einsum("tf,df->td", part, w_cols, preferred_element_type=f32)

    def weight_product(part):
        return jnp.einsum("td,tf->df", normed, part, preferred_element_type=f32).astype(bf16)

    for stage in range(1, stages - 1):
        out_ready, out_held = scatter_far(out_ready, out_held, stage)
    back_send = back_product(back_parts[0]).astype(bf16)
    back_send, proj_grad = together(back_send, proj_grad)
    in_term = weight_product(proj_grad)
    in_term, keeps, out_held = together(in_term, back_parts[1:], out_held)
    in_sum = lax.psum_scatter(in_term, "batch", scatter_dimension=0, tiled=True)
    back_ready, back_held = scatter_near(back_product, keeps, back_send)
    back_ready, out_sum, in_sum = together(back_ready, out_sum, in_sum)
    pieces = lax.all_gather(in_sum, "seq", axis=0, tiled=False)
    back_ready, back_held = scatter_far(back_ready, back_held, 0)
    out_pieces = to_owner(out_sum)[None]

    back_held["kept"], in_term, results = together(back_held["kept"], in_term, results[5:])
    gain_term, skip_term, conv_w_term, conv_b_term, bias_term, rate_term = results
    norm_gain_term = jnp.sum(in_term.astype(f32) * w_cols.astype(f32), axis=1) / norm_gain

    def among_heads(vector, per, total):
        return lax.dynamic_update_slice_in_dim(jnp.zeros((total,), f32), vector, mine * per, 0)

    def among_conv(array):
        wide = jnp.zeros((array.shape[0], inner), f32)
        wide = lax.dynamic_update_slice_in_dim(wide, array[:, :width], mine * width, 1)
        return jnp.concatenate([wide, array[:, width:]], axis=1).reshape(-1)

    skip_heads = jnp.sum(skip_term.reshape(heads, size), axis=1)
    terms = [
        norm_gain_term,
        among_conv(conv_w_term),
        among_conv(conv_b_term),
        among_heads(jnp.sum(bias_term[:heads], axis=1), heads, all_heads),
        among_heads(jnp.sum(rate_term[:heads], axis=1), heads, all_heads),
        among_heads(skip_heads, heads, all_heads),
        among_heads(gain_term[0], width, inner),
    ]
    vector = jnp.concatenate(terms)
    padding = -vector.shape[0] % (8 * LANES)
    vector = jnp.pad(vector, (0, padding)).reshape(-1, LANES)

    axes = [(axis, bit) for axis in ("seq", "batch") for bit in bits_of(lax.axis_size(axis))]
    vector = vector + exchange(vector, *axes.pop(0))
    back_ready, vector, out_pieces = together(back_ready, vector, out_pieces)
    for stage in range(1, stages - 1):
        back_ready, back_held = scatter_far(back_ready, back_held, stage)
    out_pieces = double(out_pieces, 0)
    vector = vector + exchange(vector, *axes.pop(0))
    back_held["arrived"], vector, out_pieces = together(back_held["arrived"], vector, out_pieces)
    in_weight_grad = assemble(pieces, dims).T
    for stage in range(1, stages):
        out_pieces = double(out_pieces, stage)
    while axes:
        vector = vector + exchange(vector, *axes.pop(0))
    vector = vector.reshape(-1)
    normed_grad = scatter_end(back_held)
    cot_row = cotangent[0].astype(f32)
    gained = norm_gain * normed_grad
    slope = inverse * inverse * inverse * jnp.mean(gained * tokens_row, axis=-1, keepdims=True)
    input_grad = cot_row + inverse * gained - tokens_row * slope
    own_scale = lax.dynamic_slice_in_dim(scale, mine * tok_rows, tok_rows, 0)[:, None]
    block_out = (tokens_row + own_scale * scatter_end(out_held)).astype(bf16)
    out_weight_grad = assemble_out(place, out_pieces, per_plane)

    parts, offset = [], 0
    for term in terms:
        parts.append(vector[offset : offset + term.shape[0]])
        offset += term.shape[0]
    return (
        block_out[None],
        input_grad[None],
        parts[0],
        in_weight_grad,
        parts[1].reshape(conv_weight.shape),
        parts[2],
        parts[3],
        parts[4],
        parts[5],
        parts[6],
        out_weight_grad,
    )


def solution(mesh):
    placed = (
        P("batch", "seq", None),
        P(),
        P("batch", None),
        P(),
        P(),
        P(),
        P(),
        P(),
        P(),
        P("batch", None),
        P("batch", "seq", None),
    )
    return jax.shard_map(
        body,
        mesh=mesh,
        in_specs=placed,
        out_specs=(
            P("batch", "seq", None),
            P("batch", "seq", None),
            P(),
            P("batch", None),
            P(),
            P(),
            P(),
            P(),
            P(),
            P(),
            P("batch", None),
        ),
        check_vma=False,
    )
```

```python
import functools

import jax
import jax.numpy as jnp
from jax import lax
from jax.experimental import pallas as pl
from jax.experimental.pallas import tpu as pltpu
from jax.sharding import PartitionSpec as P

GROUP = 256
LANES = 128
HALF = GROUP // 2
HALO = 8
STEP_ROWS = 16
LOG2E = 1.4426950408889634
epsilon = 1e-05
f32 = jnp.float32
bf16 = jnp.bfloat16
MIB = 2**20


def exchange(value, axis, distance):
    count = lax.axis_size(axis)
    return lax.ppermute(value, axis, [(source, source ^ distance) for source in range(count)])


def bits_of(count):
    return [1 << k for k in range(count.bit_length() - 1)]


def placed_order(count):
    return [2 * k for k in range(count // 2)] + [2 * k + 1 for k in range(count // 2)]


def together(*values):
    return lax.optimization_barrier(values)


def far_orders():
    far = bits_of(lax.axis_size("seq"))[1:]
    return far, far[::-1]


def gather_start(value):
    half = value.shape[0] // 32 * 16
    return tuple({"base": part, "fresh": None, "near": []} for part in (value[:half], value[half:]))


def gather_stage(held, stage, late=False):
    grown = []
    for half, order in zip(held, far_orders()):
        base, fresh, near = half["base"], half["fresh"], list(half["near"])
        if stage >= 1:
            merged = base if stage == len(order) else jnp.concatenate([base, fresh], axis=0)
            if not late:
                near.append(exchange(merged if stage == 1 else fresh, "seq", 1))
            elif stage == len(order):
                near = [exchange(base, "seq", 1), exchange(fresh, "seq", 1)]
            base = merged
        if stage < len(order):
            fresh = exchange(base, "seq", order[stage])
        grown.append({"base": base, "fresh": fresh, "near": near})
    return tuple(grown)


def gather_stages():
    return len(bits_of(lax.axis_size("seq")))


def gathered(held):
    arrays, table = [], {}
    for number, (half, order) in enumerate(zip(held, far_orders())):
        indices = [0]
        for bit in order:
            indices += [index | bit for index in indices]
        middle = len(indices) // 2
        groups = [(half["base"], indices[:middle]), (half["fresh"], indices[middle:])]
        bounds = [0] + [2 << k for k in range(len(order))]
        if len(half["near"]) < len(order):
            bounds = [0, middle, len(indices)]
        for value, first, last in zip(half["near"], bounds, bounds[1:]):
            groups.append((value, [index | 1 for index in indices[first:last]]))
        for value, members in groups:
            rows = value.shape[0] // len(members)
            for turn, index in enumerate(members):
                table[number, index] = (len(arrays), turn * rows, rows)
            arrays.append(value)
    return arrays, table


def token_pieces(held):
    arrays, table = gathered(held)
    indices = range(lax.axis_size("seq"))
    return arrays, tuple(table[half, index] for index in indices for half in range(2))


def gather_all(value):
    held = gather_start(value)
    for stage in range(gather_stages()):
        held = gather_stage(held, stage)
    return held


def scatter_places(count):
    far = bits_of(count)[1:]
    table = {}
    row = {}
    for near in (1, 0):
        for sent in (True, False):
            for half, order in enumerate((far, far[::-1])):
                members = [0]
                for bit in order[:0:-1]:
                    members += [member | bit for member in members]
                for member in members:
                    index = member | near | (order[0] if sent else 0)
                    array = 0 if near else (1 + half if sent else 3)
                    table[index * 2 + half] = (array, row.get(array, 0))
                    row[array] = row.get(array, 0) + GROUP
    return tuple(table[k] for k in range(2 * count))


def scatter_shapes(count, columns):
    blocks = (count, count // 4, count // 4, count // 2)
    return [jax.ShapeDtypeStruct((part * GROUP, columns), bf16) for part in blocks]


def scatter_near(product, parts, sent):
    arriving = exchange(sent, "seq", 1)
    first, second, kept = parts
    rows = first.shape[0]

    def summed(part, row):
        return (product(part) + arriving[row : row + part.shape[0]].astype(f32)).astype(bf16)

    sends = (summed(first, 0), summed(second, rows))
    sends, kept = together(sends, kept)
    return sends, {"kept": summed(kept, 2 * rows), "arrived": ([], [])}


def scatter_rows(held, half, first, last):
    top = half * (held["kept"].shape[0] // 2)
    total = held["kept"][top + first : top + last].astype(f32)
    for value in held["arrived"][half]:
        total = total + value[first:last].astype(f32)
    return total


def scatter_far(sends, held, stage):
    orders = far_orders()
    arrived = tuple(
        [*held["arrived"][half], exchange(sends[half], "seq", orders[half][stage])]
        for half in range(2)
    )
    held = {"kept": held["kept"], "arrived": arrived}
    rows = sends[0].shape[0]
    if stage + 1 == len(orders[0]):
        return (), held
    ready = tuple(
        scatter_rows(held, half, rows // 2, rows).astype(bf16) for half in range(2)
    )
    return ready, held


def scatter_end(held):
    rows = held["arrived"][0][-1].shape[0]
    return jnp.concatenate([scatter_rows(held, half, 0, rows) for half in range(2)], axis=0)


def sum_seq(value):
    for bit in bits_of(lax.axis_size("seq")):
        value = value + exchange(value, "seq", bit)
    return value


def plane_pairs(ahead):
    planes, count = lax.axis_size("batch"), lax.axis_size("seq")
    per = count // planes
    pairs = []
    for owner in range(planes):
        for piece in range(planes):
            for k in range(per):
                holder = owner * count + piece * per + k
                user = (piece + ahead) % planes * count + owner * per + k
                pairs.append((holder, user))
    return pairs


def rows_from_owner(out_weight, width):
    per = lax.axis_size("seq") // lax.axis_size("batch")
    plane, mine = lax.axis_index("batch"), lax.axis_index("seq")
    rows = lax.dynamic_slice_in_dim(out_weight, mine % per * width, width, 0)
    return lax.psum(jnp.where(plane == mine // per, rows, jnp.zeros_like(rows)), "batch")


def to_owner(summed):
    return lax.ppermute(
        summed, ("batch", "seq"), [(user, holder) for holder, user in plane_pairs(0)]
    )


def double(held, turn):
    bits = bits_of(lax.axis_size("seq"))
    return jnp.concatenate([held, exchange(held, "seq", (bits[1:] + [1])[turn])], axis=0)


def step_values(raw):
    small = jnp.exp(-jnp.abs(raw))
    step = jnp.maximum(raw, 0.0) + jnp.log1p(small)
    sig = jnp.where(raw >= 0, 1.0, small) / (1.0 + small)
    tiny = raw < -20.0
    log_step = jnp.where(tiny, raw, jnp.log(step))
    ratio = jnp.where(tiny, 1.0, sig / step)
    return step, sig, log_step, ratio


def dot(a, b):
    return jnp.dot(a, b, preferred_element_type=f32)


def dot_nt(a, b):
    return lax.dot_general(a, b, (((1,), (1,)), ((), ())), preferred_element_type=f32)


def dot_tn(a, b):
    return lax.dot_general(a, b, (((0,), (0,)), ((), ())), preferred_element_type=f32)


def sigmoid(value):
    return 0.5 * jnp.tanh(0.5 * value) + 0.5


def silu_slope(value):
    sig = sigmoid(value)
    active = value * sig
    return active, sig + active * (1.0 - sig)


def split_parts(value, count):
    parts = []
    for _ in range(count):
        part = value.astype(bf16)
        parts.append(part)
        value = value - part.astype(f32)
    return parts


def dot_split(product, a, b):
    first, second = split_parts(b, 2)
    return product(a, first) + product(a, second)


def sum_along(rows, order):
    parts = jnp.concatenate([part.astype(f32) for part in split_parts(rows, 3)], axis=0)
    total = dot(parts.astype(bf16), order)
    return total[:8] + total[8:16] + total[16:24]


def to_columns(rows):
    stacked = jnp.concatenate(rows, axis=0)
    missing = LANES - stacked.shape[0]
    return jnp.concatenate([stacked, jnp.zeros((missing, GROUP), f32)], axis=0).T


def spread_heads(value, first, heads, size):
    rows = value.shape[0]
    return jnp.concatenate(
        [jnp.broadcast_to(value[:, first + h : first + h + 1], (rows, size)) for h in range(heads)],
        axis=1,
    )


def head_ones(width, size):
    row = lax.broadcasted_iota(jnp.int32, (8, width), 0)
    column = lax.broadcasted_iota(jnp.int32, (8, width), 1)
    return (column // size == row).astype(f32).astype(bf16)


def sum_lanes(value):
    return dot_nt(jnp.ones((8, value.shape[1]), bf16), value.astype(bf16))


def ones_where(condition):
    return jnp.where(condition, 1.0, 0.0).astype(bf16)


def order_indices(length):
    row = lax.broadcasted_iota(jnp.int32, (length, length), 0)
    column = lax.broadcasted_iota(jnp.int32, (length, length), 1)
    return row, column


def fetch(arrays, table, which, target, semaphore):
    for index, (array, row, rows) in enumerate(table):

        @pl.when(which == index)
        def _():
            pltpu.make_async_copy(arrays[array].at[pl.ds(row, rows)], target, semaphore).start()


def fetched(arrays, table, buffer, semaphores, order, blocks=1):
    step = pl.program_id(0)
    slot, other = lax.rem(step, 2), lax.rem(step + 1, 2)

    def start(step, slot):
        for k in range(blocks):
            target = buffer.at[slot, pl.ds(k * GROUP, GROUP)]
            fetch(arrays, table, order(step * blocks + k), target, semaphores.at[slot])

    @pl.when(step == 0)
    def _():
        start(0, 0)

    @pl.when(step + 1 < pl.num_programs(0))
    def _():
        start(step + 1, other)

    for k in range(blocks):
        source = arrays[0].at[pl.ds(0, GROUP)]
        target = buffer.at[slot, pl.ds(k * GROUP, GROUP)]
        pltpu.make_async_copy(source, target, semaphores.at[slot]).wait()
    return buffer[slot]


def store(source, targets, table, which, semaphore):
    for index, (array, row) in enumerate(table):

        @pl.when(which == index)
        def _():
            target = targets[array].at[pl.ds(row, GROUP)]
            pltpu.make_async_copy(source, target, semaphore).start()


def stored(buffer, targets, semaphores, slot):
    target = targets[0].at[pl.ds(0, GROUP)]
    pltpu.make_async_copy(buffer.at[slot], target, semaphores.at[slot]).wait()


def in_time(place, block):
    return ((block // 2) ^ place) * 2 + block % 2


def forward_kernel(dims, table, given, place_ref, *refs):
    heads, size, states, count = dims
    width = heads * size
    conv_cols = width + 2 * states
    arrays, refs = refs[:given], refs[given:]
    w_ref, conv_w_ref, conv_b_ref, step_ref, rows_ref = refs[:5]
    conv_in_ref, active_ref, slope_ref, gate_act_ref, gate_slope_ref = refs[5:10]
    raw_ref, ssd_ref, start_ref, scaled_ref, square_ref, normed_ref = refs[10:16]
    targets = refs[16:20]
    state, padded, order, barred, buffer, semaphores, placed, out_semaphores, copied = refs[20:]
    turn = pl.program_id(0)
    slot = lax.rem(turn, 2)

    def copy_on(turn):
        target = normed_ref.at[pl.ds(pl.multiple_of(turn * GROUP, GROUP), GROUP)]
        return pltpu.make_async_copy(buffer.at[lax.rem(turn, 2)], target, copied)

    @pl.when(turn == 0)
    def _():
        state[...] = jnp.zeros_like(state)
        padded[0:HALO] = jnp.zeros_like(padded[0:HALO])
        row, column = order_indices(GROUP)
        order[...] = ones_where(row <= column)
        row, column = order_indices(HALF)
        barred[...] = jnp.where(row >= column, 0.0, -1e30)

    @pl.when(turn >= 2)
    def _():
        stored(placed, targets, out_semaphores, slot)

    @pl.when(turn >= 1)
    def _():
        copy_on(turn - 1).wait()

    normed = fetched(
        arrays, table, buffer, semaphores, lambda step: in_time(place_ref[0], step)
    )
    copy_on(turn).start()
    projected = dot(normed, w_ref[...])
    conv_in = projected[:, width : width + conv_cols].astype(bf16)
    conv_in_ref[...] = conv_in
    padded[HALO : HALO + GROUP] = conv_in.astype(f32)
    conv_w = conv_w_ref[...]
    taps = conv_w.shape[0]
    pre = conv_b_ref[...]
    for k in range(taps):
        top = HALO - (taps - 1) + k
        pre = pre + conv_w[k : k + 1] * padded[top : top + GROUP]
    padded[0:HALO] = padded[GROUP : GROUP + HALO]
    active, slope = silu_slope(pre)
    active = active.astype(bf16)
    active_ref[...] = active
    slope_ref[...] = slope.astype(bf16)
    signal = active[:, :width]
    entry = active[:, width : width + states]
    readout = active[:, width + states :]
    signal_wide = signal.astype(f32)

    raw = projected[:, width + conv_cols :].T[:8]
    raw_ref[0] = raw
    step, _, log_step, _ = step_values(raw + step_ref[0:8, 0:1])
    running = sum_along(step * step_ref[8:16, 0:1], order[...])
    later = running - log_step
    total = running[:, GROUP - 1 :]
    columns = to_columns([running * LOG2E, jnp.exp(running), jnp.exp(total - later)])
    later = later * LOG2E
    early_wide = spread_heads(columns, 8, heads, size)
    tail_wide = spread_heads(columns, 16, heads, size)
    first, second = slice(0, HALF), slice(HALF, GROUP)
    scores = dot_nt(readout[first], entry[first])
    later_scores = dot_nt(readout[second], entry)
    within = []
    for h in range(heads):
        part = signal[:, h * size : (h + 1) * size]
        begin, end = columns[first, h : h + 1], columns[second, h : h + 1]
        row_first, row_second = later[h : h + 1, first], later[h : h + 1, second]
        near = jnp.exp2(begin - row_first + barred[...]) * scores
        full = jnp.exp2(end - row_first) * later_scores[:, first]
        last = jnp.exp2(end - row_second + barred[...]) * later_scores[:, second]
        both = jnp.concatenate([full.astype(bf16), last.astype(bf16)], axis=1)
        within.append(
            jnp.concatenate([dot(near.astype(bf16), part[first]), dot(both, part)], axis=0)
        )
    start = state[...]
    start_ref[0] = start
    carried = dot_split(dot, readout, start) * early_wide
    ssd = jnp.concatenate(within, axis=1) + carried + rows_ref[0:1] * signal_wide
    tail = signal_wide * tail_wide
    state[...] = start * early_wide[GROUP - 1 :] + dot_split(dot_tn, entry, tail)

    gate_act, gate_slope = silu_slope(projected[:, :width])
    gate_act_ref[...] = gate_act.astype(bf16)
    gate_slope_ref[...] = gate_slope.astype(bf16)
    ssd_ref[...] = ssd
    gated = ssd * gate_act
    scaled = (gated * rows_ref[1:2]).astype(bf16)
    scaled_ref[...] = scaled
    square_ref[0] = sum_lanes(gated * gated)
    placed[slot] = scaled
    where = in_time(place_ref[0], turn)
    store(placed.at[slot], targets, scatter_places(count), where, out_semaphores.at[slot])

    @pl.when(turn == pl.num_programs(0) - 1)
    def _():
        copy_on(turn).wait()
        for other in range(2):
            stored(placed, targets, out_semaphores, other)


def time_estimate(microseconds, accessed):
    return pl.CostEstimate(
        flops=int(microseconds * 1.1e9), bytes_accessed=int(accessed), transcendentals=0
    )


def fixed(shape):
    return pl.BlockSpec(shape, lambda turn, place: (0,) * len(shape), pipeline_mode=pl.Buffered(1))


def anywhere(values):
    return [pl.BlockSpec(memory_space=pltpu.HBM)] * len(values)


def run_forward(place, pieces, params, dims):
    heads, size, states, count = dims
    arrays, table = pieces
    dim = params[0].shape[0]
    width, conv_cols = heads * size, params[1].shape[1]
    blocks = len(table)
    tokens = blocks * GROUP

    def moving(columns):
        return pl.BlockSpec((GROUP, columns), lambda turn, place: (turn, 0))

    def rows_of_block(height, columns):
        return pl.BlockSpec((1, height, columns), lambda turn, place: (turn, 0, 0))

    results = pl.pallas_call(
        functools.partial(forward_kernel, dims, table, len(arrays)),
        grid_spec=pltpu.PrefetchScalarGridSpec(
            num_scalar_prefetch=1,
            grid=(blocks,),
            in_specs=[*anywhere(arrays), *[fixed(param.shape) for param in params]],
            out_specs=[
                moving(conv_cols),
                moving(conv_cols),
                moving(conv_cols),
                moving(width),
                moving(width),
                rows_of_block(8, GROUP),
                moving(width),
                rows_of_block(states, width),
                moving(width),
                rows_of_block(8, GROUP),
                *anywhere(range(5)),
            ],
            scratch_shapes=[
                pltpu.VMEM((states, width), f32),
                pltpu.VMEM((HALO + GROUP, conv_cols), f32),
                pltpu.VMEM((GROUP, GROUP), bf16),
                pltpu.VMEM((HALF, HALF), f32),
                pltpu.VMEM((2, GROUP, dim), bf16),
                pltpu.SemaphoreType.DMA((2,)),
                pltpu.VMEM((2, GROUP, width), bf16),
                pltpu.SemaphoreType.DMA((2,)),
                pltpu.SemaphoreType.DMA,
            ],
        ),
        out_shape=[
            jax.ShapeDtypeStruct((tokens, conv_cols), bf16),
            jax.ShapeDtypeStruct((tokens, conv_cols), bf16),
            jax.ShapeDtypeStruct((tokens, conv_cols), bf16),
            jax.ShapeDtypeStruct((tokens, width), bf16),
            jax.ShapeDtypeStruct((tokens, width), bf16),
            jax.ShapeDtypeStruct((blocks, 8, GROUP), f32),
            jax.ShapeDtypeStruct((tokens, width), f32),
            jax.ShapeDtypeStruct((blocks, states, width), f32),
            jax.ShapeDtypeStruct((tokens, width), bf16),
            jax.ShapeDtypeStruct((blocks, 8, GROUP), f32),
            jax.ShapeDtypeStruct((tokens, dim), bf16),
            *scatter_shapes(count, width),
        ],
        compiler_params=pltpu.CompilerParams(vmem_limit_bytes=60 * MIB),
        cost_estimate=time_estimate(blocks * 3.0, tokens * (4 * dim + 24 * width)),
        name="forward_blocks",
    )(place, *arrays, *params)
    return results[:11], results[11:]


def out_grad_kernel(table, given, place_ref, *refs):
    arrays, refs = refs[:given], refs[given:]
    scaled_ref, out_rows_ref, out_grad_ref, slope_ref, cot_ref = refs[:5]
    buffer, semaphores, copied = refs[5:]
    place, turn = place_ref[0], pl.program_id(0)
    rows = buffer.shape[1]

    def copy_on(turn):
        target = cot_ref.at[pl.ds(pl.multiple_of(turn * rows, rows), rows)]
        return pltpu.make_async_copy(buffer.at[lax.rem(turn, 2)], target, copied)

    @pl.when(turn >= 1)
    def _():
        copy_on(turn - 1).wait()

    cot = fetched(arrays, table, buffer, semaphores, lambda block: in_time(place, block), 2)
    copy_on(turn).start()
    out_grad = dot_nt(cot, out_rows_ref[...])
    out_grad_ref[...] = out_grad
    for block in range(2):
        here = slice(block * GROUP, (block + 1) * GROUP)
        slope_ref[block] = sum_lanes(out_grad[here] * scaled_ref[here].astype(f32))

    @pl.when(turn == pl.num_programs(0) - 1)
    def _():
        copy_on(turn).wait()


def run_out_grad(place, cots, scaled, out_rows):
    arrays, table = cots
    width, dim = out_rows.shape
    blocks = len(table)
    tokens = blocks * GROUP
    return pl.pallas_call(
        functools.partial(out_grad_kernel, table, len(arrays)),
        grid_spec=pltpu.PrefetchScalarGridSpec(
            num_scalar_prefetch=1,
            grid=(blocks // 2,),
            in_specs=[
                *anywhere(arrays),
                pl.BlockSpec((2 * GROUP, width), lambda turn, place: (turn, 0)),
                fixed(out_rows.shape),
            ],
            out_specs=[
                pl.BlockSpec((2 * GROUP, width), lambda turn, place: (turn, 0)),
                pl.BlockSpec((2, 8, GROUP), lambda turn, place: (turn, 0, 0)),
                *anywhere(range(1)),
            ],
            scratch_shapes=[
                pltpu.VMEM((2, 2 * GROUP, dim), bf16),
                pltpu.SemaphoreType.DMA((2,)),
                pltpu.SemaphoreType.DMA,
            ],
        ),
        out_shape=[
            jax.ShapeDtypeStruct((tokens, width), f32),
            jax.ShapeDtypeStruct((blocks, 8, GROUP), f32),
            jax.ShapeDtypeStruct((tokens, dim), bf16),
        ],
        compiler_params=pltpu.CompilerParams(vmem_limit_bytes=60 * MIB),
        cost_estimate=time_estimate(12, tokens * (4 * dim + 6 * width)),
        name="out_grad",
    )(place, *arrays, scaled, out_rows)


def backward_kernel(dims, place_ref, *refs):
    heads, size, states, count = dims
    width = heads * size
    conv_cols = width + 2 * states
    conv_in_ref, active_ref, slope_ref, gate_act_ref, gate_slope_ref = refs[:5]
    raw_ref, ssd_ref, start_ref, out_grad_ref, norm_ref = refs[5:10]
    conv_w_ref, step_ref, rows_ref = refs[10:13]
    out_ref, targets = refs[13], refs[14:18]
    sums = refs[18:24]
    gain_ref, skip_ref, conv_wg_ref, conv_bg_ref, bias_ref, rate_ref = sums
    state, pre_grads, order, back_order, barred, placed, semaphores = refs[24:]
    taps = conv_w_ref.shape[0]
    turn = pl.program_id(0)
    slot = lax.rem(turn, 2)

    @pl.when(turn >= 2)
    def _():
        stored(placed, targets, semaphores, slot)

    @pl.when(pl.program_id(0) == 0)
    def _():
        state[...] = jnp.zeros_like(state)
        pre_grads[0:HALO] = jnp.zeros_like(pre_grads[0:HALO])
        for total in sums:
            total[...] = jnp.zeros_like(total)
        row, column = order_indices(GROUP)
        order[...] = ones_where(row <= column)
        back_order[...] = ones_where(row >= column)
        row, column = order_indices(HALF)
        barred[...] = jnp.where(row <= column, 0.0, -1e30)

    gate_act, ssd, out_grad = gate_act_ref[...].astype(f32), ssd_ref[...], out_grad_ref[...]
    norms = norm_ref[0].T
    scale, slope = norms[:, 0:1], norms[:, 1:2]
    gated = ssd * gate_act
    gain_ref[...] += jnp.sum(out_grad * (gated * scale), axis=0, keepdims=True)
    gated_grad = out_grad * (rows_ref[1:2] * scale) - gated * slope
    grad_low = (gated_grad * gate_act).astype(bf16)
    gate_grad = (gated_grad * ssd * gate_slope_ref[...].astype(f32)).astype(bf16)
    out_ref[:, :width] = gate_grad
    placed[slot, :, :width] = gate_grad
    ssd_grad = grad_low.astype(f32)

    raw = raw_ref[0] + step_ref[0:8, 0:1]
    rate = step_ref[8:16, 0:1]
    step, sig, log_step, ratio = step_values(raw)
    decay = step * rate
    running = sum_along(decay, order[...])
    later = running - log_step
    total = running[:, GROUP - 1 :]
    columns = to_columns([later * LOG2E, jnp.exp(running), jnp.exp(total - later)])
    running = running * LOG2E
    early_wide = spread_heads(columns, 8, heads, size)
    tail_wide = spread_heads(columns, 16, heads, size)

    signal = active_ref[:, :width]
    entry = active_ref[:, width : width + states]
    readout = active_ref[:, width + states :]
    signal_wide = signal.astype(f32)
    start = start_ref[0]
    start_low = start.astype(bf16)
    end_grad = state[...]
    end_low = end_grad.astype(bf16)
    first, second = slice(0, HALF), slice(HALF, GROUP)
    scores = dot_nt(entry[first], readout)
    later_scores = dot_nt(entry[second], readout[second])
    near_grad, far_grad, last_grad = 0.0, 0.0, 0.0
    within = []
    for h in range(heads):
        part, grad = signal[:, h * size : (h + 1) * size], grad_low[:, h * size : (h + 1) * size]
        begin, end = columns[first, h : h + 1], columns[second, h : h + 1]
        row_first, row_second = running[h : h + 1, first], running[h : h + 1, second]
        near = jnp.exp2(row_first - begin + barred[...])
        full = jnp.exp2(row_second - begin)
        last = jnp.exp2(row_second - end + barred[...])
        both = jnp.concatenate(
            [
                (near * scores[:, first]).astype(bf16),
                (full * scores[:, second]).astype(bf16),
            ],
            axis=1,
        )
        final = (last * later_scores).astype(bf16)
        within.append(jnp.concatenate([dot(both, grad), dot(final, grad[second])], axis=0))
        cross = dot_nt(part[first], grad)
        near_grad = near_grad + cross[:, first] * near
        far_grad = far_grad + cross[:, second] * full
        last_grad = last_grad + dot_nt(part[second], grad[second]) * last
    tail_grad = tail_wide * dot_split(dot, entry, end_grad)
    signal_grad = jnp.concatenate(within, axis=1) + tail_grad
    score_first = jnp.concatenate([near_grad, far_grad], axis=1).astype(bf16)
    score_second = last_grad.astype(bf16)
    tail = (signal_wide * tail_wide).astype(bf16)
    head_grad = ssd_grad * early_wide
    entry_grad = jnp.concatenate(
        [dot(score_first, readout), dot(score_second, readout[second])], axis=0
    ) + dot_nt(tail, end_low)
    readout_grad = dot_tn(score_first, entry[first]) + dot_nt(head_grad.astype(bf16), start_low)
    readout_last = readout_grad[second] + dot_tn(score_second, entry[second])
    total_wide = early_wide[GROUP - 1 :]
    state[...] = end_grad * total_wide + dot_split(dot_tn, readout, head_grad)

    skip = rows_ref[0:1]
    ones = head_ones(width, size)
    column_part = signal_wide * signal_grad
    row_part = ssd_grad * (ssd - skip * signal_wide)
    end_part = jnp.sum(signal_wide * tail_grad, axis=0, keepdims=True) + total_wide * jnp.sum(
        start * end_grad, axis=0, keepdims=True
    )

    def head_sums(value, parts):
        return sum(dot_nt(ones, part) for part in split_parts(value, parts))

    end_rows = head_sums(jnp.broadcast_to(end_part, (8, width)), 2)[:, 0:1]
    decay_grad = sum_along(head_sums(row_part - column_part, 2), back_order[...]) + end_rows
    raw_grad = head_sums(column_part, 1) * ratio + decay_grad * rate * sig
    skip_ref[...] += jnp.sum(ssd_grad * signal_wide, axis=0, keepdims=True)
    bias_ref[...] += raw_grad
    rate_ref[...] += decay_grad * decay
    raw_low = to_columns([raw_grad]).astype(bf16)
    out_ref[:, width + conv_cols :] = raw_low
    placed[slot, :, width + conv_cols :] = raw_low

    pre_grads[GROUP : GROUP + HALO] = pre_grads[0:HALO]
    pre_grads[0:GROUP, :width] = (signal_grad + skip * ssd_grad) * slope_ref[:, :width].astype(f32)
    sides = slope_ref[:, width:].astype(f32)
    pre_grads[0:GROUP, width : width + states] = entry_grad * sides[:, :states]
    pre_grads[0:HALF, width + states :] = readout_grad[first] * sides[first, states:]
    pre_grads[HALF:GROUP, width + states :] = readout_last * sides[second, states:]
    conv_w = conv_w_ref[...]
    conv_in = conv_in_ref[...].astype(f32)
    conv_grad = 0.0
    for k in range(taps):
        ahead = taps - 1 - k
        shifted = pre_grads[ahead : ahead + GROUP]
        conv_grad = conv_grad + conv_w[k : k + 1] * shifted
        conv_wg_ref[k : k + 1] += jnp.sum(shifted * conv_in, axis=0, keepdims=True)
        if ahead == 0:
            conv_bg_ref[...] += jnp.sum(shifted, axis=0, keepdims=True)
    conv_low = conv_grad.astype(bf16)
    out_ref[:, width : width + conv_cols] = conv_low
    placed[slot, :, width : width + conv_cols] = conv_low

    where = in_time(place_ref[0], pl.num_programs(0) - 1 - turn)
    store(placed.at[slot], targets, scatter_places(count), where, semaphores.at[slot])

    @pl.when(turn == pl.num_programs(0) - 1)
    def _():
        for other in range(2):
            stored(placed, targets, semaphores, other)


def run_backward(place, values, params, dims):
    heads, size, states, count = dims
    conv_cols, width = values[0].shape[1], heads * size
    tokens = values[0].shape[0]
    blocks = tokens // GROUP
    last = blocks - 1
    out_cols = width + conv_cols + LANES

    def moving(columns):
        return pl.BlockSpec((GROUP, columns), lambda turn, place: (last - turn, 0))

    def rows_of_block():
        return pl.BlockSpec((1, 8, GROUP), lambda turn, place: (last - turn, 0, 0))

    sums = [(1, width), (1, width), params[0].shape, (1, conv_cols), (8, GROUP), (8, GROUP)]
    return pl.pallas_call(
        functools.partial(backward_kernel, dims),
        grid_spec=pltpu.PrefetchScalarGridSpec(
            num_scalar_prefetch=1,
            grid=(blocks,),
            in_specs=[
                moving(conv_cols),
                moving(conv_cols),
                moving(conv_cols),
                moving(width),
                moving(width),
                rows_of_block(),
                moving(width),
                pl.BlockSpec((1, states, width), lambda turn, place: (last - turn, 0, 0)),
                moving(width),
                rows_of_block(),
                *[fixed(param.shape) for param in params],
            ],
            out_specs=[
                moving(out_cols),
                *anywhere(range(4)),
                *[fixed(shape) for shape in sums],
            ],
            scratch_shapes=[
                pltpu.VMEM((states, width), f32),
                pltpu.VMEM((GROUP + HALO, conv_cols), f32),
                pltpu.VMEM((GROUP, GROUP), bf16),
                pltpu.VMEM((GROUP, GROUP), bf16),
                pltpu.VMEM((HALF, HALF), f32),
                pltpu.VMEM((2, GROUP, out_cols), bf16),
                pltpu.SemaphoreType.DMA((2,)),
            ],
        ),
        out_shape=[
            jax.ShapeDtypeStruct((tokens, out_cols), bf16),
            *scatter_shapes(count, out_cols),
        ]
        + [jax.ShapeDtypeStruct(shape, f32) for shape in sums],
        compiler_params=pltpu.CompilerParams(vmem_limit_bytes=60 * MIB),
        cost_estimate=time_estimate(blocks * 3.5, tokens * 40 * width),
        name="backward_blocks",
    )(place, *values, *params)


def widen_kernel(place_ref, piece_ref, out_ref):
    out_ref[...] = piece_ref[0].astype(f32)


def assemble_out(place, pieces, per):
    count, size, dim = pieces.shape
    groups = count // per

    def source(turn, place):
        relative = (turn % groups * per + turn // groups) ^ place[0]
        return ((relative & 1) * (count // 2) + (relative >> 1), 0, 0)

    return pl.pallas_call(
        widen_kernel,
        grid_spec=pltpu.PrefetchScalarGridSpec(
            num_scalar_prefetch=1,
            grid=(count,),
            in_specs=[pl.BlockSpec((1, size, dim), source)],
            out_specs=pl.BlockSpec((size, dim), lambda turn, place: (turn, 0)),
        ),
        out_shape=jax.ShapeDtypeStruct((count * size, dim), f32),
        cost_estimate=time_estimate(5, count * size * dim * 6),
        name="assemble_out_weight_grad",
    )(place, pieces)


def assemble_kernel(dims, pieces_ref, out_ref):
    heads, size, states, count = dims
    width, shared = heads * size, 2 * states
    inner = count * width
    total = 0.0
    for device in range(count):
        columns = pieces_ref[device].astype(f32).T
        out_ref[device * width : (device + 1) * width] = columns[:width]
        out_ref[inner + device * width : inner + (device + 1) * width] = columns[width : 2 * width]
        total = total + columns[2 * width : 2 * width + shared]
        last = 2 * inner + shared + device * heads
        out_ref[last : last + heads] = columns[2 * width + shared : 2 * width + shared + heads]
    out_ref[2 * inner : 2 * inner + shared] = total


def assemble(pieces, dims):
    heads, size, states, count = dims
    _, rows, columns = pieces.shape
    tile = LANES if rows % LANES == 0 else rows
    out_rows = 2 * count * heads * size + 2 * states + count * heads
    return pl.pallas_call(
        functools.partial(assemble_kernel, dims),
        grid=(rows // tile,),
        in_specs=[pl.BlockSpec((count, tile, columns), lambda turn: (0, turn, 0))],
        out_specs=pl.BlockSpec((out_rows, tile), lambda turn: (0, turn)),
        out_shape=jax.ShapeDtypeStruct((out_rows, rows), f32),
        compiler_params=pltpu.CompilerParams(vmem_limit_bytes=60 * MIB),
        cost_estimate=time_estimate(8, out_rows * rows * 6),
        name="assemble_in_weight_grad",
    )(pieces)


def body(
    tokens,
    norm_gain,
    in_weight,
    conv_weight,
    conv_bias,
    dt_bias,
    decay_log,
    skip_scale,
    gate_gain,
    out_weight,
    cotangent,
):
    count, mine = lax.axis_size("seq"), lax.axis_index("seq")
    place = mine.astype(jnp.int32).reshape(1)
    inner, all_heads, conv_all = gate_gain.shape[0], dt_bias.shape[0], conv_bias.shape[0]
    size, states = inner // all_heads, (conv_all - inner) // 2
    heads, width = all_heads // count, inner // count
    dims = (heads, size, states, count)
    shared = 2 * states
    conv_cols = width + shared
    tok_rows = tokens.shape[1]
    per_plane = out_weight.shape[0] // width

    def own(vector, per, first=0):
        return lax.dynamic_slice_in_dim(vector, first + mine * per, per, vector.ndim - 1)

    def own_conv(array, first=0):
        return jnp.concatenate(
            [own(array, width, first), array[..., first + inner : first + conv_all]], axis=-1
        )

    tokens_row = tokens[0].astype(f32)
    inverse = lax.rsqrt(jnp.mean(tokens_row * tokens_row, axis=-1, keepdims=True) + epsilon)
    normed_own = (tokens_row * inverse * norm_gain).astype(bf16)
    step_own = own(in_weight, heads, inner + conv_all)
    w_own = jnp.concatenate(
        [
            own(in_weight, width),
            own_conv(in_weight, inner),
            jnp.pad(step_own, ((0, 0), (0, LANES - heads))),
        ],
        axis=1,
    )
    w_cols = lax.all_gather(w_own, "batch", axis=0, tiled=True)
    stages = gather_stages()
    held = gather_stage(gather_start(normed_own), 0)
    held, cots = together(held, gather_start(cotangent[0]))
    cots = gather_stage(cots, 0)
    held, cots = together(held, cots)
    held = gather_stage(held, 1)
    held, cots = together(held, cots)
    cots = gather_stage(cots, 1)
    for stage in range(2, stages):
        held = gather_stage(held, stage)
    w_cols, held, out_owned = together(w_cols, held, out_weight)
    out_rows = rows_from_owner(out_owned, width)

    conv_w, conv_b = own_conv(conv_weight), own_conv(conv_bias)[None]
    per_head = jnp.stack([own(dt_bias, heads), -jnp.exp(own(decay_log, heads))])
    per_head = jnp.pad(per_head, ((0, 0), (0, 8 - heads))).reshape(16, 1)
    step_rows = jnp.broadcast_to(per_head, (16, LANES))
    gain_own = own(gate_gain, width)[None]
    rows = jnp.concatenate(
        [jnp.repeat(own(skip_scale, heads), size)[None], gain_own, jnp.zeros((6, width), f32)],
        axis=0,
    )
    results, out_parts = run_forward(
        place, token_pieces(held), (w_cols, conv_w, conv_b, step_rows, rows), dims
    )
    conv_in, active, slope, gate_act, gate_slope, raw, ssd, starts, scaled, squares, normed = results
    out_parts, cots, out_rows = together(out_parts, cots, out_rows)
    for stage in range(2, stages):
        cots = gather_stage(cots, stage)

    def out_product(part):
        return dot(part, out_rows)

    out_send = out_product(out_parts[0]).astype(bf16)
    out_send, cots = together(out_send, cots)
    out_grad, slopes, cot = run_out_grad(place, token_pieces(cots), scaled, out_rows)
    sums = jnp.stack([squares[:, 0].reshape(-1), slopes[:, 0].reshape(-1)])
    out_ready, out_held = scatter_near(out_product, out_parts[1:], out_send)
    sums = sums + exchange(sums, "seq", 1)
    sums, first = together(sums, out_ready[0])
    sums = sums + exchange(sums, "seq", 2)
    sums, second = together(sums, out_ready[1])
    for bit in bits_of(count)[2:]:
        sums = sums + exchange(sums, "seq", bit)
    scale = lax.rsqrt(sums[0] / inner + epsilon)
    norms = jnp.stack([scale, scale * scale * scale * sums[1] / inner])
    norms = jnp.pad(norms, ((0, 6), (0, 0))).reshape(8, -1, GROUP).swapaxes(0, 1)
    normed_out = (scaled.astype(f32) * scale[:, None]).astype(bf16)
    out_term = jnp.einsum("te,td->ed", normed_out, cot, preferred_element_type=f32)
    out_term, norms, first, second = together(out_term.astype(bf16), norms, first, second)
    out_sum = lax.psum_scatter(out_term, "batch", scatter_dimension=0, tiled=True)
    out_ready, out_held = scatter_far((first, second), out_held, 0)

    values = (conv_in, active, slope, gate_act, gate_slope, raw, ssd, starts, out_grad, norms)
    results = run_backward(place, values, (conv_w, step_rows, rows), dims)
    proj_grad, back_parts = results[0], results[1:5]
    proj_grad, back_parts, out_ready, out_held, out_sum = together(
        proj_grad, back_parts, out_ready, out_held, out_sum
    )

    def back_product(part):
        return jnp.einsum("tf,df->td", part, w_cols, preferred_element_type=f32)

    def weight_product(part):
        return jnp.einsum("td,tf->df", normed, part, preferred_element_type=f32).astype(bf16)

    back_send = back_product(back_parts[0]).astype(bf16)
    back_send, proj_grad, out_ready = together(back_send, proj_grad, out_ready)
    for stage in range(1, stages - 1):
        out_ready, out_held = scatter_far(out_ready, out_held, stage)
    in_term = weight_product(proj_grad)
    in_term, keeps, out_held = together(in_term, back_parts[1:], out_held)
    in_sum = lax.psum_scatter(in_term, "batch", scatter_dimension=0, tiled=True)
    back_ready, back_held = scatter_near(back_product, keeps, back_send)
    back_ready, out_sum = together(back_ready, out_sum)
    back_ready, back_held = scatter_far(back_ready, back_held, 0)
    out_pieces = to_owner(out_sum)[None]

    back_held["kept"], in_term, results = together(back_held["kept"], in_term, results[5:])
    gain_term, skip_term, conv_w_term, conv_b_term, bias_term, rate_term = results
    norm_gain_term = jnp.sum(in_term.astype(f32) * w_cols.astype(f32), axis=1) / norm_gain

    def among_heads(vector, per, total):
        return lax.dynamic_update_slice_in_dim(jnp.zeros((total,), f32), vector, mine * per, 0)

    def among_conv(array):
        wide = jnp.zeros((array.shape[0], inner), f32)
        wide = lax.dynamic_update_slice_in_dim(wide, array[:, :width], mine * width, 1)
        return jnp.concatenate([wide, array[:, width:]], axis=1).reshape(-1)

    skip_heads = jnp.sum(skip_term.reshape(heads, size), axis=1)
    terms = [
        norm_gain_term,
        among_conv(conv_w_term),
        among_conv(conv_b_term),
        among_heads(jnp.sum(bias_term[:heads], axis=1), heads, all_heads),
        among_heads(jnp.sum(rate_term[:heads], axis=1), heads, all_heads),
        among_heads(skip_heads, heads, all_heads),
        among_heads(gain_term[0], width, inner),
    ]
    vector = jnp.concatenate(terms)
    padding = -vector.shape[0] % (8 * LANES)
    vector = jnp.pad(vector, (0, padding)).reshape(-1, LANES)

    axes = [(axis, bit) for axis in ("seq", "batch") for bit in bits_of(lax.axis_size(axis))]
    vector = vector + exchange(vector, *axes.pop(0))
    back_ready, vector, out_pieces = together(back_ready, vector, out_pieces)
    for stage in range(1, stages - 1):
        back_ready, back_held = scatter_far(back_ready, back_held, stage)
    out_pieces = double(out_pieces, 0)
    vector = vector + exchange(vector, *axes.pop(0))
    back_held["arrived"], vector, out_pieces, in_sum = together(
        back_held["arrived"], vector, out_pieces, in_sum
    )
    pieces = lax.all_gather(in_sum, "seq", axis=0, tiled=False)
    in_weight_grad = assemble(pieces, dims).T
    for stage in range(1, stages):
        out_pieces = double(out_pieces, stage)
    while axes:
        vector = vector + exchange(vector, *axes.pop(0))
    vector = vector.reshape(-1)
    normed_grad = scatter_end(back_held)
    cot_row = cotangent[0].astype(f32)
    gained = norm_gain * normed_grad
    slope = inverse * inverse * inverse * jnp.mean(gained * tokens_row, axis=-1, keepdims=True)
    input_grad = cot_row + inverse * gained - tokens_row * slope
    own_scale = lax.dynamic_slice_in_dim(scale, mine * tok_rows, tok_rows, 0)[:, None]
    block_out = (tokens_row + own_scale * scatter_end(out_held)).astype(bf16)
    out_weight_grad = assemble_out(place, out_pieces, per_plane)

    parts, offset = [], 0
    for term in terms:
        parts.append(vector[offset : offset + term.shape[0]])
        offset += term.shape[0]
    return (
        block_out[None],
        input_grad[None],
        parts[0],
        in_weight_grad,
        parts[1].reshape(conv_weight.shape),
        parts[2],
        parts[3],
        parts[4],
        parts[5],
        parts[6],
        out_weight_grad,
    )


def solution(mesh):
    placed = (
        P("batch", "seq", None),
        P(),
        P("batch", None),
        P(),
        P(),
        P(),
        P(),
        P(),
        P(),
        P("batch", None),
        P("batch", "seq", None),
    )
    return jax.shard_map(
        body,
        mesh=mesh,
        in_specs=placed,
        out_specs=(
            P("batch", "seq", None),
            P("batch", "seq", None),
            P(),
            P("batch", None),
            P(),
            P(),
            P(),
            P(),
            P(),
            P(),
            P("batch", None),
        ),
        check_vma=False,
    )
```

```python
import functools

import jax
import jax.numpy as jnp
from jax import lax
from jax.experimental import pallas as pl
from jax.experimental.pallas import tpu as pltpu
from jax.sharding import PartitionSpec as P

GROUP = 256
LANES = 128
HALF = GROUP // 2
HALO = 8
STEP_ROWS = 16
LOG2E = 1.4426950408889634
epsilon = 1e-05
f32 = jnp.float32
bf16 = jnp.bfloat16
MIB = 2**20


def exchange(value, axis, distance):
    count = lax.axis_size(axis)
    return lax.ppermute(value, axis, [(source, source ^ distance) for source in range(count)])


def bits_of(count):
    return [1 << k for k in range(count.bit_length() - 1)]


def placed_order(count):
    return [2 * k for k in range(count // 2)] + [2 * k + 1 for k in range(count // 2)]


def together(*values):
    return lax.optimization_barrier(values)


def far_orders():
    far = bits_of(lax.axis_size("seq"))[1:]
    return far, far[::-1]


def gather_start(value):
    half = value.shape[0] // 32 * 16
    return tuple({"base": part, "fresh": None, "near": []} for part in (value[:half], value[half:]))


def gather_stage(held, stage, late=False):
    grown = []
    for half, order in zip(held, far_orders()):
        base, fresh, near = half["base"], half["fresh"], list(half["near"])
        if stage >= 1:
            merged = base if stage == len(order) else jnp.concatenate([base, fresh], axis=0)
            if not late:
                near.append(exchange(merged if stage == 1 else fresh, "seq", 1))
            elif stage == len(order):
                near = [exchange(base, "seq", 1), exchange(fresh, "seq", 1)]
            base = merged
        if stage < len(order):
            fresh = exchange(base, "seq", order[stage])
        grown.append({"base": base, "fresh": fresh, "near": near})
    return tuple(grown)


def gather_stages():
    return len(bits_of(lax.axis_size("seq")))


def gathered(held):
    arrays, table = [], {}
    for number, (half, order) in enumerate(zip(held, far_orders())):
        indices = [0]
        for bit in order:
            indices += [index | bit for index in indices]
        middle = len(indices) // 2
        groups = [(half["base"], indices[:middle]), (half["fresh"], indices[middle:])]
        bounds = [0] + [2 << k for k in range(len(order))]
        if len(half["near"]) < len(order):
            bounds = [0, middle, len(indices)]
        for value, first, last in zip(half["near"], bounds, bounds[1:]):
            groups.append((value, [index | 1 for index in indices[first:last]]))
        for value, members in groups:
            rows = value.shape[0] // len(members)
            for turn, index in enumerate(members):
                table[number, index] = (len(arrays), turn * rows, rows)
            arrays.append(value)
    return arrays, table


def token_pieces(held):
    arrays, table = gathered(held)
    indices = range(lax.axis_size("seq"))
    return arrays, tuple(table[half, index] for index in indices for half in range(2))


def gather_all(value):
    held = gather_start(value)
    for stage in range(gather_stages()):
        held = gather_stage(held, stage)
    return held


def scatter_places(count):
    far = bits_of(count)[1:]
    table = {}
    row = {}
    for near in (1, 0):
        for sent in (True, False):
            for half, order in enumerate((far, far[::-1])):
                members = [0]
                for bit in order[:0:-1]:
                    members += [member | bit for member in members]
                for member in members:
                    index = member | near | (order[0] if sent else 0)
                    array = 0 if near else (1 + half if sent else 3)
                    table[index * 2 + half] = (array, row.get(array, 0))
                    row[array] = row.get(array, 0) + GROUP
    return tuple(table[k] for k in range(2 * count))


def scatter_shapes(count, columns):
    blocks = (count, count // 4, count // 4, count // 2)
    return [jax.ShapeDtypeStruct((part * GROUP, columns), bf16) for part in blocks]


def scatter_near(product, parts, sent):
    arriving = exchange(sent, "seq", 1)
    first, second, kept = parts
    rows = first.shape[0]

    def summed(part, row):
        return (product(part) + arriving[row : row + part.shape[0]].astype(f32)).astype(bf16)

    sends = (summed(first, 0), summed(second, rows))
    sends, kept = together(sends, kept)
    return sends, {"kept": summed(kept, 2 * rows), "arrived": ([], [])}


def scatter_rows(held, half, first, last):
    top = half * (held["kept"].shape[0] // 2)
    total = held["kept"][top + first : top + last].astype(f32)
    for value in held["arrived"][half]:
        total = total + value[first:last].astype(f32)
    return total


def scatter_far(sends, held, stage):
    orders = far_orders()
    arrived = tuple(
        [*held["arrived"][half], exchange(sends[half], "seq", orders[half][stage])]
        for half in range(2)
    )
    held = {"kept": held["kept"], "arrived": arrived}
    rows = sends[0].shape[0]
    if stage + 1 == len(orders[0]):
        return (), held
    ready = tuple(
        scatter_rows(held, half, rows // 2, rows).astype(bf16) for half in range(2)
    )
    return ready, held


def scatter_end(held):
    rows = held["arrived"][0][-1].shape[0]
    return jnp.concatenate([scatter_rows(held, half, 0, rows) for half in range(2)], axis=0)


def sum_seq(value):
    for bit in bits_of(lax.axis_size("seq")):
        value = value + exchange(value, "seq", bit)
    return value


def plane_pairs(ahead):
    planes, count = lax.axis_size("batch"), lax.axis_size("seq")
    per = count // planes
    pairs = []
    for owner in range(planes):
        for piece in range(planes):
            for k in range(per):
                holder = owner * count + piece * per + k
                user = (piece + ahead) % planes * count + owner * per + k
                pairs.append((holder, user))
    return pairs


def rows_from_owner(out_weight, width):
    per = lax.axis_size("seq") // lax.axis_size("batch")
    plane, mine = lax.axis_index("batch"), lax.axis_index("seq")
    rows = lax.dynamic_slice_in_dim(out_weight, mine % per * width, width, 0)
    return lax.psum(jnp.where(plane == mine // per, rows, jnp.zeros_like(rows)), "batch")


def to_owner(summed):
    return lax.ppermute(
        summed, ("batch", "seq"), [(user, holder) for holder, user in plane_pairs(0)]
    )


def double(held, turn):
    bits = bits_of(lax.axis_size("seq"))
    return jnp.concatenate([held, exchange(held, "seq", (bits[1:] + [1])[turn])], axis=0)


def step_values(raw):
    small = jnp.exp(-jnp.abs(raw))
    step = jnp.maximum(raw, 0.0) + jnp.log1p(small)
    sig = jnp.where(raw >= 0, 1.0, small) / (1.0 + small)
    tiny = raw < -20.0
    log_step = jnp.where(tiny, raw, jnp.log(step))
    ratio = jnp.where(tiny, 1.0, sig / step)
    return step, sig, log_step, ratio


def dot(a, b):
    return jnp.dot(a, b, preferred_element_type=f32)


def dot_nt(a, b):
    return lax.dot_general(a, b, (((1,), (1,)), ((), ())), preferred_element_type=f32)


def dot_tn(a, b):
    return lax.dot_general(a, b, (((0,), (0,)), ((), ())), preferred_element_type=f32)


def sigmoid(value):
    return 0.5 * jnp.tanh(0.5 * value) + 0.5


def silu_slope(value):
    sig = sigmoid(value)
    active = value * sig
    return active, sig + active * (1.0 - sig)


def split_parts(value, count):
    parts = []
    for _ in range(count):
        part = value.astype(bf16)
        parts.append(part)
        value = value - part.astype(f32)
    return parts


def dot_split(product, a, b):
    first, second = split_parts(b, 2)
    return product(a, first) + product(a, second)


def sum_along(rows, order):
    parts = jnp.concatenate([part.astype(f32) for part in split_parts(rows, 3)], axis=0)
    total = dot(parts.astype(bf16), order)
    return total[:8] + total[8:16] + total[16:24]


def to_columns(rows):
    stacked = jnp.concatenate(rows, axis=0)
    missing = LANES - stacked.shape[0]
    return jnp.concatenate([stacked, jnp.zeros((missing, GROUP), f32)], axis=0).T


def spread_heads(value, first, heads, size):
    rows = value.shape[0]
    return jnp.concatenate(
        [jnp.broadcast_to(value[:, first + h : first + h + 1], (rows, size)) for h in range(heads)],
        axis=1,
    )


def head_ones(width, size):
    row = lax.broadcasted_iota(jnp.int32, (8, width), 0)
    column = lax.broadcasted_iota(jnp.int32, (8, width), 1)
    return (column // size == row).astype(f32).astype(bf16)


def sum_lanes(value):
    return dot_nt(jnp.ones((8, value.shape[1]), bf16), value.astype(bf16))


def ones_where(condition):
    return jnp.where(condition, 1.0, 0.0).astype(bf16)


def order_indices(length):
    row = lax.broadcasted_iota(jnp.int32, (length, length), 0)
    column = lax.broadcasted_iota(jnp.int32, (length, length), 1)
    return row, column


def fetch(arrays, table, which, target, semaphore):
    for index, (array, row, rows) in enumerate(table):

        @pl.when(which == index)
        def _():
            pltpu.make_async_copy(arrays[array].at[pl.ds(row, rows)], target, semaphore).start()


def fetched(arrays, table, buffer, semaphores, order, blocks=1):
    step = pl.program_id(0)
    slot, other = lax.rem(step, 2), lax.rem(step + 1, 2)

    def start(step, slot):
        for k in range(blocks):
            target = buffer.at[slot, pl.ds(k * GROUP, GROUP)]
            fetch(arrays, table, order(step * blocks + k), target, semaphores.at[slot])

    @pl.when(step == 0)
    def _():
        start(0, 0)

    @pl.when(step + 1 < pl.num_programs(0))
    def _():
        start(step + 1, other)

    for k in range(blocks):
        source = arrays[0].at[pl.ds(0, GROUP)]
        target = buffer.at[slot, pl.ds(k * GROUP, GROUP)]
        pltpu.make_async_copy(source, target, semaphores.at[slot]).wait()
    return buffer[slot]


def store(source, targets, table, which, semaphore):
    for index, (array, row) in enumerate(table):

        @pl.when(which == index)
        def _():
            target = targets[array].at[pl.ds(row, GROUP)]
            pltpu.make_async_copy(source, target, semaphore).start()


def stored(buffer, targets, semaphores, slot):
    target = targets[0].at[pl.ds(0, GROUP)]
    pltpu.make_async_copy(buffer.at[slot], target, semaphores.at[slot]).wait()


def in_time(place, block):
    return ((block // 2) ^ place) * 2 + block % 2


def forward_kernel(dims, table, given, place_ref, *refs):
    heads, size, states, count = dims
    width = heads * size
    conv_cols = width + 2 * states
    arrays, refs = refs[:given], refs[given:]
    w_ref, conv_w_ref, conv_b_ref, step_ref, rows_ref = refs[:5]
    conv_in_ref, active_ref, slope_ref, gate_act_ref, gate_slope_ref = refs[5:10]
    raw_ref, ssd_ref, start_ref, scaled_ref, square_ref, normed_ref = refs[10:16]
    targets = refs[16:20]
    state, padded, order, barred, buffer, semaphores, placed, out_semaphores = refs[20:]
    turn = pl.program_id(0)
    slot = lax.rem(turn, 2)

    @pl.when(turn == 0)
    def _():
        state[...] = jnp.zeros_like(state)
        padded[0:HALO] = jnp.zeros_like(padded[0:HALO])
        row, column = order_indices(GROUP)
        order[...] = ones_where(row <= column)
        row, column = order_indices(HALF)
        barred[...] = jnp.where(row >= column, 0.0, -1e30)

    @pl.when(turn >= 2)
    def _():
        stored(placed, targets, out_semaphores, slot)

    normed = fetched(
        arrays, table, buffer, semaphores, lambda step: in_time(place_ref[0], step)
    )
    normed_ref[...] = normed
    projected = dot(normed, w_ref[...])
    conv_in = projected[:, width : width + conv_cols].astype(bf16)
    conv_in_ref[...] = conv_in
    padded[HALO : HALO + GROUP] = conv_in.astype(f32)
    conv_w = conv_w_ref[...]
    taps = conv_w.shape[0]
    pre = conv_b_ref[...]
    for k in range(taps):
        top = HALO - (taps - 1) + k
        pre = pre + conv_w[k : k + 1] * padded[top : top + GROUP]
    padded[0:HALO] = padded[GROUP : GROUP + HALO]
    active, slope = silu_slope(pre)
    active = active.astype(bf16)
    active_ref[...] = active
    slope_ref[...] = slope.astype(bf16)
    signal = active[:, :width]
    entry = active[:, width : width + states]
    readout = active[:, width + states :]
    signal_wide = signal.astype(f32)

    raw = projected[:, width + conv_cols :].T[:8]
    raw_ref[0] = raw
    step, _, log_step, _ = step_values(raw + step_ref[0:8, 0:1])
    running = sum_along(step * step_ref[8:16, 0:1], order[...])
    later = running - log_step
    total = running[:, GROUP - 1 :]
    columns = to_columns([running * LOG2E, jnp.exp(running), jnp.exp(total - later)])
    later = later * LOG2E
    early_wide = spread_heads(columns, 8, heads, size)
    tail_wide = spread_heads(columns, 16, heads, size)
    first, second = slice(0, HALF), slice(HALF, GROUP)
    scores = dot_nt(readout[first], entry[first])
    later_scores = dot_nt(readout[second], entry)
    within = []
    for h in range(heads):
        part = signal[:, h * size : (h + 1) * size]
        begin, end = columns[first, h : h + 1], columns[second, h : h + 1]
        row_first, row_second = later[h : h + 1, first], later[h : h + 1, second]
        near = jnp.exp2(begin - row_first + barred[...]) * scores
        full = jnp.exp2(end - row_first) * later_scores[:, first]
        last = jnp.exp2(end - row_second + barred[...]) * later_scores[:, second]
        both = jnp.concatenate([full.astype(bf16), last.astype(bf16)], axis=1)
        within.append(
            jnp.concatenate([dot(near.astype(bf16), part[first]), dot(both, part)], axis=0)
        )
    start = state[...]
    start_ref[0] = start
    carried = dot_split(dot, readout, start) * early_wide
    ssd = jnp.concatenate(within, axis=1) + carried + rows_ref[0:1] * signal_wide
    tail = signal_wide * tail_wide
    state[...] = start * early_wide[GROUP - 1 :] + dot_split(dot_tn, entry, tail)

    gate_act, gate_slope = silu_slope(projected[:, :width])
    gate_act_ref[...] = gate_act.astype(bf16)
    gate_slope_ref[...] = gate_slope.astype(bf16)
    ssd_ref[...] = ssd
    gated = ssd * gate_act
    scaled = (gated * rows_ref[1:2]).astype(bf16)
    scaled_ref[...] = scaled
    square_ref[0] = sum_lanes(gated * gated)
    placed[slot] = scaled
    where = in_time(place_ref[0], turn)
    store(placed.at[slot], targets, scatter_places(count), where, out_semaphores.at[slot])

    @pl.when(turn == pl.num_programs(0) - 1)
    def _():
        for other in range(2):
            stored(placed, targets, out_semaphores, other)


def time_estimate(microseconds, accessed):
    return pl.CostEstimate(
        flops=int(microseconds * 1.1e9), bytes_accessed=int(accessed), transcendentals=0
    )


def fixed(shape):
    return pl.BlockSpec(shape, lambda turn, place: (0,) * len(shape), pipeline_mode=pl.Buffered(1))


def anywhere(values):
    return [pl.BlockSpec(memory_space=pltpu.HBM)] * len(values)


def run_forward(place, pieces, params, dims):
    heads, size, states, count = dims
    arrays, table = pieces
    dim = params[0].shape[0]
    width, conv_cols = heads * size, params[1].shape[1]
    blocks = len(table)
    tokens = blocks * GROUP

    def moving(columns):
        return pl.BlockSpec((GROUP, columns), lambda turn, place: (turn, 0))

    def rows_of_block(height, columns):
        return pl.BlockSpec((1, height, columns), lambda turn, place: (turn, 0, 0))

    results = pl.pallas_call(
        functools.partial(forward_kernel, dims, table, len(arrays)),
        grid_spec=pltpu.PrefetchScalarGridSpec(
            num_scalar_prefetch=1,
            grid=(blocks,),
            in_specs=[*anywhere(arrays), *[fixed(param.shape) for param in params]],
            out_specs=[
                moving(conv_cols),
                moving(conv_cols),
                moving(conv_cols),
                moving(width),
                moving(width),
                rows_of_block(8, GROUP),
                moving(width),
                rows_of_block(states, width),
                moving(width),
                rows_of_block(8, GROUP),
                moving(dim),
                *anywhere(range(4)),
            ],
            scratch_shapes=[
                pltpu.VMEM((states, width), f32),
                pltpu.VMEM((HALO + GROUP, conv_cols), f32),
                pltpu.VMEM((GROUP, GROUP), bf16),
                pltpu.VMEM((HALF, HALF), f32),
                pltpu.VMEM((2, GROUP, dim), bf16),
                pltpu.SemaphoreType.DMA((2,)),
                pltpu.VMEM((2, GROUP, width), bf16),
                pltpu.SemaphoreType.DMA((2,)),
            ],
        ),
        out_shape=[
            jax.ShapeDtypeStruct((tokens, conv_cols), bf16),
            jax.ShapeDtypeStruct((tokens, conv_cols), bf16),
            jax.ShapeDtypeStruct((tokens, conv_cols), bf16),
            jax.ShapeDtypeStruct((tokens, width), bf16),
            jax.ShapeDtypeStruct((tokens, width), bf16),
            jax.ShapeDtypeStruct((blocks, 8, GROUP), f32),
            jax.ShapeDtypeStruct((tokens, width), f32),
            jax.ShapeDtypeStruct((blocks, states, width), f32),
            jax.ShapeDtypeStruct((tokens, width), bf16),
            jax.ShapeDtypeStruct((blocks, 8, GROUP), f32),
            jax.ShapeDtypeStruct((tokens, dim), bf16),
            *scatter_shapes(count, width),
        ],
        compiler_params=pltpu.CompilerParams(vmem_limit_bytes=60 * MIB),
        cost_estimate=time_estimate(blocks * 3.0, tokens * (4 * dim + 24 * width)),
        name="forward_blocks",
    )(place, *arrays, *params)
    return results[:11], results[11:]


def out_grad_kernel(table, given, place_ref, *refs):
    arrays, refs = refs[:given], refs[given:]
    scaled_ref, out_rows_ref, out_grad_ref, slope_ref, cot_ref = refs[:5]
    buffer, semaphores, copied = refs[5:]
    place, turn = place_ref[0], pl.program_id(0)
    rows = buffer.shape[1]

    def copy_on(turn):
        target = cot_ref.at[pl.ds(pl.multiple_of(turn * rows, rows), rows)]
        return pltpu.make_async_copy(buffer.at[lax.rem(turn, 2)], target, copied)

    @pl.when(turn >= 1)
    def _():
        copy_on(turn - 1).wait()

    cot = fetched(arrays, table, buffer, semaphores, lambda block: in_time(place, block), 2)
    copy_on(turn).start()
    out_grad = dot_nt(cot, out_rows_ref[...])
    out_grad_ref[...] = out_grad
    for block in range(2):
        here = slice(block * GROUP, (block + 1) * GROUP)
        slope_ref[block] = sum_lanes(out_grad[here] * scaled_ref[here].astype(f32))

    @pl.when(turn == pl.num_programs(0) - 1)
    def _():
        copy_on(turn).wait()


def run_out_grad(place, cots, scaled, out_rows):
    arrays, table = cots
    width, dim = out_rows.shape
    blocks = len(table)
    tokens = blocks * GROUP
    return pl.pallas_call(
        functools.partial(out_grad_kernel, table, len(arrays)),
        grid_spec=pltpu.PrefetchScalarGridSpec(
            num_scalar_prefetch=1,
            grid=(blocks // 2,),
            in_specs=[
                *anywhere(arrays),
                pl.BlockSpec((2 * GROUP, width), lambda turn, place: (turn, 0)),
                fixed(out_rows.shape),
            ],
            out_specs=[
                pl.BlockSpec((2 * GROUP, width), lambda turn, place: (turn, 0)),
                pl.BlockSpec((2, 8, GROUP), lambda turn, place: (turn, 0, 0)),
                *anywhere(range(1)),
            ],
            scratch_shapes=[
                pltpu.VMEM((2, 2 * GROUP, dim), bf16),
                pltpu.SemaphoreType.DMA((2,)),
                pltpu.SemaphoreType.DMA,
            ],
        ),
        out_shape=[
            jax.ShapeDtypeStruct((tokens, width), f32),
            jax.ShapeDtypeStruct((blocks, 8, GROUP), f32),
            jax.ShapeDtypeStruct((tokens, dim), bf16),
        ],
        compiler_params=pltpu.CompilerParams(vmem_limit_bytes=60 * MIB),
        cost_estimate=time_estimate(12, tokens * (4 * dim + 6 * width)),
        name="out_grad",
    )(place, *arrays, scaled, out_rows)


def backward_kernel(dims, place_ref, *refs):
    heads, size, states, count = dims
    width = heads * size
    conv_cols = width + 2 * states
    conv_in_ref, active_ref, slope_ref, gate_act_ref, gate_slope_ref = refs[:5]
    raw_ref, ssd_ref, start_ref, out_grad_ref, norm_ref = refs[5:10]
    conv_w_ref, step_ref, rows_ref = refs[10:13]
    out_ref, targets = refs[13], refs[14:18]
    sums = refs[18:24]
    gain_ref, skip_ref, conv_wg_ref, conv_bg_ref, bias_ref, rate_ref = sums
    state, pre_grads, order, back_order, barred, placed, semaphores = refs[24:]
    taps = conv_w_ref.shape[0]
    turn = pl.program_id(0)
    slot = lax.rem(turn, 2)

    @pl.when(turn >= 2)
    def _():
        stored(placed, targets, semaphores, slot)

    @pl.when(pl.program_id(0) == 0)
    def _():
        state[...] = jnp.zeros_like(state)
        pre_grads[0:HALO] = jnp.zeros_like(pre_grads[0:HALO])
        for total in sums:
            total[...] = jnp.zeros_like(total)
        row, column = order_indices(GROUP)
        order[...] = ones_where(row <= column)
        back_order[...] = ones_where(row >= column)
        row, column = order_indices(HALF)
        barred[...] = jnp.where(row <= column, 0.0, -1e30)

    gate_act, ssd, out_grad = gate_act_ref[...].astype(f32), ssd_ref[...], out_grad_ref[...]
    norms = norm_ref[0].T
    scale, slope = norms[:, 0:1], norms[:, 1:2]
    gated = ssd * gate_act
    gain_ref[...] += jnp.sum(out_grad * (gated * scale), axis=0, keepdims=True)
    gated_grad = out_grad * (rows_ref[1:2] * scale) - gated * slope
    grad_low = (gated_grad * gate_act).astype(bf16)
    gate_grad = (gated_grad * ssd * gate_slope_ref[...].astype(f32)).astype(bf16)
    out_ref[:, :width] = gate_grad
    placed[slot, :, :width] = gate_grad
    ssd_grad = grad_low.astype(f32)

    raw = raw_ref[0] + step_ref[0:8, 0:1]
    rate = step_ref[8:16, 0:1]
    step, sig, log_step, ratio = step_values(raw)
    decay = step * rate
    running = sum_along(decay, order[...])
    later = running - log_step
    total = running[:, GROUP - 1 :]
    columns = to_columns([later * LOG2E, jnp.exp(running), jnp.exp(total - later)])
    running = running * LOG2E
    early_wide = spread_heads(columns, 8, heads, size)
    tail_wide = spread_heads(columns, 16, heads, size)

    signal = active_ref[:, :width]
    entry = active_ref[:, width : width + states]
    readout = active_ref[:, width + states :]
    signal_wide = signal.astype(f32)
    start = start_ref[0]
    start_low = start.astype(bf16)
    end_grad = state[...]
    end_low = end_grad.astype(bf16)
    first, second = slice(0, HALF), slice(HALF, GROUP)
    scores = dot_nt(entry[first], readout)
    later_scores = dot_nt(entry[second], readout[second])
    near_grad, far_grad, last_grad = 0.0, 0.0, 0.0
    within = []
    for h in range(heads):
        part, grad = signal[:, h * size : (h + 1) * size], grad_low[:, h * size : (h + 1) * size]
        begin, end = columns[first, h : h + 1], columns[second, h : h + 1]
        row_first, row_second = running[h : h + 1, first], running[h : h + 1, second]
        near = jnp.exp2(row_first - begin + barred[...])
        full = jnp.exp2(row_second - begin)
        last = jnp.exp2(row_second - end + barred[...])
        both = jnp.concatenate(
            [
                (near * scores[:, first]).astype(bf16),
                (full * scores[:, second]).astype(bf16),
            ],
            axis=1,
        )
        final = (last * later_scores).astype(bf16)
        within.append(jnp.concatenate([dot(both, grad), dot(final, grad[second])], axis=0))
        cross = dot_nt(part[first], grad)
        near_grad = near_grad + cross[:, first] * near
        far_grad = far_grad + cross[:, second] * full
        last_grad = last_grad + dot_nt(part[second], grad[second]) * last
    tail_grad = tail_wide * dot_split(dot, entry, end_grad)
    signal_grad = jnp.concatenate(within, axis=1) + tail_grad
    score_first = jnp.concatenate([near_grad, far_grad], axis=1).astype(bf16)
    score_second = last_grad.astype(bf16)
    tail = (signal_wide * tail_wide).astype(bf16)
    head_grad = ssd_grad * early_wide
    entry_grad = jnp.concatenate(
        [dot(score_first, readout), dot(score_second, readout[second])], axis=0
    ) + dot_nt(tail, end_low)
    readout_grad = dot_tn(score_first, entry[first]) + dot_nt(head_grad.astype(bf16), start_low)
    readout_last = readout_grad[second] + dot_tn(score_second, entry[second])
    total_wide = early_wide[GROUP - 1 :]
    state[...] = end_grad * total_wide + dot_split(dot_tn, readout, head_grad)

    skip = rows_ref[0:1]
    ones = head_ones(width, size)
    column_part = signal_wide * signal_grad
    row_part = ssd_grad * (ssd - skip * signal_wide)
    end_part = jnp.sum(signal_wide * tail_grad, axis=0, keepdims=True) + total_wide * jnp.sum(
        start * end_grad, axis=0, keepdims=True
    )

    def head_sums(value, parts):
        return sum(dot_nt(ones, part) for part in split_parts(value, parts))

    end_rows = head_sums(jnp.broadcast_to(end_part, (8, width)), 2)[:, 0:1]
    decay_grad = sum_along(head_sums(row_part - column_part, 2), back_order[...]) + end_rows
    raw_grad = head_sums(column_part, 1) * ratio + decay_grad * rate * sig
    skip_ref[...] += jnp.sum(ssd_grad * signal_wide, axis=0, keepdims=True)
    bias_ref[...] += raw_grad
    rate_ref[...] += decay_grad * decay
    raw_low = to_columns([raw_grad]).astype(bf16)
    out_ref[:, width + conv_cols :] = raw_low
    placed[slot, :, width + conv_cols :] = raw_low

    pre_grads[GROUP : GROUP + HALO] = pre_grads[0:HALO]
    pre_grads[0:GROUP, :width] = (signal_grad + skip * ssd_grad) * slope_ref[:, :width].astype(f32)
    sides = slope_ref[:, width:].astype(f32)
    pre_grads[0:GROUP, width : width + states] = entry_grad * sides[:, :states]
    pre_grads[0:HALF, width + states :] = readout_grad[first] * sides[first, states:]
    pre_grads[HALF:GROUP, width + states :] = readout_last * sides[second, states:]
    conv_w = conv_w_ref[...]
    conv_in = conv_in_ref[...].astype(f32)
    conv_grad = 0.0
    for k in range(taps):
        ahead = taps - 1 - k
        shifted = pre_grads[ahead : ahead + GROUP]
        conv_grad = conv_grad + conv_w[k : k + 1] * shifted
        conv_wg_ref[k : k + 1] += jnp.sum(shifted * conv_in, axis=0, keepdims=True)
        if ahead == 0:
            conv_bg_ref[...] += jnp.sum(shifted, axis=0, keepdims=True)
    conv_low = conv_grad.astype(bf16)
    out_ref[:, width : width + conv_cols] = conv_low
    placed[slot, :, width : width + conv_cols] = conv_low

    where = in_time(place_ref[0], pl.num_programs(0) - 1 - turn)
    store(placed.at[slot], targets, scatter_places(count), where, semaphores.at[slot])

    @pl.when(turn == pl.num_programs(0) - 1)
    def _():
        for other in range(2):
            stored(placed, targets, semaphores, other)


def run_backward(place, values, params, dims):
    heads, size, states, count = dims
    conv_cols, width = values[0].shape[1], heads * size
    tokens = values[0].shape[0]
    blocks = tokens // GROUP
    last = blocks - 1
    out_cols = width + conv_cols + LANES

    def moving(columns):
        return pl.BlockSpec((GROUP, columns), lambda turn, place: (last - turn, 0))

    def rows_of_block():
        return pl.BlockSpec((1, 8, GROUP), lambda turn, place: (last - turn, 0, 0))

    sums = [(1, width), (1, width), params[0].shape, (1, conv_cols), (8, GROUP), (8, GROUP)]
    return pl.pallas_call(
        functools.partial(backward_kernel, dims),
        grid_spec=pltpu.PrefetchScalarGridSpec(
            num_scalar_prefetch=1,
            grid=(blocks,),
            in_specs=[
                moving(conv_cols),
                moving(conv_cols),
                moving(conv_cols),
                moving(width),
                moving(width),
                rows_of_block(),
                moving(width),
                pl.BlockSpec((1, states, width), lambda turn, place: (last - turn, 0, 0)),
                moving(width),
                rows_of_block(),
                *[fixed(param.shape) for param in params],
            ],
            out_specs=[
                moving(out_cols),
                *anywhere(range(4)),
                *[fixed(shape) for shape in sums],
            ],
            scratch_shapes=[
                pltpu.VMEM((states, width), f32),
                pltpu.VMEM((GROUP + HALO, conv_cols), f32),
                pltpu.VMEM((GROUP, GROUP), bf16),
                pltpu.VMEM((GROUP, GROUP), bf16),
                pltpu.VMEM((HALF, HALF), f32),
                pltpu.VMEM((2, GROUP, out_cols), bf16),
                pltpu.SemaphoreType.DMA((2,)),
            ],
        ),
        out_shape=[
            jax.ShapeDtypeStruct((tokens, out_cols), bf16),
            *scatter_shapes(count, out_cols),
        ]
        + [jax.ShapeDtypeStruct(shape, f32) for shape in sums],
        compiler_params=pltpu.CompilerParams(vmem_limit_bytes=60 * MIB),
        cost_estimate=time_estimate(blocks * 3.5, tokens * 40 * width),
        name="backward_blocks",
    )(place, *values, *params)


def widen_kernel(place_ref, piece_ref, out_ref):
    out_ref[...] = piece_ref[0].astype(f32)


def assemble_out(place, pieces, per):
    count, size, dim = pieces.shape
    groups = count // per

    def source(turn, place):
        relative = (turn % groups * per + turn // groups) ^ place[0]
        return ((relative & 1) * (count // 2) + (relative >> 1), 0, 0)

    return pl.pallas_call(
        widen_kernel,
        grid_spec=pltpu.PrefetchScalarGridSpec(
            num_scalar_prefetch=1,
            grid=(count,),
            in_specs=[pl.BlockSpec((1, size, dim), source)],
            out_specs=pl.BlockSpec((size, dim), lambda turn, place: (turn, 0)),
        ),
        out_shape=jax.ShapeDtypeStruct((count * size, dim), f32),
        cost_estimate=time_estimate(5, count * size * dim * 6),
        name="assemble_out_weight_grad",
    )(place, pieces)


def assemble_kernel(dims, pieces_ref, out_ref):
    heads, size, states, count = dims
    width, shared = heads * size, 2 * states
    inner = count * width
    total = 0.0
    for device in range(count):
        columns = pieces_ref[device].astype(f32).T
        out_ref[device * width : (device + 1) * width] = columns[:width]
        out_ref[inner + device * width : inner + (device + 1) * width] = columns[width : 2 * width]
        total = total + columns[2 * width : 2 * width + shared]
        last = 2 * inner + shared + device * heads
        out_ref[last : last + heads] = columns[2 * width + shared : 2 * width + shared + heads]
    out_ref[2 * inner : 2 * inner + shared] = total


def assemble(pieces, dims):
    heads, size, states, count = dims
    _, rows, columns = pieces.shape
    tile = LANES if rows % LANES == 0 else rows
    out_rows = 2 * count * heads * size + 2 * states + count * heads
    return pl.pallas_call(
        functools.partial(assemble_kernel, dims),
        grid=(rows // tile,),
        in_specs=[pl.BlockSpec((count, tile, columns), lambda turn: (0, turn, 0))],
        out_specs=pl.BlockSpec((out_rows, tile), lambda turn: (0, turn)),
        out_shape=jax.ShapeDtypeStruct((out_rows, rows), f32),
        compiler_params=pltpu.CompilerParams(vmem_limit_bytes=60 * MIB),
        cost_estimate=time_estimate(8, out_rows * rows * 6),
        name="assemble_in_weight_grad",
    )(pieces)


def body(
    tokens,
    norm_gain,
    in_weight,
    conv_weight,
    conv_bias,
    dt_bias,
    decay_log,
    skip_scale,
    gate_gain,
    out_weight,
    cotangent,
):
    count, mine = lax.axis_size("seq"), lax.axis_index("seq")
    place = mine.astype(jnp.int32).reshape(1)
    inner, all_heads, conv_all = gate_gain.shape[0], dt_bias.shape[0], conv_bias.shape[0]
    size, states = inner // all_heads, (conv_all - inner) // 2
    heads, width = all_heads // count, inner // count
    dims = (heads, size, states, count)
    shared = 2 * states
    conv_cols = width + shared
    tok_rows = tokens.shape[1]
    per_plane = out_weight.shape[0] // width

    def own(vector, per, first=0):
        return lax.dynamic_slice_in_dim(vector, first + mine * per, per, vector.ndim - 1)

    def own_conv(array, first=0):
        return jnp.concatenate(
            [own(array, width, first), array[..., first + inner : first + conv_all]], axis=-1
        )

    tokens_row = tokens[0].astype(f32)
    inverse = lax.rsqrt(jnp.mean(tokens_row * tokens_row, axis=-1, keepdims=True) + epsilon)
    normed_own = (tokens_row * inverse * norm_gain).astype(bf16)
    step_own = own(in_weight, heads, inner + conv_all)
    w_own = jnp.concatenate(
        [
            own(in_weight, width),
            own_conv(in_weight, inner),
            jnp.pad(step_own, ((0, 0), (0, LANES - heads))),
        ],
        axis=1,
    )
    w_cols = lax.all_gather(w_own, "batch", axis=0, tiled=True)
    stages = gather_stages()
    held = gather_stage(gather_stage(gather_start(normed_own), 0), 1)
    held, cots = together(held, gather_start(cotangent[0]))
    cots = gather_stage(cots, 0)
    for stage in range(2, stages):
        held = gather_stage(held, stage)
    w_cols, held, cots, out_owned = together(w_cols, held, cots, out_weight)
    cots = gather_stage(cots, 1)
    out_rows = rows_from_owner(out_owned, width)

    conv_w, conv_b = own_conv(conv_weight), own_conv(conv_bias)[None]
    per_head = jnp.stack([own(dt_bias, heads), -jnp.exp(own(decay_log, heads))])
    per_head = jnp.pad(per_head, ((0, 0), (0, 8 - heads))).reshape(16, 1)
    step_rows = jnp.broadcast_to(per_head, (16, LANES))
    gain_own = own(gate_gain, width)[None]
    rows = jnp.concatenate(
        [jnp.repeat(own(skip_scale, heads), size)[None], gain_own, jnp.zeros((6, width), f32)],
        axis=0,
    )
    results, out_parts = run_forward(
        place, token_pieces(held), (w_cols, conv_w, conv_b, step_rows, rows), dims
    )
    conv_in, active, slope, gate_act, gate_slope, raw, ssd, starts, scaled, squares, normed = results
    out_parts, cots, out_rows = together(out_parts, cots, out_rows)
    for stage in range(2, stages):
        cots = gather_stage(cots, stage)

    def out_product(part):
        return dot(part, out_rows)

    out_send = out_product(out_parts[0]).astype(bf16)
    out_send, cots = together(out_send, cots)
    out_grad, slopes, cot = run_out_grad(place, token_pieces(cots), scaled, out_rows)
    sums = jnp.stack([squares[:, 0].reshape(-1), slopes[:, 0].reshape(-1)])
    out_ready, out_held = scatter_near(out_product, out_parts[1:], out_send)
    sums = sums + exchange(sums, "seq", 1)
    sums, first = together(sums, out_ready[0])
    sums = sums + exchange(sums, "seq", 2)
    sums, second = together(sums, out_ready[1])
    for bit in bits_of(count)[2:]:
        sums = sums + exchange(sums, "seq", bit)
    scale = lax.rsqrt(sums[0] / inner + epsilon)
    norms = jnp.stack([scale, scale * scale * scale * sums[1] / inner])
    norms = jnp.pad(norms, ((0, 6), (0, 0))).reshape(8, -1, GROUP).swapaxes(0, 1)
    normed_out = (scaled.astype(f32) * scale[:, None]).astype(bf16)
    out_term = jnp.einsum("te,td->ed", normed_out, cot, preferred_element_type=f32)
    out_term, norms, first, second = together(out_term.astype(bf16), norms, first, second)
    out_sum = lax.psum_scatter(out_term, "batch", scatter_dimension=0, tiled=True)
    out_ready, out_held = scatter_far((first, second), out_held, 0)

    values = (conv_in, active, slope, gate_act, gate_slope, raw, ssd, starts, out_grad, norms)
    results = run_backward(place, values, (conv_w, step_rows, rows), dims)
    proj_grad, back_parts = results[0], results[1:5]
    proj_grad, back_parts, out_ready, out_held, out_sum = together(
        proj_grad, back_parts, out_ready, out_held, out_sum
    )

    def back_product(part):
        return jnp.einsum("tf,df->td", part, w_cols, preferred_element_type=f32)

    def weight_product(part):
        return jnp.einsum("td,tf->df", normed, part, preferred_element_type=f32).astype(bf16)

    for stage in range(1, stages - 1):
        out_ready, out_held = scatter_far(out_ready, out_held, stage)
    back_send = back_product(back_parts[0]).astype(bf16)
    back_send, proj_grad = together(back_send, proj_grad)
    in_term = weight_product(proj_grad)
    in_term, keeps, out_held = together(in_term, back_parts[1:], out_held)
    in_sum = lax.psum_scatter(in_term, "batch", scatter_dimension=0, tiled=True)
    back_ready, back_held = scatter_near(back_product, keeps, back_send)
    back_ready, out_sum = together(back_ready, out_sum)
    back_ready, back_held = scatter_far(back_ready, back_held, 0)
    out_pieces = to_owner(out_sum)[None]

    back_held["kept"], in_term, results = together(back_held["kept"], in_term, results[5:])
    gain_term, skip_term, conv_w_term, conv_b_term, bias_term, rate_term = results
    norm_gain_term = jnp.sum(in_term.astype(f32) * w_cols.astype(f32), axis=1) / norm_gain

    def among_heads(vector, per, total):
        return lax.dynamic_update_slice_in_dim(jnp.zeros((total,), f32), vector, mine * per, 0)

    def among_conv(array):
        wide = jnp.zeros((array.shape[0], inner), f32)
        wide = lax.dynamic_update_slice_in_dim(wide, array[:, :width], mine * width, 1)
        return jnp.concatenate([wide, array[:, width:]], axis=1).reshape(-1)

    skip_heads = jnp.sum(skip_term.reshape(heads, size), axis=1)
    terms = [
        norm_gain_term,
        among_conv(conv_w_term),
        among_conv(conv_b_term),
        among_heads(jnp.sum(bias_term[:heads], axis=1), heads, all_heads),
        among_heads(jnp.sum(rate_term[:heads], axis=1), heads, all_heads),
        among_heads(skip_heads, heads, all_heads),
        among_heads(gain_term[0], width, inner),
    ]
    vector = jnp.concatenate(terms)
    padding = -vector.shape[0] % (8 * LANES)
    vector = jnp.pad(vector, (0, padding)).reshape(-1, LANES)

    axes = [(axis, bit) for axis in ("seq", "batch") for bit in bits_of(lax.axis_size(axis))]
    vector = vector + exchange(vector, *axes.pop(0))
    back_ready, vector, out_pieces = together(back_ready, vector, out_pieces)
    for stage in range(1, stages - 1):
        back_ready, back_held = scatter_far(back_ready, back_held, stage)
    out_pieces = double(out_pieces, 0)
    vector = vector + exchange(vector, *axes.pop(0))
    back_held["arrived"], vector, out_pieces, in_sum = together(
        back_held["arrived"], vector, out_pieces, in_sum
    )
    pieces = lax.all_gather(in_sum, "seq", axis=0, tiled=False)
    in_weight_grad = assemble(pieces, dims).T
    for stage in range(1, stages):
        out_pieces = double(out_pieces, stage)
    while axes:
        vector = vector + exchange(vector, *axes.pop(0))
    vector = vector.reshape(-1)
    normed_grad = scatter_end(back_held)
    cot_row = cotangent[0].astype(f32)
    gained = norm_gain * normed_grad
    slope = inverse * inverse * inverse * jnp.mean(gained * tokens_row, axis=-1, keepdims=True)
    input_grad = cot_row + inverse * gained - tokens_row * slope
    own_scale = lax.dynamic_slice_in_dim(scale, mine * tok_rows, tok_rows, 0)[:, None]
    block_out = (tokens_row + own_scale * scatter_end(out_held)).astype(bf16)
    out_weight_grad = assemble_out(place, out_pieces, per_plane)

    parts, offset = [], 0
    for term in terms:
        parts.append(vector[offset : offset + term.shape[0]])
        offset += term.shape[0]
    return (
        block_out[None],
        input_grad[None],
        parts[0],
        in_weight_grad,
        parts[1].reshape(conv_weight.shape),
        parts[2],
        parts[3],
        parts[4],
        parts[5],
        parts[6],
        out_weight_grad,
    )


def solution(mesh):
    placed = (
        P("batch", "seq", None),
        P(),
        P("batch", None),
        P(),
        P(),
        P(),
        P(),
        P(),
        P(),
        P("batch", None),
        P("batch", "seq", None),
    )
    return jax.shard_map(
        body,
        mesh=mesh,
        in_specs=placed,
        out_specs=(
            P("batch", "seq", None),
            P("batch", "seq", None),
            P(),
            P("batch", None),
            P(),
            P(),
            P(),
            P(),
            P(),
            P(),
            P("batch", None),
        ),
        check_vma=False,
    )
```

```python
import functools

import jax
import jax.numpy as jnp
from jax import lax
from jax.experimental import pallas as pl
from jax.experimental.pallas import tpu as pltpu
from jax.sharding import PartitionSpec as P

GROUP = 256
LANES = 128
HALF = GROUP // 2
HALO = 8
STEP_ROWS = 16
LOG2E = 1.4426950408889634
epsilon = 1e-05
f32 = jnp.float32
bf16 = jnp.bfloat16
MIB = 2**20


def exchange(value, axis, distance):
    count = lax.axis_size(axis)
    return lax.ppermute(value, axis, [(source, source ^ distance) for source in range(count)])


def bits_of(count):
    return [1 << k for k in range(count.bit_length() - 1)]


def placed_order(count):
    return [2 * k for k in range(count // 2)] + [2 * k + 1 for k in range(count // 2)]


def together(*values):
    return lax.optimization_barrier(values)


def far_orders():
    far = bits_of(lax.axis_size("seq"))[1:]
    return far, far[::-1]


def gather_start(value):
    half = value.shape[0] // 32 * 16
    return tuple({"base": part, "fresh": None, "near": []} for part in (value[:half], value[half:]))


def gather_stage(held, stage, late=False):
    grown = []
    for half, order in zip(held, far_orders()):
        base, fresh, near = half["base"], half["fresh"], list(half["near"])
        if stage >= 1:
            merged = base if stage == len(order) else jnp.concatenate([base, fresh], axis=0)
            if not late:
                near.append(exchange(merged if stage == 1 else fresh, "seq", 1))
            elif stage == len(order):
                near = [exchange(base, "seq", 1), exchange(fresh, "seq", 1)]
            base = merged
        if stage < len(order):
            fresh = exchange(base, "seq", order[stage])
        grown.append({"base": base, "fresh": fresh, "near": near})
    return tuple(grown)


def gather_stages():
    return len(bits_of(lax.axis_size("seq")))


def gathered(held):
    arrays, table = [], {}
    for number, (half, order) in enumerate(zip(held, far_orders())):
        indices = [0]
        for bit in order:
            indices += [index | bit for index in indices]
        middle = len(indices) // 2
        groups = [(half["base"], indices[:middle]), (half["fresh"], indices[middle:])]
        bounds = [0] + [2 << k for k in range(len(order))]
        if len(half["near"]) < len(order):
            bounds = [0, middle, len(indices)]
        for value, first, last in zip(half["near"], bounds, bounds[1:]):
            groups.append((value, [index | 1 for index in indices[first:last]]))
        for value, members in groups:
            rows = value.shape[0] // len(members)
            for turn, index in enumerate(members):
                table[number, index] = (len(arrays), turn * rows, rows)
            arrays.append(value)
    return arrays, table


def token_pieces(held):
    arrays, table = gathered(held)
    indices = range(lax.axis_size("seq"))
    return arrays, tuple(table[half, index] for index in indices for half in range(2))


def gather_all(value):
    held = gather_start(value)
    for stage in range(gather_stages()):
        held = gather_stage(held, stage)
    return held


def scatter_places(count):
    far = bits_of(count)[1:]
    table = {}
    row = {}
    for near in (1, 0):
        for sent in (True, False):
            for half, order in enumerate((far, far[::-1])):
                members = [0]
                for bit in order[:0:-1]:
                    members += [member | bit for member in members]
                for member in members:
                    index = member | near | (order[0] if sent else 0)
                    array = 0 if near else (1 + half if sent else 3)
                    table[index * 2 + half] = (array, row.get(array, 0))
                    row[array] = row.get(array, 0) + GROUP
    return tuple(table[k] for k in range(2 * count))


def scatter_shapes(count, columns):
    blocks = (count, count // 4, count // 4, count // 2)
    return [jax.ShapeDtypeStruct((part * GROUP, columns), bf16) for part in blocks]


def scatter_near(product, parts, sent):
    arriving = exchange(sent, "seq", 1)
    first, second, kept = parts
    rows = first.shape[0]

    def summed(part, row):
        return (product(part) + arriving[row : row + part.shape[0]].astype(f32)).astype(bf16)

    sends = (summed(first, 0), summed(second, rows))
    sends, kept = together(sends, kept)
    return sends, {"kept": summed(kept, 2 * rows), "arrived": ([], [])}


def scatter_rows(held, half, first, last):
    top = half * (held["kept"].shape[0] // 2)
    total = held["kept"][top + first : top + last].astype(f32)
    for value in held["arrived"][half]:
        total = total + value[first:last].astype(f32)
    return total


def scatter_far(sends, held, stage):
    orders = far_orders()
    arrived = tuple(
        [*held["arrived"][half], exchange(sends[half], "seq", orders[half][stage])]
        for half in range(2)
    )
    held = {"kept": held["kept"], "arrived": arrived}
    rows = sends[0].shape[0]
    if stage + 1 == len(orders[0]):
        return (), held
    ready = tuple(
        scatter_rows(held, half, rows // 2, rows).astype(bf16) for half in range(2)
    )
    return ready, held


def scatter_end(held):
    rows = held["arrived"][0][-1].shape[0]
    return jnp.concatenate([scatter_rows(held, half, 0, rows) for half in range(2)], axis=0)


def sum_seq(value):
    for bit in bits_of(lax.axis_size("seq")):
        value = value + exchange(value, "seq", bit)
    return value


def plane_pairs(ahead):
    planes, count = lax.axis_size("batch"), lax.axis_size("seq")
    per = count // planes
    pairs = []
    for owner in range(planes):
        for piece in range(planes):
            for k in range(per):
                holder = owner * count + piece * per + k
                user = (piece + ahead) % planes * count + owner * per + k
                pairs.append((holder, user))
    return pairs


def rows_from_owner(out_weight, width):
    per = lax.axis_size("seq") // lax.axis_size("batch")
    plane, mine = lax.axis_index("batch"), lax.axis_index("seq")
    rows = lax.dynamic_slice_in_dim(out_weight, mine % per * width, width, 0)
    return lax.psum(jnp.where(plane == mine // per, rows, jnp.zeros_like(rows)), "batch")


def to_owner(summed):
    return lax.ppermute(
        summed, ("batch", "seq"), [(user, holder) for holder, user in plane_pairs(0)]
    )


def double(held, turn):
    bits = bits_of(lax.axis_size("seq"))
    return jnp.concatenate([held, exchange(held, "seq", (bits[1:] + [1])[turn])], axis=0)


def step_values(raw):
    small = jnp.exp(-jnp.abs(raw))
    step = jnp.maximum(raw, 0.0) + jnp.log1p(small)
    sig = jnp.where(raw >= 0, 1.0, small) / (1.0 + small)
    tiny = raw < -20.0
    log_step = jnp.where(tiny, raw, jnp.log(step))
    ratio = jnp.where(tiny, 1.0, sig / step)
    return step, sig, log_step, ratio


def dot(a, b):
    return jnp.dot(a, b, preferred_element_type=f32)


def dot_nt(a, b):
    return lax.dot_general(a, b, (((1,), (1,)), ((), ())), preferred_element_type=f32)


def dot_tn(a, b):
    return lax.dot_general(a, b, (((0,), (0,)), ((), ())), preferred_element_type=f32)


def sigmoid(value):
    return 0.5 * jnp.tanh(0.5 * value) + 0.5


def silu_slope(value):
    sig = sigmoid(value)
    active = value * sig
    return active, sig + active * (1.0 - sig)


def split_parts(value, count):
    parts = []
    for _ in range(count):
        part = value.astype(bf16)
        parts.append(part)
        value = value - part.astype(f32)
    return parts


def dot_split(product, a, b):
    first, second = split_parts(b, 2)
    return product(a, first) + product(a, second)


def sum_along(rows, order):
    parts = jnp.concatenate([part.astype(f32) for part in split_parts(rows, 3)], axis=0)
    total = dot(parts.astype(bf16), order)
    return total[:8] + total[8:16] + total[16:24]


def to_columns(rows):
    stacked = jnp.concatenate(rows, axis=0)
    missing = LANES - stacked.shape[0]
    return jnp.concatenate([stacked, jnp.zeros((missing, GROUP), f32)], axis=0).T


def spread_heads(value, first, heads, size):
    rows = value.shape[0]
    return jnp.concatenate(
        [jnp.broadcast_to(value[:, first + h : first + h + 1], (rows, size)) for h in range(heads)],
        axis=1,
    )


def head_ones(width, size):
    row = lax.broadcasted_iota(jnp.int32, (8, width), 0)
    column = lax.broadcasted_iota(jnp.int32, (8, width), 1)
    return (column // size == row).astype(f32).astype(bf16)


def sum_lanes(value):
    return dot_nt(jnp.ones((8, value.shape[1]), bf16), value.astype(bf16))


def ones_where(condition):
    return jnp.where(condition, 1.0, 0.0).astype(bf16)


def order_indices(length):
    row = lax.broadcasted_iota(jnp.int32, (length, length), 0)
    column = lax.broadcasted_iota(jnp.int32, (length, length), 1)
    return row, column


def fetch(arrays, table, which, target, semaphore):
    for index, (array, row, rows) in enumerate(table):

        @pl.when(which == index)
        def _():
            pltpu.make_async_copy(arrays[array].at[pl.ds(row, rows)], target, semaphore).start()


def fetched(arrays, table, buffer, semaphores, order, blocks=1):
    step = pl.program_id(0)
    slot, other = lax.rem(step, 2), lax.rem(step + 1, 2)

    def start(step, slot):
        for k in range(blocks):
            target = buffer.at[slot, pl.ds(k * GROUP, GROUP)]
            fetch(arrays, table, order(step * blocks + k), target, semaphores.at[slot])

    @pl.when(step == 0)
    def _():
        start(0, 0)

    @pl.when(step + 1 < pl.num_programs(0))
    def _():
        start(step + 1, other)

    for k in range(blocks):
        source = arrays[0].at[pl.ds(0, GROUP)]
        target = buffer.at[slot, pl.ds(k * GROUP, GROUP)]
        pltpu.make_async_copy(source, target, semaphores.at[slot]).wait()
    return buffer[slot]


def store(source, targets, table, which, semaphore):
    for index, (array, row) in enumerate(table):

        @pl.when(which == index)
        def _():
            target = targets[array].at[pl.ds(row, GROUP)]
            pltpu.make_async_copy(source, target, semaphore).start()


def stored(buffer, targets, semaphores, slot):
    target = targets[0].at[pl.ds(0, GROUP)]
    pltpu.make_async_copy(buffer.at[slot], target, semaphores.at[slot]).wait()


def in_time(place, block):
    return ((block // 2) ^ place) * 2 + block % 2


def forward_kernel(dims, table, given, place_ref, *refs):
    heads, size, states, count = dims
    width = heads * size
    conv_cols = width + 2 * states
    arrays, refs = refs[:given], refs[given:]
    w_ref, conv_w_ref, conv_b_ref, step_ref, rows_ref = refs[:5]
    conv_in_ref, active_ref, slope_ref, gate_act_ref, gate_slope_ref = refs[5:10]
    raw_ref, ssd_ref, start_ref, scaled_ref, square_ref, normed_ref = refs[10:16]
    targets = refs[16:20]
    state, padded, order, barred, buffer, semaphores, placed, out_semaphores = refs[20:]
    turn = pl.program_id(0)
    slot = lax.rem(turn, 2)

    @pl.when(turn == 0)
    def _():
        state[...] = jnp.zeros_like(state)
        padded[0:HALO] = jnp.zeros_like(padded[0:HALO])
        row, column = order_indices(GROUP)
        order[...] = ones_where(row <= column)
        row, column = order_indices(HALF)
        barred[...] = jnp.where(row >= column, 0.0, -1e30)

    @pl.when(turn >= 2)
    def _():
        stored(placed, targets, out_semaphores, slot)

    normed = fetched(
        arrays, table, buffer, semaphores, lambda step: in_time(place_ref[0], step)
    )
    normed_ref[...] = normed
    projected = dot(normed, w_ref[...])
    conv_in = projected[:, width : width + conv_cols].astype(bf16)
    conv_in_ref[...] = conv_in
    padded[HALO : HALO + GROUP] = conv_in.astype(f32)
    conv_w = conv_w_ref[...]
    taps = conv_w.shape[0]
    pre = conv_b_ref[...]
    for k in range(taps):
        top = HALO - (taps - 1) + k
        pre = pre + conv_w[k : k + 1] * padded[top : top + GROUP]
    padded[0:HALO] = padded[GROUP : GROUP + HALO]
    active, slope = silu_slope(pre)
    active = active.astype(bf16)
    active_ref[...] = active
    slope_ref[...] = slope.astype(bf16)
    signal = active[:, :width]
    entry = active[:, width : width + states]
    readout = active[:, width + states :]
    signal_wide = signal.astype(f32)

    raw = projected[:, width + conv_cols :].T[:8]
    raw_ref[0] = raw
    step, _, log_step, _ = step_values(raw + step_ref[0:8, 0:1])
    running = sum_along(step * step_ref[8:16, 0:1], order[...])
    later = running - log_step
    total = running[:, GROUP - 1 :]
    columns = to_columns([running * LOG2E, jnp.exp(running), jnp.exp(total - later)])
    later = later * LOG2E
    early_wide = spread_heads(columns, 8, heads, size)
    tail_wide = spread_heads(columns, 16, heads, size)
    first, second = slice(0, HALF), slice(HALF, GROUP)
    scores = dot_nt(readout[first], entry[first])
    later_scores = dot_nt(readout[second], entry)
    within = []
    for h in range(heads):
        part = signal[:, h * size : (h + 1) * size]
        begin, end = columns[first, h : h + 1], columns[second, h : h + 1]
        row_first, row_second = later[h : h + 1, first], later[h : h + 1, second]
        near = jnp.exp2(begin - row_first + barred[...]) * scores
        full = jnp.exp2(end - row_first) * later_scores[:, first]
        last = jnp.exp2(end - row_second + barred[...]) * later_scores[:, second]
        both = jnp.concatenate([full.astype(bf16), last.astype(bf16)], axis=1)
        within.append(
            jnp.concatenate([dot(near.astype(bf16), part[first]), dot(both, part)], axis=0)
        )
    start = state[...]
    start_ref[0] = start
    carried = dot_split(dot, readout, start) * early_wide
    ssd = jnp.concatenate(within, axis=1) + carried + rows_ref[0:1] * signal_wide
    tail = signal_wide * tail_wide
    state[...] = start * early_wide[GROUP - 1 :] + dot_split(dot_tn, entry, tail)

    gate_act, gate_slope = silu_slope(projected[:, :width])
    gate_act_ref[...] = gate_act.astype(bf16)
    gate_slope_ref[...] = gate_slope.astype(bf16)
    ssd_ref[...] = ssd
    gated = ssd * gate_act
    scaled = (gated * rows_ref[1:2]).astype(bf16)
    scaled_ref[...] = scaled
    square_ref[0] = sum_lanes(gated * gated)
    placed[slot] = scaled
    where = in_time(place_ref[0], turn)
    store(placed.at[slot], targets, scatter_places(count), where, out_semaphores.at[slot])

    @pl.when(turn == pl.num_programs(0) - 1)
    def _():
        for other in range(2):
            stored(placed, targets, out_semaphores, other)


def time_estimate(microseconds, accessed):
    return pl.CostEstimate(
        flops=int(microseconds * 1.1e9), bytes_accessed=int(accessed), transcendentals=0
    )


def fixed(shape):
    return pl.BlockSpec(shape, lambda turn, place: (0,) * len(shape), pipeline_mode=pl.Buffered(1))


def anywhere(values):
    return [pl.BlockSpec(memory_space=pltpu.HBM)] * len(values)


def run_forward(place, pieces, params, dims):
    heads, size, states, count = dims
    arrays, table = pieces
    dim = params[0].shape[0]
    width, conv_cols = heads * size, params[1].shape[1]
    blocks = len(table)
    tokens = blocks * GROUP

    def moving(columns):
        return pl.BlockSpec((GROUP, columns), lambda turn, place: (turn, 0))

    def rows_of_block(height, columns):
        return pl.BlockSpec((1, height, columns), lambda turn, place: (turn, 0, 0))

    results = pl.pallas_call(
        functools.partial(forward_kernel, dims, table, len(arrays)),
        grid_spec=pltpu.PrefetchScalarGridSpec(
            num_scalar_prefetch=1,
            grid=(blocks,),
            in_specs=[*anywhere(arrays), *[fixed(param.shape) for param in params]],
            out_specs=[
                moving(conv_cols),
                moving(conv_cols),
                moving(conv_cols),
                moving(width),
                moving(width),
                rows_of_block(8, GROUP),
                moving(width),
                rows_of_block(states, width),
                moving(width),
                rows_of_block(8, GROUP),
                moving(dim),
                *anywhere(range(4)),
            ],
            scratch_shapes=[
                pltpu.VMEM((states, width), f32),
                pltpu.VMEM((HALO + GROUP, conv_cols), f32),
                pltpu.VMEM((GROUP, GROUP), bf16),
                pltpu.VMEM((HALF, HALF), f32),
                pltpu.VMEM((2, GROUP, dim), bf16),
                pltpu.SemaphoreType.DMA((2,)),
                pltpu.VMEM((2, GROUP, width), bf16),
                pltpu.SemaphoreType.DMA((2,)),
            ],
        ),
        out_shape=[
            jax.ShapeDtypeStruct((tokens, conv_cols), bf16),
            jax.ShapeDtypeStruct((tokens, conv_cols), bf16),
            jax.ShapeDtypeStruct((tokens, conv_cols), bf16),
            jax.ShapeDtypeStruct((tokens, width), bf16),
            jax.ShapeDtypeStruct((tokens, width), bf16),
            jax.ShapeDtypeStruct((blocks, 8, GROUP), f32),
            jax.ShapeDtypeStruct((tokens, width), f32),
            jax.ShapeDtypeStruct((blocks, states, width), f32),
            jax.ShapeDtypeStruct((tokens, width), bf16),
            jax.ShapeDtypeStruct((blocks, 8, GROUP), f32),
            jax.ShapeDtypeStruct((tokens, dim), bf16),
            *scatter_shapes(count, width),
        ],
        compiler_params=pltpu.CompilerParams(vmem_limit_bytes=60 * MIB),
        cost_estimate=time_estimate(blocks * 3.0, tokens * (4 * dim + 24 * width)),
        name="forward_blocks",
    )(place, *arrays, *params)
    return results[:11], results[11:]


def out_grad_kernel(table, given, place_ref, *refs):
    arrays, refs = refs[:given], refs[given:]
    scaled_ref, out_rows_ref, out_grad_ref, slope_ref, cot_ref = refs[:5]
    buffer, semaphores, copied = refs[5:]
    place, turn = place_ref[0], pl.program_id(0)
    rows = buffer.shape[1]

    def copy_on(turn):
        target = cot_ref.at[pl.ds(pl.multiple_of(turn * rows, rows), rows)]
        return pltpu.make_async_copy(buffer.at[lax.rem(turn, 2)], target, copied)

    @pl.when(turn >= 1)
    def _():
        copy_on(turn - 1).wait()

    cot = fetched(arrays, table, buffer, semaphores, lambda block: in_time(place, block), 2)
    copy_on(turn).start()
    out_grad = dot_nt(cot, out_rows_ref[...])
    out_grad_ref[...] = out_grad
    for block in range(2):
        here = slice(block * GROUP, (block + 1) * GROUP)
        slope_ref[block] = sum_lanes(out_grad[here] * scaled_ref[here].astype(f32))

    @pl.when(turn == pl.num_programs(0) - 1)
    def _():
        copy_on(turn).wait()


def run_out_grad(place, cots, scaled, out_rows):
    arrays, table = cots
    width, dim = out_rows.shape
    blocks = len(table)
    tokens = blocks * GROUP
    return pl.pallas_call(
        functools.partial(out_grad_kernel, table, len(arrays)),
        grid_spec=pltpu.PrefetchScalarGridSpec(
            num_scalar_prefetch=1,
            grid=(blocks // 2,),
            in_specs=[
                *anywhere(arrays),
                pl.BlockSpec((2 * GROUP, width), lambda turn, place: (turn, 0)),
                fixed(out_rows.shape),
            ],
            out_specs=[
                pl.BlockSpec((2 * GROUP, width), lambda turn, place: (turn, 0)),
                pl.BlockSpec((2, 8, GROUP), lambda turn, place: (turn, 0, 0)),
                *anywhere(range(1)),
            ],
            scratch_shapes=[
                pltpu.VMEM((2, 2 * GROUP, dim), bf16),
                pltpu.SemaphoreType.DMA((2,)),
                pltpu.SemaphoreType.DMA,
            ],
        ),
        out_shape=[
            jax.ShapeDtypeStruct((tokens, width), f32),
            jax.ShapeDtypeStruct((blocks, 8, GROUP), f32),
            jax.ShapeDtypeStruct((tokens, dim), bf16),
        ],
        compiler_params=pltpu.CompilerParams(vmem_limit_bytes=60 * MIB),
        cost_estimate=time_estimate(12, tokens * (4 * dim + 6 * width)),
        name="out_grad",
    )(place, *arrays, scaled, out_rows)


def backward_kernel(dims, place_ref, *refs):
    heads, size, states, count = dims
    width = heads * size
    conv_cols = width + 2 * states
    conv_in_ref, active_ref, slope_ref, gate_act_ref, gate_slope_ref = refs[:5]
    raw_ref, ssd_ref, start_ref, out_grad_ref, norm_ref = refs[5:10]
    conv_w_ref, step_ref, rows_ref = refs[10:13]
    out_ref, targets = refs[13], refs[14:18]
    sums = refs[18:24]
    gain_ref, skip_ref, conv_wg_ref, conv_bg_ref, bias_ref, rate_ref = sums
    state, pre_grads, order, back_order, barred, placed, semaphores = refs[24:]
    taps = conv_w_ref.shape[0]
    turn = pl.program_id(0)
    slot = lax.rem(turn, 2)

    @pl.when(turn >= 2)
    def _():
        stored(placed, targets, semaphores, slot)

    @pl.when(pl.program_id(0) == 0)
    def _():
        state[...] = jnp.zeros_like(state)
        pre_grads[0:HALO] = jnp.zeros_like(pre_grads[0:HALO])
        for total in sums:
            total[...] = jnp.zeros_like(total)
        row, column = order_indices(GROUP)
        order[...] = ones_where(row <= column)
        back_order[...] = ones_where(row >= column)
        row, column = order_indices(HALF)
        barred[...] = jnp.where(row <= column, 0.0, -1e30)

    gate_act, ssd, out_grad = gate_act_ref[...].astype(f32), ssd_ref[...], out_grad_ref[...]
    norms = norm_ref[0].T
    scale, slope = norms[:, 0:1], norms[:, 1:2]
    gated = ssd * gate_act
    gain_ref[...] += jnp.sum(out_grad * (gated * scale), axis=0, keepdims=True)
    gated_grad = out_grad * (rows_ref[1:2] * scale) - gated * slope
    grad_low = (gated_grad * gate_act).astype(bf16)
    gate_grad = (gated_grad * ssd * gate_slope_ref[...].astype(f32)).astype(bf16)
    out_ref[:, :width] = gate_grad
    placed[slot, :, :width] = gate_grad
    ssd_grad = grad_low.astype(f32)

    raw = raw_ref[0] + step_ref[0:8, 0:1]
    rate = step_ref[8:16, 0:1]
    step, sig, log_step, ratio = step_values(raw)
    decay = step * rate
    running = sum_along(decay, order[...])
    later = running - log_step
    total = running[:, GROUP - 1 :]
    columns = to_columns([later * LOG2E, jnp.exp(running), jnp.exp(total - later)])
    running = running * LOG2E
    early_wide = spread_heads(columns, 8, heads, size)
    tail_wide = spread_heads(columns, 16, heads, size)

    signal = active_ref[:, :width]
    entry = active_ref[:, width : width + states]
    readout = active_ref[:, width + states :]
    signal_wide = signal.astype(f32)
    start = start_ref[0]
    start_low = start.astype(bf16)
    end_grad = state[...]
    end_low = end_grad.astype(bf16)
    first, second = slice(0, HALF), slice(HALF, GROUP)
    scores = dot_nt(entry[first], readout)
    later_scores = dot_nt(entry[second], readout[second])
    near_grad, far_grad, last_grad = 0.0, 0.0, 0.0
    within = []
    for h in range(heads):
        part, grad = signal[:, h * size : (h + 1) * size], grad_low[:, h * size : (h + 1) * size]
        begin, end = columns[first, h : h + 1], columns[second, h : h + 1]
        row_first, row_second = running[h : h + 1, first], running[h : h + 1, second]
        near = jnp.exp2(row_first - begin + barred[...])
        full = jnp.exp2(row_second - begin)
        last = jnp.exp2(row_second - end + barred[...])
        both = jnp.concatenate(
            [
                (near * scores[:, first]).astype(bf16),
                (full * scores[:, second]).astype(bf16),
            ],
            axis=1,
        )
        final = (last * later_scores).astype(bf16)
        within.append(jnp.concatenate([dot(both, grad), dot(final, grad[second])], axis=0))
        cross = dot_nt(part[first], grad)
        near_grad = near_grad + cross[:, first] * near
        far_grad = far_grad + cross[:, second] * full
        last_grad = last_grad + dot_nt(part[second], grad[second]) * last
    tail_grad = tail_wide * dot_split(dot, entry, end_grad)
    signal_grad = jnp.concatenate(within, axis=1) + tail_grad
    score_first = jnp.concatenate([near_grad, far_grad], axis=1).astype(bf16)
    score_second = last_grad.astype(bf16)
    tail = (signal_wide * tail_wide).astype(bf16)
    head_grad = ssd_grad * early_wide
    entry_grad = jnp.concatenate(
        [dot(score_first, readout), dot(score_second, readout[second])], axis=0
    ) + dot_nt(tail, end_low)
    readout_grad = dot_tn(score_first, entry[first]) + dot_nt(head_grad.astype(bf16), start_low)
    readout_last = readout_grad[second] + dot_tn(score_second, entry[second])
    total_wide = early_wide[GROUP - 1 :]
    state[...] = end_grad * total_wide + dot_split(dot_tn, readout, head_grad)

    skip = rows_ref[0:1]
    ones = head_ones(width, size)
    column_part = signal_wide * signal_grad
    row_part = ssd_grad * (ssd - skip * signal_wide)
    end_part = jnp.sum(signal_wide * tail_grad, axis=0, keepdims=True) + total_wide * jnp.sum(
        start * end_grad, axis=0, keepdims=True
    )

    def head_sums(value, parts):
        return sum(dot_nt(ones, part) for part in split_parts(value, parts))

    end_rows = head_sums(jnp.broadcast_to(end_part, (8, width)), 2)[:, 0:1]
    decay_grad = sum_along(head_sums(row_part - column_part, 2), back_order[...]) + end_rows
    raw_grad = head_sums(column_part, 1) * ratio + decay_grad * rate * sig
    skip_ref[...] += jnp.sum(ssd_grad * signal_wide, axis=0, keepdims=True)
    bias_ref[...] += raw_grad
    rate_ref[...] += decay_grad * decay
    raw_low = to_columns([raw_grad]).astype(bf16)
    out_ref[:, width + conv_cols :] = raw_low
    placed[slot, :, width + conv_cols :] = raw_low

    pre_grads[GROUP : GROUP + HALO] = pre_grads[0:HALO]
    pre_grads[0:GROUP, :width] = (signal_grad + skip * ssd_grad) * slope_ref[:, :width].astype(f32)
    sides = slope_ref[:, width:].astype(f32)
    pre_grads[0:GROUP, width : width + states] = entry_grad * sides[:, :states]
    pre_grads[0:HALF, width + states :] = readout_grad[first] * sides[first, states:]
    pre_grads[HALF:GROUP, width + states :] = readout_last * sides[second, states:]
    conv_w = conv_w_ref[...]
    conv_in = conv_in_ref[...].astype(f32)
    conv_grad = 0.0
    for k in range(taps):
        ahead = taps - 1 - k
        shifted = pre_grads[ahead : ahead + GROUP]
        conv_grad = conv_grad + conv_w[k : k + 1] * shifted
        conv_wg_ref[k : k + 1] += jnp.sum(shifted * conv_in, axis=0, keepdims=True)
        if ahead == 0:
            conv_bg_ref[...] += jnp.sum(shifted, axis=0, keepdims=True)
    conv_low = conv_grad.astype(bf16)
    out_ref[:, width : width + conv_cols] = conv_low
    placed[slot, :, width : width + conv_cols] = conv_low

    where = in_time(place_ref[0], pl.num_programs(0) - 1 - turn)
    store(placed.at[slot], targets, scatter_places(count), where, semaphores.at[slot])

    @pl.when(turn == pl.num_programs(0) - 1)
    def _():
        for other in range(2):
            stored(placed, targets, semaphores, other)


def run_backward(place, values, params, dims):
    heads, size, states, count = dims
    conv_cols, width = values[0].shape[1], heads * size
    tokens = values[0].shape[0]
    blocks = tokens // GROUP
    last = blocks - 1
    out_cols = width + conv_cols + LANES

    def moving(columns):
        return pl.BlockSpec((GROUP, columns), lambda turn, place: (last - turn, 0))

    def rows_of_block():
        return pl.BlockSpec((1, 8, GROUP), lambda turn, place: (last - turn, 0, 0))

    sums = [(1, width), (1, width), params[0].shape, (1, conv_cols), (8, GROUP), (8, GROUP)]
    return pl.pallas_call(
        functools.partial(backward_kernel, dims),
        grid_spec=pltpu.PrefetchScalarGridSpec(
            num_scalar_prefetch=1,
            grid=(blocks,),
            in_specs=[
                moving(conv_cols),
                moving(conv_cols),
                moving(conv_cols),
                moving(width),
                moving(width),
                rows_of_block(),
                moving(width),
                pl.BlockSpec((1, states, width), lambda turn, place: (last - turn, 0, 0)),
                moving(width),
                rows_of_block(),
                *[fixed(param.shape) for param in params],
            ],
            out_specs=[
                moving(out_cols),
                *anywhere(range(4)),
                *[fixed(shape) for shape in sums],
            ],
            scratch_shapes=[
                pltpu.VMEM((states, width), f32),
                pltpu.VMEM((GROUP + HALO, conv_cols), f32),
                pltpu.VMEM((GROUP, GROUP), bf16),
                pltpu.VMEM((GROUP, GROUP), bf16),
                pltpu.VMEM((HALF, HALF), f32),
                pltpu.VMEM((2, GROUP, out_cols), bf16),
                pltpu.SemaphoreType.DMA((2,)),
            ],
        ),
        out_shape=[
            jax.ShapeDtypeStruct((tokens, out_cols), bf16),
            *scatter_shapes(count, out_cols),
        ]
        + [jax.ShapeDtypeStruct(shape, f32) for shape in sums],
        compiler_params=pltpu.CompilerParams(vmem_limit_bytes=60 * MIB),
        cost_estimate=time_estimate(blocks * 3.5, tokens * 40 * width),
        name="backward_blocks",
    )(place, *values, *params)


def widen_kernel(place_ref, piece_ref, out_ref):
    out_ref[...] = piece_ref[0].astype(f32)


def assemble_out(place, pieces, per):
    count, size, dim = pieces.shape
    groups = count // per

    def source(turn, place):
        relative = (turn % groups * per + turn // groups) ^ place[0]
        return ((relative & 1) * (count // 2) + (relative >> 1), 0, 0)

    return pl.pallas_call(
        widen_kernel,
        grid_spec=pltpu.PrefetchScalarGridSpec(
            num_scalar_prefetch=1,
            grid=(count,),
            in_specs=[pl.BlockSpec((1, size, dim), source)],
            out_specs=pl.BlockSpec((size, dim), lambda turn, place: (turn, 0)),
        ),
        out_shape=jax.ShapeDtypeStruct((count * size, dim), f32),
        cost_estimate=time_estimate(5, count * size * dim * 6),
        name="assemble_out_weight_grad",
    )(place, pieces)


def assemble_kernel(dims, pieces_ref, out_ref):
    heads, size, states, count = dims
    width, shared = heads * size, 2 * states
    inner = count * width
    total = 0.0
    for device in range(count):
        columns = pieces_ref[device].astype(f32).T
        out_ref[device * width : (device + 1) * width] = columns[:width]
        out_ref[inner + device * width : inner + (device + 1) * width] = columns[width : 2 * width]
        total = total + columns[2 * width : 2 * width + shared]
        last = 2 * inner + shared + device * heads
        out_ref[last : last + heads] = columns[2 * width + shared : 2 * width + shared + heads]
    out_ref[2 * inner : 2 * inner + shared] = total


def assemble(pieces, dims):
    heads, size, states, count = dims
    _, rows, columns = pieces.shape
    tile = LANES if rows % LANES == 0 else rows
    out_rows = 2 * count * heads * size + 2 * states + count * heads
    return pl.pallas_call(
        functools.partial(assemble_kernel, dims),
        grid=(rows // tile,),
        in_specs=[pl.BlockSpec((count, tile, columns), lambda turn: (0, turn, 0))],
        out_specs=pl.BlockSpec((out_rows, tile), lambda turn: (0, turn)),
        out_shape=jax.ShapeDtypeStruct((out_rows, rows), f32),
        compiler_params=pltpu.CompilerParams(vmem_limit_bytes=60 * MIB),
        cost_estimate=time_estimate(8, out_rows * rows * 6),
        name="assemble_in_weight_grad",
    )(pieces)


def body(
    tokens,
    norm_gain,
    in_weight,
    conv_weight,
    conv_bias,
    dt_bias,
    decay_log,
    skip_scale,
    gate_gain,
    out_weight,
    cotangent,
):
    count, mine = lax.axis_size("seq"), lax.axis_index("seq")
    place = mine.astype(jnp.int32).reshape(1)
    inner, all_heads, conv_all = gate_gain.shape[0], dt_bias.shape[0], conv_bias.shape[0]
    size, states = inner // all_heads, (conv_all - inner) // 2
    heads, width = all_heads // count, inner // count
    dims = (heads, size, states, count)
    shared = 2 * states
    conv_cols = width + shared
    tok_rows = tokens.shape[1]
    per_plane = out_weight.shape[0] // width

    def own(vector, per, first=0):
        return lax.dynamic_slice_in_dim(vector, first + mine * per, per, vector.ndim - 1)

    def own_conv(array, first=0):
        return jnp.concatenate(
            [own(array, width, first), array[..., first + inner : first + conv_all]], axis=-1
        )

    tokens_row = tokens[0].astype(f32)
    inverse = lax.rsqrt(jnp.mean(tokens_row * tokens_row, axis=-1, keepdims=True) + epsilon)
    normed_own = (tokens_row * inverse * norm_gain).astype(bf16)
    step_own = own(in_weight, heads, inner + conv_all)
    w_own = jnp.concatenate(
        [
            own(in_weight, width),
            own_conv(in_weight, inner),
            jnp.pad(step_own, ((0, 0), (0, LANES - heads))),
        ],
        axis=1,
    )
    w_cols = lax.all_gather(w_own, "batch", axis=0, tiled=True)
    stages = gather_stages()
    held = gather_stage(gather_stage(gather_start(normed_own), 0), 1)
    held, cots = together(held, gather_start(cotangent[0]))
    cots = gather_stage(cots, 0)
    for stage in range(2, stages):
        held = gather_stage(held, stage)
    w_cols, held, cots, out_owned = together(w_cols, held, cots, out_weight)
    cots = gather_stage(cots, 1)
    out_rows = rows_from_owner(out_owned, width)

    conv_w, conv_b = own_conv(conv_weight), own_conv(conv_bias)[None]
    per_head = jnp.stack([own(dt_bias, heads), -jnp.exp(own(decay_log, heads))])
    per_head = jnp.pad(per_head, ((0, 0), (0, 8 - heads))).reshape(16, 1)
    step_rows = jnp.broadcast_to(per_head, (16, LANES))
    gain_own = own(gate_gain, width)[None]
    rows = jnp.concatenate(
        [jnp.repeat(own(skip_scale, heads), size)[None], gain_own, jnp.zeros((6, width), f32)],
        axis=0,
    )
    results, out_parts = run_forward(
        place, token_pieces(held), (w_cols, conv_w, conv_b, step_rows, rows), dims
    )
    conv_in, active, slope, gate_act, gate_slope, raw, ssd, starts, scaled, squares, normed = results
    out_parts, cots, out_rows = together(out_parts, cots, out_rows)
    for stage in range(2, stages):
        cots = gather_stage(cots, stage)

    def out_product(part):
        return dot(part, out_rows)

    out_send = out_product(out_parts[0]).astype(bf16)
    out_send, cots = together(out_send, cots)
    out_grad, slopes, cot = run_out_grad(place, token_pieces(cots), scaled, out_rows)
    sums = jnp.stack([squares[:, 0].reshape(-1), slopes[:, 0].reshape(-1)])
    out_ready, out_held = scatter_near(out_product, out_parts[1:], out_send)
    sums = sums + exchange(sums, "seq", 1)
    sums, first = together(sums, out_ready[0])
    sums = sums + exchange(sums, "seq", 2)
    sums, second = together(sums, out_ready[1])
    for bit in bits_of(count)[2:]:
        sums = sums + exchange(sums, "seq", bit)
    scale = lax.rsqrt(sums[0] / inner + epsilon)
    norms = jnp.stack([scale, scale * scale * scale * sums[1] / inner])
    norms = jnp.pad(norms, ((0, 6), (0, 0))).reshape(8, -1, GROUP).swapaxes(0, 1)
    normed_out = (scaled.astype(f32) * scale[:, None]).astype(bf16)
    out_term = jnp.einsum("te,td->ed", normed_out, cot, preferred_element_type=f32)
    out_term, norms, first, second = together(out_term.astype(bf16), norms, first, second)
    out_sum = lax.psum_scatter(out_term, "batch", scatter_dimension=0, tiled=True)
    out_ready, out_held = scatter_far((first, second), out_held, 0)

    values = (conv_in, active, slope, gate_act, gate_slope, raw, ssd, starts, out_grad, norms)
    results = run_backward(place, values, (conv_w, step_rows, rows), dims)
    proj_grad, back_parts = results[0], results[1:5]
    proj_grad, back_parts, out_ready, out_held, out_sum = together(
        proj_grad, back_parts, out_ready, out_held, out_sum
    )

    def back_product(part):
        return jnp.einsum("tf,df->td", part, w_cols, preferred_element_type=f32)

    def weight_product(part):
        return jnp.einsum("td,tf->df", normed, part, preferred_element_type=f32).astype(bf16)

    for stage in range(1, stages - 1):
        out_ready, out_held = scatter_far(out_ready, out_held, stage)
    back_send = back_product(back_parts[0]).astype(bf16)
    back_send, proj_grad = together(back_send, proj_grad)
    in_term = weight_product(proj_grad)
    in_term, keeps, out_held = together(in_term, back_parts[1:], out_held)
    in_sum = lax.psum_scatter(in_term, "batch", scatter_dimension=0, tiled=True)
    back_ready, back_held = scatter_near(back_product, keeps, back_send)
    back_ready, out_sum = together(back_ready, out_sum)
    back_ready, back_held = scatter_far(back_ready, back_held, 0)
    out_pieces = to_owner(out_sum)[None]

    back_held["kept"], in_term, results = together(back_held["kept"], in_term, results[5:])
    gain_term, skip_term, conv_w_term, conv_b_term, bias_term, rate_term = results
    norm_gain_term = jnp.sum(in_term.astype(f32) * w_cols.astype(f32), axis=1) / norm_gain

    def among_heads(vector, per, total):
        return lax.dynamic_update_slice_in_dim(jnp.zeros((total,), f32), vector, mine * per, 0)

    def among_conv(array):
        wide = jnp.zeros((array.shape[0], inner), f32)
        wide = lax.dynamic_update_slice_in_dim(wide, array[:, :width], mine * width, 1)
        return jnp.concatenate([wide, array[:, width:]], axis=1).reshape(-1)

    skip_heads = jnp.sum(skip_term.reshape(heads, size), axis=1)
    terms = [
        norm_gain_term,
        among_conv(conv_w_term),
        among_conv(conv_b_term),
        among_heads(jnp.sum(bias_term[:heads], axis=1), heads, all_heads),
        among_heads(jnp.sum(rate_term[:heads], axis=1), heads, all_heads),
        among_heads(skip_heads, heads, all_heads),
        among_heads(gain_term[0], width, inner),
    ]
    vector = jnp.concatenate(terms)
    padding = -vector.shape[0] % (8 * LANES)
    vector = jnp.pad(vector, (0, padding)).reshape(-1, LANES)

    axes = [(axis, bit) for axis in ("seq", "batch") for bit in bits_of(lax.axis_size(axis))]
    vector = vector + exchange(vector, *axes.pop(0))
    back_ready, vector, out_pieces = together(back_ready, vector, out_pieces)
    for stage in range(1, stages - 1):
        back_ready, back_held = scatter_far(back_ready, back_held, stage)
    out_pieces = double(out_pieces, 0)
    vector = vector + exchange(vector, *axes.pop(0))
    first_half, vector, out_pieces, in_sum = together(
        back_held["arrived"][0], vector, out_pieces, in_sum
    )
    back_held["arrived"] = (first_half, back_held["arrived"][1])
    pieces = lax.all_gather(in_sum, "seq", axis=0, tiled=False)
    in_weight_grad = assemble(pieces, dims).T
    for stage in range(1, stages):
        out_pieces = double(out_pieces, stage)
    while axes:
        vector = vector + exchange(vector, *axes.pop(0))
    vector = vector.reshape(-1)
    normed_grad = scatter_end(back_held)
    cot_row = cotangent[0].astype(f32)
    gained = norm_gain * normed_grad
    slope = inverse * inverse * inverse * jnp.mean(gained * tokens_row, axis=-1, keepdims=True)
    input_grad = cot_row + inverse * gained - tokens_row * slope
    own_scale = lax.dynamic_slice_in_dim(scale, mine * tok_rows, tok_rows, 0)[:, None]
    block_out = (tokens_row + own_scale * scatter_end(out_held)).astype(bf16)
    out_weight_grad = assemble_out(place, out_pieces, per_plane)

    parts, offset = [], 0
    for term in terms:
        parts.append(vector[offset : offset + term.shape[0]])
        offset += term.shape[0]
    return (
        block_out[None],
        input_grad[None],
        parts[0],
        in_weight_grad,
        parts[1].reshape(conv_weight.shape),
        parts[2],
        parts[3],
        parts[4],
        parts[5],
        parts[6],
        out_weight_grad,
    )


def solution(mesh):
    placed = (
        P("batch", "seq", None),
        P(),
        P("batch", None),
        P(),
        P(),
        P(),
        P(),
        P(),
        P(),
        P("batch", None),
        P("batch", "seq", None),
    )
    return jax.shard_map(
        body,
        mesh=mesh,
        in_specs=placed,
        out_specs=(
            P("batch", "seq", None),
            P("batch", "seq", None),
            P(),
            P("batch", None),
            P(),
            P(),
            P(),
            P(),
            P(),
            P(),
            P("batch", None),
        ),
        check_vma=False,
    )
```
